32 devices in a mesh: rep: 8 (over y, x, core), shard: 4 (over z).
Axes of the slice: x: 2, y: 2, z: 4, core: 2. Of those that a mesh axis runs over, the one named last changes fastest.
Arguments:
- tokens: bfloat16 [16, 1024, 2048], P('rep', 'shard'), may hold values from -6 to 6
- lengths: int32 [16], P('rep'), may hold values from 256 to 1024, as said below
- attn_gain: bfloat16 [2048], P('shard'), may hold values from 0.099609375 to 1.8984375
- w_query: bfloat16 [2048, 2048], P('shard'), may hold values from -0.125 to 0.125
- key_matrix: bfloat16 [2048, 1024], P('shard'), may hold values from -0.125 to 0.125
- value_matrix: bfloat16 [2048, 1024], P('shard'), may hold values from -0.125 to 0.125
- query_gain: bfloat16 [128], replicated, may hold values from 0.69921875 to 2
- key_gain: bfloat16 [128], replicated, may hold values from 0.69921875 to 2
- w_out: bfloat16 [2048, 2048], P('shard'), may hold values from -0.75 to 0.75
- mlp_gain: bfloat16 [2048], P('shard'), may hold values from 0.099609375 to 1.8984375
- w_gate: bfloat16 [2048, 6144], P('shard'), may hold values from -0.125 to 0.125
- w_up: bfloat16 [2048, 6144], P('shard'), may hold values from -0.125 to 0.125
- w_down: bfloat16 [2048, 6144], P('shard'), may hold values from -0.078125 to 0.078125
- cotangent: bfloat16 [16, 1024, 2048], P('rep', 'shard'), may hold values from -6 to 6
Outputs:
- output: bfloat16 [16, 1024, 2048], P('rep', 'shard')
- grad_tokens: bfloat16 [16, 1024, 2048], P('rep', 'shard')
- grad_attn_gain: float32 [2048], P('shard')
- grad_query: float32 [2048, 2048], P('shard')
- grad_key: float32 [2048, 1024], P('shard')
- grad_value: float32 [2048, 1024], P('shard')
- grad_query_gain: float32 [128], replicated
- grad_key_gain: float32 [128], replicated
- grad_out: float32 [2048, 2048], P('shard')
- grad_mlp_gain: float32 [2048], P('shard')
- grad_gate: float32 [2048, 6144], P('shard')
- grad_up: float32 [2048, 6144], P('shard')
- grad_down: float32 [2048, 6144], P('shard')
The draws below stay inside these ranges and needn't reach their ends.
Inputs may be any that keep to these rules, and one draw needn't show every extreme that they name: `lengths`: among the 2 sequences of each index of rep, one, drawn from the seed, has length 1024.
All inputs are finite; a program needn't handle non-finite values.
Results may differ from the reference program's by a relative error of at most 0.02.
Values may be sent and summed in bfloat16 or wider, within the bound.
No kernel may reach another device: no remote copies, remote signals or barrier semaphores. Data moves between devices by JAX's collectives and lax.ppermute only.
A program may use at most 512 MiB of HBM per device.

```python
import math
import jax
import jax.numpy as jnp
from jax import lax

MODEL_WIDTH = 2048
FF = 6144
QUERY_HEADS = 16
KEY_VALUE_HEADS = 8
HEAD_SIZE = 128
WINDOW = 512
SEQ_LEN = 1024
SEQ_GROUP = 2
SEQS = 16


def draw_lengths(key, part):
    key = jax.random.fold_in(key, 11)
    first, second = jax.random.split(key)
    ragged = jax.random.randint(first, (SEQS,), SEQ_LEN // 4, SEQ_LEN + 1)
    pick = jax.random.randint(second, (SEQS // SEQ_GROUP, 1), 0, SEQ_GROUP)
    full = (jnp.arange(SEQ_GROUP)[None, :] == pick).reshape(SEQS)
    return jnp.where(full, SEQ_LEN, ragged).astype(jnp.int32)


def steps_of(stream_key, extent, cuts, smallest, high):
    loudness = 1.0
    for position, parts in cuts:
        heights = jax.random.uniform(jax.random.fold_in(jax.random.fold_in(stream_key, 6), position), (parts,), jnp.float32, smallest / len(cuts), high / len(cuts))
        loudness = loudness * jnp.repeat(jnp.exp(heights), extent[position] // parts).reshape((-1,) + (1,) * (len(extent) - 1 - position))
    return loudness


def noise(key, shape, spread, reach, shards=(), kind=jnp.bfloat16):
    array = jax.random.normal(key, shape, jnp.float32) * spread
    if len(shards) > 0:
        array = steps_of(key, shape, shards, -0.22, 0.18) * array
    return jnp.clip(array, min=-reach, max=reach).astype(kind)


def setup_inputs(seed: int = 0) -> dict:
    key_list = jax.random.split(jax.random.key(seed), 15)
    return {
        "tokens": noise(key_list[0], (SEQS, SEQ_LEN, MODEL_WIDTH), 1.0, 6.0, ((0, 8), (1, 4))),
        "lengths": draw_lengths(jax.random.fold_in(key_list[14], 71), 0),
        "attn_gain": jnp.clip(1.0 + 0.18 * jax.random.normal(key_list[2], (MODEL_WIDTH,), jnp.float32), 0.099609375, 1.8984375).astype(jnp.bfloat16),
        "w_query": noise(key_list[3], (MODEL_WIDTH, QUERY_HEADS * HEAD_SIZE), MODEL_WIDTH ** -0.5, 0.125, ((0, 4),)),
        "key_matrix": noise(key_list[4], (MODEL_WIDTH, KEY_VALUE_HEADS * HEAD_SIZE), MODEL_WIDTH ** -0.5, 0.125, ((0, 4),)),
        "value_matrix": noise(key_list[5], (MODEL_WIDTH, KEY_VALUE_HEADS * HEAD_SIZE), MODEL_WIDTH ** -0.5, 0.125, ((0, 4),)),
        "query_gain": jnp.clip(jnp.exp(jax.random.uniform(key_list[6], (HEAD_SIZE,), jnp.float32, math.log(0.69921875), math.log(2.0))), 0.69921875, 2.0).astype(jnp.bfloat16),
        "key_gain": jnp.clip(jnp.exp(jax.random.uniform(key_list[7], (HEAD_SIZE,), jnp.float32, math.log(0.69921875), math.log(2.0))), 0.69921875, 2.0).astype(jnp.bfloat16),
        "w_out": noise(key_list[8], (MODEL_WIDTH, QUERY_HEADS * HEAD_SIZE), (QUERY_HEADS * HEAD_SIZE // 32) ** -0.5, 0.75, ((0, 4),)),
        "mlp_gain": jnp.clip(1.0 + 0.18 * jax.random.normal(key_list[9], (MODEL_WIDTH,), jnp.float32), 0.099609375, 1.8984375).astype(jnp.bfloat16),
        "w_gate": noise(key_list[10], (MODEL_WIDTH, FF), MODEL_WIDTH ** -0.5, 0.125, ((0, 4),)),
        "w_up": noise(key_list[11], (MODEL_WIDTH, FF), MODEL_WIDTH ** -0.5, 0.125, ((0, 4),)),
        "w_down": noise(key_list[12], (MODEL_WIDTH, FF), FF ** -0.5, 0.078125, ((0, 4),)),
        "cotangent": noise(key_list[13], (SEQS, SEQ_LEN, MODEL_WIDTH), 1.0, 6.0, ((0, 8), (1, 4))),
    }


EPS = 1e-06
ROPE_BASE = 1000000.0
NEG = -1e+30
HIGH = lax.Precision.HIGHEST

@jax.custom_vjp
def reduced_precision(v):
    return lax.optimization_barrier(v.astype(jnp.bfloat16)).astype(jnp.float32)

@jax.custom_vjp
def reduced_precision_back(v):
    return v

def low_keep(v):
    return (reduced_precision(v), None)

def low_pass(kept, grad):
    return (grad,)

def back_keep(v):
    return (v, None)

def back_low(kept, grad):
    return (reduced_precision(grad),)
reduced_precision.defvjp(low_keep, low_pass)
reduced_precision_back.defvjp(back_keep, back_low)

def matrix_product(left, right):
    return jnp.dot(left, right, precision=HIGH, preferred_element_type=jnp.float32)

def tables(positions):
    half = HEAD_SIZE // 2
    freq = ROPE_BASE ** (-jnp.arange(half, dtype=jnp.float32) * 2.0 / HEAD_SIZE)
    angle = positions.astype(jnp.float32)[:, None] * freq[None, :]
    angle = jnp.concatenate([angle, angle], -1)
    return (jnp.cos(angle)[:, None, :], jnp.sin(angle)[:, None, :])

def rotated_rows(value_rows):
    half = value_rows.shape[-1] // 2
    return jnp.concatenate([-value_rows[..., half:], value_rows[..., :half]], -1)

def head_norm(raw, gain):
    return raw * lax.rsqrt(lax.optimization_barrier(jnp.mean(raw * raw, -1, keepdims=True)) + EPS) * gain

def layer(x_seq, length, attn_gain, w_query, key_matrix, value_matrix, query_gain, key_gain, w_out, mlp_gain, w_gate, w_up, w_down):
    token_positions = x_seq.shape[0]
    positions = jnp.arange(token_positions, dtype=jnp.int32)
    cosine_table, sine_table = tables(positions)
    normalized_rows = reduced_precision(x_seq * lax.rsqrt(lax.optimization_barrier(jnp.mean(x_seq * x_seq, -1, keepdims=True)) + EPS) * attn_gain)
    query_raw = reduced_precision_back(matrix_product(normalized_rows, w_query)).reshape(token_positions, QUERY_HEADS, HEAD_SIZE)
    key_projected = reduced_precision_back(matrix_product(normalized_rows, key_matrix)).reshape(token_positions, KEY_VALUE_HEADS, HEAD_SIZE)
    value_rows = reduced_precision(reduced_precision_back(matrix_product(normalized_rows, value_matrix))).reshape(token_positions, KEY_VALUE_HEADS, HEAD_SIZE)
    query_rows_normalized = head_norm(query_raw, query_gain)
    key_normed = head_norm(key_projected, key_gain)
    query_rows = reduced_precision(query_rows_normalized * cosine_table + rotated_rows(query_rows_normalized) * sine_table).reshape(token_positions, KEY_VALUE_HEADS, QUERY_HEADS // KEY_VALUE_HEADS, HEAD_SIZE)
    keys = reduced_precision(key_normed * cosine_table + rotated_rows(key_normed) * sine_table)
    score = reduced_precision_back(jnp.einsum('qhgd,khd->hgqk', query_rows, keys, precision=HIGH) * HEAD_SIZE ** (-0.5))
    query_pos = positions[:, None]
    key_pos = positions[None, :]
    allowed = (key_pos <= query_pos) & (query_pos - key_pos < WINDOW) & ((key_pos < length) | (key_pos == query_pos))
    prob = jax.nn.softmax(jnp.where(allowed[None, None], score, NEG), axis=-1)
    mixed = jnp.einsum('hgqk,khd->qhgd', reduced_precision(prob), value_rows, precision=HIGH).reshape(token_positions, QUERY_HEADS * HEAD_SIZE)
    mixed = reduced_precision(reduced_precision_back(mixed))
    resid = x_seq + reduced_precision_back(matrix_product(mixed, w_out.T))
    mid = reduced_precision(resid * lax.rsqrt(lax.optimization_barrier(jnp.mean(resid * resid, -1, keepdims=True)) + EPS) * mlp_gain)
    gate = reduced_precision_back(matrix_product(mid, w_gate))
    up = reduced_precision_back(matrix_product(mid, w_up))
    act = reduced_precision(jax.nn.silu(gate) * up)
    branch = reduced_precision_back(matrix_product(act, w_down.T))
    keep = (positions < length).astype(x_seq.dtype)[:, None]
    return keep * (resid + branch)

def reference(tokens, lengths, attn_gain, w_query, key_matrix, value_matrix, query_gain, key_gain, w_out, mlp_gain, w_gate, w_up, w_down, cotangent):
    weights = tuple((w.astype(jnp.float32) for w in (attn_gain, w_query, key_matrix, value_matrix, query_gain, key_gain, w_out, mlp_gain, w_gate, w_up, w_down)))

    def one(carry, item):
        x_seq, length, grad_seq = item
        out_seq, pull = jax.vjp(lambda xs, *ws: layer(xs, length, *ws), x_seq, *weights)
        grads = pull(grad_seq)
        new_carry = tuple((c + g for c, g in zip(carry, grads[1:])))
        return (new_carry, (out_seq, grads[0]))
    start = tuple((jnp.zeros_like(w) for w in weights))
    totals, (outs, grads_in) = lax.scan(one, start, (tokens.astype(jnp.float32), lengths, cotangent.astype(jnp.float32)))
    return (outs.astype(jnp.bfloat16), grads_in.astype(jnp.bfloat16), totals[0], totals[1], totals[2], totals[3], totals[4], totals[5], totals[6], totals[7], totals[8], totals[9], totals[10])
```

```python
import jax
import jax.numpy as jnp
from jax import lax
from jax.sharding import PartitionSpec as P

WINDOW = 512


EPS = 1e-06
ROPE_BASE = 1000000.0
NEG = -1e30


def passed_along(x, axis, by):
    devices = lax.axis_size(axis)
    pairs = [(i, i + by) for i in range(devices) if 0 <= i + by < devices]
    return lax.ppermute(x, axis, pairs)


def tables(positions, head_dim):
    half = head_dim // 2
    freq = ROPE_BASE ** (-jnp.arange(half, dtype=jnp.float32) * 2.0 / head_dim)
    angle = positions.astype(jnp.float32)[:, None] * freq[None, :]
    angle = jnp.concatenate([angle, angle], -1)
    return (jnp.cos(angle)[None, :, None, :], jnp.sin(angle)[None, :, None, :])


def rotated_rows(value_rows):
    half = value_rows.shape[-1] // 2
    return jnp.concatenate([-value_rows[..., half:], value_rows[..., :half]], -1)


def head_norm(raw, gain):
    inverse = lax.rsqrt(jnp.mean(raw * raw, -1, keepdims=True) + EPS)
    unit = raw * inverse
    return (unit, inverse, unit * gain)


def norm_back(unit, inverse, grad_unit):
    return inverse * (grad_unit - unit * jnp.mean(grad_unit * unit, -1, keepdims=True))


def head_norm_back(unit, inverse, grad_normed, gain):
    grad_raw = norm_back(unit, inverse, grad_normed * gain)
    return (grad_raw, jnp.sum(unit * grad_normed, axis=(0, 1, 2)))


def scores(query_rows, keys, allowed, scale):
    raw = (
        jnp.einsum("sqhgd,skhd->shgqk", query_rows, keys, preferred_element_type=jnp.float32)
        * scale
    )
    return jnp.where(allowed[:, None, None], raw, NEG)


def outer(left, right):
    return jnp.einsum("rc,rf->cf", left, right, preferred_element_type=jnp.float32)


def on_device(
    tokens,
    lengths,
    attn_gain,
    w_query,
    key_matrix,
    value_matrix,
    query_gain,
    key_gain,
    w_out,
    mlp_gain,
    w_gate,
    w_up,
    w_down,
    cotangent,
):
    seq_count, piece, width = tokens.shape
    head_dim = query_gain.shape[0]
    heads_q = w_query.shape[1] // head_dim
    heads_kv = key_matrix.shape[1] // head_dim
    groups = heads_q // heads_kv
    rows = seq_count * piece
    scale = head_dim ** (-0.5)
    reach = (WINDOW + piece - 2) // piece
    owned = width // lax.axis_size("shard")
    shard_at = lax.axis_index("shard")
    query_pos = shard_at * piece + jnp.arange(piece, dtype=jnp.int32)
    key_pos = (shard_at - reach) * piece + jnp.arange((reach + 1) * piece, dtype=jnp.int32)
    near = (
        (key_pos[None, :] <= query_pos[:, None])
        & (query_pos[:, None] - key_pos[None, :] < WINDOW)
        & (key_pos[None, :] >= 0)
    )
    live = (key_pos[None, None, :] < lengths[:, None, None]) | (
        key_pos[None, :] == query_pos[:, None]
    )[None]
    allowed = near[None] & live
    valid = (query_pos[None, :] < lengths[:, None]).astype(jnp.float32).reshape(rows, 1)
    cosine_table, sine_table = tables(query_pos, head_dim)
    x_rows = tokens.astype(jnp.float32).reshape(rows, width)
    inverse_in = lax.rsqrt(jnp.mean(x_rows * x_rows, -1, keepdims=True) + EPS)
    x_unit = x_rows * inverse_in
    gain_piece = lax.all_gather(attn_gain, "shard", axis=0, tiled=True)
    query_piece = lax.all_gather(w_query, "shard", axis=0, tiled=True)
    key_piece = lax.all_gather(key_matrix, "shard", axis=0, tiled=True)
    value_piece = lax.all_gather(value_matrix, "shard", axis=0, tiled=True)
    normed_piece = (x_unit * gain_piece.astype(jnp.float32)).astype(jnp.bfloat16)
    acc_q = jnp.dot(normed_piece, query_piece, preferred_element_type=jnp.float32)
    acc_k = jnp.dot(normed_piece, key_piece, preferred_element_type=jnp.float32)
    acc_v = jnp.dot(normed_piece, value_piece, preferred_element_type=jnp.float32)
    normalized_rows = normed_piece
    gains = gain_piece.astype(jnp.float32)
    attn_in = normalized_rows
    attn_gains = gains
    query_unit, query_inverse, query_rows_normalized = head_norm(
        acc_q.reshape(seq_count, piece, heads_q, head_dim), query_gain.astype(jnp.float32)
    )
    key_unit, key_inverse, key_normed = head_norm(
        acc_k.reshape(seq_count, piece, heads_kv, head_dim), key_gain.astype(jnp.float32)
    )
    query_rows = (
        (query_rows_normalized * cosine_table + rotated_rows(query_rows_normalized) * sine_table)
        .astype(jnp.bfloat16)
        .reshape(seq_count, piece, heads_kv, groups, head_dim)
    )
    keys_own = (key_normed * cosine_table + rotated_rows(key_normed) * sine_table).astype(
        jnp.bfloat16
    )
    values_own = acc_v.reshape(seq_count, piece, heads_kv, head_dim).astype(jnp.bfloat16)
    own_pair = jnp.stack([keys_own, values_own])
    parts = []
    for fetch_back in range(reach, 0, -1):
        parts.append(passed_along(own_pair, "shard", fetch_back))
    parts.append(own_pair)
    near_pair = jnp.concatenate(parts, 2)
    score = scores(query_rows, near_pair[0], allowed, scale)
    top = jnp.max(score, -1, keepdims=True)
    expo = jnp.exp(score - top)
    total = jnp.sum(expo, -1, keepdims=True)
    prob = expo / total
    log_total = top + jnp.log(total)
    mixed = jnp.einsum(
        "shgqk,skhd->sqhgd",
        prob.astype(jnp.bfloat16),
        near_pair[1],
        preferred_element_type=jnp.float32,
    )
    mixed_rows = mixed.reshape(rows, heads_q * head_dim).astype(jnp.bfloat16)
    resid = x_rows + jnp.einsum(
        "rf,nf->rn",
        mixed_rows,
        lax.all_gather(w_out, "shard", axis=0, tiled=True),
        preferred_element_type=jnp.float32,
    )
    inverse_mid = lax.rsqrt(jnp.mean(resid * resid, -1, keepdims=True) + EPS)
    mid_unit = resid * inverse_mid
    gain_piece = lax.all_gather(mlp_gain, "shard", axis=0, tiled=True)
    gate_piece = lax.all_gather(w_gate, "shard", axis=0, tiled=True)
    up_piece = lax.all_gather(w_up, "shard", axis=0, tiled=True)
    normed_piece = (mid_unit * gain_piece.astype(jnp.float32)).astype(jnp.bfloat16)
    acc_gate = jnp.dot(normed_piece, gate_piece, preferred_element_type=jnp.float32)
    acc_up = jnp.dot(normed_piece, up_piece, preferred_element_type=jnp.float32)
    normalized_rows = normed_piece
    gains = gain_piece.astype(jnp.float32)
    mlp_in = normalized_rows
    sigma = jax.nn.sigmoid(acc_gate)
    swish = acc_gate * sigma
    act = (swish * acc_up).astype(jnp.bfloat16)
    mlp_out = jnp.einsum(
        "rf,nf->rn",
        act,
        lax.all_gather(w_down, "shard", axis=0, tiled=True),
        preferred_element_type=jnp.float32,
    )
    output = (valid * (resid + mlp_out)).astype(jnp.bfloat16).reshape(seq_count, piece, width)
    grad_y = cotangent.astype(jnp.float32).reshape(rows, width) * valid
    grad_y_low = grad_y.astype(jnp.bfloat16)
    grad_act = jnp.dot(
        grad_y_low,
        lax.all_gather(w_down, "shard", axis=0, tiled=True),
        preferred_element_type=jnp.float32,
    )
    grad_gate = (grad_act * acc_up * sigma * (1.0 + acc_gate * (1.0 - sigma))).astype(jnp.bfloat16)
    grad_up = (grad_act * swish).astype(jnp.bfloat16)
    gate_piece, up_piece = lax.all_gather((w_gate, w_up), "shard", axis=0, tiled=True)
    grad_mid = jnp.einsum(
        "rf,nf->rn", grad_gate, gate_piece, preferred_element_type=jnp.float32
    ) + jnp.einsum("rf,nf->rn", grad_up, up_piece, preferred_element_type=jnp.float32)
    grad_resid = grad_y + norm_back(mid_unit, inverse_mid, grad_mid * gains)
    mlp_gain_part = jnp.sum(mid_unit * grad_mid, 0)
    normalized_rows = mlp_in
    mlp_grads = jax.tree.map(
        lambda part: lax.psum_scatter(
            part.astype(jnp.bfloat16), "shard", scatter_dimension=0, tiled=True
        ).astype(jnp.float32),
        (
            outer(normalized_rows, grad_gate),
            outer(normalized_rows, grad_up),
            outer(grad_y_low, act),
        ),
    )
    resid_low = grad_resid.astype(jnp.bfloat16)
    grad_mixed = jnp.dot(
        resid_low,
        lax.all_gather(w_out, "shard", axis=0, tiled=True),
        preferred_element_type=jnp.float32,
    )
    grad_mixed = grad_mixed.astype(jnp.bfloat16).reshape(
        seq_count, piece, heads_kv, groups, head_dim
    )
    prob_again = jnp.exp(scores(query_rows, near_pair[0], allowed, scale) - log_total)
    grad_prob = jnp.einsum(
        "sqhgd,skhd->shgqk", grad_mixed, near_pair[1], preferred_element_type=jnp.float32
    )
    grad_values = jnp.einsum(
        "shgqk,sqhgd->skhd",
        prob_again.astype(jnp.bfloat16),
        grad_mixed,
        preferred_element_type=jnp.float32,
    )
    grad_score = (
        prob_again * (grad_prob - jnp.sum(prob_again * grad_prob, -1, keepdims=True))
    ).astype(jnp.bfloat16)
    grad_queries = (
        jnp.einsum(
            "shgqk,skhd->sqhgd", grad_score, near_pair[0], preferred_element_type=jnp.float32
        )
        * scale
    )
    grad_keys = (
        jnp.einsum("shgqk,sqhgd->skhd", grad_score, query_rows, preferred_element_type=jnp.float32)
        * scale
    )
    grad_pair = jnp.stack([grad_keys, grad_values])
    own_grad = grad_pair[:, :, reach * piece :]
    for back in range(1, reach + 1):
        lower = (reach - back) * piece
        own_grad = own_grad + passed_along(grad_pair[:, :, lower : lower + piece], "shard", -back)
    grad_query_post = grad_queries.reshape(seq_count, piece, heads_q, head_dim)
    grad_query_normed = grad_query_post * cosine_table - rotated_rows(grad_query_post * sine_table)
    grad_key_normed = own_grad[0] * cosine_table - rotated_rows(own_grad[0] * sine_table)
    grad_query_raw, query_gain_grad = head_norm_back(
        query_unit, query_inverse, grad_query_normed, query_gain.astype(jnp.float32)
    )
    grad_key_raw, key_gain_grad = head_norm_back(
        key_unit, key_inverse, grad_key_normed, key_gain.astype(jnp.float32)
    )
    grad_query_low = grad_query_raw.reshape(rows, heads_q * head_dim).astype(jnp.bfloat16)
    grad_key_low = grad_key_raw.reshape(rows, heads_kv * head_dim).astype(jnp.bfloat16)
    grad_value_low = own_grad[1].reshape(rows, heads_kv * head_dim).astype(jnp.bfloat16)
    query_piece, key_piece, value_piece = lax.all_gather(
        (w_query, key_matrix, value_matrix), "shard", axis=0, tiled=True
    )
    grad_in = (
        jnp.einsum("rf,nf->rn", grad_query_low, query_piece, preferred_element_type=jnp.float32)
        + jnp.einsum("rf,nf->rn", grad_key_low, key_piece, preferred_element_type=jnp.float32)
        + jnp.einsum("rf,nf->rn", grad_value_low, value_piece, preferred_element_type=jnp.float32)
    )
    grad_tokens = (
        (grad_resid + norm_back(x_unit, inverse_in, grad_in * attn_gains))
        .astype(jnp.bfloat16)
        .reshape(seq_count, piece, width)
    )
    attn_gain_part = jnp.sum(x_unit * grad_in, 0)
    normalized_rows = attn_in
    attn_grads = jax.tree.map(
        lambda part: lax.psum_scatter(
            part.astype(jnp.bfloat16), "shard", scatter_dimension=0, tiled=True
        ).astype(jnp.float32),
        (
            outer(normalized_rows, grad_query_low),
            outer(normalized_rows, grad_key_low),
            outer(normalized_rows, grad_value_low),
            outer(resid_low, mixed_rows),
        ),
    )
    head_grads = lax.psum(
        (query_gain_grad, key_gain_grad, attn_gain_part, mlp_gain_part), ("rep", "shard")
    )
    attn_gain_total = lax.dynamic_slice_in_dim(head_grads[2], shard_at * owned, owned, 0)
    mlp_gain_total = lax.dynamic_slice_in_dim(head_grads[3], shard_at * owned, owned, 0)
    summed = (
        lax.psum(attn_grads[0].astype(jnp.bfloat16), "rep").astype(jnp.float32),
        lax.psum(attn_grads[1].astype(jnp.bfloat16), "rep").astype(jnp.float32),
        lax.psum(attn_grads[2].astype(jnp.bfloat16), "rep").astype(jnp.float32),
        lax.psum(attn_grads[3].astype(jnp.bfloat16), "rep").astype(jnp.float32),
        lax.psum(mlp_grads[0].astype(jnp.bfloat16), "rep").astype(jnp.float32),
        lax.psum(mlp_grads[1].astype(jnp.bfloat16), "rep").astype(jnp.float32),
        lax.psum(mlp_grads[2].astype(jnp.bfloat16), "rep").astype(jnp.float32),
    )
    attn_grads = summed[:4]
    mlp_grads = summed[4:]
    return (
        output,
        grad_tokens,
        attn_gain_total,
        attn_grads[0],
        attn_grads[1],
        attn_grads[2],
        head_grads[0],
        head_grads[1],
        attn_grads[3],
        mlp_gain_total,
        mlp_grads[0],
        mlp_grads[1],
        mlp_grads[2],
    )


CORE, ACROSS_X, ACROSS_Y = 1, 2, 4


def across(x, mask):
    count = lax.axis_size("rep")
    return lax.ppermute(x, "rep", [(i, i ^ mask) for i in range(count)])


def around(x):
    count = lax.axis_size("shard")
    return lax.ppermute(x, "shard", [(i, (i + 1) % count) for i in range(count)])


def after(x, *done):
    return lax.optimization_barrier((x, *done))[0]


def plane_gather(piece):
    half = piece.shape[0] // 2
    from_x = across(piece, ACROSS_X)
    from_y = across(piece, ACROSS_Y)
    far = [across(from_x[:half], ACROSS_Y), across(from_y[half:], ACROSS_X)]
    return [piece, from_x, from_y, jnp.concatenate(far, 0)]


def plane_sum(blocks):
    low = jnp.bfloat16
    half = blocks[0].shape[0] // 2
    head = [b[:half] for b in blocks]
    tail = [b[half:] for b in blocks]
    head_two = head[2] + across(head[3].astype(low), ACROSS_X)
    head_own = head[0] + across(head[1].astype(low), ACROSS_X)
    tail_one = tail[1] + across(tail[3].astype(low), ACROSS_Y)
    tail_own = tail[0] + across(tail[2].astype(low), ACROSS_Y)
    head_own = head_own + across(head_two.astype(low), ACROSS_Y)
    tail_own = tail_own + across(tail_one.astype(low), ACROSS_X)
    return jnp.concatenate([head_own, tail_own], 0)


def sequence_pairs(turn):
    groups, shards = lax.axis_size("rep"), lax.axis_size("shard")
    pairs = []
    for group in range(groups):
        chip, core = divmod(group, 2)
        for at in range(shards):
            to_group, to_shard = 2 * chip + at // 2, 2 * core + (turn ^ (at & 1))
            pairs.append((group * shards + at, to_group * shards + to_shard))
    return pairs


def to_sequences(x):
    odd = lax.axis_index("shard") & 1
    came = [
        lax.ppermute(
            lax.dynamic_index_in_dim(x, turn ^ odd, 0, keepdims=False),
            ("rep", "shard"),
            sequence_pairs(turn),
        )
        for turn in range(2)
    ]
    even = odd == 0
    return jnp.concatenate(
        [jnp.where(even, came[0], came[1]), jnp.where(even, came[1], came[0])], 0
    )


def from_sequences(x):
    odd = lax.axis_index("shard") & 1
    x = x.reshape(2, x.shape[0] // 2, *x.shape[1:])
    came = [
        lax.ppermute(
            lax.dynamic_index_in_dim(x, turn ^ odd, 0, keepdims=False),
            ("rep", "shard"),
            [(to, at) for at, to in sequence_pairs(turn)],
        )
        for turn in range(2)
    ]
    even = odd == 0
    return jnp.stack([jnp.where(even, came[0], came[1]), jnp.where(even, came[1], came[0])])


def column_block(weights, at):
    cuts = [w.shape[1] // 8 for w in weights]
    return jnp.concatenate(
        [lax.dynamic_slice_in_dim(w, at * cut, cut, 1) for w, cut in zip(weights, cuts)], 1
    )


def gather_blocks(weights, first=None):
    me = lax.axis_index("rep")
    own = [column_block(weights, me ^ i) for i in range(8)]
    travelling = own[0] if first is None else after(own[0], first)
    rows = [[block] for block in own]
    for _ in range(1, lax.axis_size("shard")):
        travelling = around(travelling)
        for i, block in enumerate(plane_gather(travelling)):
            rows[2 * i].append(block)
            rows[2 * i + 1].append(across(block, CORE))
    return jnp.concatenate([jnp.concatenate(r, 0) for r in rows], 1), travelling


def rolled(x):
    count, at = lax.axis_size("shard"), lax.axis_index("shard")
    width = x.shape[1] // count
    return jnp.concatenate(
        [
            lax.dynamic_slice_in_dim(x, ((at - i) % count) * width, width, 1)
            for i in range(count)
        ],
        1,
    )


def sum_blocks(grad, columns):
    low = jnp.bfloat16
    blocks = [grad[:, i * columns : (i + 1) * columns] for i in range(8)]
    chips = [
        blocks[2 * i] + across(blocks[2 * i + 1].astype(low), CORE) for i in range(4)
    ]
    own = plane_sum(chips)
    count = lax.axis_size("shard")
    piece = own.shape[0] // count
    total = own[piece : 2 * piece]
    for i in range(2, count + 1):
        at = i % count
        total = own[at * piece : (at + 1) * piece] + around(total.astype(low))
    return total.astype(low)


def spread_blocks(block, columns):
    me = lax.axis_index("rep")
    pieces = []
    for piece in plane_gather(block):
        pieces += [piece, across(piece, CORE)]
    outs = []
    start = 0
    for width in columns:
        out = jnp.zeros((block.shape[0], 8 * width), jnp.float32)
        for i, piece in enumerate(pieces):
            out = lax.dynamic_update_slice_in_dim(
                out, piece[:, start : start + width].astype(jnp.float32), (me ^ i) * width, 1
            )
        outs.append(out)
        start += width
    return outs


def on_device_block(
    tokens,
    lengths,
    attn_gain,
    w_query,
    key_matrix,
    value_matrix,
    query_gain,
    key_gain,
    w_out,
    mlp_gain,
    w_gate,
    w_up,
    w_down,
    cotangent,
):
    low, full = jnp.bfloat16, jnp.float32
    width = tokens.shape[2]
    head_dim = query_gain.shape[0]
    heads_q = w_query.shape[1] // head_dim
    heads_kv = key_matrix.shape[1] // head_dim
    groups = heads_q // heads_kv
    scale = head_dim ** (-0.5)
    owned = width // lax.axis_size("shard")
    shard_at = lax.axis_index("shard")
    me = lax.axis_index("rep")
    core = me & 1

    x_low = to_sequences(tokens)
    rows = x_low.shape[0]
    qkv_all, qkv_came = gather_blocks((w_query, key_matrix, value_matrix))
    out_all, out_came = gather_blocks((w_out,), qkv_came)
    gate_up_own = lax.all_gather(
        after(column_block((w_gate, w_up), me), qkv_came), "shard", axis=0, tiled=True
    )
    down_own = lax.all_gather(
        after(column_block((w_down,), me), out_came), "shard", axis=0, tiled=True
    )
    gate_up = [gate_up_own, across(gate_up_own, CORE)]
    down = [down_own, across(down_own, CORE)]
    grad_y_low = to_sequences(after(cotangent, out_came))

    other_lengths = across(lengths, CORE)
    both = jnp.where(
        core == 0,
        jnp.concatenate([lengths, other_lengths]),
        jnp.concatenate([other_lengths, lengths]),
    )
    length = lax.dynamic_index_in_dim(both, shard_at, 0, keepdims=False)
    query_pos = core * rows + jnp.arange(rows, dtype=jnp.int32)
    key_pos = (core - 1) * rows + jnp.arange(2 * rows, dtype=jnp.int32)
    allowed = (
        (key_pos[None, :] <= query_pos[:, None])
        & (query_pos[:, None] - key_pos[None, :] < WINDOW)
        & (key_pos[None, :] >= 0)
        & ((key_pos[None, :] < length) | (key_pos[None, :] == query_pos[:, None]))
    )
    valid = (query_pos < length)[:, None]
    cosine_table, sine_table = tables(query_pos, head_dim)
    cosine_table, sine_table = cosine_table[0], sine_table[0]
    attn_gains = lax.all_gather(attn_gain, "shard", axis=0, tiled=True).astype(full)
    mlp_gains = lax.all_gather(mlp_gain, "shard", axis=0, tiled=True).astype(full)
    query_gains, key_gains = query_gain.astype(full), key_gain.astype(full)

    x_rows = x_low.astype(full)
    inverse_in = lax.rsqrt(jnp.mean(x_rows * x_rows, -1, keepdims=True) + EPS)
    x_unit = x_rows * inverse_in
    normed = rolled((x_unit * attn_gains).astype(low))
    qkv = jnp.dot(normed, qkv_all, preferred_element_type=full)
    qkv = qkv.reshape(rows, heads_kv, groups + 2, head_dim)
    query_unit, query_inverse, query_normed = head_norm(
        qkv[:, :, :groups].reshape(rows, heads_q, head_dim), query_gains
    )
    key_unit, key_inverse, key_normed = head_norm(qkv[:, :, groups], key_gains)
    query_rows = (query_normed * cosine_table + rotated_rows(query_normed) * sine_table).astype(low)
    query_rows = query_rows.reshape(rows, heads_kv, groups, head_dim)
    keys_own = (key_normed * cosine_table + rotated_rows(key_normed) * sine_table).astype(low)
    values_own = qkv[:, :, groups + 1].astype(low)
    own_pair = jnp.stack([keys_own, values_own])
    count = lax.axis_size("rep")

    def other_order(x):
        pairs = x.reshape(*x.shape[:2], heads_kv // 2, 2, head_dim)
        return pairs[:, :, :, ::-1].reshape(x.shape)

    earlier = lax.ppermute(
        other_order(own_pair), "rep", [(i, i + 1) for i in range(0, count, 2)]
    )
    keys, values = jnp.concatenate([earlier, own_pair], 1)

    def masked_scores():
        raw = jnp.einsum("qhgd,khd->hgqk", query_rows, keys, preferred_element_type=full) * scale
        return jnp.where(allowed[None, None], raw, NEG)

    score = masked_scores()
    top = jnp.max(score, -1, keepdims=True)
    expo = jnp.exp(score - top)
    total = jnp.sum(expo, -1, keepdims=True)
    prob = expo / total
    log_total = top + jnp.log(total)
    mixed = jnp.einsum("hgqk,khd->qhgd", prob.astype(low), values, preferred_element_type=full)
    mixed = mixed.reshape(rows, heads_q * head_dim).astype(low)
    branch = jnp.einsum("rf,nf->rn", mixed, out_all, preferred_element_type=full)

    resid = x_rows + rolled(branch)
    inverse_mid = lax.rsqrt(jnp.mean(resid * resid, -1, keepdims=True) + EPS)
    mid_unit = resid * inverse_mid
    mid = (mid_unit * mlp_gains).astype(low)

    grad_y_low = jnp.where(valid, grad_y_low, jnp.zeros_like(grad_y_low))
    grad_y_all = jnp.concatenate(plane_gather(grad_y_low), 0)
    mid_all = jnp.concatenate(plane_gather(after(mid, grad_y_all)), 0)

    acts, grads_pre = [], []
    for part in range(2):
        pre = jnp.dot(mid_all, gate_up[part], preferred_element_type=full)
        gate, up = jnp.split(pre, 2, 1)
        sigma = jax.nn.sigmoid(gate)
        swish = gate * sigma
        acts.append((swish * up).astype(low))
        grad_act = jnp.dot(grad_y_all, down[part], preferred_element_type=full)
        grad_gate = (grad_act * up * sigma * (1.0 + gate * (1.0 - sigma))).astype(low)
        grad_up = (grad_act * swish).astype(low)
        grads_pre.append(jnp.concatenate([grad_gate, grad_up], 1))

    def both_parts(left, right):
        return sum(
            jnp.einsum("rf,nf->rn", l, r, preferred_element_type=full) for l, r in zip(left, right)
        )

    grad_mid_parts = both_parts(grads_pre, gate_up)
    grad_mid = plane_sum(jnp.split(grad_mid_parts, 4, 0))
    mlp_out = plane_sum(jnp.split(after(both_parts(acts, down), grad_mid), 4, 0))
    output = from_sequences(jnp.where(valid, resid + mlp_out, 0.0).astype(low))

    def mlp_weight_grad(left, parts):
        other = outer(left, parts[1]).astype(low)
        own = outer(left, parts[0]) + across(other, CORE)
        return lax.psum_scatter(own.astype(low), "shard", scatter_dimension=0, tiled=True)

    gate_up_grad = mlp_weight_grad(mid_all, grads_pre)
    down_grad = mlp_weight_grad(grad_y_all, acts)
    grad_gate_total, grad_up_total = spread_blocks(
        gate_up_grad, (gate_up_grad.shape[1] // 2,) * 2
    )
    (grad_down_total,) = spread_blocks(down_grad, (down_grad.shape[1],))

    mlp_gain_part = jnp.sum(mid_unit * grad_mid, 0)
    grad_resid = grad_y_low.astype(full) + norm_back(mid_unit, inverse_mid, grad_mid * mlp_gains)
    resid_low = rolled(grad_resid.astype(low))
    grad_mixed = jnp.dot(resid_low, out_all, preferred_element_type=full).astype(low)
    grad_out_all = outer(resid_low, mixed)
    grad_mixed = grad_mixed.reshape(rows, heads_kv, groups, head_dim)
    prob_again = jnp.exp(masked_scores() - log_total)
    grad_prob = jnp.einsum("qhgd,khd->hgqk", grad_mixed, values, preferred_element_type=full)
    grad_values = jnp.einsum(
        "hgqk,qhgd->khd", prob_again.astype(low), grad_mixed, preferred_element_type=full
    )
    grad_score = (
        prob_again * (grad_prob - jnp.sum(prob_again * grad_prob, -1, keepdims=True))
    ).astype(low)
    grad_queries = (
        jnp.einsum("hgqk,khd->qhgd", grad_score, keys, preferred_element_type=full) * scale
    )
    grad_keys = (
        jnp.einsum("hgqk,qhgd->khd", grad_score, query_rows, preferred_element_type=full) * scale
    )
    grad_pair = jnp.stack([grad_keys, grad_values])
    own_grad = grad_pair[:, rows:] + lax.ppermute(
        other_order(grad_pair[:, :rows].astype(low)), "rep", [(i + 1, i) for i in range(0, count, 2)]
    )
    grad_query_post = grad_queries.reshape(rows, heads_q, head_dim)
    grad_query_normed = grad_query_post * cosine_table - rotated_rows(grad_query_post * sine_table)
    grad_key_normed = own_grad[0] * cosine_table - rotated_rows(own_grad[0] * sine_table)
    grad_query_raw = norm_back(query_unit, query_inverse, grad_query_normed * query_gains)
    grad_key_raw = norm_back(key_unit, key_inverse, grad_key_normed * key_gains)
    query_gain_part = jnp.sum(query_unit * grad_query_normed, axis=(0, 1))
    key_gain_part = jnp.sum(key_unit * grad_key_normed, axis=(0, 1))
    grad_qkv = jnp.concatenate(
        [
            grad_query_raw.reshape(rows, heads_kv, groups, head_dim).astype(low),
            grad_key_raw[:, :, None].astype(low),
            own_grad[1][:, :, None].astype(low),
        ],
        2,
    ).reshape(rows, -1)
    grad_in = rolled(jnp.einsum("rf,nf->rn", grad_qkv, qkv_all, preferred_element_type=full))
    grad_tokens = from_sequences(
        (grad_resid + norm_back(x_unit, inverse_in, grad_in * attn_gains)).astype(low)
    )
    attn_gain_part = jnp.sum(x_unit * grad_in, 0)

    out_block = w_out.shape[1] // 8
    qkv_block = qkv_all.shape[1] // 8
    (grad_out_total,) = spread_blocks(sum_blocks(grad_out_all, out_block), (out_block,))
    grad_query_total, grad_key_total, grad_value_total = spread_blocks(
        sum_blocks(outer(normed, grad_qkv), qkv_block),
        (groups * head_dim, head_dim, head_dim),
    )
    gain_grads = lax.psum(
        (query_gain_part, key_gain_part, attn_gain_part, mlp_gain_part), ("rep", "shard")
    )
    attn_gain_total = lax.dynamic_slice_in_dim(gain_grads[2], shard_at * owned, owned, 0)
    mlp_gain_total = lax.dynamic_slice_in_dim(gain_grads[3], shard_at * owned, owned, 0)
    return (
        output,
        grad_tokens,
        attn_gain_total,
        grad_query_total,
        grad_key_total,
        grad_value_total,
        gain_grads[0],
        gain_grads[1],
        grad_out_total,
        mlp_gain_total,
        grad_gate_total,
        grad_up_total,
        grad_down_total,
    )


def solution(mesh):
    sizes = (mesh.shape["rep"], mesh.shape["shard"])
    return jax.shard_map(
        on_device_block if sizes == (8, 4) else on_device,
        mesh=mesh,
        in_specs=(
            P("rep", "shard", None),
            P("rep"),
            P("shard"),
            P("shard", None),
            P("shard", None),
            P("shard", None),
            P(),
            P(),
            P("shard", None),
            P("shard"),
            P("shard", None),
            P("shard", None),
            P("shard", None),
            P("rep", "shard", None),
        ),
        out_specs=(
            P("rep", "shard", None),
            P("rep", "shard", None),
            P("shard"),
            P("shard", None),
            P("shard", None),
            P("shard", None),
            P(),
            P(),
            P("shard", None),
            P("shard"),
            P("shard", None),
            P("shard", None),
            P("shard", None),
        ),
        check_vma=False,
    )
```

```python
import jax
import jax.numpy as jnp
from jax import lax
from jax.experimental import pallas as pl
from jax.experimental.pallas import tpu as pltpu
from jax.sharding import PartitionSpec as P

WINDOW = 512


EPS = 1e-06
ROPE_BASE = 1000000.0
NEG = -1e30


def passed_along(x, axis, by):
    devices = lax.axis_size(axis)
    pairs = [(i, i + by) for i in range(devices) if 0 <= i + by < devices]
    return lax.ppermute(x, axis, pairs)


def tables(positions, head_dim):
    half = head_dim // 2
    freq = ROPE_BASE ** (-jnp.arange(half, dtype=jnp.float32) * 2.0 / head_dim)
    angle = positions.astype(jnp.float32)[:, None] * freq[None, :]
    angle = jnp.concatenate([angle, angle], -1)
    return (jnp.cos(angle)[None, :, None, :], jnp.sin(angle)[None, :, None, :])


def rotated_rows(value_rows):
    half = value_rows.shape[-1] // 2
    return jnp.concatenate([-value_rows[..., half:], value_rows[..., :half]], -1)


def head_norm(raw, gain):
    inverse = lax.rsqrt(jnp.mean(raw * raw, -1, keepdims=True) + EPS)
    unit = raw * inverse
    return (unit, inverse, unit * gain)


def norm_back(unit, inverse, grad_unit):
    return inverse * (grad_unit - unit * jnp.mean(grad_unit * unit, -1, keepdims=True))


def head_norm_back(unit, inverse, grad_normed, gain):
    grad_raw = norm_back(unit, inverse, grad_normed * gain)
    return (grad_raw, jnp.sum(unit * grad_normed, axis=(0, 1, 2)))


def scores(query_rows, keys, allowed, scale):
    raw = (
        jnp.einsum("sqhgd,skhd->shgqk", query_rows, keys, preferred_element_type=jnp.float32)
        * scale
    )
    return jnp.where(allowed[:, None, None], raw, NEG)


def outer(left, right):
    return jnp.einsum("rc,rf->cf", left, right, preferred_element_type=jnp.float32)


def on_device(
    tokens,
    lengths,
    attn_gain,
    w_query,
    key_matrix,
    value_matrix,
    query_gain,
    key_gain,
    w_out,
    mlp_gain,
    w_gate,
    w_up,
    w_down,
    cotangent,
):
    seq_count, piece, width = tokens.shape
    head_dim = query_gain.shape[0]
    heads_q = w_query.shape[1] // head_dim
    heads_kv = key_matrix.shape[1] // head_dim
    groups = heads_q // heads_kv
    rows = seq_count * piece
    scale = head_dim ** (-0.5)
    reach = (WINDOW + piece - 2) // piece
    owned = width // lax.axis_size("shard")
    shard_at = lax.axis_index("shard")
    query_pos = shard_at * piece + jnp.arange(piece, dtype=jnp.int32)
    key_pos = (shard_at - reach) * piece + jnp.arange((reach + 1) * piece, dtype=jnp.int32)
    near = (
        (key_pos[None, :] <= query_pos[:, None])
        & (query_pos[:, None] - key_pos[None, :] < WINDOW)
        & (key_pos[None, :] >= 0)
    )
    live = (key_pos[None, None, :] < lengths[:, None, None]) | (
        key_pos[None, :] == query_pos[:, None]
    )[None]
    allowed = near[None] & live
    valid = (query_pos[None, :] < lengths[:, None]).astype(jnp.float32).reshape(rows, 1)
    cosine_table, sine_table = tables(query_pos, head_dim)
    x_rows = tokens.astype(jnp.float32).reshape(rows, width)
    inverse_in = lax.rsqrt(jnp.mean(x_rows * x_rows, -1, keepdims=True) + EPS)
    x_unit = x_rows * inverse_in
    gain_piece = lax.all_gather(attn_gain, "shard", axis=0, tiled=True)
    query_piece = lax.all_gather(w_query, "shard", axis=0, tiled=True)
    key_piece = lax.all_gather(key_matrix, "shard", axis=0, tiled=True)
    value_piece = lax.all_gather(value_matrix, "shard", axis=0, tiled=True)
    normed_piece = (x_unit * gain_piece.astype(jnp.float32)).astype(jnp.bfloat16)
    acc_q = jnp.dot(normed_piece, query_piece, preferred_element_type=jnp.float32)
    acc_k = jnp.dot(normed_piece, key_piece, preferred_element_type=jnp.float32)
    acc_v = jnp.dot(normed_piece, value_piece, preferred_element_type=jnp.float32)
    normalized_rows = normed_piece
    gains = gain_piece.astype(jnp.float32)
    attn_in = normalized_rows
    attn_gains = gains
    query_unit, query_inverse, query_rows_normalized = head_norm(
        acc_q.reshape(seq_count, piece, heads_q, head_dim), query_gain.astype(jnp.float32)
    )
    key_unit, key_inverse, key_normed = head_norm(
        acc_k.reshape(seq_count, piece, heads_kv, head_dim), key_gain.astype(jnp.float32)
    )
    query_rows = (
        (query_rows_normalized * cosine_table + rotated_rows(query_rows_normalized) * sine_table)
        .astype(jnp.bfloat16)
        .reshape(seq_count, piece, heads_kv, groups, head_dim)
    )
    keys_own = (key_normed * cosine_table + rotated_rows(key_normed) * sine_table).astype(
        jnp.bfloat16
    )
    values_own = acc_v.reshape(seq_count, piece, heads_kv, head_dim).astype(jnp.bfloat16)
    own_pair = jnp.stack([keys_own, values_own])
    parts = []
    for fetch_back in range(reach, 0, -1):
        parts.append(passed_along(own_pair, "shard", fetch_back))
    parts.append(own_pair)
    near_pair = jnp.concatenate(parts, 2)
    score = scores(query_rows, near_pair[0], allowed, scale)
    top = jnp.max(score, -1, keepdims=True)
    expo = jnp.exp(score - top)
    total = jnp.sum(expo, -1, keepdims=True)
    prob = expo / total
    log_total = top + jnp.log(total)
    mixed = jnp.einsum(
        "shgqk,skhd->sqhgd",
        prob.astype(jnp.bfloat16),
        near_pair[1],
        preferred_element_type=jnp.float32,
    )
    mixed_rows = mixed.reshape(rows, heads_q * head_dim).astype(jnp.bfloat16)
    resid = x_rows + jnp.einsum(
        "rf,nf->rn",
        mixed_rows,
        lax.all_gather(w_out, "shard", axis=0, tiled=True),
        preferred_element_type=jnp.float32,
    )
    inverse_mid = lax.rsqrt(jnp.mean(resid * resid, -1, keepdims=True) + EPS)
    mid_unit = resid * inverse_mid
    gain_piece = lax.all_gather(mlp_gain, "shard", axis=0, tiled=True)
    gate_piece = lax.all_gather(w_gate, "shard", axis=0, tiled=True)
    up_piece = lax.all_gather(w_up, "shard", axis=0, tiled=True)
    normed_piece = (mid_unit * gain_piece.astype(jnp.float32)).astype(jnp.bfloat16)
    acc_gate = jnp.dot(normed_piece, gate_piece, preferred_element_type=jnp.float32)
    acc_up = jnp.dot(normed_piece, up_piece, preferred_element_type=jnp.float32)
    normalized_rows = normed_piece
    gains = gain_piece.astype(jnp.float32)
    mlp_in = normalized_rows
    sigma = jax.nn.sigmoid(acc_gate)
    swish = acc_gate * sigma
    act = (swish * acc_up).astype(jnp.bfloat16)
    mlp_out = jnp.einsum(
        "rf,nf->rn",
        act,
        lax.all_gather(w_down, "shard", axis=0, tiled=True),
        preferred_element_type=jnp.float32,
    )
    output = (valid * (resid + mlp_out)).astype(jnp.bfloat16).reshape(seq_count, piece, width)
    grad_y = cotangent.astype(jnp.float32).reshape(rows, width) * valid
    grad_y_low = grad_y.astype(jnp.bfloat16)
    grad_act = jnp.dot(
        grad_y_low,
        lax.all_gather(w_down, "shard", axis=0, tiled=True),
        preferred_element_type=jnp.float32,
    )
    grad_gate = (grad_act * acc_up * sigma * (1.0 + acc_gate * (1.0 - sigma))).astype(jnp.bfloat16)
    grad_up = (grad_act * swish).astype(jnp.bfloat16)
    gate_piece, up_piece = lax.all_gather((w_gate, w_up), "shard", axis=0, tiled=True)
    grad_mid = jnp.einsum(
        "rf,nf->rn", grad_gate, gate_piece, preferred_element_type=jnp.float32
    ) + jnp.einsum("rf,nf->rn", grad_up, up_piece, preferred_element_type=jnp.float32)
    grad_resid = grad_y + norm_back(mid_unit, inverse_mid, grad_mid * gains)
    mlp_gain_part = jnp.sum(mid_unit * grad_mid, 0)
    normalized_rows = mlp_in
    mlp_grads = jax.tree.map(
        lambda part: lax.psum_scatter(
            part.astype(jnp.bfloat16), "shard", scatter_dimension=0, tiled=True
        ).astype(jnp.float32),
        (
            outer(normalized_rows, grad_gate),
            outer(normalized_rows, grad_up),
            outer(grad_y_low, act),
        ),
    )
    resid_low = grad_resid.astype(jnp.bfloat16)
    grad_mixed = jnp.dot(
        resid_low,
        lax.all_gather(w_out, "shard", axis=0, tiled=True),
        preferred_element_type=jnp.float32,
    )
    grad_mixed = grad_mixed.astype(jnp.bfloat16).reshape(
        seq_count, piece, heads_kv, groups, head_dim
    )
    prob_again = jnp.exp(scores(query_rows, near_pair[0], allowed, scale) - log_total)
    grad_prob = jnp.einsum(
        "sqhgd,skhd->shgqk", grad_mixed, near_pair[1], preferred_element_type=jnp.float32
    )
    grad_values = jnp.einsum(
        "shgqk,sqhgd->skhd",
        prob_again.astype(jnp.bfloat16),
        grad_mixed,
        preferred_element_type=jnp.float32,
    )
    grad_score = (
        prob_again * (grad_prob - jnp.sum(prob_again * grad_prob, -1, keepdims=True))
    ).astype(jnp.bfloat16)
    grad_queries = (
        jnp.einsum(
            "shgqk,skhd->sqhgd", grad_score, near_pair[0], preferred_element_type=jnp.float32
        )
        * scale
    )
    grad_keys = (
        jnp.einsum("shgqk,sqhgd->skhd", grad_score, query_rows, preferred_element_type=jnp.float32)
        * scale
    )
    grad_pair = jnp.stack([grad_keys, grad_values])
    own_grad = grad_pair[:, :, reach * piece :]
    for back in range(1, reach + 1):
        lower = (reach - back) * piece
        own_grad = own_grad + passed_along(grad_pair[:, :, lower : lower + piece], "shard", -back)
    grad_query_post = grad_queries.reshape(seq_count, piece, heads_q, head_dim)
    grad_query_normed = grad_query_post * cosine_table - rotated_rows(grad_query_post * sine_table)
    grad_key_normed = own_grad[0] * cosine_table - rotated_rows(own_grad[0] * sine_table)
    grad_query_raw, query_gain_grad = head_norm_back(
        query_unit, query_inverse, grad_query_normed, query_gain.astype(jnp.float32)
    )
    grad_key_raw, key_gain_grad = head_norm_back(
        key_unit, key_inverse, grad_key_normed, key_gain.astype(jnp.float32)
    )
    grad_query_low = grad_query_raw.reshape(rows, heads_q * head_dim).astype(jnp.bfloat16)
    grad_key_low = grad_key_raw.reshape(rows, heads_kv * head_dim).astype(jnp.bfloat16)
    grad_value_low = own_grad[1].reshape(rows, heads_kv * head_dim).astype(jnp.bfloat16)
    query_piece, key_piece, value_piece = lax.all_gather(
        (w_query, key_matrix, value_matrix), "shard", axis=0, tiled=True
    )
    grad_in = (
        jnp.einsum("rf,nf->rn", grad_query_low, query_piece, preferred_element_type=jnp.float32)
        + jnp.einsum("rf,nf->rn", grad_key_low, key_piece, preferred_element_type=jnp.float32)
        + jnp.einsum("rf,nf->rn", grad_value_low, value_piece, preferred_element_type=jnp.float32)
    )
    grad_tokens = (
        (grad_resid + norm_back(x_unit, inverse_in, grad_in * attn_gains))
        .astype(jnp.bfloat16)
        .reshape(seq_count, piece, width)
    )
    attn_gain_part = jnp.sum(x_unit * grad_in, 0)
    normalized_rows = attn_in
    attn_grads = jax.tree.map(
        lambda part: lax.psum_scatter(
            part.astype(jnp.bfloat16), "shard", scatter_dimension=0, tiled=True
        ).astype(jnp.float32),
        (
            outer(normalized_rows, grad_query_low),
            outer(normalized_rows, grad_key_low),
            outer(normalized_rows, grad_value_low),
            outer(resid_low, mixed_rows),
        ),
    )
    head_grads = lax.psum(
        (query_gain_grad, key_gain_grad, attn_gain_part, mlp_gain_part), ("rep", "shard")
    )
    attn_gain_total = lax.dynamic_slice_in_dim(head_grads[2], shard_at * owned, owned, 0)
    mlp_gain_total = lax.dynamic_slice_in_dim(head_grads[3], shard_at * owned, owned, 0)
    summed = (
        lax.psum(attn_grads[0].astype(jnp.bfloat16), "rep").astype(jnp.float32),
        lax.psum(attn_grads[1].astype(jnp.bfloat16), "rep").astype(jnp.float32),
        lax.psum(attn_grads[2].astype(jnp.bfloat16), "rep").astype(jnp.float32),
        lax.psum(attn_grads[3].astype(jnp.bfloat16), "rep").astype(jnp.float32),
        lax.psum(mlp_grads[0].astype(jnp.bfloat16), "rep").astype(jnp.float32),
        lax.psum(mlp_grads[1].astype(jnp.bfloat16), "rep").astype(jnp.float32),
        lax.psum(mlp_grads[2].astype(jnp.bfloat16), "rep").astype(jnp.float32),
    )
    attn_grads = summed[:4]
    mlp_grads = summed[4:]
    return (
        output,
        grad_tokens,
        attn_gain_total,
        attn_grads[0],
        attn_grads[1],
        attn_grads[2],
        head_grads[0],
        head_grads[1],
        attn_grads[3],
        mlp_gain_total,
        mlp_grads[0],
        mlp_grads[1],
        mlp_grads[2],
    )


CORE, ACROSS_X, ACROSS_Y = 1, 2, 4
VMEM_BYTES = 56 * 2**20


def across(x, mask):
    count = lax.axis_size("rep")
    return lax.ppermute(x, "rep", [(i, i ^ mask) for i in range(count)])


def around(x, by):
    count = lax.axis_size("shard")
    return lax.ppermute(x, "shard", [(i, (i + by) % count) for i in range(count)])


def after(x, *done):
    return lax.optimization_barrier((x, *done))[0]


def ring_gather(x):
    before, behind = around(x, 1), around(x, -1)
    return [x, before, around(before, 1), behind]


def ring_sum(chunks, kind):
    last = chunks[3] + around(chunks[2].astype(kind), 1)
    return chunks[0] + around(chunks[1].astype(kind), -1) + around(last.astype(kind), 1)


def plane_gather(piece):
    half = piece.shape[0] // 2
    from_x = across(piece, ACROSS_X)
    from_y = across(piece, ACROSS_Y)
    far = [across(from_x[:half], ACROSS_Y), across(from_y[half:], ACROSS_X)]
    return [piece, from_x, from_y, jnp.concatenate(far, 0)]


def plane_sum(own, blocks):
    low = jnp.bfloat16
    half = own.shape[0] // 2
    one, two, three = blocks
    head_two = two[:half] + across(three[:half].astype(low), ACROSS_X)
    head_own = own[:half] + across(one[:half].astype(low), ACROSS_X)
    tail_one = one[half:] + across(three[half:].astype(low), ACROSS_Y)
    tail_own = own[half:] + across(two[half:].astype(low), ACROSS_Y)
    head_own = head_own + across(head_two.astype(low), ACROSS_Y)
    tail_own = tail_own + across(tail_one.astype(low), ACROSS_X)
    return jnp.concatenate([head_own, tail_own], 0)


def sequence_pairs(turn):
    groups, shards = lax.axis_size("rep"), lax.axis_size("shard")
    pairs = []
    for group in range(groups):
        chip, core = divmod(group, 2)
        for at in range(shards):
            to_group, to_shard = 2 * chip + at // 2, 2 * core + (turn ^ (at & 1))
            pairs.append((group * shards + at, to_group * shards + to_shard))
    return pairs


def rolled(x):
    count, at = lax.axis_size("shard"), lax.axis_index("shard")
    width = x.shape[1] // count
    return jnp.concatenate(
        [lax.dynamic_slice_in_dim(x, ((at - i) % count) * width, width, 1) for i in range(count)],
        1,
    )


def to_sequences(x):
    odd = lax.axis_index("shard") & 1
    came = [
        lax.ppermute(
            lax.dynamic_index_in_dim(x, turn ^ odd, 0, keepdims=False),
            ("rep", "shard"),
            sequence_pairs(turn),
        )
        for turn in range(2)
    ]
    even = odd == 0
    return rolled(
        jnp.concatenate(
            [jnp.where(even, came[0], came[1]), jnp.where(even, came[1], came[0])], 0
        )
    )


def from_sequences(x):
    odd = lax.axis_index("shard") & 1
    x = rolled(x).reshape(2, x.shape[0] // 2, x.shape[1])
    came = [
        lax.ppermute(
            lax.dynamic_index_in_dim(x, turn ^ odd, 0, keepdims=False),
            ("rep", "shard"),
            [(to, at) for at, to in sequence_pairs(turn)],
        )
        for turn in range(2)
    ]
    even = odd == 0
    return jnp.stack([jnp.where(even, came[0], came[1]), jnp.where(even, came[1], came[0])])


def column_block(weights, at):
    cuts = [w.shape[1] // 8 for w in weights]
    return jnp.concatenate(
        [lax.dynamic_slice_in_dim(w, at * cut, cut, 1) for w, cut in zip(weights, cuts)], 1
    )


def gather_blocks(weights, first=()):
    me = lax.axis_index("rep")
    own = [column_block(weights, me ^ i) for i in range(8)]
    came = ring_gather(after(own[0], *first))[1:]
    rows = [[block] for block in own]
    for shard in came:
        for i, block in enumerate(plane_gather(shard)):
            rows[2 * i].append(block)
            rows[2 * i + 1].append(across(block, CORE))
    return rows, came


def spread_blocks(block, columns):
    me = lax.axis_index("rep")
    pieces = []
    for piece in plane_gather(block):
        pieces += [piece, across(piece, CORE)]
    outs = []
    start = 0
    for width in columns:
        out = jnp.zeros((block.shape[0], 8 * width), jnp.float32)
        for i, piece in enumerate(pieces):
            out = lax.dynamic_update_slice_in_dim(
                out, piece[:, start : start + width].astype(jnp.float32), (me ^ i) * width, 1
            )
        outs.append(out)
        start += width
    return outs


def everywhere_sum(x):
    for mask in (CORE, ACROSS_X, ACROSS_Y):
        x = x + across(x, mask)
    return x


def turned(x):
    return pltpu.roll(x, x.shape[-1] // 2, x.ndim - 1)


def nt(left, right):
    return lax.dot_general(
        left, right, (((1,), (1,)), ((), ())), preferred_element_type=jnp.float32
    )


def tn(left, right):
    return lax.dot_general(
        left, right, (((0,), (0,)), ((), ())), preferred_element_type=jnp.float32
    )


def unit_of(raw):
    inverse = lax.rsqrt(jnp.mean(raw * raw, -1, keepdims=True) + EPS)
    return raw * inverse, inverse


def project_body(normed, w0, w1, w2, w3, cosine, sine, gains, raw, query, key, value):
    weights = (w0, w1, w2, w3)
    step = w0.shape[0]
    dim = cosine.shape[1]
    raw[...] = sum(
        jnp.dot(
            normed[:, i * step : (i + 1) * step], weights[i][...],
            preferred_element_type=jnp.float32,
        )
        for i in range(4)
    )
    for i in range(3):
        unit, _ = unit_of(raw[:, i * dim : (i + 1) * dim])
        head = unit * gains[i // 2 : i // 2 + 1, :]
        head = (head * cosine[...] + turned(head) * sine[...]).astype(jnp.bfloat16)
        if i < 2:
            query[:, i * dim : (i + 1) * dim] = head
        else:
            key[...] = head
    value[...] = raw[:, 3 * dim :].astype(jnp.bfloat16)


def window_scores(info, query, keys, part, scale):
    rows, columns = query.shape[0], keys.shape[0]
    half = columns - rows
    row = lax.broadcasted_iota(jnp.int32, (rows, columns), 0)
    column = lax.broadcasted_iota(jnp.int32, (rows, columns), 1)
    gap = column - row - half
    slot = column + ((info[0] - 1) * half + part * rows)
    allowed = (gap <= 0) & (gap > -half) & (slot >= 0) & ((slot < info[1]) | (gap == 0))
    return nt(query, keys) * scale, allowed


def near(before, own, part):
    rows = own.shape[0] // 2
    if part == 0:
        return jnp.concatenate([before[...], own[:rows]], 0)
    return jnp.concatenate([before[rows:], own[...]], 0)


def attend_body(info, query, key_before, key, value_before, value, mixed, log_total):
    dim = key.shape[1]
    rows = query.shape[0] // 2
    for part in range(2):
        keys, values = near(key_before, key, part), near(value_before, value, part)
        at = slice(part * rows, (part + 1) * rows)
        for head in range(2):
            on = slice(head * dim, (head + 1) * dim)
            score, allowed = window_scores(info, query[at, on], keys, part, dim**-0.5)
            score = jnp.where(allowed, score, NEG)
            top = jnp.max(score, -1, keepdims=True)
            expo = jnp.exp(score - top)
            total = jnp.sum(expo, -1, keepdims=True)
            prob = (expo * (1.0 / total)).astype(jnp.bfloat16)
            mixed[at, on] = jnp.dot(prob, values, preferred_element_type=jnp.float32).astype(
                jnp.bfloat16
            )
            log_total[at, on] = jnp.broadcast_to(top + jnp.log(total), (rows, dim))


def attend_back_body(
    info, query, key_before, key, value_before, value, log_total, grad_mixed, raw, cosine, sine,
    gain, grad_query, grad_own, grad_before, gain_part, grad_keys, grad_values,
):
    dim = key.shape[1]
    rows = query.shape[0] // 2
    scale = dim**-0.5
    grad_keys[...] = jnp.zeros_like(grad_keys)
    grad_values[...] = jnp.zeros_like(grad_values)
    gain_total = jnp.zeros((1, dim), jnp.float32)
    for part in range(2):
        keys, values = near(key_before, key, part), near(value_before, value, part)
        at = slice(part * rows, (part + 1) * rows)
        seen = slice(part * rows, part * rows + keys.shape[0])
        for head in range(2):
            on = slice(head * dim, (head + 1) * dim)
            score, allowed = window_scores(info, query[at, on], keys, part, scale)
            prob = jnp.where(allowed, jnp.exp(score - log_total[at, on][:, :1]), 0.0)
            grad_prob = nt(grad_mixed[at, on], values)
            inner = jnp.sum(prob * grad_prob, -1, keepdims=True)
            grad_score = (prob * (grad_prob - inner)).astype(jnp.bfloat16)
            grad_values[seen, :] += tn(prob.astype(jnp.bfloat16), grad_mixed[at, on])
            grad_keys[seen, :] += tn(grad_score, query[at, on]) * scale
            back = jnp.dot(grad_score, keys, preferred_element_type=jnp.float32) * scale
            back = back * cosine[at, :] - turned(back) * sine[at, :]
            unit, inverse = unit_of(raw[at, on])
            gain_total += jnp.sum(unit * back, 0, keepdims=True)
            back = back * gain[...]
            back = inverse * (back - unit * jnp.mean(back * unit, -1, keepdims=True))
            grad_query[at, on] = back.astype(jnp.bfloat16)
    gain_part[...] = gain_total
    grad_before[:, :dim] = grad_keys[: 2 * rows, :].astype(jnp.bfloat16)
    grad_before[:, dim:] = grad_values[: 2 * rows, :].astype(jnp.bfloat16)
    grad_own[:, :dim] = grad_keys[2 * rows :, :]
    grad_own[:, dim:] = grad_values[2 * rows :, :]


def finish_body(grad_query, grad_own, came, raw, cosine, sine, gain, grad_block, gain_part):
    dim = cosine.shape[1]
    back = grad_own[:, :dim] + came[:, :dim].astype(jnp.float32)
    back = back * cosine[...] - turned(back) * sine[...]
    unit, inverse = unit_of(raw[...])
    gain_part[...] = jnp.sum(unit * back, 0, keepdims=True)
    back = back * gain[...]
    back = inverse * (back - unit * jnp.mean(back * unit, -1, keepdims=True))
    grad_block[:, : 2 * dim] = grad_query[...]
    grad_block[:, 2 * dim : 3 * dim] = back.astype(jnp.bfloat16)
    grad_value = grad_own[:, dim:] + came[:, dim:].astype(jnp.float32)
    grad_block[:, 3 * dim :] = grad_value.astype(jnp.bfloat16)


def vmem_call(body, outs, flops, scratch=(), scalars=0, specs=None, name=None):
    def call(*args):
        in_specs = [
            pl.BlockSpec(memory_space=pltpu.SMEM if i < scalars else pltpu.VMEM)
            for i in range(len(args))
        ]
        for at, spec in (specs or {}).items():
            in_specs[at] = spec
        return pl.pallas_call(
            body,
            grid=(1,),
            out_shape=outs,
            in_specs=in_specs,
            out_specs=jax.tree.map(lambda _: pl.BlockSpec(memory_space=pltpu.VMEM), outs),
            scratch_shapes=scratch,
            compiler_params=pltpu.CompilerParams(vmem_limit_bytes=VMEM_BYTES),
            cost_estimate=pl.CostEstimate(
                flops=flops,
                bytes_accessed=sum(a.size * a.dtype.itemsize for a in args),
                transcendentals=0,
            ),
            name=name,
        )(*args)

    return call


def column_spec(rows, columns, at):
    return pl.BlockSpec((rows, columns), lambda i: (0, at))


def hidden_body(mid, grad_y, gate_w, up_w, down_w, act, grad_gate, grad_up):
    gate = jnp.dot(mid[...], gate_w[...], preferred_element_type=jnp.float32)
    up = jnp.dot(mid[...], up_w[...], preferred_element_type=jnp.float32)
    grad_act = jnp.dot(grad_y[...], down_w[...], preferred_element_type=jnp.float32)
    sigma = jax.nn.sigmoid(gate)
    swish = gate * sigma
    act[...] = (swish * up).astype(jnp.bfloat16)
    grad_gate[...] = (grad_act * up * sigma * (1.0 + gate * (1.0 - sigma))).astype(jnp.bfloat16)
    grad_up[...] = (grad_act * swish).astype(jnp.bfloat16)


def hidden_units(mid, grad_y, gate_w, up_w, down_w):
    rows, width = mid.shape
    units = gate_w.shape[1]
    high, cut = rows // 2, units // 6
    row_spec = pl.BlockSpec((high, width), lambda i, j: (i, 0))
    weight_spec = pl.BlockSpec((width, cut), lambda i, j: (0, j))
    out_spec = pl.BlockSpec((high, cut), lambda i, j: (i, j))
    return pl.pallas_call(
        hidden_body,
        grid=(2, 6),
        out_shape=[jax.ShapeDtypeStruct((rows, units), jnp.bfloat16)] * 3,
        in_specs=[row_spec, row_spec, weight_spec, weight_spec, weight_spec],
        out_specs=[out_spec] * 3,
        compiler_params=pltpu.CompilerParams(vmem_limit_bytes=VMEM_BYTES),
        cost_estimate=pl.CostEstimate(
            flops=6 * rows * width * units, bytes_accessed=10 * rows * width, transcendentals=0
        ),
        name="hidden_units",
    )(mid, grad_y, gate_w, up_w, down_w)


def from_hidden(lefts, rights, first_block, blocks):
    count = len(lefts)
    rows, units = lefts[0].shape[0] // 4, lefts[0].shape[1]
    width = rights[0].shape[0]
    cut = width // 4

    def body(*refs):
        out = refs[-1]
        out[...] = sum(nt(refs[i][...], refs[count + i][...]) for i in range(count)).astype(
            jnp.bfloat16
        )

    return pl.pallas_call(
        body,
        grid=(blocks, 4),
        out_shape=jax.ShapeDtypeStruct((blocks * rows, width), jnp.bfloat16),
        in_specs=[pl.BlockSpec((rows, units), lambda i, j: (i + first_block, 0))] * count
        + [pl.BlockSpec((cut, units), lambda i, j: (j, 0))] * count,
        out_specs=pl.BlockSpec((rows, cut), lambda i, j: (i, j)),
        compiler_params=pltpu.CompilerParams(vmem_limit_bytes=VMEM_BYTES),
        cost_estimate=pl.CostEstimate(
            flops=2 * count * blocks * rows * width * units,
            bytes_accessed=2 * count * width * units,
            transcendentals=0,
        ),
        name="from_hidden",
    )(*lefts, *rights)


def on_device_block(
    tokens,
    lengths,
    attn_gain,
    w_query,
    key_matrix,
    value_matrix,
    query_gain,
    key_gain,
    w_out,
    mlp_gain,
    w_gate,
    w_up,
    w_down,
    cotangent,
):
    low, full = jnp.bfloat16, jnp.float32
    width = tokens.shape[2]
    head_dim = query_gain.shape[0]
    shards = lax.axis_size("shard")
    shard_at = lax.axis_index("shard")
    me = lax.axis_index("rep")
    core = me & 1
    count = lax.axis_size("rep")

    qkv_rows, qkv_came = gather_blocks((w_query, key_matrix, value_matrix))
    x_low = to_sequences(after(tokens, qkv_came[0], qkv_came[2]))
    rows = x_low.shape[0]
    out_rows, out_came = gather_blocks((w_out,), (x_low,))
    gains = jnp.concatenate(
        ring_gather(jnp.stack([attn_gain, mlp_gain])), 1
    ).astype(full)
    attn_gains, mlp_gains = gains[:1], gains[1:]
    query_gains = query_gain.astype(full)[None]
    key_gains = key_gain.astype(full)[None]

    other_lengths = across(lengths, CORE)
    both = jnp.where(
        core == 0,
        jnp.concatenate([lengths, other_lengths]),
        jnp.concatenate([other_lengths, lengths]),
    )
    length = lax.dynamic_index_in_dim(both, shard_at, 0, keepdims=False)
    info = jnp.stack([core, length]).astype(jnp.int32)
    query_pos = core * rows + jnp.arange(rows, dtype=jnp.int32)
    valid = (query_pos < length)[:, None]
    cosine, sine = tables(query_pos, head_dim)
    cosine, sine = cosine[0, :, 0], sine[0, :, 0]
    sine = jnp.concatenate([-sine[:, : head_dim // 2], sine[:, head_dim // 2 :]], 1)

    gate_up_own = [column_block((w_gate, w_up), me ^ i) for i in range(2)]
    down_own = [column_block((w_down,), me ^ i) for i in range(2)]
    gate_up_came = ring_gather(after(gate_up_own[0], *out_came))[1:]
    grad_y_low = to_sequences(after(cotangent, gate_up_came[0], gate_up_came[2]))
    down_came = ring_gather(after(down_own[0], grad_y_low))[1:]

    def whole(own, came):
        came = [own[0], *came], [own[1], *(across(c, CORE) for c in came)]
        return [jnp.concatenate(part, 0) for part in came]

    gate_up = whole(gate_up_own, gate_up_came)
    units = gate_up[0].shape[1] // 2
    gate_all = jnp.concatenate([part[:, :units] for part in gate_up], 1)
    up_all = jnp.concatenate([part[:, units:] for part in gate_up], 1)
    down_all = jnp.concatenate(whole(down_own, down_came), 1)

    x_rows = x_low.astype(full)
    inverse_in = lax.rsqrt(jnp.mean(x_rows * x_rows, -1, keepdims=True) + EPS)
    x_unit = x_rows * inverse_in
    normed = (x_unit * attn_gains).astype(low)
    pair_columns = 2 * head_dim
    head_rows = jax.ShapeDtypeStruct((rows, head_dim), low)
    pair_rows = jax.ShapeDtypeStruct((rows, pair_columns), low)
    project = vmem_call(
        project_body,
        [jax.ShapeDtypeStruct((rows, 2 * pair_columns), full), pair_rows, head_rows, head_rows],
        4 * rows * width * pair_columns,
        name="project",
    )
    attend = vmem_call(
        attend_body,
        [pair_rows, jax.ShapeDtypeStruct((rows, pair_columns), full)],
        12 * rows * rows * pair_columns,
        scalars=1,
        name="attend",
    )
    head_gains = jnp.concatenate([query_gains, key_gains], 0)
    upward = [(i, i + 1) for i in range(0, count, 2)]
    downward = [(i + 1, i) for i in range(0, count, 2)]
    raws, queries, kept, own_pairs = [], [], [], []
    for i in range(8):
        raw, query, key, value = project(normed, *qkv_rows[i], cosine, sine, head_gains)
        raws.append(raw)
        queries.append(query)
        own_pairs.append((key, value))
    mixed_blocks, log_totals = [], []
    for i in range(8):
        key, value = own_pairs[i]
        key_before, value_before = (
            lax.ppermute(part, "rep", upward) for part in own_pairs[i ^ 1]
        )
        pairs = (key_before, key, value_before, value)
        mixed, log_total = attend(info, queries[i], *pairs)
        kept.append(pairs)
        mixed_blocks.append(mixed)
        log_totals.append(log_total)
    mixed = jnp.concatenate(mixed_blocks, 1)
    out_all = jnp.concatenate([jnp.concatenate(r, 0) for r in out_rows], 1)
    branch = jnp.einsum("rf,nf->rn", mixed, out_all, preferred_element_type=full)

    resid = x_rows + branch
    inverse_mid = lax.rsqrt(jnp.mean(resid * resid, -1, keepdims=True) + EPS)
    mid_unit = resid * inverse_mid
    mid = (mid_unit * mlp_gains).astype(low)
    mid_all = jnp.concatenate(plane_gather(mid), 0)
    grad_y_low = jnp.where(valid, grad_y_low, jnp.zeros_like(grad_y_low))
    grad_y_all = jnp.concatenate(plane_gather(grad_y_low), 0)
    act, grad_gate, grad_up = hidden_units(mid_all, grad_y_all, gate_all, up_all, down_all)

    def plane_total(lefts, rights):
        far = from_hidden(lefts, rights, 1, 3)
        own = from_hidden([after(left, far) for left in lefts], rights, 0, 1)
        return plane_sum(own.astype(full), jnp.split(far, 3, 0))

    grad_mid = plane_total((grad_gate, grad_up), (gate_all, up_all))
    mlp_out = plane_total((act,), (down_all,))
    output = from_sequences(jnp.where(valid, resid + mlp_out, 0.0).astype(low))

    others = [
        outer(left, right[:, units:]).astype(low)
        for left, right in ((grad_y_all, act), (mid_all, grad_gate), (mid_all, grad_up))
    ]
    owns = [
        (outer(left, right[:, :units]) + across(other, CORE)).astype(low)
        for (left, right), other in zip(
            ((grad_y_all, act), (mid_all, grad_gate), (mid_all, grad_up)), others
        )
    ]
    grad_mid = after(grad_mid, *owns)
    totals = [ring_sum(jnp.split(own, shards, 0), low).astype(low) for own in owns]
    (grad_down_total,), (grad_gate_total,), (grad_up_total,) = (
        spread_blocks(total, (units,)) for total in totals
    )

    mlp_gain_part = jnp.sum(mid_unit * grad_mid, 0)
    grad_resid = grad_y_low.astype(full) + norm_back(mid_unit, inverse_mid, grad_mid * mlp_gains)
    resid_low = grad_resid.astype(low)
    grad_mixed = jnp.dot(resid_low, out_all, preferred_element_type=full).astype(low)
    grad_blocks = [None] * 8
    query_gain_part, key_gain_part = 0.0, 0.0
    finish = vmem_call(
        finish_body,
        [
            jax.ShapeDtypeStruct((rows, 2 * pair_columns), low),
            jax.ShapeDtypeStruct((1, head_dim), full),
        ],
        rows * head_dim,
        specs={3: column_spec(rows, head_dim, 2)},
        name="finish",
    )
    order = (7, 6, 3, 2, 5, 4, 1, 0)
    backs = [None] * 8
    for i in order:
        attend_back = vmem_call(
            attend_back_body,
            [
                pair_rows,
                jax.ShapeDtypeStruct((rows, pair_columns), full),
                pair_rows,
                jax.ShapeDtypeStruct((1, head_dim), full),
            ],
            30 * rows * rows * pair_columns,
            scratch=[pltpu.VMEM((2 * rows, head_dim), full)] * 2,
            scalars=1,
            specs={
                7: column_spec(rows, pair_columns, i),
                8: column_spec(rows, pair_columns, 0),
            },
            name="attend_back",
        )
        backs[i] = attend_back(
            info, queries[i], *kept[i], log_totals[i], grad_mixed, raws[i], cosine, sine,
            query_gains,
        )
        query_gain_part += backs[i][3]
    for i in order:
        came = lax.ppermute(backs[i ^ 1][2], "rep", downward)
        grad_blocks[i], part = finish(
            backs[i][0], backs[i][1], came, raws[i], cosine, sine, key_gains
        )
        key_gain_part += part

    def block_totals(left, blocks):
        chips = [None] * 4
        for i in (3, 1, 2, 0):
            other = outer(left, blocks[2 * i + 1]).astype(low)
            chips[i] = outer(left, blocks[2 * i]) + across(other, CORE)
        own = plane_sum(chips[0], chips[1:])
        return ring_sum(jnp.split(own, shards, 0), low).astype(low)

    out_total = block_totals(resid_low, mixed_blocks)
    (grad_out_total,) = spread_blocks(out_total, (pair_columns,))
    qkv_total = block_totals(normed, grad_blocks)
    grad_query_total, grad_key_total, grad_value_total = spread_blocks(
        qkv_total, (pair_columns, head_dim, head_dim)
    )

    grad_qkv = jnp.concatenate(grad_blocks, 1)
    qkv_all = jnp.concatenate([jnp.concatenate(r, 0) for r in qkv_rows], 1)
    grad_in = jnp.einsum("rf,nf->rn", grad_qkv, qkv_all, preferred_element_type=full)
    grad_tokens = from_sequences(
        (grad_resid + norm_back(x_unit, inverse_in, grad_in * attn_gains)).astype(low)
    )
    attn_gain_part = jnp.sum(x_unit * grad_in, 0)

    parts = everywhere_sum(
        jnp.concatenate(
            [attn_gain_part, mlp_gain_part, query_gain_part[0], key_gain_part[0]]
        )
    )
    wide = parts[: 2 * width].reshape(2, shards, width // shards)
    wide = ring_sum([wide[:, i] for i in range(shards)], full)
    narrow = parts[2 * width :]
    for by in (1, 2):
        narrow = narrow + lax.ppermute(narrow, "shard", [(i, i ^ by) for i in range(shards)])
    return (
        output,
        grad_tokens,
        wide[0],
        grad_query_total,
        grad_key_total,
        grad_value_total,
        narrow[:head_dim],
        narrow[head_dim:],
        grad_out_total,
        wide[1],
        grad_gate_total,
        grad_up_total,
        grad_down_total,
    )


def solution(mesh):
    sizes = (mesh.shape["rep"], mesh.shape["shard"])
    return jax.shard_map(
        on_device_block if sizes == (8, 4) else on_device,
        mesh=mesh,
        in_specs=(
            P("rep", "shard", None),
            P("rep"),
            P("shard"),
            P("shard", None),
            P("shard", None),
            P("shard", None),
            P(),
            P(),
            P("shard", None),
            P("shard"),
            P("shard", None),
            P("shard", None),
            P("shard", None),
            P("rep", "shard", None),
        ),
        out_specs=(
            P("rep", "shard", None),
            P("rep", "shard", None),
            P("shard"),
            P("shard", None),
            P("shard", None),
            P("shard", None),
            P(),
            P(),
            P("shard", None),
            P("shard"),
            P("shard", None),
            P("shard", None),
            P("shard", None),
        ),
        check_vma=False,
    )
```

```python
import jax
import jax.numpy as jnp
from jax import lax
from jax.experimental import pallas as pl
from jax.experimental.pallas import tpu as pltpu
from jax.sharding import PartitionSpec as P

WINDOW = 512


EPS = 1e-06
ROPE_BASE = 1000000.0
NEG = -1e30


def passed_along(x, axis, by):
    devices = lax.axis_size(axis)
    pairs = [(i, i + by) for i in range(devices) if 0 <= i + by < devices]
    return lax.ppermute(x, axis, pairs)


def tables(positions, head_dim):
    half = head_dim // 2
    freq = ROPE_BASE ** (-jnp.arange(half, dtype=jnp.float32) * 2.0 / head_dim)
    angle = positions.astype(jnp.float32)[:, None] * freq[None, :]
    angle = jnp.concatenate([angle, angle], -1)
    return (jnp.cos(angle)[None, :, None, :], jnp.sin(angle)[None, :, None, :])


def rotated_rows(value_rows):
    half = value_rows.shape[-1] // 2
    return jnp.concatenate([-value_rows[..., half:], value_rows[..., :half]], -1)


def head_norm(raw, gain):
    inverse = lax.rsqrt(jnp.mean(raw * raw, -1, keepdims=True) + EPS)
    unit = raw * inverse
    return (unit, inverse, unit * gain)


def norm_back(unit, inverse, grad_unit):
    return inverse * (grad_unit - unit * jnp.mean(grad_unit * unit, -1, keepdims=True))


def head_norm_back(unit, inverse, grad_normed, gain):
    grad_raw = norm_back(unit, inverse, grad_normed * gain)
    return (grad_raw, jnp.sum(unit * grad_normed, axis=(0, 1, 2)))


def scores(query_rows, keys, allowed, scale):
    raw = (
        jnp.einsum("sqhgd,skhd->shgqk", query_rows, keys, preferred_element_type=jnp.float32)
        * scale
    )
    return jnp.where(allowed[:, None, None], raw, NEG)


def outer(left, right):
    return jnp.einsum("rc,rf->cf", left, right, preferred_element_type=jnp.float32)


def on_device(
    tokens,
    lengths,
    attn_gain,
    w_query,
    key_matrix,
    value_matrix,
    query_gain,
    key_gain,
    w_out,
    mlp_gain,
    w_gate,
    w_up,
    w_down,
    cotangent,
):
    seq_count, piece, width = tokens.shape
    head_dim = query_gain.shape[0]
    heads_q = w_query.shape[1] // head_dim
    heads_kv = key_matrix.shape[1] // head_dim
    groups = heads_q // heads_kv
    rows = seq_count * piece
    scale = head_dim ** (-0.5)
    reach = (WINDOW + piece - 2) // piece
    owned = width // lax.axis_size("shard")
    shard_at = lax.axis_index("shard")
    query_pos = shard_at * piece + jnp.arange(piece, dtype=jnp.int32)
    key_pos = (shard_at - reach) * piece + jnp.arange((reach + 1) * piece, dtype=jnp.int32)
    near = (
        (key_pos[None, :] <= query_pos[:, None])
        & (query_pos[:, None] - key_pos[None, :] < WINDOW)
        & (key_pos[None, :] >= 0)
    )
    live = (key_pos[None, None, :] < lengths[:, None, None]) | (
        key_pos[None, :] == query_pos[:, None]
    )[None]
    allowed = near[None] & live
    valid = (query_pos[None, :] < lengths[:, None]).astype(jnp.float32).reshape(rows, 1)
    cosine_table, sine_table = tables(query_pos, head_dim)
    x_rows = tokens.astype(jnp.float32).reshape(rows, width)
    inverse_in = lax.rsqrt(jnp.mean(x_rows * x_rows, -1, keepdims=True) + EPS)
    x_unit = x_rows * inverse_in
    gain_piece = lax.all_gather(attn_gain, "shard", axis=0, tiled=True)
    query_piece = lax.all_gather(w_query, "shard", axis=0, tiled=True)
    key_piece = lax.all_gather(key_matrix, "shard", axis=0, tiled=True)
    value_piece = lax.all_gather(value_matrix, "shard", axis=0, tiled=True)
    normed_piece = (x_unit * gain_piece.astype(jnp.float32)).astype(jnp.bfloat16)
    acc_q = jnp.dot(normed_piece, query_piece, preferred_element_type=jnp.float32)
    acc_k = jnp.dot(normed_piece, key_piece, preferred_element_type=jnp.float32)
    acc_v = jnp.dot(normed_piece, value_piece, preferred_element_type=jnp.float32)
    normalized_rows = normed_piece
    gains = gain_piece.astype(jnp.float32)
    attn_in = normalized_rows
    attn_gains = gains
    query_unit, query_inverse, query_rows_normalized = head_norm(
        acc_q.reshape(seq_count, piece, heads_q, head_dim), query_gain.astype(jnp.float32)
    )
    key_unit, key_inverse, key_normed = head_norm(
        acc_k.reshape(seq_count, piece, heads_kv, head_dim), key_gain.astype(jnp.float32)
    )
    query_rows = (
        (query_rows_normalized * cosine_table + rotated_rows(query_rows_normalized) * sine_table)
        .astype(jnp.bfloat16)
        .reshape(seq_count, piece, heads_kv, groups, head_dim)
    )
    keys_own = (key_normed * cosine_table + rotated_rows(key_normed) * sine_table).astype(
        jnp.bfloat16
    )
    values_own = acc_v.reshape(seq_count, piece, heads_kv, head_dim).astype(jnp.bfloat16)
    own_pair = jnp.stack([keys_own, values_own])
    parts = []
    for fetch_back in range(reach, 0, -1):
        parts.append(passed_along(own_pair, "shard", fetch_back))
    parts.append(own_pair)
    near_pair = jnp.concatenate(parts, 2)
    score = scores(query_rows, near_pair[0], allowed, scale)
    top = jnp.max(score, -1, keepdims=True)
    expo = jnp.exp(score - top)
    total = jnp.sum(expo, -1, keepdims=True)
    prob = expo / total
    log_total = top + jnp.log(total)
    mixed = jnp.einsum(
        "shgqk,skhd->sqhgd",
        prob.astype(jnp.bfloat16),
        near_pair[1],
        preferred_element_type=jnp.float32,
    )
    mixed_rows = mixed.reshape(rows, heads_q * head_dim).astype(jnp.bfloat16)
    resid = x_rows + jnp.einsum(
        "rf,nf->rn",
        mixed_rows,
        lax.all_gather(w_out, "shard", axis=0, tiled=True),
        preferred_element_type=jnp.float32,
    )
    inverse_mid = lax.rsqrt(jnp.mean(resid * resid, -1, keepdims=True) + EPS)
    mid_unit = resid * inverse_mid
    gain_piece = lax.all_gather(mlp_gain, "shard", axis=0, tiled=True)
    gate_piece = lax.all_gather(w_gate, "shard", axis=0, tiled=True)
    up_piece = lax.all_gather(w_up, "shard", axis=0, tiled=True)
    normed_piece = (mid_unit * gain_piece.astype(jnp.float32)).astype(jnp.bfloat16)
    acc_gate = jnp.dot(normed_piece, gate_piece, preferred_element_type=jnp.float32)
    acc_up = jnp.dot(normed_piece, up_piece, preferred_element_type=jnp.float32)
    normalized_rows = normed_piece
    gains = gain_piece.astype(jnp.float32)
    mlp_in = normalized_rows
    sigma = jax.nn.sigmoid(acc_gate)
    swish = acc_gate * sigma
    act = (swish * acc_up).astype(jnp.bfloat16)
    mlp_out = jnp.einsum(
        "rf,nf->rn",
        act,
        lax.all_gather(w_down, "shard", axis=0, tiled=True),
        preferred_element_type=jnp.float32,
    )
    output = (valid * (resid + mlp_out)).astype(jnp.bfloat16).reshape(seq_count, piece, width)
    grad_y = cotangent.astype(jnp.float32).reshape(rows, width) * valid
    grad_y_low = grad_y.astype(jnp.bfloat16)
    grad_act = jnp.dot(
        grad_y_low,
        lax.all_gather(w_down, "shard", axis=0, tiled=True),
        preferred_element_type=jnp.float32,
    )
    grad_gate = (grad_act * acc_up * sigma * (1.0 + acc_gate * (1.0 - sigma))).astype(jnp.bfloat16)
    grad_up = (grad_act * swish).astype(jnp.bfloat16)
    gate_piece, up_piece = lax.all_gather((w_gate, w_up), "shard", axis=0, tiled=True)
    grad_mid = jnp.einsum(
        "rf,nf->rn", grad_gate, gate_piece, preferred_element_type=jnp.float32
    ) + jnp.einsum("rf,nf->rn", grad_up, up_piece, preferred_element_type=jnp.float32)
    grad_resid = grad_y + norm_back(mid_unit, inverse_mid, grad_mid * gains)
    mlp_gain_part = jnp.sum(mid_unit * grad_mid, 0)
    normalized_rows = mlp_in
    mlp_grads = jax.tree.map(
        lambda part: lax.psum_scatter(
            part.astype(jnp.bfloat16), "shard", scatter_dimension=0, tiled=True
        ).astype(jnp.float32),
        (
            outer(normalized_rows, grad_gate),
            outer(normalized_rows, grad_up),
            outer(grad_y_low, act),
        ),
    )
    resid_low = grad_resid.astype(jnp.bfloat16)
    grad_mixed = jnp.dot(
        resid_low,
        lax.all_gather(w_out, "shard", axis=0, tiled=True),
        preferred_element_type=jnp.float32,
    )
    grad_mixed = grad_mixed.astype(jnp.bfloat16).reshape(
        seq_count, piece, heads_kv, groups, head_dim
    )
    prob_again = jnp.exp(scores(query_rows, near_pair[0], allowed, scale) - log_total)
    grad_prob = jnp.einsum(
        "sqhgd,skhd->shgqk", grad_mixed, near_pair[1], preferred_element_type=jnp.float32
    )
    grad_values = jnp.einsum(
        "shgqk,sqhgd->skhd",
        prob_again.astype(jnp.bfloat16),
        grad_mixed,
        preferred_element_type=jnp.float32,
    )
    grad_score = (
        prob_again * (grad_prob - jnp.sum(prob_again * grad_prob, -1, keepdims=True))
    ).astype(jnp.bfloat16)
    grad_queries = (
        jnp.einsum(
            "shgqk,skhd->sqhgd", grad_score, near_pair[0], preferred_element_type=jnp.float32
        )
        * scale
    )
    grad_keys = (
        jnp.einsum("shgqk,sqhgd->skhd", grad_score, query_rows, preferred_element_type=jnp.float32)
        * scale
    )
    grad_pair = jnp.stack([grad_keys, grad_values])
    own_grad = grad_pair[:, :, reach * piece :]
    for back in range(1, reach + 1):
        lower = (reach - back) * piece
        own_grad = own_grad + passed_along(grad_pair[:, :, lower : lower + piece], "shard", -back)
    grad_query_post = grad_queries.reshape(seq_count, piece, heads_q, head_dim)
    grad_query_normed = grad_query_post * cosine_table - rotated_rows(grad_query_post * sine_table)
    grad_key_normed = own_grad[0] * cosine_table - rotated_rows(own_grad[0] * sine_table)
    grad_query_raw, query_gain_grad = head_norm_back(
        query_unit, query_inverse, grad_query_normed, query_gain.astype(jnp.float32)
    )
    grad_key_raw, key_gain_grad = head_norm_back(
        key_unit, key_inverse, grad_key_normed, key_gain.astype(jnp.float32)
    )
    grad_query_low = grad_query_raw.reshape(rows, heads_q * head_dim).astype(jnp.bfloat16)
    grad_key_low = grad_key_raw.reshape(rows, heads_kv * head_dim).astype(jnp.bfloat16)
    grad_value_low = own_grad[1].reshape(rows, heads_kv * head_dim).astype(jnp.bfloat16)
    query_piece, key_piece, value_piece = lax.all_gather(
        (w_query, key_matrix, value_matrix), "shard", axis=0, tiled=True
    )
    grad_in = (
        jnp.einsum("rf,nf->rn", grad_query_low, query_piece, preferred_element_type=jnp.float32)
        + jnp.einsum("rf,nf->rn", grad_key_low, key_piece, preferred_element_type=jnp.float32)
        + jnp.einsum("rf,nf->rn", grad_value_low, value_piece, preferred_element_type=jnp.float32)
    )
    grad_tokens = (
        (grad_resid + norm_back(x_unit, inverse_in, grad_in * attn_gains))
        .astype(jnp.bfloat16)
        .reshape(seq_count, piece, width)
    )
    attn_gain_part = jnp.sum(x_unit * grad_in, 0)
    normalized_rows = attn_in
    attn_grads = jax.tree.map(
        lambda part: lax.psum_scatter(
            part.astype(jnp.bfloat16), "shard", scatter_dimension=0, tiled=True
        ).astype(jnp.float32),
        (
            outer(normalized_rows, grad_query_low),
            outer(normalized_rows, grad_key_low),
            outer(normalized_rows, grad_value_low),
            outer(resid_low, mixed_rows),
        ),
    )
    head_grads = lax.psum(
        (query_gain_grad, key_gain_grad, attn_gain_part, mlp_gain_part), ("rep", "shard")
    )
    attn_gain_total = lax.dynamic_slice_in_dim(head_grads[2], shard_at * owned, owned, 0)
    mlp_gain_total = lax.dynamic_slice_in_dim(head_grads[3], shard_at * owned, owned, 0)
    summed = (
        lax.psum(attn_grads[0].astype(jnp.bfloat16), "rep").astype(jnp.float32),
        lax.psum(attn_grads[1].astype(jnp.bfloat16), "rep").astype(jnp.float32),
        lax.psum(attn_grads[2].astype(jnp.bfloat16), "rep").astype(jnp.float32),
        lax.psum(attn_grads[3].astype(jnp.bfloat16), "rep").astype(jnp.float32),
        lax.psum(mlp_grads[0].astype(jnp.bfloat16), "rep").astype(jnp.float32),
        lax.psum(mlp_grads[1].astype(jnp.bfloat16), "rep").astype(jnp.float32),
        lax.psum(mlp_grads[2].astype(jnp.bfloat16), "rep").astype(jnp.float32),
    )
    attn_grads = summed[:4]
    mlp_grads = summed[4:]
    return (
        output,
        grad_tokens,
        attn_gain_total,
        attn_grads[0],
        attn_grads[1],
        attn_grads[2],
        head_grads[0],
        head_grads[1],
        attn_grads[3],
        mlp_gain_total,
        mlp_grads[0],
        mlp_grads[1],
        mlp_grads[2],
    )


CORE, ACROSS_X, ACROSS_Y = 1, 2, 4
VMEM_BYTES = 56 * 2**20


def across(x, mask):
    count = lax.axis_size("rep")
    return lax.ppermute(x, "rep", [(i, i ^ mask) for i in range(count)])


def around(x, by):
    count = lax.axis_size("shard")
    return lax.ppermute(x, "shard", [(i, (i + by) % count) for i in range(count)])


def after(x, *done):
    return lax.optimization_barrier((x, *done))[0]


def ring_gather(x):
    before, behind = around(x, 1), around(x, -1)
    return [x, before, around(before, 1), behind]


def ring_sum(chunks, kind):
    last = chunks[3] + around(chunks[2].astype(kind), 1)
    return chunks[0] + around(chunks[1].astype(kind), -1) + around(last.astype(kind), 1)


def plane_gather(piece):
    half = piece.shape[0] // 2
    from_x = across(piece, ACROSS_X)
    from_y = across(piece, ACROSS_Y)
    far = [across(from_x[:half], ACROSS_Y), across(from_y[half:], ACROSS_X)]
    return [piece, from_x, from_y, jnp.concatenate(far, 0)]


def plane_sum(own_head, own_tail, to_x, to_y, two_head, one_tail):
    low = jnp.bfloat16
    from_x, from_y = across(to_x, ACROSS_X), across(to_y, ACROSS_Y)
    half = own_head.shape[0]
    two_head = two_head + from_x[half:]
    one_tail = one_tail + from_y[half:]
    own_head = own_head + from_x[:half] + across(two_head.astype(low), ACROSS_Y)
    own_tail = own_tail + from_y[:half] + across(one_tail.astype(low), ACROSS_X)
    return own_head, own_tail


def sequence_pairs(turn):
    groups, shards = lax.axis_size("rep"), lax.axis_size("shard")
    pairs = []
    for group in range(groups):
        chip, core = divmod(group, 2)
        for at in range(shards):
            to_group, to_shard = 2 * chip + at // 2, 2 * core + (turn ^ (at & 1))
            pairs.append((group * shards + at, to_group * shards + to_shard))
    return pairs


def rolled(x):
    count, at = lax.axis_size("shard"), lax.axis_index("shard")
    width = x.shape[1] // count
    return jnp.concatenate(
        [lax.dynamic_slice_in_dim(x, ((at - i) % count) * width, width, 1) for i in range(count)],
        1,
    )


def to_sequences(x):
    odd = lax.axis_index("shard") & 1
    came = [
        lax.ppermute(
            lax.dynamic_index_in_dim(x, turn ^ odd, 0, keepdims=False),
            ("rep", "shard"),
            sequence_pairs(turn),
        )
        for turn in range(2)
    ]
    even = odd == 0
    return jnp.concatenate(
        [jnp.where(even, came[0], came[1]), jnp.where(even, came[1], came[0])], 0
    )


def from_sequences(x):
    odd = lax.axis_index("shard") & 1
    x = x.reshape(2, x.shape[0] // 2, x.shape[1])
    came = [
        lax.ppermute(
            lax.dynamic_index_in_dim(x, turn ^ odd, 0, keepdims=False),
            ("rep", "shard"),
            [(to, at) for at, to in sequence_pairs(turn)],
        )
        for turn in range(2)
    ]
    even = odd == 0
    return jnp.stack([jnp.where(even, came[0], came[1]), jnp.where(even, came[1], came[0])])


def column_block(weights, at):
    cuts = [w.shape[1] // 8 for w in weights]
    return jnp.concatenate(
        [lax.dynamic_slice_in_dim(w, at * cut, cut, 1) for w, cut in zip(weights, cuts)], 1
    )


def spread_blocks(block):
    own = jnp.concatenate(plane_gather(block), 0)
    return own, across(own, CORE)


def whole_body(me, own, other, out):
    mine = (me[0] ^ pl.program_id(0)) & 1 == 0

    @pl.when(mine)
    def _():
        out[...] = own[...].astype(jnp.float32)

    @pl.when(jnp.logical_not(mine))
    def _():
        out[...] = other[...].astype(jnp.float32)


def whole_columns(me, own, other, first, width):
    rows = own.shape[0] // 4
    spec = pl.BlockSpec((rows, width), lambda i, at: ((at[0] ^ i) >> 1, first // width))
    return pl.pallas_call(
        whole_body,
        grid_spec=pltpu.PrefetchScalarGridSpec(
            num_scalar_prefetch=1,
            grid=(8,),
            in_specs=[spec, spec],
            out_specs=pl.BlockSpec((rows, width), lambda i, at: (0, i)),
        ),
        out_shape=jax.ShapeDtypeStruct((rows, 8 * width), jnp.float32),
        compiler_params=pltpu.CompilerParams(vmem_limit_bytes=VMEM_BYTES),
        cost_estimate=pl.CostEstimate(
            flops=rows * 8 * width, bytes_accessed=48 * rows * width, transcendentals=0
        ),
        name="whole_columns",
    )(me, own, other)


def everywhere_sum(x):
    for mask in (CORE, ACROSS_X, ACROSS_Y):
        x = x + across(x, mask)
    return x


def turned(x):
    return pltpu.roll(x, x.shape[-1] // 2, x.ndim - 1)


def nt(left, right):
    return lax.dot_general(
        left, right, (((1,), (1,)), ((), ())), preferred_element_type=jnp.float32
    )


def tn(left, right):
    return lax.dot_general(
        left, right, (((0,), (0,)), ((), ())), preferred_element_type=jnp.float32
    )


def unit_of(raw):
    inverse = lax.rsqrt(jnp.mean(raw * raw, -1, keepdims=True) + EPS)
    return raw * inverse, inverse


def project_body(
    normed, own0, side0, far0, own1, side1, far1, cosine, sine, gains, raw, query, key_value
):
    step = own0.shape[0]
    dim = cosine.shape[1]
    for block, (own, side, far) in enumerate(((own0, side0, far0), (own1, side1, far1))):
        at = block * 4 * dim
        raw[:, at : at + 4 * dim] = (
            jnp.dot(normed[:, :step], own[...], preferred_element_type=jnp.float32)
            + jnp.dot(
                normed[:, step : 2 * step], side[:step], preferred_element_type=jnp.float32
            )
            + jnp.dot(
                normed[:, 2 * step : 3 * step], far[...], preferred_element_type=jnp.float32
            )
            + jnp.dot(normed[:, 3 * step :], side[step:], preferred_element_type=jnp.float32)
        )
        for i in range(3):
            unit, _ = unit_of(raw[:, at + i * dim : at + (i + 1) * dim])
            head = unit * gains[i // 2 : i // 2 + 1, :]
            head = (head * cosine[...] + turned(head) * sine[...]).astype(jnp.bfloat16)
            if i < 2:
                query[:, (2 * block + i) * dim : (2 * block + i + 1) * dim] = head
            else:
                key_value[:, 2 * block * dim : (2 * block + 1) * dim] = head
        key_value[:, (2 * block + 1) * dim : (2 * block + 2) * dim] = raw[
            :, at + 3 * dim : at + 4 * dim
        ].astype(jnp.bfloat16)


def window_scores(info, query, keys, part, scale):
    rows, columns = query.shape[0], keys.shape[0]
    half = columns - rows
    row = lax.broadcasted_iota(jnp.int32, (rows, columns), 0)
    column = lax.broadcasted_iota(jnp.int32, (rows, columns), 1)
    gap = column - row - half
    slot = column + ((info[0] - 1) * half + part * rows)
    allowed = (gap <= 0) & (gap > -half) & (slot >= 0) & ((slot < info[1]) | (gap == 0))
    return nt(query, keys) * scale, allowed


def key_columns(block, dim):
    key = slice(2 * block * dim, (2 * block + 1) * dim)
    value = slice((2 * block + 1) * dim, (2 * block + 2) * dim)
    return key, value


def seen_pair(before, own, part, block, dim):
    here, there = key_columns(block, dim), key_columns(1 - block, dim)
    rows = own.shape[0] // 2
    if part == 0:
        return [
            jnp.concatenate([before[:, t], own[:rows, h]], 0) for h, t in zip(here, there)
        ]
    return [jnp.concatenate([before[rows:, t], own[:, h]], 0) for h, t in zip(here, there)]


def attend_body(info, query, before, own, mixed, log_total):
    dim = own.shape[1] // 4
    rows = query.shape[0] // 2
    for part in range(2):
        at = slice(part * rows, (part + 1) * rows)
        for block in range(2):
            keys, values = seen_pair(before, own, part, block, dim)
            for head in (2 * block, 2 * block + 1):
                on = slice(head * dim, (head + 1) * dim)
                score, allowed = window_scores(info, query[at, on], keys, part, dim**-0.5)
                score = jnp.where(allowed, score, NEG)
                top = jnp.max(score, -1, keepdims=True)
                expo = jnp.exp(score - top)
                total = jnp.sum(expo, -1, keepdims=True)
                prob = (expo * (1.0 / total)).astype(jnp.bfloat16)
                mixed[at, on] = jnp.dot(
                    prob, values, preferred_element_type=jnp.float32
                ).astype(jnp.bfloat16)
                log_total[at, on] = jnp.broadcast_to(top + jnp.log(total), (rows, dim))


def attend_back_body(
    info, query, before, own, log_total, grad_mixed, raw, cosine, sine, gain,
    grad_query, grad_own, grad_before, gain_part, grad_keys, grad_values,
):
    dim = own.shape[1] // 4
    rows = query.shape[0] // 2
    scale = dim**-0.5
    gain_total = jnp.zeros((1, dim), jnp.float32)
    for block in range(2):
        grad_keys[...] = jnp.zeros_like(grad_keys)
        grad_values[...] = jnp.zeros_like(grad_values)
        for part in range(2):
            keys, values = seen_pair(before, own, part, block, dim)
            at = slice(part * rows, (part + 1) * rows)
            seen = slice(part * rows, part * rows + keys.shape[0])
            for head in (2 * block, 2 * block + 1):
                on = slice(head * dim, (head + 1) * dim)
                score, allowed = window_scores(info, query[at, on], keys, part, scale)
                prob = jnp.where(allowed, jnp.exp(score - log_total[at, on][:, :1]), 0.0)
                grad_prob = nt(grad_mixed[at, on], values)
                inner = jnp.sum(prob * grad_prob, -1, keepdims=True)
                grad_score = (prob * (grad_prob - inner)).astype(jnp.bfloat16)
                grad_values[seen, :] += tn(prob.astype(jnp.bfloat16), grad_mixed[at, on])
                grad_keys[seen, :] += tn(grad_score, query[at, on]) * scale
                back = jnp.dot(grad_score, keys, preferred_element_type=jnp.float32) * scale
                back = back * cosine[at, :] - turned(back) * sine[at, :]
                there = (2 * head - head % 2) * dim
                unit, inverse = unit_of(raw[at, there : there + dim])
                gain_total += jnp.sum(unit * back, 0, keepdims=True)
                back = back * gain[...]
                back = inverse * (back - unit * jnp.mean(back * unit, -1, keepdims=True))
                grad_query[at, on] = back.astype(jnp.bfloat16)
        for grad, here, there in zip(
            (grad_keys, grad_values), key_columns(block, dim), key_columns(1 - block, dim)
        ):
            grad_before[:, there] = grad[: 2 * rows, :].astype(jnp.bfloat16)
            grad_own[:, here] = grad[2 * rows :, :]
    gain_part[...] = gain_total


def finish_body(grad_query, grad_own, came, raw, cosine, sine, gain, even, odd, gain_part):
    dim = cosine.shape[1]
    total = jnp.zeros((1, dim), jnp.float32)
    for block, out in enumerate((even, odd)):
        key, value = key_columns(block, dim)
        back = grad_own[:, key] + came[:, key].astype(jnp.float32)
        back = back * cosine[...] - turned(back) * sine[...]
        unit, inverse = unit_of(raw[:, (4 * block + 2) * dim : (4 * block + 3) * dim])
        total += jnp.sum(unit * back, 0, keepdims=True)
        back = back * gain[...]
        back = inverse * (back - unit * jnp.mean(back * unit, -1, keepdims=True))
        out[:, : 2 * dim] = grad_query[:, 2 * block * dim : (2 * block + 2) * dim]
        out[:, 2 * dim : 3 * dim] = back.astype(jnp.bfloat16)
        grad_value = grad_own[:, value] + came[:, value].astype(jnp.float32)
        out[:, 3 * dim :] = grad_value.astype(jnp.bfloat16)
    gain_part[...] = total


def vmem_call(body, outs, flops, scratch=(), scalars=0, specs=None, name=None):
    def call(*args):
        in_specs = [
            pl.BlockSpec(memory_space=pltpu.SMEM if i < scalars else pltpu.VMEM)
            for i in range(len(args))
        ]
        for at, spec in (specs or {}).items():
            in_specs[at] = spec
        return pl.pallas_call(
            body,
            grid=(1,),
            out_shape=outs,
            in_specs=in_specs,
            out_specs=jax.tree.map(lambda _: pl.BlockSpec(memory_space=pltpu.VMEM), outs),
            scratch_shapes=scratch,
            compiler_params=pltpu.CompilerParams(vmem_limit_bytes=VMEM_BYTES),
            cost_estimate=pl.CostEstimate(
                flops=flops,
                bytes_accessed=sum(a.size * a.dtype.itemsize for a in args),
                transcendentals=0,
            ),
            name=name,
        )(*args)

    return call


def column_spec(rows, columns, at):
    return pl.BlockSpec((rows, columns), lambda i: (0, at))


def hidden_body(mid, grad_y, gate_w, up_w, down_w, act, grad_gate, grad_up):
    gate = jnp.dot(mid[...], gate_w[...], preferred_element_type=jnp.float32)
    up = jnp.dot(mid[...], up_w[...], preferred_element_type=jnp.float32)
    grad_act = jnp.dot(grad_y[...], down_w[...], preferred_element_type=jnp.float32)
    sigma = jax.nn.sigmoid(gate)
    swish = gate * sigma
    act[...] = (swish * up).astype(jnp.bfloat16)
    grad_gate[...] = (grad_act * up * sigma * (1.0 + gate * (1.0 - sigma))).astype(jnp.bfloat16)
    grad_up[...] = (grad_act * swish).astype(jnp.bfloat16)


def hidden_units(mid, grad_y, gate_up_w, down_w):
    rows, width = mid.shape
    units = down_w.shape[1]
    high, cut = rows // 2, units // 3
    row_spec = pl.BlockSpec((high, width), lambda i, j: (i, 0))
    out_spec = pl.BlockSpec((high, cut), lambda i, j: (i, j))
    return pl.pallas_call(
        hidden_body,
        grid=(2, 3),
        out_shape=[jax.ShapeDtypeStruct((rows, units), jnp.bfloat16)] * 3,
        in_specs=[
            row_spec,
            row_spec,
            pl.BlockSpec((width, cut), lambda i, j: (0, j)),
            pl.BlockSpec((width, cut), lambda i, j: (0, j + 3)),
            pl.BlockSpec((width, cut), lambda i, j: (0, j)),
        ],
        out_specs=[out_spec] * 3,
        compiler_params=pltpu.CompilerParams(vmem_limit_bytes=VMEM_BYTES),
        cost_estimate=pl.CostEstimate(
            flops=6 * rows * width * units, bytes_accessed=10 * rows * width, transcendentals=0
        ),
        name="hidden_units",
    )(mid, grad_y, gate_up_w, gate_up_w, down_w)


def from_hidden(pairs, first, step):
    count = len(pairs)
    rows, units = pairs[0][0].shape[0] // 8, pairs[0][0].shape[1]
    width = pairs[0][1].shape[0]
    cut = width // 4

    def body(*refs):
        refs, out = refs[:-1], refs[-1]
        out[...] = sum(
            nt(
                jnp.concatenate([refs[3 * i][...], refs[3 * i + 1][...]], 0),
                refs[3 * i + 2][...],
            )
            for i in range(count)
        ).astype(jnp.bfloat16)

    specs, args = [], []
    for left, right, at in pairs:
        specs += [
            pl.BlockSpec((rows, units), lambda j: (first, 0)),
            pl.BlockSpec((rows, units), lambda j: (first + step, 0)),
            pl.BlockSpec((cut, units), lambda j, at=at: (j, at)),
        ]
        args += [left, left, right]
    return pl.pallas_call(
        body,
        grid=(4,),
        out_shape=jax.ShapeDtypeStruct((2 * rows, width), jnp.bfloat16),
        in_specs=specs,
        out_specs=pl.BlockSpec((2 * rows, cut), lambda j: (0, j)),
        compiler_params=pltpu.CompilerParams(vmem_limit_bytes=VMEM_BYTES),
        cost_estimate=pl.CostEstimate(
            flops=4 * count * rows * width * units,
            bytes_accessed=2 * count * width * units,
            transcendentals=0,
        ),
        name="from_hidden",
    )(*args)


def on_device_block(
    tokens,
    lengths,
    attn_gain,
    w_query,
    key_matrix,
    value_matrix,
    query_gain,
    key_gain,
    w_out,
    mlp_gain,
    w_gate,
    w_up,
    w_down,
    cotangent,
):
    low, full = jnp.bfloat16, jnp.float32
    width = tokens.shape[2]
    head_dim = query_gain.shape[0]
    shards = lax.axis_size("shard")
    shard_at = lax.axis_index("shard")
    me = lax.axis_index("rep")
    core = me & 1
    count = lax.axis_size("rep")

    own_blocks = [
        column_block((w_query, key_matrix, value_matrix), me ^ i) for i in range(8)
    ]
    before, behind = around(own_blocks[0], 1), around(own_blocks[0], -1)
    x_low = to_sequences(after(tokens, before, behind))
    rows = x_low.shape[0]
    far = around(before, 1)
    side_blocks = plane_gather(jnp.concatenate([before, behind], 0))
    far_blocks = plane_gather(far)
    other_side = [across(block, CORE) for block in side_blocks]
    other_far = [across(block, CORE) for block in far_blocks]
    qkv_refs = [
        (
            own_blocks[2 * i], side_blocks[i], far_blocks[i],
            own_blocks[2 * i + 1], other_side[i], other_far[i],
        )
        for i in range(4)
    ]
    out_own = lax.all_gather(
        after(column_block((w_out,), me), far), "shard", axis=0, tiled=True
    )
    gain_parts = jnp.stack([attn_gain, mlp_gain])
    gains = jnp.concatenate(
        [gain_parts, *(around(gain_parts, by) for by in (1, 2, 3))], 1
    ).astype(full)
    gains = rolled(gains)
    attn_gains, mlp_gains = gains[:1], gains[1:]
    query_gains = query_gain.astype(full)[None]
    key_gains = key_gain.astype(full)[None]

    other_lengths = across(lengths, CORE)
    both = jnp.where(
        core == 0,
        jnp.concatenate([lengths, other_lengths]),
        jnp.concatenate([other_lengths, lengths]),
    )
    length = lax.dynamic_index_in_dim(both, shard_at, 0, keepdims=False)
    info = jnp.stack([core, length]).astype(jnp.int32)
    query_pos = core * rows + jnp.arange(rows, dtype=jnp.int32)
    valid = (query_pos < length)[:, None]
    cosine, sine = tables(query_pos, head_dim)
    cosine, sine = cosine[0, :, 0], sine[0, :, 0]
    sine = jnp.concatenate([-sine[:, : head_dim // 2], sine[:, head_dim // 2 :]], 1)

    gate_up_own = lax.all_gather(
        after(column_block((w_gate, w_up), me), out_own), "shard", axis=0, tiled=True
    )
    down_own = lax.all_gather(
        after(column_block((w_down,), me), gate_up_own), "shard", axis=0, tiled=True
    )
    out_chips = plane_gather(after(out_own, *far_blocks))
    out_blocks = [block for chip in out_chips for block in (chip, across(chip, CORE))]
    grad_y_low = to_sequences(after(cotangent, out_own))
    gate_up = [gate_up_own, across(gate_up_own, CORE)]
    down = [down_own, across(down_own, CORE)]
    units = down_own.shape[1]

    x_rows = x_low.astype(full)
    inverse_in = lax.rsqrt(jnp.mean(x_rows * x_rows, -1, keepdims=True) + EPS)
    x_unit = x_rows * inverse_in
    normed = rolled((x_unit * attn_gains).astype(low))
    head_columns = 2 * head_dim
    block_columns = 4 * head_dim
    quad_rows = jax.ShapeDtypeStruct((rows, block_columns), low)
    project = vmem_call(
        project_body,
        [jax.ShapeDtypeStruct((rows, 2 * block_columns), full), quad_rows, quad_rows],
        4 * rows * width * block_columns,
        name="project",
    )
    attend = vmem_call(
        attend_body,
        [quad_rows, jax.ShapeDtypeStruct((rows, block_columns), full)],
        12 * rows * rows * block_columns,
        scalars=1,
        name="attend",
    )
    head_gains = jnp.concatenate([query_gains, key_gains], 0)
    upward = [(i, i + 1) for i in range(0, count, 2)]
    downward = [(i + 1, i) for i in range(0, count, 2)]
    projected = [project(normed, *qkv_refs[i], cosine, sine, head_gains) for i in range(4)]
    earlier = [lax.ppermute(p[2], "rep", upward) for p in projected]
    attended = [
        attend(info, projected[i][1], earlier[i], projected[i][2]) for i in range(4)
    ]
    mixed = jnp.concatenate([a[0] for a in attended], 1)
    out_all = jnp.concatenate(out_blocks, 1)
    branch = jnp.einsum("rf,nf->rn", mixed, out_all, preferred_element_type=full)

    resid = x_rows + branch
    inverse_mid = lax.rsqrt(jnp.mean(resid * resid, -1, keepdims=True) + EPS)
    mid_unit = resid * inverse_mid
    mid = (mid_unit * mlp_gains).astype(low)
    mid_all = jnp.concatenate(plane_gather(mid), 0)
    grad_y_low = jnp.where(valid, grad_y_low, jnp.zeros_like(grad_y_low))
    grad_y_all = jnp.concatenate(plane_gather(grad_y_low), 0)
    hidden = [hidden_units(mid_all, grad_y_all, gate_up[i], down[i]) for i in range(2)]

    def plane_total(pairs, first=()):
        def some(at, step, *done):
            left = after(pairs[0][0], *done) if done else pairs[0][0]
            return from_hidden([(left, *pairs[0][1:]), *pairs[1:]], at, step)

        to_x = some(2, 4, *first)
        to_y = some(5, 2, to_x)
        rest = some(3, 1, to_y)
        own = some(0, 1, rest)
        half = own.shape[0] // 2
        parts = plane_sum(
            own[:half].astype(full), own[half:].astype(full), to_x, to_y,
            rest[half:].astype(full), rest[:half].astype(full),
        )
        return jnp.concatenate(parts, 0)

    grad_mid = plane_total(
        [(hidden[i][1 + j], gate_up[i], j) for i in range(2) for j in range(2)]
    )
    others, owns = [], []
    for i, left in ((0, grad_y_all), (1, mid_all), (2, mid_all)):
        others.append(outer(left, hidden[1][i]).astype(low))
    for i, left in ((0, grad_y_all), (1, mid_all), (2, mid_all)):
        owns.append((outer(left, hidden[0][i]) + across(others[i], CORE)).astype(low))
    totals = [
        lax.psum_scatter(own, "shard", scatter_dimension=0, tiled=True) for own in owns
    ]
    grad_mid = after(grad_mid, *owns)
    mlp_out = plane_total([(hidden[i][0], down[i], 0) for i in range(2)], (grad_mid,))
    output = from_sequences(jnp.where(valid, resid + mlp_out, 0.0).astype(low))
    my_group = me.astype(jnp.int32)[None]
    grad_down_total, grad_gate_total, grad_up_total = (
        whole_columns(my_group, *spread_blocks(total), 0, units) for total in totals
    )

    mlp_gain_part = jnp.sum(mid_unit * grad_mid, 0)
    grad_resid = grad_y_low.astype(full) + norm_back(mid_unit, inverse_mid, grad_mid * mlp_gains)
    resid_low = grad_resid.astype(low)
    grad_mixed = jnp.dot(resid_low, out_all, preferred_element_type=full).astype(low)
    attend_back = [
        vmem_call(
            attend_back_body,
            [
                quad_rows,
                jax.ShapeDtypeStruct((rows, block_columns), full),
                quad_rows,
                jax.ShapeDtypeStruct((1, head_dim), full),
            ],
            30 * rows * rows * block_columns,
            scratch=[pltpu.VMEM((2 * rows, head_dim), full)] * 2,
            scalars=1,
            specs={5: column_spec(rows, block_columns, i)},
            name="attend_back",
        )
        for i in range(4)
    ]
    finish = vmem_call(
        finish_body,
        [quad_rows, quad_rows, jax.ShapeDtypeStruct((1, head_dim), full)],
        rows * head_dim,
        name="finish",
    )
    order = (3, 1, 2, 0)
    order_of_chips = (1, 3, 2, 0)
    backs, finished = {}, {}
    for i in order:
        raw, query, own_pair = projected[i]
        backs[i] = attend_back[i](
            info, query, earlier[i], own_pair, attended[i][1], grad_mixed, raw, cosine, sine,
            query_gains,
        )
    for i in order:
        came = lax.ppermute(backs[i][2], "rep", downward)
        finished[i] = finish(
            backs[i][0], backs[i][1], came, projected[i][0], cosine, sine, key_gains
        )
    query_gain_part = sum(backs[i][3] for i in order)
    key_gain_part = sum(finished[i][2] for i in order)

    def block_total(left, even, odd):
        columns = even[0].shape[1]
        half = width // 2
        even, odd = jnp.concatenate(even, 1), jnp.concatenate(odd, 1)
        other = outer(left, odd).astype(low)
        total = outer(left, even) + across(other, CORE)
        to_x = total[:half, : 2 * columns].astype(low)
        to_y = total[half:, columns : 3 * columns].astype(low)
        head, tail = plane_sum(
            total[:half, 3 * columns :], total[half:, 3 * columns :],
            jnp.concatenate([to_x[:, :columns], to_x[:, columns:]], 0),
            jnp.concatenate([to_y[:, columns:], to_y[:, :columns]], 0),
            total[:half, 2 * columns : 3 * columns], total[half:, :columns],
        )
        own = jnp.concatenate([head, tail], 0)
        return ring_sum(jnp.split(own, shards, 0), low).astype(low)

    out_total = block_total(
        rolled(resid_low),
        [attended[i][0][:, :head_columns] for i in order_of_chips],
        [attended[i][0][:, head_columns:] for i in order_of_chips],
    )
    qkv_total = block_total(
        normed,
        [finished[i][0] for i in order_of_chips],
        [finished[i][1] for i in order_of_chips],
    )
    grad_out_total = whole_columns(my_group, *spread_blocks(out_total), 0, head_columns)
    qkv_spread = spread_blocks(qkv_total)
    grad_query_total = whole_columns(my_group, *qkv_spread, 0, head_columns)
    grad_key_total = whole_columns(my_group, *qkv_spread, head_columns, head_dim)
    grad_value_total = whole_columns(my_group, *qkv_spread, 3 * head_dim, head_dim)

    grad_qkv = jnp.concatenate([part for i in range(4) for part in finished[i][:2]], 1)
    step = width // shards
    qkv_all = jnp.concatenate(
        [
            jnp.concatenate([own, side[:step], ahead, side[step:]], 0)
            for refs in qkv_refs
            for own, side, ahead in (refs[:3], refs[3:])
        ],
        1,
    )
    grad_in = rolled(
        jnp.einsum("rf,nf->rn", grad_qkv, qkv_all, preferred_element_type=full)
    )
    grad_tokens = from_sequences(
        (grad_resid + norm_back(x_unit, inverse_in, grad_in * attn_gains)).astype(low)
    )
    attn_gain_part = jnp.sum(x_unit * grad_in, 0)

    parts = everywhere_sum(
        jnp.concatenate(
            [attn_gain_part, mlp_gain_part, query_gain_part[0], key_gain_part[0]]
        )
    )
    for by in (1, 2):
        parts = parts + lax.ppermute(parts, "shard", [(i, i ^ by) for i in range(shards)])
    wide = lax.dynamic_slice_in_dim(
        parts[: 2 * width].reshape(2, width), shard_at * step, step, 1
    )
    narrow = parts[2 * width :]
    return (
        output,
        grad_tokens,
        wide[0],
        grad_query_total,
        grad_key_total,
        grad_value_total,
        narrow[:head_dim],
        narrow[head_dim:],
        grad_out_total,
        wide[1],
        grad_gate_total,
        grad_up_total,
        grad_down_total,
    )


def solution(mesh):
    sizes = (mesh.shape["rep"], mesh.shape["shard"])
    return jax.shard_map(
        on_device_block if sizes == (8, 4) else on_device,
        mesh=mesh,
        in_specs=(
            P("rep", "shard", None),
            P("rep"),
            P("shard"),
            P("shard", None),
            P("shard", None),
            P("shard", None),
            P(),
            P(),
            P("shard", None),
            P("shard"),
            P("shard", None),
            P("shard", None),
            P("shard", None),
            P("rep", "shard", None),
        ),
        out_specs=(
            P("rep", "shard", None),
            P("rep", "shard", None),
            P("shard"),
            P("shard", None),
            P("shard", None),
            P("shard", None),
            P(),
            P(),
            P("shard", None),
            P("shard"),
            P("shard", None),
            P("shard", None),
            P("shard", None),
        ),
        check_vma=False,
    )
```

```python
import jax
import jax.numpy as jnp
from jax import lax
from jax.experimental import pallas as pl
from jax.experimental.pallas import tpu as pltpu
from jax.sharding import PartitionSpec as P

WINDOW = 512


EPS = 1e-06
ROPE_BASE = 1000000.0
NEG = -1e30


def passed_along(x, axis, by):
    devices = lax.axis_size(axis)
    pairs = [(i, i + by) for i in range(devices) if 0 <= i + by < devices]
    return lax.ppermute(x, axis, pairs)


def tables(positions, head_dim):
    half = head_dim // 2
    freq = ROPE_BASE ** (-jnp.arange(half, dtype=jnp.float32) * 2.0 / head_dim)
    angle = positions.astype(jnp.float32)[:, None] * freq[None, :]
    angle = jnp.concatenate([angle, angle], -1)
    return (jnp.cos(angle)[None, :, None, :], jnp.sin(angle)[None, :, None, :])


def rotated_rows(value_rows):
    half = value_rows.shape[-1] // 2
    return jnp.concatenate([-value_rows[..., half:], value_rows[..., :half]], -1)


def head_norm(raw, gain):
    inverse = lax.rsqrt(jnp.mean(raw * raw, -1, keepdims=True) + EPS)
    unit = raw * inverse
    return (unit, inverse, unit * gain)


def norm_back(unit, inverse, grad_unit):
    return inverse * (grad_unit - unit * jnp.mean(grad_unit * unit, -1, keepdims=True))


def head_norm_back(unit, inverse, grad_normed, gain):
    grad_raw = norm_back(unit, inverse, grad_normed * gain)
    return (grad_raw, jnp.sum(unit * grad_normed, axis=(0, 1, 2)))


def scores(query_rows, keys, allowed, scale):
    raw = (
        jnp.einsum("sqhgd,skhd->shgqk", query_rows, keys, preferred_element_type=jnp.float32)
        * scale
    )
    return jnp.where(allowed[:, None, None], raw, NEG)


def outer(left, right):
    return jnp.einsum("rc,rf->cf", left, right, preferred_element_type=jnp.float32)


def on_device(
    tokens,
    lengths,
    attn_gain,
    w_query,
    key_matrix,
    value_matrix,
    query_gain,
    key_gain,
    w_out,
    mlp_gain,
    w_gate,
    w_up,
    w_down,
    cotangent,
):
    seq_count, piece, width = tokens.shape
    head_dim = query_gain.shape[0]
    heads_q = w_query.shape[1] // head_dim
    heads_kv = key_matrix.shape[1] // head_dim
    groups = heads_q // heads_kv
    rows = seq_count * piece
    scale = head_dim ** (-0.5)
    reach = (WINDOW + piece - 2) // piece
    owned = width // lax.axis_size("shard")
    shard_at = lax.axis_index("shard")
    query_pos = shard_at * piece + jnp.arange(piece, dtype=jnp.int32)
    key_pos = (shard_at - reach) * piece + jnp.arange((reach + 1) * piece, dtype=jnp.int32)
    near = (
        (key_pos[None, :] <= query_pos[:, None])
        & (query_pos[:, None] - key_pos[None, :] < WINDOW)
        & (key_pos[None, :] >= 0)
    )
    live = (key_pos[None, None, :] < lengths[:, None, None]) | (
        key_pos[None, :] == query_pos[:, None]
    )[None]
    allowed = near[None] & live
    valid = (query_pos[None, :] < lengths[:, None]).astype(jnp.float32).reshape(rows, 1)
    cosine_table, sine_table = tables(query_pos, head_dim)
    x_rows = tokens.astype(jnp.float32).reshape(rows, width)
    inverse_in = lax.rsqrt(jnp.mean(x_rows * x_rows, -1, keepdims=True) + EPS)
    x_unit = x_rows * inverse_in
    gain_piece = lax.all_gather(attn_gain, "shard", axis=0, tiled=True)
    query_piece = lax.all_gather(w_query, "shard", axis=0, tiled=True)
    key_piece = lax.all_gather(key_matrix, "shard", axis=0, tiled=True)
    value_piece = lax.all_gather(value_matrix, "shard", axis=0, tiled=True)
    normed_piece = (x_unit * gain_piece.astype(jnp.float32)).astype(jnp.bfloat16)
    acc_q = jnp.dot(normed_piece, query_piece, preferred_element_type=jnp.float32)
    acc_k = jnp.dot(normed_piece, key_piece, preferred_element_type=jnp.float32)
    acc_v = jnp.dot(normed_piece, value_piece, preferred_element_type=jnp.float32)
    normalized_rows = normed_piece
    gains = gain_piece.astype(jnp.float32)
    attn_in = normalized_rows
    attn_gains = gains
    query_unit, query_inverse, query_rows_normalized = head_norm(
        acc_q.reshape(seq_count, piece, heads_q, head_dim), query_gain.astype(jnp.float32)
    )
    key_unit, key_inverse, key_normed = head_norm(
        acc_k.reshape(seq_count, piece, heads_kv, head_dim), key_gain.astype(jnp.float32)
    )
    query_rows = (
        (query_rows_normalized * cosine_table + rotated_rows(query_rows_normalized) * sine_table)
        .astype(jnp.bfloat16)
        .reshape(seq_count, piece, heads_kv, groups, head_dim)
    )
    keys_own = (key_normed * cosine_table + rotated_rows(key_normed) * sine_table).astype(
        jnp.bfloat16
    )
    values_own = acc_v.reshape(seq_count, piece, heads_kv, head_dim).astype(jnp.bfloat16)
    own_pair = jnp.stack([keys_own, values_own])
    parts = []
    for fetch_back in range(reach, 0, -1):
        parts.append(passed_along(own_pair, "shard", fetch_back))
    parts.append(own_pair)
    near_pair = jnp.concatenate(parts, 2)
    score = scores(query_rows, near_pair[0], allowed, scale)
    top = jnp.max(score, -1, keepdims=True)
    expo = jnp.exp(score - top)
    total = jnp.sum(expo, -1, keepdims=True)
    prob = expo / total
    log_total = top + jnp.log(total)
    mixed = jnp.einsum(
        "shgqk,skhd->sqhgd",
        prob.astype(jnp.bfloat16),
        near_pair[1],
        preferred_element_type=jnp.float32,
    )
    mixed_rows = mixed.reshape(rows, heads_q * head_dim).astype(jnp.bfloat16)
    resid = x_rows + jnp.einsum(
        "rf,nf->rn",
        mixed_rows,
        lax.all_gather(w_out, "shard", axis=0, tiled=True),
        preferred_element_type=jnp.float32,
    )
    inverse_mid = lax.rsqrt(jnp.mean(resid * resid, -1, keepdims=True) + EPS)
    mid_unit = resid * inverse_mid
    gain_piece = lax.all_gather(mlp_gain, "shard", axis=0, tiled=True)
    gate_piece = lax.all_gather(w_gate, "shard", axis=0, tiled=True)
    up_piece = lax.all_gather(w_up, "shard", axis=0, tiled=True)
    normed_piece = (mid_unit * gain_piece.astype(jnp.float32)).astype(jnp.bfloat16)
    acc_gate = jnp.dot(normed_piece, gate_piece, preferred_element_type=jnp.float32)
    acc_up = jnp.dot(normed_piece, up_piece, preferred_element_type=jnp.float32)
    normalized_rows = normed_piece
    gains = gain_piece.astype(jnp.float32)
    mlp_in = normalized_rows
    sigma = jax.nn.sigmoid(acc_gate)
    swish = acc_gate * sigma
    act = (swish * acc_up).astype(jnp.bfloat16)
    mlp_out = jnp.einsum(
        "rf,nf->rn",
        act,
        lax.all_gather(w_down, "shard", axis=0, tiled=True),
        preferred_element_type=jnp.float32,
    )
    output = (valid * (resid + mlp_out)).astype(jnp.bfloat16).reshape(seq_count, piece, width)
    grad_y = cotangent.astype(jnp.float32).reshape(rows, width) * valid
    grad_y_low = grad_y.astype(jnp.bfloat16)
    grad_act = jnp.dot(
        grad_y_low,
        lax.all_gather(w_down, "shard", axis=0, tiled=True),
        preferred_element_type=jnp.float32,
    )
    grad_gate = (grad_act * acc_up * sigma * (1.0 + acc_gate * (1.0 - sigma))).astype(jnp.bfloat16)
    grad_up = (grad_act * swish).astype(jnp.bfloat16)
    gate_piece, up_piece = lax.all_gather((w_gate, w_up), "shard", axis=0, tiled=True)
    grad_mid = jnp.einsum(
        "rf,nf->rn", grad_gate, gate_piece, preferred_element_type=jnp.float32
    ) + jnp.einsum("rf,nf->rn", grad_up, up_piece, preferred_element_type=jnp.float32)
    grad_resid = grad_y + norm_back(mid_unit, inverse_mid, grad_mid * gains)
    mlp_gain_part = jnp.sum(mid_unit * grad_mid, 0)
    normalized_rows = mlp_in
    mlp_grads = jax.tree.map(
        lambda part: lax.psum_scatter(
            part.astype(jnp.bfloat16), "shard", scatter_dimension=0, tiled=True
        ).astype(jnp.float32),
        (
            outer(normalized_rows, grad_gate),
            outer(normalized_rows, grad_up),
            outer(grad_y_low, act),
        ),
    )
    resid_low = grad_resid.astype(jnp.bfloat16)
    grad_mixed = jnp.dot(
        resid_low,
        lax.all_gather(w_out, "shard", axis=0, tiled=True),
        preferred_element_type=jnp.float32,
    )
    grad_mixed = grad_mixed.astype(jnp.bfloat16).reshape(
        seq_count, piece, heads_kv, groups, head_dim
    )
    prob_again = jnp.exp(scores(query_rows, near_pair[0], allowed, scale) - log_total)
    grad_prob = jnp.einsum(
        "sqhgd,skhd->shgqk", grad_mixed, near_pair[1], preferred_element_type=jnp.float32
    )
    grad_values = jnp.einsum(
        "shgqk,sqhgd->skhd",
        prob_again.astype(jnp.bfloat16),
        grad_mixed,
        preferred_element_type=jnp.float32,
    )
    grad_score = (
        prob_again * (grad_prob - jnp.sum(prob_again * grad_prob, -1, keepdims=True))
    ).astype(jnp.bfloat16)
    grad_queries = (
        jnp.einsum(
            "shgqk,skhd->sqhgd", grad_score, near_pair[0], preferred_element_type=jnp.float32
        )
        * scale
    )
    grad_keys = (
        jnp.einsum("shgqk,sqhgd->skhd", grad_score, query_rows, preferred_element_type=jnp.float32)
        * scale
    )
    grad_pair = jnp.stack([grad_keys, grad_values])
    own_grad = grad_pair[:, :, reach * piece :]
    for back in range(1, reach + 1):
        lower = (reach - back) * piece
        own_grad = own_grad + passed_along(grad_pair[:, :, lower : lower + piece], "shard", -back)
    grad_query_post = grad_queries.reshape(seq_count, piece, heads_q, head_dim)
    grad_query_normed = grad_query_post * cosine_table - rotated_rows(grad_query_post * sine_table)
    grad_key_normed = own_grad[0] * cosine_table - rotated_rows(own_grad[0] * sine_table)
    grad_query_raw, query_gain_grad = head_norm_back(
        query_unit, query_inverse, grad_query_normed, query_gain.astype(jnp.float32)
    )
    grad_key_raw, key_gain_grad = head_norm_back(
        key_unit, key_inverse, grad_key_normed, key_gain.astype(jnp.float32)
    )
    grad_query_low = grad_query_raw.reshape(rows, heads_q * head_dim).astype(jnp.bfloat16)
    grad_key_low = grad_key_raw.reshape(rows, heads_kv * head_dim).astype(jnp.bfloat16)
    grad_value_low = own_grad[1].reshape(rows, heads_kv * head_dim).astype(jnp.bfloat16)
    query_piece, key_piece, value_piece = lax.all_gather(
        (w_query, key_matrix, value_matrix), "shard", axis=0, tiled=True
    )
    grad_in = (
        jnp.einsum("rf,nf->rn", grad_query_low, query_piece, preferred_element_type=jnp.float32)
        + jnp.einsum("rf,nf->rn", grad_key_low, key_piece, preferred_element_type=jnp.float32)
        + jnp.einsum("rf,nf->rn", grad_value_low, value_piece, preferred_element_type=jnp.float32)
    )
    grad_tokens = (
        (grad_resid + norm_back(x_unit, inverse_in, grad_in * attn_gains))
        .astype(jnp.bfloat16)
        .reshape(seq_count, piece, width)
    )
    attn_gain_part = jnp.sum(x_unit * grad_in, 0)
    normalized_rows = attn_in
    attn_grads = jax.tree.map(
        lambda part: lax.psum_scatter(
            part.astype(jnp.bfloat16), "shard", scatter_dimension=0, tiled=True
        ).astype(jnp.float32),
        (
            outer(normalized_rows, grad_query_low),
            outer(normalized_rows, grad_key_low),
            outer(normalized_rows, grad_value_low),
            outer(resid_low, mixed_rows),
        ),
    )
    head_grads = lax.psum(
        (query_gain_grad, key_gain_grad, attn_gain_part, mlp_gain_part), ("rep", "shard")
    )
    attn_gain_total = lax.dynamic_slice_in_dim(head_grads[2], shard_at * owned, owned, 0)
    mlp_gain_total = lax.dynamic_slice_in_dim(head_grads[3], shard_at * owned, owned, 0)
    summed = (
        lax.psum(attn_grads[0].astype(jnp.bfloat16), "rep").astype(jnp.float32),
        lax.psum(attn_grads[1].astype(jnp.bfloat16), "rep").astype(jnp.float32),
        lax.psum(attn_grads[2].astype(jnp.bfloat16), "rep").astype(jnp.float32),
        lax.psum(attn_grads[3].astype(jnp.bfloat16), "rep").astype(jnp.float32),
        lax.psum(mlp_grads[0].astype(jnp.bfloat16), "rep").astype(jnp.float32),
        lax.psum(mlp_grads[1].astype(jnp.bfloat16), "rep").astype(jnp.float32),
        lax.psum(mlp_grads[2].astype(jnp.bfloat16), "rep").astype(jnp.float32),
    )
    attn_grads = summed[:4]
    mlp_grads = summed[4:]
    return (
        output,
        grad_tokens,
        attn_gain_total,
        attn_grads[0],
        attn_grads[1],
        attn_grads[2],
        head_grads[0],
        head_grads[1],
        attn_grads[3],
        mlp_gain_total,
        mlp_grads[0],
        mlp_grads[1],
        mlp_grads[2],
    )


CORE, ACROSS_X, ACROSS_Y = 1, 2, 4
VMEM_BYTES = 56 * 2**20


def across(x, mask):
    count = lax.axis_size("rep")
    return lax.ppermute(x, "rep", [(i, i ^ mask) for i in range(count)])


def around(x, by):
    count = lax.axis_size("shard")
    return lax.ppermute(x, "shard", [(i, (i + by) % count) for i in range(count)])


def after(x, *done):
    return lax.optimization_barrier((x, *done))[0]


def ring_gather(x):
    before, behind = around(x, 1), around(x, -1)
    return [x, before, around(before, 1), behind]


def ring_sum(chunks, kind):
    last = chunks[3] + around(chunks[2].astype(kind), 1)
    return chunks[0] + around(chunks[1].astype(kind), -1) + around(last.astype(kind), 1)


class Links:
    def __init__(self):
        self.sent = {ACROSS_X: [], ACROSS_Y: []}

    def send(self, x, mask):
        sent = self.sent[mask]
        if len(sent) > 1:
            x = after(x, sent[-2])
        sent.append(across(x, mask))
        return sent[-1]

    def gather(self, *pieces):
        near = [(self.send(p, ACROSS_X), self.send(p, ACROSS_Y)) for p in pieces]
        out = []
        for piece, (from_x, from_y) in zip(pieces, near):
            half = piece.shape[0] // 2
            far = self.send(from_x[:half], ACROSS_Y), self.send(from_y[half:], ACROSS_X)
            out.append([piece, from_x, from_y, *far])
        return out

    def total(self, to_x, to_y, split, own_head, own_tail, two_head, one_tail):
        low, full = jnp.bfloat16, jnp.float32
        x_own, x_two = split(self.send(to_x, ACROSS_X))
        y_own, y_one = split(self.send(to_y, ACROSS_Y))
        two_head = (two_head.astype(full) + x_two).astype(low)
        one_tail = (one_tail.astype(full) + y_one).astype(low)
        own_head = own_head.astype(full) + x_own + self.send(two_head, ACROSS_Y)
        own_tail = own_tail.astype(full) + y_own + self.send(one_tail, ACROSS_X)
        return jnp.concatenate([own_head, own_tail], 0)


def sequence_pairs(turn):
    groups, shards = lax.axis_size("rep"), lax.axis_size("shard")
    pairs = []
    for group in range(groups):
        chip, core = divmod(group, 2)
        for at in range(shards):
            to_group, to_shard = 2 * chip + at // 2, 2 * core + (turn ^ (at & 1))
            pairs.append((group * shards + at, to_group * shards + to_shard))
    return pairs


def rolled(x):
    count, at = lax.axis_size("shard"), lax.axis_index("shard")
    width = x.shape[1] // count
    return jnp.concatenate(
        [lax.dynamic_slice_in_dim(x, ((at - i) % count) * width, width, 1) for i in range(count)],
        1,
    )


def to_sequences(x):
    odd = lax.axis_index("shard") & 1
    came = [
        lax.ppermute(
            lax.dynamic_index_in_dim(x, turn ^ odd, 0, keepdims=False),
            ("rep", "shard"),
            sequence_pairs(turn),
        )
        for turn in range(2)
    ]
    even = odd == 0
    return jnp.concatenate(
        [jnp.where(even, came[0], came[1]), jnp.where(even, came[1], came[0])], 0
    )


def from_sequences(x):
    odd = lax.axis_index("shard") & 1
    x = x.reshape(2, x.shape[0] // 2, x.shape[1])
    came = [
        lax.ppermute(
            lax.dynamic_index_in_dim(x, turn ^ odd, 0, keepdims=False),
            ("rep", "shard"),
            [(to, at) for at, to in sequence_pairs(turn)],
        )
        for turn in range(2)
    ]
    even = odd == 0
    return jnp.stack([jnp.where(even, came[0], came[1]), jnp.where(even, came[1], came[0])])


def column_block(weights, at):
    cuts = [w.shape[1] // 8 for w in weights]
    return jnp.concatenate(
        [lax.dynamic_slice_in_dim(w, at * cut, cut, 1) for w, cut in zip(weights, cuts)], 1
    )


def spread_blocks(links, block):
    own = jnp.concatenate(links.gather(block)[0], 0)
    return own, across(own, CORE)


def whole_body(me, own, other, out):
    mine = (me[0] ^ pl.program_id(0)) & 1 == 0

    @pl.when(mine)
    def _():
        out[...] = own[...].astype(jnp.float32)

    @pl.when(jnp.logical_not(mine))
    def _():
        out[...] = other[...].astype(jnp.float32)


def whole_columns(me, own, other, first, width):
    rows = own.shape[0] // 4
    spec = pl.BlockSpec((rows, width), lambda i, at: ((at[0] ^ i) >> 1, first // width))
    return pl.pallas_call(
        whole_body,
        grid_spec=pltpu.PrefetchScalarGridSpec(
            num_scalar_prefetch=1,
            grid=(8,),
            in_specs=[spec, spec],
            out_specs=pl.BlockSpec((rows, width), lambda i, at: (0, i)),
        ),
        out_shape=jax.ShapeDtypeStruct((rows, 8 * width), jnp.float32),
        compiler_params=pltpu.CompilerParams(vmem_limit_bytes=VMEM_BYTES),
        cost_estimate=pl.CostEstimate(
            flops=rows * 8 * width, bytes_accessed=48 * rows * width, transcendentals=0
        ),
        name="whole_columns",
    )(me, own, other)


def everywhere_sum(x):
    for mask in (CORE, ACROSS_X, ACROSS_Y):
        x = x + across(x, mask)
    return x


def turned(x):
    return pltpu.roll(x, x.shape[-1] // 2, x.ndim - 1)


def nt(left, right):
    return lax.dot_general(
        left, right, (((1,), (1,)), ((), ())), preferred_element_type=jnp.float32
    )


def tn(left, right):
    return lax.dot_general(
        left, right, (((0,), (0,)), ((), ())), preferred_element_type=jnp.float32
    )


def unit_of(raw):
    inverse = lax.rsqrt(jnp.mean(raw * raw, -1, keepdims=True) + EPS)
    return raw * inverse, inverse


def project_body(
    normed, own0, side0, far0, own1, side1, far1, cosine, sine, gains, raw, query, key_value
):
    step = own0.shape[0]
    dim = cosine.shape[1]
    for block, (own, side, far) in enumerate(((own0, side0, far0), (own1, side1, far1))):
        at = block * 4 * dim
        raw[:, at : at + 4 * dim] = (
            jnp.dot(normed[:, :step], own[...], preferred_element_type=jnp.float32)
            + jnp.dot(
                normed[:, step : 2 * step], side[:step], preferred_element_type=jnp.float32
            )
            + jnp.dot(
                normed[:, 2 * step : 3 * step], far[...], preferred_element_type=jnp.float32
            )
            + jnp.dot(normed[:, 3 * step :], side[step:], preferred_element_type=jnp.float32)
        )
        for i in range(3):
            unit, _ = unit_of(raw[:, at + i * dim : at + (i + 1) * dim])
            head = unit * gains[i // 2 : i // 2 + 1, :]
            head = (head * cosine[...] + turned(head) * sine[...]).astype(jnp.bfloat16)
            if i < 2:
                query[:, (2 * block + i) * dim : (2 * block + i + 1) * dim] = head
            else:
                key_value[:, 2 * block * dim : (2 * block + 1) * dim] = head
        key_value[:, (2 * block + 1) * dim : (2 * block + 2) * dim] = raw[
            :, at + 3 * dim : at + 4 * dim
        ].astype(jnp.bfloat16)


def window_scores(info, query, keys, part, scale):
    rows, columns = query.shape[0], keys.shape[0]
    half = columns - rows
    row = lax.broadcasted_iota(jnp.int32, (rows, columns), 0)
    column = lax.broadcasted_iota(jnp.int32, (rows, columns), 1)
    gap = column - row - half
    slot = column + ((info[0] - 1) * half + part * rows)
    allowed = (gap <= 0) & (gap > -half) & (slot >= 0) & ((slot < info[1]) | (gap == 0))
    return nt(query, keys) * scale, allowed


def key_columns(block, dim):
    key = slice(2 * block * dim, (2 * block + 1) * dim)
    value = slice((2 * block + 1) * dim, (2 * block + 2) * dim)
    return key, value


def seen_pair(before, own, part, block, dim):
    here, there = key_columns(block, dim), key_columns(1 - block, dim)
    rows = own.shape[0] // 2
    if part == 0:
        return [
            jnp.concatenate([before[:, t], own[:rows, h]], 0) for h, t in zip(here, there)
        ]
    return [jnp.concatenate([before[rows:, t], own[:, h]], 0) for h, t in zip(here, there)]


def attend_body(info, query, before, own, mixed, log_total):
    dim = own.shape[1] // 4
    rows = query.shape[0] // 2
    for part in range(2):
        at = slice(part * rows, (part + 1) * rows)
        for block in range(2):
            keys, values = seen_pair(before, own, part, block, dim)
            for head in (2 * block, 2 * block + 1):
                on = slice(head * dim, (head + 1) * dim)
                score, allowed = window_scores(info, query[at, on], keys, part, dim**-0.5)
                score = jnp.where(allowed, score, NEG)
                top = jnp.max(score, -1, keepdims=True)
                expo = jnp.exp(score - top)
                total = jnp.sum(expo, -1, keepdims=True)
                prob = (expo * (1.0 / total)).astype(jnp.bfloat16)
                mixed[at, on] = jnp.dot(
                    prob, values, preferred_element_type=jnp.float32
                ).astype(jnp.bfloat16)
                log_total[at, on] = jnp.broadcast_to(top + jnp.log(total), (rows, dim))


def attend_back_body(
    info, query, before, own, log_total, grad_resid, weight0, weight1, raw, cosine, sine, gain,
    grad_query, grad_own, grad_before, gain_part, grad_keys, grad_values, grad_mixed,
):
    dim = own.shape[1] // 4
    rows = query.shape[0] // 2
    scale = dim**-0.5
    gain_total = jnp.zeros((1, dim), jnp.float32)
    for block, weight in enumerate((weight0, weight1)):
        on = slice(2 * block * dim, 2 * (block + 1) * dim)
        grad_mixed[:, on] = jnp.dot(
            grad_resid[...], weight[...], preferred_element_type=jnp.float32
        ).astype(jnp.bfloat16)
        grad_keys[...] = jnp.zeros_like(grad_keys)
        grad_values[...] = jnp.zeros_like(grad_values)
        for part in range(2):
            keys, values = seen_pair(before, own, part, block, dim)
            at = slice(part * rows, (part + 1) * rows)
            seen = slice(part * rows, part * rows + keys.shape[0])
            for head in (2 * block, 2 * block + 1):
                on = slice(head * dim, (head + 1) * dim)
                score, allowed = window_scores(info, query[at, on], keys, part, scale)
                prob = jnp.where(allowed, jnp.exp(score - log_total[at, on][:, :1]), 0.0)
                grad_prob = nt(grad_mixed[at, on], values)
                inner = jnp.sum(prob * grad_prob, -1, keepdims=True)
                grad_score = (prob * (grad_prob - inner)).astype(jnp.bfloat16)
                grad_values[seen, :] += tn(prob.astype(jnp.bfloat16), grad_mixed[at, on])
                grad_keys[seen, :] += tn(grad_score, query[at, on]) * scale
                back = jnp.dot(grad_score, keys, preferred_element_type=jnp.float32) * scale
                back = back * cosine[at, :] - turned(back) * sine[at, :]
                there = (2 * head - head % 2) * dim
                unit, inverse = unit_of(raw[at, there : there + dim])
                gain_total += jnp.sum(unit * back, 0, keepdims=True)
                back = back * gain[...]
                back = inverse * (back - unit * jnp.mean(back * unit, -1, keepdims=True))
                grad_query[at, on] = back.astype(jnp.bfloat16)
        for grad, here, there in zip(
            (grad_keys, grad_values), key_columns(block, dim), key_columns(1 - block, dim)
        ):
            grad_before[:, there] = grad[: 2 * rows, :].astype(jnp.bfloat16)
            grad_own[:, here] = grad[2 * rows :, :]
    gain_part[...] = gain_total


def finish_body(grad_query, grad_own, came, raw, cosine, sine, gain, even, odd, gain_part):
    dim = cosine.shape[1]
    total = jnp.zeros((1, dim), jnp.float32)
    for block, out in enumerate((even, odd)):
        key, value = key_columns(block, dim)
        back = grad_own[:, key] + came[:, key].astype(jnp.float32)
        back = back * cosine[...] - turned(back) * sine[...]
        unit, inverse = unit_of(raw[:, (4 * block + 2) * dim : (4 * block + 3) * dim])
        total += jnp.sum(unit * back, 0, keepdims=True)
        back = back * gain[...]
        back = inverse * (back - unit * jnp.mean(back * unit, -1, keepdims=True))
        out[:, : 2 * dim] = grad_query[:, 2 * block * dim : (2 * block + 2) * dim]
        out[:, 2 * dim : 3 * dim] = back.astype(jnp.bfloat16)
        grad_value = grad_own[:, value] + came[:, value].astype(jnp.float32)
        out[:, 3 * dim :] = grad_value.astype(jnp.bfloat16)
    gain_part[...] = total


def vmem_call(body, outs, flops, scratch=(), scalars=0, name=None):
    def call(*args):
        in_specs = [
            pl.BlockSpec(memory_space=pltpu.SMEM if i < scalars else pltpu.VMEM)
            for i in range(len(args))
        ]
        return pl.pallas_call(
            body,
            grid=(1,),
            out_shape=outs,
            in_specs=in_specs,
            out_specs=jax.tree.map(lambda _: pl.BlockSpec(memory_space=pltpu.VMEM), outs),
            scratch_shapes=scratch,
            compiler_params=pltpu.CompilerParams(vmem_limit_bytes=VMEM_BYTES),
            cost_estimate=pl.CostEstimate(
                flops=flops,
                bytes_accessed=sum(a.size * a.dtype.itemsize for a in args),
                transcendentals=0,
            ),
            name=name,
        )(*args)

    return call


def hidden_units(mids, grads_y, weights):
    width, units = weights.shape[0], weights.shape[1] // 3
    count = len(mids)
    heights = [m.shape[0] for m in mids]
    rows, cut = sum(heights), units // 3

    def body(*refs):
        gate_w, up_w, w_down, act, grad_gate, grad_up = refs[2 * count :]
        start = 0
        for mid, grad_y in zip(refs[:count], refs[count : 2 * count]):
            at = slice(start, start + mid.shape[0])
            start += mid.shape[0]
            gate = jnp.dot(mid[...], gate_w[...], preferred_element_type=jnp.float32)
            up = jnp.dot(mid[...], up_w[...], preferred_element_type=jnp.float32)
            grad_act = jnp.dot(grad_y[...], w_down[...], preferred_element_type=jnp.float32)
            sigma = jax.nn.sigmoid(gate)
            swish = gate * sigma
            act[at, :] = (swish * up).astype(jnp.bfloat16)
            slope = grad_act * up * sigma * (1.0 + gate * (1.0 - sigma))
            grad_gate[at, :] = slope.astype(jnp.bfloat16)
            grad_up[at, :] = (grad_act * swish).astype(jnp.bfloat16)

    row_specs = [
        pl.BlockSpec((h, width), lambda j: (0, 0), pipeline_mode=pl.Buffered(1)) for h in heights
    ]
    return pl.pallas_call(
        body,
        grid=(3,),
        out_shape=[jax.ShapeDtypeStruct((rows, units), jnp.bfloat16)] * 3,
        in_specs=[
            *row_specs,
            *row_specs,
            pl.BlockSpec((width, cut), lambda j: (0, j)),
            pl.BlockSpec((width, cut), lambda j: (0, j + 3)),
            pl.BlockSpec((width, cut), lambda j: (0, j + 6)),
        ],
        out_specs=[pl.BlockSpec((rows, cut), lambda j: (0, j))] * 3,
        compiler_params=pltpu.CompilerParams(vmem_limit_bytes=VMEM_BYTES),
        cost_estimate=pl.CostEstimate(
            flops=6 * rows * width * units, bytes_accessed=10 * rows * width, transcendentals=0
        ),
        name="hidden_units",
    )(*mids, *grads_y, weights, weights, weights)


def from_hidden(pairs, eighths):
    count, parts = len(pairs), len(eighths)
    rows, units = pairs[0][0].shape[0] // 8, pairs[0][0].shape[1]
    width = pairs[0][1].shape[0]
    cut = width // 4

    def body(*refs):
        ins, outs = refs[: -(parts // 2)], refs[-(parts // 2) :]
        total = 0.0
        for i in range(count):
            part = ins[i * (parts + 1) : (i + 1) * (parts + 1)]
            left = jnp.concatenate([p[...] for p in part[:-1]], 0)
            total = total + nt(left, part[-1][...])
        for i, out in enumerate(outs):
            out[...] = total[2 * i * rows : 2 * (i + 1) * rows].astype(jnp.bfloat16)

    specs, args = [], []
    for left, right, at in pairs:
        specs += [pl.BlockSpec((rows, units), lambda j, e=e: (e, 0)) for e in eighths]
        specs.append(pl.BlockSpec((cut, units), lambda j, at=at: (j, at)))
        args += [left] * parts + [right]
    return pl.pallas_call(
        body,
        grid=(4,),
        out_shape=[jax.ShapeDtypeStruct((2 * rows, width), jnp.bfloat16)] * (parts // 2),
        in_specs=specs,
        out_specs=[pl.BlockSpec((2 * rows, cut), lambda j: (0, j))] * (parts // 2),
        compiler_params=pltpu.CompilerParams(vmem_limit_bytes=VMEM_BYTES),
        cost_estimate=pl.CostEstimate(
            flops=2 * parts * count * rows * width * units,
            bytes_accessed=2 * count * width * units,
            transcendentals=0,
        ),
        name="from_hidden",
    )(*args)


def row_outer(lefts, groups, first, tiles, added=None, places=None):
    rights = [right for group in groups for right in group]
    places = range(len(rights)) if places is None else places
    added = [] if added is None else [added] * len(rights)
    width = lefts[0].shape[1]
    tile = width // 8
    count = len(lefts)
    rows = sum(left.shape[0] for left in lefts)
    columns = [sum(right.shape[1] for right in group) for group in groups]

    def body(*refs):
        left_refs = refs[:count]
        right_refs = refs[count : count + len(rights)]
        add_refs = refs[count + len(rights) : count + len(rights) + len(added)]
        outs = refs[count + len(rights) + len(added) :]
        place = 0
        for i, group in enumerate(groups):
            column = 0
            for right in group:
                on = slice(column, column + right.shape[1])
                total, start = 0.0, 0
                for left in left_refs:
                    stop = start + left.shape[0]
                    total = total + tn(left[...], right_refs[place][start:stop, :])
                    start = stop
                if added:
                    total = total + add_refs[place][...].astype(jnp.float32)
                outs[i][:, on] = total.astype(jnp.bfloat16)
                place += 1
                column += right.shape[1]

    return pl.pallas_call(
        body,
        grid=(tiles,),
        out_shape=[jax.ShapeDtypeStruct((tiles * tile, c), jnp.bfloat16) for c in columns],
        in_specs=[
            *(pl.BlockSpec((left.shape[0], tile), lambda j: (0, j + first)) for left in lefts),
            *(
                pl.BlockSpec(right.shape, lambda j: (0, 0), pipeline_mode=pl.Buffered(1))
                for right in rights
            ),
            *(
                pl.BlockSpec((tile, rights[0].shape[1]), lambda j, at=at: (j + first, at))
                for at in places[: len(added)]
            ),
        ],
        out_specs=[pl.BlockSpec((tile, c), lambda j: (j, 0)) for c in columns],
        compiler_params=pltpu.CompilerParams(vmem_limit_bytes=VMEM_BYTES),
        cost_estimate=pl.CostEstimate(
            flops=2 * rows * tiles * tile * sum(columns),
            bytes_accessed=2 * rows * (width + sum(columns)),
            transcendentals=0,
        ),
        name="row_outer",
    )(*lefts, *rights, *added)


def close_body(x, *refs):
    mixed, weights = refs[:4], refs[4:12]
    gains, resid, mid = refs[12:]
    at = pl.program_id(0)
    step = x.shape[1]
    columns = weights[0].shape[1]
    total = x[...].astype(jnp.float32)
    for i in range(8):
        part = mixed[i // 2][:, (i % 2) * columns : (i % 2 + 1) * columns]
        total = total + nt(part, weights[i][...])
    resid[:, pl.ds(pl.multiple_of(at * step, step), step)] = total

    @pl.when(at == 3)
    def _():
        unit, _ = unit_of(resid[...])
        mid[...] = (unit * gains[...]).astype(jnp.bfloat16)


def close_attention(x, mixed, weights, gains):
    rows, width = x.shape
    step = width // 4
    whole = lambda a: pl.BlockSpec(a.shape, lambda j: (0, 0))
    return pl.pallas_call(
        close_body,
        grid=(4,),
        out_shape=[
            jax.ShapeDtypeStruct((rows, width), jnp.float32),
            jax.ShapeDtypeStruct((rows, width), jnp.bfloat16),
        ],
        in_specs=[
            pl.BlockSpec((rows, step), lambda j: (0, j)),
            *(whole(m) for m in mixed),
            *(pl.BlockSpec((step, w.shape[1]), lambda j: (j, 0)) for w in weights),
            whole(gains),
        ],
        out_specs=[pl.BlockSpec((rows, width), lambda j: (0, 0))] * 2,
        compiler_params=pltpu.CompilerParams(vmem_limit_bytes=VMEM_BYTES),
        cost_estimate=pl.CostEstimate(
            flops=2 * rows * width * width, bytes_accessed=2 * width * width, transcendentals=0
        ),
        name="close_attention",
    )(x, *mixed, *weights, gains)


def back_to_rows(blocks, weights):
    rows = blocks[0].shape[0]
    step, columns = weights[0][0].shape
    count = len(blocks)

    def body(*refs):
        lefts = refs[:count]
        hbm = refs[count : 4 * count]
        out = refs[4 * count]
        held, sems = refs[4 * count + 1 :]
        copies = []
        for i in range(count):
            own, side, far = hbm[3 * i : 3 * i + 3]
            copies.append(
                [
                    pltpu.make_async_copy(own, held.at[i, :step], sems.at[i, 0]),
                    pltpu.make_async_copy(
                        side.at[:step], held.at[i, step : 2 * step], sems.at[i, 1]
                    ),
                    pltpu.make_async_copy(far, held.at[i, 2 * step : 3 * step], sems.at[i, 2]),
                    pltpu.make_async_copy(side.at[step:], held.at[i, 3 * step :], sems.at[i, 3]),
                ]
            )
        for some in copies:
            for copy in some:
                copy.start()
        for i in range(count):
            for copy in copies[i]:
                copy.wait()
            for k in range(4):
                on = slice(k * step, (k + 1) * step)
                part = nt(lefts[i][...], held[i, on])
                if i == 0:
                    out[:, on] = part
                else:
                    out[:, on] += part

    return pl.pallas_call(
        body,
        grid=(1,),
        out_shape=jax.ShapeDtypeStruct((rows, 4 * step), jnp.float32),
        in_specs=[pl.BlockSpec(memory_space=pltpu.VMEM)] * count
        + [pl.BlockSpec(memory_space=pl.ANY)] * (3 * count),
        out_specs=pl.BlockSpec(memory_space=pltpu.VMEM),
        scratch_shapes=[
            pltpu.VMEM((count, 4 * step, columns), jnp.bfloat16),
            pltpu.SemaphoreType.DMA((count, 4)),
        ],
        compiler_params=pltpu.CompilerParams(vmem_limit_bytes=VMEM_BYTES),
        cost_estimate=pl.CostEstimate(
            flops=8 * rows * step * columns * count,
            bytes_accessed=8 * step * columns * count,
            transcendentals=0,
        ),
        name="back_to_rows",
    )(*blocks, *(part for w in weights for part in w))


def on_device_block(
    tokens,
    lengths,
    attn_gain,
    w_query,
    key_matrix,
    value_matrix,
    query_gain,
    key_gain,
    w_out,
    mlp_gain,
    w_gate,
    w_up,
    w_down,
    cotangent,
):
    low, full = jnp.bfloat16, jnp.float32
    width = tokens.shape[2]
    head_dim = query_gain.shape[0]
    shards = lax.axis_size("shard")
    shard_at = lax.axis_index("shard")
    me = lax.axis_index("rep")
    core = me & 1
    count = lax.axis_size("rep")

    links = Links()
    own_blocks = [
        column_block((w_query, key_matrix, value_matrix), me ^ i) for i in range(8)
    ]
    before, behind = around(own_blocks[0], 1), around(own_blocks[0], -1)
    x_low = to_sequences(after(tokens, before, behind))
    rows = x_low.shape[0]
    far = around(before, 1)
    out_own = lax.all_gather(
        after(column_block((w_out,), me), before, behind), "shard", axis=0, tiled=True
    )
    ffn_own = lax.all_gather(
        after(column_block((w_gate, w_up, w_down), me), x_low), "shard", axis=0, tiled=True
    )
    side_blocks, far_blocks = (
        [*blocks[:3], jnp.concatenate(blocks[3:], 0)]
        for blocks in links.gather(jnp.concatenate([before, behind], 0), far)
    )
    other_side = [across(block, CORE) for block in side_blocks]
    other_far = [across(block, CORE) for block in far_blocks]
    qkv_weights = [
        part
        for i in range(4)
        for part in (
            (own_blocks[2 * i], side_blocks[i], far_blocks[i]),
            (own_blocks[2 * i + 1], other_side[i], other_far[i]),
        )
    ]
    gain_parts = jnp.stack([attn_gain, mlp_gain])
    gains = jnp.concatenate(
        [gain_parts, *(around(gain_parts, by) for by in (1, 2, 3))], 1
    ).astype(full)
    gains = rolled(gains)
    attn_gains, mlp_gains = gains[:1], gains[1:]
    query_gains = query_gain.astype(full)[None]
    key_gains = key_gain.astype(full)[None]

    other_lengths = across(lengths, CORE)
    both = jnp.where(
        core == 0,
        jnp.concatenate([lengths, other_lengths]),
        jnp.concatenate([other_lengths, lengths]),
    )
    length = lax.dynamic_index_in_dim(both, shard_at, 0, keepdims=False)
    info = jnp.stack([core, length]).astype(jnp.int32)
    query_pos = core * rows + jnp.arange(rows, dtype=jnp.int32)
    valid = (query_pos < length)[:, None]
    cosine, sine = tables(query_pos, head_dim)
    cosine, sine = cosine[0, :, 0], sine[0, :, 0]
    sine = jnp.concatenate([-sine[:, : head_dim // 2], sine[:, head_dim // 2 :]], 1)

    out_chips = links.gather(out_own)[0]
    out_chips = [*out_chips[:3], jnp.concatenate(out_chips[3:], 0)]
    out_blocks = [block for chip in out_chips for block in (chip, across(chip, CORE))]
    grad_y_low = to_sequences(after(cotangent, x_low, out_own))
    grad_y_low = jnp.where(valid, grad_y_low, jnp.zeros_like(grad_y_low))
    grads_y = links.gather(grad_y_low)[0]
    ffn = [ffn_own, across(ffn_own, CORE)]
    units = ffn_own.shape[1] // 3

    x_rows = x_low.astype(full)
    inverse_in = lax.rsqrt(jnp.mean(x_rows * x_rows, -1, keepdims=True) + EPS)
    x_unit = x_rows * inverse_in
    normed = rolled((x_unit * attn_gains).astype(low))
    head_columns = 2 * head_dim
    block_columns = 4 * head_dim
    quad_rows = jax.ShapeDtypeStruct((rows, block_columns), low)
    project = vmem_call(
        project_body,
        [jax.ShapeDtypeStruct((rows, 2 * block_columns), full), quad_rows, quad_rows],
        4 * rows * width * block_columns,
        name="project",
    )
    attend = vmem_call(
        attend_body,
        [quad_rows, jax.ShapeDtypeStruct((rows, block_columns), full)],
        12 * rows * rows * block_columns,
        scalars=1,
        name="attend",
    )
    head_gains = jnp.concatenate([query_gains, key_gains], 0)
    upward = [(i, i + 1) for i in range(0, count, 2)]
    downward = [(i + 1, i) for i in range(0, count, 2)]
    projected = [
        project(normed, *qkv_weights[2 * i], *qkv_weights[2 * i + 1], cosine, sine, head_gains)
        for i in range(4)
    ]
    earlier = [lax.ppermute(p[2], "rep", upward) for p in projected]
    attended = [
        attend(info, projected[i][1], earlier[i], projected[i][2]) for i in range(4)
    ]
    mixed = [a[0] for a in attended]
    resid, mid = close_attention(x_low, mixed, out_blocks, mlp_gains)
    inverse_mid = lax.rsqrt(jnp.mean(resid * resid, -1, keepdims=True) + EPS)
    mid_unit = resid * inverse_mid

    mids = links.gather(mid)[0]
    hidden = [hidden_units(mids, grads_y, ffn[i]) for i in range(2)]

    def plane_total(pairs):
        to_x, to_y = from_hidden(pairs, (2, 6, 5, 7))
        rest, own = from_hidden([(after(pairs[0][0], to_x), *pairs[0][1:]), *pairs[1:]], (3, 4, 0, 1))
        half = rows // 2
        total = links.total(
            to_x, to_y, lambda a: (a[:half], a[half:]),
            own[:half], own[half:], rest[half:], rest[:half],
        )
        return total, own

    grad_mid, last = plane_total(
        [(hidden[i][1 + j], ffn[i], j) for i in range(2) for j in range(2)]
    )
    acts = [after(hidden[0][0], last), hidden[1][0]]
    mlp_out, last = plane_total([(acts[i], ffn[i], 2) for i in range(2)])
    output = from_sequences(jnp.where(valid, resid + mlp_out, 0.0).astype(low))

    def owned_part(lefts, rights, *done):
        (other,) = row_outer(lefts, [[after(rights[1][0], *done), *rights[1][1:]]], 0, 8)
        (own,) = row_outer(lefts, [rights[0]], 0, 8, across(other, CORE))
        return own, other, lax.psum_scatter(own, "shard", scatter_dimension=0, tiled=True)

    down_own, last, down_total = owned_part(grads_y, [[h[0]] for h in hidden], last)
    gate_up_own, _, gate_up_total = owned_part(mids, [h[1:] for h in hidden], last)
    grad_mid = after(grad_mid, down_own, gate_up_own)

    mlp_gain_part = jnp.sum(mid_unit * grad_mid, 0)
    grad_resid = grad_y_low.astype(full) + norm_back(mid_unit, inverse_mid, grad_mid * mlp_gains)
    resid_low = grad_resid.astype(low)
    attend_back = vmem_call(
        attend_back_body,
        [
            quad_rows,
            jax.ShapeDtypeStruct((rows, block_columns), full),
            quad_rows,
            jax.ShapeDtypeStruct((1, head_dim), full),
        ],
        32 * rows * rows * block_columns,
        scratch=[pltpu.VMEM((2 * rows, head_dim), full)] * 2
        + [pltpu.VMEM((rows, block_columns), low)],
        scalars=1,
        name="attend_back",
    )
    finish = vmem_call(
        finish_body,
        [quad_rows, quad_rows, jax.ShapeDtypeStruct((1, head_dim), full)],
        rows * head_dim,
        name="finish",
    )
    order = (3, 1, 2, 0)
    backs, finished = {}, {}
    for i in order:
        raw, query, own_pair = projected[i]
        backs[i] = attend_back(
            info, query, earlier[i], own_pair, attended[i][1], resid_low, *out_blocks[2 * i : 2 * i + 2],
            raw, cosine, sine, query_gains,
        )
    for i in order:
        came = lax.ppermute(backs[i][2], "rep", downward)
        finished[i] = finish(
            backs[i][0], backs[i][1], came, projected[i][0], cosine, sine, key_gains
        )
    query_gain_part = sum(backs[i][3] for i in order)
    key_gain_part = sum(finished[i][2] for i in order)

    def block_total(left, even, odd):
        columns = even[0].shape[1]
        (other,) = row_outer([left], [odd], 0, 8)
        came = across(other, CORE)
        to_x, two_head, own_head = row_outer(
            [left], [[even[1], even[3]], [even[2]], [even[0]]], 0, 4, came, (1, 3, 2, 0)
        )
        to_y, one_tail, own_tail = row_outer(
            [left], [[even[2], even[3]], [even[1]], [even[0]]], 4, 4, came, (2, 3, 1, 0)
        )
        own = links.total(
            to_x, to_y, lambda a: (a[:, :columns], a[:, columns:]),
            own_head, own_tail, two_head, one_tail,
        )
        return ring_sum(jnp.split(own, shards, 0), low).astype(low)

    out_total = block_total(
        rolled(resid_low),
        [m[:, :head_columns] for m in mixed],
        [m[:, head_columns:] for m in mixed],
    )
    my_group = me.astype(jnp.int32)[None]
    grad_down_total = whole_columns(my_group, *spread_blocks(links, down_total), 0, units)
    qkv_total = block_total(
        normed, [finished[i][0] for i in range(4)], [finished[i][1] for i in range(4)]
    )
    gate_up_spread = spread_blocks(links, gate_up_total)
    grad_gate_total = whole_columns(my_group, *gate_up_spread, 0, units)
    grad_up_total = whole_columns(my_group, *gate_up_spread, units, units)
    out_spread = spread_blocks(links, out_total)
    grad_out_total = whole_columns(my_group, *out_spread, 0, head_columns)
    qkv_spread = spread_blocks(links, qkv_total)
    grad_query_total = whole_columns(my_group, *qkv_spread, 0, head_columns)
    grad_key_total = whole_columns(my_group, *qkv_spread, head_columns, head_dim)
    grad_value_total = whole_columns(my_group, *qkv_spread, 3 * head_dim, head_dim)

    step = width // shards
    grad_in = rolled(
        back_to_rows([part for i in range(4) for part in finished[i][:2]], qkv_weights)
    )
    grad_tokens = from_sequences(
        (grad_resid + norm_back(x_unit, inverse_in, grad_in * attn_gains)).astype(low)
    )
    attn_gain_part = jnp.sum(x_unit * grad_in, 0)

    parts = everywhere_sum(
        jnp.concatenate(
            [attn_gain_part, mlp_gain_part, query_gain_part[0], key_gain_part[0]]
        )
    )
    for by in (1, 2):
        parts = parts + lax.ppermute(parts, "shard", [(i, i ^ by) for i in range(shards)])
    wide = lax.dynamic_slice_in_dim(
        parts[: 2 * width].reshape(2, width), shard_at * step, step, 1
    )
    narrow = parts[2 * width :]
    return (
        output,
        grad_tokens,
        wide[0],
        grad_query_total,
        grad_key_total,
        grad_value_total,
        narrow[:head_dim],
        narrow[head_dim:],
        grad_out_total,
        wide[1],
        grad_gate_total,
        grad_up_total,
        grad_down_total,
    )


def solution(mesh):
    sizes = (mesh.shape["rep"], mesh.shape["shard"])
    return jax.shard_map(
        on_device_block if sizes == (8, 4) else on_device,
        mesh=mesh,
        in_specs=(
            P("rep", "shard", None),
            P("rep"),
            P("shard"),
            P("shard", None),
            P("shard", None),
            P("shard", None),
            P(),
            P(),
            P("shard", None),
            P("shard"),
            P("shard", None),
            P("shard", None),
            P("shard", None),
            P("rep", "shard", None),
        ),
        out_specs=(
            P("rep", "shard", None),
            P("rep", "shard", None),
            P("shard"),
            P("shard", None),
            P("shard", None),
            P("shard", None),
            P(),
            P(),
            P("shard", None),
            P("shard"),
            P("shard", None),
            P("shard", None),
            P("shard", None),
        ),
        check_vma=False,
    )
```

```python
import jax
import jax.numpy as jnp
from jax import lax
from jax.experimental import pallas as pl
from jax.experimental.pallas import tpu as pltpu
from jax.sharding import PartitionSpec as P

WINDOW = 512


EPS = 1e-06
ROPE_BASE = 1000000.0
NEG = -1e30


def passed_along(x, axis, by):
    devices = lax.axis_size(axis)
    pairs = [(i, i + by) for i in range(devices) if 0 <= i + by < devices]
    return lax.ppermute(x, axis, pairs)


def tables(positions, head_dim):
    half = head_dim // 2
    freq = ROPE_BASE ** (-jnp.arange(half, dtype=jnp.float32) * 2.0 / head_dim)
    angle = positions.astype(jnp.float32)[:, None] * freq[None, :]
    angle = jnp.concatenate([angle, angle], -1)
    return (jnp.cos(angle)[None, :, None, :], jnp.sin(angle)[None, :, None, :])


def rotated_rows(value_rows):
    half = value_rows.shape[-1] // 2
    return jnp.concatenate([-value_rows[..., half:], value_rows[..., :half]], -1)


def head_norm(raw, gain):
    inverse = lax.rsqrt(jnp.mean(raw * raw, -1, keepdims=True) + EPS)
    unit = raw * inverse
    return (unit, inverse, unit * gain)


def norm_back(unit, inverse, grad_unit):
    return inverse * (grad_unit - unit * jnp.mean(grad_unit * unit, -1, keepdims=True))


def head_norm_back(unit, inverse, grad_normed, gain):
    grad_raw = norm_back(unit, inverse, grad_normed * gain)
    return (grad_raw, jnp.sum(unit * grad_normed, axis=(0, 1, 2)))


def scores(query_rows, keys, allowed, scale):
    raw = (
        jnp.einsum("sqhgd,skhd->shgqk", query_rows, keys, preferred_element_type=jnp.float32)
        * scale
    )
    return jnp.where(allowed[:, None, None], raw, NEG)


def outer(left, right):
    return jnp.einsum("rc,rf->cf", left, right, preferred_element_type=jnp.float32)


def on_device(
    tokens,
    lengths,
    attn_gain,
    w_query,
    key_matrix,
    value_matrix,
    query_gain,
    key_gain,
    w_out,
    mlp_gain,
    w_gate,
    w_up,
    w_down,
    cotangent,
):
    seq_count, piece, width = tokens.shape
    head_dim = query_gain.shape[0]
    heads_q = w_query.shape[1] // head_dim
    heads_kv = key_matrix.shape[1] // head_dim
    groups = heads_q // heads_kv
    rows = seq_count * piece
    scale = head_dim ** (-0.5)
    reach = (WINDOW + piece - 2) // piece
    owned = width // lax.axis_size("shard")
    shard_at = lax.axis_index("shard")
    query_pos = shard_at * piece + jnp.arange(piece, dtype=jnp.int32)
    key_pos = (shard_at - reach) * piece + jnp.arange((reach + 1) * piece, dtype=jnp.int32)
    near = (
        (key_pos[None, :] <= query_pos[:, None])
        & (query_pos[:, None] - key_pos[None, :] < WINDOW)
        & (key_pos[None, :] >= 0)
    )
    live = (key_pos[None, None, :] < lengths[:, None, None]) | (
        key_pos[None, :] == query_pos[:, None]
    )[None]
    allowed = near[None] & live
    valid = (query_pos[None, :] < lengths[:, None]).astype(jnp.float32).reshape(rows, 1)
    cosine_table, sine_table = tables(query_pos, head_dim)
    x_rows = tokens.astype(jnp.float32).reshape(rows, width)
    inverse_in = lax.rsqrt(jnp.mean(x_rows * x_rows, -1, keepdims=True) + EPS)
    x_unit = x_rows * inverse_in
    gain_piece = lax.all_gather(attn_gain, "shard", axis=0, tiled=True)
    query_piece = lax.all_gather(w_query, "shard", axis=0, tiled=True)
    key_piece = lax.all_gather(key_matrix, "shard", axis=0, tiled=True)
    value_piece = lax.all_gather(value_matrix, "shard", axis=0, tiled=True)
    normed_piece = (x_unit * gain_piece.astype(jnp.float32)).astype(jnp.bfloat16)
    acc_q = jnp.dot(normed_piece, query_piece, preferred_element_type=jnp.float32)
    acc_k = jnp.dot(normed_piece, key_piece, preferred_element_type=jnp.float32)
    acc_v = jnp.dot(normed_piece, value_piece, preferred_element_type=jnp.float32)
    normalized_rows = normed_piece
    gains = gain_piece.astype(jnp.float32)
    attn_in = normalized_rows
    attn_gains = gains
    query_unit, query_inverse, query_rows_normalized = head_norm(
        acc_q.reshape(seq_count, piece, heads_q, head_dim), query_gain.astype(jnp.float32)
    )
    key_unit, key_inverse, key_normed = head_norm(
        acc_k.reshape(seq_count, piece, heads_kv, head_dim), key_gain.astype(jnp.float32)
    )
    query_rows = (
        (query_rows_normalized * cosine_table + rotated_rows(query_rows_normalized) * sine_table)
        .astype(jnp.bfloat16)
        .reshape(seq_count, piece, heads_kv, groups, head_dim)
    )
    keys_own = (key_normed * cosine_table + rotated_rows(key_normed) * sine_table).astype(
        jnp.bfloat16
    )
    values_own = acc_v.reshape(seq_count, piece, heads_kv, head_dim).astype(jnp.bfloat16)
    own_pair = jnp.stack([keys_own, values_own])
    parts = []
    for fetch_back in range(reach, 0, -1):
        parts.append(passed_along(own_pair, "shard", fetch_back))
    parts.append(own_pair)
    near_pair = jnp.concatenate(parts, 2)
    score = scores(query_rows, near_pair[0], allowed, scale)
    top = jnp.max(score, -1, keepdims=True)
    expo = jnp.exp(score - top)
    total = jnp.sum(expo, -1, keepdims=True)
    prob = expo / total
    log_total = top + jnp.log(total)
    mixed = jnp.einsum(
        "shgqk,skhd->sqhgd",
        prob.astype(jnp.bfloat16),
        near_pair[1],
        preferred_element_type=jnp.float32,
    )
    mixed_rows = mixed.reshape(rows, heads_q * head_dim).astype(jnp.bfloat16)
    resid = x_rows + jnp.einsum(
        "rf,nf->rn",
        mixed_rows,
        lax.all_gather(w_out, "shard", axis=0, tiled=True),
        preferred_element_type=jnp.float32,
    )
    inverse_mid = lax.rsqrt(jnp.mean(resid * resid, -1, keepdims=True) + EPS)
    mid_unit = resid * inverse_mid
    gain_piece = lax.all_gather(mlp_gain, "shard", axis=0, tiled=True)
    gate_piece = lax.all_gather(w_gate, "shard", axis=0, tiled=True)
    up_piece = lax.all_gather(w_up, "shard", axis=0, tiled=True)
    normed_piece = (mid_unit * gain_piece.astype(jnp.float32)).astype(jnp.bfloat16)
    acc_gate = jnp.dot(normed_piece, gate_piece, preferred_element_type=jnp.float32)
    acc_up = jnp.dot(normed_piece, up_piece, preferred_element_type=jnp.float32)
    normalized_rows = normed_piece
    gains = gain_piece.astype(jnp.float32)
    mlp_in = normalized_rows
    sigma = jax.nn.sigmoid(acc_gate)
    swish = acc_gate * sigma
    act = (swish * acc_up).astype(jnp.bfloat16)
    mlp_out = jnp.einsum(
        "rf,nf->rn",
        act,
        lax.all_gather(w_down, "shard", axis=0, tiled=True),
        preferred_element_type=jnp.float32,
    )
    output = (valid * (resid + mlp_out)).astype(jnp.bfloat16).reshape(seq_count, piece, width)
    grad_y = cotangent.astype(jnp.float32).reshape(rows, width) * valid
    grad_y_low = grad_y.astype(jnp.bfloat16)
    grad_act = jnp.dot(
        grad_y_low,
        lax.all_gather(w_down, "shard", axis=0, tiled=True),
        preferred_element_type=jnp.float32,
    )
    grad_gate = (grad_act * acc_up * sigma * (1.0 + acc_gate * (1.0 - sigma))).astype(jnp.bfloat16)
    grad_up = (grad_act * swish).astype(jnp.bfloat16)
    gate_piece, up_piece = lax.all_gather((w_gate, w_up), "shard", axis=0, tiled=True)
    grad_mid = jnp.einsum(
        "rf,nf->rn", grad_gate, gate_piece, preferred_element_type=jnp.float32
    ) + jnp.einsum("rf,nf->rn", grad_up, up_piece, preferred_element_type=jnp.float32)
    grad_resid = grad_y + norm_back(mid_unit, inverse_mid, grad_mid * gains)
    mlp_gain_part = jnp.sum(mid_unit * grad_mid, 0)
    normalized_rows = mlp_in
    mlp_grads = jax.tree.map(
        lambda part: lax.psum_scatter(
            part.astype(jnp.bfloat16), "shard", scatter_dimension=0, tiled=True
        ).astype(jnp.float32),
        (
            outer(normalized_rows, grad_gate),
            outer(normalized_rows, grad_up),
            outer(grad_y_low, act),
        ),
    )
    resid_low = grad_resid.astype(jnp.bfloat16)
    grad_mixed = jnp.dot(
        resid_low,
        lax.all_gather(w_out, "shard", axis=0, tiled=True),
        preferred_element_type=jnp.float32,
    )
    grad_mixed = grad_mixed.astype(jnp.bfloat16).reshape(
        seq_count, piece, heads_kv, groups, head_dim
    )
    prob_again = jnp.exp(scores(query_rows, near_pair[0], allowed, scale) - log_total)
    grad_prob = jnp.einsum(
        "sqhgd,skhd->shgqk", grad_mixed, near_pair[1], preferred_element_type=jnp.float32
    )
    grad_values = jnp.einsum(
        "shgqk,sqhgd->skhd",
        prob_again.astype(jnp.bfloat16),
        grad_mixed,
        preferred_element_type=jnp.float32,
    )
    grad_score = (
        prob_again * (grad_prob - jnp.sum(prob_again * grad_prob, -1, keepdims=True))
    ).astype(jnp.bfloat16)
    grad_queries = (
        jnp.einsum(
            "shgqk,skhd->sqhgd", grad_score, near_pair[0], preferred_element_type=jnp.float32
        )
        * scale
    )
    grad_keys = (
        jnp.einsum("shgqk,sqhgd->skhd", grad_score, query_rows, preferred_element_type=jnp.float32)
        * scale
    )
    grad_pair = jnp.stack([grad_keys, grad_values])
    own_grad = grad_pair[:, :, reach * piece :]
    for back in range(1, reach + 1):
        lower = (reach - back) * piece
        own_grad = own_grad + passed_along(grad_pair[:, :, lower : lower + piece], "shard", -back)
    grad_query_post = grad_queries.reshape(seq_count, piece, heads_q, head_dim)
    grad_query_normed = grad_query_post * cosine_table - rotated_rows(grad_query_post * sine_table)
    grad_key_normed = own_grad[0] * cosine_table - rotated_rows(own_grad[0] * sine_table)
    grad_query_raw, query_gain_grad = head_norm_back(
        query_unit, query_inverse, grad_query_normed, query_gain.astype(jnp.float32)
    )
    grad_key_raw, key_gain_grad = head_norm_back(
        key_unit, key_inverse, grad_key_normed, key_gain.astype(jnp.float32)
    )
    grad_query_low = grad_query_raw.reshape(rows, heads_q * head_dim).astype(jnp.bfloat16)
    grad_key_low = grad_key_raw.reshape(rows, heads_kv * head_dim).astype(jnp.bfloat16)
    grad_value_low = own_grad[1].reshape(rows, heads_kv * head_dim).astype(jnp.bfloat16)
    query_piece, key_piece, value_piece = lax.all_gather(
        (w_query, key_matrix, value_matrix), "shard", axis=0, tiled=True
    )
    grad_in = (
        jnp.einsum("rf,nf->rn", grad_query_low, query_piece, preferred_element_type=jnp.float32)
        + jnp.einsum("rf,nf->rn", grad_key_low, key_piece, preferred_element_type=jnp.float32)
        + jnp.einsum("rf,nf->rn", grad_value_low, value_piece, preferred_element_type=jnp.float32)
    )
    grad_tokens = (
        (grad_resid + norm_back(x_unit, inverse_in, grad_in * attn_gains))
        .astype(jnp.bfloat16)
        .reshape(seq_count, piece, width)
    )
    attn_gain_part = jnp.sum(x_unit * grad_in, 0)
    normalized_rows = attn_in
    attn_grads = jax.tree.map(
        lambda part: lax.psum_scatter(
            part.astype(jnp.bfloat16), "shard", scatter_dimension=0, tiled=True
        ).astype(jnp.float32),
        (
            outer(normalized_rows, grad_query_low),
            outer(normalized_rows, grad_key_low),
            outer(normalized_rows, grad_value_low),
            outer(resid_low, mixed_rows),
        ),
    )
    head_grads = lax.psum(
        (query_gain_grad, key_gain_grad, attn_gain_part, mlp_gain_part), ("rep", "shard")
    )
    attn_gain_total = lax.dynamic_slice_in_dim(head_grads[2], shard_at * owned, owned, 0)
    mlp_gain_total = lax.dynamic_slice_in_dim(head_grads[3], shard_at * owned, owned, 0)
    summed = (
        lax.psum(attn_grads[0].astype(jnp.bfloat16), "rep").astype(jnp.float32),
        lax.psum(attn_grads[1].astype(jnp.bfloat16), "rep").astype(jnp.float32),
        lax.psum(attn_grads[2].astype(jnp.bfloat16), "rep").astype(jnp.float32),
        lax.psum(attn_grads[3].astype(jnp.bfloat16), "rep").astype(jnp.float32),
        lax.psum(mlp_grads[0].astype(jnp.bfloat16), "rep").astype(jnp.float32),
        lax.psum(mlp_grads[1].astype(jnp.bfloat16), "rep").astype(jnp.float32),
        lax.psum(mlp_grads[2].astype(jnp.bfloat16), "rep").astype(jnp.float32),
    )
    attn_grads = summed[:4]
    mlp_grads = summed[4:]
    return (
        output,
        grad_tokens,
        attn_gain_total,
        attn_grads[0],
        attn_grads[1],
        attn_grads[2],
        head_grads[0],
        head_grads[1],
        attn_grads[3],
        mlp_gain_total,
        mlp_grads[0],
        mlp_grads[1],
        mlp_grads[2],
    )


CORE, ACROSS_X, ACROSS_Y = 1, 2, 4
VMEM_BYTES = 56 * 2**20
FREE = pl.CostEstimate(flops=1, bytes_accessed=1, transcendentals=0)


def across(x, mask):
    count = lax.axis_size("rep")
    return lax.ppermute(x, "rep", [(i, i ^ mask) for i in range(count)])


def around(x, by):
    count = lax.axis_size("shard")
    return lax.ppermute(x, "shard", [(i, (i + by) % count) for i in range(count)])


class Stage(dict):
    __getattr__ = dict.__getitem__
    __setattr__ = dict.__setitem__

    def end(self, *gone):
        for name in gone:
            del self[name]
        self.update(lax.optimization_barrier(dict(self)))


def in_order(calls):
    outs = []
    for call, first, *rest in calls:
        if outs:
            last = outs[-1][0] if isinstance(outs[-1], (list, tuple)) else outs[-1]
            first = lax.optimization_barrier((first, last))[0]
        outs.append(call(first, *rest))
    return outs


def ring_sum_first(chunks):
    return around(chunks[2], 1), around(chunks[1], -1)


def near(piece):
    return across(piece, ACROSS_X), across(piece, ACROSS_Y)


def far(from_x, from_y):
    half = from_x.shape[0] // 2
    return across(from_x[:half], ACROSS_Y), across(from_y[half:], ACROSS_X)


def rounded_sum(*parts):
    return sum(part.astype(jnp.float32) for part in parts).astype(jnp.bfloat16)


def sequence_pairs(turn):
    groups, shards = lax.axis_size("rep"), lax.axis_size("shard")
    pairs = []
    for group in range(groups):
        chip, core = divmod(group, 2)
        for at in range(shards):
            to_group, to_shard = 2 * chip + at // 2, 2 * core + (turn ^ (at & 1))
            pairs.append((group * shards + at, to_group * shards + to_shard))
    return pairs


def rolled(x):
    count, at = lax.axis_size("shard"), lax.axis_index("shard")
    width = x.shape[1] // count
    return jnp.concatenate(
        [lax.dynamic_slice_in_dim(x, ((at - i) % count) * width, width, 1) for i in range(count)],
        1,
    )


def to_sequences_send(x):
    odd = lax.axis_index("shard") & 1
    return [
        lax.ppermute(
            lax.dynamic_index_in_dim(x, turn ^ odd, 0, keepdims=False),
            ("rep", "shard"),
            sequence_pairs(turn),
        )
        for turn in range(2)
    ]


def from_sequences_send(x):
    odd = lax.axis_index("shard") & 1
    x = x.reshape(2, x.shape[0] // 2, x.shape[1])
    return [
        lax.ppermute(
            lax.dynamic_index_in_dim(x, turn ^ odd, 0, keepdims=False),
            ("rep", "shard"),
            [(to, at) for at, to in sequence_pairs(turn)],
        )
        for turn in range(2)
    ]


def in_turn(came):
    even = lax.axis_index("shard") & 1 == 0
    return [jnp.where(even, came[0], came[1]), jnp.where(even, came[1], came[0])]


def column_block(weights, at):
    cuts = [w.shape[1] // 8 for w in weights]
    return jnp.concatenate(
        [lax.dynamic_slice_in_dim(w, at * cut, cut, 1) for w, cut in zip(weights, cuts)], 1
    )


def whole_columns(me, own, other, widths):
    rows, columns = own.shape[0] // 4, own.shape[1]

    def body(me_ref, own_ref, other_ref, *outs):
        def put(block):
            start = 0
            for out, width in zip(outs, widths):
                out[...] = block[:, start : start + width].astype(jnp.float32)
                start += width

        mine = (me_ref[0] ^ pl.program_id(0)) & 1 == 0
        pl.when(mine)(lambda: put(own_ref))
        pl.when(jnp.logical_not(mine))(lambda: put(other_ref))

    spec = pl.BlockSpec((rows, columns), lambda i, at: ((at[0] ^ i) >> 1, 0))
    return pl.pallas_call(
        body,
        grid_spec=pltpu.PrefetchScalarGridSpec(
            num_scalar_prefetch=1,
            grid=(8,),
            in_specs=[spec, spec],
            out_specs=[pl.BlockSpec((rows, w), lambda i, at: (0, i)) for w in widths],
        ),
        out_shape=[jax.ShapeDtypeStruct((rows, 8 * w), jnp.float32) for w in widths],
        compiler_params=pltpu.CompilerParams(vmem_limit_bytes=VMEM_BYTES),
        cost_estimate=FREE,
        name="whole_columns",
    )(me, own, other)


def turned(x):
    return pltpu.roll(x, x.shape[-1] // 2, x.ndim - 1)


def nt(left, right):
    return lax.dot_general(
        left, right, (((1,), (1,)), ((), ())), preferred_element_type=jnp.float32
    )


def tn(left, right):
    return lax.dot_general(
        left, right, (((0,), (0,)), ((), ())), preferred_element_type=jnp.float32
    )


def unit_of(raw):
    inverse = lax.rsqrt(jnp.mean(raw * raw, -1, keepdims=True) + EPS)
    return raw * inverse, inverse


def project_body(
    normed, own0, came0, own1, came1, cosine, sine, gains, raw, query, key_value
):
    step = own0.shape[0]
    dim = cosine.shape[1]
    for block, (own, came) in enumerate(((own0, came0), (own1, came1))):
        at = block * 4 * dim
        raw[:, at : at + 4 * dim] = jnp.dot(
            normed[:, :step], own[...], preferred_element_type=jnp.float32
        ) + jnp.dot(normed[:, step:], came[...], preferred_element_type=jnp.float32)
        for i in range(3):
            unit, _ = unit_of(raw[:, at + i * dim : at + (i + 1) * dim])
            head = unit * gains[i // 2 : i // 2 + 1, :]
            head = (head * cosine[...] + turned(head) * sine[...]).astype(jnp.bfloat16)
            if i < 2:
                query[:, (2 * block + i) * dim : (2 * block + i + 1) * dim] = head
            else:
                key_value[:, 2 * block * dim : (2 * block + 1) * dim] = head
        key_value[:, (2 * block + 1) * dim : (2 * block + 2) * dim] = raw[
            :, at + 3 * dim : at + 4 * dim
        ].astype(jnp.bfloat16)


def window_scores(info, query, keys, part, scale):
    rows, columns = query.shape[0], keys.shape[0]
    half = columns - rows
    row = lax.broadcasted_iota(jnp.int32, (rows, columns), 0)
    column = lax.broadcasted_iota(jnp.int32, (rows, columns), 1)
    gap = column - row - half
    slot = column + ((info[0] - 1) * half + part * rows)
    allowed = (gap <= 0) & (gap > -half) & (slot >= 0) & ((slot < info[1]) | (gap == 0))
    return nt(query, keys) * scale, allowed


def key_columns(block, dim):
    key = slice(2 * block * dim, (2 * block + 1) * dim)
    value = slice((2 * block + 1) * dim, (2 * block + 2) * dim)
    return key, value


def seen_pair(before, own, part, block, dim):
    here, there = key_columns(block, dim), key_columns(1 - block, dim)
    rows = own.shape[0] // 2
    if part == 0:
        return [
            jnp.concatenate([before[:, t], own[:rows, h]], 0) for h, t in zip(here, there)
        ]
    return [jnp.concatenate([before[rows:, t], own[:, h]], 0) for h, t in zip(here, there)]


def attend_body(info, query, before, own, mixed, log_total):
    dim = own.shape[1] // 4
    rows = query.shape[0] // 2
    for part in range(2):
        at = slice(part * rows, (part + 1) * rows)
        for block in range(2):
            keys, values = seen_pair(before, own, part, block, dim)
            for head in (2 * block, 2 * block + 1):
                on = slice(head * dim, (head + 1) * dim)
                score, allowed = window_scores(info, query[at, on], keys, part, dim**-0.5)
                score = jnp.where(allowed, score, NEG)
                top = jnp.max(score, -1, keepdims=True)
                expo = jnp.exp(score - top)
                total = jnp.sum(expo, -1, keepdims=True)
                prob = (expo * (1.0 / total)).astype(jnp.bfloat16)
                mixed[at, on] = jnp.dot(
                    prob, values, preferred_element_type=jnp.float32
                ).astype(jnp.bfloat16)
                log_total[at, on] = jnp.broadcast_to(top + jnp.log(total), (rows, dim))


def attend_back_body(
    info, query, before, own, log_total, grad_resid, weight0, weight1, raw, cosine, sine, gain,
    grad_query, grad_own, grad_before, gain_part, grad_keys, grad_values, grad_mixed,
):
    dim = own.shape[1] // 4
    rows = query.shape[0] // 2
    scale = dim**-0.5
    gain_total = jnp.zeros((1, dim), jnp.float32)
    for block, weight in enumerate((weight0, weight1)):
        on = slice(2 * block * dim, 2 * (block + 1) * dim)
        grad_mixed[:, on] = jnp.dot(
            grad_resid[...], weight[...], preferred_element_type=jnp.float32
        ).astype(jnp.bfloat16)
        grad_keys[...] = jnp.zeros_like(grad_keys)
        grad_values[...] = jnp.zeros_like(grad_values)
        for part in range(2):
            keys, values = seen_pair(before, own, part, block, dim)
            at = slice(part * rows, (part + 1) * rows)
            seen = slice(part * rows, part * rows + keys.shape[0])
            for head in (2 * block, 2 * block + 1):
                on = slice(head * dim, (head + 1) * dim)
                score, allowed = window_scores(info, query[at, on], keys, part, scale)
                prob = jnp.where(allowed, jnp.exp(score - log_total[at, on][:, :1]), 0.0)
                grad_prob = nt(grad_mixed[at, on], values)
                inner = jnp.sum(prob * grad_prob, -1, keepdims=True)
                grad_score = (prob * (grad_prob - inner)).astype(jnp.bfloat16)
                grad_values[seen, :] += tn(prob.astype(jnp.bfloat16), grad_mixed[at, on])
                grad_keys[seen, :] += tn(grad_score, query[at, on]) * scale
                back = jnp.dot(grad_score, keys, preferred_element_type=jnp.float32) * scale
                back = back * cosine[at, :] - turned(back) * sine[at, :]
                there = (2 * head - head % 2) * dim
                unit, inverse = unit_of(raw[at, there : there + dim])
                gain_total += jnp.sum(unit * back, 0, keepdims=True)
                back = back * gain[...]
                back = inverse * (back - unit * jnp.mean(back * unit, -1, keepdims=True))
                grad_query[at, on] = back.astype(jnp.bfloat16)
        for grad, here, there in zip(
            (grad_keys, grad_values), key_columns(block, dim), key_columns(1 - block, dim)
        ):
            grad_before[:, there] = grad[: 2 * rows, :].astype(jnp.bfloat16)
            grad_own[:, here] = grad[2 * rows :, :]
    gain_part[...] = gain_total


def finish_body(grad_query, grad_own, came, raw, cosine, sine, gain, even, odd, gain_part):
    dim = cosine.shape[1]
    total = jnp.zeros((1, dim), jnp.float32)
    for block, out in enumerate((even, odd)):
        key, value = key_columns(block, dim)
        back = grad_own[:, key] + came[:, key].astype(jnp.float32)
        back = back * cosine[...] - turned(back) * sine[...]
        unit, inverse = unit_of(raw[:, (4 * block + 2) * dim : (4 * block + 3) * dim])
        total += jnp.sum(unit * back, 0, keepdims=True)
        back = back * gain[...]
        back = inverse * (back - unit * jnp.mean(back * unit, -1, keepdims=True))
        out[:, : 2 * dim] = grad_query[:, 2 * block * dim : (2 * block + 2) * dim]
        out[:, 2 * dim : 3 * dim] = back.astype(jnp.bfloat16)
        grad_value = grad_own[:, value] + came[:, value].astype(jnp.float32)
        out[:, 3 * dim :] = grad_value.astype(jnp.bfloat16)
    gain_part[...] = total


def vmem_call(body, outs, scratch=(), scalars=0, name=None):
    def call(*args):
        in_specs = [
            pl.BlockSpec(memory_space=pltpu.SMEM if i < scalars else pltpu.VMEM)
            for i in range(len(args))
        ]
        return pl.pallas_call(
            body,
            grid=(1,),
            out_shape=outs,
            in_specs=in_specs,
            out_specs=jax.tree.map(lambda _: pl.BlockSpec(memory_space=pltpu.VMEM), outs),
            scratch_shapes=scratch,
            compiler_params=pltpu.CompilerParams(vmem_limit_bytes=VMEM_BYTES),
        cost_estimate=FREE,
            name=name,
        )(*args)

    return call


def hidden_units(mids, grads_y, weights):
    width, units = weights.shape[0], weights.shape[1] // 3
    count = len(mids)
    heights = [m.shape[0] for m in mids]
    rows, cut = sum(heights), units // 3

    def body(*refs):
        gate_w, up_w, w_down, act, grad_gate, grad_up = refs[2 * count :]
        start = 0
        for mid, grad_y in zip(refs[:count], refs[count : 2 * count]):
            at = slice(start, start + mid.shape[0])
            start += mid.shape[0]
            gate = jnp.dot(mid[...], gate_w[...], preferred_element_type=jnp.float32)
            up = jnp.dot(mid[...], up_w[...], preferred_element_type=jnp.float32)
            grad_act = jnp.dot(grad_y[...], w_down[...], preferred_element_type=jnp.float32)
            sigma = jax.nn.sigmoid(gate)
            swish = gate * sigma
            act[at, :] = (swish * up).astype(jnp.bfloat16)
            slope = grad_act * up * sigma * (1.0 + gate * (1.0 - sigma))
            grad_gate[at, :] = slope.astype(jnp.bfloat16)
            grad_up[at, :] = (grad_act * swish).astype(jnp.bfloat16)

    row_specs = [
        pl.BlockSpec((h, width), lambda j: (0, 0), pipeline_mode=pl.Buffered(1)) for h in heights
    ]
    return pl.pallas_call(
        body,
        grid=(3,),
        out_shape=[jax.ShapeDtypeStruct((rows, units), jnp.bfloat16)] * 3,
        in_specs=[
            *row_specs,
            *row_specs,
            pl.BlockSpec((width, cut), lambda j: (0, j)),
            pl.BlockSpec((width, cut), lambda j: (0, j + 3)),
            pl.BlockSpec((width, cut), lambda j: (0, j + 6)),
        ],
        out_specs=[pl.BlockSpec((rows, cut), lambda j: (0, j))] * 3,
        compiler_params=pltpu.CompilerParams(vmem_limit_bytes=VMEM_BYTES),
        cost_estimate=FREE,
        name="hidden_units",
    )(*mids, *grads_y, weights, weights, weights)


def from_hidden(pairs, eighths):
    count, parts = len(pairs), len(eighths)
    rows, units = pairs[0][0].shape[0] // 8, pairs[0][0].shape[1]
    width = pairs[0][1].shape[0]
    cut = width // 4

    def body(*refs):
        ins, outs = refs[: -(parts // 2)], refs[-(parts // 2) :]
        total = 0.0
        for i in range(count):
            part = ins[i * (parts + 1) : (i + 1) * (parts + 1)]
            left = jnp.concatenate([p[...] for p in part[:-1]], 0)
            total = total + nt(left, part[-1][...])
        for i, out in enumerate(outs):
            out[...] = total[2 * i * rows : 2 * (i + 1) * rows].astype(jnp.bfloat16)

    specs, args = [], []
    for left, right, at in pairs:
        specs += [pl.BlockSpec((rows, units), lambda j, e=e: (e, 0)) for e in eighths]
        specs.append(pl.BlockSpec((cut, units), lambda j, at=at: (j, at)))
        args += [left] * parts + [right]
    return pl.pallas_call(
        body,
        grid=(4,),
        out_shape=[jax.ShapeDtypeStruct((2 * rows, width), jnp.bfloat16)] * (parts // 2),
        in_specs=specs,
        out_specs=[pl.BlockSpec((2 * rows, cut), lambda j: (0, j))] * (parts // 2),
        compiler_params=pltpu.CompilerParams(vmem_limit_bytes=VMEM_BYTES),
        cost_estimate=FREE,
        name="from_hidden",
    )(*args)


def row_outer(lefts, groups, first, tiles, added=None, places=None):
    rights = [right for group in groups for right in group]
    places = range(len(rights)) if places is None else places
    added = [] if added is None else [added] * len(rights)
    width = lefts[0].shape[1]
    tile = width // 8
    count = len(lefts)
    rows = sum(left.shape[0] for left in lefts)
    columns = [sum(right.shape[1] for right in group) for group in groups]

    def body(*refs):
        left_refs = refs[:count]
        right_refs = refs[count : count + len(rights)]
        add_refs = refs[count + len(rights) : count + len(rights) + len(added)]
        outs = refs[count + len(rights) + len(added) :]
        place = 0
        for i, group in enumerate(groups):
            column = 0
            for right in group:
                on = slice(column, column + right.shape[1])
                total, start = 0.0, 0
                for left in left_refs:
                    stop = start + left.shape[0]
                    total = total + tn(left[...], right_refs[place][start:stop, :])
                    start = stop
                if added:
                    total = total + add_refs[place][...].astype(jnp.float32)
                outs[i][:, on] = total.astype(jnp.bfloat16)
                place += 1
                column += right.shape[1]

    return pl.pallas_call(
        body,
        grid=(tiles,),
        out_shape=[jax.ShapeDtypeStruct((tiles * tile, c), jnp.bfloat16) for c in columns],
        in_specs=[
            *(pl.BlockSpec((left.shape[0], tile), lambda j: (0, j + first)) for left in lefts),
            *(
                pl.BlockSpec(right.shape, lambda j: (0, 0), pipeline_mode=pl.Buffered(1))
                for right in rights
            ),
            *(
                pl.BlockSpec((tile, rights[0].shape[1]), lambda j, at=at: (j + first, at))
                for at in places[: len(added)]
            ),
        ],
        out_specs=[pl.BlockSpec((tile, c), lambda j: (j, 0)) for c in columns],
        compiler_params=pltpu.CompilerParams(vmem_limit_bytes=VMEM_BYTES),
        cost_estimate=pl.CostEstimate(
            flops=2 * rows * tiles * tile * sum(columns),
            bytes_accessed=2 * rows * (width + sum(columns)),
            transcendentals=0,
        ),
        name="row_outer",
    )(*lefts, *rights, *added)


def close_body(x, *refs):
    mixed, weights = refs[:4], refs[4:12]
    gains, resid, mid = refs[12:]
    at = pl.program_id(0)
    step = x.shape[1]
    columns = weights[0].shape[1]
    total = x[...].astype(jnp.float32)
    for i in range(8):
        part = mixed[i // 2][:, (i % 2) * columns : (i % 2 + 1) * columns]
        total = total + nt(part, weights[i][...])
    resid[:, pl.ds(pl.multiple_of(at * step, step), step)] = total

    @pl.when(at == 3)
    def _():
        unit, _ = unit_of(resid[...])
        mid[...] = (unit * gains[...]).astype(jnp.bfloat16)


def close_attention(x, mixed, weights, gains):
    rows, width = x.shape
    step = width // 4
    whole = lambda a: pl.BlockSpec(a.shape, lambda j: (0, 0))
    return pl.pallas_call(
        close_body,
        grid=(4,),
        out_shape=[
            jax.ShapeDtypeStruct((rows, width), jnp.float32),
            jax.ShapeDtypeStruct((rows, width), jnp.bfloat16),
        ],
        in_specs=[
            pl.BlockSpec((rows, step), lambda j: (0, j)),
            *(whole(m) for m in mixed),
            *(pl.BlockSpec((step, w.shape[1]), lambda j: (j, 0)) for w in weights),
            whole(gains),
        ],
        out_specs=[pl.BlockSpec((rows, width), lambda j: (0, 0))] * 2,
        compiler_params=pltpu.CompilerParams(vmem_limit_bytes=VMEM_BYTES),
        cost_estimate=FREE,
        name="close_attention",
    )(x, *mixed, *weights, gains)


def back_to_rows(blocks, weights):
    rows = blocks[0].shape[0]
    step, columns = weights[0][0].shape
    count = len(blocks)

    def body(*refs):
        lefts = refs[:count]
        hbm = refs[count : 3 * count]
        out = refs[3 * count]
        held, sems = refs[3 * count + 1 :]
        copies = []
        for i in range(count):
            own, came = hbm[2 * i : 2 * i + 2]
            copies.append(
                [
                    pltpu.make_async_copy(own, held.at[i, :step], sems.at[i, 0]),
                    pltpu.make_async_copy(came, held.at[i, step:], sems.at[i, 1]),
                ]
            )
        for some in copies:
            for copy in some:
                copy.start()
        for i in range(count):
            for copy in copies[i]:
                copy.wait()
            for k in range(4):
                on = slice(k * step, (k + 1) * step)
                part = nt(lefts[i][...], held[i, on])
                if i == 0:
                    out[:, on] = part
                else:
                    out[:, on] += part

    return pl.pallas_call(
        body,
        grid=(1,),
        out_shape=jax.ShapeDtypeStruct((rows, 4 * step), jnp.float32),
        in_specs=[pl.BlockSpec(memory_space=pltpu.VMEM)] * count
        + [pl.BlockSpec(memory_space=pl.ANY)] * (2 * count),
        out_specs=pl.BlockSpec(memory_space=pltpu.VMEM),
        scratch_shapes=[
            pltpu.VMEM((count, 4 * step, columns), jnp.bfloat16),
            pltpu.SemaphoreType.DMA((count, 2)),
        ],
        compiler_params=pltpu.CompilerParams(vmem_limit_bytes=VMEM_BYTES),
        cost_estimate=FREE,
        name="back_to_rows",
    )(*blocks, *(part for w in weights for part in w))


def on_device_block(
    tokens,
    lengths,
    attn_gain,
    w_query,
    key_matrix,
    value_matrix,
    query_gain,
    key_gain,
    w_out,
    mlp_gain,
    w_gate,
    w_up,
    w_down,
    cotangent,
):
    low, full = jnp.bfloat16, jnp.float32
    width = tokens.shape[2]
    head_dim = query_gain.shape[0]
    shards = lax.axis_size("shard")
    shard_at = lax.axis_index("shard")
    me = lax.axis_index("rep")
    core = me & 1
    count = lax.axis_size("rep")

    s = Stage(tokens=tokens, cotangent=cotangent)
    piece = width // shards

    s.own_blocks = [
        column_block((w_query, key_matrix, value_matrix), me ^ i) for i in range(8)
    ]
    gain_rows = jnp.concatenate(
        [jnp.stack([attn_gain, mlp_gain]), jnp.zeros((14, piece), low)], 0
    )
    travelling = jnp.concatenate([s.own_blocks[0], gain_rows], 0)
    s.out_block = column_block((w_out,), me)
    s.ffn_block = column_block((w_gate, w_up, w_down), me)
    s.before, s.behind = around(travelling, 1), around(travelling, -1)
    s.other_lengths = across(lengths, CORE)
    s.end()

    s.ahead = around(s.before, 1)
    tokens_sent = to_sequences_send(s.tokens)
    out_own = lax.all_gather(s.out_block, "shard", axis=0, tiled=True)
    s.end("out_block", "tokens")

    parts = (s.before, s.ahead, s.behind)
    s.came = jnp.concatenate([part[:piece] for part in parts], 0)
    s.gains = jnp.concatenate([gain_rows[:2], *(part[piece : piece + 2] for part in parts)], 1)
    s.came_near = near(s.came)
    s.x_came = tokens_sent
    s.end("before", "behind", "ahead")

    s.came_far = far(*s.came_near)
    s.came_other = [across(block, CORE) for block in (s.came, *s.came_near)]
    gains = rolled(s.gains.astype(full))
    s.mlp_gains = gains[1:]
    s.attn_gains = gains[:1]
    s.x_low = jnp.concatenate(in_turn(s.x_came), 0)
    rows = s.x_low.shape[0]
    x_rows = s.x_low.astype(full)
    s.inverse_in = lax.rsqrt(jnp.mean(x_rows * x_rows, -1, keepdims=True) + EPS)
    s.normed = rolled((x_rows * s.inverse_in * s.attn_gains).astype(low))
    query_gains = query_gain.astype(full)[None]
    key_gains = key_gain.astype(full)[None]
    s.head_gains = jnp.concatenate([query_gains, key_gains], 0)
    both = jnp.where(
        core == 0,
        jnp.concatenate([lengths, s.other_lengths]),
        jnp.concatenate([s.other_lengths, lengths]),
    )
    length = lax.dynamic_index_in_dim(both, shard_at, 0, keepdims=False)
    s.info = jnp.stack([core, length]).astype(jnp.int32)
    query_pos = core * rows + jnp.arange(rows, dtype=jnp.int32)
    s.valid = (query_pos < length)[:, None].astype(full)
    cosine, sine = tables(query_pos, head_dim)
    s.cosine, sine = cosine[0, :, 0], sine[0, :, 0]
    s.sine = jnp.concatenate([-sine[:, : head_dim // 2], sine[:, head_dim // 2 :]], 1)
    s.out_own = out_own
    s.end("gains", "x_came", "other_lengths")

    head_columns = 2 * head_dim
    block_columns = 4 * head_dim
    quad_rows = jax.ShapeDtypeStruct((rows, block_columns), low)
    quad_sums = jax.ShapeDtypeStruct((rows, block_columns), full)
    gain_sum = jax.ShapeDtypeStruct((1, head_dim), full)
    project = vmem_call(
        project_body,
        [jax.ShapeDtypeStruct((rows, 2 * block_columns), full), quad_rows, quad_rows],
        name="project",
    )
    attend = vmem_call(attend_body, [quad_rows, quad_sums], scalars=1, name="attend")
    attend_back = vmem_call(
        attend_back_body,
        [quad_rows, quad_sums, quad_rows, gain_sum],
        scratch=[pltpu.VMEM((2 * rows, head_dim), full)] * 2
        + [pltpu.VMEM((rows, block_columns), low)],
        scalars=1,
        name="attend_back",
    )
    finish = vmem_call(finish_body, [quad_rows, quad_rows, gain_sum], name="finish")
    upward = [(i, i + 1) for i in range(0, count, 2)]
    downward = [(i + 1, i) for i in range(0, count, 2)]

    def project_call(i, came, other):
        return (
            project, s.normed, s.own_blocks[2 * i], came, s.own_blocks[2 * i + 1], other,
            s.cosine, s.sine, s.head_gains,
        )

    ffn_own = lax.all_gather(s.ffn_block, "shard", axis=0, tiled=True)
    came_last = jnp.concatenate(s.came_far, 0)
    s.came_last = (came_last, across(came_last, CORE))
    s.out_near = near(s.out_own)
    s.projected = in_order(
        [
            project_call(i, block, other)
            for i, (block, other) in enumerate(zip((s.came, *s.came_near), s.came_other))
        ]
    )
    s.end("came_far", "ffn_block")

    s.out_far = far(*s.out_near)
    s.earlier = [lax.ppermute(p[2], "rep", upward) for p in s.projected]
    s.projected_last = project_call(3, *s.came_last)[0](*project_call(3, *s.came_last)[1:])
    s.end()

    out_chips = (s.out_own, *s.out_near, jnp.concatenate(s.out_far, 0))
    s.out_chips = [(block, across(block, CORE)) for block in out_chips]
    s.earlier_last = lax.ppermute(s.projected_last[2], "rep", upward)

    def attend_call(projected, earlier):
        return (
            lambda query, own, before: attend(s.info, query, before, own),
            *projected[1:], earlier,
        )

    s.attended = in_order([attend_call(*pair) for pair in zip(s.projected, s.earlier)])
    s.end("out_own", "out_near", "out_far")

    grad_y_sent = to_sequences_send(s.cotangent)
    s.projected = [*s.projected, s.projected_last]
    s.earlier = [*s.earlier, s.earlier_last]
    s.out_blocks = [block for chip in s.out_chips for block in chip]
    (last,) = in_order([attend_call(s.projected_last, s.earlier_last)])
    s.attended = [*s.attended, last]
    s.mixed = [a[0] for a in s.attended]
    s.resid, s.mid = close_attention(s.x_low, s.mixed, s.out_blocks, s.mlp_gains)
    s.end("out_chips", "projected_last", "earlier_last", "cotangent")

    s.mid_near = near(s.mid)
    s.grad_y_came = grad_y_sent
    s.end()

    s.mid_far = far(*s.mid_near)
    grad_y = jnp.concatenate(in_turn(s.grad_y_came), 0)
    s.grad_y = jnp.where(s.valid > 0, grad_y, jnp.zeros_like(grad_y))
    s.grad_y_near = near(s.grad_y)
    s.ffn_own = ffn_own
    s.end("grad_y_came")

    s.grad_y_far = far(*s.grad_y_near)
    s.end()

    s.mids = [s.mid, *s.mid_near, *s.mid_far]
    s.grads_y = [s.grad_y, *s.grad_y_near, *s.grad_y_far]
    s.ffn_other = across(s.ffn_own, CORE)
    units = s.ffn_own.shape[1] // 3
    s.hidden_own = hidden_units(s.mids, s.grads_y, s.ffn_own)
    s.end("mid", "mid_near", "mid_far", "grad_y_near", "grad_y_far")

    def hidden_pairs(own, other, first, last):
        return [
            (hidden[i], weights, at)
            for hidden, weights in ((own, s.ffn_own), (other, s.ffn_other))
            for at, i in enumerate(range(first, last))
        ]

    def gate_up_pairs(other):
        return hidden_pairs(s.hidden_own, other, 1, 3)

    def down_pairs():
        return [(s.hidden_own[0], s.ffn_own, 2), (s.hidden_other[0], s.ffn_other, 2)]

    def from_hidden_call(pairs, eighths):
        return (
            lambda first: from_hidden([(first, *pairs[0][1:]), *pairs[1:]], eighths),
            pairs[0][0],
        )

    def outer_call(lefts, rights, *added):
        return lambda first: row_outer(lefts, [[first, *rights[1:]]], 0, 8, *added)[0], rights[0]

    to_plane, rest_of_plane = (2, 6, 5, 7), (3, 4, 0, 1)
    s.hidden_other = hidden_units(s.mids, s.grads_y, s.ffn_other)
    s.mid_sent = from_hidden(gate_up_pairs(s.hidden_other), to_plane)
    s.end()

    def send_near(sent):
        return across(sent[0], ACROSS_X), across(sent[1], ACROSS_Y)

    def send_far(came, rest, split):
        one_tail, two_head = rest
        return (
            across(rounded_sum(one_tail, split(came[1])[1]), ACROSS_X),
            across(rounded_sum(two_head, split(came[0])[1]), ACROSS_Y),
        )

    def total(came, came_far, own, split):
        head, tail = own
        full_sum = lambda *parts: sum(part.astype(full) for part in parts)
        return jnp.concatenate(
            [
                full_sum(head, split(came[0])[0], came_far[1]),
                full_sum(tail, split(came[1])[0], came_far[0]),
            ],
            0,
        )

    by_rows = lambda a: jnp.split(a, 2, 0)
    by_columns = lambda a: jnp.split(a, 2, 1)

    s.mid_came = send_near(s.mid_sent)
    s.mid_rest, s.down_outer, s.gate_up_outer = in_order(
        [
            from_hidden_call(gate_up_pairs(s.hidden_other), rest_of_plane),
            outer_call(s.grads_y, s.hidden_other[:1]),
            outer_call(s.mids, s.hidden_other[1:]),
        ]
    )
    s.end("mid_sent")

    s.mid_came_far = send_far(s.mid_came, by_rows(s.mid_rest[0]), by_rows)
    s.down_came = across(s.down_outer, CORE)
    s.gate_up_came = across(s.gate_up_outer, CORE)
    s.mlp_sent, s.mlp_rest = in_order(
        [
            from_hidden_call(down_pairs(), to_plane),
            from_hidden_call(down_pairs(), rest_of_plane),
        ]
    )
    s.end("down_outer", "gate_up_outer")

    mlp_came = send_near(s.mlp_sent)
    grad_mid = total(s.mid_came, s.mid_came_far, by_rows(s.mid_rest[1]), by_rows)
    inverse_mid = lax.rsqrt(jnp.mean(s.resid * s.resid, -1, keepdims=True) + EPS)
    mid_unit = s.resid * inverse_mid
    s.mlp_gain_part = jnp.sum(mid_unit * grad_mid, 0)
    s.grad_resid = s.grad_y.astype(full) + norm_back(
        mid_unit, inverse_mid, grad_mid * s.mlp_gains
    )
    s.resid_low = s.grad_resid.astype(low)
    s.resid_rolled = rolled(s.resid_low)
    (s.down_mine,) = in_order([outer_call(s.grads_y, s.hidden_own[:1], s.down_came)])
    s.end("mid_came", "mid_came_far", "mid_rest", "down_came")

    def back_call(i):
        raw, query, own_pair = s.projected[i]
        return (
            lambda query, *rest: attend_back(s.info, query, *rest),
            query, s.earlier[i], own_pair, s.attended[i][1], s.resid_low,
            *s.out_blocks[2 * i : 2 * i + 2], raw, s.cosine, s.sine, s.head_gains[:1],
        )

    def finish_call(i):
        return (
            finish, s[f"back{i}"][0], s[f"back{i}"][1], s[f"returned{i}"], s.projected[i][0],
            s.cosine, s.sine, s.head_gains[1:],
        )

    def give_back(*chips):
        for i in chips:
            s[f"returned{i}"] = lax.ppermute(s[f"back{i}"][2], "rep", downward)

    def odd_call(left, blocks):
        return lambda first: row_outer([first], [blocks], 0, 8)[0], left

    def head_call(left, blocks, came):
        groups = [[blocks[1], blocks[3]], [blocks[2]], [blocks[0]]]
        return lambda first: row_outer([first], groups, 0, 4, came, (1, 3, 2, 0)), left

    def tail_call(left, blocks, came):
        groups = [[blocks[2], blocks[3]], [blocks[1]], [blocks[0]]]
        return lambda first: row_outer([first], groups, 4, 4, came, (2, 3, 1, 0)), left

    down_total = lax.psum_scatter(s.down_mine, "shard", scatter_dimension=0, tiled=True)
    mixed_even = [m[:, :head_columns] for m in s.mixed]
    mixed_odd = [m[:, head_columns:] for m in s.mixed]
    s.out_odd, s.back3 = in_order([odd_call(s.resid_rolled, mixed_odd), back_call(3)])
    s.mlp_came = mlp_came
    s.end("down_mine")

    s.mlp_came_far = send_far(s.mlp_came, by_rows(s.mlp_rest[0]), by_rows)
    s.out_came = across(s.out_odd, CORE)
    give_back(3)
    s.back1, s.back2 = in_order([back_call(1), back_call(2)])
    s.end("out_odd", "mlp_sent")

    give_back(1, 2)
    mlp_out = total(s.mlp_came, s.mlp_came_far, by_rows(s.mlp_rest[1]), by_rows)
    s.output = (s.valid * (s.resid + mlp_out)).astype(low)
    s.out_head, s.out_tail, s.back0, s.finished3 = in_order(
        [
            head_call(s.resid_rolled, mixed_even, s.out_came),
            tail_call(s.resid_rolled, mixed_even, s.out_came),
            back_call(0),
            finish_call(3),
        ]
    )
    s.end("mlp_came", "mlp_came_far", "mlp_rest", "out_came", "resid")

    output_sent = from_sequences_send(s.output)
    s.out_near = send_near((s.out_head[0], s.out_tail[0]))
    give_back(0)
    s.gate_up_mine, s.finished1, s.finished2 = in_order(
        [
            outer_call(s.mids, s.hidden_own[1:], s.gate_up_came),
            finish_call(1),
            finish_call(2),
        ]
    )
    s.end("gate_up_came", "hidden_own", "hidden_other", "output")

    gate_up_total = lax.psum_scatter(s.gate_up_mine, "shard", scatter_dimension=0, tiled=True)
    s.out_far = send_far(s.out_near, (s.out_tail[1], s.out_head[1]), by_columns)
    ((s.finished0),) = in_order([finish_call(0)])
    s.finished = [s.finished0, s.finished1, s.finished2, s.finished3]
    (s.qkv_odd,) = in_order([odd_call(s.normed, [f[1] for f in s.finished])])
    s.down_total = down_total
    s.output_came = output_sent
    s.end("gate_up_mine", "finished0", "finished1", "finished2", "finished3")

    s.qkv_came = across(s.qkv_odd, CORE)
    s.down_near = near(s.down_total)
    out_sum = total(s.out_near, s.out_far, (s.out_head[2], s.out_tail[2]), by_columns)
    s.out_chunks = jnp.split(out_sum.astype(low), shards, 0)
    s.out_ring = ring_sum_first(s.out_chunks)
    grad_in = rolled(
        back_to_rows(
            [part for f in s.finished for part in f[:2]],
            [
                pair
                for i, block in enumerate(zip((s.came, *s.came_near), s.came_other))
                for pair in ((s.own_blocks[2 * i], block[0]), (s.own_blocks[2 * i + 1], block[1]))
            ]
            + [(s.own_blocks[6 + i], s.came_last[i]) for i in range(2)],
        )
    )
    x_unit = s.x_low.astype(full) * s.inverse_in
    s.attn_gain_part = jnp.sum(x_unit * grad_in, 0)
    s.grad_tokens = (
        s.grad_resid + norm_back(x_unit, s.inverse_in, grad_in * s.attn_gains)
    ).astype(low)
    s.end("qkv_odd", "out_near", "out_far", "out_head", "out_tail")

    s.down_far = far(*s.down_near)
    s.out_ring_last = around(rounded_sum(s.out_chunks[3], s.out_ring[0]), 1)
    grad_tokens_sent = from_sequences_send(s.grad_tokens)
    s.qkv_head, s.qkv_tail = in_order(
        [
            head_call(s.normed, [f[0] for f in s.finished], s.qkv_came),
            tail_call(s.normed, [f[0] for f in s.finished], s.qkv_came),
        ]
    )
    s.gain_parts = jnp.concatenate(
        [
            s.attn_gain_part,
            s.mlp_gain_part,
            sum(s[f"back{i}"][3] for i in range(4))[0],
            sum(f[2] for f in s.finished)[0],
        ]
    )
    s.end("qkv_came", "grad_tokens", "finished")

    my_group = me.astype(jnp.int32)[None]

    def whole(spread, widths):
        return whole_columns(my_group, *spread, widths)

    s.qkv_near = send_near((s.qkv_head[0], s.qkv_tail[0]))
    s.down_own = jnp.concatenate([s.down_total, *s.down_near, *s.down_far], 0)
    s.down_other = across(s.down_own, CORE)
    s.out_total = rounded_sum(s.out_chunks[0], s.out_ring[1], s.out_ring_last)
    s.gain_came = across(s.gain_parts, CORE)
    s.tokens_came = grad_tokens_sent
    s.end("out_chunks", "out_ring", "out_ring_last")

    s.qkv_far = send_far(s.qkv_near, (s.qkv_tail[1], s.qkv_head[1]), by_columns)
    s.gain_parts = s.gain_parts + s.gain_came
    s.gain_came = across(s.gain_parts, ACROSS_X)
    s.whole_down = whole((s.down_own, s.down_other), (units,))
    s.gate_up_total = gate_up_total
    s.end("down_own", "down_other")

    qkv_sum = total(s.qkv_near, s.qkv_far, (s.qkv_head[2], s.qkv_tail[2]), by_columns)
    s.qkv_chunks = jnp.split(qkv_sum.astype(low), shards, 0)
    s.qkv_ring = ring_sum_first(s.qkv_chunks)
    s.gate_up_near = near(s.gate_up_total)
    s.gain_parts = s.gain_parts + s.gain_came
    s.gain_came = across(s.gain_parts, ACROSS_Y)
    s.end("qkv_near", "qkv_far", "qkv_head", "qkv_tail")

    s.qkv_ring_last = around(rounded_sum(s.qkv_chunks[3], s.qkv_ring[0]), 1)
    s.gate_up_far = far(*s.gate_up_near)
    s.gain_parts = s.gain_parts + s.gain_came
    s.gain_came = lax.ppermute(s.gain_parts, "shard", [(i, i ^ 1) for i in range(shards)])
    s.end()

    qkv_total = rounded_sum(s.qkv_chunks[0], s.qkv_ring[1], s.qkv_ring_last)
    s.attn_total = jnp.concatenate([qkv_total, s.out_total], 1)
    s.attn_near = near(s.attn_total)
    s.gate_up_own = jnp.concatenate([s.gate_up_total, *s.gate_up_near, *s.gate_up_far], 0)
    s.gate_up_other = across(s.gate_up_own, CORE)
    s.gain_parts = s.gain_parts + s.gain_came
    s.gain_came = lax.ppermute(s.gain_parts, "shard", [(i, i ^ 2) for i in range(shards)])
    s.end("qkv_chunks", "qkv_ring", "qkv_ring_last", "gate_up_near", "gate_up_far")

    s.attn_far = far(*s.attn_near)
    s.whole_gate_up = whole((s.gate_up_own, s.gate_up_other), (units, units))
    s.end("gate_up_own", "gate_up_other")

    s.attn_own = jnp.concatenate([s.attn_total, *s.attn_near, *s.attn_far], 0)
    s.attn_other = across(s.attn_own, CORE)
    s.end()

    whole_query, whole_key, whole_value, whole_out = whole(
        (s.attn_own, s.attn_other), (head_columns, head_dim, head_dim, head_columns)
    )
    gain_sums = s.gain_parts + s.gain_came
    wide = lax.dynamic_slice_in_dim(
        gain_sums[: 2 * width].reshape(2, width), shard_at * piece, piece, 1
    )
    narrow = gain_sums[2 * width :]
    return (
        jnp.stack(in_turn(s.output_came)),
        jnp.stack(in_turn(s.tokens_came)),
        wide[0],
        whole_query,
        whole_key,
        whole_value,
        narrow[:head_dim],
        narrow[head_dim:],
        whole_out,
        wide[1],
        *s.whole_gate_up,
        *s.whole_down,
    )


def solution(mesh):
    sizes = (mesh.shape["rep"], mesh.shape["shard"])
    return jax.shard_map(
        on_device_block if sizes == (8, 4) else on_device,
        mesh=mesh,
        in_specs=(
            P("rep", "shard", None),
            P("rep"),
            P("shard"),
            P("shard", None),
            P("shard", None),
            P("shard", None),
            P(),
            P(),
            P("shard", None),
            P("shard"),
            P("shard", None),
            P("shard", None),
            P("shard", None),
            P("rep", "shard", None),
        ),
        out_specs=(
            P("rep", "shard", None),
            P("rep", "shard", None),
            P("shard"),
            P("shard", None),
            P("shard", None),
            P("shard", None),
            P(),
            P(),
            P("shard", None),
            P("shard"),
            P("shard", None),
            P("shard", None),
            P("shard", None),
        ),
        check_vma=False,
    )
```

```python
import jax
import jax.numpy as jnp
from jax import lax
from jax.experimental import pallas as pl
from jax.experimental.pallas import tpu as pltpu
from jax.sharding import PartitionSpec as P

WINDOW = 512


EPS = 1e-06
ROPE_BASE = 1000000.0
NEG = -1e30


def passed_along(x, axis, by):
    devices = lax.axis_size(axis)
    pairs = [(i, i + by) for i in range(devices) if 0 <= i + by < devices]
    return lax.ppermute(x, axis, pairs)


def tables(positions, head_dim):
    half = head_dim // 2
    freq = ROPE_BASE ** (-jnp.arange(half, dtype=jnp.float32) * 2.0 / head_dim)
    angle = positions.astype(jnp.float32)[:, None] * freq[None, :]
    angle = jnp.concatenate([angle, angle], -1)
    return (jnp.cos(angle)[None, :, None, :], jnp.sin(angle)[None, :, None, :])


def rotated_rows(value_rows):
    half = value_rows.shape[-1] // 2
    return jnp.concatenate([-value_rows[..., half:], value_rows[..., :half]], -1)


def head_norm(raw, gain):
    inverse = lax.rsqrt(jnp.mean(raw * raw, -1, keepdims=True) + EPS)
    unit = raw * inverse
    return (unit, inverse, unit * gain)


def norm_back(unit, inverse, grad_unit):
    return inverse * (grad_unit - unit * jnp.mean(grad_unit * unit, -1, keepdims=True))


def head_norm_back(unit, inverse, grad_normed, gain):
    grad_raw = norm_back(unit, inverse, grad_normed * gain)
    return (grad_raw, jnp.sum(unit * grad_normed, axis=(0, 1, 2)))


def scores(query_rows, keys, allowed, scale):
    raw = (
        jnp.einsum("sqhgd,skhd->shgqk", query_rows, keys, preferred_element_type=jnp.float32)
        * scale
    )
    return jnp.where(allowed[:, None, None], raw, NEG)


def outer(left, right):
    return jnp.einsum("rc,rf->cf", left, right, preferred_element_type=jnp.float32)


def on_device(
    tokens,
    lengths,
    attn_gain,
    w_query,
    key_matrix,
    value_matrix,
    query_gain,
    key_gain,
    w_out,
    mlp_gain,
    w_gate,
    w_up,
    w_down,
    cotangent,
):
    seq_count, piece, width = tokens.shape
    head_dim = query_gain.shape[0]
    heads_q = w_query.shape[1] // head_dim
    heads_kv = key_matrix.shape[1] // head_dim
    groups = heads_q // heads_kv
    rows = seq_count * piece
    scale = head_dim ** (-0.5)
    reach = (WINDOW + piece - 2) // piece
    owned = width // lax.axis_size("shard")
    shard_at = lax.axis_index("shard")
    query_pos = shard_at * piece + jnp.arange(piece, dtype=jnp.int32)
    key_pos = (shard_at - reach) * piece + jnp.arange((reach + 1) * piece, dtype=jnp.int32)
    near = (
        (key_pos[None, :] <= query_pos[:, None])
        & (query_pos[:, None] - key_pos[None, :] < WINDOW)
        & (key_pos[None, :] >= 0)
    )
    live = (key_pos[None, None, :] < lengths[:, None, None]) | (
        key_pos[None, :] == query_pos[:, None]
    )[None]
    allowed = near[None] & live
    valid = (query_pos[None, :] < lengths[:, None]).astype(jnp.float32).reshape(rows, 1)
    cosine_table, sine_table = tables(query_pos, head_dim)
    x_rows = tokens.astype(jnp.float32).reshape(rows, width)
    inverse_in = lax.rsqrt(jnp.mean(x_rows * x_rows, -1, keepdims=True) + EPS)
    x_unit = x_rows * inverse_in
    gain_piece = lax.all_gather(attn_gain, "shard", axis=0, tiled=True)
    query_piece = lax.all_gather(w_query, "shard", axis=0, tiled=True)
    key_piece = lax.all_gather(key_matrix, "shard", axis=0, tiled=True)
    value_piece = lax.all_gather(value_matrix, "shard", axis=0, tiled=True)
    normed_piece = (x_unit * gain_piece.astype(jnp.float32)).astype(jnp.bfloat16)
    acc_q = jnp.dot(normed_piece, query_piece, preferred_element_type=jnp.float32)
    acc_k = jnp.dot(normed_piece, key_piece, preferred_element_type=jnp.float32)
    acc_v = jnp.dot(normed_piece, value_piece, preferred_element_type=jnp.float32)
    normalized_rows = normed_piece
    gains = gain_piece.astype(jnp.float32)
    attn_in = normalized_rows
    attn_gains = gains
    query_unit, query_inverse, query_rows_normalized = head_norm(
        acc_q.reshape(seq_count, piece, heads_q, head_dim), query_gain.astype(jnp.float32)
    )
    key_unit, key_inverse, key_normed = head_norm(
        acc_k.reshape(seq_count, piece, heads_kv, head_dim), key_gain.astype(jnp.float32)
    )
    query_rows = (
        (query_rows_normalized * cosine_table + rotated_rows(query_rows_normalized) * sine_table)
        .astype(jnp.bfloat16)
        .reshape(seq_count, piece, heads_kv, groups, head_dim)
    )
    keys_own = (key_normed * cosine_table + rotated_rows(key_normed) * sine_table).astype(
        jnp.bfloat16
    )
    values_own = acc_v.reshape(seq_count, piece, heads_kv, head_dim).astype(jnp.bfloat16)
    own_pair = jnp.stack([keys_own, values_own])
    parts = []
    for fetch_back in range(reach, 0, -1):
        parts.append(passed_along(own_pair, "shard", fetch_back))
    parts.append(own_pair)
    near_pair = jnp.concatenate(parts, 2)
    score = scores(query_rows, near_pair[0], allowed, scale)
    top = jnp.max(score, -1, keepdims=True)
    expo = jnp.exp(score - top)
    total = jnp.sum(expo, -1, keepdims=True)
    prob = expo / total
    log_total = top + jnp.log(total)
    mixed = jnp.einsum(
        "shgqk,skhd->sqhgd",
        prob.astype(jnp.bfloat16),
        near_pair[1],
        preferred_element_type=jnp.float32,
    )
    mixed_rows = mixed.reshape(rows, heads_q * head_dim).astype(jnp.bfloat16)
    resid = x_rows + jnp.einsum(
        "rf,nf->rn",
        mixed_rows,
        lax.all_gather(w_out, "shard", axis=0, tiled=True),
        preferred_element_type=jnp.float32,
    )
    inverse_mid = lax.rsqrt(jnp.mean(resid * resid, -1, keepdims=True) + EPS)
    mid_unit = resid * inverse_mid
    gain_piece = lax.all_gather(mlp_gain, "shard", axis=0, tiled=True)
    gate_piece = lax.all_gather(w_gate, "shard", axis=0, tiled=True)
    up_piece = lax.all_gather(w_up, "shard", axis=0, tiled=True)
    normed_piece = (mid_unit * gain_piece.astype(jnp.float32)).astype(jnp.bfloat16)
    acc_gate = jnp.dot(normed_piece, gate_piece, preferred_element_type=jnp.float32)
    acc_up = jnp.dot(normed_piece, up_piece, preferred_element_type=jnp.float32)
    normalized_rows = normed_piece
    gains = gain_piece.astype(jnp.float32)
    mlp_in = normalized_rows
    sigma = jax.nn.sigmoid(acc_gate)
    swish = acc_gate * sigma
    act = (swish * acc_up).astype(jnp.bfloat16)
    mlp_out = jnp.einsum(
        "rf,nf->rn",
        act,
        lax.all_gather(w_down, "shard", axis=0, tiled=True),
        preferred_element_type=jnp.float32,
    )
    output = (valid * (resid + mlp_out)).astype(jnp.bfloat16).reshape(seq_count, piece, width)
    grad_y = cotangent.astype(jnp.float32).reshape(rows, width) * valid
    grad_y_low = grad_y.astype(jnp.bfloat16)
    grad_act = jnp.dot(
        grad_y_low,
        lax.all_gather(w_down, "shard", axis=0, tiled=True),
        preferred_element_type=jnp.float32,
    )
    grad_gate = (grad_act * acc_up * sigma * (1.0 + acc_gate * (1.0 - sigma))).astype(jnp.bfloat16)
    grad_up = (grad_act * swish).astype(jnp.bfloat16)
    gate_piece, up_piece = lax.all_gather((w_gate, w_up), "shard", axis=0, tiled=True)
    grad_mid = jnp.einsum(
        "rf,nf->rn", grad_gate, gate_piece, preferred_element_type=jnp.float32
    ) + jnp.einsum("rf,nf->rn", grad_up, up_piece, preferred_element_type=jnp.float32)
    grad_resid = grad_y + norm_back(mid_unit, inverse_mid, grad_mid * gains)
    mlp_gain_part = jnp.sum(mid_unit * grad_mid, 0)
    normalized_rows = mlp_in
    mlp_grads = jax.tree.map(
        lambda part: lax.psum_scatter(
            part.astype(jnp.bfloat16), "shard", scatter_dimension=0, tiled=True
        ).astype(jnp.float32),
        (
            outer(normalized_rows, grad_gate),
            outer(normalized_rows, grad_up),
            outer(grad_y_low, act),
        ),
    )
    resid_low = grad_resid.astype(jnp.bfloat16)
    grad_mixed = jnp.dot(
        resid_low,
        lax.all_gather(w_out, "shard", axis=0, tiled=True),
        preferred_element_type=jnp.float32,
    )
    grad_mixed = grad_mixed.astype(jnp.bfloat16).reshape(
        seq_count, piece, heads_kv, groups, head_dim
    )
    prob_again = jnp.exp(scores(query_rows, near_pair[0], allowed, scale) - log_total)
    grad_prob = jnp.einsum(
        "sqhgd,skhd->shgqk", grad_mixed, near_pair[1], preferred_element_type=jnp.float32
    )
    grad_values = jnp.einsum(
        "shgqk,sqhgd->skhd",
        prob_again.astype(jnp.bfloat16),
        grad_mixed,
        preferred_element_type=jnp.float32,
    )
    grad_score = (
        prob_again * (grad_prob - jnp.sum(prob_again * grad_prob, -1, keepdims=True))
    ).astype(jnp.bfloat16)
    grad_queries = (
        jnp.einsum(
            "shgqk,skhd->sqhgd", grad_score, near_pair[0], preferred_element_type=jnp.float32
        )
        * scale
    )
    grad_keys = (
        jnp.einsum("shgqk,sqhgd->skhd", grad_score, query_rows, preferred_element_type=jnp.float32)
        * scale
    )
    grad_pair = jnp.stack([grad_keys, grad_values])
    own_grad = grad_pair[:, :, reach * piece :]
    for back in range(1, reach + 1):
        lower = (reach - back) * piece
        own_grad = own_grad + passed_along(grad_pair[:, :, lower : lower + piece], "shard", -back)
    grad_query_post = grad_queries.reshape(seq_count, piece, heads_q, head_dim)
    grad_query_normed = grad_query_post * cosine_table - rotated_rows(grad_query_post * sine_table)
    grad_key_normed = own_grad[0] * cosine_table - rotated_rows(own_grad[0] * sine_table)
    grad_query_raw, query_gain_grad = head_norm_back(
        query_unit, query_inverse, grad_query_normed, query_gain.astype(jnp.float32)
    )
    grad_key_raw, key_gain_grad = head_norm_back(
        key_unit, key_inverse, grad_key_normed, key_gain.astype(jnp.float32)
    )
    grad_query_low = grad_query_raw.reshape(rows, heads_q * head_dim).astype(jnp.bfloat16)
    grad_key_low = grad_key_raw.reshape(rows, heads_kv * head_dim).astype(jnp.bfloat16)
    grad_value_low = own_grad[1].reshape(rows, heads_kv * head_dim).astype(jnp.bfloat16)
    query_piece, key_piece, value_piece = lax.all_gather(
        (w_query, key_matrix, value_matrix), "shard", axis=0, tiled=True
    )
    grad_in = (
        jnp.einsum("rf,nf->rn", grad_query_low, query_piece, preferred_element_type=jnp.float32)
        + jnp.einsum("rf,nf->rn", grad_key_low, key_piece, preferred_element_type=jnp.float32)
        + jnp.einsum("rf,nf->rn", grad_value_low, value_piece, preferred_element_type=jnp.float32)
    )
    grad_tokens = (
        (grad_resid + norm_back(x_unit, inverse_in, grad_in * attn_gains))
        .astype(jnp.bfloat16)
        .reshape(seq_count, piece, width)
    )
    attn_gain_part = jnp.sum(x_unit * grad_in, 0)
    normalized_rows = attn_in
    attn_grads = jax.tree.map(
        lambda part: lax.psum_scatter(
            part.astype(jnp.bfloat16), "shard", scatter_dimension=0, tiled=True
        ).astype(jnp.float32),
        (
            outer(normalized_rows, grad_query_low),
            outer(normalized_rows, grad_key_low),
            outer(normalized_rows, grad_value_low),
            outer(resid_low, mixed_rows),
        ),
    )
    head_grads = lax.psum(
        (query_gain_grad, key_gain_grad, attn_gain_part, mlp_gain_part), ("rep", "shard")
    )
    attn_gain_total = lax.dynamic_slice_in_dim(head_grads[2], shard_at * owned, owned, 0)
    mlp_gain_total = lax.dynamic_slice_in_dim(head_grads[3], shard_at * owned, owned, 0)
    summed = (
        lax.psum(attn_grads[0].astype(jnp.bfloat16), "rep").astype(jnp.float32),
        lax.psum(attn_grads[1].astype(jnp.bfloat16), "rep").astype(jnp.float32),
        lax.psum(attn_grads[2].astype(jnp.bfloat16), "rep").astype(jnp.float32),
        lax.psum(attn_grads[3].astype(jnp.bfloat16), "rep").astype(jnp.float32),
        lax.psum(mlp_grads[0].astype(jnp.bfloat16), "rep").astype(jnp.float32),
        lax.psum(mlp_grads[1].astype(jnp.bfloat16), "rep").astype(jnp.float32),
        lax.psum(mlp_grads[2].astype(jnp.bfloat16), "rep").astype(jnp.float32),
    )
    attn_grads = summed[:4]
    mlp_grads = summed[4:]
    return (
        output,
        grad_tokens,
        attn_gain_total,
        attn_grads[0],
        attn_grads[1],
        attn_grads[2],
        head_grads[0],
        head_grads[1],
        attn_grads[3],
        mlp_gain_total,
        mlp_grads[0],
        mlp_grads[1],
        mlp_grads[2],
    )


CORE, ACROSS_X, ACROSS_Y = 1, 2, 4
VMEM_BYTES = 56 * 2**20
FREE = pl.CostEstimate(flops=1, bytes_accessed=1, transcendentals=0)


def across(x, mask):
    count = lax.axis_size("rep")
    return lax.ppermute(x, "rep", [(i, i ^ mask) for i in range(count)])


def around(x, by):
    count = lax.axis_size("shard")
    return lax.ppermute(x, "shard", [(i, (i + by) % count) for i in range(count)])


class Stage(dict):
    __getattr__ = dict.__getitem__
    __setattr__ = dict.__setitem__
    __delattr__ = dict.__delitem__

    def end(self):
        self.update(lax.optimization_barrier(dict(self)))


def in_order(calls):
    outs = []
    for call, first, *rest in calls:
        if outs:
            last = outs[-1][0] if isinstance(outs[-1], (list, tuple)) else outs[-1]
            first = lax.optimization_barrier((first, last))[0]
        outs.append(call(first, *rest))
    return outs


def ring_chunks(x):
    count, at = lax.axis_size("shard"), lax.axis_index("shard")
    rows = x.shape[0] // count
    return [
        lax.dynamic_slice_in_dim(x, ((at - i) % count) * rows, rows, 0) for i in range(count)
    ]


def ring_sum_first(chunks):
    return around(chunks[2], 1), around(chunks[1], -1)


def near(piece):
    return across(piece, ACROSS_X), across(piece, ACROSS_Y)


def far(from_x, from_y):
    half = from_x.shape[0] // 2
    return across(from_x[:half], ACROSS_Y), across(from_y[half:], ACROSS_X)


def rounded_sum(*parts):
    return sum(part.astype(jnp.float32) for part in parts).astype(jnp.bfloat16)


def sequence_pairs(turn):
    groups, shards = lax.axis_size("rep"), lax.axis_size("shard")
    pairs = []
    for group in range(groups):
        chip, core = divmod(group, 2)
        for at in range(shards):
            to_group, to_shard = 2 * chip + at // 2, 2 * core + (turn ^ (at & 1))
            pairs.append((group * shards + at, to_group * shards + to_shard))
    return pairs


def rolled(x):
    count, at = lax.axis_size("shard"), lax.axis_index("shard")
    width = x.shape[1] // count
    return jnp.concatenate(
        [lax.dynamic_slice_in_dim(x, ((at - i) % count) * width, width, 1) for i in range(count)],
        1,
    )


def to_sequences_send(x):
    odd = lax.axis_index("shard") & 1
    return [
        lax.ppermute(
            lax.dynamic_index_in_dim(x, turn ^ odd, 0, keepdims=False),
            ("rep", "shard"),
            sequence_pairs(turn),
        )
        for turn in range(2)
    ]


def from_sequences_send(x):
    odd = lax.axis_index("shard") & 1
    x = x.reshape(2, x.shape[0] // 2, x.shape[1])
    return [
        lax.ppermute(
            lax.dynamic_index_in_dim(x, turn ^ odd, 0, keepdims=False),
            ("rep", "shard"),
            [(to, at) for at, to in sequence_pairs(turn)],
        )
        for turn in range(2)
    ]


def in_turn(came):
    even = lax.axis_index("shard") & 1 == 0
    return [jnp.where(even, came[0], came[1]), jnp.where(even, came[1], came[0])]


def column_block(weights, at):
    cuts = [w.shape[1] // 8 for w in weights]
    return jnp.concatenate(
        [lax.dynamic_slice_in_dim(w, at * cut, cut, 1) for w, cut in zip(weights, cuts)], 1
    )


def whole_columns(me, own, other, widths):
    rows, columns = own.shape[0] // 4, own.shape[1]

    def body(me_ref, own_ref, other_ref, *outs):
        def put(block):
            start = 0
            for out, width in zip(outs, widths):
                out[...] = block[:, start : start + width].astype(jnp.float32)
                start += width

        mine = (me_ref[0] ^ pl.program_id(0)) & 1 == 0
        pl.when(mine)(lambda: put(own_ref))
        pl.when(jnp.logical_not(mine))(lambda: put(other_ref))

    spec = pl.BlockSpec((rows, columns), lambda i, at: ((at[0] ^ i) >> 1, 0))
    return pl.pallas_call(
        body,
        grid_spec=pltpu.PrefetchScalarGridSpec(
            num_scalar_prefetch=1,
            grid=(8,),
            in_specs=[spec, spec],
            out_specs=[pl.BlockSpec((rows, w), lambda i, at: (0, i)) for w in widths],
        ),
        out_shape=[jax.ShapeDtypeStruct((rows, 8 * w), jnp.float32) for w in widths],
        compiler_params=pltpu.CompilerParams(vmem_limit_bytes=VMEM_BYTES),
        cost_estimate=FREE,
        name="whole_columns",
    )(me, own, other)


def turned(x):
    return pltpu.roll(x, x.shape[-1] // 2, x.ndim - 1)


def nt(left, right):
    return lax.dot_general(
        left, right, (((1,), (1,)), ((), ())), preferred_element_type=jnp.float32
    )


def tn(left, right):
    return lax.dot_general(
        left, right, (((0,), (0,)), ((), ())), preferred_element_type=jnp.float32
    )


def unit_of(raw):
    inverse = lax.rsqrt(jnp.mean(raw * raw, -1, keepdims=True) + EPS)
    return raw * inverse, inverse


def project_body(
    normed, own0, came0, own1, came1, cosine, sine, gains, raw, query, key_value
):
    step = own0.shape[0]
    dim = cosine.shape[1]
    for block, (own, came) in enumerate(((own0, came0), (own1, came1))):
        at = block * 4 * dim
        raw[:, at : at + 4 * dim] = jnp.dot(
            normed[:, :step], own[...], preferred_element_type=jnp.float32
        ) + jnp.dot(normed[:, step:], came[...], preferred_element_type=jnp.float32)
        for i in range(3):
            unit, _ = unit_of(raw[:, at + i * dim : at + (i + 1) * dim])
            head = unit * gains[i // 2 : i // 2 + 1, :]
            head = (head * cosine[...] + turned(head) * sine[...]).astype(jnp.bfloat16)
            if i < 2:
                query[:, (2 * block + i) * dim : (2 * block + i + 1) * dim] = head
            else:
                key_value[:, 2 * block * dim : (2 * block + 1) * dim] = head
        key_value[:, (2 * block + 1) * dim : (2 * block + 2) * dim] = raw[
            :, at + 3 * dim : at + 4 * dim
        ].astype(jnp.bfloat16)


def window_scores(info, query, keys, part, scale):
    rows, columns = query.shape[0], keys.shape[0]
    half = columns - rows
    row = lax.broadcasted_iota(jnp.int32, (rows, columns), 0)
    column = lax.broadcasted_iota(jnp.int32, (rows, columns), 1)
    gap = column - row - half
    slot = column + ((info[0] - 1) * half + part * rows)
    allowed = (gap <= 0) & (gap > -half) & (slot >= 0) & ((slot < info[1]) | (gap == 0))
    return nt(query, keys) * scale, allowed


def key_columns(block, dim):
    key = slice(2 * block * dim, (2 * block + 1) * dim)
    value = slice((2 * block + 1) * dim, (2 * block + 2) * dim)
    return key, value


def seen_pair(before, own, part, block, dim):
    here, there = key_columns(block, dim), key_columns(1 - block, dim)
    rows = own.shape[0] // 2
    if part == 0:
        return [
            jnp.concatenate([before[:, t], own[:rows, h]], 0) for h, t in zip(here, there)
        ]
    return [jnp.concatenate([before[rows:, t], own[:, h]], 0) for h, t in zip(here, there)]


def attend_body(info, query, before, own, mixed, log_total):
    dim = own.shape[1] // 4
    rows = query.shape[0] // 2
    for part in range(2):
        at = slice(part * rows, (part + 1) * rows)
        for block in range(2):
            keys, values = seen_pair(before, own, part, block, dim)
            for head in (2 * block, 2 * block + 1):
                on = slice(head * dim, (head + 1) * dim)
                score, allowed = window_scores(info, query[at, on], keys, part, dim**-0.5)
                score = jnp.where(allowed, score, NEG)
                top = jnp.max(score, -1, keepdims=True)
                expo = jnp.exp(score - top)
                total = jnp.sum(expo, -1, keepdims=True)
                prob = (expo * (1.0 / total)).astype(jnp.bfloat16)
                mixed[at, on] = jnp.dot(
                    prob, values, preferred_element_type=jnp.float32
                ).astype(jnp.bfloat16)
                log_total[at, on] = jnp.broadcast_to(top + jnp.log(total), (rows, dim))


def attend_back_body(
    info, query, before, own, log_total, grad_resid, weight0, weight1, raw, cosine, sine, gain,
    grad_query, grad_own, grad_before, gain_part, grad_keys, grad_values, grad_mixed,
):
    dim = own.shape[1] // 4
    rows = query.shape[0] // 2
    scale = dim**-0.5
    gain_total = jnp.zeros((1, dim), jnp.float32)
    for block, weight in enumerate((weight0, weight1)):
        on = slice(2 * block * dim, 2 * (block + 1) * dim)
        grad_mixed[:, on] = jnp.dot(
            grad_resid[...], weight[...], preferred_element_type=jnp.float32
        ).astype(jnp.bfloat16)
        grad_keys[...] = jnp.zeros_like(grad_keys)
        grad_values[...] = jnp.zeros_like(grad_values)
        for part in range(2):
            keys, values = seen_pair(before, own, part, block, dim)
            at = slice(part * rows, (part + 1) * rows)
            seen = slice(part * rows, part * rows + keys.shape[0])
            for head in (2 * block, 2 * block + 1):
                on = slice(head * dim, (head + 1) * dim)
                score, allowed = window_scores(info, query[at, on], keys, part, scale)
                prob = jnp.where(allowed, jnp.exp(score - log_total[at, on][:, :1]), 0.0)
                grad_prob = nt(grad_mixed[at, on], values)
                inner = jnp.sum(prob * grad_prob, -1, keepdims=True)
                grad_score = (prob * (grad_prob - inner)).astype(jnp.bfloat16)
                grad_values[seen, :] += tn(prob.astype(jnp.bfloat16), grad_mixed[at, on])
                grad_keys[seen, :] += tn(grad_score, query[at, on]) * scale
                back = jnp.dot(grad_score, keys, preferred_element_type=jnp.float32) * scale
                back = back * cosine[at, :] - turned(back) * sine[at, :]
                there = (2 * head - head % 2) * dim
                unit, inverse = unit_of(raw[at, there : there + dim])
                gain_total += jnp.sum(unit * back, 0, keepdims=True)
                back = back * gain[...]
                back = inverse * (back - unit * jnp.mean(back * unit, -1, keepdims=True))
                grad_query[at, on] = back.astype(jnp.bfloat16)
        for grad, here, there in zip(
            (grad_keys, grad_values), key_columns(block, dim), key_columns(1 - block, dim)
        ):
            grad_before[:, there] = grad[: 2 * rows, :].astype(jnp.bfloat16)
            grad_own[:, here] = grad[2 * rows :, :]
    gain_part[...] = gain_total


def finish_body(grad_query, grad_own, came, raw, cosine, sine, gain, even, odd, gain_part):
    dim = cosine.shape[1]
    total = jnp.zeros((1, dim), jnp.float32)
    for block, out in enumerate((even, odd)):
        key, value = key_columns(block, dim)
        back = grad_own[:, key] + came[:, key].astype(jnp.float32)
        back = back * cosine[...] - turned(back) * sine[...]
        unit, inverse = unit_of(raw[:, (4 * block + 2) * dim : (4 * block + 3) * dim])
        total += jnp.sum(unit * back, 0, keepdims=True)
        back = back * gain[...]
        back = inverse * (back - unit * jnp.mean(back * unit, -1, keepdims=True))
        out[:, : 2 * dim] = grad_query[:, 2 * block * dim : (2 * block + 2) * dim]
        out[:, 2 * dim : 3 * dim] = back.astype(jnp.bfloat16)
        grad_value = grad_own[:, value] + came[:, value].astype(jnp.float32)
        out[:, 3 * dim :] = grad_value.astype(jnp.bfloat16)
    gain_part[...] = total


def vmem_call(body, outs, scratch=(), scalars=0, name=None):
    def call(*args):
        in_specs = [
            pl.BlockSpec(memory_space=pltpu.SMEM if i < scalars else pltpu.VMEM)
            for i in range(len(args))
        ]
        return pl.pallas_call(
            body,
            grid=(1,),
            out_shape=outs,
            in_specs=in_specs,
            out_specs=jax.tree.map(lambda _: pl.BlockSpec(memory_space=pltpu.VMEM), outs),
            scratch_shapes=scratch,
            compiler_params=pltpu.CompilerParams(vmem_limit_bytes=VMEM_BYTES),
        cost_estimate=FREE,
            name=name,
        )(*args)

    return call


def hidden_units(mids, grads_y, weights):
    width, units = weights.shape[0], weights.shape[1] // 3
    count = len(mids)
    heights = [m.shape[0] for m in mids]
    rows, cut = sum(heights), units // 3

    def body(*refs):
        gate_w, up_w, w_down, act, grad_gate, grad_up = refs[2 * count :]
        start = 0
        for mid, grad_y in zip(refs[:count], refs[count : 2 * count]):
            at = slice(start, start + mid.shape[0])
            start += mid.shape[0]
            gate = jnp.dot(mid[...], gate_w[...], preferred_element_type=jnp.float32)
            up = jnp.dot(mid[...], up_w[...], preferred_element_type=jnp.float32)
            grad_act = jnp.dot(grad_y[...], w_down[...], preferred_element_type=jnp.float32)
            sigma = jax.nn.sigmoid(gate)
            swish = gate * sigma
            act[at, :] = (swish * up).astype(jnp.bfloat16)
            slope = grad_act * up * sigma * (1.0 + gate * (1.0 - sigma))
            grad_gate[at, :] = slope.astype(jnp.bfloat16)
            grad_up[at, :] = (grad_act * swish).astype(jnp.bfloat16)

    row_specs = [
        pl.BlockSpec((h, width), lambda j: (0, 0), pipeline_mode=pl.Buffered(1)) for h in heights
    ]
    return pl.pallas_call(
        body,
        grid=(3,),
        out_shape=[jax.ShapeDtypeStruct((rows, units), jnp.bfloat16)] * 3,
        in_specs=[
            *row_specs,
            *row_specs,
            pl.BlockSpec((width, cut), lambda j: (0, j)),
            pl.BlockSpec((width, cut), lambda j: (0, j + 3)),
            pl.BlockSpec((width, cut), lambda j: (0, j + 6)),
        ],
        out_specs=[pl.BlockSpec((rows, cut), lambda j: (0, j))] * 3,
        compiler_params=pltpu.CompilerParams(vmem_limit_bytes=VMEM_BYTES),
        cost_estimate=FREE,
        name="hidden_units",
    )(*mids, *grads_y, weights, weights, weights)


def from_hidden(pairs, eighths):
    count, parts = len(pairs), len(eighths)
    rows, units = pairs[0][0].shape[0] // 8, pairs[0][0].shape[1]
    width = pairs[0][1].shape[0]
    cut = width // 4

    def body(*refs):
        ins, outs = refs[: -(parts // 2)], refs[-(parts // 2) :]
        total = 0.0
        for i in range(count):
            part = ins[i * (parts + 1) : (i + 1) * (parts + 1)]
            left = jnp.concatenate([p[...] for p in part[:-1]], 0)
            total = total + nt(left, part[-1][...])
        for i, out in enumerate(outs):
            out[...] = total[2 * i * rows : 2 * (i + 1) * rows].astype(jnp.bfloat16)

    specs, args = [], []
    for left, right, at in pairs:
        specs += [pl.BlockSpec((rows, units), lambda j, e=e: (e, 0)) for e in eighths]
        specs.append(pl.BlockSpec((cut, units), lambda j, at=at: (j, at)))
        args += [left] * parts + [right]
    return pl.pallas_call(
        body,
        grid=(4,),
        out_shape=[jax.ShapeDtypeStruct((2 * rows, width), jnp.bfloat16)] * (parts // 2),
        in_specs=specs,
        out_specs=[pl.BlockSpec((2 * rows, cut), lambda j: (0, j))] * (parts // 2),
        compiler_params=pltpu.CompilerParams(vmem_limit_bytes=VMEM_BYTES),
        cost_estimate=FREE,
        name="from_hidden",
    )(*args)


def row_outer(lefts, groups, first, tiles, added=None, places=None):
    rights = [right for group in groups for right in group]
    places = range(len(rights)) if places is None else places
    added = [] if added is None else [added] * len(rights)
    width = lefts[0].shape[1]
    tile = width // 8
    count = len(lefts)
    rows = sum(left.shape[0] for left in lefts)
    columns = [sum(right.shape[1] for right in group) for group in groups]

    def body(*refs):
        left_refs = refs[:count]
        right_refs = refs[count : count + len(rights)]
        add_refs = refs[count + len(rights) : count + len(rights) + len(added)]
        outs = refs[count + len(rights) + len(added) :]
        place = 0
        for i, group in enumerate(groups):
            column = 0
            for right in group:
                on = slice(column, column + right.shape[1])
                total, start = 0.0, 0
                for left in left_refs:
                    stop = start + left.shape[0]
                    total = total + tn(left[...], right_refs[place][start:stop, :])
                    start = stop
                if added:
                    total = total + add_refs[place][...].astype(jnp.float32)
                outs[i][:, on] = total.astype(jnp.bfloat16)
                place += 1
                column += right.shape[1]

    return pl.pallas_call(
        body,
        grid=(tiles,),
        out_shape=[jax.ShapeDtypeStruct((tiles * tile, c), jnp.bfloat16) for c in columns],
        in_specs=[
            *(pl.BlockSpec((left.shape[0], tile), lambda j: (0, j + first)) for left in lefts),
            *(
                pl.BlockSpec(right.shape, lambda j: (0, 0), pipeline_mode=pl.Buffered(1))
                for right in rights
            ),
            *(
                pl.BlockSpec((tile, rights[0].shape[1]), lambda j, at=at: (j + first, at))
                for at in places[: len(added)]
            ),
        ],
        out_specs=[pl.BlockSpec((tile, c), lambda j: (j, 0)) for c in columns],
        compiler_params=pltpu.CompilerParams(vmem_limit_bytes=VMEM_BYTES),
        cost_estimate=pl.CostEstimate(
            flops=2 * rows * tiles * tile * sum(columns),
            bytes_accessed=2 * rows * (width + sum(columns)),
            transcendentals=0,
        ),
        name="row_outer",
    )(*lefts, *rights, *added)


def close_body(x, *refs):
    mixed, weights = refs[:4], refs[4:12]
    gains, resid, mid = refs[12:]
    at = pl.program_id(0)
    step = x.shape[1]
    columns = weights[0].shape[1]
    total = x[...].astype(jnp.float32)
    for i in range(8):
        part = mixed[i // 2][:, (i % 2) * columns : (i % 2 + 1) * columns]
        total = total + nt(part, weights[i][...])
    resid[:, pl.ds(pl.multiple_of(at * step, step), step)] = total

    @pl.when(at == 3)
    def _():
        unit, _ = unit_of(resid[...])
        mid[...] = (unit * gains[...]).astype(jnp.bfloat16)


def close_attention(x, mixed, weights, gains):
    rows, width = x.shape
    step = width // 4
    whole = lambda a: pl.BlockSpec(a.shape, lambda j: (0, 0))
    return pl.pallas_call(
        close_body,
        grid=(4,),
        out_shape=[
            jax.ShapeDtypeStruct((rows, width), jnp.float32),
            jax.ShapeDtypeStruct((rows, width), jnp.bfloat16),
        ],
        in_specs=[
            pl.BlockSpec((rows, step), lambda j: (0, j)),
            *(whole(m) for m in mixed),
            *(pl.BlockSpec((step, w.shape[1]), lambda j: (j, 0)) for w in weights),
            whole(gains),
        ],
        out_specs=[pl.BlockSpec((rows, width), lambda j: (0, 0))] * 2,
        compiler_params=pltpu.CompilerParams(vmem_limit_bytes=VMEM_BYTES),
        cost_estimate=FREE,
        name="close_attention",
    )(x, *mixed, *weights, gains)


def back_to_rows(blocks, weights):
    rows = blocks[0].shape[0]
    step, columns = weights[0][0].shape
    count = len(blocks)

    def body(*refs):
        lefts = refs[:count]
        hbm = refs[count : 3 * count]
        out = refs[3 * count]
        held, sems = refs[3 * count + 1 :]
        copies = []
        for i in range(count):
            own, came = hbm[2 * i : 2 * i + 2]
            copies.append(
                [
                    pltpu.make_async_copy(own, held.at[i, :step], sems.at[i, 0]),
                    pltpu.make_async_copy(came, held.at[i, step:], sems.at[i, 1]),
                ]
            )
        for some in copies:
            for copy in some:
                copy.start()
        for i in range(count):
            for copy in copies[i]:
                copy.wait()
            for k in range(4):
                on = slice(k * step, (k + 1) * step)
                part = nt(lefts[i][...], held[i, on])
                if i == 0:
                    out[:, on] = part
                else:
                    out[:, on] += part

    return pl.pallas_call(
        body,
        grid=(1,),
        out_shape=jax.ShapeDtypeStruct((rows, 4 * step), jnp.float32),
        in_specs=[pl.BlockSpec(memory_space=pltpu.VMEM)] * count
        + [pl.BlockSpec(memory_space=pl.ANY)] * (2 * count),
        out_specs=pl.BlockSpec(memory_space=pltpu.VMEM),
        scratch_shapes=[
            pltpu.VMEM((count, 4 * step, columns), jnp.bfloat16),
            pltpu.SemaphoreType.DMA((count, 2)),
        ],
        compiler_params=pltpu.CompilerParams(vmem_limit_bytes=VMEM_BYTES),
        cost_estimate=FREE,
        name="back_to_rows",
    )(*blocks, *(part for w in weights for part in w))


def on_device_block(
    tokens,
    lengths,
    attn_gain,
    w_query,
    key_matrix,
    value_matrix,
    query_gain,
    key_gain,
    w_out,
    mlp_gain,
    w_gate,
    w_up,
    w_down,
    cotangent,
):
    low, full = jnp.bfloat16, jnp.float32
    width = tokens.shape[2]
    head_dim = query_gain.shape[0]
    shards = lax.axis_size("shard")
    shard_at = lax.axis_index("shard")
    me = lax.axis_index("rep")
    core = me & 1
    count = lax.axis_size("rep")

    s = Stage()
    s.cotangent = cotangent
    piece = width // shards

    s.own_blocks = [
        column_block((w_query, key_matrix, value_matrix), me ^ i) for i in range(8)
    ]
    gain_rows = jnp.concatenate(
        [jnp.stack([attn_gain, mlp_gain]), jnp.zeros((14, piece), low)], 0
    )
    travelling = jnp.concatenate([s.own_blocks[0], gain_rows], 0)
    s.tokens = tokens
    s.out_block = column_block((w_out,), me)
    s.ffn_block = column_block((w_gate, w_up, w_down), me)
    s.before, s.behind = around(travelling, 1), around(travelling, -1)
    s.other_lengths = across(lengths, CORE)
    s.end()

    s.ahead = around(s.before, 1)
    tokens_sent = to_sequences_send(s.tokens)
    out_own = lax.all_gather(s.out_block, "shard", axis=0, tiled=True)
    del s.out_block, s.tokens
    s.end()

    parts = (s.before, s.ahead, s.behind)
    s.came = jnp.concatenate([part[:piece] for part in parts], 0)
    s.gains = jnp.concatenate([gain_rows[:2], *(part[piece : piece + 2] for part in parts)], 1)
    s.came_near = near(s.came)
    s.x_came = tokens_sent
    del s.before, s.behind, s.ahead
    s.end()

    ffn_own = lax.all_gather(s.ffn_block, "shard", axis=0, tiled=True)
    grad_y_sent = to_sequences_send(s.cotangent)
    s.came_far = far(*s.came_near)
    s.came_other = [across(block, CORE) for block in (s.came, *s.came_near)]
    gains = rolled(s.gains.astype(full))
    s.mlp_gains = gains[1:]
    s.attn_gains = gains[:1]
    s.x_low = jnp.concatenate(in_turn(s.x_came), 0)
    rows = s.x_low.shape[0]
    x_rows = s.x_low.astype(full)
    s.inverse_in = lax.rsqrt(jnp.mean(x_rows * x_rows, -1, keepdims=True) + EPS)
    s.normed = rolled((x_rows * s.inverse_in * s.attn_gains).astype(low))
    query_gains = query_gain.astype(full)[None]
    key_gains = key_gain.astype(full)[None]
    s.head_gains = jnp.concatenate([query_gains, key_gains], 0)
    both = jnp.where(
        core == 0,
        jnp.concatenate([lengths, s.other_lengths]),
        jnp.concatenate([s.other_lengths, lengths]),
    )
    length = lax.dynamic_index_in_dim(both, shard_at, 0, keepdims=False)
    s.info = jnp.stack([core, length]).astype(jnp.int32)
    query_pos = core * rows + jnp.arange(rows, dtype=jnp.int32)
    s.valid = (query_pos < length)[:, None].astype(full)
    cosine, sine = tables(query_pos, head_dim)
    s.cosine, sine = cosine[0, :, 0], sine[0, :, 0]
    s.sine = jnp.concatenate([-sine[:, : head_dim // 2], sine[:, head_dim // 2 :]], 1)
    s.out_own = out_own
    del s.gains, s.x_came, s.other_lengths, s.ffn_block, s.cotangent
    s.end()

    head_columns = 2 * head_dim
    block_columns = 4 * head_dim
    quad_rows = jax.ShapeDtypeStruct((rows, block_columns), low)
    quad_sums = jax.ShapeDtypeStruct((rows, block_columns), full)
    gain_sum = jax.ShapeDtypeStruct((1, head_dim), full)
    project = vmem_call(
        project_body,
        [jax.ShapeDtypeStruct((rows, 2 * block_columns), full), quad_rows, quad_rows],
        name="project",
    )
    attend = vmem_call(attend_body, [quad_rows, quad_sums], scalars=1, name="attend")
    attend_back = vmem_call(
        attend_back_body,
        [quad_rows, quad_sums, quad_rows, gain_sum],
        scratch=[pltpu.VMEM((2 * rows, head_dim), full)] * 2
        + [pltpu.VMEM((rows, block_columns), low)],
        scalars=1,
        name="attend_back",
    )
    finish = vmem_call(finish_body, [quad_rows, quad_rows, gain_sum], name="finish")
    upward = [(i, i + 1) for i in range(0, count, 2)]
    downward = [(i + 1, i) for i in range(0, count, 2)]

    def project_call(i, came, other):
        return (
            project, s.normed, s.own_blocks[2 * i], came, s.own_blocks[2 * i + 1], other,
            s.cosine, s.sine, s.head_gains,
        )

    def attend_call(projected, earlier):
        return (
            lambda query, own, before: attend(s.info, query, before, own),
            *projected[1:], earlier,
        )

    came_last = jnp.concatenate(s.came_far, 0)
    s.came_last = (came_last, across(came_last, CORE))
    s.out_near = near(s.out_own)
    s.out_own_other = across(s.out_own, CORE)
    s.projected = in_order(
        [
            project_call(i, block, other)
            for i, (block, other) in enumerate(zip((s.came, *s.came_near), s.came_other))
        ]
    )
    del s.came_far
    s.end()

    s.out_far = far(*s.out_near)
    s.out_near_other = [across(block, CORE) for block in s.out_near]
    s.earlier = [lax.ppermute(p[2], "rep", upward) for p in s.projected]
    (s.projected_last,) = in_order([project_call(3, *s.came_last)])
    s.grad_y_came = grad_y_sent
    s.end()

    grad_y = jnp.concatenate(in_turn(s.grad_y_came), 0)
    s.grad_y = jnp.where(s.valid > 0, grad_y, jnp.zeros_like(grad_y))
    grad_y_near = near(s.grad_y)
    out_last = jnp.concatenate(s.out_far, 0)
    s.out_last = (out_last, across(out_last, CORE))
    s.earlier_last = lax.ppermute(s.projected_last[2], "rep", upward)
    s.attended = in_order([attend_call(*pair) for pair in zip(s.projected, s.earlier)])
    del s.out_far, s.grad_y_came
    s.end()

    s.projected = [*s.projected, s.projected_last]
    s.earlier = [*s.earlier, s.earlier_last]
    s.out_blocks = [
        s.out_own, s.out_own_other, s.out_near[0], s.out_near_other[0], s.out_near[1],
        s.out_near_other[1], *s.out_last,
    ]
    (last,) = in_order([attend_call(s.projected_last, s.earlier_last)])
    s.attended = [*s.attended, last]
    s.mixed = [a[0] for a in s.attended]
    s.resid, s.mid = close_attention(s.x_low, s.mixed, s.out_blocks, s.mlp_gains)
    s.grad_y_near = grad_y_near
    del s.out_own, s.out_own_other, s.out_near, s.out_near_other, s.out_last
    del s.projected_last, s.earlier_last
    s.end()

    s.mid_near = near(s.mid)
    s.grad_y_far = far(*s.grad_y_near)
    s.end()

    s.mid_far = far(*s.mid_near)
    s.ffn_own = ffn_own
    s.end()

    s.mids = [s.mid, *s.mid_near, *s.mid_far]
    s.grads_y = [s.grad_y, *s.grad_y_near, *s.grad_y_far]
    s.ffn_other = across(s.ffn_own, CORE)
    units = s.ffn_own.shape[1] // 3
    s.hidden_own = hidden_units(s.mids, s.grads_y, s.ffn_own)
    del s.mid, s.mid_near, s.mid_far, s.grad_y_near, s.grad_y_far
    s.end()

    def gate_up_pairs():
        return [
            (hidden[i], weights, i - 1)
            for hidden, weights in ((s.hidden_own, s.ffn_own), (s.hidden_other, s.ffn_other))
            for i in (1, 2)
        ]

    def down_pairs():
        return [(s.hidden_own[0], s.ffn_own, 2), (s.hidden_other[0], s.ffn_other, 2)]

    def from_hidden_call(pairs, eighths):
        return (
            lambda first: from_hidden([(first, *pairs[0][1:]), *pairs[1:]], eighths),
            pairs[0][0],
        )

    def outer_call(lefts, rights, *added):
        return lambda first: row_outer(lefts, [[first, *rights[1:]]], 0, 8, *added)[0], rights[0]

    def send_near(sent):
        return across(sent[0], ACROSS_X), across(sent[1], ACROSS_Y)

    def send_far(came, rest, split):
        one_tail, two_head = rest
        return (
            across(rounded_sum(one_tail, split(came[1])[1]), ACROSS_X),
            across(rounded_sum(two_head, split(came[0])[1]), ACROSS_Y),
        )

    def total(came, came_far, own, split):
        head, tail = own
        full_sum = lambda *parts: sum(part.astype(full) for part in parts)
        return jnp.concatenate(
            [
                full_sum(head, split(came[0])[0], came_far[1]),
                full_sum(tail, split(came[1])[0], came_far[0]),
            ],
            0,
        )

    by_rows = lambda a: jnp.split(a, 2, 0)
    by_columns = lambda a: jnp.split(a, 2, 1)
    to_plane, rest_of_plane = (2, 6, 5, 7), (3, 4, 0, 1)

    s.hidden_other = hidden_units(s.mids, s.grads_y, s.ffn_other)
    (s.down_outer,) = in_order([outer_call(s.grads_y, s.hidden_other[:1])])
    s.end()

    s.down_came = across(s.down_outer, CORE)
    s.mid_sent = from_hidden(gate_up_pairs(), to_plane)
    del s.down_outer
    s.end()

    s.mid_came = send_near(s.mid_sent)
    s.down_mine, s.mid_rest, s.gate_up_outer = in_order(
        [
            outer_call(s.grads_y, s.hidden_own[:1], s.down_came),
            from_hidden_call(gate_up_pairs(), rest_of_plane),
            outer_call(s.mids, s.hidden_other[1:]),
        ]
    )
    del s.mid_sent, s.down_came
    s.end()

    s.down_chunks = ring_chunks(s.down_mine)
    s.down_ring = ring_sum_first(s.down_chunks)
    s.mid_came_far = send_far(s.mid_came, by_rows(s.mid_rest[0]), by_rows)
    s.gate_up_came = across(s.gate_up_outer, CORE)
    s.mlp_sent, s.mlp_rest = in_order(
        [
            from_hidden_call(down_pairs(), to_plane),
            from_hidden_call(down_pairs(), rest_of_plane),
        ]
    )
    del s.gate_up_outer, s.down_mine
    s.end()

    mlp_came = send_near(s.mlp_sent)
    s.down_last = around(rounded_sum(s.down_chunks[3], s.down_ring[0]), 1)
    grad_mid = total(s.mid_came, s.mid_came_far, by_rows(s.mid_rest[1]), by_rows)
    inverse_mid = lax.rsqrt(jnp.mean(s.resid * s.resid, -1, keepdims=True) + EPS)
    mid_unit = s.resid * inverse_mid
    s.mlp_gain_part = jnp.sum(mid_unit * grad_mid, 0)
    s.grad_resid = s.grad_y.astype(full) + norm_back(
        mid_unit, inverse_mid, grad_mid * s.mlp_gains
    )
    s.resid_low = s.grad_resid.astype(low)
    s.resid_rolled = rolled(s.resid_low)
    (s.gate_up_mine,) = in_order([outer_call(s.mids, s.hidden_own[1:], s.gate_up_came)])
    del s.mid_came, s.mid_came_far, s.mid_rest, s.gate_up_came, s.hidden_own, s.hidden_other
    del s.mids, s.grads_y, s.ffn_own, s.ffn_other
    s.end()

    def back_call(i):
        raw, query, own_pair = s.projected[i]
        return (
            lambda query, *rest: attend_back(s.info, query, *rest),
            query, s.earlier[i], own_pair, s.attended[i][1], s.resid_low,
            *s.out_blocks[2 * i : 2 * i + 2], raw, s.cosine, s.sine, s.head_gains[:1],
        )

    def finish_call(i):
        return (
            finish, s.backs[i][0], s.backs[i][1], s.returned[i], s.projected[i][0],
            s.cosine, s.sine, s.head_gains[1:],
        )

    def give_back(*chips):
        s.returned = s.returned | {
            i: lax.ppermute(s.backs[i][2], "rep", downward) for i in chips
        }

    def odd_call(left, blocks):
        return lambda first: row_outer([first], [blocks], 0, 8)[0], left

    def head_call(left, blocks, came):
        groups = [[blocks[1], blocks[3]], [blocks[2]], [blocks[0]]]
        return lambda first: row_outer([first], groups, 0, 4, came, (1, 3, 2, 0)), left

    def tail_call(left, blocks, came):
        groups = [[blocks[2], blocks[3]], [blocks[1]], [blocks[0]]]
        return lambda first: row_outer([first], groups, 4, 4, came, (2, 3, 1, 0)), left

    s.down_total = rounded_sum(s.down_chunks[0], s.down_ring[1], s.down_last)
    s.gate_up_chunks = ring_chunks(s.gate_up_mine)
    gate_up_ring = ring_sum_first(s.gate_up_chunks)
    mixed_even = [m[:, :head_columns] for m in s.mixed]
    mixed_odd = [m[:, head_columns:] for m in s.mixed]
    s.returned = {}
    s.out_odd, back = in_order([odd_call(s.resid_rolled, mixed_odd), back_call(3)])
    s.backs = {3: back}
    s.mlp_came = mlp_came
    del s.gate_up_mine, s.mlp_sent, s.down_chunks, s.down_ring, s.down_last
    s.end()

    s.mlp_came_far = send_far(s.mlp_came, by_rows(s.mlp_rest[0]), by_rows)
    s.out_came = across(s.out_odd, CORE)
    give_back(3)
    back1, back2 = in_order([back_call(1), back_call(2)])
    s.backs = s.backs | {1: back1, 2: back2}
    del s.out_odd
    s.end()

    s.down_near = near(s.down_total)
    give_back(1, 2)
    mlp_out = total(s.mlp_came, s.mlp_came_far, by_rows(s.mlp_rest[1]), by_rows)
    s.output = (s.valid * (s.resid + mlp_out)).astype(low)
    s.out_head, s.out_tail, back, finished = in_order(
        [
            head_call(s.resid_rolled, mixed_even, s.out_came),
            tail_call(s.resid_rolled, mixed_even, s.out_came),
            back_call(0),
            finish_call(3),
        ]
    )
    s.backs = s.backs | {0: back}
    s.finished = {3: finished}
    s.gate_up_ring = gate_up_ring
    del s.mlp_came, s.mlp_came_far, s.mlp_rest, s.out_came, s.resid
    s.end()

    gate_up_last = around(rounded_sum(s.gate_up_chunks[3], s.gate_up_ring[0]), 1)
    s.out_near = send_near((s.out_head[0], s.out_tail[0]))
    s.down_far = far(*s.down_near)
    give_back(0)
    finished1, finished2 = in_order([finish_call(1), finish_call(2)])
    s.finished = s.finished | {1: finished1, 2: finished2}
    s.end()

    s.out_far = send_far(s.out_near, (s.out_tail[1], s.out_head[1]), by_columns)
    s.down_own = jnp.concatenate([s.down_total, *s.down_near, *s.down_far], 0)
    s.down_other = across(s.down_own, CORE)
    (finished,) = in_order([finish_call(0)])
    s.finished = s.finished | {0: finished}
    (s.qkv_odd,) = in_order([odd_call(s.normed, [s.finished[i][1] for i in range(4)])])
    s.gate_up_last = gate_up_last
    del s.down_total, s.down_near, s.down_far
    s.end()

    my_group = me.astype(jnp.int32)[None]

    def whole_call(widths, own, other):
        return lambda first: whole_columns(my_group, first, other, widths), own

    s.qkv_came = across(s.qkv_odd, CORE)
    s.gate_up_total = rounded_sum(s.gate_up_chunks[0], s.gate_up_ring[1], s.gate_up_last)
    s.gate_up_near = near(s.gate_up_total)
    output_sent = from_sequences_send(s.output)
    out_sum = total(s.out_near, s.out_far, (s.out_head[2], s.out_tail[2]), by_columns)
    s.out_chunks = jnp.split(out_sum.astype(low), shards, 0)
    s.out_ring = ring_sum_first(s.out_chunks)
    weights = [
        pair
        for i, block in enumerate(zip((s.came, *s.came_near), s.came_other))
        for pair in ((s.own_blocks[2 * i], block[0]), (s.own_blocks[2 * i + 1], block[1]))
    ] + [(s.own_blocks[6 + i], s.came_last[i]) for i in range(2)]
    blocks = [part for i in range(4) for part in s.finished[i][:2]]
    grad_in, s.whole_down = in_order(
        [
            (lambda first: back_to_rows([first, *blocks[1:]], weights), blocks[0]),
            whole_call((units,), s.down_own, s.down_other),
        ]
    )
    grad_in = rolled(grad_in)
    x_unit = s.x_low.astype(full) * s.inverse_in
    s.attn_gain_part = jnp.sum(x_unit * grad_in, 0)
    s.grad_tokens = (
        s.grad_resid + norm_back(x_unit, s.inverse_in, grad_in * s.attn_gains)
    ).astype(low)
    del s.gate_up_chunks, s.gate_up_ring, s.gate_up_last, s.output
    del s.qkv_odd, s.out_near, s.out_far, s.out_head, s.out_tail, s.down_own, s.down_other
    del s.own_blocks, s.came, s.came_near, s.came_other, s.came_last, s.grad_resid, s.x_low
    s.end()

    s.gate_up_far = far(*s.gate_up_near)
    s.out_ring_last = around(rounded_sum(s.out_chunks[3], s.out_ring[0]), 1)
    even = [s.finished[i][0] for i in range(4)]
    halves = [
        [block[:, half * head_columns : (half + 1) * head_columns] for block in even]
        for half in range(2)
    ]
    came_halves = [
        jnp.concatenate(
            [
                s.qkv_came[:, i * block_columns + half * head_columns :][:, :head_columns]
                for i in range(4)
            ],
            1,
        )
        for half in range(2)
    ]
    first_head, first_tail, second_head, second_tail = in_order(
        [
            call(s.normed, halves[half], came_halves[half])
            for half in range(2)
            for call in (head_call, tail_call)
        ]
    )
    s.heads = [first_head, second_head]
    s.tails = [first_tail, second_tail]
    s.gain_parts = jnp.concatenate(
        [
            s.attn_gain_part,
            s.mlp_gain_part,
            sum(s.backs[i][3] for i in range(4))[0],
            sum(s.finished[i][2] for i in range(4))[0],
        ]
    )
    del s.qkv_came, s.finished, s.backs
    s.end()

    grad_tokens_sent = from_sequences_send(s.grad_tokens)

    def qkv_near(half):
        return send_near((s.heads[half][0], s.tails[half][0]))

    def qkv_far(came, half):
        return send_far(came, (s.tails[half][1], s.heads[half][1]), by_columns)

    def qkv_chunks(came, came_far, half):
        own = total(came, came_far, (s.heads[half][2], s.tails[half][2]), by_columns)
        return jnp.split(own.astype(low), shards, 0)

    s.near0 = qkv_near(0)
    s.gate_up_own = jnp.concatenate([s.gate_up_total, *s.gate_up_near, *s.gate_up_far], 0)
    s.gate_up_other = across(s.gate_up_own, CORE)
    s.out_total = rounded_sum(s.out_chunks[0], s.out_ring[1], s.out_ring_last)
    s.gain_came = across(s.gain_parts, CORE)
    del s.out_chunks, s.out_ring, s.out_ring_last, s.gate_up_near, s.gate_up_far
    s.output_came = output_sent
    del s.gate_up_total, s.grad_tokens
    s.end()

    s.far0 = qkv_far(s.near0, 0)
    s.near1 = qkv_near(1)
    s.gain_parts = s.gain_parts + s.gain_came
    s.gain_came = across(s.gain_parts, ACROSS_X)
    (s.whole_gate_up,) = in_order([whole_call((units, units), s.gate_up_own, s.gate_up_other)])
    s.tokens_came = grad_tokens_sent
    del s.gate_up_own, s.gate_up_other
    s.end()

    s.chunks0 = qkv_chunks(s.near0, s.far0, 0)
    s.ring0 = ring_sum_first(s.chunks0)
    s.far1 = qkv_far(s.near1, 1)
    s.gain_parts = s.gain_parts + s.gain_came
    s.gain_came = across(s.gain_parts, ACROSS_Y)
    del s.near0, s.far0
    s.end()

    s.last0 = around(rounded_sum(s.chunks0[3], s.ring0[0]), 1)
    s.chunks1 = qkv_chunks(s.near1, s.far1, 1)
    s.ring1 = ring_sum_first(s.chunks1)
    s.gain_parts = s.gain_parts + s.gain_came
    s.gain_came = lax.ppermute(s.gain_parts, "shard", [(i, i ^ 1) for i in range(shards)])
    del s.near1, s.far1, s.heads, s.tails
    s.end()

    query_total = rounded_sum(s.chunks0[0], s.ring0[1], s.last0)
    s.total0 = jnp.concatenate([query_total, s.out_total], 1)
    s.spread0 = near(s.total0)
    s.last1 = around(rounded_sum(s.chunks1[3], s.ring1[0]), 1)
    s.gain_parts = s.gain_parts + s.gain_came
    s.gain_came = lax.ppermute(s.gain_parts, "shard", [(i, i ^ 2) for i in range(shards)])
    del s.chunks0, s.ring0, s.last0, s.out_total
    s.end()

    s.spread_far0 = far(*s.spread0)
    s.total1 = rounded_sum(s.chunks1[0], s.ring1[1], s.last1)
    s.spread1 = near(s.total1)
    del s.chunks1, s.ring1, s.last1
    s.end()

    s.own0 = jnp.concatenate([s.total0, *s.spread0, *s.spread_far0], 0)
    s.other0 = across(s.own0, CORE)
    s.spread_far1 = far(*s.spread1)
    del s.total0, s.spread0, s.spread_far0
    s.end()

    s.own1 = jnp.concatenate([s.total1, *s.spread1, *s.spread_far1], 0)
    s.other1 = across(s.own1, CORE)
    (s.whole0,) = in_order([whole_call((head_columns, head_columns), s.own0, s.other0)])
    del s.own0, s.other0, s.total1, s.spread1, s.spread_far1
    s.end()

    ((whole_key, whole_value),) = in_order(
        [whole_call((head_dim, head_dim), s.own1, s.other1)]
    )
    gain_sums = s.gain_parts + s.gain_came
    wide = lax.dynamic_slice_in_dim(
        gain_sums[: 2 * width].reshape(2, width), shard_at * piece, piece, 1
    )
    narrow = gain_sums[2 * width :]
    return (
        jnp.stack(in_turn(s.output_came)),
        jnp.stack(in_turn(s.tokens_came)),
        wide[0],
        s.whole0[0],
        whole_key,
        whole_value,
        narrow[:head_dim],
        narrow[head_dim:],
        s.whole0[1],
        wide[1],
        *s.whole_gate_up,
        *s.whole_down,
    )


def solution(mesh):
    sizes = (mesh.shape["rep"], mesh.shape["shard"])
    return jax.shard_map(
        on_device_block if sizes == (8, 4) else on_device,
        mesh=mesh,
        in_specs=(
            P("rep", "shard", None),
            P("rep"),
            P("shard"),
            P("shard", None),
            P("shard", None),
            P("shard", None),
            P(),
            P(),
            P("shard", None),
            P("shard"),
            P("shard", None),
            P("shard", None),
            P("shard", None),
            P("rep", "shard", None),
        ),
        out_specs=(
            P("rep", "shard", None),
            P("rep", "shard", None),
            P("shard"),
            P("shard", None),
            P("shard", None),
            P("shard", None),
            P(),
            P(),
            P("shard", None),
            P("shard"),
            P("shard", None),
            P("shard", None),
            P("shard", None),
        ),
        check_vma=False,
    )
```

```python
import jax
import jax.numpy as jnp
from jax import lax
from jax.experimental import pallas as pl
from jax.experimental.pallas import tpu as pltpu
from jax.sharding import PartitionSpec as P

WINDOW = 512


EPS = 1e-06
ROPE_BASE = 1000000.0
NEG = -1e30


def passed_along(x, axis, by):
    devices = lax.axis_size(axis)
    pairs = [(i, i + by) for i in range(devices) if 0 <= i + by < devices]
    return lax.ppermute(x, axis, pairs)


def tables(positions, head_dim):
    half = head_dim // 2
    freq = ROPE_BASE ** (-jnp.arange(half, dtype=jnp.float32) * 2.0 / head_dim)
    angle = positions.astype(jnp.float32)[:, None] * freq[None, :]
    angle = jnp.concatenate([angle, angle], -1)
    return (jnp.cos(angle)[None, :, None, :], jnp.sin(angle)[None, :, None, :])


def rotated_rows(value_rows):
    half = value_rows.shape[-1] // 2
    return jnp.concatenate([-value_rows[..., half:], value_rows[..., :half]], -1)


def head_norm(raw, gain):
    inverse = lax.rsqrt(jnp.mean(raw * raw, -1, keepdims=True) + EPS)
    unit = raw * inverse
    return (unit, inverse, unit * gain)


def norm_back(unit, inverse, grad_unit):
    return inverse * (grad_unit - unit * jnp.mean(grad_unit * unit, -1, keepdims=True))


def head_norm_back(unit, inverse, grad_normed, gain):
    grad_raw = norm_back(unit, inverse, grad_normed * gain)
    return (grad_raw, jnp.sum(unit * grad_normed, axis=(0, 1, 2)))


def scores(query_rows, keys, allowed, scale):
    raw = (
        jnp.einsum("sqhgd,skhd->shgqk", query_rows, keys, preferred_element_type=jnp.float32)
        * scale
    )
    return jnp.where(allowed[:, None, None], raw, NEG)


def outer(left, right):
    return jnp.einsum("rc,rf->cf", left, right, preferred_element_type=jnp.float32)


def on_device(
    tokens,
    lengths,
    attn_gain,
    w_query,
    key_matrix,
    value_matrix,
    query_gain,
    key_gain,
    w_out,
    mlp_gain,
    w_gate,
    w_up,
    w_down,
    cotangent,
):
    seq_count, piece, width = tokens.shape
    head_dim = query_gain.shape[0]
    heads_q = w_query.shape[1] // head_dim
    heads_kv = key_matrix.shape[1] // head_dim
    groups = heads_q // heads_kv
    rows = seq_count * piece
    scale = head_dim ** (-0.5)
    reach = (WINDOW + piece - 2) // piece
    owned = width // lax.axis_size("shard")
    shard_at = lax.axis_index("shard")
    query_pos = shard_at * piece + jnp.arange(piece, dtype=jnp.int32)
    key_pos = (shard_at - reach) * piece + jnp.arange((reach + 1) * piece, dtype=jnp.int32)
    near = (
        (key_pos[None, :] <= query_pos[:, None])
        & (query_pos[:, None] - key_pos[None, :] < WINDOW)
        & (key_pos[None, :] >= 0)
    )
    live = (key_pos[None, None, :] < lengths[:, None, None]) | (
        key_pos[None, :] == query_pos[:, None]
    )[None]
    allowed = near[None] & live
    valid = (query_pos[None, :] < lengths[:, None]).astype(jnp.float32).reshape(rows, 1)
    cosine_table, sine_table = tables(query_pos, head_dim)
    x_rows = tokens.astype(jnp.float32).reshape(rows, width)
    inverse_in = lax.rsqrt(jnp.mean(x_rows * x_rows, -1, keepdims=True) + EPS)
    x_unit = x_rows * inverse_in
    gain_piece = lax.all_gather(attn_gain, "shard", axis=0, tiled=True)
    query_piece = lax.all_gather(w_query, "shard", axis=0, tiled=True)
    key_piece = lax.all_gather(key_matrix, "shard", axis=0, tiled=True)
    value_piece = lax.all_gather(value_matrix, "shard", axis=0, tiled=True)
    normed_piece = (x_unit * gain_piece.astype(jnp.float32)).astype(jnp.bfloat16)
    acc_q = jnp.dot(normed_piece, query_piece, preferred_element_type=jnp.float32)
    acc_k = jnp.dot(normed_piece, key_piece, preferred_element_type=jnp.float32)
    acc_v = jnp.dot(normed_piece, value_piece, preferred_element_type=jnp.float32)
    normalized_rows = normed_piece
    gains = gain_piece.astype(jnp.float32)
    attn_in = normalized_rows
    attn_gains = gains
    query_unit, query_inverse, query_rows_normalized = head_norm(
        acc_q.reshape(seq_count, piece, heads_q, head_dim), query_gain.astype(jnp.float32)
    )
    key_unit, key_inverse, key_normed = head_norm(
        acc_k.reshape(seq_count, piece, heads_kv, head_dim), key_gain.astype(jnp.float32)
    )
    query_rows = (
        (query_rows_normalized * cosine_table + rotated_rows(query_rows_normalized) * sine_table)
        .astype(jnp.bfloat16)
        .reshape(seq_count, piece, heads_kv, groups, head_dim)
    )
    keys_own = (key_normed * cosine_table + rotated_rows(key_normed) * sine_table).astype(
        jnp.bfloat16
    )
    values_own = acc_v.reshape(seq_count, piece, heads_kv, head_dim).astype(jnp.bfloat16)
    own_pair = jnp.stack([keys_own, values_own])
    parts = []
    for fetch_back in range(reach, 0, -1):
        parts.append(passed_along(own_pair, "shard", fetch_back))
    parts.append(own_pair)
    near_pair = jnp.concatenate(parts, 2)
    score = scores(query_rows, near_pair[0], allowed, scale)
    top = jnp.max(score, -1, keepdims=True)
    expo = jnp.exp(score - top)
    total = jnp.sum(expo, -1, keepdims=True)
    prob = expo / total
    log_total = top + jnp.log(total)
    mixed = jnp.einsum(
        "shgqk,skhd->sqhgd",
        prob.astype(jnp.bfloat16),
        near_pair[1],
        preferred_element_type=jnp.float32,
    )
    mixed_rows = mixed.reshape(rows, heads_q * head_dim).astype(jnp.bfloat16)
    resid = x_rows + jnp.einsum(
        "rf,nf->rn",
        mixed_rows,
        lax.all_gather(w_out, "shard", axis=0, tiled=True),
        preferred_element_type=jnp.float32,
    )
    inverse_mid = lax.rsqrt(jnp.mean(resid * resid, -1, keepdims=True) + EPS)
    mid_unit = resid * inverse_mid
    gain_piece = lax.all_gather(mlp_gain, "shard", axis=0, tiled=True)
    gate_piece = lax.all_gather(w_gate, "shard", axis=0, tiled=True)
    up_piece = lax.all_gather(w_up, "shard", axis=0, tiled=True)
    normed_piece = (mid_unit * gain_piece.astype(jnp.float32)).astype(jnp.bfloat16)
    acc_gate = jnp.dot(normed_piece, gate_piece, preferred_element_type=jnp.float32)
    acc_up = jnp.dot(normed_piece, up_piece, preferred_element_type=jnp.float32)
    normalized_rows = normed_piece
    gains = gain_piece.astype(jnp.float32)
    mlp_in = normalized_rows
    sigma = jax.nn.sigmoid(acc_gate)
    swish = acc_gate * sigma
    act = (swish * acc_up).astype(jnp.bfloat16)
    mlp_out = jnp.einsum(
        "rf,nf->rn",
        act,
        lax.all_gather(w_down, "shard", axis=0, tiled=True),
        preferred_element_type=jnp.float32,
    )
    output = (valid * (resid + mlp_out)).astype(jnp.bfloat16).reshape(seq_count, piece, width)
    grad_y = cotangent.astype(jnp.float32).reshape(rows, width) * valid
    grad_y_low = grad_y.astype(jnp.bfloat16)
    grad_act = jnp.dot(
        grad_y_low,
        lax.all_gather(w_down, "shard", axis=0, tiled=True),
        preferred_element_type=jnp.float32,
    )
    grad_gate = (grad_act * acc_up * sigma * (1.0 + acc_gate * (1.0 - sigma))).astype(jnp.bfloat16)
    grad_up = (grad_act * swish).astype(jnp.bfloat16)
    gate_piece, up_piece = lax.all_gather((w_gate, w_up), "shard", axis=0, tiled=True)
    grad_mid = jnp.einsum(
        "rf,nf->rn", grad_gate, gate_piece, preferred_element_type=jnp.float32
    ) + jnp.einsum("rf,nf->rn", grad_up, up_piece, preferred_element_type=jnp.float32)
    grad_resid = grad_y + norm_back(mid_unit, inverse_mid, grad_mid * gains)
    mlp_gain_part = jnp.sum(mid_unit * grad_mid, 0)
    normalized_rows = mlp_in
    mlp_grads = jax.tree.map(
        lambda part: lax.psum_scatter(
            part.astype(jnp.bfloat16), "shard", scatter_dimension=0, tiled=True
        ).astype(jnp.float32),
        (
            outer(normalized_rows, grad_gate),
            outer(normalized_rows, grad_up),
            outer(grad_y_low, act),
        ),
    )
    resid_low = grad_resid.astype(jnp.bfloat16)
    grad_mixed = jnp.dot(
        resid_low,
        lax.all_gather(w_out, "shard", axis=0, tiled=True),
        preferred_element_type=jnp.float32,
    )
    grad_mixed = grad_mixed.astype(jnp.bfloat16).reshape(
        seq_count, piece, heads_kv, groups, head_dim
    )
    prob_again = jnp.exp(scores(query_rows, near_pair[0], allowed, scale) - log_total)
    grad_prob = jnp.einsum(
        "sqhgd,skhd->shgqk", grad_mixed, near_pair[1], preferred_element_type=jnp.float32
    )
    grad_values = jnp.einsum(
        "shgqk,sqhgd->skhd",
        prob_again.astype(jnp.bfloat16),
        grad_mixed,
        preferred_element_type=jnp.float32,
    )
    grad_score = (
        prob_again * (grad_prob - jnp.sum(prob_again * grad_prob, -1, keepdims=True))
    ).astype(jnp.bfloat16)
    grad_queries = (
        jnp.einsum(
            "shgqk,skhd->sqhgd", grad_score, near_pair[0], preferred_element_type=jnp.float32
        )
        * scale
    )
    grad_keys = (
        jnp.einsum("shgqk,sqhgd->skhd", grad_score, query_rows, preferred_element_type=jnp.float32)
        * scale
    )
    grad_pair = jnp.stack([grad_keys, grad_values])
    own_grad = grad_pair[:, :, reach * piece :]
    for back in range(1, reach + 1):
        lower = (reach - back) * piece
        own_grad = own_grad + passed_along(grad_pair[:, :, lower : lower + piece], "shard", -back)
    grad_query_post = grad_queries.reshape(seq_count, piece, heads_q, head_dim)
    grad_query_normed = grad_query_post * cosine_table - rotated_rows(grad_query_post * sine_table)
    grad_key_normed = own_grad[0] * cosine_table - rotated_rows(own_grad[0] * sine_table)
    grad_query_raw, query_gain_grad = head_norm_back(
        query_unit, query_inverse, grad_query_normed, query_gain.astype(jnp.float32)
    )
    grad_key_raw, key_gain_grad = head_norm_back(
        key_unit, key_inverse, grad_key_normed, key_gain.astype(jnp.float32)
    )
    grad_query_low = grad_query_raw.reshape(rows, heads_q * head_dim).astype(jnp.bfloat16)
    grad_key_low = grad_key_raw.reshape(rows, heads_kv * head_dim).astype(jnp.bfloat16)
    grad_value_low = own_grad[1].reshape(rows, heads_kv * head_dim).astype(jnp.bfloat16)
    query_piece, key_piece, value_piece = lax.all_gather(
        (w_query, key_matrix, value_matrix), "shard", axis=0, tiled=True
    )
    grad_in = (
        jnp.einsum("rf,nf->rn", grad_query_low, query_piece, preferred_element_type=jnp.float32)
        + jnp.einsum("rf,nf->rn", grad_key_low, key_piece, preferred_element_type=jnp.float32)
        + jnp.einsum("rf,nf->rn", grad_value_low, value_piece, preferred_element_type=jnp.float32)
    )
    grad_tokens = (
        (grad_resid + norm_back(x_unit, inverse_in, grad_in * attn_gains))
        .astype(jnp.bfloat16)
        .reshape(seq_count, piece, width)
    )
    attn_gain_part = jnp.sum(x_unit * grad_in, 0)
    normalized_rows = attn_in
    attn_grads = jax.tree.map(
        lambda part: lax.psum_scatter(
            part.astype(jnp.bfloat16), "shard", scatter_dimension=0, tiled=True
        ).astype(jnp.float32),
        (
            outer(normalized_rows, grad_query_low),
            outer(normalized_rows, grad_key_low),
            outer(normalized_rows, grad_value_low),
            outer(resid_low, mixed_rows),
        ),
    )
    head_grads = lax.psum(
        (query_gain_grad, key_gain_grad, attn_gain_part, mlp_gain_part), ("rep", "shard")
    )
    attn_gain_total = lax.dynamic_slice_in_dim(head_grads[2], shard_at * owned, owned, 0)
    mlp_gain_total = lax.dynamic_slice_in_dim(head_grads[3], shard_at * owned, owned, 0)
    summed = (
        lax.psum(attn_grads[0].astype(jnp.bfloat16), "rep").astype(jnp.float32),
        lax.psum(attn_grads[1].astype(jnp.bfloat16), "rep").astype(jnp.float32),
        lax.psum(attn_grads[2].astype(jnp.bfloat16), "rep").astype(jnp.float32),
        lax.psum(attn_grads[3].astype(jnp.bfloat16), "rep").astype(jnp.float32),
        lax.psum(mlp_grads[0].astype(jnp.bfloat16), "rep").astype(jnp.float32),
        lax.psum(mlp_grads[1].astype(jnp.bfloat16), "rep").astype(jnp.float32),
        lax.psum(mlp_grads[2].astype(jnp.bfloat16), "rep").astype(jnp.float32),
    )
    attn_grads = summed[:4]
    mlp_grads = summed[4:]
    return (
        output,
        grad_tokens,
        attn_gain_total,
        attn_grads[0],
        attn_grads[1],
        attn_grads[2],
        head_grads[0],
        head_grads[1],
        attn_grads[3],
        mlp_gain_total,
        mlp_grads[0],
        mlp_grads[1],
        mlp_grads[2],
    )


CORE, ACROSS_X, ACROSS_Y = 1, 2, 4
VMEM_BYTES = 56 * 2**20
FREE = pl.CostEstimate(flops=1, bytes_accessed=1, transcendentals=0)


def across(x, mask):
    count = lax.axis_size("rep")
    return lax.ppermute(x, "rep", [(i, i ^ mask) for i in range(count)])


def around(x, by):
    count = lax.axis_size("shard")
    return lax.ppermute(x, "shard", [(i, (i + by) % count) for i in range(count)])


class Stage(dict):
    __getattr__ = dict.__getitem__
    __setattr__ = dict.__setitem__
    __delattr__ = dict.__delitem__

    def end(self):
        self.update(lax.optimization_barrier(dict(self)))


def in_order(calls):
    outs = []
    for call, first, *rest in calls:
        if outs:
            last = outs[-1][0] if isinstance(outs[-1], (list, tuple)) else outs[-1]
            first = lax.optimization_barrier((first, last))[0]
        outs.append(call(first, *rest))
    return outs


def ring_sum_first(chunks):
    return around(chunks[2], 1), around(chunks[1], -1)


def near(piece):
    return across(piece, ACROSS_X), across(piece, ACROSS_Y)


def far(from_x, from_y):
    half = from_x.shape[0] // 2
    return across(from_x[:half], ACROSS_Y), across(from_y[half:], ACROSS_X)


def rounded_sum(*parts):
    return sum(part.astype(jnp.float32) for part in parts).astype(jnp.bfloat16)


def sequence_pairs(turn):
    groups, shards = lax.axis_size("rep"), lax.axis_size("shard")
    pairs = []
    for group in range(groups):
        chip, core = divmod(group, 2)
        for at in range(shards):
            to_group, to_shard = 2 * chip + at // 2, 2 * core + (turn ^ (at & 1))
            pairs.append((group * shards + at, to_group * shards + to_shard))
    return pairs


def rolled(x):
    count, at = lax.axis_size("shard"), lax.axis_index("shard")
    width = x.shape[1] // count
    return jnp.concatenate(
        [lax.dynamic_slice_in_dim(x, ((at - i) % count) * width, width, 1) for i in range(count)],
        1,
    )


def to_sequences_send(x):
    odd = lax.axis_index("shard") & 1
    return [
        lax.ppermute(
            lax.dynamic_index_in_dim(x, turn ^ odd, 0, keepdims=False),
            ("rep", "shard"),
            sequence_pairs(turn),
        )
        for turn in range(2)
    ]


def from_sequences_send(x):
    odd = lax.axis_index("shard") & 1
    x = x.reshape(2, x.shape[0] // 2, x.shape[1])
    return [
        lax.ppermute(
            lax.dynamic_index_in_dim(x, turn ^ odd, 0, keepdims=False),
            ("rep", "shard"),
            [(to, at) for at, to in sequence_pairs(turn)],
        )
        for turn in range(2)
    ]


def in_turn(came):
    even = lax.axis_index("shard") & 1 == 0
    return [jnp.where(even, came[0], came[1]), jnp.where(even, came[1], came[0])]


def column_block(weights, at):
    cuts = [w.shape[1] // 8 for w in weights]
    return jnp.concatenate(
        [lax.dynamic_slice_in_dim(w, at * cut, cut, 1) for w, cut in zip(weights, cuts)], 1
    )


def whole_columns(me, own, other, widths):
    rows, columns = own.shape[0] // 4, own.shape[1]

    def body(me_ref, own_ref, other_ref, *outs):
        def put(block):
            start = 0
            for out, width in zip(outs, widths):
                out[...] = block[:, start : start + width].astype(jnp.float32)
                start += width

        mine = (me_ref[0] ^ pl.program_id(0)) & 1 == 0
        pl.when(mine)(lambda: put(own_ref))
        pl.when(jnp.logical_not(mine))(lambda: put(other_ref))

    spec = pl.BlockSpec((rows, columns), lambda i, at: ((at[0] ^ i) >> 1, 0))
    return pl.pallas_call(
        body,
        grid_spec=pltpu.PrefetchScalarGridSpec(
            num_scalar_prefetch=1,
            grid=(8,),
            in_specs=[spec, spec],
            out_specs=[pl.BlockSpec((rows, w), lambda i, at: (0, i)) for w in widths],
        ),
        out_shape=[jax.ShapeDtypeStruct((rows, 8 * w), jnp.float32) for w in widths],
        compiler_params=pltpu.CompilerParams(vmem_limit_bytes=VMEM_BYTES),
        cost_estimate=FREE,
        name="whole_columns",
    )(me, own, other)


def turned(x):
    return pltpu.roll(x, x.shape[-1] // 2, x.ndim - 1)


def nt(left, right):
    return lax.dot_general(
        left, right, (((1,), (1,)), ((), ())), preferred_element_type=jnp.float32
    )


def tn(left, right):
    return lax.dot_general(
        left, right, (((0,), (0,)), ((), ())), preferred_element_type=jnp.float32
    )


def unit_of(raw):
    inverse = lax.rsqrt(jnp.mean(raw * raw, -1, keepdims=True) + EPS)
    return raw * inverse, inverse


def project_body(
    normed, own0, came0, own1, came1, cosine, sine, gains, raw, query, key_value
):
    step = own0.shape[0]
    dim = cosine.shape[1]
    for block, (own, came) in enumerate(((own0, came0), (own1, came1))):
        at = block * 4 * dim
        raw[:, at : at + 4 * dim] = jnp.dot(
            normed[:, :step], own[...], preferred_element_type=jnp.float32
        ) + jnp.dot(normed[:, step:], came[...], preferred_element_type=jnp.float32)
        for i in range(3):
            unit, _ = unit_of(raw[:, at + i * dim : at + (i + 1) * dim])
            head = unit * gains[i // 2 : i // 2 + 1, :]
            head = (head * cosine[...] + turned(head) * sine[...]).astype(jnp.bfloat16)
            if i < 2:
                query[:, (2 * block + i) * dim : (2 * block + i + 1) * dim] = head
            else:
                key_value[:, 2 * block * dim : (2 * block + 1) * dim] = head
        key_value[:, (2 * block + 1) * dim : (2 * block + 2) * dim] = raw[
            :, at + 3 * dim : at + 4 * dim
        ].astype(jnp.bfloat16)


def window_scores(info, query, keys, part, scale):
    rows, columns = query.shape[0], keys.shape[0]
    half = columns - rows
    row = lax.broadcasted_iota(jnp.int32, (rows, columns), 0)
    column = lax.broadcasted_iota(jnp.int32, (rows, columns), 1)
    gap = column - row - half
    slot = column + ((info[0] - 1) * half + part * rows)
    allowed = (gap <= 0) & (gap > -half) & (slot >= 0) & ((slot < info[1]) | (gap == 0))
    return nt(query, keys) * scale, allowed


def key_columns(block, dim):
    key = slice(2 * block * dim, (2 * block + 1) * dim)
    value = slice((2 * block + 1) * dim, (2 * block + 2) * dim)
    return key, value


def seen_pair(before, own, part, block, dim):
    here, there = key_columns(block, dim), key_columns(1 - block, dim)
    rows = own.shape[0] // 2
    if part == 0:
        return [
            jnp.concatenate([before[:, t], own[:rows, h]], 0) for h, t in zip(here, there)
        ]
    return [jnp.concatenate([before[rows:, t], own[:, h]], 0) for h, t in zip(here, there)]


def attend_body(info, query, before, own, mixed, log_total):
    dim = own.shape[1] // 4
    rows = query.shape[0] // 2
    for part in range(2):
        at = slice(part * rows, (part + 1) * rows)
        for block in range(2):
            keys, values = seen_pair(before, own, part, block, dim)
            for head in (2 * block, 2 * block + 1):
                on = slice(head * dim, (head + 1) * dim)
                score, allowed = window_scores(info, query[at, on], keys, part, dim**-0.5)
                score = jnp.where(allowed, score, NEG)
                top = jnp.max(score, -1, keepdims=True)
                expo = jnp.exp(score - top)
                total = jnp.sum(expo, -1, keepdims=True)
                prob = (expo * (1.0 / total)).astype(jnp.bfloat16)
                mixed[at, on] = jnp.dot(
                    prob, values, preferred_element_type=jnp.float32
                ).astype(jnp.bfloat16)
                log_total[at, on] = jnp.broadcast_to(top + jnp.log(total), (rows, dim))


def attend_back_body(
    info, query, before, own, log_total, grad_resid, weight0, weight1, raw, cosine, sine, gain,
    grad_query, grad_own, grad_before, gain_part, grad_keys, grad_values, grad_mixed,
):
    dim = own.shape[1] // 4
    rows = query.shape[0] // 2
    scale = dim**-0.5
    gain_total = jnp.zeros((1, dim), jnp.float32)
    for block, weight in enumerate((weight0, weight1)):
        on = slice(2 * block * dim, 2 * (block + 1) * dim)
        grad_mixed[:, on] = jnp.dot(
            grad_resid[...], weight[...], preferred_element_type=jnp.float32
        ).astype(jnp.bfloat16)
        grad_keys[...] = jnp.zeros_like(grad_keys)
        grad_values[...] = jnp.zeros_like(grad_values)
        for part in range(2):
            keys, values = seen_pair(before, own, part, block, dim)
            at = slice(part * rows, (part + 1) * rows)
            seen = slice(part * rows, part * rows + keys.shape[0])
            for head in (2 * block, 2 * block + 1):
                on = slice(head * dim, (head + 1) * dim)
                score, allowed = window_scores(info, query[at, on], keys, part, scale)
                prob = jnp.where(allowed, jnp.exp(score - log_total[at, on][:, :1]), 0.0)
                grad_prob = nt(grad_mixed[at, on], values)
                inner = jnp.sum(prob * grad_prob, -1, keepdims=True)
                grad_score = (prob * (grad_prob - inner)).astype(jnp.bfloat16)
                grad_values[seen, :] += tn(prob.astype(jnp.bfloat16), grad_mixed[at, on])
                grad_keys[seen, :] += tn(grad_score, query[at, on]) * scale
                back = jnp.dot(grad_score, keys, preferred_element_type=jnp.float32) * scale
                back = back * cosine[at, :] - turned(back) * sine[at, :]
                there = (2 * head - head % 2) * dim
                unit, inverse = unit_of(raw[at, there : there + dim])
                gain_total += jnp.sum(unit * back, 0, keepdims=True)
                back = back * gain[...]
                back = inverse * (back - unit * jnp.mean(back * unit, -1, keepdims=True))
                grad_query[at, on] = back.astype(jnp.bfloat16)
        for grad, here, there in zip(
            (grad_keys, grad_values), key_columns(block, dim), key_columns(1 - block, dim)
        ):
            grad_before[:, there] = grad[: 2 * rows, :].astype(jnp.bfloat16)
            grad_own[:, here] = grad[2 * rows :, :]
    gain_part[...] = gain_total


def finish_body(grad_query, grad_own, came, raw, cosine, sine, gain, even, odd, gain_part):
    dim = cosine.shape[1]
    total = jnp.zeros((1, dim), jnp.float32)
    for block, out in enumerate((even, odd)):
        key, value = key_columns(block, dim)
        back = grad_own[:, key] + came[:, key].astype(jnp.float32)
        back = back * cosine[...] - turned(back) * sine[...]
        unit, inverse = unit_of(raw[:, (4 * block + 2) * dim : (4 * block + 3) * dim])
        total += jnp.sum(unit * back, 0, keepdims=True)
        back = back * gain[...]
        back = inverse * (back - unit * jnp.mean(back * unit, -1, keepdims=True))
        out[:, : 2 * dim] = grad_query[:, 2 * block * dim : (2 * block + 2) * dim]
        out[:, 2 * dim : 3 * dim] = back.astype(jnp.bfloat16)
        grad_value = grad_own[:, value] + came[:, value].astype(jnp.float32)
        out[:, 3 * dim :] = grad_value.astype(jnp.bfloat16)
    gain_part[...] = total


def vmem_call(body, outs, scratch=(), scalars=0, name=None):
    def call(*args):
        in_specs = [
            pl.BlockSpec(memory_space=pltpu.SMEM if i < scalars else pltpu.VMEM)
            for i in range(len(args))
        ]
        return pl.pallas_call(
            body,
            grid=(1,),
            out_shape=outs,
            in_specs=in_specs,
            out_specs=jax.tree.map(lambda _: pl.BlockSpec(memory_space=pltpu.VMEM), outs),
            scratch_shapes=scratch,
            compiler_params=pltpu.CompilerParams(vmem_limit_bytes=VMEM_BYTES),
        cost_estimate=FREE,
            name=name,
        )(*args)

    return call


def hidden_units(mids, grads_y, weights):
    width, units = weights.shape[0], weights.shape[1] // 3
    count = len(mids)
    heights = [m.shape[0] for m in mids]
    rows, cut = sum(heights), units // 3

    def body(*refs):
        gate_w, up_w, w_down, act, grad_gate, grad_up = refs[2 * count :]
        start = 0
        for mid, grad_y in zip(refs[:count], refs[count : 2 * count]):
            at = slice(start, start + mid.shape[0])
            start += mid.shape[0]
            gate = jnp.dot(mid[...], gate_w[...], preferred_element_type=jnp.float32)
            up = jnp.dot(mid[...], up_w[...], preferred_element_type=jnp.float32)
            grad_act = jnp.dot(grad_y[...], w_down[...], preferred_element_type=jnp.float32)
            sigma = jax.nn.sigmoid(gate)
            swish = gate * sigma
            act[at, :] = (swish * up).astype(jnp.bfloat16)
            slope = grad_act * up * sigma * (1.0 + gate * (1.0 - sigma))
            grad_gate[at, :] = slope.astype(jnp.bfloat16)
            grad_up[at, :] = (grad_act * swish).astype(jnp.bfloat16)

    row_specs = [
        pl.BlockSpec((h, width), lambda j: (0, 0), pipeline_mode=pl.Buffered(1)) for h in heights
    ]
    return pl.pallas_call(
        body,
        grid=(3,),
        out_shape=[jax.ShapeDtypeStruct((rows, units), jnp.bfloat16)] * 3,
        in_specs=[
            *row_specs,
            *row_specs,
            pl.BlockSpec((width, cut), lambda j: (0, j)),
            pl.BlockSpec((width, cut), lambda j: (0, j + 3)),
            pl.BlockSpec((width, cut), lambda j: (0, j + 6)),
        ],
        out_specs=[pl.BlockSpec((rows, cut), lambda j: (0, j))] * 3,
        compiler_params=pltpu.CompilerParams(vmem_limit_bytes=VMEM_BYTES),
        cost_estimate=FREE,
        name="hidden_units",
    )(*mids, *grads_y, weights, weights, weights)


def from_hidden(pairs, eighths):
    count, parts = len(pairs), len(eighths)
    rows, units = pairs[0][0].shape[0] // 8, pairs[0][0].shape[1]
    width = pairs[0][1].shape[0]
    cut = width // 4

    def body(*refs):
        ins, outs = refs[: -(parts // 2)], refs[-(parts // 2) :]
        total = 0.0
        for i in range(count):
            part = ins[i * (parts + 1) : (i + 1) * (parts + 1)]
            left = jnp.concatenate([p[...] for p in part[:-1]], 0)
            total = total + nt(left, part[-1][...])
        for i, out in enumerate(outs):
            out[...] = total[2 * i * rows : 2 * (i + 1) * rows].astype(jnp.bfloat16)

    specs, args = [], []
    for left, right, at in pairs:
        specs += [pl.BlockSpec((rows, units), lambda j, e=e: (e, 0)) for e in eighths]
        specs.append(pl.BlockSpec((cut, units), lambda j, at=at: (j, at)))
        args += [left] * parts + [right]
    return pl.pallas_call(
        body,
        grid=(4,),
        out_shape=[jax.ShapeDtypeStruct((2 * rows, width), jnp.bfloat16)] * (parts // 2),
        in_specs=specs,
        out_specs=[pl.BlockSpec((2 * rows, cut), lambda j: (0, j))] * (parts // 2),
        compiler_params=pltpu.CompilerParams(vmem_limit_bytes=VMEM_BYTES),
        cost_estimate=FREE,
        name="from_hidden",
    )(*args)


def row_outer(lefts, groups, first, tiles, added=None, places=None, part=None):
    rights = [right for group in groups for right in group]
    places = range(len(rights)) if places is None else places
    added = [] if added is None else [added] * len(rights)
    width = lefts[0].shape[1]
    tile = width // 8
    count = len(lefts)
    rows = sum(left.shape[0] for left in lefts)
    wide = rights[0].shape[1] // (1 if part is None else 2)
    columns = [wide * len(group) for group in groups]

    def body(*refs):
        left_refs = refs[:count]
        right_refs = refs[count : count + len(rights)]
        add_refs = refs[count + len(rights) : count + len(rights) + len(added)]
        outs = refs[count + len(rights) + len(added) :]
        place = 0
        for i, group in enumerate(groups):
            column = 0
            for _ in group:
                on = slice(column, column + wide)
                total, start = 0.0, 0
                for left in left_refs:
                    stop = start + left.shape[0]
                    total = total + tn(left[...], right_refs[place][start:stop, :])
                    start = stop
                if added:
                    total = total + add_refs[place][...].astype(jnp.float32)
                outs[i][:, on] = total.astype(jnp.bfloat16)
                place += 1
                column += wide

    return pl.pallas_call(
        body,
        grid=(tiles,),
        out_shape=[jax.ShapeDtypeStruct((tiles * tile, c), jnp.bfloat16) for c in columns],
        in_specs=[
            *(pl.BlockSpec((left.shape[0], tile), lambda j: (0, j + first)) for left in lefts),
            *(
                pl.BlockSpec(
                    (right.shape[0], wide), lambda j: (0, part or 0), pipeline_mode=pl.Buffered(1)
                )
                for right in rights
            ),
            *(
                pl.BlockSpec((tile, wide), lambda j, at=at: (j + first, at))
                for at in places[: len(added)]
            ),
        ],
        out_specs=[pl.BlockSpec((tile, c), lambda j: (j, 0)) for c in columns],
        compiler_params=pltpu.CompilerParams(vmem_limit_bytes=VMEM_BYTES),
        cost_estimate=pl.CostEstimate(
            flops=2 * rows * tiles * tile * sum(columns),
            bytes_accessed=2 * rows * (width + sum(columns)),
            transcendentals=0,
        ),
        name="row_outer",
    )(*lefts, *rights, *added)


def close_body(x, *refs):
    mixed, weights = refs[:4], refs[4:12]
    gains, resid, mid = refs[12:]
    at = pl.program_id(0)
    step = x.shape[1]
    columns = weights[0].shape[1]
    total = x[...].astype(jnp.float32)
    for i in range(8):
        part = mixed[i // 2][:, (i % 2) * columns : (i % 2 + 1) * columns]
        total = total + nt(part, weights[i][...])
    resid[:, pl.ds(pl.multiple_of(at * step, step), step)] = total

    @pl.when(at == 3)
    def _():
        unit, _ = unit_of(resid[...])
        mid[...] = (unit * gains[...]).astype(jnp.bfloat16)


def close_attention(x, mixed, weights, gains):
    rows, width = x.shape
    step = width // 4
    whole = lambda a: pl.BlockSpec(a.shape, lambda j: (0, 0))
    return pl.pallas_call(
        close_body,
        grid=(4,),
        out_shape=[
            jax.ShapeDtypeStruct((rows, width), jnp.float32),
            jax.ShapeDtypeStruct((rows, width), jnp.bfloat16),
        ],
        in_specs=[
            pl.BlockSpec((rows, step), lambda j: (0, j)),
            *(whole(m) for m in mixed),
            *(pl.BlockSpec((step, w.shape[1]), lambda j: (j, 0)) for w in weights),
            whole(gains),
        ],
        out_specs=[pl.BlockSpec((rows, width), lambda j: (0, 0))] * 2,
        compiler_params=pltpu.CompilerParams(vmem_limit_bytes=VMEM_BYTES),
        cost_estimate=FREE,
        name="close_attention",
    )(x, *mixed, *weights, gains)


def back_to_rows(blocks, weights):
    rows = blocks[0].shape[0]
    step, columns = weights[0][0].shape
    count = len(blocks)

    def body(*refs):
        lefts = refs[:count]
        hbm = refs[count : 3 * count]
        out = refs[3 * count]
        held, sems = refs[3 * count + 1 :]
        copies = []
        for i in range(count):
            own, came = hbm[2 * i : 2 * i + 2]
            copies.append(
                [
                    pltpu.make_async_copy(own, held.at[i, :step], sems.at[i, 0]),
                    pltpu.make_async_copy(came, held.at[i, step:], sems.at[i, 1]),
                ]
            )
        for some in copies:
            for copy in some:
                copy.start()
        for i in range(count):
            for copy in copies[i]:
                copy.wait()
            for k in range(4):
                on = slice(k * step, (k + 1) * step)
                part = nt(lefts[i][...], held[i, on])
                if i == 0:
                    out[:, on] = part
                else:
                    out[:, on] += part

    return pl.pallas_call(
        body,
        grid=(1,),
        out_shape=jax.ShapeDtypeStruct((rows, 4 * step), jnp.float32),
        in_specs=[pl.BlockSpec(memory_space=pltpu.VMEM)] * count
        + [pl.BlockSpec(memory_space=pl.ANY)] * (2 * count),
        out_specs=pl.BlockSpec(memory_space=pltpu.VMEM),
        scratch_shapes=[
            pltpu.VMEM((count, 4 * step, columns), jnp.bfloat16),
            pltpu.SemaphoreType.DMA((count, 2)),
        ],
        compiler_params=pltpu.CompilerParams(vmem_limit_bytes=VMEM_BYTES),
        cost_estimate=FREE,
        name="back_to_rows",
    )(*blocks, *(part for w in weights for part in w))


def on_device_block(
    tokens,
    lengths,
    attn_gain,
    w_query,
    key_matrix,
    value_matrix,
    query_gain,
    key_gain,
    w_out,
    mlp_gain,
    w_gate,
    w_up,
    w_down,
    cotangent,
):
    low, full = jnp.bfloat16, jnp.float32
    width = tokens.shape[2]
    head_dim = query_gain.shape[0]
    shards = lax.axis_size("shard")
    shard_at = lax.axis_index("shard")
    me = lax.axis_index("rep")
    core = me & 1
    count = lax.axis_size("rep")

    s = Stage()
    s.cotangent = cotangent
    piece = width // shards

    s.own_blocks = [
        column_block((w_query, key_matrix, value_matrix), me ^ i) for i in range(8)
    ]
    gain_rows = jnp.concatenate(
        [jnp.stack([attn_gain, mlp_gain]), jnp.zeros((14, piece), low)], 0
    )
    travelling = jnp.concatenate([s.own_blocks[0], gain_rows], 0)
    s.tokens = tokens
    s.out_block = column_block((w_out,), me)
    s.ffn_block = column_block((w_gate, w_up, w_down), me)
    s.before, s.behind = around(travelling, 1), around(travelling, -1)
    s.other_lengths = across(lengths, CORE)
    s.end()

    s.ahead = around(s.before, 1)
    tokens_sent = to_sequences_send(s.tokens)
    out_own = lax.all_gather(s.out_block, "shard", axis=0, tiled=True)
    del s.out_block, s.tokens
    s.end()

    parts = (s.before, s.ahead, s.behind)
    s.came = jnp.concatenate([part[:piece] for part in parts], 0)
    s.gains = jnp.concatenate([gain_rows[:2], *(part[piece : piece + 2] for part in parts)], 1)
    s.came_near = near(s.came)
    s.x_came = tokens_sent
    del s.before, s.behind, s.ahead
    s.end()

    grad_y_sent = to_sequences_send(s.cotangent)
    s.came_far = far(*s.came_near)
    s.came_other = [across(block, CORE) for block in (s.came, *s.came_near)]
    gains = rolled(s.gains.astype(full))
    s.mlp_gains = gains[1:]
    s.attn_gains = gains[:1]
    s.x_low = jnp.concatenate(in_turn(s.x_came), 0)
    rows = s.x_low.shape[0]
    x_rows = s.x_low.astype(full)
    s.inverse_in = lax.rsqrt(jnp.mean(x_rows * x_rows, -1, keepdims=True) + EPS)
    s.normed = rolled((x_rows * s.inverse_in * s.attn_gains).astype(low))
    query_gains = query_gain.astype(full)[None]
    key_gains = key_gain.astype(full)[None]
    s.head_gains = jnp.concatenate([query_gains, key_gains], 0)
    both = jnp.where(
        core == 0,
        jnp.concatenate([lengths, s.other_lengths]),
        jnp.concatenate([s.other_lengths, lengths]),
    )
    length = lax.dynamic_index_in_dim(both, shard_at, 0, keepdims=False)
    s.info = jnp.stack([core, length]).astype(jnp.int32)
    query_pos = core * rows + jnp.arange(rows, dtype=jnp.int32)
    s.valid = (query_pos < length)[:, None].astype(full)
    cosine, sine = tables(query_pos, head_dim)
    s.cosine, sine = cosine[0, :, 0], sine[0, :, 0]
    s.sine = jnp.concatenate([-sine[:, : head_dim // 2], sine[:, head_dim // 2 :]], 1)
    s.out_own = out_own
    del s.gains, s.x_came, s.other_lengths, s.cotangent
    s.end()

    head_columns = 2 * head_dim
    block_columns = 4 * head_dim
    quad_rows = jax.ShapeDtypeStruct((rows, block_columns), low)
    quad_sums = jax.ShapeDtypeStruct((rows, block_columns), full)
    gain_sum = jax.ShapeDtypeStruct((1, head_dim), full)
    project = vmem_call(
        project_body,
        [jax.ShapeDtypeStruct((rows, 2 * block_columns), full), quad_rows, quad_rows],
        name="project",
    )
    attend = vmem_call(attend_body, [quad_rows, quad_sums], scalars=1, name="attend")
    attend_back = vmem_call(
        attend_back_body,
        [quad_rows, quad_sums, quad_rows, gain_sum],
        scratch=[pltpu.VMEM((2 * rows, head_dim), full)] * 2
        + [pltpu.VMEM((rows, block_columns), low)],
        scalars=1,
        name="attend_back",
    )
    finish = vmem_call(finish_body, [quad_rows, quad_rows, gain_sum], name="finish")
    upward = [(i, i + 1) for i in range(0, count, 2)]
    downward = [(i + 1, i) for i in range(0, count, 2)]

    def project_call(i, came, other):
        return (
            project, s.normed, s.own_blocks[2 * i], came, s.own_blocks[2 * i + 1], other,
            s.cosine, s.sine, s.head_gains,
        )

    def attend_call(projected, earlier):
        return (
            lambda query, own, before: attend(s.info, query, before, own),
            *projected[1:], earlier,
        )

    came_last = jnp.concatenate(s.came_far, 0)
    s.came_last = (came_last, across(came_last, CORE))
    s.out_near = near(s.out_own)
    s.out_own_other = across(s.out_own, CORE)
    s.projected = in_order(
        [
            project_call(i, block, other)
            for i, (block, other) in enumerate(zip((s.came, *s.came_near), s.came_other))
        ]
    )
    s.grad_y_came = grad_y_sent
    del s.came_far
    s.end()

    ffn_own = lax.all_gather(s.ffn_block, "shard", axis=0, tiled=True)
    s.out_far = far(*s.out_near)
    s.out_near_other = [across(block, CORE) for block in s.out_near]
    s.earlier = [lax.ppermute(p[2], "rep", upward) for p in s.projected]
    (s.projected_last,) = in_order([project_call(3, *s.came_last)])
    del s.ffn_block
    s.end()

    grad_y = jnp.concatenate(in_turn(s.grad_y_came), 0)
    s.grad_y = jnp.where(s.valid > 0, grad_y, jnp.zeros_like(grad_y))
    grad_y_near = near(s.grad_y)
    out_last = jnp.concatenate(s.out_far, 0)
    s.out_last = (out_last, across(out_last, CORE))
    s.earlier_last = lax.ppermute(s.projected_last[2], "rep", upward)
    s.attended = in_order([attend_call(*pair) for pair in zip(s.projected, s.earlier)])
    del s.out_far, s.grad_y_came
    s.end()

    s.projected = [*s.projected, s.projected_last]
    s.earlier = [*s.earlier, s.earlier_last]
    s.out_blocks = [
        s.out_own, s.out_own_other, s.out_near[0], s.out_near_other[0], s.out_near[1],
        s.out_near_other[1], *s.out_last,
    ]
    (last,) = in_order([attend_call(s.projected_last, s.earlier_last)])
    s.attended = [*s.attended, last]
    s.mixed = [a[0] for a in s.attended]
    s.resid, s.mid = close_attention(s.x_low, s.mixed, s.out_blocks, s.mlp_gains)
    s.grad_y_near = grad_y_near
    del s.out_own, s.out_own_other, s.out_near, s.out_near_other, s.out_last
    del s.projected_last, s.earlier_last
    s.end()

    s.mid_near = near(s.mid)
    s.grad_y_far = far(*s.grad_y_near)
    s.end()

    s.mid_far = far(*s.mid_near)
    s.ffn_own = ffn_own
    s.end()

    s.mids = [s.mid, *s.mid_near, *s.mid_far]
    s.grads_y = [s.grad_y, *s.grad_y_near, *s.grad_y_far]
    s.ffn_other = across(s.ffn_own, CORE)
    units = s.ffn_own.shape[1] // 3
    s.hidden_own = hidden_units(s.mids, s.grads_y, s.ffn_own)
    del s.mid, s.mid_near, s.mid_far, s.grad_y_near, s.grad_y_far
    s.end()

    def gate_up_pairs():
        return [
            (hidden[i], weights, i - 1)
            for hidden, weights in ((s.hidden_own, s.ffn_own), (s.hidden_other, s.ffn_other))
            for i in (1, 2)
        ]

    def down_pairs():
        return [(s.hidden_own[0], s.ffn_own, 2), (s.hidden_other[0], s.ffn_other, 2)]

    def from_hidden_call(pairs, eighths):
        return (
            lambda first: from_hidden([(first, *pairs[0][1:]), *pairs[1:]], eighths),
            pairs[0][0],
        )

    def outer_call(lefts, rights, *added):
        return lambda first: row_outer(lefts, [[first, *rights[1:]]], 0, 8, *added)[0], rights[0]

    def send_near(sent):
        return across(sent[0], ACROSS_X), across(sent[1], ACROSS_Y)

    def send_far(came, rest, split):
        one_tail, two_head = rest
        return (
            across(rounded_sum(one_tail, split(came[1])[1]), ACROSS_X),
            across(rounded_sum(two_head, split(came[0])[1]), ACROSS_Y),
        )

    def total(came, came_far, own, split):
        head, tail = own
        full_sum = lambda *parts: sum(part.astype(full) for part in parts)
        return jnp.concatenate(
            [
                full_sum(head, split(came[0])[0], came_far[1]),
                full_sum(tail, split(came[1])[0], came_far[0]),
            ],
            0,
        )

    by_rows = lambda a: jnp.split(a, 2, 0)
    by_columns = lambda a: jnp.split(a, 2, 1)
    to_plane, rest_of_plane = (2, 6, 5, 7), (3, 4, 0, 1)

    s.hidden_other = hidden_units(s.mids, s.grads_y, s.ffn_other)
    (s.down_outer,) = in_order([outer_call(s.grads_y, s.hidden_other[:1])])
    s.end()

    s.down_came = across(s.down_outer, CORE)
    s.mid_sent = from_hidden(gate_up_pairs(), to_plane)
    del s.down_outer
    s.end()

    s.mid_came = send_near(s.mid_sent)
    s.down_mine, s.mid_rest, s.gate_up_outer = in_order(
        [
            outer_call(s.grads_y, s.hidden_own[:1], s.down_came),
            from_hidden_call(gate_up_pairs(), rest_of_plane),
            outer_call(s.mids, s.hidden_other[1:]),
        ]
    )
    del s.mid_sent, s.down_came
    s.end()

    down_total = lax.psum_scatter(s.down_mine, "shard", scatter_dimension=0, tiled=True)
    s.mid_came_far = send_far(s.mid_came, by_rows(s.mid_rest[0]), by_rows)
    s.gate_up_came = across(s.gate_up_outer, CORE)
    s.mlp_sent, s.mlp_rest = in_order(
        [
            from_hidden_call(down_pairs(), to_plane),
            from_hidden_call(down_pairs(), rest_of_plane),
        ]
    )
    del s.gate_up_outer, s.down_mine
    s.end()

    mlp_came = send_near(s.mlp_sent)
    grad_mid = total(s.mid_came, s.mid_came_far, by_rows(s.mid_rest[1]), by_rows)
    inverse_mid = lax.rsqrt(jnp.mean(s.resid * s.resid, -1, keepdims=True) + EPS)
    mid_unit = s.resid * inverse_mid
    s.mlp_gain_part = jnp.sum(mid_unit * grad_mid, 0)
    s.grad_resid = s.grad_y.astype(full) + norm_back(
        mid_unit, inverse_mid, grad_mid * s.mlp_gains
    )
    s.resid_low = s.grad_resid.astype(low)
    s.resid_rolled = rolled(s.resid_low)
    (s.gate_up_mine,) = in_order([outer_call(s.mids, s.hidden_own[1:], s.gate_up_came)])
    del s.mid_came, s.mid_came_far, s.mid_rest, s.gate_up_came, s.hidden_own, s.hidden_other
    del s.mids, s.grads_y, s.ffn_own, s.ffn_other
    s.end()

    def back_call(i):
        raw, query, own_pair = s.projected[i]
        return (
            lambda query, *rest: attend_back(s.info, query, *rest),
            query, s.earlier[i], own_pair, s.attended[i][1], s.resid_low,
            *s.out_blocks[2 * i : 2 * i + 2], raw, s.cosine, s.sine, s.head_gains[:1],
        )

    def finish_call(i):
        return (
            finish, s.backs[i][0], s.backs[i][1], s.returned[i], s.projected[i][0],
            s.cosine, s.sine, s.head_gains[1:],
        )

    def give_back(*chips):
        s.returned = s.returned | {
            i: lax.ppermute(s.backs[i][2], "rep", downward) for i in chips
        }

    def odd_call(left, blocks, part=None):
        return lambda first: row_outer([first], [blocks], 0, 8, part=part)[0], left

    def head_call(left, blocks, came, part=None, places=(0, 1, 2, 3)):
        groups = [[blocks[1], blocks[3]], [blocks[2]], [blocks[0]]]
        at = [places[i] for i in (1, 3, 2, 0)]
        return lambda first: row_outer([first], groups, 0, 4, came, at, part), left

    def tail_call(left, blocks, came, part=None, places=(0, 1, 2, 3)):
        groups = [[blocks[2], blocks[3]], [blocks[1]], [blocks[0]]]
        at = [places[i] for i in (2, 3, 1, 0)]
        return lambda first: row_outer([first], groups, 4, 4, came, at, part), left

    gate_up_total = lax.psum_scatter(s.gate_up_mine, "shard", scatter_dimension=0, tiled=True)
    s.returned = {}
    s.out_odd, back = in_order([odd_call(s.resid_rolled, s.mixed, 1), back_call(3)])
    s.backs = {3: back}
    s.mlp_came = mlp_came
    s.down_total = down_total
    del s.gate_up_mine, s.mlp_sent
    s.end()

    s.mlp_came_far = send_far(s.mlp_came, by_rows(s.mlp_rest[0]), by_rows)
    s.out_came = across(s.out_odd, CORE)
    give_back(3)
    back1, back2 = in_order([back_call(1), back_call(2)])
    s.backs = s.backs | {1: back1, 2: back2}
    del s.out_odd
    s.end()

    s.down_near = near(s.down_total)
    give_back(1, 2)
    mlp_out = total(s.mlp_came, s.mlp_came_far, by_rows(s.mlp_rest[1]), by_rows)
    s.output = (s.valid * (s.resid + mlp_out)).astype(low)
    s.out_head, s.out_tail, back, finished = in_order(
        [
            head_call(s.resid_rolled, s.mixed, s.out_came, 0),
            tail_call(s.resid_rolled, s.mixed, s.out_came, 0),
            back_call(0),
            finish_call(3),
        ]
    )
    s.backs = s.backs | {0: back}
    s.finished = {3: finished}
    del s.mlp_came, s.mlp_came_far, s.mlp_rest, s.out_came, s.resid
    s.end()

    output_sent = from_sequences_send(s.output)
    s.out_near = send_near((s.out_head[0], s.out_tail[0]))
    s.down_far = far(*s.down_near)
    give_back(0)
    finished1, finished2 = in_order([finish_call(1), finish_call(2)])
    s.finished = s.finished | {1: finished1, 2: finished2}
    del s.output
    s.end()

    s.out_far = send_far(s.out_near, (s.out_tail[1], s.out_head[1]), by_columns)
    s.down_own = jnp.concatenate([s.down_total, *s.down_near, *s.down_far], 0)
    s.down_other = across(s.down_own, CORE)
    (finished,) = in_order([finish_call(0)])
    s.finished = s.finished | {0: finished}
    (s.qkv_odd,) = in_order([odd_call(s.normed, [s.finished[i][1] for i in range(4)])])
    s.gate_up_total = gate_up_total
    del s.down_total, s.down_near, s.down_far
    s.end()

    my_group = me.astype(jnp.int32)[None]

    def whole_call(widths, own, other):
        return lambda first: whole_columns(my_group, first, other, widths), own

    s.qkv_came = across(s.qkv_odd, CORE)
    s.gate_up_near = near(s.gate_up_total)
    out_sum = total(s.out_near, s.out_far, (s.out_head[2], s.out_tail[2]), by_columns)
    s.out_chunks = jnp.split(out_sum.astype(low), shards, 0)
    s.out_ring = ring_sum_first(s.out_chunks)
    weights = [
        pair
        for i, block in enumerate(zip((s.came, *s.came_near), s.came_other))
        for pair in ((s.own_blocks[2 * i], block[0]), (s.own_blocks[2 * i + 1], block[1]))
    ] + [(s.own_blocks[6 + i], s.came_last[i]) for i in range(2)]
    blocks = [part for i in range(4) for part in s.finished[i][:2]]
    grad_in, s.whole_down = in_order(
        [
            (lambda first: back_to_rows([first, *blocks[1:]], weights), blocks[0]),
            whole_call((units,), s.down_own, s.down_other),
        ]
    )
    grad_in = rolled(grad_in)
    x_unit = s.x_low.astype(full) * s.inverse_in
    s.attn_gain_part = jnp.sum(x_unit * grad_in, 0)
    s.grad_tokens = (
        s.grad_resid + norm_back(x_unit, s.inverse_in, grad_in * s.attn_gains)
    ).astype(low)
    s.output_came = output_sent
    del s.qkv_odd, s.out_near, s.out_far, s.out_head, s.out_tail, s.down_own, s.down_other
    del s.own_blocks, s.came, s.came_near, s.came_other, s.came_last, s.grad_resid, s.x_low
    s.end()

    s.gate_up_far = far(*s.gate_up_near)
    s.out_ring_last = around(rounded_sum(s.out_chunks[3], s.out_ring[0]), 1)
    even = [s.finished[i][0] for i in range(4)]
    first_head, first_tail, second_head, second_tail = in_order(
        [
            call(s.normed, even, s.qkv_came, half, range(half, 8, 2))
            for half in range(2)
            for call in (head_call, tail_call)
        ]
    )
    s.heads = [first_head, second_head]
    s.tails = [first_tail, second_tail]
    s.gain_parts = jnp.concatenate(
        [
            s.attn_gain_part,
            s.mlp_gain_part,
            sum(s.backs[i][3] for i in range(4))[0],
            sum(s.finished[i][2] for i in range(4))[0],
        ]
    )
    del s.qkv_came, s.finished, s.backs
    s.end()

    grad_tokens_sent = from_sequences_send(s.grad_tokens)

    def qkv_near(half):
        return send_near((s.heads[half][0], s.tails[half][0]))

    def qkv_far(came, half):
        return send_far(came, (s.tails[half][1], s.heads[half][1]), by_columns)

    def qkv_chunks(came, came_far, half):
        own = total(came, came_far, (s.heads[half][2], s.tails[half][2]), by_columns)
        return jnp.split(own.astype(low), shards, 0)

    s.near0 = qkv_near(0)
    s.gate_up_own = jnp.concatenate([s.gate_up_total, *s.gate_up_near, *s.gate_up_far], 0)
    s.gate_up_other = across(s.gate_up_own, CORE)
    s.out_total = rounded_sum(s.out_chunks[0], s.out_ring[1], s.out_ring_last)
    s.gain_came = across(s.gain_parts, CORE)
    del s.out_chunks, s.out_ring, s.out_ring_last, s.gate_up_near, s.gate_up_far
    del s.gate_up_total, s.grad_tokens
    s.end()

    s.far0 = qkv_far(s.near0, 0)
    s.near1 = qkv_near(1)
    s.gain_parts = s.gain_parts + s.gain_came
    s.gain_came = across(s.gain_parts, ACROSS_X)
    (s.whole_gate_up,) = in_order([whole_call((units, units), s.gate_up_own, s.gate_up_other)])
    del s.gate_up_own, s.gate_up_other
    s.end()

    s.chunks0 = qkv_chunks(s.near0, s.far0, 0)
    s.ring0 = ring_sum_first(s.chunks0)
    s.far1 = qkv_far(s.near1, 1)
    s.gain_parts = s.gain_parts + s.gain_came
    s.gain_came = across(s.gain_parts, ACROSS_Y)
    del s.near0, s.far0
    s.tokens_came = grad_tokens_sent
    s.end()

    s.last0 = around(rounded_sum(s.chunks0[3], s.ring0[0]), 1)
    s.chunks1 = qkv_chunks(s.near1, s.far1, 1)
    s.ring1 = ring_sum_first(s.chunks1)
    s.gain_parts = s.gain_parts + s.gain_came
    s.gain_came = lax.ppermute(s.gain_parts, "shard", [(i, i ^ 1) for i in range(shards)])
    del s.near1, s.far1, s.heads, s.tails
    s.end()

    query_total = rounded_sum(s.chunks0[0], s.ring0[1], s.last0)
    s.total0 = jnp.concatenate([query_total, s.out_total], 1)
    s.spread0 = near(s.total0)
    s.last1 = around(rounded_sum(s.chunks1[3], s.ring1[0]), 1)
    s.gain_parts = s.gain_parts + s.gain_came
    s.gain_came = lax.ppermute(s.gain_parts, "shard", [(i, i ^ 2) for i in range(shards)])
    del s.chunks0, s.ring0, s.last0, s.out_total
    s.end()

    s.spread_far0 = far(*s.spread0)
    s.total1 = rounded_sum(s.chunks1[0], s.ring1[1], s.last1)
    s.spread1 = near(s.total1)
    del s.chunks1, s.ring1, s.last1
    s.end()

    s.own0 = jnp.concatenate([s.total0, *s.spread0, *s.spread_far0], 0)
    s.other0 = across(s.own0, CORE)
    s.spread_far1 = far(*s.spread1)
    del s.total0, s.spread0, s.spread_far0
    s.end()

    s.own1 = jnp.concatenate([s.total1, *s.spread1, *s.spread_far1], 0)
    s.other1 = across(s.own1, CORE)
    (s.whole0,) = in_order([whole_call((head_columns, head_columns), s.own0, s.other0)])
    del s.own0, s.other0, s.total1, s.spread1, s.spread_far1
    s.end()

    ((whole_key, whole_value),) = in_order(
        [whole_call((head_dim, head_dim), s.own1, s.other1)]
    )
    gain_sums = s.gain_parts + s.gain_came
    wide = lax.dynamic_slice_in_dim(
        gain_sums[: 2 * width].reshape(2, width), shard_at * piece, piece, 1
    )
    narrow = gain_sums[2 * width :]
    return (
        jnp.stack(in_turn(s.output_came)),
        jnp.stack(in_turn(s.tokens_came)),
        wide[0],
        s.whole0[0],
        whole_key,
        whole_value,
        narrow[:head_dim],
        narrow[head_dim:],
        s.whole0[1],
        wide[1],
        *s.whole_gate_up,
        *s.whole_down,
    )


def solution(mesh):
    sizes = (mesh.shape["rep"], mesh.shape["shard"])
    return jax.shard_map(
        on_device_block if sizes == (8, 4) else on_device,
        mesh=mesh,
        in_specs=(
            P("rep", "shard", None),
            P("rep"),
            P("shard"),
            P("shard", None),
            P("shard", None),
            P("shard", None),
            P(),
            P(),
            P("shard", None),
            P("shard"),
            P("shard", None),
            P("shard", None),
            P("shard", None),
            P("rep", "shard", None),
        ),
        out_specs=(
            P("rep", "shard", None),
            P("rep", "shard", None),
            P("shard"),
            P("shard", None),
            P("shard", None),
            P("shard", None),
            P(),
            P(),
            P("shard", None),
            P("shard"),
            P("shard", None),
            P("shard", None),
            P("shard", None),
        ),
        check_vma=False,
    )
```

```python
import jax
import jax.numpy as jnp
from jax import lax
from jax.experimental import pallas as pl
from jax.experimental.pallas import tpu as pltpu
from jax.sharding import PartitionSpec as P

WINDOW = 512


EPS = 1e-06
ROPE_BASE = 1000000.0
NEG = -1e30


def passed_along(x, axis, by):
    devices = lax.axis_size(axis)
    pairs = [(i, i + by) for i in range(devices) if 0 <= i + by < devices]
    return lax.ppermute(x, axis, pairs)


def tables(positions, head_dim):
    half = head_dim // 2
    freq = ROPE_BASE ** (-jnp.arange(half, dtype=jnp.float32) * 2.0 / head_dim)
    angle = positions.astype(jnp.float32)[:, None] * freq[None, :]
    angle = jnp.concatenate([angle, angle], -1)
    return (jnp.cos(angle)[None, :, None, :], jnp.sin(angle)[None, :, None, :])


def rotated_rows(value_rows):
    half = value_rows.shape[-1] // 2
    return jnp.concatenate([-value_rows[..., half:], value_rows[..., :half]], -1)


def head_norm(raw, gain):
    inverse = lax.rsqrt(jnp.mean(raw * raw, -1, keepdims=True) + EPS)
    unit = raw * inverse
    return (unit, inverse, unit * gain)


def norm_back(unit, inverse, grad_unit):
    return inverse * (grad_unit - unit * jnp.mean(grad_unit * unit, -1, keepdims=True))


def head_norm_back(unit, inverse, grad_normed, gain):
    grad_raw = norm_back(unit, inverse, grad_normed * gain)
    return (grad_raw, jnp.sum(unit * grad_normed, axis=(0, 1, 2)))


def scores(query_rows, keys, allowed, scale):
    raw = (
        jnp.einsum("sqhgd,skhd->shgqk", query_rows, keys, preferred_element_type=jnp.float32)
        * scale
    )
    return jnp.where(allowed[:, None, None], raw, NEG)


def outer(left, right):
    return jnp.einsum("rc,rf->cf", left, right, preferred_element_type=jnp.float32)


def on_device(
    tokens,
    lengths,
    attn_gain,
    w_query,
    key_matrix,
    value_matrix,
    query_gain,
    key_gain,
    w_out,
    mlp_gain,
    w_gate,
    w_up,
    w_down,
    cotangent,
):
    seq_count, piece, width = tokens.shape
    head_dim = query_gain.shape[0]
    heads_q = w_query.shape[1] // head_dim
    heads_kv = key_matrix.shape[1] // head_dim
    groups = heads_q // heads_kv
    rows = seq_count * piece
    scale = head_dim ** (-0.5)
    reach = (WINDOW + piece - 2) // piece
    owned = width // lax.axis_size("shard")
    shard_at = lax.axis_index("shard")
    query_pos = shard_at * piece + jnp.arange(piece, dtype=jnp.int32)
    key_pos = (shard_at - reach) * piece + jnp.arange((reach + 1) * piece, dtype=jnp.int32)
    near = (
        (key_pos[None, :] <= query_pos[:, None])
        & (query_pos[:, None] - key_pos[None, :] < WINDOW)
        & (key_pos[None, :] >= 0)
    )
    live = (key_pos[None, None, :] < lengths[:, None, None]) | (
        key_pos[None, :] == query_pos[:, None]
    )[None]
    allowed = near[None] & live
    valid = (query_pos[None, :] < lengths[:, None]).astype(jnp.float32).reshape(rows, 1)
    cosine_table, sine_table = tables(query_pos, head_dim)
    x_rows = tokens.astype(jnp.float32).reshape(rows, width)
    inverse_in = lax.rsqrt(jnp.mean(x_rows * x_rows, -1, keepdims=True) + EPS)
    x_unit = x_rows * inverse_in
    gain_piece = lax.all_gather(attn_gain, "shard", axis=0, tiled=True)
    query_piece = lax.all_gather(w_query, "shard", axis=0, tiled=True)
    key_piece = lax.all_gather(key_matrix, "shard", axis=0, tiled=True)
    value_piece = lax.all_gather(value_matrix, "shard", axis=0, tiled=True)
    normed_piece = (x_unit * gain_piece.astype(jnp.float32)).astype(jnp.bfloat16)
    acc_q = jnp.dot(normed_piece, query_piece, preferred_element_type=jnp.float32)
    acc_k = jnp.dot(normed_piece, key_piece, preferred_element_type=jnp.float32)
    acc_v = jnp.dot(normed_piece, value_piece, preferred_element_type=jnp.float32)
    normalized_rows = normed_piece
    gains = gain_piece.astype(jnp.float32)
    attn_in = normalized_rows
    attn_gains = gains
    query_unit, query_inverse, query_rows_normalized = head_norm(
        acc_q.reshape(seq_count, piece, heads_q, head_dim), query_gain.astype(jnp.float32)
    )
    key_unit, key_inverse, key_normed = head_norm(
        acc_k.reshape(seq_count, piece, heads_kv, head_dim), key_gain.astype(jnp.float32)
    )
    query_rows = (
        (query_rows_normalized * cosine_table + rotated_rows(query_rows_normalized) * sine_table)
        .astype(jnp.bfloat16)
        .reshape(seq_count, piece, heads_kv, groups, head_dim)
    )
    keys_own = (key_normed * cosine_table + rotated_rows(key_normed) * sine_table).astype(
        jnp.bfloat16
    )
    values_own = acc_v.reshape(seq_count, piece, heads_kv, head_dim).astype(jnp.bfloat16)
    own_pair = jnp.stack([keys_own, values_own])
    parts = []
    for fetch_back in range(reach, 0, -1):
        parts.append(passed_along(own_pair, "shard", fetch_back))
    parts.append(own_pair)
    near_pair = jnp.concatenate(parts, 2)
    score = scores(query_rows, near_pair[0], allowed, scale)
    top = jnp.max(score, -1, keepdims=True)
    expo = jnp.exp(score - top)
    total = jnp.sum(expo, -1, keepdims=True)
    prob = expo / total
    log_total = top + jnp.log(total)
    mixed = jnp.einsum(
        "shgqk,skhd->sqhgd",
        prob.astype(jnp.bfloat16),
        near_pair[1],
        preferred_element_type=jnp.float32,
    )
    mixed_rows = mixed.reshape(rows, heads_q * head_dim).astype(jnp.bfloat16)
    resid = x_rows + jnp.einsum(
        "rf,nf->rn",
        mixed_rows,
        lax.all_gather(w_out, "shard", axis=0, tiled=True),
        preferred_element_type=jnp.float32,
    )
    inverse_mid = lax.rsqrt(jnp.mean(resid * resid, -1, keepdims=True) + EPS)
    mid_unit = resid * inverse_mid
    gain_piece = lax.all_gather(mlp_gain, "shard", axis=0, tiled=True)
    gate_piece = lax.all_gather(w_gate, "shard", axis=0, tiled=True)
    up_piece = lax.all_gather(w_up, "shard", axis=0, tiled=True)
    normed_piece = (mid_unit * gain_piece.astype(jnp.float32)).astype(jnp.bfloat16)
    acc_gate = jnp.dot(normed_piece, gate_piece, preferred_element_type=jnp.float32)
    acc_up = jnp.dot(normed_piece, up_piece, preferred_element_type=jnp.float32)
    normalized_rows = normed_piece
    gains = gain_piece.astype(jnp.float32)
    mlp_in = normalized_rows
    sigma = jax.nn.sigmoid(acc_gate)
    swish = acc_gate * sigma
    act = (swish * acc_up).astype(jnp.bfloat16)
    mlp_out = jnp.einsum(
        "rf,nf->rn",
        act,
        lax.all_gather(w_down, "shard", axis=0, tiled=True),
        preferred_element_type=jnp.float32,
    )
    output = (valid * (resid + mlp_out)).astype(jnp.bfloat16).reshape(seq_count, piece, width)
    grad_y = cotangent.astype(jnp.float32).reshape(rows, width) * valid
    grad_y_low = grad_y.astype(jnp.bfloat16)
    grad_act = jnp.dot(
        grad_y_low,
        lax.all_gather(w_down, "shard", axis=0, tiled=True),
        preferred_element_type=jnp.float32,
    )
    grad_gate = (grad_act * acc_up * sigma * (1.0 + acc_gate * (1.0 - sigma))).astype(jnp.bfloat16)
    grad_up = (grad_act * swish).astype(jnp.bfloat16)
    gate_piece, up_piece = lax.all_gather((w_gate, w_up), "shard", axis=0, tiled=True)
    grad_mid = jnp.einsum(
        "rf,nf->rn", grad_gate, gate_piece, preferred_element_type=jnp.float32
    ) + jnp.einsum("rf,nf->rn", grad_up, up_piece, preferred_element_type=jnp.float32)
    grad_resid = grad_y + norm_back(mid_unit, inverse_mid, grad_mid * gains)
    mlp_gain_part = jnp.sum(mid_unit * grad_mid, 0)
    normalized_rows = mlp_in
    mlp_grads = jax.tree.map(
        lambda part: lax.psum_scatter(
            part.astype(jnp.bfloat16), "shard", scatter_dimension=0, tiled=True
        ).astype(jnp.float32),
        (
            outer(normalized_rows, grad_gate),
            outer(normalized_rows, grad_up),
            outer(grad_y_low, act),
        ),
    )
    resid_low = grad_resid.astype(jnp.bfloat16)
    grad_mixed = jnp.dot(
        resid_low,
        lax.all_gather(w_out, "shard", axis=0, tiled=True),
        preferred_element_type=jnp.float32,
    )
    grad_mixed = grad_mixed.astype(jnp.bfloat16).reshape(
        seq_count, piece, heads_kv, groups, head_dim
    )
    prob_again = jnp.exp(scores(query_rows, near_pair[0], allowed, scale) - log_total)
    grad_prob = jnp.einsum(
        "sqhgd,skhd->shgqk", grad_mixed, near_pair[1], preferred_element_type=jnp.float32
    )
    grad_values = jnp.einsum(
        "shgqk,sqhgd->skhd",
        prob_again.astype(jnp.bfloat16),
        grad_mixed,
        preferred_element_type=jnp.float32,
    )
    grad_score = (
        prob_again * (grad_prob - jnp.sum(prob_again * grad_prob, -1, keepdims=True))
    ).astype(jnp.bfloat16)
    grad_queries = (
        jnp.einsum(
            "shgqk,skhd->sqhgd", grad_score, near_pair[0], preferred_element_type=jnp.float32
        )
        * scale
    )
    grad_keys = (
        jnp.einsum("shgqk,sqhgd->skhd", grad_score, query_rows, preferred_element_type=jnp.float32)
        * scale
    )
    grad_pair = jnp.stack([grad_keys, grad_values])
    own_grad = grad_pair[:, :, reach * piece :]
    for back in range(1, reach + 1):
        lower = (reach - back) * piece
        own_grad = own_grad + passed_along(grad_pair[:, :, lower : lower + piece], "shard", -back)
    grad_query_post = grad_queries.reshape(seq_count, piece, heads_q, head_dim)
    grad_query_normed = grad_query_post * cosine_table - rotated_rows(grad_query_post * sine_table)
    grad_key_normed = own_grad[0] * cosine_table - rotated_rows(own_grad[0] * sine_table)
    grad_query_raw, query_gain_grad = head_norm_back(
        query_unit, query_inverse, grad_query_normed, query_gain.astype(jnp.float32)
    )
    grad_key_raw, key_gain_grad = head_norm_back(
        key_unit, key_inverse, grad_key_normed, key_gain.astype(jnp.float32)
    )
    grad_query_low = grad_query_raw.reshape(rows, heads_q * head_dim).astype(jnp.bfloat16)
    grad_key_low = grad_key_raw.reshape(rows, heads_kv * head_dim).astype(jnp.bfloat16)
    grad_value_low = own_grad[1].reshape(rows, heads_kv * head_dim).astype(jnp.bfloat16)
    query_piece, key_piece, value_piece = lax.all_gather(
        (w_query, key_matrix, value_matrix), "shard", axis=0, tiled=True
    )
    grad_in = (
        jnp.einsum("rf,nf->rn", grad_query_low, query_piece, preferred_element_type=jnp.float32)
        + jnp.einsum("rf,nf->rn", grad_key_low, key_piece, preferred_element_type=jnp.float32)
        + jnp.einsum("rf,nf->rn", grad_value_low, value_piece, preferred_element_type=jnp.float32)
    )
    grad_tokens = (
        (grad_resid + norm_back(x_unit, inverse_in, grad_in * attn_gains))
        .astype(jnp.bfloat16)
        .reshape(seq_count, piece, width)
    )
    attn_gain_part = jnp.sum(x_unit * grad_in, 0)
    normalized_rows = attn_in
    attn_grads = jax.tree.map(
        lambda part: lax.psum_scatter(
            part.astype(jnp.bfloat16), "shard", scatter_dimension=0, tiled=True
        ).astype(jnp.float32),
        (
            outer(normalized_rows, grad_query_low),
            outer(normalized_rows, grad_key_low),
            outer(normalized_rows, grad_value_low),
            outer(resid_low, mixed_rows),
        ),
    )
    head_grads = lax.psum(
        (query_gain_grad, key_gain_grad, attn_gain_part, mlp_gain_part), ("rep", "shard")
    )
    attn_gain_total = lax.dynamic_slice_in_dim(head_grads[2], shard_at * owned, owned, 0)
    mlp_gain_total = lax.dynamic_slice_in_dim(head_grads[3], shard_at * owned, owned, 0)
    summed = (
        lax.psum(attn_grads[0].astype(jnp.bfloat16), "rep").astype(jnp.float32),
        lax.psum(attn_grads[1].astype(jnp.bfloat16), "rep").astype(jnp.float32),
        lax.psum(attn_grads[2].astype(jnp.bfloat16), "rep").astype(jnp.float32),
        lax.psum(attn_grads[3].astype(jnp.bfloat16), "rep").astype(jnp.float32),
        lax.psum(mlp_grads[0].astype(jnp.bfloat16), "rep").astype(jnp.float32),
        lax.psum(mlp_grads[1].astype(jnp.bfloat16), "rep").astype(jnp.float32),
        lax.psum(mlp_grads[2].astype(jnp.bfloat16), "rep").astype(jnp.float32),
    )
    attn_grads = summed[:4]
    mlp_grads = summed[4:]
    return (
        output,
        grad_tokens,
        attn_gain_total,
        attn_grads[0],
        attn_grads[1],
        attn_grads[2],
        head_grads[0],
        head_grads[1],
        attn_grads[3],
        mlp_gain_total,
        mlp_grads[0],
        mlp_grads[1],
        mlp_grads[2],
    )


CORE, ACROSS_X, ACROSS_Y = 1, 2, 4
VMEM_BYTES = 56 * 2**20
FREE = pl.CostEstimate(flops=1, bytes_accessed=1, transcendentals=0)


def across(x, mask):
    count = lax.axis_size("rep")
    return lax.ppermute(x, "rep", [(i, i ^ mask) for i in range(count)])


def around(x, by):
    count = lax.axis_size("shard")
    return lax.ppermute(x, "shard", [(i, (i + by) % count) for i in range(count)])


class Stage(dict):
    __getattr__ = dict.__getitem__
    __setattr__ = dict.__setitem__
    __delattr__ = dict.__delitem__

    def end(self):
        self.update(lax.optimization_barrier(dict(self)))


def in_order(calls):
    outs = []
    for call, first, *rest in calls:
        if outs:
            last = outs[-1][0] if isinstance(outs[-1], (list, tuple)) else outs[-1]
            first = lax.optimization_barrier((first, last))[0]
        outs.append(call(first, *rest))
    return outs


def ring_sum_first(chunks):
    return around(chunks[2], 1), around(chunks[1], -1)


def near(piece):
    return across(piece, ACROSS_X), across(piece, ACROSS_Y)


def far(from_x, from_y):
    half = from_x.shape[0] // 2
    return across(from_x[:half], ACROSS_Y), across(from_y[half:], ACROSS_X)


def rounded_sum(*parts):
    return sum(part.astype(jnp.float32) for part in parts).astype(jnp.bfloat16)


def sequence_pairs(turn):
    groups, shards = lax.axis_size("rep"), lax.axis_size("shard")
    pairs = []
    for group in range(groups):
        chip, core = divmod(group, 2)
        for at in range(shards):
            to_group, to_shard = 2 * chip + at // 2, 2 * core + (turn ^ (at & 1))
            pairs.append((group * shards + at, to_group * shards + to_shard))
    return pairs


def rolled(x):
    count, at = lax.axis_size("shard"), lax.axis_index("shard")
    width = x.shape[1] // count
    return jnp.concatenate(
        [lax.dynamic_slice_in_dim(x, ((at - i) % count) * width, width, 1) for i in range(count)],
        1,
    )


def to_sequences_send(x):
    odd = lax.axis_index("shard") & 1
    return [
        lax.ppermute(
            lax.dynamic_index_in_dim(x, turn ^ odd, 0, keepdims=False),
            ("rep", "shard"),
            sequence_pairs(turn),
        )
        for turn in range(2)
    ]


def from_sequences_send(x):
    odd = lax.axis_index("shard") & 1
    x = x.reshape(2, x.shape[0] // 2, x.shape[1])
    return [
        lax.ppermute(
            lax.dynamic_index_in_dim(x, turn ^ odd, 0, keepdims=False),
            ("rep", "shard"),
            [(to, at) for at, to in sequence_pairs(turn)],
        )
        for turn in range(2)
    ]


def in_turn(came):
    even = lax.axis_index("shard") & 1 == 0
    return [jnp.where(even, came[0], came[1]), jnp.where(even, came[1], came[0])]


def column_block(weights, at):
    cuts = [w.shape[1] // 8 for w in weights]
    return jnp.concatenate(
        [lax.dynamic_slice_in_dim(w, at * cut, cut, 1) for w, cut in zip(weights, cuts)], 1
    )


def whole_columns(me, own, other, widths):
    rows, columns = own.shape[0] // 4, own.shape[1]

    def body(me_ref, own_ref, other_ref, *outs):
        def put(block):
            start = 0
            for out, width in zip(outs, widths):
                out[...] = block[:, start : start + width].astype(jnp.float32)
                start += width

        mine = (me_ref[0] ^ pl.program_id(0)) & 1 == 0
        pl.when(mine)(lambda: put(own_ref))
        pl.when(jnp.logical_not(mine))(lambda: put(other_ref))

    spec = pl.BlockSpec((rows, columns), lambda i, at: ((at[0] ^ i) >> 1, 0))
    return pl.pallas_call(
        body,
        grid_spec=pltpu.PrefetchScalarGridSpec(
            num_scalar_prefetch=1,
            grid=(8,),
            in_specs=[spec, spec],
            out_specs=[pl.BlockSpec((rows, w), lambda i, at: (0, i)) for w in widths],
        ),
        out_shape=[jax.ShapeDtypeStruct((rows, 8 * w), jnp.float32) for w in widths],
        compiler_params=pltpu.CompilerParams(vmem_limit_bytes=VMEM_BYTES),
        cost_estimate=FREE,
        name="whole_columns",
    )(me, own, other)


def turned(x):
    return pltpu.roll(x, x.shape[-1] // 2, x.ndim - 1)


def nt(left, right):
    return lax.dot_general(
        left, right, (((1,), (1,)), ((), ())), preferred_element_type=jnp.float32
    )


def tn(left, right):
    return lax.dot_general(
        left, right, (((0,), (0,)), ((), ())), preferred_element_type=jnp.float32
    )


def unit_of(raw):
    inverse = lax.rsqrt(jnp.mean(raw * raw, -1, keepdims=True) + EPS)
    return raw * inverse, inverse


def project_body(
    normed, own0, came0, own1, came1, cosine, sine, gains, raw, query, key_value
):
    step = own0.shape[0]
    dim = cosine.shape[1]
    for block, (own, came) in enumerate(((own0, came0), (own1, came1))):
        at = block * 4 * dim
        raw[:, at : at + 4 * dim] = jnp.dot(
            normed[:, :step], own[...], preferred_element_type=jnp.float32
        ) + jnp.dot(normed[:, step:], came[...], preferred_element_type=jnp.float32)
        for i in range(3):
            unit, _ = unit_of(raw[:, at + i * dim : at + (i + 1) * dim])
            head = unit * gains[i // 2 : i // 2 + 1, :]
            head = (head * cosine[...] + turned(head) * sine[...]).astype(jnp.bfloat16)
            if i < 2:
                query[:, (2 * block + i) * dim : (2 * block + i + 1) * dim] = head
            else:
                key_value[:, 2 * block * dim : (2 * block + 1) * dim] = head
        key_value[:, (2 * block + 1) * dim : (2 * block + 2) * dim] = raw[
            :, at + 3 * dim : at + 4 * dim
        ].astype(jnp.bfloat16)


def window_mask(info, part, rows, columns):
    half = columns - rows
    row = lax.broadcasted_iota(jnp.int32, (rows, columns), 0)
    column = lax.broadcasted_iota(jnp.int32, (rows, columns), 1)
    gap = column - row - half
    slot = column + ((info[0] - 1) * half + part * rows)
    allowed = (gap <= 0) & (gap > -half) & (slot >= 0) & ((slot < info[1]) | (gap == 0))
    mask = jnp.where(allowed, 0.0, NEG)
    return jnp.concatenate([mask, mask], 0)


def two_heads(ref, at, block, dim):
    return jnp.concatenate(
        [ref[at, h * dim : (h + 1) * dim] for h in (2 * block, 2 * block + 1)], 0
    )


def key_columns(block, dim):
    key = slice(2 * block * dim, (2 * block + 1) * dim)
    value = slice((2 * block + 1) * dim, (2 * block + 2) * dim)
    return key, value


def seen_pair(before, own, part, block, dim):
    here, there = key_columns(block, dim), key_columns(1 - block, dim)
    rows = own.shape[0] // 2
    if part == 0:
        return [
            jnp.concatenate([before[:, t], own[:rows, h]], 0) for h, t in zip(here, there)
        ]
    return [jnp.concatenate([before[rows:, t], own[:, h]], 0) for h, t in zip(here, there)]


def attend_body(info, query, before, own, mixed, log_total):
    dim = own.shape[1] // 4
    rows = query.shape[0] // 2
    for part in range(2):
        at = slice(part * rows, (part + 1) * rows)
        mask = window_mask(info, part, rows, 3 * rows)
        for block in range(2):
            keys, values = seen_pair(before, own, part, block, dim)
            score = nt(two_heads(query, at, block, dim), keys) * dim**-0.5 + mask
            top = jnp.max(score, -1, keepdims=True)
            expo = jnp.exp(score - top)
            total = jnp.sum(expo, -1, keepdims=True)
            prob = (expo * (1.0 / total)).astype(jnp.bfloat16)
            out = jnp.dot(prob, values, preferred_element_type=jnp.float32).astype(jnp.bfloat16)
            log = jnp.broadcast_to(top + jnp.log(total), (2 * rows, dim))
            for i in range(2):
                on = slice((2 * block + i) * dim, (2 * block + i + 1) * dim)
                mixed[at, on] = out[i * rows : (i + 1) * rows]
                log_total[at, on] = log[i * rows : (i + 1) * rows]


def attend_back_body(
    info, query, before, own, log_total, grad_resid, weight0, weight1, raw, cosine, sine, gain,
    grad_query, grad_own, grad_before, gain_part, grad_keys, grad_values, grad_mixed,
):
    dim = own.shape[1] // 4
    rows = query.shape[0] // 2
    scale = dim**-0.5
    gain_total = jnp.zeros((1, dim), jnp.float32)
    masks = [window_mask(info, part, rows, 3 * rows) for part in range(2)]
    for block, weight in enumerate((weight0, weight1)):
        on = slice(2 * block * dim, 2 * (block + 1) * dim)
        grad_mixed[:, on] = jnp.dot(
            grad_resid[...], weight[...], preferred_element_type=jnp.float32
        ).astype(jnp.bfloat16)
        grad_keys[...] = jnp.zeros_like(grad_keys)
        grad_values[...] = jnp.zeros_like(grad_values)
        for part in range(2):
            keys, values = seen_pair(before, own, part, block, dim)
            at = slice(part * rows, (part + 1) * rows)
            seen = slice(part * rows, part * rows + 3 * rows)
            queries = two_heads(query, at, block, dim)
            grads = two_heads(grad_mixed, at, block, dim)
            log = two_heads(log_total, at, block, dim)[:, :1]
            prob = jnp.exp(nt(queries, keys) * scale + masks[part] - log)
            grad_prob = nt(grads, values)
            inner = jnp.sum(prob * grad_prob, -1, keepdims=True)
            grad_score = (prob * (grad_prob - inner)).astype(jnp.bfloat16)
            grad_values[seen, :] += tn(prob.astype(jnp.bfloat16), grads)
            grad_keys[seen, :] += tn(grad_score, queries) * scale
            both = jnp.dot(grad_score, keys, preferred_element_type=jnp.float32) * scale
            for i in range(2):
                head = 2 * block + i
                back = both[i * rows : (i + 1) * rows]
                back = back * cosine[at, :] - turned(back) * sine[at, :]
                there = (2 * head - head % 2) * dim
                unit, inverse = unit_of(raw[at, there : there + dim])
                gain_total += jnp.sum(unit * back, 0, keepdims=True)
                back = back * gain[...]
                back = inverse * (back - unit * jnp.mean(back * unit, -1, keepdims=True))
                grad_query[at, head * dim : (head + 1) * dim] = back.astype(jnp.bfloat16)
        for grad, here, there in zip(
            (grad_keys, grad_values), key_columns(block, dim), key_columns(1 - block, dim)
        ):
            grad_before[:, there] = grad[: 2 * rows, :].astype(jnp.bfloat16)
            grad_own[:, here] = grad[2 * rows :, :]
    gain_part[...] = gain_total


def finish_body(grad_query, grad_own, came, raw, cosine, sine, gain, even, odd, gain_part):
    dim = cosine.shape[1]
    total = jnp.zeros((1, dim), jnp.float32)
    for block, out in enumerate((even, odd)):
        key, value = key_columns(block, dim)
        back = grad_own[:, key] + came[:, key].astype(jnp.float32)
        back = back * cosine[...] - turned(back) * sine[...]
        unit, inverse = unit_of(raw[:, (4 * block + 2) * dim : (4 * block + 3) * dim])
        total += jnp.sum(unit * back, 0, keepdims=True)
        back = back * gain[...]
        back = inverse * (back - unit * jnp.mean(back * unit, -1, keepdims=True))
        out[:, : 2 * dim] = grad_query[:, 2 * block * dim : (2 * block + 2) * dim]
        out[:, 2 * dim : 3 * dim] = back.astype(jnp.bfloat16)
        grad_value = grad_own[:, value] + came[:, value].astype(jnp.float32)
        out[:, 3 * dim :] = grad_value.astype(jnp.bfloat16)
    gain_part[...] = total


def vmem_call(body, outs, scratch=(), scalars=0, name=None):
    def call(*args):
        in_specs = [
            pl.BlockSpec(memory_space=pltpu.SMEM if i < scalars else pltpu.VMEM)
            for i in range(len(args))
        ]
        return pl.pallas_call(
            body,
            grid=(1,),
            out_shape=outs,
            in_specs=in_specs,
            out_specs=jax.tree.map(lambda _: pl.BlockSpec(memory_space=pltpu.VMEM), outs),
            scratch_shapes=scratch,
            compiler_params=pltpu.CompilerParams(vmem_limit_bytes=VMEM_BYTES),
        cost_estimate=FREE,
            name=name,
        )(*args)

    return call


def hidden_units(mids, grads_y, weights):
    width, units = weights.shape[0], weights.shape[1] // 3
    count = len(mids)
    heights = [m.shape[0] for m in mids]
    rows, cut = sum(heights), units // 3

    def body(*refs):
        gate_w, up_w, w_down, act, grad_gate, grad_up = refs[2 * count :]
        start = 0
        for mid, grad_y in zip(refs[:count], refs[count : 2 * count]):
            at = slice(start, start + mid.shape[0])
            start += mid.shape[0]
            gate = jnp.dot(mid[...], gate_w[...], preferred_element_type=jnp.float32)
            up = jnp.dot(mid[...], up_w[...], preferred_element_type=jnp.float32)
            grad_act = jnp.dot(grad_y[...], w_down[...], preferred_element_type=jnp.float32)
            sigma = jax.nn.sigmoid(gate)
            swish = gate * sigma
            act[at, :] = (swish * up).astype(jnp.bfloat16)
            slope = grad_act * up * sigma * (1.0 + gate * (1.0 - sigma))
            grad_gate[at, :] = slope.astype(jnp.bfloat16)
            grad_up[at, :] = (grad_act * swish).astype(jnp.bfloat16)

    row_specs = [
        pl.BlockSpec((h, width), lambda j: (0, 0), pipeline_mode=pl.Buffered(1)) for h in heights
    ]
    return pl.pallas_call(
        body,
        grid=(3,),
        out_shape=[jax.ShapeDtypeStruct((rows, units), jnp.bfloat16)] * 3,
        in_specs=[
            *row_specs,
            *row_specs,
            pl.BlockSpec((width, cut), lambda j: (0, j)),
            pl.BlockSpec((width, cut), lambda j: (0, j + 3)),
            pl.BlockSpec((width, cut), lambda j: (0, j + 6)),
        ],
        out_specs=[pl.BlockSpec((rows, cut), lambda j: (0, j))] * 3,
        compiler_params=pltpu.CompilerParams(vmem_limit_bytes=VMEM_BYTES),
        cost_estimate=FREE,
        name="hidden_units",
    )(*mids, *grads_y, weights, weights, weights)


def from_hidden(pairs, eighths):
    count, parts = len(pairs), len(eighths)
    rows, units = pairs[0][0].shape[0] // 8, pairs[0][0].shape[1]
    width = pairs[0][1].shape[0]
    cut = width // 4

    def body(*refs):
        ins, outs = refs[: -(parts // 2)], refs[-(parts // 2) :]
        total = 0.0
        for i in range(count):
            part = ins[i * (parts + 1) : (i + 1) * (parts + 1)]
            left = jnp.concatenate([p[...] for p in part[:-1]], 0)
            total = total + nt(left, part[-1][...])
        for i, out in enumerate(outs):
            out[...] = total[2 * i * rows : 2 * (i + 1) * rows].astype(jnp.bfloat16)

    specs, args = [], []
    for left, right, at in pairs:
        specs += [pl.BlockSpec((rows, units), lambda j, e=e: (e, 0)) for e in eighths]
        specs.append(pl.BlockSpec((cut, units), lambda j, at=at: (j, at)))
        args += [left] * parts + [right]
    return pl.pallas_call(
        body,
        grid=(4,),
        out_shape=[jax.ShapeDtypeStruct((2 * rows, width), jnp.bfloat16)] * (parts // 2),
        in_specs=specs,
        out_specs=[pl.BlockSpec((2 * rows, cut), lambda j: (0, j))] * (parts // 2),
        compiler_params=pltpu.CompilerParams(vmem_limit_bytes=VMEM_BYTES),
        cost_estimate=FREE,
        name="from_hidden",
    )(*args)


def row_outer(lefts, groups, first, tiles, added=None, places=None, part=None):
    rights = [right for group in groups for right in group]
    places = range(len(rights)) if places is None else places
    added = [] if added is None else [added] * len(rights)
    width = lefts[0].shape[1]
    tile = width // 8
    count = len(lefts)
    rows = sum(left.shape[0] for left in lefts)
    wide = rights[0].shape[1] // (1 if part is None else 2)
    columns = [wide * len(group) for group in groups]

    def body(*refs):
        left_refs = refs[:count]
        right_refs = refs[count : count + len(rights)]
        add_refs = refs[count + len(rights) : count + len(rights) + len(added)]
        outs = refs[count + len(rights) + len(added) :]
        place = 0
        for i, group in enumerate(groups):
            column = 0
            for _ in group:
                on = slice(column, column + wide)
                total, start = 0.0, 0
                for left in left_refs:
                    stop = start + left.shape[0]
                    total = total + tn(left[...], right_refs[place][start:stop, :])
                    start = stop
                if added:
                    total = total + add_refs[place][...].astype(jnp.float32)
                outs[i][:, on] = total.astype(jnp.bfloat16)
                place += 1
                column += wide

    return pl.pallas_call(
        body,
        grid=(tiles,),
        out_shape=[jax.ShapeDtypeStruct((tiles * tile, c), jnp.bfloat16) for c in columns],
        in_specs=[
            *(pl.BlockSpec((left.shape[0], tile), lambda j: (0, j + first)) for left in lefts),
            *(
                pl.BlockSpec(
                    (right.shape[0], wide), lambda j: (0, part or 0), pipeline_mode=pl.Buffered(1)
                )
                for right in rights
            ),
            *(
                pl.BlockSpec((tile, wide), lambda j, at=at: (j + first, at))
                for at in places[: len(added)]
            ),
        ],
        out_specs=[pl.BlockSpec((tile, c), lambda j: (j, 0)) for c in columns],
        compiler_params=pltpu.CompilerParams(vmem_limit_bytes=VMEM_BYTES),
        cost_estimate=pl.CostEstimate(
            flops=2 * rows * tiles * tile * sum(columns),
            bytes_accessed=2 * rows * (width + sum(columns)),
            transcendentals=0,
        ),
        name="row_outer",
    )(*lefts, *rights, *added)


def close_body(x, *refs):
    mixed, weights = refs[:4], refs[4:12]
    gains, resid, mid = refs[12:]
    at = pl.program_id(0)
    step = x.shape[1]
    columns = weights[0].shape[1]
    total = x[...].astype(jnp.float32)
    for i in range(8):
        part = mixed[i // 2][:, (i % 2) * columns : (i % 2 + 1) * columns]
        total = total + nt(part, weights[i][...])
    resid[:, pl.ds(pl.multiple_of(at * step, step), step)] = total

    @pl.when(at == 3)
    def _():
        unit, _ = unit_of(resid[...])
        mid[...] = (unit * gains[...]).astype(jnp.bfloat16)


def close_attention(x, mixed, weights, gains):
    rows, width = x.shape
    step = width // 4
    whole = lambda a: pl.BlockSpec(a.shape, lambda j: (0, 0))
    return pl.pallas_call(
        close_body,
        grid=(4,),
        out_shape=[
            jax.ShapeDtypeStruct((rows, width), jnp.float32),
            jax.ShapeDtypeStruct((rows, width), jnp.bfloat16),
        ],
        in_specs=[
            pl.BlockSpec((rows, step), lambda j: (0, j)),
            *(whole(m) for m in mixed),
            *(pl.BlockSpec((step, w.shape[1]), lambda j: (j, 0)) for w in weights),
            whole(gains),
        ],
        out_specs=[pl.BlockSpec((rows, width), lambda j: (0, 0))] * 2,
        compiler_params=pltpu.CompilerParams(vmem_limit_bytes=VMEM_BYTES),
        cost_estimate=FREE,
        name="close_attention",
    )(x, *mixed, *weights, gains)


def back_to_rows(blocks, weights):
    rows = blocks[0].shape[0]
    step, columns = weights[0][0].shape
    count = len(blocks)

    def body(*refs):
        lefts = refs[:count]
        hbm = refs[count : 3 * count]
        out = refs[3 * count]
        held, sems = refs[3 * count + 1 :]
        copies = []
        for i in range(count):
            own, came = hbm[2 * i : 2 * i + 2]
            copies.append(
                [
                    pltpu.make_async_copy(own, held.at[i, :step], sems.at[i, 0]),
                    pltpu.make_async_copy(came, held.at[i, step:], sems.at[i, 1]),
                ]
            )
        for some in copies:
            for copy in some:
                copy.start()
        for i in range(count):
            for copy in copies[i]:
                copy.wait()
            for k in range(4):
                on = slice(k * step, (k + 1) * step)
                part = nt(lefts[i][...], held[i, on])
                if i == 0:
                    out[:, on] = part
                else:
                    out[:, on] += part

    return pl.pallas_call(
        body,
        grid=(1,),
        out_shape=jax.ShapeDtypeStruct((rows, 4 * step), jnp.float32),
        in_specs=[pl.BlockSpec(memory_space=pltpu.VMEM)] * count
        + [pl.BlockSpec(memory_space=pl.ANY)] * (2 * count),
        out_specs=pl.BlockSpec(memory_space=pltpu.VMEM),
        scratch_shapes=[
            pltpu.VMEM((count, 4 * step, columns), jnp.bfloat16),
            pltpu.SemaphoreType.DMA((count, 2)),
        ],
        compiler_params=pltpu.CompilerParams(vmem_limit_bytes=VMEM_BYTES),
        cost_estimate=FREE,
        name="back_to_rows",
    )(*blocks, *(part for w in weights for part in w))


def on_device_block(
    tokens,
    lengths,
    attn_gain,
    w_query,
    key_matrix,
    value_matrix,
    query_gain,
    key_gain,
    w_out,
    mlp_gain,
    w_gate,
    w_up,
    w_down,
    cotangent,
):
    low, full = jnp.bfloat16, jnp.float32
    width = tokens.shape[2]
    head_dim = query_gain.shape[0]
    shards = lax.axis_size("shard")
    shard_at = lax.axis_index("shard")
    me = lax.axis_index("rep")
    core = me & 1
    count = lax.axis_size("rep")

    s = Stage()
    s.cotangent = cotangent
    piece = width // shards

    s.own_blocks = [
        column_block((w_query, key_matrix, value_matrix), me ^ i) for i in range(8)
    ]
    gain_rows = jnp.concatenate(
        [jnp.stack([attn_gain, mlp_gain]), jnp.zeros((14, piece), low)], 0
    )
    travelling = jnp.concatenate([s.own_blocks[0], gain_rows], 0)
    s.tokens = tokens
    s.out_block = column_block((w_out,), me)
    s.ffn_block = column_block((w_gate, w_up, w_down), me)
    s.before, s.behind = around(travelling, 1), around(travelling, -1)
    s.other_lengths = across(lengths, CORE)
    s.end()

    s.ahead = around(s.before, 1)
    tokens_sent = to_sequences_send(s.tokens)
    out_own = lax.all_gather(s.out_block, "shard", axis=0, tiled=True)
    del s.out_block, s.tokens
    s.end()

    parts = (s.before, s.ahead, s.behind)
    s.came = jnp.concatenate([part[:piece] for part in parts], 0)
    s.gains = jnp.concatenate([gain_rows[:2], *(part[piece : piece + 2] for part in parts)], 1)
    s.came_near = near(s.came)
    s.came_own = across(s.came, CORE)
    s.x_came = tokens_sent
    del s.before, s.behind, s.ahead
    s.end()

    grad_y_sent = to_sequences_send(s.cotangent)
    s.came_far = far(*s.came_near)
    s.came_other = [s.came_own, *(across(block, CORE) for block in s.came_near)]
    s.grad_y_came = grad_y_sent
    gains = rolled(s.gains.astype(full))
    s.mlp_gains = gains[1:]
    s.attn_gains = gains[:1]
    s.x_low = jnp.concatenate(in_turn(s.x_came), 0)
    rows = s.x_low.shape[0]
    x_rows = s.x_low.astype(full)
    s.inverse_in = lax.rsqrt(jnp.mean(x_rows * x_rows, -1, keepdims=True) + EPS)
    s.normed = rolled((x_rows * s.inverse_in * s.attn_gains).astype(low))
    query_gains = query_gain.astype(full)[None]
    key_gains = key_gain.astype(full)[None]
    s.head_gains = jnp.concatenate([query_gains, key_gains], 0)
    both = jnp.where(
        core == 0,
        jnp.concatenate([lengths, s.other_lengths]),
        jnp.concatenate([s.other_lengths, lengths]),
    )
    length = lax.dynamic_index_in_dim(both, shard_at, 0, keepdims=False)
    s.info = jnp.stack([core, length]).astype(jnp.int32)
    query_pos = core * rows + jnp.arange(rows, dtype=jnp.int32)
    s.valid = (query_pos < length)[:, None].astype(full)
    cosine, sine = tables(query_pos, head_dim)
    s.cosine, sine = cosine[0, :, 0], sine[0, :, 0]
    s.sine = jnp.concatenate([-sine[:, : head_dim // 2], sine[:, head_dim // 2 :]], 1)
    s.out_own = out_own
    del s.gains, s.x_came, s.other_lengths, s.cotangent, s.came_own
    s.end()

    head_columns = 2 * head_dim
    block_columns = 4 * head_dim
    quad_rows = jax.ShapeDtypeStruct((rows, block_columns), low)
    quad_sums = jax.ShapeDtypeStruct((rows, block_columns), full)
    gain_sum = jax.ShapeDtypeStruct((1, head_dim), full)
    project = vmem_call(
        project_body,
        [jax.ShapeDtypeStruct((rows, 2 * block_columns), full), quad_rows, quad_rows],
        name="project",
    )
    attend = vmem_call(attend_body, [quad_rows, quad_sums], scalars=1, name="attend")
    attend_back = vmem_call(
        attend_back_body,
        [quad_rows, quad_sums, quad_rows, gain_sum],
        scratch=[pltpu.VMEM((2 * rows, head_dim), full)] * 2
        + [pltpu.VMEM((rows, block_columns), low)],
        scalars=1,
        name="attend_back",
    )
    finish = vmem_call(finish_body, [quad_rows, quad_rows, gain_sum], name="finish")
    upward = [(i, i + 1) for i in range(0, count, 2)]
    downward = [(i + 1, i) for i in range(0, count, 2)]

    def project_call(i, came, other):
        return (
            project, s.normed, s.own_blocks[2 * i], came, s.own_blocks[2 * i + 1], other,
            s.cosine, s.sine, s.head_gains,
        )

    def attend_call(projected, earlier):
        return (
            lambda query, own, before: attend(s.info, query, before, own),
            *projected[1:], earlier,
        )

    ffn_own = lax.all_gather(s.ffn_block, "shard", axis=0, tiled=True)
    came_last = jnp.concatenate(s.came_far, 0)
    s.came_last = (came_last, across(came_last, CORE))
    s.out_near = near(s.out_own)
    s.out_own_other = across(s.out_own, CORE)
    s.projected = in_order(
        [
            project_call(i, block, other)
            for i, (block, other) in enumerate(zip((s.came, *s.came_near), s.came_other))
        ]
    )
    del s.came_far, s.ffn_block
    s.end()

    s.out_far = far(*s.out_near)
    s.out_near_other = [across(block, CORE) for block in s.out_near]
    s.earlier = [lax.ppermute(p[2], "rep", upward) for p in s.projected]
    (s.projected_last,) = in_order([project_call(3, *s.came_last)])
    s.end()

    grad_y = jnp.concatenate(in_turn(s.grad_y_came), 0)
    s.grad_y = jnp.where(s.valid > 0, grad_y, jnp.zeros_like(grad_y))
    grad_y_near = near(s.grad_y)
    out_last = jnp.concatenate(s.out_far, 0)
    s.out_last = (out_last, across(out_last, CORE))
    s.earlier_last = lax.ppermute(s.projected_last[2], "rep", upward)
    s.attended = in_order([attend_call(*pair) for pair in zip(s.projected, s.earlier)])
    del s.out_far, s.grad_y_came
    s.end()

    s.projected = [*s.projected, s.projected_last]
    s.earlier = [*s.earlier, s.earlier_last]
    s.out_blocks = [
        s.out_own, s.out_own_other, s.out_near[0], s.out_near_other[0], s.out_near[1],
        s.out_near_other[1], *s.out_last,
    ]
    (last,) = in_order([attend_call(s.projected_last, s.earlier_last)])
    s.attended = [*s.attended, last]
    s.mixed = [a[0] for a in s.attended]
    s.resid, s.mid = close_attention(s.x_low, s.mixed, s.out_blocks, s.mlp_gains)
    s.grad_y_near = grad_y_near
    del s.out_own, s.out_own_other, s.out_near, s.out_near_other, s.out_last
    del s.projected_last, s.earlier_last
    s.end()

    s.mid_near = near(s.mid)
    s.grad_y_far = far(*s.grad_y_near)
    s.end()

    s.mid_far = far(*s.mid_near)
    s.ffn_own = ffn_own
    s.end()

    s.mids = [s.mid, *s.mid_near, *s.mid_far]
    s.grads_y = [s.grad_y, *s.grad_y_near, *s.grad_y_far]
    s.ffn_other = across(s.ffn_own, CORE)
    units = s.ffn_own.shape[1] // 3
    s.hidden_own = hidden_units(s.mids, s.grads_y, s.ffn_own)
    del s.mid, s.mid_near, s.mid_far, s.grad_y_near, s.grad_y_far
    s.end()

    def gate_up_pairs():
        return [
            (hidden[i], weights, i - 1)
            for hidden, weights in ((s.hidden_own, s.ffn_own), (s.hidden_other, s.ffn_other))
            for i in (1, 2)
        ]

    def down_pairs():
        return [(s.hidden_own[0], s.ffn_own, 2), (s.hidden_other[0], s.ffn_other, 2)]

    def from_hidden_call(pairs, eighths):
        return (
            lambda first: from_hidden([(first, *pairs[0][1:]), *pairs[1:]], eighths),
            pairs[0][0],
        )

    def outer_call(lefts, rights, *added):
        return lambda first: row_outer(lefts, [[first, *rights[1:]]], 0, 8, *added)[0], rights[0]

    def send_near(sent):
        return across(sent[0], ACROSS_X), across(sent[1], ACROSS_Y)

    def send_far(came, rest, split):
        one_tail, two_head = rest
        return (
            across(rounded_sum(one_tail, split(came[1])[1]), ACROSS_X),
            across(rounded_sum(two_head, split(came[0])[1]), ACROSS_Y),
        )

    def total(came, came_far, own, split):
        head, tail = own
        full_sum = lambda *parts: sum(part.astype(full) for part in parts)
        return jnp.concatenate(
            [
                full_sum(head, split(came[0])[0], came_far[1]),
                full_sum(tail, split(came[1])[0], came_far[0]),
            ],
            0,
        )

    by_rows = lambda a: jnp.split(a, 2, 0)
    by_columns = lambda a: jnp.split(a, 2, 1)
    to_plane, rest_of_plane = (2, 6, 5, 7), (3, 4, 0, 1)

    s.hidden_other = hidden_units(s.mids, s.grads_y, s.ffn_other)
    (s.down_outer,) = in_order([outer_call(s.grads_y, s.hidden_other[:1])])
    s.end()

    s.down_came = across(s.down_outer, CORE)
    s.mid_sent = from_hidden(gate_up_pairs(), to_plane)
    del s.down_outer
    s.end()

    s.mid_came = send_near(s.mid_sent)
    s.down_mine, s.mid_rest, s.gate_up_outer = in_order(
        [
            outer_call(s.grads_y, s.hidden_own[:1], s.down_came),
            from_hidden_call(gate_up_pairs(), rest_of_plane),
            outer_call(s.mids, s.hidden_other[1:]),
        ]
    )
    del s.mid_sent, s.down_came
    s.end()

    down_total = lax.psum_scatter(s.down_mine, "shard", scatter_dimension=0, tiled=True)
    s.mid_came_far = send_far(s.mid_came, by_rows(s.mid_rest[0]), by_rows)
    s.gate_up_came = across(s.gate_up_outer, CORE)
    s.mlp_sent, s.mlp_rest = in_order(
        [
            from_hidden_call(down_pairs(), to_plane),
            from_hidden_call(down_pairs(), rest_of_plane),
        ]
    )
    del s.gate_up_outer, s.down_mine
    s.end()

    mlp_came = send_near(s.mlp_sent)
    grad_mid = total(s.mid_came, s.mid_came_far, by_rows(s.mid_rest[1]), by_rows)
    inverse_mid = lax.rsqrt(jnp.mean(s.resid * s.resid, -1, keepdims=True) + EPS)
    mid_unit = s.resid * inverse_mid
    s.mlp_gain_part = jnp.sum(mid_unit * grad_mid, 0)
    s.grad_resid = s.grad_y.astype(full) + norm_back(
        mid_unit, inverse_mid, grad_mid * s.mlp_gains
    )
    s.resid_low = s.grad_resid.astype(low)
    s.resid_rolled = rolled(s.resid_low)
    (s.gate_up_mine,) = in_order([outer_call(s.mids, s.hidden_own[1:], s.gate_up_came)])
    del s.mid_came, s.mid_came_far, s.mid_rest, s.gate_up_came, s.hidden_own, s.hidden_other
    del s.mids, s.grads_y, s.ffn_own, s.ffn_other
    s.end()

    def back_call(i):
        raw, query, own_pair = s.projected[i]
        return (
            lambda query, *rest: attend_back(s.info, query, *rest),
            query, s.earlier[i], own_pair, s.attended[i][1], s.resid_low,
            *s.out_blocks[2 * i : 2 * i + 2], raw, s.cosine, s.sine, s.head_gains[:1],
        )

    def finish_call(i):
        return (
            finish, s.backs[i][0], s.backs[i][1], s.returned[i], s.projected[i][0],
            s.cosine, s.sine, s.head_gains[1:],
        )

    def give_back(*chips):
        s.returned = s.returned | {
            i: lax.ppermute(s.backs[i][2], "rep", downward) for i in chips
        }

    def odd_call(left, blocks, part=None):
        return lambda first: row_outer([first], [blocks], 0, 8, part=part)[0], left

    def head_call(left, blocks, came, part=None, places=(0, 1, 2, 3)):
        groups = [[blocks[1], blocks[3]], [blocks[2]], [blocks[0]]]
        at = [places[i] for i in (1, 3, 2, 0)]
        return lambda first: row_outer([first], groups, 0, 4, came, at, part), left

    def tail_call(left, blocks, came, part=None, places=(0, 1, 2, 3)):
        groups = [[blocks[2], blocks[3]], [blocks[1]], [blocks[0]]]
        at = [places[i] for i in (2, 3, 1, 0)]
        return lambda first: row_outer([first], groups, 4, 4, came, at, part), left

    gate_up_total = lax.psum_scatter(s.gate_up_mine, "shard", scatter_dimension=0, tiled=True)
    s.returned = {}
    s.out_odd, back = in_order([odd_call(s.resid_rolled, s.mixed, 1), back_call(3)])
    s.backs = {3: back}
    s.mlp_came = mlp_came
    s.down_total = down_total
    del s.gate_up_mine, s.mlp_sent
    s.end()

    s.mlp_came_far = send_far(s.mlp_came, by_rows(s.mlp_rest[0]), by_rows)
    s.out_came = across(s.out_odd, CORE)
    give_back(3)
    back1, back2 = in_order([back_call(1), back_call(2)])
    s.backs = s.backs | {1: back1, 2: back2}
    del s.out_odd
    s.end()

    s.down_near = near(s.down_total)
    give_back(1, 2)
    mlp_out = total(s.mlp_came, s.mlp_came_far, by_rows(s.mlp_rest[1]), by_rows)
    s.output = (s.valid * (s.resid + mlp_out)).astype(low)
    s.out_head, s.out_tail, back, finished = in_order(
        [
            head_call(s.resid_rolled, s.mixed, s.out_came, 0),
            tail_call(s.resid_rolled, s.mixed, s.out_came, 0),
            back_call(0),
            finish_call(3),
        ]
    )
    s.backs = s.backs | {0: back}
    s.finished = {3: finished}
    del s.mlp_came, s.mlp_came_far, s.mlp_rest, s.out_came, s.resid
    s.end()

    output_sent = from_sequences_send(s.output)
    s.output_first = output_sent[0]
    s.out_near = send_near((s.out_head[0], s.out_tail[0]))
    s.down_far = far(*s.down_near)
    give_back(0)
    finished1, finished2 = in_order([finish_call(1), finish_call(2)])
    s.finished = s.finished | {1: finished1, 2: finished2}
    del s.output
    s.gate_up_total = gate_up_total
    s.end()

    s.out_far = send_far(s.out_near, (s.out_tail[1], s.out_head[1]), by_columns)
    s.down_own = jnp.concatenate([s.down_total, *s.down_near, *s.down_far], 0)
    s.down_other = across(s.down_own, CORE)
    (finished,) = in_order([finish_call(0)])
    s.finished = s.finished | {0: finished}
    (s.qkv_odd,) = in_order([odd_call(s.normed, [s.finished[i][1] for i in range(4)])])
    s.output_second = output_sent[1]
    del s.down_total, s.down_near, s.down_far
    s.end()

    my_group = me.astype(jnp.int32)[None]

    def whole_call(widths, own, other):
        return lambda first: whole_columns(my_group, first, other, widths), own

    s.qkv_came = across(s.qkv_odd, CORE)
    s.gate_up_near = near(s.gate_up_total)
    out_sum = total(s.out_near, s.out_far, (s.out_head[2], s.out_tail[2]), by_columns)
    s.out_chunks = jnp.split(out_sum.astype(low), shards, 0)
    s.out_ring = ring_sum_first(s.out_chunks)
    weights = [
        pair
        for i, block in enumerate(zip((s.came, *s.came_near), s.came_other))
        for pair in ((s.own_blocks[2 * i], block[0]), (s.own_blocks[2 * i + 1], block[1]))
    ] + [(s.own_blocks[6 + i], s.came_last[i]) for i in range(2)]
    blocks = [part for i in range(4) for part in s.finished[i][:2]]
    grad_in, s.whole_down = in_order(
        [
            (lambda first: back_to_rows([first, *blocks[1:]], weights), blocks[0]),
            whole_call((units,), s.down_own, s.down_other),
        ]
    )
    grad_in = rolled(grad_in)
    x_unit = s.x_low.astype(full) * s.inverse_in
    s.attn_gain_part = jnp.sum(x_unit * grad_in, 0)
    s.grad_tokens = (
        s.grad_resid + norm_back(x_unit, s.inverse_in, grad_in * s.attn_gains)
    ).astype(low)
    del s.qkv_odd, s.out_near, s.out_far, s.out_head, s.out_tail, s.down_own, s.down_other
    del s.own_blocks, s.came, s.came_near, s.came_other, s.came_last, s.grad_resid, s.x_low
    s.end()

    s.gate_up_far = far(*s.gate_up_near)
    s.out_ring_last = around(rounded_sum(s.out_chunks[3], s.out_ring[0]), 1)
    even = [s.finished[i][0] for i in range(4)]
    first_head, first_tail, second_head, second_tail = in_order(
        [
            call(s.normed, even, s.qkv_came, half, range(half, 8, 2))
            for half in range(2)
            for call in (head_call, tail_call)
        ]
    )
    s.heads = [first_head, second_head]
    s.tails = [first_tail, second_tail]
    s.gain_parts = jnp.concatenate(
        [
            s.attn_gain_part,
            s.mlp_gain_part,
            sum(s.backs[i][3] for i in range(4))[0],
            sum(s.finished[i][2] for i in range(4))[0],
        ]
    )
    s.gain_came = across(s.gain_parts, CORE)
    del s.qkv_came, s.finished, s.backs
    s.end()

    grad_tokens_sent = from_sequences_send(s.grad_tokens)

    def qkv_near(half):
        return send_near((s.heads[half][0], s.tails[half][0]))

    def qkv_far(came, half):
        return send_far(came, (s.tails[half][1], s.heads[half][1]), by_columns)

    def qkv_chunks(came, came_far, half):
        own = total(came, came_far, (s.heads[half][2], s.tails[half][2]), by_columns)
        return jnp.split(own.astype(low), shards, 0)

    s.near0 = qkv_near(0)
    s.gate_up_own = jnp.concatenate([s.gate_up_total, *s.gate_up_near, *s.gate_up_far], 0)
    s.gate_up_other = across(s.gate_up_own, CORE)
    s.out_total = rounded_sum(s.out_chunks[0], s.out_ring[1], s.out_ring_last)
    s.gain_parts = s.gain_parts + s.gain_came
    s.gain_came = across(s.gain_parts, ACROSS_X)
    s.tokens_first = grad_tokens_sent[0]
    del s.out_chunks, s.out_ring, s.out_ring_last, s.gate_up_near, s.gate_up_far
    del s.gate_up_total, s.grad_tokens
    s.end()

    s.far0 = qkv_far(s.near0, 0)
    s.near1 = qkv_near(1)
    s.gain_parts = s.gain_parts + s.gain_came
    s.gain_came = across(s.gain_parts, ACROSS_Y)
    s.tokens_second = grad_tokens_sent[1]
    (s.whole_gate_up,) = in_order([whole_call((units, units), s.gate_up_own, s.gate_up_other)])
    del s.gate_up_own, s.gate_up_other
    s.end()

    s.chunks0 = qkv_chunks(s.near0, s.far0, 0)
    s.ring0 = ring_sum_first(s.chunks0)
    s.far1 = qkv_far(s.near1, 1)
    s.gain_parts = s.gain_parts + s.gain_came
    s.gain_came = lax.ppermute(s.gain_parts, "shard", [(i, i ^ 1) for i in range(shards)])
    del s.near0, s.far0
    s.end()

    s.last0 = around(rounded_sum(s.chunks0[3], s.ring0[0]), 1)
    s.chunks1 = qkv_chunks(s.near1, s.far1, 1)
    s.ring1 = ring_sum_first(s.chunks1)
    s.gain_parts = s.gain_parts + s.gain_came
    s.gain_came = lax.ppermute(s.gain_parts, "shard", [(i, i ^ 2) for i in range(shards)])
    del s.near1, s.far1, s.heads, s.tails
    s.end()

    query_total = rounded_sum(s.chunks0[0], s.ring0[1], s.last0)
    s.total0 = jnp.concatenate([query_total, s.out_total], 1)
    s.spread0 = near(s.total0)
    s.last1 = around(rounded_sum(s.chunks1[3], s.ring1[0]), 1)
    s.gain_sums = s.gain_parts + s.gain_came
    del s.chunks0, s.ring0, s.last0, s.out_total
    s.end()

    s.spread_far0 = far(*s.spread0)
    s.total1 = rounded_sum(s.chunks1[0], s.ring1[1], s.last1)
    s.spread1 = near(s.total1)
    del s.chunks1, s.ring1, s.last1
    s.end()

    s.own0 = jnp.concatenate([s.total0, *s.spread0, *s.spread_far0], 0)
    s.other0 = across(s.own0, CORE)
    s.spread_far1 = far(*s.spread1)
    del s.total0, s.spread0, s.spread_far0
    s.end()

    s.own1 = jnp.concatenate([s.total1, *s.spread1, *s.spread_far1], 0)
    s.other1 = across(s.own1, CORE)
    (s.whole0,) = in_order([whole_call((head_columns, head_columns), s.own0, s.other0)])
    del s.own0, s.other0, s.total1, s.spread1, s.spread_far1
    s.end()

    ((whole_key, whole_value),) = in_order(
        [whole_call((head_dim, head_dim), s.own1, s.other1)]
    )
    gain_sums = s.gain_sums
    wide = lax.dynamic_slice_in_dim(
        gain_sums[: 2 * width].reshape(2, width), shard_at * piece, piece, 1
    )
    narrow = gain_sums[2 * width :]
    return (
        jnp.stack(in_turn([s.output_first, s.output_second])),
        jnp.stack(in_turn([s.tokens_first, s.tokens_second])),
        wide[0],
        s.whole0[0],
        whole_key,
        whole_value,
        narrow[:head_dim],
        narrow[head_dim:],
        s.whole0[1],
        wide[1],
        *s.whole_gate_up,
        *s.whole_down,
    )


def solution(mesh):
    sizes = (mesh.shape["rep"], mesh.shape["shard"])
    return jax.shard_map(
        on_device_block if sizes == (8, 4) else on_device,
        mesh=mesh,
        in_specs=(
            P("rep", "shard", None),
            P("rep"),
            P("shard"),
            P("shard", None),
            P("shard", None),
            P("shard", None),
            P(),
            P(),
            P("shard", None),
            P("shard"),
            P("shard", None),
            P("shard", None),
            P("shard", None),
            P("rep", "shard", None),
        ),
        out_specs=(
            P("rep", "shard", None),
            P("rep", "shard", None),
            P("shard"),
            P("shard", None),
            P("shard", None),
            P("shard", None),
            P(),
            P(),
            P("shard", None),
            P("shard"),
            P("shard", None),
            P("shard", None),
            P("shard", None),
        ),
        check_vma=False,
    )
```

```python
import jax
import jax.numpy as jnp
from jax import lax
from jax.experimental import pallas as pl
from jax.experimental.pallas import tpu as pltpu
from jax.sharding import PartitionSpec as P

WINDOW = 512


EPS = 1e-06
ROPE_BASE = 1000000.0
NEG = -1e30


def passed_along(x, axis, by):
    devices = lax.axis_size(axis)
    pairs = [(i, i + by) for i in range(devices) if 0 <= i + by < devices]
    return lax.ppermute(x, axis, pairs)


def tables(positions, head_dim):
    half = head_dim // 2
    freq = ROPE_BASE ** (-jnp.arange(half, dtype=jnp.float32) * 2.0 / head_dim)
    angle = positions.astype(jnp.float32)[:, None] * freq[None, :]
    angle = jnp.concatenate([angle, angle], -1)
    return (jnp.cos(angle)[None, :, None, :], jnp.sin(angle)[None, :, None, :])


def rotated_rows(value_rows):
    half = value_rows.shape[-1] // 2
    return jnp.concatenate([-value_rows[..., half:], value_rows[..., :half]], -1)


def head_norm(raw, gain):
    inverse = lax.rsqrt(jnp.mean(raw * raw, -1, keepdims=True) + EPS)
    unit = raw * inverse
    return (unit, inverse, unit * gain)


def norm_back(unit, inverse, grad_unit):
    return inverse * (grad_unit - unit * jnp.mean(grad_unit * unit, -1, keepdims=True))


def head_norm_back(unit, inverse, grad_normed, gain):
    grad_raw = norm_back(unit, inverse, grad_normed * gain)
    return (grad_raw, jnp.sum(unit * grad_normed, axis=(0, 1, 2)))


def scores(query_rows, keys, allowed, scale):
    raw = (
        jnp.einsum("sqhgd,skhd->shgqk", query_rows, keys, preferred_element_type=jnp.float32)
        * scale
    )
    return jnp.where(allowed[:, None, None], raw, NEG)


def outer(left, right):
    return jnp.einsum("rc,rf->cf", left, right, preferred_element_type=jnp.float32)


def on_device(
    tokens,
    lengths,
    attn_gain,
    w_query,
    key_matrix,
    value_matrix,
    query_gain,
    key_gain,
    w_out,
    mlp_gain,
    w_gate,
    w_up,
    w_down,
    cotangent,
):
    seq_count, piece, width = tokens.shape
    head_dim = query_gain.shape[0]
    heads_q = w_query.shape[1] // head_dim
    heads_kv = key_matrix.shape[1] // head_dim
    groups = heads_q // heads_kv
    rows = seq_count * piece
    scale = head_dim ** (-0.5)
    reach = (WINDOW + piece - 2) // piece
    owned = width // lax.axis_size("shard")
    shard_at = lax.axis_index("shard")
    query_pos = shard_at * piece + jnp.arange(piece, dtype=jnp.int32)
    key_pos = (shard_at - reach) * piece + jnp.arange((reach + 1) * piece, dtype=jnp.int32)
    near = (
        (key_pos[None, :] <= query_pos[:, None])
        & (query_pos[:, None] - key_pos[None, :] < WINDOW)
        & (key_pos[None, :] >= 0)
    )
    live = (key_pos[None, None, :] < lengths[:, None, None]) | (
        key_pos[None, :] == query_pos[:, None]
    )[None]
    allowed = near[None] & live
    valid = (query_pos[None, :] < lengths[:, None]).astype(jnp.float32).reshape(rows, 1)
    cosine_table, sine_table = tables(query_pos, head_dim)
    x_rows = tokens.astype(jnp.float32).reshape(rows, width)
    inverse_in = lax.rsqrt(jnp.mean(x_rows * x_rows, -1, keepdims=True) + EPS)
    x_unit = x_rows * inverse_in
    gain_piece = lax.all_gather(attn_gain, "shard", axis=0, tiled=True)
    query_piece = lax.all_gather(w_query, "shard", axis=0, tiled=True)
    key_piece = lax.all_gather(key_matrix, "shard", axis=0, tiled=True)
    value_piece = lax.all_gather(value_matrix, "shard", axis=0, tiled=True)
    normed_piece = (x_unit * gain_piece.astype(jnp.float32)).astype(jnp.bfloat16)
    acc_q = jnp.dot(normed_piece, query_piece, preferred_element_type=jnp.float32)
    acc_k = jnp.dot(normed_piece, key_piece, preferred_element_type=jnp.float32)
    acc_v = jnp.dot(normed_piece, value_piece, preferred_element_type=jnp.float32)
    normalized_rows = normed_piece
    gains = gain_piece.astype(jnp.float32)
    attn_in = normalized_rows
    attn_gains = gains
    query_unit, query_inverse, query_rows_normalized = head_norm(
        acc_q.reshape(seq_count, piece, heads_q, head_dim), query_gain.astype(jnp.float32)
    )
    key_unit, key_inverse, key_normed = head_norm(
        acc_k.reshape(seq_count, piece, heads_kv, head_dim), key_gain.astype(jnp.float32)
    )
    query_rows = (
        (query_rows_normalized * cosine_table + rotated_rows(query_rows_normalized) * sine_table)
        .astype(jnp.bfloat16)
        .reshape(seq_count, piece, heads_kv, groups, head_dim)
    )
    keys_own = (key_normed * cosine_table + rotated_rows(key_normed) * sine_table).astype(
        jnp.bfloat16
    )
    values_own = acc_v.reshape(seq_count, piece, heads_kv, head_dim).astype(jnp.bfloat16)
    own_pair = jnp.stack([keys_own, values_own])
    parts = []
    for fetch_back in range(reach, 0, -1):
        parts.append(passed_along(own_pair, "shard", fetch_back))
    parts.append(own_pair)
    near_pair = jnp.concatenate(parts, 2)
    score = scores(query_rows, near_pair[0], allowed, scale)
    top = jnp.max(score, -1, keepdims=True)
    expo = jnp.exp(score - top)
    total = jnp.sum(expo, -1, keepdims=True)
    prob = expo / total
    log_total = top + jnp.log(total)
    mixed = jnp.einsum(
        "shgqk,skhd->sqhgd",
        prob.astype(jnp.bfloat16),
        near_pair[1],
        preferred_element_type=jnp.float32,
    )
    mixed_rows = mixed.reshape(rows, heads_q * head_dim).astype(jnp.bfloat16)
    resid = x_rows + jnp.einsum(
        "rf,nf->rn",
        mixed_rows,
        lax.all_gather(w_out, "shard", axis=0, tiled=True),
        preferred_element_type=jnp.float32,
    )
    inverse_mid = lax.rsqrt(jnp.mean(resid * resid, -1, keepdims=True) + EPS)
    mid_unit = resid * inverse_mid
    gain_piece = lax.all_gather(mlp_gain, "shard", axis=0, tiled=True)
    gate_piece = lax.all_gather(w_gate, "shard", axis=0, tiled=True)
    up_piece = lax.all_gather(w_up, "shard", axis=0, tiled=True)
    normed_piece = (mid_unit * gain_piece.astype(jnp.float32)).astype(jnp.bfloat16)
    acc_gate = jnp.dot(normed_piece, gate_piece, preferred_element_type=jnp.float32)
    acc_up = jnp.dot(normed_piece, up_piece, preferred_element_type=jnp.float32)
    normalized_rows = normed_piece
    gains = gain_piece.astype(jnp.float32)
    mlp_in = normalized_rows
    sigma = jax.nn.sigmoid(acc_gate)
    swish = acc_gate * sigma
    act = (swish * acc_up).astype(jnp.bfloat16)
    mlp_out = jnp.einsum(
        "rf,nf->rn",
        act,
        lax.all_gather(w_down, "shard", axis=0, tiled=True),
        preferred_element_type=jnp.float32,
    )
    output = (valid * (resid + mlp_out)).astype(jnp.bfloat16).reshape(seq_count, piece, width)
    grad_y = cotangent.astype(jnp.float32).reshape(rows, width) * valid
    grad_y_low = grad_y.astype(jnp.bfloat16)
    grad_act = jnp.dot(
        grad_y_low,
        lax.all_gather(w_down, "shard", axis=0, tiled=True),
        preferred_element_type=jnp.float32,
    )
    grad_gate = (grad_act * acc_up * sigma * (1.0 + acc_gate * (1.0 - sigma))).astype(jnp.bfloat16)
    grad_up = (grad_act * swish).astype(jnp.bfloat16)
    gate_piece, up_piece = lax.all_gather((w_gate, w_up), "shard", axis=0, tiled=True)
    grad_mid = jnp.einsum(
        "rf,nf->rn", grad_gate, gate_piece, preferred_element_type=jnp.float32
    ) + jnp.einsum("rf,nf->rn", grad_up, up_piece, preferred_element_type=jnp.float32)
    grad_resid = grad_y + norm_back(mid_unit, inverse_mid, grad_mid * gains)
    mlp_gain_part = jnp.sum(mid_unit * grad_mid, 0)
    normalized_rows = mlp_in
    mlp_grads = jax.tree.map(
        lambda part: lax.psum_scatter(
            part.astype(jnp.bfloat16), "shard", scatter_dimension=0, tiled=True
        ).astype(jnp.float32),
        (
            outer(normalized_rows, grad_gate),
            outer(normalized_rows, grad_up),
            outer(grad_y_low, act),
        ),
    )
    resid_low = grad_resid.astype(jnp.bfloat16)
    grad_mixed = jnp.dot(
        resid_low,
        lax.all_gather(w_out, "shard", axis=0, tiled=True),
        preferred_element_type=jnp.float32,
    )
    grad_mixed = grad_mixed.astype(jnp.bfloat16).reshape(
        seq_count, piece, heads_kv, groups, head_dim
    )
    prob_again = jnp.exp(scores(query_rows, near_pair[0], allowed, scale) - log_total)
    grad_prob = jnp.einsum(
        "sqhgd,skhd->shgqk", grad_mixed, near_pair[1], preferred_element_type=jnp.float32
    )
    grad_values = jnp.einsum(
        "shgqk,sqhgd->skhd",
        prob_again.astype(jnp.bfloat16),
        grad_mixed,
        preferred_element_type=jnp.float32,
    )
    grad_score = (
        prob_again * (grad_prob - jnp.sum(prob_again * grad_prob, -1, keepdims=True))
    ).astype(jnp.bfloat16)
    grad_queries = (
        jnp.einsum(
            "shgqk,skhd->sqhgd", grad_score, near_pair[0], preferred_element_type=jnp.float32
        )
        * scale
    )
    grad_keys = (
        jnp.einsum("shgqk,sqhgd->skhd", grad_score, query_rows, preferred_element_type=jnp.float32)
        * scale
    )
    grad_pair = jnp.stack([grad_keys, grad_values])
    own_grad = grad_pair[:, :, reach * piece :]
    for back in range(1, reach + 1):
        lower = (reach - back) * piece
        own_grad = own_grad + passed_along(grad_pair[:, :, lower : lower + piece], "shard", -back)
    grad_query_post = grad_queries.reshape(seq_count, piece, heads_q, head_dim)
    grad_query_normed = grad_query_post * cosine_table - rotated_rows(grad_query_post * sine_table)
    grad_key_normed = own_grad[0] * cosine_table - rotated_rows(own_grad[0] * sine_table)
    grad_query_raw, query_gain_grad = head_norm_back(
        query_unit, query_inverse, grad_query_normed, query_gain.astype(jnp.float32)
    )
    grad_key_raw, key_gain_grad = head_norm_back(
        key_unit, key_inverse, grad_key_normed, key_gain.astype(jnp.float32)
    )
    grad_query_low = grad_query_raw.reshape(rows, heads_q * head_dim).astype(jnp.bfloat16)
    grad_key_low = grad_key_raw.reshape(rows, heads_kv * head_dim).astype(jnp.bfloat16)
    grad_value_low = own_grad[1].reshape(rows, heads_kv * head_dim).astype(jnp.bfloat16)
    query_piece, key_piece, value_piece = lax.all_gather(
        (w_query, key_matrix, value_matrix), "shard", axis=0, tiled=True
    )
    grad_in = (
        jnp.einsum("rf,nf->rn", grad_query_low, query_piece, preferred_element_type=jnp.float32)
        + jnp.einsum("rf,nf->rn", grad_key_low, key_piece, preferred_element_type=jnp.float32)
        + jnp.einsum("rf,nf->rn", grad_value_low, value_piece, preferred_element_type=jnp.float32)
    )
    grad_tokens = (
        (grad_resid + norm_back(x_unit, inverse_in, grad_in * attn_gains))
        .astype(jnp.bfloat16)
        .reshape(seq_count, piece, width)
    )
    attn_gain_part = jnp.sum(x_unit * grad_in, 0)
    normalized_rows = attn_in
    attn_grads = jax.tree.map(
        lambda part: lax.psum_scatter(
            part.astype(jnp.bfloat16), "shard", scatter_dimension=0, tiled=True
        ).astype(jnp.float32),
        (
            outer(normalized_rows, grad_query_low),
            outer(normalized_rows, grad_key_low),
            outer(normalized_rows, grad_value_low),
            outer(resid_low, mixed_rows),
        ),
    )
    head_grads = lax.psum(
        (query_gain_grad, key_gain_grad, attn_gain_part, mlp_gain_part), ("rep", "shard")
    )
    attn_gain_total = lax.dynamic_slice_in_dim(head_grads[2], shard_at * owned, owned, 0)
    mlp_gain_total = lax.dynamic_slice_in_dim(head_grads[3], shard_at * owned, owned, 0)
    summed = (
        lax.psum(attn_grads[0].astype(jnp.bfloat16), "rep").astype(jnp.float32),
        lax.psum(attn_grads[1].astype(jnp.bfloat16), "rep").astype(jnp.float32),
        lax.psum(attn_grads[2].astype(jnp.bfloat16), "rep").astype(jnp.float32),
        lax.psum(attn_grads[3].astype(jnp.bfloat16), "rep").astype(jnp.float32),
        lax.psum(mlp_grads[0].astype(jnp.bfloat16), "rep").astype(jnp.float32),
        lax.psum(mlp_grads[1].astype(jnp.bfloat16), "rep").astype(jnp.float32),
        lax.psum(mlp_grads[2].astype(jnp.bfloat16), "rep").astype(jnp.float32),
    )
    attn_grads = summed[:4]
    mlp_grads = summed[4:]
    return (
        output,
        grad_tokens,
        attn_gain_total,
        attn_grads[0],
        attn_grads[1],
        attn_grads[2],
        head_grads[0],
        head_grads[1],
        attn_grads[3],
        mlp_gain_total,
        mlp_grads[0],
        mlp_grads[1],
        mlp_grads[2],
    )


CORE, ACROSS_X, ACROSS_Y = 1, 2, 4
VMEM_BYTES = 56 * 2**20
FREE = pl.CostEstimate(flops=1, bytes_accessed=1, transcendentals=0)


def across(x, mask):
    count = lax.axis_size("rep")
    return lax.ppermute(x, "rep", [(i, i ^ mask) for i in range(count)])


def around(x, by):
    count = lax.axis_size("shard")
    return lax.ppermute(x, "shard", [(i, (i + by) % count) for i in range(count)])


class Stage(dict):
    __getattr__ = dict.__getitem__
    __setattr__ = dict.__setitem__
    __delattr__ = dict.__delitem__

    def end(self):
        self.update(lax.optimization_barrier(dict(self)))


def in_order(calls):
    outs = []
    for call, first, *rest in calls:
        if outs:
            last = outs[-1][0] if isinstance(outs[-1], (list, tuple)) else outs[-1]
            first = lax.optimization_barrier((first, last))[0]
        outs.append(call(first, *rest))
    return outs


def ring_sum_first(chunks):
    return around(chunks[2], 1), around(chunks[1], -1)


def near(piece):
    return across(piece, ACROSS_X), across(piece, ACROSS_Y)


def far(from_x, from_y):
    half = from_x.shape[0] // 2
    return across(from_x[:half], ACROSS_Y), across(from_y[half:], ACROSS_X)


def rounded_sum(*parts):
    return sum(part.astype(jnp.float32) for part in parts).astype(jnp.bfloat16)


def sequence_pairs(turn):
    groups, shards = lax.axis_size("rep"), lax.axis_size("shard")
    pairs = []
    for group in range(groups):
        chip, core = divmod(group, 2)
        for at in range(shards):
            to_group, to_shard = 2 * chip + at // 2, 2 * core + (turn ^ (at & 1))
            pairs.append((group * shards + at, to_group * shards + to_shard))
    return pairs


def rolled(x):
    count, at = lax.axis_size("shard"), lax.axis_index("shard")
    width = x.shape[1] // count
    return jnp.concatenate(
        [lax.dynamic_slice_in_dim(x, ((at - i) % count) * width, width, 1) for i in range(count)],
        1,
    )


def to_sequences_send(x):
    odd = lax.axis_index("shard") & 1
    return [
        lax.ppermute(
            lax.dynamic_index_in_dim(x, turn ^ odd, 0, keepdims=False),
            ("rep", "shard"),
            sequence_pairs(turn),
        )
        for turn in range(2)
    ]


def from_sequences_send(x):
    odd = lax.axis_index("shard") & 1
    x = x.reshape(2, x.shape[0] // 2, x.shape[1])
    return [
        lax.ppermute(
            lax.dynamic_index_in_dim(x, turn ^ odd, 0, keepdims=False),
            ("rep", "shard"),
            [(to, at) for at, to in sequence_pairs(turn)],
        )
        for turn in range(2)
    ]


def in_turn(came):
    even = lax.axis_index("shard") & 1 == 0
    return [jnp.where(even, came[0], came[1]), jnp.where(even, came[1], came[0])]


def column_block(weights, at):
    cuts = [w.shape[1] // 8 for w in weights]
    return jnp.concatenate(
        [lax.dynamic_slice_in_dim(w, at * cut, cut, 1) for w, cut in zip(weights, cuts)], 1
    )


def whole_columns(me, own, other, widths):
    rows, columns = own.shape[0] // 4, own.shape[1]

    def body(me_ref, own_ref, other_ref, *outs):
        def put(block):
            start = 0
            for out, width in zip(outs, widths):
                out[...] = block[:, start : start + width].astype(jnp.float32)
                start += width

        mine = (me_ref[0] ^ pl.program_id(0)) & 1 == 0
        pl.when(mine)(lambda: put(own_ref))
        pl.when(jnp.logical_not(mine))(lambda: put(other_ref))

    spec = pl.BlockSpec((rows, columns), lambda i, at: ((at[0] ^ i) >> 1, 0))
    return pl.pallas_call(
        body,
        grid_spec=pltpu.PrefetchScalarGridSpec(
            num_scalar_prefetch=1,
            grid=(8,),
            in_specs=[spec, spec],
            out_specs=[pl.BlockSpec((rows, w), lambda i, at: (0, i)) for w in widths],
        ),
        out_shape=[jax.ShapeDtypeStruct((rows, 8 * w), jnp.float32) for w in widths],
        compiler_params=pltpu.CompilerParams(vmem_limit_bytes=VMEM_BYTES),
        cost_estimate=FREE,
        name="whole_columns",
    )(me, own, other)


def turned(x):
    return pltpu.roll(x, x.shape[-1] // 2, x.ndim - 1)


def nt(left, right):
    return lax.dot_general(
        left, right, (((1,), (1,)), ((), ())), preferred_element_type=jnp.float32
    )


def tn(left, right):
    return lax.dot_general(
        left, right, (((0,), (0,)), ((), ())), preferred_element_type=jnp.float32
    )


def unit_of(raw):
    inverse = lax.rsqrt(jnp.mean(raw * raw, -1, keepdims=True) + EPS)
    return raw * inverse, inverse


def project_body(
    normed, own0, came0, own1, came1, cosine, sine, gains, raw, query, key_value
):
    step = own0.shape[0]
    dim = cosine.shape[1]
    for block, (own, came) in enumerate(((own0, came0), (own1, came1))):
        at = block * 4 * dim
        raw[:, at : at + 4 * dim] = jnp.dot(
            normed[:, :step], own[...], preferred_element_type=jnp.float32
        ) + jnp.dot(normed[:, step:], came[...], preferred_element_type=jnp.float32)
        for i in range(3):
            unit, _ = unit_of(raw[:, at + i * dim : at + (i + 1) * dim])
            head = unit * gains[i // 2 : i // 2 + 1, :]
            head = (head * cosine[...] + turned(head) * sine[...]).astype(jnp.bfloat16)
            if i < 2:
                query[:, (2 * block + i) * dim : (2 * block + i + 1) * dim] = head
            else:
                key_value[:, 2 * block * dim : (2 * block + 1) * dim] = head
        key_value[:, (2 * block + 1) * dim : (2 * block + 2) * dim] = raw[
            :, at + 3 * dim : at + 4 * dim
        ].astype(jnp.bfloat16)


def window_mask(info, part, rows, columns):
    half = columns - rows
    row = lax.broadcasted_iota(jnp.int32, (rows, columns), 0)
    column = lax.broadcasted_iota(jnp.int32, (rows, columns), 1)
    gap = column - row - half
    slot = column + ((info[0] - 1) * half + part * rows)
    allowed = (gap <= 0) & (gap > -half) & (slot >= 0) & ((slot < info[1]) | (gap == 0))
    mask = jnp.where(allowed, 0.0, NEG)
    return jnp.concatenate([mask, mask], 0)


def two_heads(ref, at, block, dim):
    return jnp.concatenate(
        [ref[at, h * dim : (h + 1) * dim] for h in (2 * block, 2 * block + 1)], 0
    )


def key_columns(block, dim):
    key = slice(2 * block * dim, (2 * block + 1) * dim)
    value = slice((2 * block + 1) * dim, (2 * block + 2) * dim)
    return key, value


def seen_pair(before, own, part, block, dim):
    here, there = key_columns(block, dim), key_columns(1 - block, dim)
    rows = own.shape[0] // 2
    if part == 0:
        return [
            jnp.concatenate([before[:, t], own[:rows, h]], 0) for h, t in zip(here, there)
        ]
    return [jnp.concatenate([before[rows:, t], own[:, h]], 0) for h, t in zip(here, there)]


def attend_body(info, query, before, own, mixed, log_total):
    dim = own.shape[1] // 4
    rows = query.shape[0] // 2
    for part in range(2):
        at = slice(part * rows, (part + 1) * rows)
        mask = window_mask(info, part, rows, 3 * rows)
        for block in range(2):
            keys, values = seen_pair(before, own, part, block, dim)
            score = nt(two_heads(query, at, block, dim), keys) * dim**-0.5 + mask
            top = jnp.max(score, -1, keepdims=True)
            expo = jnp.exp(score - top)
            total = jnp.sum(expo, -1, keepdims=True)
            prob = (expo * (1.0 / total)).astype(jnp.bfloat16)
            out = jnp.dot(prob, values, preferred_element_type=jnp.float32).astype(jnp.bfloat16)
            log = jnp.broadcast_to(top + jnp.log(total), (2 * rows, dim))
            for i in range(2):
                on = slice((2 * block + i) * dim, (2 * block + i + 1) * dim)
                mixed[at, on] = out[i * rows : (i + 1) * rows]
                log_total[at, on] = log[i * rows : (i + 1) * rows]


def attend_back_body(
    info, query, before, own, log_total, grad_resid, weight0, weight1, raw, cosine, sine, gain,
    grad_query, grad_own, grad_before, gain_part, grad_keys, grad_values, grad_mixed,
):
    dim = own.shape[1] // 4
    rows = query.shape[0] // 2
    scale = dim**-0.5
    gain_total = jnp.zeros((1, dim), jnp.float32)
    masks = [window_mask(info, part, rows, 3 * rows) for part in range(2)]
    for block, weight in enumerate((weight0, weight1)):
        on = slice(2 * block * dim, 2 * (block + 1) * dim)
        grad_mixed[:, on] = jnp.dot(
            grad_resid[...], weight[...], preferred_element_type=jnp.float32
        ).astype(jnp.bfloat16)
        grad_keys[...] = jnp.zeros_like(grad_keys)
        grad_values[...] = jnp.zeros_like(grad_values)
        for part in range(2):
            keys, values = seen_pair(before, own, part, block, dim)
            at = slice(part * rows, (part + 1) * rows)
            seen = slice(part * rows, part * rows + 3 * rows)
            queries = two_heads(query, at, block, dim)
            grads = two_heads(grad_mixed, at, block, dim)
            log = two_heads(log_total, at, block, dim)[:, :1]
            prob = jnp.exp(nt(queries, keys) * scale + masks[part] - log)
            grad_prob = nt(grads, values)
            inner = jnp.sum(prob * grad_prob, -1, keepdims=True)
            grad_score = (prob * (grad_prob - inner)).astype(jnp.bfloat16)
            grad_values[seen, :] += tn(prob.astype(jnp.bfloat16), grads)
            grad_keys[seen, :] += tn(grad_score, queries) * scale
            both = jnp.dot(grad_score, keys, preferred_element_type=jnp.float32) * scale
            for i in range(2):
                head = 2 * block + i
                back = both[i * rows : (i + 1) * rows]
                back = back * cosine[at, :] - turned(back) * sine[at, :]
                there = (2 * head - head % 2) * dim
                unit, inverse = unit_of(raw[at, there : there + dim])
                gain_total += jnp.sum(unit * back, 0, keepdims=True)
                back = back * gain[...]
                back = inverse * (back - unit * jnp.mean(back * unit, -1, keepdims=True))
                grad_query[at, head * dim : (head + 1) * dim] = back.astype(jnp.bfloat16)
        for grad, here, there in zip(
            (grad_keys, grad_values), key_columns(block, dim), key_columns(1 - block, dim)
        ):
            grad_before[:, there] = grad[: 2 * rows, :].astype(jnp.bfloat16)
            grad_own[:, here] = grad[2 * rows :, :]
    gain_part[...] = gain_total


def finish_body(grad_query, grad_own, came, raw, cosine, sine, gain, even, odd, gain_part):
    dim = cosine.shape[1]
    total = jnp.zeros((1, dim), jnp.float32)
    for block, out in enumerate((even, odd)):
        key, value = key_columns(block, dim)
        back = grad_own[:, key] + came[:, key].astype(jnp.float32)
        back = back * cosine[...] - turned(back) * sine[...]
        unit, inverse = unit_of(raw[:, (4 * block + 2) * dim : (4 * block + 3) * dim])
        total += jnp.sum(unit * back, 0, keepdims=True)
        back = back * gain[...]
        back = inverse * (back - unit * jnp.mean(back * unit, -1, keepdims=True))
        out[:, : 2 * dim] = grad_query[:, 2 * block * dim : (2 * block + 2) * dim]
        out[:, 2 * dim : 3 * dim] = back.astype(jnp.bfloat16)
        grad_value = grad_own[:, value] + came[:, value].astype(jnp.float32)
        out[:, 3 * dim :] = grad_value.astype(jnp.bfloat16)
    gain_part[...] = total


def vmem_call(body, outs, scratch=(), scalars=0, name=None):
    def call(*args):
        in_specs = [
            pl.BlockSpec(memory_space=pltpu.SMEM if i < scalars else pltpu.VMEM)
            for i in range(len(args))
        ]
        return pl.pallas_call(
            body,
            grid=(1,),
            out_shape=outs,
            in_specs=in_specs,
            out_specs=jax.tree.map(lambda _: pl.BlockSpec(memory_space=pltpu.VMEM), outs),
            scratch_shapes=scratch,
            compiler_params=pltpu.CompilerParams(vmem_limit_bytes=VMEM_BYTES),
        cost_estimate=FREE,
            name=name,
        )(*args)

    return call


def hidden_units(mids, grads_y, weights):
    width, units = weights.shape[0], weights.shape[1] // 3
    count = len(mids)
    heights = [m.shape[0] for m in mids]
    rows, cut = sum(heights), units // 3

    def body(*refs):
        gate_w, up_w, w_down, act, grad_gate, grad_up = refs[2 * count :]
        start = 0
        for mid, grad_y in zip(refs[:count], refs[count : 2 * count]):
            at = slice(start, start + mid.shape[0])
            start += mid.shape[0]
            gate = jnp.dot(mid[...], gate_w[...], preferred_element_type=jnp.float32)
            up = jnp.dot(mid[...], up_w[...], preferred_element_type=jnp.float32)
            grad_act = jnp.dot(grad_y[...], w_down[...], preferred_element_type=jnp.float32)
            sigma = jax.nn.sigmoid(gate)
            swish = gate * sigma
            act[at, :] = (swish * up).astype(jnp.bfloat16)
            slope = grad_act * up * sigma * (1.0 + gate * (1.0 - sigma))
            grad_gate[at, :] = slope.astype(jnp.bfloat16)
            grad_up[at, :] = (grad_act * swish).astype(jnp.bfloat16)

    row_specs = [
        pl.BlockSpec((h, width), lambda j: (0, 0), pipeline_mode=pl.Buffered(1)) for h in heights
    ]
    return pl.pallas_call(
        body,
        grid=(3,),
        out_shape=[jax.ShapeDtypeStruct((rows, units), jnp.bfloat16)] * 3,
        in_specs=[
            *row_specs,
            *row_specs,
            pl.BlockSpec((width, cut), lambda j: (0, j)),
            pl.BlockSpec((width, cut), lambda j: (0, j + 3)),
            pl.BlockSpec((width, cut), lambda j: (0, j + 6)),
        ],
        out_specs=[pl.BlockSpec((rows, cut), lambda j: (0, j))] * 3,
        compiler_params=pltpu.CompilerParams(vmem_limit_bytes=VMEM_BYTES),
        cost_estimate=FREE,
        name="hidden_units",
    )(*mids, *grads_y, weights, weights, weights)


def from_hidden(pairs, eighths):
    count, parts = len(pairs), len(eighths)
    rows, units = pairs[0][0].shape[0] // 8, pairs[0][0].shape[1]
    width = pairs[0][1].shape[0]
    cut = width // 4

    def body(*refs):
        ins, outs = refs[: -(parts // 2)], refs[-(parts // 2) :]
        total = 0.0
        for i in range(count):
            part = ins[i * (parts + 1) : (i + 1) * (parts + 1)]
            left = jnp.concatenate([p[...] for p in part[:-1]], 0)
            total = total + nt(left, part[-1][...])
        for i, out in enumerate(outs):
            out[...] = total[2 * i * rows : 2 * (i + 1) * rows].astype(jnp.bfloat16)

    specs, args = [], []
    for left, right, at in pairs:
        specs += [pl.BlockSpec((rows, units), lambda j, e=e: (e, 0)) for e in eighths]
        specs.append(pl.BlockSpec((cut, units), lambda j, at=at: (j, at)))
        args += [left] * parts + [right]
    return pl.pallas_call(
        body,
        grid=(4,),
        out_shape=[jax.ShapeDtypeStruct((2 * rows, width), jnp.bfloat16)] * (parts // 2),
        in_specs=specs,
        out_specs=[pl.BlockSpec((2 * rows, cut), lambda j: (0, j))] * (parts // 2),
        compiler_params=pltpu.CompilerParams(vmem_limit_bytes=VMEM_BYTES),
        cost_estimate=FREE,
        name="from_hidden",
    )(*args)


def row_outer(lefts, groups, first, tiles, added=None, places=None, part=None):
    rights = [right for group in groups for right in group]
    places = range(len(rights)) if places is None else places
    added = [] if added is None else [added] * len(rights)
    width = lefts[0].shape[1]
    tile = width // 8
    count = len(lefts)
    rows = sum(left.shape[0] for left in lefts)
    wide = rights[0].shape[1] // (1 if part is None else 2)
    columns = [wide * len(group) for group in groups]

    def body(*refs):
        left_refs = refs[:count]
        right_refs = refs[count : count + len(rights)]
        add_refs = refs[count + len(rights) : count + len(rights) + len(added)]
        outs = refs[count + len(rights) + len(added) :]
        place = 0
        for i, group in enumerate(groups):
            column = 0
            for _ in group:
                on = slice(column, column + wide)
                total, start = 0.0, 0
                for left in left_refs:
                    stop = start + left.shape[0]
                    total = total + tn(left[...], right_refs[place][start:stop, :])
                    start = stop
                if added:
                    total = total + add_refs[place][...].astype(jnp.float32)
                outs[i][:, on] = total.astype(jnp.bfloat16)
                place += 1
                column += wide

    return pl.pallas_call(
        body,
        grid=(tiles,),
        out_shape=[jax.ShapeDtypeStruct((tiles * tile, c), jnp.bfloat16) for c in columns],
        in_specs=[
            *(pl.BlockSpec((left.shape[0], tile), lambda j: (0, j + first)) for left in lefts),
            *(
                pl.BlockSpec(
                    (right.shape[0], wide), lambda j: (0, part or 0), pipeline_mode=pl.Buffered(1)
                )
                for right in rights
            ),
            *(
                pl.BlockSpec((tile, wide), lambda j, at=at: (j + first, at))
                for at in places[: len(added)]
            ),
        ],
        out_specs=[pl.BlockSpec((tile, c), lambda j: (j, 0)) for c in columns],
        compiler_params=pltpu.CompilerParams(vmem_limit_bytes=VMEM_BYTES),
        cost_estimate=pl.CostEstimate(
            flops=2 * rows * tiles * tile * sum(columns),
            bytes_accessed=2 * rows * (width + sum(columns)),
            transcendentals=0,
        ),
        name="row_outer",
    )(*lefts, *rights, *added)


def close_body(x, *refs):
    mixed, weights = refs[:4], refs[4:12]
    gains, resid, mid = refs[12:]
    at = pl.program_id(0)
    step = x.shape[1]
    columns = weights[0].shape[1]
    total = x[...].astype(jnp.float32)
    for i in range(8):
        part = mixed[i // 2][:, (i % 2) * columns : (i % 2 + 1) * columns]
        total = total + nt(part, weights[i][...])
    resid[:, pl.ds(pl.multiple_of(at * step, step), step)] = total

    @pl.when(at == 3)
    def _():
        unit, _ = unit_of(resid[...])
        mid[...] = (unit * gains[...]).astype(jnp.bfloat16)


def close_attention(x, mixed, weights, gains):
    rows, width = x.shape
    step = width // 4
    whole = lambda a: pl.BlockSpec(a.shape, lambda j: (0, 0))
    return pl.pallas_call(
        close_body,
        grid=(4,),
        out_shape=[
            jax.ShapeDtypeStruct((rows, width), jnp.float32),
            jax.ShapeDtypeStruct((rows, width), jnp.bfloat16),
        ],
        in_specs=[
            pl.BlockSpec((rows, step), lambda j: (0, j)),
            *(whole(m) for m in mixed),
            *(pl.BlockSpec((step, w.shape[1]), lambda j: (j, 0)) for w in weights),
            whole(gains),
        ],
        out_specs=[pl.BlockSpec((rows, width), lambda j: (0, 0))] * 2,
        compiler_params=pltpu.CompilerParams(vmem_limit_bytes=VMEM_BYTES),
        cost_estimate=FREE,
        name="close_attention",
    )(x, *mixed, *weights, gains)


def back_to_rows(blocks, weights):
    rows = blocks[0].shape[0]
    step, columns = weights[0][0].shape
    count = len(blocks)

    def body(*refs):
        lefts = refs[:count]
        hbm = refs[count : 3 * count]
        out = refs[3 * count]
        held, sems = refs[3 * count + 1 :]
        copies = []
        for i in range(count):
            own, came = hbm[2 * i : 2 * i + 2]
            copies.append(
                [
                    pltpu.make_async_copy(own, held.at[i, :step], sems.at[i, 0]),
                    pltpu.make_async_copy(came, held.at[i, step:], sems.at[i, 1]),
                ]
            )
        for some in copies:
            for copy in some:
                copy.start()
        for i in range(count):
            for copy in copies[i]:
                copy.wait()
            for k in range(4):
                on = slice(k * step, (k + 1) * step)
                part = nt(lefts[i][...], held[i, on])
                if i == 0:
                    out[:, on] = part
                else:
                    out[:, on] += part

    return pl.pallas_call(
        body,
        grid=(1,),
        out_shape=jax.ShapeDtypeStruct((rows, 4 * step), jnp.float32),
        in_specs=[pl.BlockSpec(memory_space=pltpu.VMEM)] * count
        + [pl.BlockSpec(memory_space=pl.ANY)] * (2 * count),
        out_specs=pl.BlockSpec(memory_space=pltpu.VMEM),
        scratch_shapes=[
            pltpu.VMEM((count, 4 * step, columns), jnp.bfloat16),
            pltpu.SemaphoreType.DMA((count, 2)),
        ],
        compiler_params=pltpu.CompilerParams(vmem_limit_bytes=VMEM_BYTES),
        cost_estimate=FREE,
        name="back_to_rows",
    )(*blocks, *(part for w in weights for part in w))


def on_device_block(
    tokens,
    lengths,
    attn_gain,
    w_query,
    key_matrix,
    value_matrix,
    query_gain,
    key_gain,
    w_out,
    mlp_gain,
    w_gate,
    w_up,
    w_down,
    cotangent,
):
    low, full = jnp.bfloat16, jnp.float32
    width = tokens.shape[2]
    head_dim = query_gain.shape[0]
    shards = lax.axis_size("shard")
    shard_at = lax.axis_index("shard")
    me = lax.axis_index("rep")
    core = me & 1
    count = lax.axis_size("rep")

    s = Stage()
    s.cotangent = cotangent
    piece = width // shards

    s.own_blocks = [
        column_block((w_query, key_matrix, value_matrix), me ^ i) for i in range(8)
    ]
    gain_rows = jnp.concatenate(
        [jnp.stack([attn_gain, mlp_gain]), jnp.zeros((14, piece), low)], 0
    )
    travelling = jnp.concatenate([s.own_blocks[0], gain_rows], 0)
    s.tokens = tokens
    s.out_block = column_block((w_out,), me)
    s.ffn_block = column_block((w_gate, w_up, w_down), me)
    s.before, s.behind = around(travelling, 1), around(travelling, -1)
    s.other_lengths = across(lengths, CORE)
    s.end()

    s.ahead = around(s.before, 1)
    tokens_sent = to_sequences_send(s.tokens)
    out_own = lax.all_gather(s.out_block, "shard", axis=0, tiled=True)
    del s.out_block, s.tokens
    s.end()

    parts = (s.before, s.ahead, s.behind)
    s.came = jnp.concatenate([part[:piece] for part in parts], 0)
    s.gains = jnp.concatenate([gain_rows[:2], *(part[piece : piece + 2] for part in parts)], 1)
    s.came_near = near(s.came)
    s.came_own = across(s.came, CORE)
    s.x_came = tokens_sent
    del s.before, s.behind, s.ahead
    s.end()

    grad_y_sent = to_sequences_send(s.cotangent)
    s.came_far = far(*s.came_near)
    s.came_other = [s.came_own, *(across(block, CORE) for block in s.came_near)]
    gains = rolled(s.gains.astype(full))
    s.mlp_gains = gains[1:]
    s.attn_gains = gains[:1]
    s.x_low = jnp.concatenate(in_turn(s.x_came), 0)
    rows = s.x_low.shape[0]
    x_rows = s.x_low.astype(full)
    s.inverse_in = lax.rsqrt(jnp.mean(x_rows * x_rows, -1, keepdims=True) + EPS)
    s.normed = rolled((x_rows * s.inverse_in * s.attn_gains).astype(low))
    query_gains = query_gain.astype(full)[None]
    key_gains = key_gain.astype(full)[None]
    s.head_gains = jnp.concatenate([query_gains, key_gains], 0)
    both = jnp.where(
        core == 0,
        jnp.concatenate([lengths, s.other_lengths]),
        jnp.concatenate([s.other_lengths, lengths]),
    )
    length = lax.dynamic_index_in_dim(both, shard_at, 0, keepdims=False)
    s.info = jnp.stack([core, length]).astype(jnp.int32)
    query_pos = core * rows + jnp.arange(rows, dtype=jnp.int32)
    s.valid = (query_pos < length)[:, None].astype(full)
    cosine, sine = tables(query_pos, head_dim)
    s.cosine, sine = cosine[0, :, 0], sine[0, :, 0]
    s.sine = jnp.concatenate([-sine[:, : head_dim // 2], sine[:, head_dim // 2 :]], 1)
    s.out_own = out_own
    del s.gains, s.x_came, s.other_lengths, s.cotangent, s.came_own
    s.end()

    head_columns = 2 * head_dim
    block_columns = 4 * head_dim
    quad_rows = jax.ShapeDtypeStruct((rows, block_columns), low)
    quad_sums = jax.ShapeDtypeStruct((rows, block_columns), full)
    gain_sum = jax.ShapeDtypeStruct((1, head_dim), full)
    project = vmem_call(
        project_body,
        [jax.ShapeDtypeStruct((rows, 2 * block_columns), full), quad_rows, quad_rows],
        name="project",
    )
    attend = vmem_call(attend_body, [quad_rows, quad_sums], scalars=1, name="attend")
    attend_back = vmem_call(
        attend_back_body,
        [quad_rows, quad_sums, quad_rows, gain_sum],
        scratch=[pltpu.VMEM((2 * rows, head_dim), full)] * 2
        + [pltpu.VMEM((rows, block_columns), low)],
        scalars=1,
        name="attend_back",
    )
    finish = vmem_call(finish_body, [quad_rows, quad_rows, gain_sum], name="finish")
    upward = [(i, i + 1) for i in range(0, count, 2)]
    downward = [(i + 1, i) for i in range(0, count, 2)]

    def project_call(i, came, other):
        return (
            project, s.normed, s.own_blocks[2 * i], came, s.own_blocks[2 * i + 1], other,
            s.cosine, s.sine, s.head_gains,
        )

    def attend_call(projected, earlier):
        return (
            lambda query, own, before: attend(s.info, query, before, own),
            *projected[1:], earlier,
        )

    came_last = jnp.concatenate(s.came_far, 0)
    s.came_last = (came_last, across(came_last, CORE))
    s.out_near = near(s.out_own)
    s.out_own_other = across(s.out_own, CORE)
    s.projected = in_order(
        [
            project_call(i, block, other)
            for i, (block, other) in enumerate(zip((s.came, *s.came_near), s.came_other))
        ]
    )
    s.grad_y_came = grad_y_sent
    del s.came_far
    s.end()

    ffn_own = lax.all_gather(s.ffn_block, "shard", axis=0, tiled=True)
    grad_y = jnp.concatenate(in_turn(s.grad_y_came), 0)
    s.grad_y = jnp.where(s.valid > 0, grad_y, jnp.zeros_like(grad_y))
    grad_y_near = near(s.grad_y)
    s.out_far = far(*s.out_near)
    s.out_near_other = [across(block, CORE) for block in s.out_near]
    s.earlier = [lax.ppermute(p[2], "rep", upward) for p in s.projected]
    (s.projected_last,) = in_order([project_call(3, *s.came_last)])
    del s.ffn_block, s.grad_y_came
    s.end()

    out_last = jnp.concatenate(s.out_far, 0)
    s.out_last = (out_last, across(out_last, CORE))
    s.earlier_last = lax.ppermute(s.projected_last[2], "rep", upward)
    s.attended = in_order([attend_call(*pair) for pair in zip(s.projected, s.earlier)])
    s.grad_y_near = grad_y_near
    del s.out_far
    s.end()

    s.projected = [*s.projected, s.projected_last]
    s.earlier = [*s.earlier, s.earlier_last]
    s.out_blocks = [
        s.out_own, s.out_own_other, s.out_near[0], s.out_near_other[0], s.out_near[1],
        s.out_near_other[1], *s.out_last,
    ]
    (last,) = in_order([attend_call(s.projected_last, s.earlier_last)])
    s.attended = [*s.attended, last]
    s.mixed = [a[0] for a in s.attended]
    s.resid, s.mid = close_attention(s.x_low, s.mixed, s.out_blocks, s.mlp_gains)
    s.grad_y_far = far(*s.grad_y_near)
    del s.out_own, s.out_own_other, s.out_near, s.out_near_other, s.out_last
    del s.projected_last, s.earlier_last
    s.end()

    s.mid_near = near(s.mid)
    s.end()

    s.mid_far = far(*s.mid_near)
    s.ffn_own = ffn_own
    s.end()

    s.mids = [s.mid, *s.mid_near, *s.mid_far]
    s.grads_y = [s.grad_y, *s.grad_y_near, *s.grad_y_far]
    s.ffn_other = across(s.ffn_own, CORE)
    units = s.ffn_own.shape[1] // 3
    s.hidden_own = hidden_units(s.mids, s.grads_y, s.ffn_own)
    del s.mid, s.mid_near, s.mid_far, s.grad_y_near, s.grad_y_far
    s.end()

    def gate_up_pairs():
        return [
            (hidden[i], weights, i - 1)
            for hidden, weights in ((s.hidden_own, s.ffn_own), (s.hidden_other, s.ffn_other))
            for i in (1, 2)
        ]

    def down_pairs():
        return [(s.hidden_own[0], s.ffn_own, 2), (s.hidden_other[0], s.ffn_other, 2)]

    def from_hidden_call(pairs, eighths):
        return (
            lambda first: from_hidden([(first, *pairs[0][1:]), *pairs[1:]], eighths),
            pairs[0][0],
        )

    def outer_call(lefts, rights, *added):
        return lambda first: row_outer(lefts, [[first, *rights[1:]]], 0, 8, *added)[0], rights[0]

    def send_near(sent):
        return across(sent[0], ACROSS_X), across(sent[1], ACROSS_Y)

    def send_far(came, rest, split):
        one_tail, two_head = rest
        return (
            across(rounded_sum(one_tail, split(came[1])[1]), ACROSS_X),
            across(rounded_sum(two_head, split(came[0])[1]), ACROSS_Y),
        )

    def total(came, came_far, own, split):
        head, tail = own
        full_sum = lambda *parts: sum(part.astype(full) for part in parts)
        return jnp.concatenate(
            [
                full_sum(head, split(came[0])[0], came_far[1]),
                full_sum(tail, split(came[1])[0], came_far[0]),
            ],
            0,
        )

    by_rows = lambda a: jnp.split(a, 2, 0)
    by_columns = lambda a: jnp.split(a, 2, 1)
    to_plane, rest_of_plane = (2, 6, 5, 7), (3, 4, 0, 1)

    s.hidden_other = hidden_units(s.mids, s.grads_y, s.ffn_other)
    (s.down_outer,) = in_order([outer_call(s.grads_y, s.hidden_other[:1])])
    s.end()

    s.down_came = across(s.down_outer, CORE)
    s.mid_sent = from_hidden(gate_up_pairs(), to_plane)
    del s.down_outer
    s.end()

    s.mid_came = send_near(s.mid_sent)
    s.down_mine, s.mid_rest, s.gate_up_outer = in_order(
        [
            outer_call(s.grads_y, s.hidden_own[:1], s.down_came),
            from_hidden_call(gate_up_pairs(), rest_of_plane),
            outer_call(s.mids, s.hidden_other[1:]),
        ]
    )
    del s.mid_sent, s.down_came
    s.end()

    down_total = lax.psum_scatter(s.down_mine, "shard", scatter_dimension=0, tiled=True)
    s.mid_came_far = send_far(s.mid_came, by_rows(s.mid_rest[0]), by_rows)
    s.gate_up_came = across(s.gate_up_outer, CORE)
    s.mlp_sent, s.mlp_rest = in_order(
        [
            from_hidden_call(down_pairs(), to_plane),
            from_hidden_call(down_pairs(), rest_of_plane),
        ]
    )
    del s.gate_up_outer, s.down_mine
    s.end()

    def back_call(i):
        raw, query, own_pair = s.projected[i]
        return (
            lambda query, *rest: attend_back(s.info, query, *rest),
            query, s.earlier[i], own_pair, s.attended[i][1], s.resid_low,
            *s.out_blocks[2 * i : 2 * i + 2], raw, s.cosine, s.sine, s.head_gains[:1],
        )

    def finish_call(i):
        return (
            finish, s.backs[i][0], s.backs[i][1], s.returned[i], s.projected[i][0],
            s.cosine, s.sine, s.head_gains[1:],
        )

    def give_back(*chips):
        s.returned = s.returned | {
            i: lax.ppermute(s.backs[i][2], "rep", downward) for i in chips
        }

    def odd_call(left, blocks, part=None):
        return lambda first: row_outer([first], [blocks], 0, 8, part=part)[0], left

    def head_call(left, blocks, came, part=None, places=(0, 1, 2, 3)):
        groups = [[blocks[1], blocks[3]], [blocks[2]], [blocks[0]]]
        at = [places[i] for i in (1, 3, 2, 0)]
        return lambda first: row_outer([first], groups, 0, 4, came, at, part), left

    def tail_call(left, blocks, came, part=None, places=(0, 1, 2, 3)):
        groups = [[blocks[2], blocks[3]], [blocks[1]], [blocks[0]]]
        at = [places[i] for i in (2, 3, 1, 0)]
        return lambda first: row_outer([first], groups, 4, 4, came, at, part), left

    s.mlp_came = send_near(s.mlp_sent)
    grad_mid = total(s.mid_came, s.mid_came_far, by_rows(s.mid_rest[1]), by_rows)
    inverse_mid = lax.rsqrt(jnp.mean(s.resid * s.resid, -1, keepdims=True) + EPS)
    mid_unit = s.resid * inverse_mid
    s.mlp_gain_part = jnp.sum(mid_unit * grad_mid, 0)
    s.grad_resid = s.grad_y.astype(full) + norm_back(
        mid_unit, inverse_mid, grad_mid * s.mlp_gains
    )
    s.resid_low = s.grad_resid.astype(low)
    s.resid_rolled = rolled(s.resid_low)
    s.returned = {}
    back, s.out_odd, s.gate_up_mine = in_order(
        [
            back_call(3),
            odd_call(s.resid_rolled, s.mixed, 1),
            outer_call(s.mids, s.hidden_own[1:], s.gate_up_came),
        ]
    )
    s.backs = {3: back}
    s.down_total = down_total
    del s.mid_came, s.mid_came_far, s.mid_rest, s.gate_up_came, s.hidden_own, s.hidden_other
    del s.mids, s.grads_y, s.ffn_own, s.ffn_other, s.mlp_sent
    s.end()

    gate_up_total = lax.psum_scatter(s.gate_up_mine, "shard", scatter_dimension=0, tiled=True)
    s.mlp_came_far = send_far(s.mlp_came, by_rows(s.mlp_rest[0]), by_rows)
    s.out_came = across(s.out_odd, CORE)
    give_back(3)
    back1, back2 = in_order([back_call(1), back_call(2)])
    s.backs = s.backs | {1: back1, 2: back2}
    del s.out_odd, s.gate_up_mine
    s.end()

    s.down_near = near(s.down_total)
    give_back(1, 2)
    mlp_out = total(s.mlp_came, s.mlp_came_far, by_rows(s.mlp_rest[1]), by_rows)
    s.output = (s.valid * (s.resid + mlp_out)).astype(low)
    s.out_head, s.out_tail, back, finished = in_order(
        [
            head_call(s.resid_rolled, s.mixed, s.out_came, 0),
            tail_call(s.resid_rolled, s.mixed, s.out_came, 0),
            back_call(0),
            finish_call(3),
        ]
    )
    s.backs = s.backs | {0: back}
    s.finished = {3: finished}
    del s.mlp_came, s.mlp_came_far, s.mlp_rest, s.out_came, s.resid
    s.end()

    s.out_near = send_near((s.out_head[0], s.out_tail[0]))
    s.down_far = far(*s.down_near)
    give_back(0)
    finished1, finished2 = in_order([finish_call(1), finish_call(2)])
    s.finished = s.finished | {1: finished1, 2: finished2}
    s.gate_up_total = gate_up_total
    s.end()

    def odd_half(half):
        return odd_call(s.normed, [s.finished[i][1] for i in range(4)], half)

    s.out_far = send_far(s.out_near, (s.out_tail[1], s.out_head[1]), by_columns)
    s.down_spread = jnp.concatenate([s.down_total, *s.down_near, *s.down_far], 0)
    s.down_spread_other = across(s.down_spread, CORE)
    (finished,) = in_order([finish_call(0)])
    s.finished = s.finished | {0: finished}
    (s.odd0,) = in_order([odd_half(0)])
    del s.down_total, s.down_near, s.down_far
    s.end()

    my_group = me.astype(jnp.int32)[None]

    def whole_call(widths, own, other):
        return lambda first: whole_columns(my_group, first, other, widths), own

    s.gate_up_near = near(s.gate_up_total)
    s.came0 = across(s.odd0, CORE)
    out_sum = total(s.out_near, s.out_far, (s.out_head[2], s.out_tail[2]), by_columns)
    s.out_chunks = jnp.split(out_sum.astype(low), shards, 0)
    s.out_ring = ring_sum_first(s.out_chunks)
    weights = [
        pair
        for i, block in enumerate(zip((s.came, *s.came_near), s.came_other))
        for pair in ((s.own_blocks[2 * i], block[0]), (s.own_blocks[2 * i + 1], block[1]))
    ] + [(s.own_blocks[6 + i], s.came_last[i]) for i in range(2)]
    blocks = [part for i in range(4) for part in s.finished[i][:2]]
    s.odd1, grad_in = in_order(
        [
            odd_half(1),
            (lambda first: back_to_rows([first, *blocks[1:]], weights), blocks[0]),
        ]
    )
    grad_in = rolled(grad_in)
    x_unit = s.x_low.astype(full) * s.inverse_in
    s.gain_parts = jnp.concatenate(
        [
            jnp.sum(x_unit * grad_in, 0),
            s.mlp_gain_part,
            sum(s.backs[i][3] for i in range(4))[0],
            sum(s.finished[i][2] for i in range(4))[0],
        ]
    )
    s.grad_tokens = (
        s.grad_resid + norm_back(x_unit, s.inverse_in, grad_in * s.attn_gains)
    ).astype(low)
    del s.odd0, s.out_near, s.out_far, s.out_head, s.out_tail, s.backs
    del s.own_blocks, s.came, s.came_near, s.came_other, s.came_last, s.grad_resid, s.x_low
    s.end()

    def halves_call(half, came):
        even = [s.finished[i][0] for i in range(4)]
        return [call(s.normed, even, came, half) for call in (head_call, tail_call)]

    output_sent = from_sequences_send(s.output)
    s.came1 = across(s.odd1, CORE)
    s.out_ring_last = around(rounded_sum(s.out_chunks[3], s.out_ring[0]), 1)
    s.head0, s.tail0 = in_order(halves_call(0, s.came0))
    del s.odd1, s.came0
    s.end()

    def qkv_chunks(came, came_far, head, tail):
        own = total(came, came_far, (head[2], tail[2]), by_columns)
        return jnp.split(own.astype(low), shards, 0)

    s.near0 = send_near((s.head0[0], s.tail0[0]))
    s.gain_came = across(s.gain_parts, CORE)
    s.head1, s.tail1, s.whole_down = in_order(
        [*halves_call(1, s.came1), whole_call((units,), s.down_spread, s.down_spread_other)]
    )
    s.out_total = rounded_sum(s.out_chunks[0], s.out_ring[1], s.out_ring_last)
    s.output_came = output_sent
    del s.came1, s.down_spread, s.down_spread_other, s.output, s.finished
    del s.out_chunks, s.out_ring, s.out_ring_last
    s.end()

    tokens_sent = from_sequences_send(s.grad_tokens)
    s.far0 = send_far(s.near0, (s.tail0[1], s.head0[1]), by_columns)
    s.near1 = send_near((s.head1[0], s.tail1[0]))
    s.gain_parts = s.gain_parts + s.gain_came
    s.tokens_first = tokens_sent[0]
    s.end()

    s.chunks0 = qkv_chunks(s.near0, s.far0, s.head0, s.tail0)
    s.ring0 = ring_sum_first(s.chunks0)
    s.far1 = send_far(s.near1, (s.tail1[1], s.head1[1]), by_columns)
    s.gain_came = across(s.gain_parts, ACROSS_X)
    del s.near0, s.far0, s.head0, s.tail0
    s.end()

    s.last0 = around(rounded_sum(s.chunks0[3], s.ring0[0]), 1)
    s.chunks1 = qkv_chunks(s.near1, s.far1, s.head1, s.tail1)
    s.ring1 = ring_sum_first(s.chunks1)
    s.gate_up_far = far(*s.gate_up_near)
    s.gain_parts = s.gain_parts + s.gain_came
    del s.near1, s.far1, s.head1, s.tail1
    s.end()

    query_total = rounded_sum(s.chunks0[0], s.ring0[1], s.last0)
    s.total0 = jnp.concatenate([query_total, s.out_total], 1)
    s.spread0 = near(s.total0)
    s.last1 = around(rounded_sum(s.chunks1[3], s.ring1[0]), 1)
    s.gate_up_own = jnp.concatenate([s.gate_up_total, *s.gate_up_near, *s.gate_up_far], 0)
    s.gate_up_other = across(s.gate_up_own, CORE)
    s.gain_came = across(s.gain_parts, ACROSS_Y)
    del s.chunks0, s.ring0, s.last0, s.out_total, s.gate_up_near, s.gate_up_far, s.gate_up_total
    s.end()

    s.spread_far0 = far(*s.spread0)
    s.total1 = rounded_sum(s.chunks1[0], s.ring1[1], s.last1)
    s.spread1 = near(s.total1)
    s.gain_parts = s.gain_parts + s.gain_came
    s.gain_came = lax.ppermute(s.gain_parts, "shard", [(i, i ^ 1) for i in range(shards)])
    (s.whole_gate_up,) = in_order([whole_call((units, units), s.gate_up_own, s.gate_up_other)])
    del s.chunks1, s.ring1, s.last1, s.gate_up_own, s.gate_up_other
    s.end()

    s.own0 = jnp.concatenate([s.total0, *s.spread0, *s.spread_far0], 0)
    s.other0 = across(s.own0, CORE)
    s.spread_far1 = far(*s.spread1)
    s.gain_parts = s.gain_parts + s.gain_came
    s.gain_came = lax.ppermute(s.gain_parts, "shard", [(i, i ^ 2) for i in range(shards)])
    del s.total0, s.spread0, s.spread_far0
    s.end()

    s.own1 = jnp.concatenate([s.total1, *s.spread1, *s.spread_far1], 0)
    s.other1 = across(s.own1, CORE)
    (s.whole0,) = in_order([whole_call((head_columns, head_columns), s.own0, s.other0)])
    gain_sums = s.gain_parts + s.gain_came
    s.wide = lax.dynamic_slice_in_dim(
        gain_sums[: 2 * width].reshape(2, width), shard_at * piece, piece, 1
    )
    s.narrow = gain_sums[2 * width :]
    del s.own0, s.other0, s.total1, s.spread1, s.spread_far1
    s.end()

    ((whole_key, whole_value),) = in_order(
        [whole_call((head_dim, head_dim), s.own1, s.other1)]
    )
    return (
        jnp.stack(in_turn(s.output_came)),
        jnp.stack(in_turn([s.tokens_first, tokens_sent[1]])),
        s.wide[0],
        s.whole0[0],
        whole_key,
        whole_value,
        s.narrow[:head_dim],
        s.narrow[head_dim:],
        s.whole0[1],
        s.wide[1],
        *s.whole_gate_up,
        *s.whole_down,
    )


def solution(mesh):
    sizes = (mesh.shape["rep"], mesh.shape["shard"])
    return jax.shard_map(
        on_device_block if sizes == (8, 4) else on_device,
        mesh=mesh,
        in_specs=(
            P("rep", "shard", None),
            P("rep"),
            P("shard"),
            P("shard", None),
            P("shard", None),
            P("shard", None),
            P(),
            P(),
            P("shard", None),
            P("shard"),
            P("shard", None),
            P("shard", None),
            P("shard", None),
            P("rep", "shard", None),
        ),
        out_specs=(
            P("rep", "shard", None),
            P("rep", "shard", None),
            P("shard"),
            P("shard", None),
            P("shard", None),
            P("shard", None),
            P(),
            P(),
            P("shard", None),
            P("shard"),
            P("shard", None),
            P("shard", None),
            P("shard", None),
        ),
        check_vma=False,
    )
```

```python
import jax
import jax.numpy as jnp
from jax import lax
from jax.experimental import pallas as pl
from jax.experimental.pallas import tpu as pltpu
from jax.sharding import PartitionSpec as P

WINDOW = 512


EPS = 1e-06
ROPE_BASE = 1000000.0
NEG = -1e30


def passed_along(x, axis, by):
    devices = lax.axis_size(axis)
    pairs = [(i, i + by) for i in range(devices) if 0 <= i + by < devices]
    return lax.ppermute(x, axis, pairs)


def tables(positions, head_dim):
    half = head_dim // 2
    freq = ROPE_BASE ** (-jnp.arange(half, dtype=jnp.float32) * 2.0 / head_dim)
    angle = positions.astype(jnp.float32)[:, None] * freq[None, :]
    angle = jnp.concatenate([angle, angle], -1)
    return (jnp.cos(angle)[None, :, None, :], jnp.sin(angle)[None, :, None, :])


def rotated_rows(value_rows):
    half = value_rows.shape[-1] // 2
    return jnp.concatenate([-value_rows[..., half:], value_rows[..., :half]], -1)


def head_norm(raw, gain):
    inverse = lax.rsqrt(jnp.mean(raw * raw, -1, keepdims=True) + EPS)
    unit = raw * inverse
    return (unit, inverse, unit * gain)


def norm_back(unit, inverse, grad_unit):
    return inverse * (grad_unit - unit * jnp.mean(grad_unit * unit, -1, keepdims=True))


def head_norm_back(unit, inverse, grad_normed, gain):
    grad_raw = norm_back(unit, inverse, grad_normed * gain)
    return (grad_raw, jnp.sum(unit * grad_normed, axis=(0, 1, 2)))


def scores(query_rows, keys, allowed, scale):
    raw = (
        jnp.einsum("sqhgd,skhd->shgqk", query_rows, keys, preferred_element_type=jnp.float32)
        * scale
    )
    return jnp.where(allowed[:, None, None], raw, NEG)


def outer(left, right):
    return jnp.einsum("rc,rf->cf", left, right, preferred_element_type=jnp.float32)


def on_device(
    tokens,
    lengths,
    attn_gain,
    w_query,
    key_matrix,
    value_matrix,
    query_gain,
    key_gain,
    w_out,
    mlp_gain,
    w_gate,
    w_up,
    w_down,
    cotangent,
):
    seq_count, piece, width = tokens.shape
    head_dim = query_gain.shape[0]
    heads_q = w_query.shape[1] // head_dim
    heads_kv = key_matrix.shape[1] // head_dim
    groups = heads_q // heads_kv
    rows = seq_count * piece
    scale = head_dim ** (-0.5)
    reach = (WINDOW + piece - 2) // piece
    owned = width // lax.axis_size("shard")
    shard_at = lax.axis_index("shard")
    query_pos = shard_at * piece + jnp.arange(piece, dtype=jnp.int32)
    key_pos = (shard_at - reach) * piece + jnp.arange((reach + 1) * piece, dtype=jnp.int32)
    near = (
        (key_pos[None, :] <= query_pos[:, None])
        & (query_pos[:, None] - key_pos[None, :] < WINDOW)
        & (key_pos[None, :] >= 0)
    )
    live = (key_pos[None, None, :] < lengths[:, None, None]) | (
        key_pos[None, :] == query_pos[:, None]
    )[None]
    allowed = near[None] & live
    valid = (query_pos[None, :] < lengths[:, None]).astype(jnp.float32).reshape(rows, 1)
    cosine_table, sine_table = tables(query_pos, head_dim)
    x_rows = tokens.astype(jnp.float32).reshape(rows, width)
    inverse_in = lax.rsqrt(jnp.mean(x_rows * x_rows, -1, keepdims=True) + EPS)
    x_unit = x_rows * inverse_in
    gain_piece = lax.all_gather(attn_gain, "shard", axis=0, tiled=True)
    query_piece = lax.all_gather(w_query, "shard", axis=0, tiled=True)
    key_piece = lax.all_gather(key_matrix, "shard", axis=0, tiled=True)
    value_piece = lax.all_gather(value_matrix, "shard", axis=0, tiled=True)
    normed_piece = (x_unit * gain_piece.astype(jnp.float32)).astype(jnp.bfloat16)
    acc_q = jnp.dot(normed_piece, query_piece, preferred_element_type=jnp.float32)
    acc_k = jnp.dot(normed_piece, key_piece, preferred_element_type=jnp.float32)
    acc_v = jnp.dot(normed_piece, value_piece, preferred_element_type=jnp.float32)
    normalized_rows = normed_piece
    gains = gain_piece.astype(jnp.float32)
    attn_in = normalized_rows
    attn_gains = gains
    query_unit, query_inverse, query_rows_normalized = head_norm(
        acc_q.reshape(seq_count, piece, heads_q, head_dim), query_gain.astype(jnp.float32)
    )
    key_unit, key_inverse, key_normed = head_norm(
        acc_k.reshape(seq_count, piece, heads_kv, head_dim), key_gain.astype(jnp.float32)
    )
    query_rows = (
        (query_rows_normalized * cosine_table + rotated_rows(query_rows_normalized) * sine_table)
        .astype(jnp.bfloat16)
        .reshape(seq_count, piece, heads_kv, groups, head_dim)
    )
    keys_own = (key_normed * cosine_table + rotated_rows(key_normed) * sine_table).astype(
        jnp.bfloat16
    )
    values_own = acc_v.reshape(seq_count, piece, heads_kv, head_dim).astype(jnp.bfloat16)
    own_pair = jnp.stack([keys_own, values_own])
    parts = []
    for fetch_back in range(reach, 0, -1):
        parts.append(passed_along(own_pair, "shard", fetch_back))
    parts.append(own_pair)
    near_pair = jnp.concatenate(parts, 2)
    score = scores(query_rows, near_pair[0], allowed, scale)
    top = jnp.max(score, -1, keepdims=True)
    expo = jnp.exp(score - top)
    total = jnp.sum(expo, -1, keepdims=True)
    prob = expo / total
    log_total = top + jnp.log(total)
    mixed = jnp.einsum(
        "shgqk,skhd->sqhgd",
        prob.astype(jnp.bfloat16),
        near_pair[1],
        preferred_element_type=jnp.float32,
    )
    mixed_rows = mixed.reshape(rows, heads_q * head_dim).astype(jnp.bfloat16)
    resid = x_rows + jnp.einsum(
        "rf,nf->rn",
        mixed_rows,
        lax.all_gather(w_out, "shard", axis=0, tiled=True),
        preferred_element_type=jnp.float32,
    )
    inverse_mid = lax.rsqrt(jnp.mean(resid * resid, -1, keepdims=True) + EPS)
    mid_unit = resid * inverse_mid
    gain_piece = lax.all_gather(mlp_gain, "shard", axis=0, tiled=True)
    gate_piece = lax.all_gather(w_gate, "shard", axis=0, tiled=True)
    up_piece = lax.all_gather(w_up, "shard", axis=0, tiled=True)
    normed_piece = (mid_unit * gain_piece.astype(jnp.float32)).astype(jnp.bfloat16)
    acc_gate = jnp.dot(normed_piece, gate_piece, preferred_element_type=jnp.float32)
    acc_up = jnp.dot(normed_piece, up_piece, preferred_element_type=jnp.float32)
    normalized_rows = normed_piece
    gains = gain_piece.astype(jnp.float32)
    mlp_in = normalized_rows
    sigma = jax.nn.sigmoid(acc_gate)
    swish = acc_gate * sigma
    act = (swish * acc_up).astype(jnp.bfloat16)
    mlp_out = jnp.einsum(
        "rf,nf->rn",
        act,
        lax.all_gather(w_down, "shard", axis=0, tiled=True),
        preferred_element_type=jnp.float32,
    )
    output = (valid * (resid + mlp_out)).astype(jnp.bfloat16).reshape(seq_count, piece, width)
    grad_y = cotangent.astype(jnp.float32).reshape(rows, width) * valid
    grad_y_low = grad_y.astype(jnp.bfloat16)
    grad_act = jnp.dot(
        grad_y_low,
        lax.all_gather(w_down, "shard", axis=0, tiled=True),
        preferred_element_type=jnp.float32,
    )
    grad_gate = (grad_act * acc_up * sigma * (1.0 + acc_gate * (1.0 - sigma))).astype(jnp.bfloat16)
    grad_up = (grad_act * swish).astype(jnp.bfloat16)
    gate_piece, up_piece = lax.all_gather((w_gate, w_up), "shard", axis=0, tiled=True)
    grad_mid = jnp.einsum(
        "rf,nf->rn", grad_gate, gate_piece, preferred_element_type=jnp.float32
    ) + jnp.einsum("rf,nf->rn", grad_up, up_piece, preferred_element_type=jnp.float32)
    grad_resid = grad_y + norm_back(mid_unit, inverse_mid, grad_mid * gains)
    mlp_gain_part = jnp.sum(mid_unit * grad_mid, 0)
    normalized_rows = mlp_in
    mlp_grads = jax.tree.map(
        lambda part: lax.psum_scatter(
            part.astype(jnp.bfloat16), "shard", scatter_dimension=0, tiled=True
        ).astype(jnp.float32),
        (
            outer(normalized_rows, grad_gate),
            outer(normalized_rows, grad_up),
            outer(grad_y_low, act),
        ),
    )
    resid_low = grad_resid.astype(jnp.bfloat16)
    grad_mixed = jnp.dot(
        resid_low,
        lax.all_gather(w_out, "shard", axis=0, tiled=True),
        preferred_element_type=jnp.float32,
    )
    grad_mixed = grad_mixed.astype(jnp.bfloat16).reshape(
        seq_count, piece, heads_kv, groups, head_dim
    )
    prob_again = jnp.exp(scores(query_rows, near_pair[0], allowed, scale) - log_total)
    grad_prob = jnp.einsum(
        "sqhgd,skhd->shgqk", grad_mixed, near_pair[1], preferred_element_type=jnp.float32
    )
    grad_values = jnp.einsum(
        "shgqk,sqhgd->skhd",
        prob_again.astype(jnp.bfloat16),
        grad_mixed,
        preferred_element_type=jnp.float32,
    )
    grad_score = (
        prob_again * (grad_prob - jnp.sum(prob_again * grad_prob, -1, keepdims=True))
    ).astype(jnp.bfloat16)
    grad_queries = (
        jnp.einsum(
            "shgqk,skhd->sqhgd", grad_score, near_pair[0], preferred_element_type=jnp.float32
        )
        * scale
    )
    grad_keys = (
        jnp.einsum("shgqk,sqhgd->skhd", grad_score, query_rows, preferred_element_type=jnp.float32)
        * scale
    )
    grad_pair = jnp.stack([grad_keys, grad_values])
    own_grad = grad_pair[:, :, reach * piece :]
    for back in range(1, reach + 1):
        lower = (reach - back) * piece
        own_grad = own_grad + passed_along(grad_pair[:, :, lower : lower + piece], "shard", -back)
    grad_query_post = grad_queries.reshape(seq_count, piece, heads_q, head_dim)
    grad_query_normed = grad_query_post * cosine_table - rotated_rows(grad_query_post * sine_table)
    grad_key_normed = own_grad[0] * cosine_table - rotated_rows(own_grad[0] * sine_table)
    grad_query_raw, query_gain_grad = head_norm_back(
        query_unit, query_inverse, grad_query_normed, query_gain.astype(jnp.float32)
    )
    grad_key_raw, key_gain_grad = head_norm_back(
        key_unit, key_inverse, grad_key_normed, key_gain.astype(jnp.float32)
    )
    grad_query_low = grad_query_raw.reshape(rows, heads_q * head_dim).astype(jnp.bfloat16)
    grad_key_low = grad_key_raw.reshape(rows, heads_kv * head_dim).astype(jnp.bfloat16)
    grad_value_low = own_grad[1].reshape(rows, heads_kv * head_dim).astype(jnp.bfloat16)
    query_piece, key_piece, value_piece = lax.all_gather(
        (w_query, key_matrix, value_matrix), "shard", axis=0, tiled=True
    )
    grad_in = (
        jnp.einsum("rf,nf->rn", grad_query_low, query_piece, preferred_element_type=jnp.float32)
        + jnp.einsum("rf,nf->rn", grad_key_low, key_piece, preferred_element_type=jnp.float32)
        + jnp.einsum("rf,nf->rn", grad_value_low, value_piece, preferred_element_type=jnp.float32)
    )
    grad_tokens = (
        (grad_resid + norm_back(x_unit, inverse_in, grad_in * attn_gains))
        .astype(jnp.bfloat16)
        .reshape(seq_count, piece, width)
    )
    attn_gain_part = jnp.sum(x_unit * grad_in, 0)
    normalized_rows = attn_in
    attn_grads = jax.tree.map(
        lambda part: lax.psum_scatter(
            part.astype(jnp.bfloat16), "shard", scatter_dimension=0, tiled=True
        ).astype(jnp.float32),
        (
            outer(normalized_rows, grad_query_low),
            outer(normalized_rows, grad_key_low),
            outer(normalized_rows, grad_value_low),
            outer(resid_low, mixed_rows),
        ),
    )
    head_grads = lax.psum(
        (query_gain_grad, key_gain_grad, attn_gain_part, mlp_gain_part), ("rep", "shard")
    )
    attn_gain_total = lax.dynamic_slice_in_dim(head_grads[2], shard_at * owned, owned, 0)
    mlp_gain_total = lax.dynamic_slice_in_dim(head_grads[3], shard_at * owned, owned, 0)
    summed = (
        lax.psum(attn_grads[0].astype(jnp.bfloat16), "rep").astype(jnp.float32),
        lax.psum(attn_grads[1].astype(jnp.bfloat16), "rep").astype(jnp.float32),
        lax.psum(attn_grads[2].astype(jnp.bfloat16), "rep").astype(jnp.float32),
        lax.psum(attn_grads[3].astype(jnp.bfloat16), "rep").astype(jnp.float32),
        lax.psum(mlp_grads[0].astype(jnp.bfloat16), "rep").astype(jnp.float32),
        lax.psum(mlp_grads[1].astype(jnp.bfloat16), "rep").astype(jnp.float32),
        lax.psum(mlp_grads[2].astype(jnp.bfloat16), "rep").astype(jnp.float32),
    )
    attn_grads = summed[:4]
    mlp_grads = summed[4:]
    return (
        output,
        grad_tokens,
        attn_gain_total,
        attn_grads[0],
        attn_grads[1],
        attn_grads[2],
        head_grads[0],
        head_grads[1],
        attn_grads[3],
        mlp_gain_total,
        mlp_grads[0],
        mlp_grads[1],
        mlp_grads[2],
    )


CORE, ACROSS_X, ACROSS_Y = 1, 2, 4
VMEM_BYTES = 56 * 2**20
FREE = pl.CostEstimate(flops=1, bytes_accessed=1, transcendentals=0)


def across(x, mask):
    count = lax.axis_size("rep")
    return lax.ppermute(x, "rep", [(i, i ^ mask) for i in range(count)])


def around(x, by):
    count = lax.axis_size("shard")
    return lax.ppermute(x, "shard", [(i, (i + by) % count) for i in range(count)])


class Stage(dict):
    __getattr__ = dict.__getitem__
    __setattr__ = dict.__setitem__
    __delattr__ = dict.__delitem__

    def end(self):
        self.update(lax.optimization_barrier(dict(self)))


def in_order(calls):
    outs = []
    for call, first, *rest in calls:
        if outs:
            last = outs[-1][0] if isinstance(outs[-1], (list, tuple)) else outs[-1]
            first = lax.optimization_barrier((first, last))[0]
        outs.append(call(first, *rest))
    return outs


def ring_sum_first(chunks):
    return around(chunks[2], 1), around(chunks[1], -1)


def near(piece):
    return across(piece, ACROSS_X), across(piece, ACROSS_Y)


def far(from_x, from_y):
    half = from_x.shape[0] // 2
    return across(from_x[:half], ACROSS_Y), across(from_y[half:], ACROSS_X)


def rounded_sum(*parts):
    return sum(part.astype(jnp.float32) for part in parts).astype(jnp.bfloat16)


def sequence_pairs(turn):
    groups, shards = lax.axis_size("rep"), lax.axis_size("shard")
    pairs = []
    for group in range(groups):
        chip, core = divmod(group, 2)
        for at in range(shards):
            to_group, to_shard = 2 * chip + at // 2, 2 * core + (turn ^ (at & 1))
            pairs.append((group * shards + at, to_group * shards + to_shard))
    return pairs


def rolled(x):
    count, at = lax.axis_size("shard"), lax.axis_index("shard")
    width = x.shape[1] // count
    return jnp.concatenate(
        [lax.dynamic_slice_in_dim(x, ((at - i) % count) * width, width, 1) for i in range(count)],
        1,
    )


def sequence_cuts(x):
    odd = lax.axis_index("shard") & 1
    return [lax.dynamic_index_in_dim(x, turn ^ odd, 0, keepdims=False) for turn in range(2)]


def to_sequence(cut, turn):
    return lax.ppermute(cut, ("rep", "shard"), sequence_pairs(turn))


def from_sequences_send(x):
    odd = lax.axis_index("shard") & 1
    x = x.reshape(2, x.shape[0] // 2, x.shape[1])
    return [
        lax.ppermute(
            lax.dynamic_index_in_dim(x, turn ^ odd, 0, keepdims=False),
            ("rep", "shard"),
            [(to, at) for at, to in sequence_pairs(turn)],
        )
        for turn in range(2)
    ]


def in_turn(came):
    even = lax.axis_index("shard") & 1 == 0
    return [jnp.where(even, came[0], came[1]), jnp.where(even, came[1], came[0])]


def column_block(weights, at):
    cuts = [w.shape[1] // 8 for w in weights]
    return jnp.concatenate(
        [lax.dynamic_slice_in_dim(w, at * cut, cut, 1) for w, cut in zip(weights, cuts)], 1
    )


def whole_columns(me, own, other, widths, part=0):
    rows, columns = own.shape[0] // 4, sum(widths)

    def body(me_ref, own_ref, other_ref, *outs):
        def put(block):
            start = 0
            for out, width in zip(outs, widths):
                out[...] = block[:, start : start + width].astype(jnp.float32)
                start += width

        mine = (me_ref[0] ^ pl.program_id(0)) & 1 == 0
        pl.when(mine)(lambda: put(own_ref))
        pl.when(jnp.logical_not(mine))(lambda: put(other_ref))

    spec = pl.BlockSpec((rows, columns), lambda i, at: ((at[0] ^ i) >> 1, part))
    return pl.pallas_call(
        body,
        grid_spec=pltpu.PrefetchScalarGridSpec(
            num_scalar_prefetch=1,
            grid=(8,),
            in_specs=[spec, spec],
            out_specs=[pl.BlockSpec((rows, w), lambda i, at: (0, i)) for w in widths],
        ),
        out_shape=[jax.ShapeDtypeStruct((rows, 8 * w), jnp.float32) for w in widths],
        compiler_params=pltpu.CompilerParams(vmem_limit_bytes=VMEM_BYTES),
        cost_estimate=FREE,
        name="whole_columns",
    )(me, own, other)


def turned(x):
    return pltpu.roll(x, x.shape[-1] // 2, x.ndim - 1)


def nt(left, right):
    return lax.dot_general(
        left, right, (((1,), (1,)), ((), ())), preferred_element_type=jnp.float32
    )


def tn(left, right):
    return lax.dot_general(
        left, right, (((0,), (0,)), ((), ())), preferred_element_type=jnp.float32
    )


def unit_of(raw):
    inverse = lax.rsqrt(jnp.mean(raw * raw, -1, keepdims=True) + EPS)
    return raw * inverse, inverse


def project_body(
    normed, own0, came0, own1, came1, cosine, sine, gains, raw, query, key_value
):
    step = own0.shape[0]
    dim = cosine.shape[1]
    for block, (own, came) in enumerate(((own0, came0), (own1, came1))):
        at = block * 4 * dim
        raw[:, at : at + 4 * dim] = jnp.dot(
            normed[:, :step], own[...], preferred_element_type=jnp.float32
        ) + jnp.dot(normed[:, step:], came[...], preferred_element_type=jnp.float32)
        for i in range(3):
            unit, _ = unit_of(raw[:, at + i * dim : at + (i + 1) * dim])
            head = unit * gains[i // 2 : i // 2 + 1, :]
            head = (head * cosine[...] + turned(head) * sine[...]).astype(jnp.bfloat16)
            if i < 2:
                query[:, (2 * block + i) * dim : (2 * block + i + 1) * dim] = head
            else:
                key_value[:, 2 * block * dim : (2 * block + 1) * dim] = head
        key_value[:, (2 * block + 1) * dim : (2 * block + 2) * dim] = raw[
            :, at + 3 * dim : at + 4 * dim
        ].astype(jnp.bfloat16)


def window_mask(info, part, rows, columns):
    half = columns - rows
    row = lax.broadcasted_iota(jnp.int32, (rows, columns), 0)
    column = lax.broadcasted_iota(jnp.int32, (rows, columns), 1)
    gap = column - row - half
    slot = column + ((info[0] - 1) * half + part * rows)
    allowed = (gap <= 0) & (gap > -half) & (slot >= 0) & ((slot < info[1]) | (gap == 0))
    mask = jnp.where(allowed, 0.0, NEG)
    return jnp.concatenate([mask, mask], 0)


def two_heads(ref, at, block, dim):
    return jnp.concatenate(
        [ref[at, h * dim : (h + 1) * dim] for h in (2 * block, 2 * block + 1)], 0
    )


def key_columns(block, dim):
    key = slice(2 * block * dim, (2 * block + 1) * dim)
    value = slice((2 * block + 1) * dim, (2 * block + 2) * dim)
    return key, value


def seen_pair(before, own, part, block, dim):
    here, there = key_columns(block, dim), key_columns(1 - block, dim)
    rows = own.shape[0] // 2
    if part == 0:
        return [
            jnp.concatenate([before[:, t], own[:rows, h]], 0) for h, t in zip(here, there)
        ]
    return [jnp.concatenate([before[rows:, t], own[:, h]], 0) for h, t in zip(here, there)]


def attend_body(info, query, before, own, mixed, log_total):
    dim = own.shape[1] // 4
    rows = query.shape[0] // 2
    for part in range(2):
        at = slice(part * rows, (part + 1) * rows)
        mask = window_mask(info, part, rows, 3 * rows)
        for block in range(2):
            keys, values = seen_pair(before, own, part, block, dim)
            score = nt(two_heads(query, at, block, dim), keys) * dim**-0.5 + mask
            top = jnp.max(score, -1, keepdims=True)
            expo = jnp.exp(score - top)
            total = jnp.sum(expo, -1, keepdims=True)
            prob = (expo * (1.0 / total)).astype(jnp.bfloat16)
            out = jnp.dot(prob, values, preferred_element_type=jnp.float32).astype(jnp.bfloat16)
            log = jnp.broadcast_to(top + jnp.log(total), (2 * rows, dim))
            for i in range(2):
                on = slice((2 * block + i) * dim, (2 * block + i + 1) * dim)
                mixed[at, on] = out[i * rows : (i + 1) * rows]
                log_total[at, on] = log[i * rows : (i + 1) * rows]


def attend_back_body(
    info, query, before, own, log_total, grad_resid, weight0, weight1, raw, cosine, sine, gain,
    grad_query, grad_own, grad_before, gain_part, grad_keys, grad_values, grad_mixed,
):
    dim = own.shape[1] // 4
    rows = query.shape[0] // 2
    scale = dim**-0.5
    gain_total = jnp.zeros((1, dim), jnp.float32)
    masks = [window_mask(info, part, rows, 3 * rows) for part in range(2)]
    for block, weight in enumerate((weight0, weight1)):
        on = slice(2 * block * dim, 2 * (block + 1) * dim)
        grad_mixed[:, on] = jnp.dot(
            grad_resid[...], weight[...], preferred_element_type=jnp.float32
        ).astype(jnp.bfloat16)
        grad_keys[...] = jnp.zeros_like(grad_keys)
        grad_values[...] = jnp.zeros_like(grad_values)
        for part in range(2):
            keys, values = seen_pair(before, own, part, block, dim)
            at = slice(part * rows, (part + 1) * rows)
            seen = slice(part * rows, part * rows + 3 * rows)
            queries = two_heads(query, at, block, dim)
            grads = two_heads(grad_mixed, at, block, dim)
            log = two_heads(log_total, at, block, dim)[:, :1]
            prob = jnp.exp(nt(queries, keys) * scale + masks[part] - log)
            grad_prob = nt(grads, values)
            inner = jnp.sum(prob * grad_prob, -1, keepdims=True)
            grad_score = (prob * (grad_prob - inner)).astype(jnp.bfloat16)
            grad_values[seen, :] += tn(prob.astype(jnp.bfloat16), grads)
            grad_keys[seen, :] += tn(grad_score, queries) * scale
            both = jnp.dot(grad_score, keys, preferred_element_type=jnp.float32) * scale
            for i in range(2):
                head = 2 * block + i
                back = both[i * rows : (i + 1) * rows]
                back = back * cosine[at, :] - turned(back) * sine[at, :]
                there = (2 * head - head % 2) * dim
                unit, inverse = unit_of(raw[at, there : there + dim])
                gain_total += jnp.sum(unit * back, 0, keepdims=True)
                back = back * gain[...]
                back = inverse * (back - unit * jnp.mean(back * unit, -1, keepdims=True))
                grad_query[at, head * dim : (head + 1) * dim] = back.astype(jnp.bfloat16)
        for grad, here, there in zip(
            (grad_keys, grad_values), key_columns(block, dim), key_columns(1 - block, dim)
        ):
            grad_before[:, there] = grad[: 2 * rows, :].astype(jnp.bfloat16)
            grad_own[:, here] = grad[2 * rows :, :]
    gain_part[...] = gain_total


def finish_body(grad_query, grad_own, came, raw, cosine, sine, gain, even, odd, gain_part):
    dim = cosine.shape[1]
    total = jnp.zeros((1, dim), jnp.float32)
    for block, out in enumerate((even, odd)):
        key, value = key_columns(block, dim)
        back = grad_own[:, key] + came[:, key].astype(jnp.float32)
        back = back * cosine[...] - turned(back) * sine[...]
        unit, inverse = unit_of(raw[:, (4 * block + 2) * dim : (4 * block + 3) * dim])
        total += jnp.sum(unit * back, 0, keepdims=True)
        back = back * gain[...]
        back = inverse * (back - unit * jnp.mean(back * unit, -1, keepdims=True))
        out[:, : 2 * dim] = grad_query[:, 2 * block * dim : (2 * block + 2) * dim]
        out[:, 2 * dim : 3 * dim] = back.astype(jnp.bfloat16)
        grad_value = grad_own[:, value] + came[:, value].astype(jnp.float32)
        out[:, 3 * dim :] = grad_value.astype(jnp.bfloat16)
    gain_part[...] = total


def vmem_call(body, outs, scratch=(), scalars=0, name=None):
    def call(*args):
        in_specs = [
            pl.BlockSpec(memory_space=pltpu.SMEM if i < scalars else pltpu.VMEM)
            for i in range(len(args))
        ]
        return pl.pallas_call(
            body,
            grid=(1,),
            out_shape=outs,
            in_specs=in_specs,
            out_specs=jax.tree.map(lambda _: pl.BlockSpec(memory_space=pltpu.VMEM), outs),
            scratch_shapes=scratch,
            compiler_params=pltpu.CompilerParams(vmem_limit_bytes=VMEM_BYTES),
        cost_estimate=FREE,
            name=name,
        )(*args)

    return call


def hidden_units(mids, grads_y, weights):
    width, units = weights.shape[0], weights.shape[1] // 3
    count = len(mids)
    heights = [m.shape[0] for m in mids]
    rows, cut = sum(heights), units // 3

    def body(*refs):
        gate_w, up_w, w_down, act, grad_gate, grad_up = refs[2 * count :]
        start = 0
        for mid, grad_y in zip(refs[:count], refs[count : 2 * count]):
            at = slice(start, start + mid.shape[0])
            start += mid.shape[0]
            gate = jnp.dot(mid[...], gate_w[...], preferred_element_type=jnp.float32)
            up = jnp.dot(mid[...], up_w[...], preferred_element_type=jnp.float32)
            grad_act = jnp.dot(grad_y[...], w_down[...], preferred_element_type=jnp.float32)
            sigma = jax.nn.sigmoid(gate)
            swish = gate * sigma
            act[at, :] = (swish * up).astype(jnp.bfloat16)
            slope = grad_act * up * sigma * (1.0 + gate * (1.0 - sigma))
            grad_gate[at, :] = slope.astype(jnp.bfloat16)
            grad_up[at, :] = (grad_act * swish).astype(jnp.bfloat16)

    row_specs = [
        pl.BlockSpec((h, width), lambda j: (0, 0), pipeline_mode=pl.Buffered(1)) for h in heights
    ]
    return pl.pallas_call(
        body,
        grid=(3,),
        out_shape=[jax.ShapeDtypeStruct((rows, units), jnp.bfloat16)] * 3,
        in_specs=[
            *row_specs,
            *row_specs,
            pl.BlockSpec((width, cut), lambda j: (0, j)),
            pl.BlockSpec((width, cut), lambda j: (0, j + 3)),
            pl.BlockSpec((width, cut), lambda j: (0, j + 6)),
        ],
        out_specs=[pl.BlockSpec((rows, cut), lambda j: (0, j))] * 3,
        compiler_params=pltpu.CompilerParams(vmem_limit_bytes=VMEM_BYTES),
        cost_estimate=FREE,
        name="hidden_units",
    )(*mids, *grads_y, weights, weights, weights)


def from_hidden(pairs, eighths):
    count, parts = len(pairs), len(eighths)
    rows, units = pairs[0][0].shape[0] // 8, pairs[0][0].shape[1]
    width = pairs[0][1].shape[0]
    cut = width // 4

    def body(*refs):
        ins, outs = refs[: -(parts // 2)], refs[-(parts // 2) :]
        total = 0.0
        for i in range(count):
            part = ins[i * (parts + 1) : (i + 1) * (parts + 1)]
            left = jnp.concatenate([p[...] for p in part[:-1]], 0)
            total = total + nt(left, part[-1][...])
        for i, out in enumerate(outs):
            out[...] = total[2 * i * rows : 2 * (i + 1) * rows].astype(jnp.bfloat16)

    specs, args = [], []
    for left, right, at in pairs:
        specs += [pl.BlockSpec((rows, units), lambda j, e=e: (e, 0)) for e in eighths]
        specs.append(pl.BlockSpec((cut, units), lambda j, at=at: (j, at)))
        args += [left] * parts + [right]
    return pl.pallas_call(
        body,
        grid=(4,),
        out_shape=[jax.ShapeDtypeStruct((2 * rows, width), jnp.bfloat16)] * (parts // 2),
        in_specs=specs,
        out_specs=[pl.BlockSpec((2 * rows, cut), lambda j: (0, j))] * (parts // 2),
        compiler_params=pltpu.CompilerParams(vmem_limit_bytes=VMEM_BYTES),
        cost_estimate=FREE,
        name="from_hidden",
    )(*args)


def row_outer(lefts, groups, first, tiles, added=None, places=None, part=None):
    rights = [right for group in groups for right in group]
    places = range(len(rights)) if places is None else places
    added = [] if added is None else [added] * len(rights)
    width = lefts[0].shape[1]
    tile = width // 8
    count = len(lefts)
    rows = sum(left.shape[0] for left in lefts)
    wide = rights[0].shape[1] // (1 if part is None else 2)
    columns = [wide * len(group) for group in groups]

    def body(*refs):
        left_refs = refs[:count]
        right_refs = refs[count : count + len(rights)]
        add_refs = refs[count + len(rights) : count + len(rights) + len(added)]
        outs = refs[count + len(rights) + len(added) :]
        place = 0
        for i, group in enumerate(groups):
            column = 0
            for _ in group:
                on = slice(column, column + wide)
                total, start = 0.0, 0
                for left in left_refs:
                    stop = start + left.shape[0]
                    total = total + tn(left[...], right_refs[place][start:stop, :])
                    start = stop
                if added:
                    total = total + add_refs[place][...].astype(jnp.float32)
                outs[i][:, on] = total.astype(jnp.bfloat16)
                place += 1
                column += wide

    return pl.pallas_call(
        body,
        grid=(tiles,),
        out_shape=[jax.ShapeDtypeStruct((tiles * tile, c), jnp.bfloat16) for c in columns],
        in_specs=[
            *(pl.BlockSpec((left.shape[0], tile), lambda j: (0, j + first)) for left in lefts),
            *(
                pl.BlockSpec(
                    (right.shape[0], wide), lambda j: (0, part or 0), pipeline_mode=pl.Buffered(1)
                )
                for right in rights
            ),
            *(
                pl.BlockSpec((tile, wide), lambda j, at=at: (j + first, at))
                for at in places[: len(added)]
            ),
        ],
        out_specs=[pl.BlockSpec((tile, c), lambda j: (j, 0)) for c in columns],
        compiler_params=pltpu.CompilerParams(vmem_limit_bytes=VMEM_BYTES),
        cost_estimate=pl.CostEstimate(
            flops=2 * rows * tiles * tile * sum(columns),
            bytes_accessed=2 * rows * (width + sum(columns)),
            transcendentals=0,
        ),
        name="row_outer",
    )(*lefts, *rights, *added)


def close_body(x, *refs):
    mixed, weights = refs[:4], refs[4:12]
    gains, resid, mid = refs[12:]
    at = pl.program_id(0)
    step = x.shape[1]
    columns = weights[0].shape[1]
    total = x[...].astype(jnp.float32)
    for i in range(8):
        part = mixed[i // 2][:, (i % 2) * columns : (i % 2 + 1) * columns]
        total = total + nt(part, weights[i][...])
    resid[:, pl.ds(pl.multiple_of(at * step, step), step)] = total

    @pl.when(at == 3)
    def _():
        unit, _ = unit_of(resid[...])
        mid[...] = (unit * gains[...]).astype(jnp.bfloat16)


def close_attention(x, mixed, weights, gains):
    rows, width = x.shape
    step = width // 4
    whole = lambda a: pl.BlockSpec(a.shape, lambda j: (0, 0))
    return pl.pallas_call(
        close_body,
        grid=(4,),
        out_shape=[
            jax.ShapeDtypeStruct((rows, width), jnp.float32),
            jax.ShapeDtypeStruct((rows, width), jnp.bfloat16),
        ],
        in_specs=[
            pl.BlockSpec((rows, step), lambda j: (0, j)),
            *(whole(m) for m in mixed),
            *(pl.BlockSpec((step, w.shape[1]), lambda j: (j, 0)) for w in weights),
            whole(gains),
        ],
        out_specs=[pl.BlockSpec((rows, width), lambda j: (0, 0))] * 2,
        compiler_params=pltpu.CompilerParams(vmem_limit_bytes=VMEM_BYTES),
        cost_estimate=FREE,
        name="close_attention",
    )(x, *mixed, *weights, gains)


def back_to_rows(blocks, weights):
    rows = blocks[0].shape[0]
    step, columns = weights[0][0].shape
    count = len(blocks)

    def body(*refs):
        lefts = refs[:count]
        hbm = refs[count : 3 * count]
        out = refs[3 * count]
        held, sems = refs[3 * count + 1 :]
        copies = []
        for i in range(count):
            own, came = hbm[2 * i : 2 * i + 2]
            copies.append(
                [
                    pltpu.make_async_copy(own, held.at[i, :step], sems.at[i, 0]),
                    pltpu.make_async_copy(came, held.at[i, step:], sems.at[i, 1]),
                ]
            )
        for some in copies:
            for copy in some:
                copy.start()
        for i in range(count):
            for copy in copies[i]:
                copy.wait()
            for k in range(4):
                on = slice(k * step, (k + 1) * step)
                part = nt(lefts[i][...], held[i, on])
                if i == 0:
                    out[:, on] = part
                else:
                    out[:, on] += part

    return pl.pallas_call(
        body,
        grid=(1,),
        out_shape=jax.ShapeDtypeStruct((rows, 4 * step), jnp.float32),
        in_specs=[pl.BlockSpec(memory_space=pltpu.VMEM)] * count
        + [pl.BlockSpec(memory_space=pl.ANY)] * (2 * count),
        out_specs=pl.BlockSpec(memory_space=pltpu.VMEM),
        scratch_shapes=[
            pltpu.VMEM((count, 4 * step, columns), jnp.bfloat16),
            pltpu.SemaphoreType.DMA((count, 2)),
        ],
        compiler_params=pltpu.CompilerParams(vmem_limit_bytes=VMEM_BYTES),
        cost_estimate=FREE,
        name="back_to_rows",
    )(*blocks, *(part for w in weights for part in w))


def on_device_block(
    tokens,
    lengths,
    attn_gain,
    w_query,
    key_matrix,
    value_matrix,
    query_gain,
    key_gain,
    w_out,
    mlp_gain,
    w_gate,
    w_up,
    w_down,
    cotangent,
):
    low, full = jnp.bfloat16, jnp.float32
    width = tokens.shape[2]
    head_dim = query_gain.shape[0]
    shards = lax.axis_size("shard")
    shard_at = lax.axis_index("shard")
    me = lax.axis_index("rep")
    core = me & 1
    count = lax.axis_size("rep")

    s = Stage()
    piece = width // shards

    s.own_blocks = [
        column_block((w_query, key_matrix, value_matrix), me ^ i) for i in range(8)
    ]
    gain_rows = jnp.concatenate(
        [jnp.stack([attn_gain, mlp_gain]), jnp.zeros((14, piece), low)], 0
    )
    travelling = jnp.concatenate([s.own_blocks[0], gain_rows], 0)
    s.tokens_cuts = sequence_cuts(tokens)
    s.cotangent_cuts = sequence_cuts(cotangent)
    s.out_block = column_block((w_out,), me)
    s.ffn_block = column_block((w_gate, w_up, w_down), me)
    s.before, s.behind = around(travelling, 1), around(travelling, -1)
    s.other_lengths = across(lengths, CORE)
    s.end()

    s.ahead = around(s.before, 1)
    s.side = jnp.concatenate([s.before[:piece], s.behind[:piece]], 0)
    s.side_near = near(s.side)
    s.x_first = to_sequence(s.tokens_cuts[0], 0)
    s.end()

    out_own = lax.all_gather(s.out_block, "shard", axis=0, tiled=True)
    s.far_piece = s.ahead[:piece]
    s.far_near = near(s.far_piece)
    s.side_last = far(*s.side_near)
    s.x_second = to_sequence(s.tokens_cuts[1], 1)
    s.gains = jnp.concatenate(
        [gain_rows[:2], *(part[piece : piece + 2] for part in (s.before, s.ahead, s.behind))], 1
    )
    del s.out_block, s.tokens_cuts, s.before, s.behind, s.ahead
    s.end()

    def three(side, far_shard):
        return jnp.concatenate([side[:piece], far_shard, side[piece:]], 0)

    s.far_last = far(*s.far_near)
    s.grad_y_first = to_sequence(s.cotangent_cuts[0], 0)
    s.came = [
        three(*pair) for pair in zip((s.side, *s.side_near), (s.far_piece, *s.far_near))
    ]
    s.came_other = [across(block, CORE) for block in s.came]
    gains = rolled(s.gains.astype(full))
    s.mlp_gains = gains[1:]
    s.attn_gains = gains[:1]
    s.x_low = jnp.concatenate(in_turn([s.x_first, s.x_second]), 0)
    rows = s.x_low.shape[0]
    x_rows = s.x_low.astype(full)
    s.inverse_in = lax.rsqrt(jnp.mean(x_rows * x_rows, -1, keepdims=True) + EPS)
    s.normed = rolled((x_rows * s.inverse_in * s.attn_gains).astype(low))
    query_gains = query_gain.astype(full)[None]
    key_gains = key_gain.astype(full)[None]
    s.head_gains = jnp.concatenate([query_gains, key_gains], 0)
    both = jnp.where(
        core == 0,
        jnp.concatenate([lengths, s.other_lengths]),
        jnp.concatenate([s.other_lengths, lengths]),
    )
    length = lax.dynamic_index_in_dim(both, shard_at, 0, keepdims=False)
    s.info = jnp.stack([core, length]).astype(jnp.int32)
    query_pos = core * rows + jnp.arange(rows, dtype=jnp.int32)
    s.valid = (query_pos < length)[:, None].astype(full)
    cosine, sine = tables(query_pos, head_dim)
    s.cosine, sine = cosine[0, :, 0], sine[0, :, 0]
    s.sine = jnp.concatenate([-sine[:, : head_dim // 2], sine[:, head_dim // 2 :]], 1)
    s.out_own = out_own
    del s.gains, s.x_first, s.x_second, s.other_lengths
    del s.side, s.side_near, s.far_piece, s.far_near
    s.end()

    head_columns = 2 * head_dim
    block_columns = 4 * head_dim
    quad_rows = jax.ShapeDtypeStruct((rows, block_columns), low)
    quad_sums = jax.ShapeDtypeStruct((rows, block_columns), full)
    gain_sum = jax.ShapeDtypeStruct((1, head_dim), full)
    project = vmem_call(
        project_body,
        [jax.ShapeDtypeStruct((rows, 2 * block_columns), full), quad_rows, quad_rows],
        name="project",
    )
    attend = vmem_call(attend_body, [quad_rows, quad_sums], scalars=1, name="attend")
    attend_back = vmem_call(
        attend_back_body,
        [quad_rows, quad_sums, quad_rows, gain_sum],
        scratch=[pltpu.VMEM((2 * rows, head_dim), full)] * 2
        + [pltpu.VMEM((rows, block_columns), low)],
        scalars=1,
        name="attend_back",
    )
    finish = vmem_call(finish_body, [quad_rows, quad_rows, gain_sum], name="finish")
    upward = [(i, i + 1) for i in range(0, count, 2)]
    downward = [(i + 1, i) for i in range(0, count, 2)]

    def project_call(i):
        return (
            project, s.normed, s.own_blocks[2 * i], s.came[i], s.own_blocks[2 * i + 1],
            s.came_other[i], s.cosine, s.sine, s.head_gains,
        )

    def attend_call(i):
        return (
            lambda query, own, before: attend(s.info, query, before, own),
            *s.projected[i][1:], s.earlier[i],
        )

    def give_up(i):
        s.earlier = s.earlier | {i: lax.ppermute(s.projected[i][2], "rep", upward)}

    def compute(projected, attended):
        calls = [project_call(i) for i in projected] + [attend_call(i) for i in attended]
        outs = in_order(calls)
        s.projected = s.projected | dict(zip(projected, outs))
        s.attended = s.attended | dict(zip(attended, outs[len(projected) :]))

    s.projected, s.earlier, s.attended = {}, {}, {}
    grad_y_second = to_sequence(s.cotangent_cuts[1], 1)
    came_last = three(jnp.concatenate(s.side_last, 0), jnp.concatenate(s.far_last, 0))
    out_near = near(s.out_own)
    other_last = across(came_last, CORE)
    compute([0], [])
    s.came = [*s.came, came_last]
    s.came_other = [*s.came_other, other_last]
    del s.side_last, s.far_last, s.cotangent_cuts
    s.end()

    give_up(0)
    s.out_other = [across(s.out_own, CORE)]
    compute([1], [])
    s.end()

    give_up(1)
    compute([2], [0])
    s.out_near = out_near
    s.grad_y_second = grad_y_second
    s.end()

    ffn_own = lax.all_gather(s.ffn_block, "shard", axis=0, tiled=True)
    s.out_far = far(*s.out_near)
    s.out_other = [*s.out_other, *(across(block, CORE) for block in s.out_near)]
    give_up(2)
    grad_y = jnp.concatenate(in_turn([s.grad_y_first, s.grad_y_second]), 0)
    s.grad_y = jnp.where(s.valid > 0, grad_y, jnp.zeros_like(grad_y))
    compute([3], [1])
    del s.ffn_block, s.grad_y_first, s.grad_y_second
    s.end()

    grad_y_near = near(s.grad_y)
    out_last = jnp.concatenate(s.out_far, 0)
    s.out_other = [*s.out_other, across(out_last, CORE)]
    s.out_mine = [s.out_own, *s.out_near, out_last]
    give_up(3)
    compute([], [2])
    del s.out_own, s.out_near, s.out_far
    s.end()

    compute([], [3])
    s.out_blocks = [part for pair in zip(s.out_mine, s.out_other) for part in pair]
    s.mixed = [s.attended[i][0] for i in range(4)]
    s.resid, s.mid = close_attention(s.x_low, s.mixed, s.out_blocks, s.mlp_gains)
    del s.out_mine, s.out_other
    s.end()

    s.mid_near = near(s.mid)
    s.grad_y_near = grad_y_near
    s.end()

    s.grad_y_far = far(*s.grad_y_near)
    s.mid_far = far(*s.mid_near)
    s.ffn_own = ffn_own
    s.end()

    s.mids = [s.mid, *s.mid_near, *s.mid_far]
    s.grads_y = [s.grad_y, *s.grad_y_near, *s.grad_y_far]
    s.ffn_other = across(s.ffn_own, CORE)
    units = s.ffn_own.shape[1] // 3
    s.hidden_own = hidden_units(s.mids, s.grads_y, s.ffn_own)
    del s.mid, s.mid_near, s.mid_far, s.grad_y_near, s.grad_y_far
    s.end()

    def gate_up_pairs():
        return [
            (hidden[i], weights, i - 1)
            for hidden, weights in ((s.hidden_own, s.ffn_own), (s.hidden_other, s.ffn_other))
            for i in (1, 2)
        ]

    def down_pairs():
        return [(s.hidden_own[0], s.ffn_own, 2), (s.hidden_other[0], s.ffn_other, 2)]

    def from_hidden_call(pairs, eighths):
        return (
            lambda first: from_hidden([(first, *pairs[0][1:]), *pairs[1:]], eighths),
            pairs[0][0],
        )

    def outer_call(lefts, rights, *added):
        return lambda first: row_outer(lefts, [[first, *rights[1:]]], 0, 8, *added)[0], rights[0]

    def send_near(sent):
        return across(sent[0], ACROSS_X), across(sent[1], ACROSS_Y)

    def send_far(came, rest, split):
        one_tail, two_head = rest
        return (
            across(rounded_sum(one_tail, split(came[1])[1]), ACROSS_X),
            across(rounded_sum(two_head, split(came[0])[1]), ACROSS_Y),
        )

    def total(came, came_far, own, split):
        head, tail = own
        full_sum = lambda *parts: sum(part.astype(full) for part in parts)
        return jnp.concatenate(
            [
                full_sum(head, split(came[0])[0], came_far[1]),
                full_sum(tail, split(came[1])[0], came_far[0]),
            ],
            0,
        )

    by_rows = lambda a: jnp.split(a, 2, 0)
    by_columns = lambda a: jnp.split(a, 2, 1)
    to_plane, rest_of_plane = (2, 6, 5, 7), (3, 4, 0, 1)

    s.hidden_other = hidden_units(s.mids, s.grads_y, s.ffn_other)
    (s.down_outer,) = in_order([outer_call(s.grads_y, s.hidden_other[:1])])
    s.end()

    s.down_came = across(s.down_outer, CORE)
    s.mid_sent = from_hidden(gate_up_pairs(), to_plane)
    del s.down_outer
    s.end()

    s.mid_came = send_near(s.mid_sent)
    s.down_mine, s.mid_rest, s.gate_up_outer = in_order(
        [
            outer_call(s.grads_y, s.hidden_own[:1], s.down_came),
            from_hidden_call(gate_up_pairs(), rest_of_plane),
            outer_call(s.mids, s.hidden_other[1:]),
        ]
    )
    del s.mid_sent, s.down_came
    s.end()

    down_total = lax.psum_scatter(s.down_mine, "shard", scatter_dimension=0, tiled=True)
    s.mid_came_far = send_far(s.mid_came, by_rows(s.mid_rest[0]), by_rows)
    s.gate_up_came = across(s.gate_up_outer, CORE)
    s.mlp_sent, s.mlp_rest = in_order(
        [
            from_hidden_call(down_pairs(), to_plane),
            from_hidden_call(down_pairs(), rest_of_plane),
        ]
    )
    del s.gate_up_outer, s.down_mine
    s.end()

    def back_call(i):
        raw, query, own_pair = s.projected[i]
        return (
            lambda query, *rest: attend_back(s.info, query, *rest),
            query, s.earlier[i], own_pair, s.attended[i][1], s.resid_low,
            *s.out_blocks[2 * i : 2 * i + 2], raw, s.cosine, s.sine, s.head_gains[:1],
        )

    def finish_call(i):
        return (
            finish, s.backs[i][0], s.backs[i][1], s.returned[i], s.projected[i][0],
            s.cosine, s.sine, s.head_gains[1:],
        )

    def give_back(*chips):
        s.returned = s.returned | {
            i: lax.ppermute(s.backs[i][2], "rep", downward) for i in chips
        }

    def odd_call(left, blocks, part=None):
        return lambda first: row_outer([first], [blocks], 0, 8, part=part)[0], left

    def head_call(left, blocks, came, part=None, places=(0, 1, 2, 3)):
        groups = [[blocks[1], blocks[3]], [blocks[2]], [blocks[0]]]
        at = [places[i] for i in (1, 3, 2, 0)]
        return lambda first: row_outer([first], groups, 0, 4, came, at, part), left

    def tail_call(left, blocks, came, part=None, places=(0, 1, 2, 3)):
        groups = [[blocks[2], blocks[3]], [blocks[1]], [blocks[0]]]
        at = [places[i] for i in (2, 3, 1, 0)]
        return lambda first: row_outer([first], groups, 4, 4, came, at, part), left

    s.mlp_came = send_near(s.mlp_sent)
    grad_mid = total(s.mid_came, s.mid_came_far, by_rows(s.mid_rest[1]), by_rows)
    inverse_mid = lax.rsqrt(jnp.mean(s.resid * s.resid, -1, keepdims=True) + EPS)
    mid_unit = s.resid * inverse_mid
    s.mlp_gain_part = jnp.sum(mid_unit * grad_mid, 0)
    s.grad_resid = s.grad_y.astype(full) + norm_back(
        mid_unit, inverse_mid, grad_mid * s.mlp_gains
    )
    s.resid_low = s.grad_resid.astype(low)
    s.resid_rolled = rolled(s.resid_low)
    s.returned = {}
    back, s.out_odd, s.gate_up_mine = in_order(
        [
            back_call(3),
            odd_call(s.resid_rolled, s.mixed, 1),
            outer_call(s.mids, s.hidden_own[1:], s.gate_up_came),
        ]
    )
    s.backs = {3: back}
    s.down_total = down_total
    del s.mid_came, s.mid_came_far, s.mid_rest, s.gate_up_came, s.hidden_own, s.hidden_other
    del s.mids, s.grads_y, s.ffn_own, s.ffn_other, s.mlp_sent
    s.end()

    gate_up_total = lax.psum_scatter(s.gate_up_mine, "shard", scatter_dimension=0, tiled=True)
    s.mlp_came_far = send_far(s.mlp_came, by_rows(s.mlp_rest[0]), by_rows)
    s.out_came = across(s.out_odd, CORE)
    give_back(3)
    back1, back2 = in_order([back_call(1), back_call(2)])
    s.backs = s.backs | {1: back1, 2: back2}
    del s.out_odd, s.gate_up_mine
    s.end()

    s.down_near = near(s.down_total)
    give_back(1, 2)
    mlp_out = total(s.mlp_came, s.mlp_came_far, by_rows(s.mlp_rest[1]), by_rows)
    s.output = (s.valid * (s.resid + mlp_out)).astype(low)
    s.out_head, s.out_tail, back, finished = in_order(
        [
            head_call(s.resid_rolled, s.mixed, s.out_came, 0),
            tail_call(s.resid_rolled, s.mixed, s.out_came, 0),
            back_call(0),
            finish_call(3),
        ]
    )
    s.backs = s.backs | {0: back}
    s.finished = {3: finished}
    del s.mlp_came, s.mlp_came_far, s.mlp_rest, s.out_came, s.resid
    s.end()

    s.out_near = send_near((s.out_head[0], s.out_tail[0]))
    s.down_far = far(*s.down_near)
    give_back(0)
    finished1, finished2 = in_order([finish_call(1), finish_call(2)])
    s.finished = s.finished | {1: finished1, 2: finished2}
    s.gate_up_total = gate_up_total
    s.end()

    def odd_half(half):
        return odd_call(s.normed, [s.finished[i][1] for i in range(4)], half)

    s.out_far = send_far(s.out_near, (s.out_tail[1], s.out_head[1]), by_columns)
    s.down_spread = jnp.concatenate([s.down_total, *s.down_near, *s.down_far], 0)
    s.down_spread_other = across(s.down_spread, CORE)
    (finished,) = in_order([finish_call(0)])
    s.finished = s.finished | {0: finished}
    (s.odd0,) = in_order([odd_half(0)])
    del s.down_total, s.down_near, s.down_far
    s.end()

    my_group = me.astype(jnp.int32)[None]

    def whole_call(widths, own, other, part=0):
        return lambda first: whole_columns(my_group, first, other, widths, part), own

    s.gate_up_near = near(s.gate_up_total)
    s.came0 = across(s.odd0, CORE)
    out_sum = total(s.out_near, s.out_far, (s.out_head[2], s.out_tail[2]), by_columns)
    s.out_chunks = jnp.split(out_sum.astype(low), shards, 0)
    s.out_ring = ring_sum_first(s.out_chunks)
    weights = [
        pair
        for i in range(4)
        for pair in (
            (s.own_blocks[2 * i], s.came[i]), (s.own_blocks[2 * i + 1], s.came_other[i])
        )
    ]
    blocks = [part for i in range(4) for part in s.finished[i][:2]]
    s.odd1, grad_in = in_order(
        [
            odd_half(1),
            (lambda first: back_to_rows([first, *blocks[1:]], weights), blocks[0]),
        ]
    )
    grad_in = rolled(grad_in)
    x_unit = s.x_low.astype(full) * s.inverse_in
    s.gain_parts = jnp.concatenate(
        [
            jnp.sum(x_unit * grad_in, 0),
            s.mlp_gain_part,
            sum(s.backs[i][3] for i in range(4))[0],
            sum(s.finished[i][2] for i in range(4))[0],
        ]
    )
    s.grad_tokens = (
        s.grad_resid + norm_back(x_unit, s.inverse_in, grad_in * s.attn_gains)
    ).astype(low)
    del s.odd0, s.out_near, s.out_far, s.out_head, s.out_tail, s.backs
    del s.own_blocks, s.came, s.came_other, s.grad_resid, s.x_low
    s.end()

    def halves_call(half, came):
        even = [s.finished[i][0] for i in range(4)]
        return [call(s.normed, even, came, half) for call in (head_call, tail_call)]

    output_sent = from_sequences_send(s.output)
    s.came1 = across(s.odd1, CORE)
    s.out_ring_last = around(rounded_sum(s.out_chunks[3], s.out_ring[0]), 1)
    s.head0, s.tail0 = in_order(halves_call(0, s.came0))
    del s.odd1, s.came0
    s.end()

    def qkv_chunks(came, came_far, head, tail):
        own = total(came, came_far, (head[2], tail[2]), by_columns)
        return jnp.split(own.astype(low), shards, 0)

    s.near0 = send_near((s.head0[0], s.tail0[0]))
    s.gain_came = across(s.gain_parts, CORE)
    s.head1, s.tail1, s.whole_down = in_order(
        [*halves_call(1, s.came1), whole_call((units,), s.down_spread, s.down_spread_other)]
    )
    s.out_total = rounded_sum(s.out_chunks[0], s.out_ring[1], s.out_ring_last)
    s.output_first = output_sent[0]
    del s.came1, s.down_spread, s.down_spread_other, s.output, s.finished
    del s.out_chunks, s.out_ring, s.out_ring_last
    s.end()

    s.far0 = send_far(s.near0, (s.tail0[1], s.head0[1]), by_columns)
    s.near1 = send_near((s.head1[0], s.tail1[0]))
    s.gain_parts = s.gain_parts + s.gain_came
    s.output_second = output_sent[1]
    s.end()

    s.chunks0 = qkv_chunks(s.near0, s.far0, s.head0, s.tail0)
    s.ring0 = ring_sum_first(s.chunks0)
    s.far1 = send_far(s.near1, (s.tail1[1], s.head1[1]), by_columns)
    s.gain_came = across(s.gain_parts, ACROSS_X)
    del s.near0, s.far0, s.head0, s.tail0
    s.end()

    s.last0 = around(rounded_sum(s.chunks0[3], s.ring0[0]), 1)
    s.chunks1 = qkv_chunks(s.near1, s.far1, s.head1, s.tail1)
    s.ring1 = ring_sum_first(s.chunks1)
    s.gate_up_far = far(*s.gate_up_near)
    s.gain_parts = s.gain_parts + s.gain_came
    del s.near1, s.far1, s.head1, s.tail1
    s.end()

    tokens_sent = from_sequences_send(s.grad_tokens)
    query_total = rounded_sum(s.chunks0[0], s.ring0[1], s.last0)
    s.total0 = jnp.concatenate([query_total, s.out_total], 1)
    s.spread0 = near(s.total0)
    s.last1 = around(rounded_sum(s.chunks1[3], s.ring1[0]), 1)
    s.gate_up_own = jnp.concatenate([s.gate_up_total, *s.gate_up_near, *s.gate_up_far], 0)
    s.gate_up_other = across(s.gate_up_own, CORE)
    s.gain_came = across(s.gain_parts, ACROSS_Y)
    del s.chunks0, s.ring0, s.last0, s.out_total, s.gate_up_near, s.gate_up_far, s.gate_up_total
    s.end()

    s.spread_far0 = far(*s.spread0)
    s.total1 = rounded_sum(s.chunks1[0], s.ring1[1], s.last1)
    s.spread1 = near(s.total1)
    s.gain_parts = s.gain_parts + s.gain_came
    s.gain_came = lax.ppermute(s.gain_parts, "shard", [(i, i ^ 1) for i in range(shards)])
    ((s.whole_gate,),) = in_order([whole_call((units,), s.gate_up_own, s.gate_up_other)])
    del s.chunks1, s.ring1, s.last1
    s.end()

    s.own0 = jnp.concatenate([s.total0, *s.spread0, *s.spread_far0], 0)
    s.other0 = across(s.own0, CORE)
    s.spread_far1 = far(*s.spread1)
    s.gain_parts = s.gain_parts + s.gain_came
    s.gain_came = lax.ppermute(s.gain_parts, "shard", [(i, i ^ 2) for i in range(shards)])
    ((s.whole_up,),) = in_order([whole_call((units,), s.gate_up_own, s.gate_up_other, 1)])
    s.tokens_first = tokens_sent[0]
    del s.total0, s.spread0, s.spread_far0, s.gate_up_own, s.gate_up_other
    s.end()

    s.own1 = jnp.concatenate([s.total1, *s.spread1, *s.spread_far1], 0)
    s.other1 = across(s.own1, CORE)
    (s.whole0,) = in_order([whole_call((head_columns, head_columns), s.own0, s.other0)])
    gain_sums = s.gain_parts + s.gain_came
    s.wide = lax.dynamic_slice_in_dim(
        gain_sums[: 2 * width].reshape(2, width), shard_at * piece, piece, 1
    )
    s.narrow = gain_sums[2 * width :]
    del s.own0, s.other0, s.total1, s.spread1, s.spread_far1
    s.end()

    ((whole_key, whole_value),) = in_order(
        [whole_call((head_dim, head_dim), s.own1, s.other1)]
    )
    return (
        jnp.stack(in_turn([s.output_first, s.output_second])),
        jnp.stack(in_turn([s.tokens_first, tokens_sent[1]])),
        s.wide[0],
        s.whole0[0],
        whole_key,
        whole_value,
        s.narrow[:head_dim],
        s.narrow[head_dim:],
        s.whole0[1],
        s.wide[1],
        s.whole_gate,
        s.whole_up,
        *s.whole_down,
    )


def solution(mesh):
    sizes = (mesh.shape["rep"], mesh.shape["shard"])
    return jax.shard_map(
        on_device_block if sizes == (8, 4) else on_device,
        mesh=mesh,
        in_specs=(
            P("rep", "shard", None),
            P("rep"),
            P("shard"),
            P("shard", None),
            P("shard", None),
            P("shard", None),
            P(),
            P(),
            P("shard", None),
            P("shard"),
            P("shard", None),
            P("shard", None),
            P("shard", None),
            P("rep", "shard", None),
        ),
        out_specs=(
            P("rep", "shard", None),
            P("rep", "shard", None),
            P("shard"),
            P("shard", None),
            P("shard", None),
            P("shard", None),
            P(),
            P(),
            P("shard", None),
            P("shard"),
            P("shard", None),
            P("shard", None),
            P("shard", None),
        ),
        check_vma=False,
    )
```

```python
import jax
import jax.numpy as jnp
from jax import lax
from jax.experimental import pallas as pl
from jax.experimental.pallas import tpu as pltpu
from jax.sharding import PartitionSpec as P

WINDOW = 512


EPS = 1e-06
ROPE_BASE = 1000000.0
NEG = -1e30


def passed_along(x, axis, by):
    devices = lax.axis_size(axis)
    pairs = [(i, i + by) for i in range(devices) if 0 <= i + by < devices]
    return lax.ppermute(x, axis, pairs)


def tables(positions, head_dim):
    half = head_dim // 2
    freq = ROPE_BASE ** (-jnp.arange(half, dtype=jnp.float32) * 2.0 / head_dim)
    angle = positions.astype(jnp.float32)[:, None] * freq[None, :]
    angle = jnp.concatenate([angle, angle], -1)
    return (jnp.cos(angle)[None, :, None, :], jnp.sin(angle)[None, :, None, :])


def rotated_rows(value_rows):
    half = value_rows.shape[-1] // 2
    return jnp.concatenate([-value_rows[..., half:], value_rows[..., :half]], -1)


def head_norm(raw, gain):
    inverse = lax.rsqrt(jnp.mean(raw * raw, -1, keepdims=True) + EPS)
    unit = raw * inverse
    return (unit, inverse, unit * gain)


def norm_back(unit, inverse, grad_unit):
    return inverse * (grad_unit - unit * jnp.mean(grad_unit * unit, -1, keepdims=True))


def head_norm_back(unit, inverse, grad_normed, gain):
    grad_raw = norm_back(unit, inverse, grad_normed * gain)
    return (grad_raw, jnp.sum(unit * grad_normed, axis=(0, 1, 2)))


def scores(query_rows, keys, allowed, scale):
    raw = (
        jnp.einsum("sqhgd,skhd->shgqk", query_rows, keys, preferred_element_type=jnp.float32)
        * scale
    )
    return jnp.where(allowed[:, None, None], raw, NEG)


def outer(left, right):
    return jnp.einsum("rc,rf->cf", left, right, preferred_element_type=jnp.float32)


def on_device(
    tokens,
    lengths,
    attn_gain,
    w_query,
    key_matrix,
    value_matrix,
    query_gain,
    key_gain,
    w_out,
    mlp_gain,
    w_gate,
    w_up,
    w_down,
    cotangent,
):
    seq_count, piece, width = tokens.shape
    head_dim = query_gain.shape[0]
    heads_q = w_query.shape[1] // head_dim
    heads_kv = key_matrix.shape[1] // head_dim
    groups = heads_q // heads_kv
    rows = seq_count * piece
    scale = head_dim ** (-0.5)
    reach = (WINDOW + piece - 2) // piece
    owned = width // lax.axis_size("shard")
    shard_at = lax.axis_index("shard")
    query_pos = shard_at * piece + jnp.arange(piece, dtype=jnp.int32)
    key_pos = (shard_at - reach) * piece + jnp.arange((reach + 1) * piece, dtype=jnp.int32)
    near = (
        (key_pos[None, :] <= query_pos[:, None])
        & (query_pos[:, None] - key_pos[None, :] < WINDOW)
        & (key_pos[None, :] >= 0)
    )
    live = (key_pos[None, None, :] < lengths[:, None, None]) | (
        key_pos[None, :] == query_pos[:, None]
    )[None]
    allowed = near[None] & live
    valid = (query_pos[None, :] < lengths[:, None]).astype(jnp.float32).reshape(rows, 1)
    cosine_table, sine_table = tables(query_pos, head_dim)
    x_rows = tokens.astype(jnp.float32).reshape(rows, width)
    inverse_in = lax.rsqrt(jnp.mean(x_rows * x_rows, -1, keepdims=True) + EPS)
    x_unit = x_rows * inverse_in
    gain_piece = lax.all_gather(attn_gain, "shard", axis=0, tiled=True)
    query_piece = lax.all_gather(w_query, "shard", axis=0, tiled=True)
    key_piece = lax.all_gather(key_matrix, "shard", axis=0, tiled=True)
    value_piece = lax.all_gather(value_matrix, "shard", axis=0, tiled=True)
    normed_piece = (x_unit * gain_piece.astype(jnp.float32)).astype(jnp.bfloat16)
    acc_q = jnp.dot(normed_piece, query_piece, preferred_element_type=jnp.float32)
    acc_k = jnp.dot(normed_piece, key_piece, preferred_element_type=jnp.float32)
    acc_v = jnp.dot(normed_piece, value_piece, preferred_element_type=jnp.float32)
    normalized_rows = normed_piece
    gains = gain_piece.astype(jnp.float32)
    attn_in = normalized_rows
    attn_gains = gains
    query_unit, query_inverse, query_rows_normalized = head_norm(
        acc_q.reshape(seq_count, piece, heads_q, head_dim), query_gain.astype(jnp.float32)
    )
    key_unit, key_inverse, key_normed = head_norm(
        acc_k.reshape(seq_count, piece, heads_kv, head_dim), key_gain.astype(jnp.float32)
    )
    query_rows = (
        (query_rows_normalized * cosine_table + rotated_rows(query_rows_normalized) * sine_table)
        .astype(jnp.bfloat16)
        .reshape(seq_count, piece, heads_kv, groups, head_dim)
    )
    keys_own = (key_normed * cosine_table + rotated_rows(key_normed) * sine_table).astype(
        jnp.bfloat16
    )
    values_own = acc_v.reshape(seq_count, piece, heads_kv, head_dim).astype(jnp.bfloat16)
    own_pair = jnp.stack([keys_own, values_own])
    parts = []
    for fetch_back in range(reach, 0, -1):
        parts.append(passed_along(own_pair, "shard", fetch_back))
    parts.append(own_pair)
    near_pair = jnp.concatenate(parts, 2)
    score = scores(query_rows, near_pair[0], allowed, scale)
    top = jnp.max(score, -1, keepdims=True)
    expo = jnp.exp(score - top)
    total = jnp.sum(expo, -1, keepdims=True)
    prob = expo / total
    log_total = top + jnp.log(total)
    mixed = jnp.einsum(
        "shgqk,skhd->sqhgd",
        prob.astype(jnp.bfloat16),
        near_pair[1],
        preferred_element_type=jnp.float32,
    )
    mixed_rows = mixed.reshape(rows, heads_q * head_dim).astype(jnp.bfloat16)
    resid = x_rows + jnp.einsum(
        "rf,nf->rn",
        mixed_rows,
        lax.all_gather(w_out, "shard", axis=0, tiled=True),
        preferred_element_type=jnp.float32,
    )
    inverse_mid = lax.rsqrt(jnp.mean(resid * resid, -1, keepdims=True) + EPS)
    mid_unit = resid * inverse_mid
    gain_piece = lax.all_gather(mlp_gain, "shard", axis=0, tiled=True)
    gate_piece = lax.all_gather(w_gate, "shard", axis=0, tiled=True)
    up_piece = lax.all_gather(w_up, "shard", axis=0, tiled=True)
    normed_piece = (mid_unit * gain_piece.astype(jnp.float32)).astype(jnp.bfloat16)
    acc_gate = jnp.dot(normed_piece, gate_piece, preferred_element_type=jnp.float32)
    acc_up = jnp.dot(normed_piece, up_piece, preferred_element_type=jnp.float32)
    normalized_rows = normed_piece
    gains = gain_piece.astype(jnp.float32)
    mlp_in = normalized_rows
    sigma = jax.nn.sigmoid(acc_gate)
    swish = acc_gate * sigma
    act = (swish * acc_up).astype(jnp.bfloat16)
    mlp_out = jnp.einsum(
        "rf,nf->rn",
        act,
        lax.all_gather(w_down, "shard", axis=0, tiled=True),
        preferred_element_type=jnp.float32,
    )
    output = (valid * (resid + mlp_out)).astype(jnp.bfloat16).reshape(seq_count, piece, width)
    grad_y = cotangent.astype(jnp.float32).reshape(rows, width) * valid
    grad_y_low = grad_y.astype(jnp.bfloat16)
    grad_act = jnp.dot(
        grad_y_low,
        lax.all_gather(w_down, "shard", axis=0, tiled=True),
        preferred_element_type=jnp.float32,
    )
    grad_gate = (grad_act * acc_up * sigma * (1.0 + acc_gate * (1.0 - sigma))).astype(jnp.bfloat16)
    grad_up = (grad_act * swish).astype(jnp.bfloat16)
    gate_piece, up_piece = lax.all_gather((w_gate, w_up), "shard", axis=0, tiled=True)
    grad_mid = jnp.einsum(
        "rf,nf->rn", grad_gate, gate_piece, preferred_element_type=jnp.float32
    ) + jnp.einsum("rf,nf->rn", grad_up, up_piece, preferred_element_type=jnp.float32)
    grad_resid = grad_y + norm_back(mid_unit, inverse_mid, grad_mid * gains)
    mlp_gain_part = jnp.sum(mid_unit * grad_mid, 0)
    normalized_rows = mlp_in
    mlp_grads = jax.tree.map(
        lambda part: lax.psum_scatter(
            part.astype(jnp.bfloat16), "shard", scatter_dimension=0, tiled=True
        ).astype(jnp.float32),
        (
            outer(normalized_rows, grad_gate),
            outer(normalized_rows, grad_up),
            outer(grad_y_low, act),
        ),
    )
    resid_low = grad_resid.astype(jnp.bfloat16)
    grad_mixed = jnp.dot(
        resid_low,
        lax.all_gather(w_out, "shard", axis=0, tiled=True),
        preferred_element_type=jnp.float32,
    )
    grad_mixed = grad_mixed.astype(jnp.bfloat16).reshape(
        seq_count, piece, heads_kv, groups, head_dim
    )
    prob_again = jnp.exp(scores(query_rows, near_pair[0], allowed, scale) - log_total)
    grad_prob = jnp.einsum(
        "sqhgd,skhd->shgqk", grad_mixed, near_pair[1], preferred_element_type=jnp.float32
    )
    grad_values = jnp.einsum(
        "shgqk,sqhgd->skhd",
        prob_again.astype(jnp.bfloat16),
        grad_mixed,
        preferred_element_type=jnp.float32,
    )
    grad_score = (
        prob_again * (grad_prob - jnp.sum(prob_again * grad_prob, -1, keepdims=True))
    ).astype(jnp.bfloat16)
    grad_queries = (
        jnp.einsum(
            "shgqk,skhd->sqhgd", grad_score, near_pair[0], preferred_element_type=jnp.float32
        )
        * scale
    )
    grad_keys = (
        jnp.einsum("shgqk,sqhgd->skhd", grad_score, query_rows, preferred_element_type=jnp.float32)
        * scale
    )
    grad_pair = jnp.stack([grad_keys, grad_values])
    own_grad = grad_pair[:, :, reach * piece :]
    for back in range(1, reach + 1):
        lower = (reach - back) * piece
        own_grad = own_grad + passed_along(grad_pair[:, :, lower : lower + piece], "shard", -back)
    grad_query_post = grad_queries.reshape(seq_count, piece, heads_q, head_dim)
    grad_query_normed = grad_query_post * cosine_table - rotated_rows(grad_query_post * sine_table)
    grad_key_normed = own_grad[0] * cosine_table - rotated_rows(own_grad[0] * sine_table)
    grad_query_raw, query_gain_grad = head_norm_back(
        query_unit, query_inverse, grad_query_normed, query_gain.astype(jnp.float32)
    )
    grad_key_raw, key_gain_grad = head_norm_back(
        key_unit, key_inverse, grad_key_normed, key_gain.astype(jnp.float32)
    )
    grad_query_low = grad_query_raw.reshape(rows, heads_q * head_dim).astype(jnp.bfloat16)
    grad_key_low = grad_key_raw.reshape(rows, heads_kv * head_dim).astype(jnp.bfloat16)
    grad_value_low = own_grad[1].reshape(rows, heads_kv * head_dim).astype(jnp.bfloat16)
    query_piece, key_piece, value_piece = lax.all_gather(
        (w_query, key_matrix, value_matrix), "shard", axis=0, tiled=True
    )
    grad_in = (
        jnp.einsum("rf,nf->rn", grad_query_low, query_piece, preferred_element_type=jnp.float32)
        + jnp.einsum("rf,nf->rn", grad_key_low, key_piece, preferred_element_type=jnp.float32)
        + jnp.einsum("rf,nf->rn", grad_value_low, value_piece, preferred_element_type=jnp.float32)
    )
    grad_tokens = (
        (grad_resid + norm_back(x_unit, inverse_in, grad_in * attn_gains))
        .astype(jnp.bfloat16)
        .reshape(seq_count, piece, width)
    )
    attn_gain_part = jnp.sum(x_unit * grad_in, 0)
    normalized_rows = attn_in
    attn_grads = jax.tree.map(
        lambda part: lax.psum_scatter(
            part.astype(jnp.bfloat16), "shard", scatter_dimension=0, tiled=True
        ).astype(jnp.float32),
        (
            outer(normalized_rows, grad_query_low),
            outer(normalized_rows, grad_key_low),
            outer(normalized_rows, grad_value_low),
            outer(resid_low, mixed_rows),
        ),
    )
    head_grads = lax.psum(
        (query_gain_grad, key_gain_grad, attn_gain_part, mlp_gain_part), ("rep", "shard")
    )
    attn_gain_total = lax.dynamic_slice_in_dim(head_grads[2], shard_at * owned, owned, 0)
    mlp_gain_total = lax.dynamic_slice_in_dim(head_grads[3], shard_at * owned, owned, 0)
    summed = (
        lax.psum(attn_grads[0].astype(jnp.bfloat16), "rep").astype(jnp.float32),
        lax.psum(attn_grads[1].astype(jnp.bfloat16), "rep").astype(jnp.float32),
        lax.psum(attn_grads[2].astype(jnp.bfloat16), "rep").astype(jnp.float32),
        lax.psum(attn_grads[3].astype(jnp.bfloat16), "rep").astype(jnp.float32),
        lax.psum(mlp_grads[0].astype(jnp.bfloat16), "rep").astype(jnp.float32),
        lax.psum(mlp_grads[1].astype(jnp.bfloat16), "rep").astype(jnp.float32),
        lax.psum(mlp_grads[2].astype(jnp.bfloat16), "rep").astype(jnp.float32),
    )
    attn_grads = summed[:4]
    mlp_grads = summed[4:]
    return (
        output,
        grad_tokens,
        attn_gain_total,
        attn_grads[0],
        attn_grads[1],
        attn_grads[2],
        head_grads[0],
        head_grads[1],
        attn_grads[3],
        mlp_gain_total,
        mlp_grads[0],
        mlp_grads[1],
        mlp_grads[2],
    )


CORE, ACROSS_X, ACROSS_Y = 1, 2, 4
VMEM_BYTES = 56 * 2**20
FREE = pl.CostEstimate(flops=1, bytes_accessed=1, transcendentals=0)


def across(x, mask):
    count = lax.axis_size("rep")
    return lax.ppermute(x, "rep", [(i, i ^ mask) for i in range(count)])


def around(x, by):
    count = lax.axis_size("shard")
    return lax.ppermute(x, "shard", [(i, (i + by) % count) for i in range(count)])


class Stage(dict):
    __getattr__ = dict.__getitem__
    __setattr__ = dict.__setitem__
    __delattr__ = dict.__delitem__

    def end(self):
        self.update(lax.optimization_barrier(dict(self)))


def in_order(calls):
    outs = []
    for call, first, *rest in calls:
        if outs:
            last = outs[-1][0] if isinstance(outs[-1], (list, tuple)) else outs[-1]
            first = lax.optimization_barrier((first, last))[0]
        outs.append(call(first, *rest))
    return outs


def ring_sum_first(chunks):
    return around(chunks[2], 1), around(chunks[1], -1)


def near(piece):
    return across(piece, ACROSS_X), across(piece, ACROSS_Y)


def far(from_x, from_y):
    half = from_x.shape[0] // 2
    return across(from_x[:half], ACROSS_Y), across(from_y[half:], ACROSS_X)


def rounded_sum(*parts):
    return sum(part.astype(jnp.float32) for part in parts).astype(jnp.bfloat16)


def sequence_pairs(turn):
    groups, shards = lax.axis_size("rep"), lax.axis_size("shard")
    pairs = []
    for group in range(groups):
        chip, core = divmod(group, 2)
        for at in range(shards):
            to_group, to_shard = 2 * chip + at // 2, 2 * core + (turn ^ (at & 1))
            pairs.append((group * shards + at, to_group * shards + to_shard))
    return pairs


def rolled(x):
    count, at = lax.axis_size("shard"), lax.axis_index("shard")
    width = x.shape[1] // count
    return jnp.concatenate(
        [lax.dynamic_slice_in_dim(x, ((at - i) % count) * width, width, 1) for i in range(count)],
        1,
    )


def sequence_cuts(x):
    odd = lax.axis_index("shard") & 1
    return [lax.dynamic_index_in_dim(x, turn ^ odd, 0, keepdims=False) for turn in range(2)]


def to_sequence(cut, turn):
    return lax.ppermute(cut, ("rep", "shard"), sequence_pairs(turn))


def from_sequences_send(x):
    odd = lax.axis_index("shard") & 1
    x = x.reshape(2, x.shape[0] // 2, x.shape[1])
    return [
        lax.ppermute(
            lax.dynamic_index_in_dim(x, turn ^ odd, 0, keepdims=False),
            ("rep", "shard"),
            [(to, at) for at, to in sequence_pairs(turn)],
        )
        for turn in range(2)
    ]


def in_turn(came):
    even = lax.axis_index("shard") & 1 == 0
    return [jnp.where(even, came[0], came[1]), jnp.where(even, came[1], came[0])]


def column_block(weights, at):
    cuts = [w.shape[1] // 8 for w in weights]
    return jnp.concatenate(
        [lax.dynamic_slice_in_dim(w, at * cut, cut, 1) for w, cut in zip(weights, cuts)], 1
    )


def whole_columns(me, own, other, widths, part=0):
    rows, columns = own.shape[0] // 4, sum(widths)

    def body(me_ref, own_ref, other_ref, *outs):
        def put(block):
            start = 0
            for out, width in zip(outs, widths):
                out[...] = block[:, start : start + width].astype(jnp.float32)
                start += width

        mine = (me_ref[0] ^ pl.program_id(0)) & 1 == 0
        pl.when(mine)(lambda: put(own_ref))
        pl.when(jnp.logical_not(mine))(lambda: put(other_ref))

    spec = pl.BlockSpec((rows, columns), lambda i, at: ((at[0] ^ i) >> 1, part))
    return pl.pallas_call(
        body,
        grid_spec=pltpu.PrefetchScalarGridSpec(
            num_scalar_prefetch=1,
            grid=(8,),
            in_specs=[spec, spec],
            out_specs=[pl.BlockSpec((rows, w), lambda i, at: (0, i)) for w in widths],
        ),
        out_shape=[jax.ShapeDtypeStruct((rows, 8 * w), jnp.float32) for w in widths],
        compiler_params=pltpu.CompilerParams(vmem_limit_bytes=VMEM_BYTES),
        cost_estimate=FREE,
        name="whole_columns",
    )(me, own, other)


def turned(x):
    return pltpu.roll(x, x.shape[-1] // 2, x.ndim - 1)


def nt(left, right):
    return lax.dot_general(
        left, right, (((1,), (1,)), ((), ())), preferred_element_type=jnp.float32
    )


def tn(left, right):
    return lax.dot_general(
        left, right, (((0,), (0,)), ((), ())), preferred_element_type=jnp.float32
    )


def unit_of(raw):
    inverse = lax.rsqrt(jnp.mean(raw * raw, -1, keepdims=True) + EPS)
    return raw * inverse, inverse


def project_body(
    normed, own0, came0, own1, came1, cosine, sine, gains, raw, query, key_value
):
    step = own0.shape[0]
    dim = cosine.shape[1]
    for block, (own, came) in enumerate(((own0, came0), (own1, came1))):
        at = block * 4 * dim
        raw[:, at : at + 4 * dim] = jnp.dot(
            normed[:, :step], own[...], preferred_element_type=jnp.float32
        ) + jnp.dot(normed[:, step:], came[...], preferred_element_type=jnp.float32)
        for i in range(3):
            unit, _ = unit_of(raw[:, at + i * dim : at + (i + 1) * dim])
            head = unit * gains[i // 2 : i // 2 + 1, :]
            head = (head * cosine[...] + turned(head) * sine[...]).astype(jnp.bfloat16)
            if i < 2:
                query[:, (2 * block + i) * dim : (2 * block + i + 1) * dim] = head
            else:
                key_value[:, 2 * block * dim : (2 * block + 1) * dim] = head
        key_value[:, (2 * block + 1) * dim : (2 * block + 2) * dim] = raw[
            :, at + 3 * dim : at + 4 * dim
        ].astype(jnp.bfloat16)


def window_mask(info, part, rows, columns):
    half = columns - rows
    row = lax.broadcasted_iota(jnp.int32, (rows, columns), 0)
    column = lax.broadcasted_iota(jnp.int32, (rows, columns), 1)
    gap = column - row - half
    slot = column + ((info[0] - 1) * half + part * rows)
    allowed = (gap <= 0) & (gap > -half) & (slot >= 0) & ((slot < info[1]) | (gap == 0))
    mask = jnp.where(allowed, 0.0, NEG)
    return jnp.concatenate([mask, mask], 0)


def two_heads(ref, at, block, dim):
    return jnp.concatenate(
        [ref[at, h * dim : (h + 1) * dim] for h in (2 * block, 2 * block + 1)], 0
    )


def key_columns(block, dim):
    key = slice(2 * block * dim, (2 * block + 1) * dim)
    value = slice((2 * block + 1) * dim, (2 * block + 2) * dim)
    return key, value


def seen_pair(before, own, part, block, dim):
    here, there = key_columns(block, dim), key_columns(1 - block, dim)
    rows = own.shape[0] // 2
    if part == 0:
        return [
            jnp.concatenate([before[:, t], own[:rows, h]], 0) for h, t in zip(here, there)
        ]
    return [jnp.concatenate([before[rows:, t], own[:, h]], 0) for h, t in zip(here, there)]


def attend_body(info, query, before, own, mixed, log_total):
    dim = own.shape[1] // 4
    rows = query.shape[0] // 2
    for part in range(2):
        at = slice(part * rows, (part + 1) * rows)
        mask = window_mask(info, part, rows, 3 * rows)
        for block in range(2):
            keys, values = seen_pair(before, own, part, block, dim)
            score = nt(two_heads(query, at, block, dim), keys) * dim**-0.5 + mask
            top = jnp.max(score, -1, keepdims=True)
            expo = jnp.exp(score - top)
            total = jnp.sum(expo, -1, keepdims=True)
            prob = (expo * (1.0 / total)).astype(jnp.bfloat16)
            out = jnp.dot(prob, values, preferred_element_type=jnp.float32).astype(jnp.bfloat16)
            log = jnp.broadcast_to(top + jnp.log(total), (2 * rows, dim))
            for i in range(2):
                on = slice((2 * block + i) * dim, (2 * block + i + 1) * dim)
                mixed[at, on] = out[i * rows : (i + 1) * rows]
                log_total[at, on] = log[i * rows : (i + 1) * rows]


def attend_back_body(
    info, query, before, own, log_total, grad_resid, weight0, weight1, raw, cosine, sine, gain,
    grad_query, grad_own, grad_before, gain_part, grad_keys, grad_values, grad_mixed,
):
    dim = own.shape[1] // 4
    rows = query.shape[0] // 2
    scale = dim**-0.5
    gain_total = jnp.zeros((1, dim), jnp.float32)
    masks = [window_mask(info, part, rows, 3 * rows) for part in range(2)]
    for block, weight in enumerate((weight0, weight1)):
        on = slice(2 * block * dim, 2 * (block + 1) * dim)
        grad_mixed[:, on] = jnp.dot(
            grad_resid[...], weight[...], preferred_element_type=jnp.float32
        ).astype(jnp.bfloat16)
        grad_keys[...] = jnp.zeros_like(grad_keys)
        grad_values[...] = jnp.zeros_like(grad_values)
        for part in range(2):
            keys, values = seen_pair(before, own, part, block, dim)
            at = slice(part * rows, (part + 1) * rows)
            seen = slice(part * rows, part * rows + 3 * rows)
            queries = two_heads(query, at, block, dim)
            grads = two_heads(grad_mixed, at, block, dim)
            log = two_heads(log_total, at, block, dim)[:, :1]
            prob = jnp.exp(nt(queries, keys) * scale + masks[part] - log)
            grad_prob = nt(grads, values)
            inner = jnp.sum(prob * grad_prob, -1, keepdims=True)
            grad_score = (prob * (grad_prob - inner)).astype(jnp.bfloat16)
            grad_values[seen, :] += tn(prob.astype(jnp.bfloat16), grads)
            grad_keys[seen, :] += tn(grad_score, queries) * scale
            both = jnp.dot(grad_score, keys, preferred_element_type=jnp.float32) * scale
            for i in range(2):
                head = 2 * block + i
                back = both[i * rows : (i + 1) * rows]
                back = back * cosine[at, :] - turned(back) * sine[at, :]
                there = (2 * head - head % 2) * dim
                unit, inverse = unit_of(raw[at, there : there + dim])
                gain_total += jnp.sum(unit * back, 0, keepdims=True)
                back = back * gain[...]
                back = inverse * (back - unit * jnp.mean(back * unit, -1, keepdims=True))
                grad_query[at, head * dim : (head + 1) * dim] = back.astype(jnp.bfloat16)
        for grad, here, there in zip(
            (grad_keys, grad_values), key_columns(block, dim), key_columns(1 - block, dim)
        ):
            grad_before[:, there] = grad[: 2 * rows, :].astype(jnp.bfloat16)
            grad_own[:, here] = grad[2 * rows :, :]
    gain_part[...] = gain_total


def finish_body(grad_query, grad_own, came, raw, cosine, sine, gain, even, odd, gain_part):
    dim = cosine.shape[1]
    total = jnp.zeros((1, dim), jnp.float32)
    for block, out in enumerate((even, odd)):
        key, value = key_columns(block, dim)
        back = grad_own[:, key] + came[:, key].astype(jnp.float32)
        back = back * cosine[...] - turned(back) * sine[...]
        unit, inverse = unit_of(raw[:, (4 * block + 2) * dim : (4 * block + 3) * dim])
        total += jnp.sum(unit * back, 0, keepdims=True)
        back = back * gain[...]
        back = inverse * (back - unit * jnp.mean(back * unit, -1, keepdims=True))
        out[:, : 2 * dim] = grad_query[:, 2 * block * dim : (2 * block + 2) * dim]
        out[:, 2 * dim : 3 * dim] = back.astype(jnp.bfloat16)
        grad_value = grad_own[:, value] + came[:, value].astype(jnp.float32)
        out[:, 3 * dim :] = grad_value.astype(jnp.bfloat16)
    gain_part[...] = total


def vmem_call(body, outs, scratch=(), scalars=0, name=None):
    def call(*args):
        in_specs = [
            pl.BlockSpec(memory_space=pltpu.SMEM if i < scalars else pltpu.VMEM)
            for i in range(len(args))
        ]
        return pl.pallas_call(
            body,
            grid=(1,),
            out_shape=outs,
            in_specs=in_specs,
            out_specs=jax.tree.map(lambda _: pl.BlockSpec(memory_space=pltpu.VMEM), outs),
            scratch_shapes=scratch,
            compiler_params=pltpu.CompilerParams(vmem_limit_bytes=VMEM_BYTES),
        cost_estimate=FREE,
            name=name,
        )(*args)

    return call


def hidden_units(mids, grads_y, weights):
    width, units = weights.shape[0], weights.shape[1] // 3
    count = len(mids)
    heights = [m.shape[0] for m in mids]
    rows, cut = sum(heights), units // 3

    def body(*refs):
        gate_w, up_w, w_down, act, grad_gate, grad_up = refs[2 * count :]
        start = 0
        for mid, grad_y in zip(refs[:count], refs[count : 2 * count]):
            at = slice(start, start + mid.shape[0])
            start += mid.shape[0]
            gate = jnp.dot(mid[...], gate_w[...], preferred_element_type=jnp.float32)
            up = jnp.dot(mid[...], up_w[...], preferred_element_type=jnp.float32)
            grad_act = jnp.dot(grad_y[...], w_down[...], preferred_element_type=jnp.float32)
            sigma = jax.nn.sigmoid(gate)
            swish = gate * sigma
            act[at, :] = (swish * up).astype(jnp.bfloat16)
            slope = grad_act * up * sigma * (1.0 + gate * (1.0 - sigma))
            grad_gate[at, :] = slope.astype(jnp.bfloat16)
            grad_up[at, :] = (grad_act * swish).astype(jnp.bfloat16)

    row_specs = [
        pl.BlockSpec((h, width), lambda j: (0, 0), pipeline_mode=pl.Buffered(1)) for h in heights
    ]
    return pl.pallas_call(
        body,
        grid=(3,),
        out_shape=[jax.ShapeDtypeStruct((rows, units), jnp.bfloat16)] * 3,
        in_specs=[
            *row_specs,
            *row_specs,
            pl.BlockSpec((width, cut), lambda j: (0, j)),
            pl.BlockSpec((width, cut), lambda j: (0, j + 3)),
            pl.BlockSpec((width, cut), lambda j: (0, j + 6)),
        ],
        out_specs=[pl.BlockSpec((rows, cut), lambda j: (0, j))] * 3,
        compiler_params=pltpu.CompilerParams(vmem_limit_bytes=VMEM_BYTES),
        cost_estimate=FREE,
        name="hidden_units",
    )(*mids, *grads_y, weights, weights, weights)


def from_hidden(pairs, eighths):
    count, parts = len(pairs), len(eighths)
    rows, units = pairs[0][0].shape[0] // 8, pairs[0][0].shape[1]
    width = pairs[0][1].shape[0]
    cut = width // 4

    def body(*refs):
        ins, outs = refs[: -(parts // 2)], refs[-(parts // 2) :]
        total = 0.0
        for i in range(count):
            part = ins[i * (parts + 1) : (i + 1) * (parts + 1)]
            left = jnp.concatenate([p[...] for p in part[:-1]], 0)
            total = total + nt(left, part[-1][...])
        for i, out in enumerate(outs):
            out[...] = total[2 * i * rows : 2 * (i + 1) * rows].astype(jnp.bfloat16)

    specs, args = [], []
    for left, right, at in pairs:
        specs += [pl.BlockSpec((rows, units), lambda j, e=e: (e, 0)) for e in eighths]
        specs.append(pl.BlockSpec((cut, units), lambda j, at=at: (j, at)))
        args += [left] * parts + [right]
    return pl.pallas_call(
        body,
        grid=(4,),
        out_shape=[jax.ShapeDtypeStruct((2 * rows, width), jnp.bfloat16)] * (parts // 2),
        in_specs=specs,
        out_specs=[pl.BlockSpec((2 * rows, cut), lambda j: (0, j))] * (parts // 2),
        compiler_params=pltpu.CompilerParams(vmem_limit_bytes=VMEM_BYTES),
        cost_estimate=FREE,
        name="from_hidden",
    )(*args)


def row_outer(lefts, groups, first, tiles, added=None, places=None, part=None):
    rights = [right for group in groups for right in group]
    places = range(len(rights)) if places is None else places
    added = [] if added is None else [added] * len(rights)
    width = lefts[0].shape[1]
    tile = width // 8
    count = len(lefts)
    rows = sum(left.shape[0] for left in lefts)
    wide = rights[0].shape[1] // (1 if part is None else 2)
    columns = [wide * len(group) for group in groups]

    def body(*refs):
        left_refs = refs[:count]
        right_refs = refs[count : count + len(rights)]
        add_refs = refs[count + len(rights) : count + len(rights) + len(added)]
        outs = refs[count + len(rights) + len(added) :]
        place = 0
        for i, group in enumerate(groups):
            column = 0
            for _ in group:
                on = slice(column, column + wide)
                total, start = 0.0, 0
                for left in left_refs:
                    stop = start + left.shape[0]
                    total = total + tn(left[...], right_refs[place][start:stop, :])
                    start = stop
                if added:
                    total = total + add_refs[place][...].astype(jnp.float32)
                outs[i][:, on] = total.astype(jnp.bfloat16)
                place += 1
                column += wide

    return pl.pallas_call(
        body,
        grid=(tiles,),
        out_shape=[jax.ShapeDtypeStruct((tiles * tile, c), jnp.bfloat16) for c in columns],
        in_specs=[
            *(pl.BlockSpec((left.shape[0], tile), lambda j: (0, j + first)) for left in lefts),
            *(
                pl.BlockSpec(
                    (right.shape[0], wide), lambda j: (0, part or 0), pipeline_mode=pl.Buffered(1)
                )
                for right in rights
            ),
            *(
                pl.BlockSpec((tile, wide), lambda j, at=at: (j + first, at))
                for at in places[: len(added)]
            ),
        ],
        out_specs=[pl.BlockSpec((tile, c), lambda j: (j, 0)) for c in columns],
        compiler_params=pltpu.CompilerParams(vmem_limit_bytes=VMEM_BYTES),
        cost_estimate=pl.CostEstimate(
            flops=2 * rows * tiles * tile * sum(columns),
            bytes_accessed=2 * rows * (width + sum(columns)),
            transcendentals=0,
        ),
        name="row_outer",
    )(*lefts, *rights, *added)


def close_body(x, *refs):
    mixed, weights = refs[:4], refs[4:12]
    gains, resid, mid = refs[12:]
    at = pl.program_id(0)
    step = x.shape[1]
    columns = weights[0].shape[1]
    total = x[...].astype(jnp.float32)
    for i in range(8):
        part = mixed[i // 2][:, (i % 2) * columns : (i % 2 + 1) * columns]
        total = total + nt(part, weights[i][...])
    resid[:, pl.ds(pl.multiple_of(at * step, step), step)] = total

    @pl.when(at == 3)
    def _():
        unit, _ = unit_of(resid[...])
        mid[...] = (unit * gains[...]).astype(jnp.bfloat16)


def close_attention(x, mixed, weights, gains):
    rows, width = x.shape
    step = width // 4
    whole = lambda a: pl.BlockSpec(a.shape, lambda j: (0, 0))
    return pl.pallas_call(
        close_body,
        grid=(4,),
        out_shape=[
            jax.ShapeDtypeStruct((rows, width), jnp.float32),
            jax.ShapeDtypeStruct((rows, width), jnp.bfloat16),
        ],
        in_specs=[
            pl.BlockSpec((rows, step), lambda j: (0, j)),
            *(whole(m) for m in mixed),
            *(pl.BlockSpec((step, w.shape[1]), lambda j: (j, 0)) for w in weights),
            whole(gains),
        ],
        out_specs=[pl.BlockSpec((rows, width), lambda j: (0, 0))] * 2,
        compiler_params=pltpu.CompilerParams(vmem_limit_bytes=VMEM_BYTES),
        cost_estimate=FREE,
        name="close_attention",
    )(x, *mixed, *weights, gains)


def back_to_rows(blocks, weights):
    rows = blocks[0].shape[0]
    step, columns = weights[0][0].shape
    count = len(blocks)

    def body(*refs):
        lefts = refs[:count]
        hbm = refs[count : 3 * count]
        out = refs[3 * count]
        held, sems = refs[3 * count + 1 :]
        copies = []
        for i in range(count):
            own, came = hbm[2 * i : 2 * i + 2]
            copies.append(
                [
                    pltpu.make_async_copy(own, held.at[i, :step], sems.at[i, 0]),
                    pltpu.make_async_copy(came, held.at[i, step:], sems.at[i, 1]),
                ]
            )
        for some in copies:
            for copy in some:
                copy.start()
        for i in range(count):
            for copy in copies[i]:
                copy.wait()
            for k in range(4):
                on = slice(k * step, (k + 1) * step)
                part = nt(lefts[i][...], held[i, on])
                if i == 0:
                    out[:, on] = part
                else:
                    out[:, on] += part

    return pl.pallas_call(
        body,
        grid=(1,),
        out_shape=jax.ShapeDtypeStruct((rows, 4 * step), jnp.float32),
        in_specs=[pl.BlockSpec(memory_space=pltpu.VMEM)] * count
        + [pl.BlockSpec(memory_space=pl.ANY)] * (2 * count),
        out_specs=pl.BlockSpec(memory_space=pltpu.VMEM),
        scratch_shapes=[
            pltpu.VMEM((count, 4 * step, columns), jnp.bfloat16),
            pltpu.SemaphoreType.DMA((count, 2)),
        ],
        compiler_params=pltpu.CompilerParams(vmem_limit_bytes=VMEM_BYTES),
        cost_estimate=FREE,
        name="back_to_rows",
    )(*blocks, *(part for w in weights for part in w))


def on_device_block(
    tokens,
    lengths,
    attn_gain,
    w_query,
    key_matrix,
    value_matrix,
    query_gain,
    key_gain,
    w_out,
    mlp_gain,
    w_gate,
    w_up,
    w_down,
    cotangent,
):
    low, full = jnp.bfloat16, jnp.float32
    width = tokens.shape[2]
    head_dim = query_gain.shape[0]
    shards = lax.axis_size("shard")
    shard_at = lax.axis_index("shard")
    me = lax.axis_index("rep")
    core = me & 1
    count = lax.axis_size("rep")

    s = Stage()
    piece = width // shards

    def three(side, far_shard):
        return jnp.concatenate([side[:piece], far_shard, side[piece:]], 0)

    s.own_blocks = [
        column_block((w_query, key_matrix, value_matrix), me ^ i) for i in range(8)
    ]
    gain_rows = jnp.concatenate(
        [jnp.stack([attn_gain, mlp_gain]), jnp.zeros((14, piece), low)], 0
    )
    travelling = jnp.concatenate([s.own_blocks[0], gain_rows], 0)
    s.tokens_cuts = sequence_cuts(tokens)
    s.cotangent_cuts = sequence_cuts(cotangent)
    out_own = lax.all_gather(column_block((w_out,), me), "shard", axis=0, tiled=True)
    s.ffn_block = column_block((w_gate, w_up, w_down), me)
    s.before, s.behind = around(travelling, 1), around(travelling, -1)
    s.other_lengths = across(lengths, CORE)
    s.end()

    s.ahead = around(s.before, 1)
    s.side = jnp.concatenate([s.before[:piece], s.behind[:piece]], 0)
    s.side_near = near(s.side)
    s.x_first = to_sequence(s.tokens_cuts[0], 0)
    s.end()

    s.far_piece = s.ahead[:piece]
    s.came_own = three(s.side, s.far_piece)
    s.came_own_other = across(s.came_own, CORE)
    s.far_near = near(s.far_piece)
    s.side_last = far(*s.side_near)
    s.x_second = to_sequence(s.tokens_cuts[1], 1)
    s.gains = jnp.concatenate(
        [gain_rows[:2], *(part[piece : piece + 2] for part in (s.before, s.ahead, s.behind))], 1
    )
    s.out_own = out_own
    del s.tokens_cuts, s.before, s.behind, s.ahead
    s.end()

    s.far_last = far(*s.far_near)
    s.grad_y_first = to_sequence(s.cotangent_cuts[0], 0)
    came = [three(*pair) for pair in zip(s.side_near, s.far_near)]
    s.came_other = [s.came_own_other, *(across(block, CORE) for block in came)]
    s.came = [s.came_own, *came]
    gains = rolled(s.gains.astype(full))
    s.mlp_gains = gains[1:]
    s.attn_gains = gains[:1]
    s.x_low = jnp.concatenate(in_turn([s.x_first, s.x_second]), 0)
    rows = s.x_low.shape[0]
    x_rows = s.x_low.astype(full)
    s.inverse_in = lax.rsqrt(jnp.mean(x_rows * x_rows, -1, keepdims=True) + EPS)
    s.normed = rolled((x_rows * s.inverse_in * s.attn_gains).astype(low))
    query_gains = query_gain.astype(full)[None]
    key_gains = key_gain.astype(full)[None]
    s.head_gains = jnp.concatenate([query_gains, key_gains], 0)
    both = jnp.where(
        core == 0,
        jnp.concatenate([lengths, s.other_lengths]),
        jnp.concatenate([s.other_lengths, lengths]),
    )
    length = lax.dynamic_index_in_dim(both, shard_at, 0, keepdims=False)
    s.info = jnp.stack([core, length]).astype(jnp.int32)
    query_pos = core * rows + jnp.arange(rows, dtype=jnp.int32)
    s.valid = (query_pos < length)[:, None].astype(full)
    cosine, sine = tables(query_pos, head_dim)
    s.cosine, sine = cosine[0, :, 0], sine[0, :, 0]
    s.sine = jnp.concatenate([-sine[:, : head_dim // 2], sine[:, head_dim // 2 :]], 1)
    del s.came_own, s.came_own_other
    del s.gains, s.x_first, s.x_second, s.other_lengths
    del s.side, s.side_near, s.far_piece, s.far_near
    s.end()

    head_columns = 2 * head_dim
    block_columns = 4 * head_dim
    quad_rows = jax.ShapeDtypeStruct((rows, block_columns), low)
    quad_sums = jax.ShapeDtypeStruct((rows, block_columns), full)
    gain_sum = jax.ShapeDtypeStruct((1, head_dim), full)
    project = vmem_call(
        project_body,
        [jax.ShapeDtypeStruct((rows, 2 * block_columns), full), quad_rows, quad_rows],
        name="project",
    )
    attend = vmem_call(attend_body, [quad_rows, quad_sums], scalars=1, name="attend")
    attend_back = vmem_call(
        attend_back_body,
        [quad_rows, quad_sums, quad_rows, gain_sum],
        scratch=[pltpu.VMEM((2 * rows, head_dim), full)] * 2
        + [pltpu.VMEM((rows, block_columns), low)],
        scalars=1,
        name="attend_back",
    )
    finish = vmem_call(finish_body, [quad_rows, quad_rows, gain_sum], name="finish")
    upward = [(i, i + 1) for i in range(0, count, 2)]
    downward = [(i + 1, i) for i in range(0, count, 2)]

    def project_call(i):
        return (
            project, s.normed, s.own_blocks[2 * i], s.came[i], s.own_blocks[2 * i + 1],
            s.came_other[i], s.cosine, s.sine, s.head_gains,
        )

    def attend_call(i):
        return (
            lambda query, own, before: attend(s.info, query, before, own),
            *s.projected[i][1:], s.earlier[i],
        )

    def give_up(i):
        s.earlier = s.earlier | {i: lax.ppermute(s.projected[i][2], "rep", upward)}

    def compute(projected, attended):
        calls = [project_call(i) for i in projected] + [attend_call(i) for i in attended]
        outs = in_order(calls)
        s.projected = s.projected | dict(zip(projected, outs))
        s.attended = s.attended | dict(zip(attended, outs[len(projected) :]))

    s.projected, s.earlier, s.attended = {}, {}, {}
    grad_y_second = to_sequence(s.cotangent_cuts[1], 1)
    came_last = three(jnp.concatenate(s.side_last, 0), jnp.concatenate(s.far_last, 0))
    out_near = near(s.out_own)
    other_last = across(came_last, CORE)
    compute([0], [])
    s.came = [*s.came, came_last]
    s.came_other = [*s.came_other, other_last]
    del s.side_last, s.far_last, s.cotangent_cuts
    s.end()

    give_up(0)
    s.out_other = [across(s.out_own, CORE)]
    compute([1], [])
    s.grad_y_second = grad_y_second
    s.end()

    ffn_own = lax.all_gather(s.ffn_block, "shard", axis=0, tiled=True)
    give_up(1)
    compute([2], [0])
    s.out_near = out_near
    s.end()

    s.out_far = far(*s.out_near)
    s.out_other = [*s.out_other, *(across(block, CORE) for block in s.out_near)]
    give_up(2)
    grad_y = jnp.concatenate(in_turn([s.grad_y_first, s.grad_y_second]), 0)
    s.grad_y = jnp.where(s.valid > 0, grad_y, jnp.zeros_like(grad_y))
    compute([3], [1])
    del s.ffn_block, s.grad_y_first, s.grad_y_second
    s.end()

    grad_y_near = near(s.grad_y)
    out_last = jnp.concatenate(s.out_far, 0)
    s.out_other = [*s.out_other, across(out_last, CORE)]
    s.out_mine = [s.out_own, *s.out_near, out_last]
    give_up(3)
    compute([], [2])
    del s.out_own, s.out_near, s.out_far
    s.end()

    compute([], [3])
    s.out_blocks = [part for pair in zip(s.out_mine, s.out_other) for part in pair]
    s.mixed = [s.attended[i][0] for i in range(4)]
    s.resid, s.mid = close_attention(s.x_low, s.mixed, s.out_blocks, s.mlp_gains)
    del s.out_mine, s.out_other
    s.end()

    s.mid_near = near(s.mid)
    s.grad_y_near = grad_y_near
    s.end()

    s.grad_y_far = far(*s.grad_y_near)
    s.mid_far = far(*s.mid_near)
    s.ffn_own = ffn_own
    s.end()

    s.mids = [s.mid, *s.mid_near, *s.mid_far]
    s.grads_y = [s.grad_y, *s.grad_y_near, *s.grad_y_far]
    s.ffn_other = across(s.ffn_own, CORE)
    units = s.ffn_own.shape[1] // 3
    s.hidden_own = hidden_units(s.mids, s.grads_y, s.ffn_own)
    del s.mid, s.mid_near, s.mid_far, s.grad_y_near, s.grad_y_far
    s.end()

    def gate_up_pairs():
        return [
            (hidden[i], weights, i - 1)
            for hidden, weights in ((s.hidden_own, s.ffn_own), (s.hidden_other, s.ffn_other))
            for i in (1, 2)
        ]

    def down_pairs():
        return [(s.hidden_own[0], s.ffn_own, 2), (s.hidden_other[0], s.ffn_other, 2)]

    def from_hidden_call(pairs, eighths):
        return (
            lambda first: from_hidden([(first, *pairs[0][1:]), *pairs[1:]], eighths),
            pairs[0][0],
        )

    def outer_call(lefts, rights, *added):
        return lambda first: row_outer(lefts, [[first, *rights[1:]]], 0, 8, *added)[0], rights[0]

    def send_near(sent):
        return across(sent[0], ACROSS_X), across(sent[1], ACROSS_Y)

    def send_far(came, rest, split):
        one_tail, two_head = rest
        return (
            across(rounded_sum(one_tail, split(came[1])[1]), ACROSS_X),
            across(rounded_sum(two_head, split(came[0])[1]), ACROSS_Y),
        )

    def total(came, came_far, own, split):
        head, tail = own
        full_sum = lambda *parts: sum(part.astype(full) for part in parts)
        return jnp.concatenate(
            [
                full_sum(head, split(came[0])[0], came_far[1]),
                full_sum(tail, split(came[1])[0], came_far[0]),
            ],
            0,
        )

    by_rows = lambda a: jnp.split(a, 2, 0)
    by_columns = lambda a: jnp.split(a, 2, 1)
    to_plane, rest_of_plane = (2, 6, 5, 7), (3, 4, 0, 1)

    s.hidden_other = hidden_units(s.mids, s.grads_y, s.ffn_other)
    (s.down_outer,) = in_order([outer_call(s.grads_y, s.hidden_other[:1])])
    s.end()

    s.down_came = across(s.down_outer, CORE)
    s.mid_sent = from_hidden(gate_up_pairs(), to_plane)
    del s.down_outer
    s.end()

    s.mid_came = send_near(s.mid_sent)
    s.down_mine, s.mid_rest, s.gate_up_outer = in_order(
        [
            outer_call(s.grads_y, s.hidden_own[:1], s.down_came),
            from_hidden_call(gate_up_pairs(), rest_of_plane),
            outer_call(s.mids, s.hidden_other[1:]),
        ]
    )
    del s.mid_sent, s.down_came
    s.end()

    down_total = lax.psum_scatter(s.down_mine, "shard", scatter_dimension=0, tiled=True)
    s.mid_came_far = send_far(s.mid_came, by_rows(s.mid_rest[0]), by_rows)
    s.gate_up_came = across(s.gate_up_outer, CORE)
    s.mlp_sent, s.mlp_rest = in_order(
        [
            from_hidden_call(down_pairs(), to_plane),
            from_hidden_call(down_pairs(), rest_of_plane),
        ]
    )
    del s.gate_up_outer, s.down_mine
    s.end()

    def back_call(i):
        raw, query, own_pair = s.projected[i]
        return (
            lambda query, *rest: attend_back(s.info, query, *rest),
            query, s.earlier[i], own_pair, s.attended[i][1], s.resid_low,
            *s.out_blocks[2 * i : 2 * i + 2], raw, s.cosine, s.sine, s.head_gains[:1],
        )

    def finish_call(i):
        return (
            finish, s.backs[i][0], s.backs[i][1], s.returned[i], s.projected[i][0],
            s.cosine, s.sine, s.head_gains[1:],
        )

    def give_back(*chips):
        s.returned = s.returned | {
            i: lax.ppermute(s.backs[i][2], "rep", downward) for i in chips
        }

    def odd_call(left, blocks, part=None):
        return lambda first: row_outer([first], [blocks], 0, 8, part=part)[0], left

    def head_call(left, blocks, came, part=None, places=(0, 1, 2, 3)):
        groups = [[blocks[1], blocks[3]], [blocks[2]], [blocks[0]]]
        at = [places[i] for i in (1, 3, 2, 0)]
        return lambda first: row_outer([first], groups, 0, 4, came, at, part), left

    def tail_call(left, blocks, came, part=None, places=(0, 1, 2, 3)):
        groups = [[blocks[2], blocks[3]], [blocks[1]], [blocks[0]]]
        at = [places[i] for i in (2, 3, 1, 0)]
        return lambda first: row_outer([first], groups, 4, 4, came, at, part), left

    s.mlp_came = send_near(s.mlp_sent)
    grad_mid = total(s.mid_came, s.mid_came_far, by_rows(s.mid_rest[1]), by_rows)
    inverse_mid = lax.rsqrt(jnp.mean(s.resid * s.resid, -1, keepdims=True) + EPS)
    mid_unit = s.resid * inverse_mid
    s.mlp_gain_part = jnp.sum(mid_unit * grad_mid, 0)
    s.grad_resid = s.grad_y.astype(full) + norm_back(
        mid_unit, inverse_mid, grad_mid * s.mlp_gains
    )
    s.resid_low = s.grad_resid.astype(low)
    s.resid_rolled = rolled(s.resid_low)
    s.returned = {}
    back, s.out_odd, s.gate_up_mine = in_order(
        [
            back_call(3),
            odd_call(s.resid_rolled, s.mixed, 1),
            outer_call(s.mids, s.hidden_own[1:], s.gate_up_came),
        ]
    )
    s.backs = {3: back}
    s.down_total = down_total
    del s.mid_came, s.mid_came_far, s.mid_rest, s.gate_up_came, s.hidden_own, s.hidden_other
    del s.mids, s.grads_y, s.ffn_own, s.ffn_other, s.mlp_sent
    s.end()

    gate_up_total = lax.psum_scatter(s.gate_up_mine, "shard", scatter_dimension=0, tiled=True)
    s.mlp_came_far = send_far(s.mlp_came, by_rows(s.mlp_rest[0]), by_rows)
    s.out_came = across(s.out_odd, CORE)
    give_back(3)
    back1, back2 = in_order([back_call(1), back_call(2)])
    s.backs = s.backs | {1: back1, 2: back2}
    del s.out_odd, s.gate_up_mine
    s.end()

    s.down_near = near(s.down_total)
    give_back(1, 2)
    mlp_out = total(s.mlp_came, s.mlp_came_far, by_rows(s.mlp_rest[1]), by_rows)
    s.output = (s.valid * (s.resid + mlp_out)).astype(low)
    s.out_head, s.out_tail, back, finished = in_order(
        [
            head_call(s.resid_rolled, s.mixed, s.out_came, 0),
            tail_call(s.resid_rolled, s.mixed, s.out_came, 0),
            back_call(0),
            finish_call(3),
        ]
    )
    s.backs = s.backs | {0: back}
    s.finished = {3: finished}
    del s.mlp_came, s.mlp_came_far, s.mlp_rest, s.out_came, s.resid
    s.end()

    s.out_near = send_near((s.out_head[0], s.out_tail[0]))
    output_sent = from_sequences_send(s.output)
    give_back(0)
    finished1, finished2 = in_order([finish_call(1), finish_call(2)])
    s.finished = s.finished | {1: finished1, 2: finished2}
    s.end()

    def odd_half(half):
        return odd_call(s.normed, [s.finished[i][1] for i in range(4)], half)

    s.out_far = send_far(s.out_near, (s.out_tail[1], s.out_head[1]), by_columns)
    s.down_far = far(*s.down_near)
    (finished,) = in_order([finish_call(0)])
    s.finished = s.finished | {0: finished}
    (s.odd0,) = in_order([odd_half(0)])
    s.gate_up_total = gate_up_total
    s.output_first = output_sent[0]
    s.end()

    my_group = me.astype(jnp.int32)[None]

    def whole_call(widths, own, other, part=0):
        return lambda first: whole_columns(my_group, first, other, widths, part), own

    s.gate_up_near = near(s.gate_up_total)
    s.came0 = across(s.odd0, CORE)
    s.down_spread = jnp.concatenate([s.down_total, *s.down_near, *s.down_far], 0)
    s.down_spread_other = across(s.down_spread, CORE)
    out_sum = total(s.out_near, s.out_far, (s.out_head[2], s.out_tail[2]), by_columns)
    s.out_chunks = jnp.split(out_sum.astype(low), shards, 0)
    s.output_second = output_sent[1]
    weights = [
        pair
        for i in range(4)
        for pair in (
            (s.own_blocks[2 * i], s.came[i]), (s.own_blocks[2 * i + 1], s.came_other[i])
        )
    ]
    blocks = [part for i in range(4) for part in s.finished[i][:2]]
    s.odd1, grad_in = in_order(
        [
            odd_half(1),
            (lambda first: back_to_rows([first, *blocks[1:]], weights), blocks[0]),
        ]
    )
    grad_in = rolled(grad_in)
    x_unit = s.x_low.astype(full) * s.inverse_in
    s.gain_parts = jnp.concatenate(
        [
            jnp.sum(x_unit * grad_in, 0),
            s.mlp_gain_part,
            sum(s.backs[i][3] for i in range(4))[0],
            sum(s.finished[i][2] for i in range(4))[0],
        ]
    )
    s.grad_tokens = (
        s.grad_resid + norm_back(x_unit, s.inverse_in, grad_in * s.attn_gains)
    ).astype(low)
    del s.down_total, s.down_near, s.down_far, s.output
    del s.odd0, s.out_near, s.out_far, s.out_head, s.out_tail, s.backs
    del s.own_blocks, s.came, s.came_other, s.grad_resid, s.x_low
    s.end()

    def halves_call(half, came):
        even = [s.finished[i][0] for i in range(4)]
        return [call(s.normed, even, came, half) for call in (head_call, tail_call)]

    tokens_sent = from_sequences_send(s.grad_tokens)
    s.came1 = across(s.odd1, CORE)
    s.out_ring = ring_sum_first(s.out_chunks)
    s.gate_up_far = far(*s.gate_up_near)
    s.head0, s.tail0 = in_order(halves_call(0, s.came0))
    del s.odd1, s.came0
    s.end()

    def qkv_chunks(came, came_far, head, tail):
        own = total(came, came_far, (head[2], tail[2]), by_columns)
        return jnp.split(own.astype(low), shards, 0)

    s.near0 = send_near((s.head0[0], s.tail0[0]))
    s.gate_up_own = jnp.concatenate([s.gate_up_total, *s.gate_up_near, *s.gate_up_far], 0)
    s.gate_up_other = across(s.gate_up_own, CORE)
    s.head1, s.tail1, s.whole_down = in_order(
        [*halves_call(1, s.came1), whole_call((units,), s.down_spread, s.down_spread_other)]
    )
    s.out_ring_last = around(rounded_sum(s.out_chunks[3], s.out_ring[0]), 1)
    s.tokens_first = tokens_sent[0]
    del s.came1, s.down_spread, s.down_spread_other, s.finished
    del s.gate_up_near, s.gate_up_far, s.gate_up_total
    s.end()

    s.far0 = send_far(s.near0, (s.tail0[1], s.head0[1]), by_columns)
    s.near1 = send_near((s.head1[0], s.tail1[0]))
    s.out_total = rounded_sum(s.out_chunks[0], s.out_ring[1], s.out_ring_last)
    (s.whole_gate_up,) = in_order([whole_call((units, units), s.gate_up_own, s.gate_up_other)])
    s.tokens_second = tokens_sent[1]
    del s.out_chunks, s.out_ring, s.out_ring_last, s.gate_up_own, s.gate_up_other, s.grad_tokens
    s.end()

    s.chunks0 = qkv_chunks(s.near0, s.far0, s.head0, s.tail0)
    s.ring0 = ring_sum_first(s.chunks0)
    s.far1 = send_far(s.near1, (s.tail1[1], s.head1[1]), by_columns)
    s.gain_came = across(s.gain_parts, CORE)
    del s.near0, s.far0, s.head0, s.tail0
    s.end()

    s.last0 = around(rounded_sum(s.chunks0[3], s.ring0[0]), 1)
    s.chunks1 = qkv_chunks(s.near1, s.far1, s.head1, s.tail1)
    s.ring1 = ring_sum_first(s.chunks1)
    s.gain_parts = s.gain_parts + s.gain_came
    s.gain_came = across(s.gain_parts, ACROSS_X)
    del s.near1, s.far1, s.head1, s.tail1
    s.end()

    query_total = rounded_sum(s.chunks0[0], s.ring0[1], s.last0)
    s.total0 = jnp.concatenate([query_total, s.out_total], 1)
    s.spread0 = near(s.total0)
    s.last1 = around(rounded_sum(s.chunks1[3], s.ring1[0]), 1)
    s.gain_parts = s.gain_parts + s.gain_came
    s.gain_came = across(s.gain_parts, ACROSS_Y)
    del s.chunks0, s.ring0, s.last0, s.out_total
    s.end()

    s.spread_far0 = far(*s.spread0)
    s.total1 = rounded_sum(s.chunks1[0], s.ring1[1], s.last1)
    s.spread1 = near(s.total1)
    s.gain_parts = s.gain_parts + s.gain_came
    s.gain_came = lax.ppermute(s.gain_parts, "shard", [(i, i ^ 1) for i in range(shards)])
    del s.chunks1, s.ring1, s.last1
    s.end()

    s.own0 = jnp.concatenate([s.total0, *s.spread0, *s.spread_far0], 0)
    s.other0 = across(s.own0, CORE)
    s.spread_far1 = far(*s.spread1)
    s.gain_parts = s.gain_parts + s.gain_came
    s.gain_came = lax.ppermute(s.gain_parts, "shard", [(i, i ^ 2) for i in range(shards)])
    del s.total0, s.spread0, s.spread_far0
    s.end()

    s.own1 = jnp.concatenate([s.total1, *s.spread1, *s.spread_far1], 0)
    s.other1 = across(s.own1, CORE)
    (s.whole0,) = in_order([whole_call((head_columns, head_columns), s.own0, s.other0)])
    gain_sums = s.gain_parts + s.gain_came
    s.wide = lax.dynamic_slice_in_dim(
        gain_sums[: 2 * width].reshape(2, width), shard_at * piece, piece, 1
    )
    s.narrow = gain_sums[2 * width :]
    del s.own0, s.other0, s.total1, s.spread1, s.spread_far1
    s.end()

    ((whole_key, whole_value),) = in_order(
        [whole_call((head_dim, head_dim), s.own1, s.other1)]
    )
    return (
        jnp.stack(in_turn([s.output_first, s.output_second])),
        jnp.stack(in_turn([s.tokens_first, s.tokens_second])),
        s.wide[0],
        s.whole0[0],
        whole_key,
        whole_value,
        s.narrow[:head_dim],
        s.narrow[head_dim:],
        s.whole0[1],
        s.wide[1],
        *s.whole_gate_up,
        *s.whole_down,
    )


def solution(mesh):
    sizes = (mesh.shape["rep"], mesh.shape["shard"])
    return jax.shard_map(
        on_device_block if sizes == (8, 4) else on_device,
        mesh=mesh,
        in_specs=(
            P("rep", "shard", None),
            P("rep"),
            P("shard"),
            P("shard", None),
            P("shard", None),
            P("shard", None),
            P(),
            P(),
            P("shard", None),
            P("shard"),
            P("shard", None),
            P("shard", None),
            P("shard", None),
            P("rep", "shard", None),
        ),
        out_specs=(
            P("rep", "shard", None),
            P("rep", "shard", None),
            P("shard"),
            P("shard", None),
            P("shard", None),
            P("shard", None),
            P(),
            P(),
            P("shard", None),
            P("shard"),
            P("shard", None),
            P("shard", None),
            P("shard", None),
        ),
        check_vma=False,
    )
```

```python
import jax
import jax.numpy as jnp
from jax import lax
from jax.experimental import pallas as pl
from jax.experimental.pallas import tpu as pltpu
from jax.sharding import PartitionSpec as P

WINDOW = 512


EPS = 1e-06
ROPE_BASE = 1000000.0
NEG = -1e30


def passed_along(x, axis, by):
    devices = lax.axis_size(axis)
    pairs = [(i, i + by) for i in range(devices) if 0 <= i + by < devices]
    return lax.ppermute(x, axis, pairs)


def tables(positions, head_dim):
    half = head_dim // 2
    freq = ROPE_BASE ** (-jnp.arange(half, dtype=jnp.float32) * 2.0 / head_dim)
    angle = positions.astype(jnp.float32)[:, None] * freq[None, :]
    angle = jnp.concatenate([angle, angle], -1)
    return (jnp.cos(angle)[None, :, None, :], jnp.sin(angle)[None, :, None, :])


def rotated_rows(value_rows):
    half = value_rows.shape[-1] // 2
    return jnp.concatenate([-value_rows[..., half:], value_rows[..., :half]], -1)


def head_norm(raw, gain):
    inverse = lax.rsqrt(jnp.mean(raw * raw, -1, keepdims=True) + EPS)
    unit = raw * inverse
    return (unit, inverse, unit * gain)


def norm_back(unit, inverse, grad_unit):
    return inverse * (grad_unit - unit * jnp.mean(grad_unit * unit, -1, keepdims=True))


def head_norm_back(unit, inverse, grad_normed, gain):
    grad_raw = norm_back(unit, inverse, grad_normed * gain)
    return (grad_raw, jnp.sum(unit * grad_normed, axis=(0, 1, 2)))


def scores(query_rows, keys, allowed, scale):
    raw = (
        jnp.einsum("sqhgd,skhd->shgqk", query_rows, keys, preferred_element_type=jnp.float32)
        * scale
    )
    return jnp.where(allowed[:, None, None], raw, NEG)


def outer(left, right):
    return jnp.einsum("rc,rf->cf", left, right, preferred_element_type=jnp.float32)


def on_device(
    tokens,
    lengths,
    attn_gain,
    w_query,
    key_matrix,
    value_matrix,
    query_gain,
    key_gain,
    w_out,
    mlp_gain,
    w_gate,
    w_up,
    w_down,
    cotangent,
):
    seq_count, piece, width = tokens.shape
    head_dim = query_gain.shape[0]
    heads_q = w_query.shape[1] // head_dim
    heads_kv = key_matrix.shape[1] // head_dim
    groups = heads_q // heads_kv
    rows = seq_count * piece
    scale = head_dim ** (-0.5)
    reach = (WINDOW + piece - 2) // piece
    owned = width // lax.axis_size("shard")
    shard_at = lax.axis_index("shard")
    query_pos = shard_at * piece + jnp.arange(piece, dtype=jnp.int32)
    key_pos = (shard_at - reach) * piece + jnp.arange((reach + 1) * piece, dtype=jnp.int32)
    near = (
        (key_pos[None, :] <= query_pos[:, None])
        & (query_pos[:, None] - key_pos[None, :] < WINDOW)
        & (key_pos[None, :] >= 0)
    )
    live = (key_pos[None, None, :] < lengths[:, None, None]) | (
        key_pos[None, :] == query_pos[:, None]
    )[None]
    allowed = near[None] & live
    valid = (query_pos[None, :] < lengths[:, None]).astype(jnp.float32).reshape(rows, 1)
    cosine_table, sine_table = tables(query_pos, head_dim)
    x_rows = tokens.astype(jnp.float32).reshape(rows, width)
    inverse_in = lax.rsqrt(jnp.mean(x_rows * x_rows, -1, keepdims=True) + EPS)
    x_unit = x_rows * inverse_in
    gain_piece = lax.all_gather(attn_gain, "shard", axis=0, tiled=True)
    query_piece = lax.all_gather(w_query, "shard", axis=0, tiled=True)
    key_piece = lax.all_gather(key_matrix, "shard", axis=0, tiled=True)
    value_piece = lax.all_gather(value_matrix, "shard", axis=0, tiled=True)
    normed_piece = (x_unit * gain_piece.astype(jnp.float32)).astype(jnp.bfloat16)
    acc_q = jnp.dot(normed_piece, query_piece, preferred_element_type=jnp.float32)
    acc_k = jnp.dot(normed_piece, key_piece, preferred_element_type=jnp.float32)
    acc_v = jnp.dot(normed_piece, value_piece, preferred_element_type=jnp.float32)
    normalized_rows = normed_piece
    gains = gain_piece.astype(jnp.float32)
    attn_in = normalized_rows
    attn_gains = gains
    query_unit, query_inverse, query_rows_normalized = head_norm(
        acc_q.reshape(seq_count, piece, heads_q, head_dim), query_gain.astype(jnp.float32)
    )
    key_unit, key_inverse, key_normed = head_norm(
        acc_k.reshape(seq_count, piece, heads_kv, head_dim), key_gain.astype(jnp.float32)
    )
    query_rows = (
        (query_rows_normalized * cosine_table + rotated_rows(query_rows_normalized) * sine_table)
        .astype(jnp.bfloat16)
        .reshape(seq_count, piece, heads_kv, groups, head_dim)
    )
    keys_own = (key_normed * cosine_table + rotated_rows(key_normed) * sine_table).astype(
        jnp.bfloat16
    )
    values_own = acc_v.reshape(seq_count, piece, heads_kv, head_dim).astype(jnp.bfloat16)
    own_pair = jnp.stack([keys_own, values_own])
    parts = []
    for fetch_back in range(reach, 0, -1):
        parts.append(passed_along(own_pair, "shard", fetch_back))
    parts.append(own_pair)
    near_pair = jnp.concatenate(parts, 2)
    score = scores(query_rows, near_pair[0], allowed, scale)
    top = jnp.max(score, -1, keepdims=True)
    expo = jnp.exp(score - top)
    total = jnp.sum(expo, -1, keepdims=True)
    prob = expo / total
    log_total = top + jnp.log(total)
    mixed = jnp.einsum(
        "shgqk,skhd->sqhgd",
        prob.astype(jnp.bfloat16),
        near_pair[1],
        preferred_element_type=jnp.float32,
    )
    mixed_rows = mixed.reshape(rows, heads_q * head_dim).astype(jnp.bfloat16)
    resid = x_rows + jnp.einsum(
        "rf,nf->rn",
        mixed_rows,
        lax.all_gather(w_out, "shard", axis=0, tiled=True),
        preferred_element_type=jnp.float32,
    )
    inverse_mid = lax.rsqrt(jnp.mean(resid * resid, -1, keepdims=True) + EPS)
    mid_unit = resid * inverse_mid
    gain_piece = lax.all_gather(mlp_gain, "shard", axis=0, tiled=True)
    gate_piece = lax.all_gather(w_gate, "shard", axis=0, tiled=True)
    up_piece = lax.all_gather(w_up, "shard", axis=0, tiled=True)
    normed_piece = (mid_unit * gain_piece.astype(jnp.float32)).astype(jnp.bfloat16)
    acc_gate = jnp.dot(normed_piece, gate_piece, preferred_element_type=jnp.float32)
    acc_up = jnp.dot(normed_piece, up_piece, preferred_element_type=jnp.float32)
    normalized_rows = normed_piece
    gains = gain_piece.astype(jnp.float32)
    mlp_in = normalized_rows
    sigma = jax.nn.sigmoid(acc_gate)
    swish = acc_gate * sigma
    act = (swish * acc_up).astype(jnp.bfloat16)
    mlp_out = jnp.einsum(
        "rf,nf->rn",
        act,
        lax.all_gather(w_down, "shard", axis=0, tiled=True),
        preferred_element_type=jnp.float32,
    )
    output = (valid * (resid + mlp_out)).astype(jnp.bfloat16).reshape(seq_count, piece, width)
    grad_y = cotangent.astype(jnp.float32).reshape(rows, width) * valid
    grad_y_low = grad_y.astype(jnp.bfloat16)
    grad_act = jnp.dot(
        grad_y_low,
        lax.all_gather(w_down, "shard", axis=0, tiled=True),
        preferred_element_type=jnp.float32,
    )
    grad_gate = (grad_act * acc_up * sigma * (1.0 + acc_gate * (1.0 - sigma))).astype(jnp.bfloat16)
    grad_up = (grad_act * swish).astype(jnp.bfloat16)
    gate_piece, up_piece = lax.all_gather((w_gate, w_up), "shard", axis=0, tiled=True)
    grad_mid = jnp.einsum(
        "rf,nf->rn", grad_gate, gate_piece, preferred_element_type=jnp.float32
    ) + jnp.einsum("rf,nf->rn", grad_up, up_piece, preferred_element_type=jnp.float32)
    grad_resid = grad_y + norm_back(mid_unit, inverse_mid, grad_mid * gains)
    mlp_gain_part = jnp.sum(mid_unit * grad_mid, 0)
    normalized_rows = mlp_in
    mlp_grads = jax.tree.map(
        lambda part: lax.psum_scatter(
            part.astype(jnp.bfloat16), "shard", scatter_dimension=0, tiled=True
        ).astype(jnp.float32),
        (
            outer(normalized_rows, grad_gate),
            outer(normalized_rows, grad_up),
            outer(grad_y_low, act),
        ),
    )
    resid_low = grad_resid.astype(jnp.bfloat16)
    grad_mixed = jnp.dot(
        resid_low,
        lax.all_gather(w_out, "shard", axis=0, tiled=True),
        preferred_element_type=jnp.float32,
    )
    grad_mixed = grad_mixed.astype(jnp.bfloat16).reshape(
        seq_count, piece, heads_kv, groups, head_dim
    )
    prob_again = jnp.exp(scores(query_rows, near_pair[0], allowed, scale) - log_total)
    grad_prob = jnp.einsum(
        "sqhgd,skhd->shgqk", grad_mixed, near_pair[1], preferred_element_type=jnp.float32
    )
    grad_values = jnp.einsum(
        "shgqk,sqhgd->skhd",
        prob_again.astype(jnp.bfloat16),
        grad_mixed,
        preferred_element_type=jnp.float32,
    )
    grad_score = (
        prob_again * (grad_prob - jnp.sum(prob_again * grad_prob, -1, keepdims=True))
    ).astype(jnp.bfloat16)
    grad_queries = (
        jnp.einsum(
            "shgqk,skhd->sqhgd", grad_score, near_pair[0], preferred_element_type=jnp.float32
        )
        * scale
    )
    grad_keys = (
        jnp.einsum("shgqk,sqhgd->skhd", grad_score, query_rows, preferred_element_type=jnp.float32)
        * scale
    )
    grad_pair = jnp.stack([grad_keys, grad_values])
    own_grad = grad_pair[:, :, reach * piece :]
    for back in range(1, reach + 1):
        lower = (reach - back) * piece
        own_grad = own_grad + passed_along(grad_pair[:, :, lower : lower + piece], "shard", -back)
    grad_query_post = grad_queries.reshape(seq_count, piece, heads_q, head_dim)
    grad_query_normed = grad_query_post * cosine_table - rotated_rows(grad_query_post * sine_table)
    grad_key_normed = own_grad[0] * cosine_table - rotated_rows(own_grad[0] * sine_table)
    grad_query_raw, query_gain_grad = head_norm_back(
        query_unit, query_inverse, grad_query_normed, query_gain.astype(jnp.float32)
    )
    grad_key_raw, key_gain_grad = head_norm_back(
        key_unit, key_inverse, grad_key_normed, key_gain.astype(jnp.float32)
    )
    grad_query_low = grad_query_raw.reshape(rows, heads_q * head_dim).astype(jnp.bfloat16)
    grad_key_low = grad_key_raw.reshape(rows, heads_kv * head_dim).astype(jnp.bfloat16)
    grad_value_low = own_grad[1].reshape(rows, heads_kv * head_dim).astype(jnp.bfloat16)
    query_piece, key_piece, value_piece = lax.all_gather(
        (w_query, key_matrix, value_matrix), "shard", axis=0, tiled=True
    )
    grad_in = (
        jnp.einsum("rf,nf->rn", grad_query_low, query_piece, preferred_element_type=jnp.float32)
        + jnp.einsum("rf,nf->rn", grad_key_low, key_piece, preferred_element_type=jnp.float32)
        + jnp.einsum("rf,nf->rn", grad_value_low, value_piece, preferred_element_type=jnp.float32)
    )
    grad_tokens = (
        (grad_resid + norm_back(x_unit, inverse_in, grad_in * attn_gains))
        .astype(jnp.bfloat16)
        .reshape(seq_count, piece, width)
    )
    attn_gain_part = jnp.sum(x_unit * grad_in, 0)
    normalized_rows = attn_in
    attn_grads = jax.tree.map(
        lambda part: lax.psum_scatter(
            part.astype(jnp.bfloat16), "shard", scatter_dimension=0, tiled=True
        ).astype(jnp.float32),
        (
            outer(normalized_rows, grad_query_low),
            outer(normalized_rows, grad_key_low),
            outer(normalized_rows, grad_value_low),
            outer(resid_low, mixed_rows),
        ),
    )
    head_grads = lax.psum(
        (query_gain_grad, key_gain_grad, attn_gain_part, mlp_gain_part), ("rep", "shard")
    )
    attn_gain_total = lax.dynamic_slice_in_dim(head_grads[2], shard_at * owned, owned, 0)
    mlp_gain_total = lax.dynamic_slice_in_dim(head_grads[3], shard_at * owned, owned, 0)
    summed = (
        lax.psum(attn_grads[0].astype(jnp.bfloat16), "rep").astype(jnp.float32),
        lax.psum(attn_grads[1].astype(jnp.bfloat16), "rep").astype(jnp.float32),
        lax.psum(attn_grads[2].astype(jnp.bfloat16), "rep").astype(jnp.float32),
        lax.psum(attn_grads[3].astype(jnp.bfloat16), "rep").astype(jnp.float32),
        lax.psum(mlp_grads[0].astype(jnp.bfloat16), "rep").astype(jnp.float32),
        lax.psum(mlp_grads[1].astype(jnp.bfloat16), "rep").astype(jnp.float32),
        lax.psum(mlp_grads[2].astype(jnp.bfloat16), "rep").astype(jnp.float32),
    )
    attn_grads = summed[:4]
    mlp_grads = summed[4:]
    return (
        output,
        grad_tokens,
        attn_gain_total,
        attn_grads[0],
        attn_grads[1],
        attn_grads[2],
        head_grads[0],
        head_grads[1],
        attn_grads[3],
        mlp_gain_total,
        mlp_grads[0],
        mlp_grads[1],
        mlp_grads[2],
    )


CORE, ACROSS_X, ACROSS_Y = 1, 2, 4
VMEM_BYTES = 56 * 2**20
FREE = pl.CostEstimate(flops=1, bytes_accessed=1, transcendentals=0)


def across(x, mask):
    count = lax.axis_size("rep")
    return lax.ppermute(x, "rep", [(i, i ^ mask) for i in range(count)])


def around(x, by):
    count = lax.axis_size("shard")
    return lax.ppermute(x, "shard", [(i, (i + by) % count) for i in range(count)])


class Stage(dict):
    __getattr__ = dict.__getitem__
    __setattr__ = dict.__setitem__
    __delattr__ = dict.__delitem__

    def end(self):
        self.update(lax.optimization_barrier(dict(self)))


def in_order(calls):
    outs = []
    for call, first, *rest in calls:
        if outs:
            last = outs[-1][0] if isinstance(outs[-1], (list, tuple)) else outs[-1]
            first = lax.optimization_barrier((first, last))[0]
        outs.append(call(first, *rest))
    return outs


def ring_sum_first(chunks):
    return around(chunks[2], 1), around(chunks[1], -1)


def near(piece):
    return across(piece, ACROSS_X), across(piece, ACROSS_Y)


def far(from_x, from_y):
    half = from_x.shape[0] // 2
    return across(from_x[:half], ACROSS_Y), across(from_y[half:], ACROSS_X)


def rounded_sum(*parts):
    return sum(part.astype(jnp.float32) for part in parts).astype(jnp.bfloat16)


def sequence_pairs(turn):
    groups, shards = lax.axis_size("rep"), lax.axis_size("shard")
    pairs = []
    for group in range(groups):
        chip, core = divmod(group, 2)
        for at in range(shards):
            to_group, to_shard = 2 * chip + at // 2, 2 * core + (turn ^ (at & 1))
            pairs.append((group * shards + at, to_group * shards + to_shard))
    return pairs


def rolled(x):
    count, at = lax.axis_size("shard"), lax.axis_index("shard")
    width = x.shape[1] // count
    return jnp.concatenate(
        [lax.dynamic_slice_in_dim(x, ((at - i) % count) * width, width, 1) for i in range(count)],
        1,
    )


def sequence_cuts(x):
    odd = lax.axis_index("shard") & 1
    return [lax.dynamic_index_in_dim(x, turn ^ odd, 0, keepdims=False) for turn in range(2)]


def to_sequence(cut, turn):
    return lax.ppermute(cut, ("rep", "shard"), sequence_pairs(turn))


def from_sequences_send(x):
    odd = lax.axis_index("shard") & 1
    x = x.reshape(2, x.shape[0] // 2, x.shape[1])
    return [
        lax.ppermute(
            lax.dynamic_index_in_dim(x, turn ^ odd, 0, keepdims=False),
            ("rep", "shard"),
            [(to, at) for at, to in sequence_pairs(turn)],
        )
        for turn in range(2)
    ]


def in_turn(came):
    even = lax.axis_index("shard") & 1 == 0
    return [jnp.where(even, came[0], came[1]), jnp.where(even, came[1], came[0])]


def column_block(weights, at):
    cuts = [w.shape[1] // 8 for w in weights]
    return jnp.concatenate(
        [lax.dynamic_slice_in_dim(w, at * cut, cut, 1) for w, cut in zip(weights, cuts)], 1
    )


def whole_columns(me, own, other, widths, part=0):
    rows, columns = own.shape[0] // 4, sum(widths)

    def body(me_ref, own_ref, other_ref, *outs):
        def put(block):
            start = 0
            for out, width in zip(outs, widths):
                out[...] = block[:, start : start + width].astype(jnp.float32)
                start += width

        mine = (me_ref[0] ^ pl.program_id(0)) & 1 == 0
        pl.when(mine)(lambda: put(own_ref))
        pl.when(jnp.logical_not(mine))(lambda: put(other_ref))

    spec = pl.BlockSpec((rows, columns), lambda i, at: ((at[0] ^ i) >> 1, part))
    return pl.pallas_call(
        body,
        grid_spec=pltpu.PrefetchScalarGridSpec(
            num_scalar_prefetch=1,
            grid=(8,),
            in_specs=[spec, spec],
            out_specs=[pl.BlockSpec((rows, w), lambda i, at: (0, i)) for w in widths],
        ),
        out_shape=[jax.ShapeDtypeStruct((rows, 8 * w), jnp.float32) for w in widths],
        compiler_params=pltpu.CompilerParams(vmem_limit_bytes=VMEM_BYTES),
        cost_estimate=FREE,
        name="whole_columns",
    )(me, own, other)


def turned(x):
    return pltpu.roll(x, x.shape[-1] // 2, x.ndim - 1)


def nt(left, right):
    return lax.dot_general(
        left, right, (((1,), (1,)), ((), ())), preferred_element_type=jnp.float32
    )


def tn(left, right):
    return lax.dot_general(
        left, right, (((0,), (0,)), ((), ())), preferred_element_type=jnp.float32
    )


def unit_of(raw):
    inverse = lax.rsqrt(jnp.mean(raw * raw, -1, keepdims=True) + EPS)
    return raw * inverse, inverse


def project_body(
    normed, own0, came0, own1, came1, cosine, sine, gains, raw, query, key_value
):
    step = own0.shape[0]
    dim = cosine.shape[1]
    for block, (own, came) in enumerate(((own0, came0), (own1, came1))):
        at = block * 4 * dim
        raw[:, at : at + 4 * dim] = jnp.dot(
            normed[:, :step], own[...], preferred_element_type=jnp.float32
        ) + jnp.dot(normed[:, step:], came[...], preferred_element_type=jnp.float32)
        for i in range(3):
            unit, _ = unit_of(raw[:, at + i * dim : at + (i + 1) * dim])
            head = unit * gains[i // 2 : i // 2 + 1, :]
            head = (head * cosine[...] + turned(head) * sine[...]).astype(jnp.bfloat16)
            if i < 2:
                query[:, (2 * block + i) * dim : (2 * block + i + 1) * dim] = head
            else:
                key_value[:, 2 * block * dim : (2 * block + 1) * dim] = head
        key_value[:, (2 * block + 1) * dim : (2 * block + 2) * dim] = raw[
            :, at + 3 * dim : at + 4 * dim
        ].astype(jnp.bfloat16)


def window_mask(info, part, rows, columns):
    half = columns - rows
    row = lax.broadcasted_iota(jnp.int32, (rows, columns), 0)
    column = lax.broadcasted_iota(jnp.int32, (rows, columns), 1)
    gap = column - row - half
    slot = column + ((info[0] - 1) * half + part * rows)
    allowed = (gap <= 0) & (gap > -half) & (slot >= 0) & ((slot < info[1]) | (gap == 0))
    mask = jnp.where(allowed, 0.0, NEG)
    return jnp.concatenate([mask, mask], 0)


def two_heads(ref, at, block, dim):
    return jnp.concatenate(
        [ref[at, h * dim : (h + 1) * dim] for h in (2 * block, 2 * block + 1)], 0
    )


def key_columns(block, dim):
    key = slice(2 * block * dim, (2 * block + 1) * dim)
    value = slice((2 * block + 1) * dim, (2 * block + 2) * dim)
    return key, value


def seen_pair(before, own, part, block, dim):
    here, there = key_columns(block, dim), key_columns(1 - block, dim)
    rows = own.shape[0] // 2
    if part == 0:
        return [
            jnp.concatenate([before[:, t], own[:rows, h]], 0) for h, t in zip(here, there)
        ]
    return [jnp.concatenate([before[rows:, t], own[:, h]], 0) for h, t in zip(here, there)]


def attend_body(info, query, before, own, mixed, log_total):
    dim = own.shape[1] // 4
    rows = query.shape[0] // 2
    for part in range(2):
        at = slice(part * rows, (part + 1) * rows)
        mask = window_mask(info, part, rows, 3 * rows)
        for block in range(2):
            keys, values = seen_pair(before, own, part, block, dim)
            score = nt(two_heads(query, at, block, dim), keys) * dim**-0.5 + mask
            top = jnp.max(score, -1, keepdims=True)
            expo = jnp.exp(score - top)
            total = jnp.sum(expo, -1, keepdims=True)
            prob = (expo * (1.0 / total)).astype(jnp.bfloat16)
            out = jnp.dot(prob, values, preferred_element_type=jnp.float32).astype(jnp.bfloat16)
            log = jnp.broadcast_to(top + jnp.log(total), (2 * rows, dim))
            for i in range(2):
                on = slice((2 * block + i) * dim, (2 * block + i + 1) * dim)
                mixed[at, on] = out[i * rows : (i + 1) * rows]
                log_total[at, on] = log[i * rows : (i + 1) * rows]


def attend_back_body(
    info, query, before, own, log_total, grad_resid, weight0, weight1, raw, cosine, sine, gain,
    grad_query, grad_own, grad_before, gain_part, grad_keys, grad_values, grad_mixed,
):
    dim = own.shape[1] // 4
    rows = query.shape[0] // 2
    scale = dim**-0.5
    gain_total = jnp.zeros((1, dim), jnp.float32)
    masks = [window_mask(info, part, rows, 3 * rows) for part in range(2)]
    for block, weight in enumerate((weight0, weight1)):
        on = slice(2 * block * dim, 2 * (block + 1) * dim)
        grad_mixed[:, on] = jnp.dot(
            grad_resid[...], weight[...], preferred_element_type=jnp.float32
        ).astype(jnp.bfloat16)
        grad_keys[...] = jnp.zeros_like(grad_keys)
        grad_values[...] = jnp.zeros_like(grad_values)
        for part in range(2):
            keys, values = seen_pair(before, own, part, block, dim)
            at = slice(part * rows, (part + 1) * rows)
            seen = slice(part * rows, part * rows + 3 * rows)
            queries = two_heads(query, at, block, dim)
            grads = two_heads(grad_mixed, at, block, dim)
            log = two_heads(log_total, at, block, dim)[:, :1]
            prob = jnp.exp(nt(queries, keys) * scale + masks[part] - log)
            grad_prob = nt(grads, values)
            inner = jnp.sum(prob * grad_prob, -1, keepdims=True)
            grad_score = (prob * (grad_prob - inner)).astype(jnp.bfloat16)
            grad_values[seen, :] += tn(prob.astype(jnp.bfloat16), grads)
            grad_keys[seen, :] += tn(grad_score, queries) * scale
            both = jnp.dot(grad_score, keys, preferred_element_type=jnp.float32) * scale
            for i in range(2):
                head = 2 * block + i
                back = both[i * rows : (i + 1) * rows]
                back = back * cosine[at, :] - turned(back) * sine[at, :]
                there = (2 * head - head % 2) * dim
                unit, inverse = unit_of(raw[at, there : there + dim])
                gain_total += jnp.sum(unit * back, 0, keepdims=True)
                back = back * gain[...]
                back = inverse * (back - unit * jnp.mean(back * unit, -1, keepdims=True))
                grad_query[at, head * dim : (head + 1) * dim] = back.astype(jnp.bfloat16)
        for grad, here, there in zip(
            (grad_keys, grad_values), key_columns(block, dim), key_columns(1 - block, dim)
        ):
            grad_before[:, there] = grad[: 2 * rows, :].astype(jnp.bfloat16)
            grad_own[:, here] = grad[2 * rows :, :]
    gain_part[...] = gain_total


def finish_body(grad_query, grad_own, came, raw, cosine, sine, gain, even, odd, gain_part):
    dim = cosine.shape[1]
    total = jnp.zeros((1, dim), jnp.float32)
    for block, out in enumerate((even, odd)):
        key, value = key_columns(block, dim)
        back = grad_own[:, key] + came[:, key].astype(jnp.float32)
        back = back * cosine[...] - turned(back) * sine[...]
        unit, inverse = unit_of(raw[:, (4 * block + 2) * dim : (4 * block + 3) * dim])
        total += jnp.sum(unit * back, 0, keepdims=True)
        back = back * gain[...]
        back = inverse * (back - unit * jnp.mean(back * unit, -1, keepdims=True))
        out[:, : 2 * dim] = grad_query[:, 2 * block * dim : (2 * block + 2) * dim]
        out[:, 2 * dim : 3 * dim] = back.astype(jnp.bfloat16)
        grad_value = grad_own[:, value] + came[:, value].astype(jnp.float32)
        out[:, 3 * dim :] = grad_value.astype(jnp.bfloat16)
    gain_part[...] = total


def vmem_call(body, outs, scratch=(), scalars=0, name=None):
    def call(*args):
        in_specs = [
            pl.BlockSpec(memory_space=pltpu.SMEM if i < scalars else pltpu.VMEM)
            for i in range(len(args))
        ]
        return pl.pallas_call(
            body,
            grid=(1,),
            out_shape=outs,
            in_specs=in_specs,
            out_specs=jax.tree.map(lambda _: pl.BlockSpec(memory_space=pltpu.VMEM), outs),
            scratch_shapes=scratch,
            compiler_params=pltpu.CompilerParams(vmem_limit_bytes=VMEM_BYTES),
        cost_estimate=FREE,
            name=name,
        )(*args)

    return call


def hidden_units(mids, grads_y, weights):
    width, units = weights.shape[0], weights.shape[1] // 3
    count = len(mids)
    heights = [m.shape[0] for m in mids]
    rows, cut = sum(heights), units // 3

    def body(*refs):
        gate_w, up_w, w_down, act, grad_gate, grad_up = refs[2 * count :]
        start = 0
        for mid, grad_y in zip(refs[:count], refs[count : 2 * count]):
            at = slice(start, start + mid.shape[0])
            start += mid.shape[0]
            gate = jnp.dot(mid[...], gate_w[...], preferred_element_type=jnp.float32)
            up = jnp.dot(mid[...], up_w[...], preferred_element_type=jnp.float32)
            grad_act = jnp.dot(grad_y[...], w_down[...], preferred_element_type=jnp.float32)
            sigma = jax.nn.sigmoid(gate)
            swish = gate * sigma
            act[at, :] = (swish * up).astype(jnp.bfloat16)
            slope = grad_act * up * sigma * (1.0 + gate * (1.0 - sigma))
            grad_gate[at, :] = slope.astype(jnp.bfloat16)
            grad_up[at, :] = (grad_act * swish).astype(jnp.bfloat16)

    row_specs = [
        pl.BlockSpec((h, width), lambda j: (0, 0), pipeline_mode=pl.Buffered(1)) for h in heights
    ]
    return pl.pallas_call(
        body,
        grid=(3,),
        out_shape=[jax.ShapeDtypeStruct((rows, units), jnp.bfloat16)] * 3,
        in_specs=[
            *row_specs,
            *row_specs,
            pl.BlockSpec((width, cut), lambda j: (0, j)),
            pl.BlockSpec((width, cut), lambda j: (0, j + 3)),
            pl.BlockSpec((width, cut), lambda j: (0, j + 6)),
        ],
        out_specs=[pl.BlockSpec((rows, cut), lambda j: (0, j))] * 3,
        compiler_params=pltpu.CompilerParams(vmem_limit_bytes=VMEM_BYTES),
        cost_estimate=FREE,
        name="hidden_units",
    )(*mids, *grads_y, weights, weights, weights)


def from_hidden(pairs, eighths):
    count, parts = len(pairs), len(eighths)
    rows, units = pairs[0][0].shape[0] // 8, pairs[0][0].shape[1]
    width = pairs[0][1].shape[0]
    cut = width // 4

    def body(*refs):
        ins, outs = refs[: -(parts // 2)], refs[-(parts // 2) :]
        total = 0.0
        for i in range(count):
            part = ins[i * (parts + 1) : (i + 1) * (parts + 1)]
            left = jnp.concatenate([p[...] for p in part[:-1]], 0)
            total = total + nt(left, part[-1][...])
        for i, out in enumerate(outs):
            out[...] = total[2 * i * rows : 2 * (i + 1) * rows].astype(jnp.bfloat16)

    specs, args = [], []
    for left, right, at in pairs:
        specs += [pl.BlockSpec((rows, units), lambda j, e=e: (e, 0)) for e in eighths]
        specs.append(pl.BlockSpec((cut, units), lambda j, at=at: (j, at)))
        args += [left] * parts + [right]
    return pl.pallas_call(
        body,
        grid=(4,),
        out_shape=[jax.ShapeDtypeStruct((2 * rows, width), jnp.bfloat16)] * (parts // 2),
        in_specs=specs,
        out_specs=[pl.BlockSpec((2 * rows, cut), lambda j: (0, j))] * (parts // 2),
        compiler_params=pltpu.CompilerParams(vmem_limit_bytes=VMEM_BYTES),
        cost_estimate=FREE,
        name="from_hidden",
    )(*args)


def row_outer(lefts, groups, first, tiles, added=None, places=None, part=None):
    rights = [right for group in groups for right in group]
    places = range(len(rights)) if places is None else places
    added = [] if added is None else [added] * len(rights)
    width = lefts[0].shape[1]
    tile = width // 8
    count = len(lefts)
    rows = sum(left.shape[0] for left in lefts)
    wide = rights[0].shape[1] // (1 if part is None else 2)
    columns = [wide * len(group) for group in groups]

    def body(*refs):
        left_refs = refs[:count]
        right_refs = refs[count : count + len(rights)]
        add_refs = refs[count + len(rights) : count + len(rights) + len(added)]
        outs = refs[count + len(rights) + len(added) :]
        place = 0
        for i, group in enumerate(groups):
            column = 0
            for _ in group:
                on = slice(column, column + wide)
                total, start = 0.0, 0
                for left in left_refs:
                    stop = start + left.shape[0]
                    total = total + tn(left[...], right_refs[place][start:stop, :])
                    start = stop
                if added:
                    total = total + add_refs[place][...].astype(jnp.float32)
                outs[i][:, on] = total.astype(jnp.bfloat16)
                place += 1
                column += wide

    return pl.pallas_call(
        body,
        grid=(tiles,),
        out_shape=[jax.ShapeDtypeStruct((tiles * tile, c), jnp.bfloat16) for c in columns],
        in_specs=[
            *(pl.BlockSpec((left.shape[0], tile), lambda j: (0, j + first)) for left in lefts),
            *(
                pl.BlockSpec(
                    (right.shape[0], wide), lambda j: (0, part or 0), pipeline_mode=pl.Buffered(1)
                )
                for right in rights
            ),
            *(
                pl.BlockSpec((tile, wide), lambda j, at=at: (j + first, at))
                for at in places[: len(added)]
            ),
        ],
        out_specs=[pl.BlockSpec((tile, c), lambda j: (j, 0)) for c in columns],
        compiler_params=pltpu.CompilerParams(vmem_limit_bytes=VMEM_BYTES),
        cost_estimate=pl.CostEstimate(
            flops=2 * rows * tiles * tile * sum(columns),
            bytes_accessed=2 * rows * (width + sum(columns)),
            transcendentals=0,
        ),
        name="row_outer",
    )(*lefts, *rights, *added)


def close_body(x, *refs):
    mixed, weights = refs[:4], refs[4:12]
    gains, resid, mid = refs[12:]
    at = pl.program_id(0)
    step = x.shape[1]
    columns = weights[0].shape[1]
    total = x[...].astype(jnp.float32)
    for i in range(8):
        part = mixed[i // 2][:, (i % 2) * columns : (i % 2 + 1) * columns]
        total = total + nt(part, weights[i][...])
    resid[:, pl.ds(pl.multiple_of(at * step, step), step)] = total

    @pl.when(at == 3)
    def _():
        unit, _ = unit_of(resid[...])
        mid[...] = (unit * gains[...]).astype(jnp.bfloat16)


def close_attention(x, mixed, weights, gains):
    rows, width = x.shape
    step = width // 4
    whole = lambda a: pl.BlockSpec(a.shape, lambda j: (0, 0))
    return pl.pallas_call(
        close_body,
        grid=(4,),
        out_shape=[
            jax.ShapeDtypeStruct((rows, width), jnp.float32),
            jax.ShapeDtypeStruct((rows, width), jnp.bfloat16),
        ],
        in_specs=[
            pl.BlockSpec((rows, step), lambda j: (0, j)),
            *(whole(m) for m in mixed),
            *(pl.BlockSpec((step, w.shape[1]), lambda j: (j, 0)) for w in weights),
            whole(gains),
        ],
        out_specs=[pl.BlockSpec((rows, width), lambda j: (0, 0))] * 2,
        compiler_params=pltpu.CompilerParams(vmem_limit_bytes=VMEM_BYTES),
        cost_estimate=FREE,
        name="close_attention",
    )(x, *mixed, *weights, gains)


def back_to_rows(blocks, weights):
    rows = blocks[0].shape[0]
    step, columns = weights[0][0].shape
    count = len(blocks)

    def body(*refs):
        lefts = refs[:count]
        hbm = refs[count : 3 * count]
        out = refs[3 * count]
        held, sems = refs[3 * count + 1 :]
        copies = []
        for i in range(count):
            own, came = hbm[2 * i : 2 * i + 2]
            copies.append(
                [
                    pltpu.make_async_copy(own, held.at[i, :step], sems.at[i, 0]),
                    pltpu.make_async_copy(came, held.at[i, step:], sems.at[i, 1]),
                ]
            )
        for some in copies:
            for copy in some:
                copy.start()
        for i in range(count):
            for copy in copies[i]:
                copy.wait()
            for k in range(4):
                on = slice(k * step, (k + 1) * step)
                part = nt(lefts[i][...], held[i, on])
                if i == 0:
                    out[:, on] = part
                else:
                    out[:, on] += part

    return pl.pallas_call(
        body,
        grid=(1,),
        out_shape=jax.ShapeDtypeStruct((rows, 4 * step), jnp.float32),
        in_specs=[pl.BlockSpec(memory_space=pltpu.VMEM)] * count
        + [pl.BlockSpec(memory_space=pl.ANY)] * (2 * count),
        out_specs=pl.BlockSpec(memory_space=pltpu.VMEM),
        scratch_shapes=[
            pltpu.VMEM((count, 4 * step, columns), jnp.bfloat16),
            pltpu.SemaphoreType.DMA((count, 2)),
        ],
        compiler_params=pltpu.CompilerParams(vmem_limit_bytes=VMEM_BYTES),
        cost_estimate=FREE,
        name="back_to_rows",
    )(*blocks, *(part for w in weights for part in w))


def on_device_block(
    tokens,
    lengths,
    attn_gain,
    w_query,
    key_matrix,
    value_matrix,
    query_gain,
    key_gain,
    w_out,
    mlp_gain,
    w_gate,
    w_up,
    w_down,
    cotangent,
):
    low, full = jnp.bfloat16, jnp.float32
    width = tokens.shape[2]
    head_dim = query_gain.shape[0]
    shards = lax.axis_size("shard")
    shard_at = lax.axis_index("shard")
    me = lax.axis_index("rep")
    core = me & 1
    count = lax.axis_size("rep")

    s = Stage()
    piece = width // shards

    s.own_blocks = [
        column_block((w_query, key_matrix, value_matrix), me ^ i) for i in range(8)
    ]
    gain_rows = jnp.concatenate(
        [jnp.stack([attn_gain, mlp_gain]), jnp.zeros((14, piece), low)], 0
    )
    travelling = jnp.concatenate([s.own_blocks[0], gain_rows], 0)
    s.tokens_cuts, s.cotangent_cuts = sequence_cuts(tokens), sequence_cuts(cotangent)
    s.out_block = column_block((w_out,), me)
    s.ffn_block = column_block((w_gate, w_up, w_down), me)
    s.before, s.behind = around(travelling, 1), around(travelling, -1)
    s.other_lengths = across(lengths, CORE)
    s.end()

    s.ahead = around(s.before, 1)
    tokens_sent = [to_sequence(cut, turn) for turn, cut in enumerate(s.tokens_cuts)]
    out_own = lax.all_gather(s.out_block, "shard", axis=0, tiled=True)
    del s.out_block, s.tokens_cuts
    s.end()

    parts = (s.before, s.ahead, s.behind)
    s.came = jnp.concatenate([part[:piece] for part in parts], 0)
    s.gains = jnp.concatenate([gain_rows[:2], *(part[piece : piece + 2] for part in parts)], 1)
    s.came_near = near(s.came)
    s.came_own = across(s.came, CORE)
    s.x_came = tokens_sent
    del s.before, s.behind, s.ahead
    s.end()

    grad_y_sent = [to_sequence(cut, turn) for turn, cut in enumerate(s.cotangent_cuts)]
    s.came_far = far(*s.came_near)
    s.came_other = [s.came_own, *(across(block, CORE) for block in s.came_near)]
    gains = rolled(s.gains.astype(full))
    s.mlp_gains = gains[1:]
    s.attn_gains = gains[:1]
    s.x_low = jnp.concatenate(in_turn(s.x_came), 0)
    rows = s.x_low.shape[0]
    x_rows = s.x_low.astype(full)
    s.inverse_in = lax.rsqrt(jnp.mean(x_rows * x_rows, -1, keepdims=True) + EPS)
    s.normed = rolled((x_rows * s.inverse_in * s.attn_gains).astype(low))
    query_gains = query_gain.astype(full)[None]
    key_gains = key_gain.astype(full)[None]
    s.head_gains = jnp.concatenate([query_gains, key_gains], 0)
    both = jnp.where(
        core == 0,
        jnp.concatenate([lengths, s.other_lengths]),
        jnp.concatenate([s.other_lengths, lengths]),
    )
    length = lax.dynamic_index_in_dim(both, shard_at, 0, keepdims=False)
    s.info = jnp.stack([core, length]).astype(jnp.int32)
    query_pos = core * rows + jnp.arange(rows, dtype=jnp.int32)
    s.valid = (query_pos < length)[:, None].astype(full)
    cosine, sine = tables(query_pos, head_dim)
    s.cosine, sine = cosine[0, :, 0], sine[0, :, 0]
    s.sine = jnp.concatenate([-sine[:, : head_dim // 2], sine[:, head_dim // 2 :]], 1)
    s.out_own = out_own
    del s.gains, s.x_came, s.other_lengths, s.cotangent_cuts, s.came_own
    s.end()

    head_columns = 2 * head_dim
    block_columns = 4 * head_dim
    quad_rows = jax.ShapeDtypeStruct((rows, block_columns), low)
    quad_sums = jax.ShapeDtypeStruct((rows, block_columns), full)
    gain_sum = jax.ShapeDtypeStruct((1, head_dim), full)
    project = vmem_call(
        project_body,
        [jax.ShapeDtypeStruct((rows, 2 * block_columns), full), quad_rows, quad_rows],
        name="project",
    )
    attend = vmem_call(attend_body, [quad_rows, quad_sums], scalars=1, name="attend")
    attend_back = vmem_call(
        attend_back_body,
        [quad_rows, quad_sums, quad_rows, gain_sum],
        scratch=[pltpu.VMEM((2 * rows, head_dim), full)] * 2
        + [pltpu.VMEM((rows, block_columns), low)],
        scalars=1,
        name="attend_back",
    )
    finish = vmem_call(finish_body, [quad_rows, quad_rows, gain_sum], name="finish")
    upward = [(i, i + 1) for i in range(0, count, 2)]
    downward = [(i + 1, i) for i in range(0, count, 2)]

    def project_call(i, came, other):
        return (
            project, s.normed, s.own_blocks[2 * i], came, s.own_blocks[2 * i + 1], other,
            s.cosine, s.sine, s.head_gains,
        )

    def attend_call(projected, earlier):
        return (
            lambda query, own, before: attend(s.info, query, before, own),
            *projected[1:], earlier,
        )

    came_last = jnp.concatenate(s.came_far, 0)
    s.came_last = (came_last, across(came_last, CORE))
    s.out_near = near(s.out_own)
    s.out_own_other = across(s.out_own, CORE)
    s.projected = in_order(
        [
            project_call(i, block, other)
            for i, (block, other) in enumerate(zip((s.came, *s.came_near), s.came_other))
        ]
    )
    s.grad_y_came = grad_y_sent
    del s.came_far
    s.end()

    ffn_own = lax.all_gather(s.ffn_block, "shard", axis=0, tiled=True)
    grad_y = jnp.concatenate(in_turn(s.grad_y_came), 0)
    s.grad_y = jnp.where(s.valid > 0, grad_y, jnp.zeros_like(grad_y))
    grad_y_near = near(s.grad_y)
    s.out_far = far(*s.out_near)
    s.out_near_other = [across(block, CORE) for block in s.out_near]
    s.earlier = [lax.ppermute(p[2], "rep", upward) for p in s.projected]
    (s.projected_last,) = in_order([project_call(3, *s.came_last)])
    del s.ffn_block, s.grad_y_came
    s.end()

    out_last = jnp.concatenate(s.out_far, 0)
    s.out_last = (out_last, across(out_last, CORE))
    s.earlier_last = lax.ppermute(s.projected_last[2], "rep", upward)
    s.attended = in_order([attend_call(*pair) for pair in zip(s.projected, s.earlier)])
    s.grad_y_near = grad_y_near
    del s.out_far
    s.end()

    s.projected = [*s.projected, s.projected_last]
    s.earlier = [*s.earlier, s.earlier_last]
    s.out_blocks = [
        s.out_own, s.out_own_other, s.out_near[0], s.out_near_other[0], s.out_near[1],
        s.out_near_other[1], *s.out_last,
    ]
    (last,) = in_order([attend_call(s.projected_last, s.earlier_last)])
    s.attended = [*s.attended, last]
    s.mixed = [a[0] for a in s.attended]
    s.resid, s.mid = close_attention(s.x_low, s.mixed, s.out_blocks, s.mlp_gains)
    s.grad_y_far = far(*s.grad_y_near)
    s.came = [s.came, *s.came_near, s.came_last[0]]
    s.came_other = [*s.came_other, s.came_last[1]]
    del s.came_near, s.came_last
    del s.out_own, s.out_own_other, s.out_near, s.out_near_other, s.out_last
    del s.projected_last, s.earlier_last
    s.end()

    s.mid_near = near(s.mid)
    s.end()

    s.mid_far = far(*s.mid_near)
    s.ffn_own = ffn_own
    s.end()

    s.mids = [s.mid, *s.mid_near, *s.mid_far]
    s.grads_y = [s.grad_y, *s.grad_y_near, *s.grad_y_far]
    s.ffn_other = across(s.ffn_own, CORE)
    units = s.ffn_own.shape[1] // 3
    s.hidden_own = hidden_units(s.mids, s.grads_y, s.ffn_own)
    del s.mid, s.mid_near, s.mid_far, s.grad_y_near, s.grad_y_far
    s.end()

    def gate_up_pairs():
        return [
            (hidden[i], weights, i - 1)
            for hidden, weights in ((s.hidden_own, s.ffn_own), (s.hidden_other, s.ffn_other))
            for i in (1, 2)
        ]

    def down_pairs():
        return [(s.hidden_own[0], s.ffn_own, 2), (s.hidden_other[0], s.ffn_other, 2)]

    def from_hidden_call(pairs, eighths):
        return (
            lambda first: from_hidden([(first, *pairs[0][1:]), *pairs[1:]], eighths),
            pairs[0][0],
        )

    def outer_call(lefts, rights, *added):
        return lambda first: row_outer(lefts, [[first, *rights[1:]]], 0, 8, *added)[0], rights[0]

    def send_near(sent):
        return across(sent[0], ACROSS_X), across(sent[1], ACROSS_Y)

    def send_far(came, rest, split):
        one_tail, two_head = rest
        return (
            across(rounded_sum(one_tail, split(came[1])[1]), ACROSS_X),
            across(rounded_sum(two_head, split(came[0])[1]), ACROSS_Y),
        )

    def total(came, came_far, own, split):
        head, tail = own
        full_sum = lambda *parts: sum(part.astype(full) for part in parts)
        return jnp.concatenate(
            [
                full_sum(head, split(came[0])[0], came_far[1]),
                full_sum(tail, split(came[1])[0], came_far[0]),
            ],
            0,
        )

    by_rows = lambda a: jnp.split(a, 2, 0)
    by_columns = lambda a: jnp.split(a, 2, 1)
    to_plane, rest_of_plane = (2, 6, 5, 7), (3, 4, 0, 1)

    s.hidden_other = hidden_units(s.mids, s.grads_y, s.ffn_other)
    (s.down_outer,) = in_order([outer_call(s.grads_y, s.hidden_other[:1])])
    s.end()

    s.down_came = across(s.down_outer, CORE)
    s.mid_sent = from_hidden(gate_up_pairs(), to_plane)
    del s.down_outer
    s.end()

    s.mid_came = send_near(s.mid_sent)
    s.down_mine, s.mid_rest, s.gate_up_outer = in_order(
        [
            outer_call(s.grads_y, s.hidden_own[:1], s.down_came),
            from_hidden_call(gate_up_pairs(), rest_of_plane),
            outer_call(s.mids, s.hidden_other[1:]),
        ]
    )
    del s.mid_sent, s.down_came
    s.end()

    down_total = lax.psum_scatter(s.down_mine, "shard", scatter_dimension=0, tiled=True)
    s.mid_came_far = send_far(s.mid_came, by_rows(s.mid_rest[0]), by_rows)
    s.gate_up_came = across(s.gate_up_outer, CORE)
    s.mlp_sent, s.mlp_rest = in_order(
        [
            from_hidden_call(down_pairs(), to_plane),
            from_hidden_call(down_pairs(), rest_of_plane),
        ]
    )
    del s.gate_up_outer, s.down_mine
    s.end()

    def back_call(i):
        raw, query, own_pair = s.projected[i]
        return (
            lambda query, *rest: attend_back(s.info, query, *rest),
            query, s.earlier[i], own_pair, s.attended[i][1], s.resid_low,
            *s.out_blocks[2 * i : 2 * i + 2], raw, s.cosine, s.sine, s.head_gains[:1],
        )

    def finish_call(i):
        return (
            finish, s.backs[i][0], s.backs[i][1], s.returned[i], s.projected[i][0],
            s.cosine, s.sine, s.head_gains[1:],
        )

    def give_back(*chips):
        s.returned = s.returned | {
            i: lax.ppermute(s.backs[i][2], "rep", downward) for i in chips
        }

    def odd_call(left, blocks, part=None):
        return lambda first: row_outer([first], [blocks], 0, 8, part=part)[0], left

    def head_call(left, blocks, came, part=None, places=(0, 1, 2, 3)):
        groups = [[blocks[1], blocks[3]], [blocks[2]], [blocks[0]]]
        at = [places[i] for i in (1, 3, 2, 0)]
        return lambda first: row_outer([first], groups, 0, 4, came, at, part), left

    def tail_call(left, blocks, came, part=None, places=(0, 1, 2, 3)):
        groups = [[blocks[2], blocks[3]], [blocks[1]], [blocks[0]]]
        at = [places[i] for i in (2, 3, 1, 0)]
        return lambda first: row_outer([first], groups, 4, 4, came, at, part), left

    s.mlp_came = send_near(s.mlp_sent)
    grad_mid = total(s.mid_came, s.mid_came_far, by_rows(s.mid_rest[1]), by_rows)
    inverse_mid = lax.rsqrt(jnp.mean(s.resid * s.resid, -1, keepdims=True) + EPS)
    mid_unit = s.resid * inverse_mid
    s.mlp_gain_part = jnp.sum(mid_unit * grad_mid, 0)
    s.grad_resid = s.grad_y.astype(full) + norm_back(
        mid_unit, inverse_mid, grad_mid * s.mlp_gains
    )
    s.resid_low = s.grad_resid.astype(low)
    s.resid_rolled = rolled(s.resid_low)
    s.returned = {}
    back, s.out_odd, s.gate_up_mine = in_order(
        [
            back_call(3),
            odd_call(s.resid_rolled, s.mixed, 1),
            outer_call(s.mids, s.hidden_own[1:], s.gate_up_came),
        ]
    )
    s.backs = {3: back}
    s.down_total = down_total
    del s.mid_came, s.mid_came_far, s.mid_rest, s.gate_up_came, s.hidden_own, s.hidden_other
    del s.mids, s.grads_y, s.ffn_own, s.ffn_other, s.mlp_sent
    s.end()

    gate_up_total = lax.psum_scatter(s.gate_up_mine, "shard", scatter_dimension=0, tiled=True)
    s.mlp_came_far = send_far(s.mlp_came, by_rows(s.mlp_rest[0]), by_rows)
    s.out_came = across(s.out_odd, CORE)
    give_back(3)
    back1, back2 = in_order([back_call(1), back_call(2)])
    s.backs = s.backs | {1: back1, 2: back2}
    del s.out_odd, s.gate_up_mine
    s.end()

    s.down_near = near(s.down_total)
    give_back(1, 2)
    s.out_head, s.out_tail, back, finished = in_order(
        [
            head_call(s.resid_rolled, s.mixed, s.out_came, 0),
            tail_call(s.resid_rolled, s.mixed, s.out_came, 0),
            back_call(0),
            finish_call(3),
        ]
    )
    s.backs = s.backs | {0: back}
    s.finished = {3: finished}
    del s.out_came
    s.end()

    s.out_near = send_near((s.out_head[0], s.out_tail[0]))
    mlp_out = total(s.mlp_came, s.mlp_came_far, by_rows(s.mlp_rest[1]), by_rows)
    s.output = (s.valid * (s.resid + mlp_out)).astype(low)
    give_back(0)
    finished1, finished2 = in_order([finish_call(1), finish_call(2)])
    s.finished = s.finished | {1: finished1, 2: finished2}
    del s.mlp_came, s.mlp_came_far, s.mlp_rest, s.resid
    s.end()

    output_sent = from_sequences_send(s.output)
    s.out_far = send_far(s.out_near, (s.out_tail[1], s.out_head[1]), by_columns)
    s.down_far = far(*s.down_near)
    (finished,) = in_order([finish_call(0)])
    s.finished = s.finished | {0: finished}
    (s.odd,) = in_order([odd_call(s.normed, [s.finished[i][1] for i in range(4)])])
    s.gate_up_total = gate_up_total
    s.output_first = output_sent[0]
    del s.output
    s.end()

    my_group = me.astype(jnp.int32)[None]

    def whole_call(widths, own, other, part=0):
        return lambda first: whole_columns(my_group, first, other, widths, part), own

    s.gate_up_near = near(s.gate_up_total)
    s.qkv_came = across(s.odd, CORE)
    out_sum = total(s.out_near, s.out_far, (s.out_head[2], s.out_tail[2]), by_columns)
    s.out_chunks = jnp.split(out_sum.astype(low), shards, 0)
    s.out_ring = ring_sum_first(s.out_chunks)
    weights = [
        pair
        for i in range(4)
        for pair in (
            (s.own_blocks[2 * i], s.came[i]), (s.own_blocks[2 * i + 1], s.came_other[i])
        )
    ]
    blocks = [part for i in range(4) for part in s.finished[i][:2]]
    grad_in = rolled(back_to_rows(blocks, weights))
    x_unit = s.x_low.astype(full) * s.inverse_in
    s.gain_parts = jnp.concatenate(
        [
            jnp.sum(x_unit * grad_in, 0),
            s.mlp_gain_part,
            sum(s.backs[i][3] for i in range(4))[0],
            sum(s.finished[i][2] for i in range(4))[0],
        ]
    )
    s.grad_tokens = (
        s.grad_resid + norm_back(x_unit, s.inverse_in, grad_in * s.attn_gains)
    ).astype(low)
    del s.odd, s.out_near, s.out_far, s.out_head, s.out_tail, s.backs
    del s.own_blocks, s.came, s.came_other, s.grad_resid, s.x_low
    s.end()

    even = [s.finished[i][0] for i in range(4)]
    s.head0, s.tail0, s.head1, s.tail1 = in_order(
        [
            call(s.normed, even, s.qkv_came, half, range(half, 8, 2))
            for half in range(2)
            for call in (head_call, tail_call)
        ]
    )
    tokens_sent = from_sequences_send(s.grad_tokens)
    s.down_spread = jnp.concatenate([s.down_total, *s.down_near, *s.down_far], 0)
    s.down_spread_other = across(s.down_spread, CORE)
    s.output_second = output_sent[1]
    s.out_ring_last = around(rounded_sum(s.out_chunks[3], s.out_ring[0]), 1)
    s.gate_up_far = far(*s.gate_up_near)
    del s.qkv_came, s.finished, s.down_total, s.down_near, s.down_far
    s.end()

    def qkv_chunks(came, came_far, head, tail):
        own = total(came, came_far, (head[2], tail[2]), by_columns)
        return jnp.split(own.astype(low), shards, 0)

    s.near0 = send_near((s.head0[0], s.tail0[0]))
    s.gate_up_own = jnp.concatenate([s.gate_up_total, *s.gate_up_near, *s.gate_up_far], 0)
    s.gate_up_other = across(s.gate_up_own, CORE)
    (s.whole_down,) = in_order([whole_call((units,), s.down_spread, s.down_spread_other)])
    s.out_total = rounded_sum(s.out_chunks[0], s.out_ring[1], s.out_ring_last)
    s.tokens_first = tokens_sent[0]
    del s.down_spread, s.down_spread_other, s.out_chunks, s.out_ring, s.out_ring_last
    del s.gate_up_near, s.gate_up_far, s.gate_up_total
    s.end()

    s.far0 = send_far(s.near0, (s.tail0[1], s.head0[1]), by_columns)
    s.near1 = send_near((s.head1[0], s.tail1[0]))
    (s.whole_gate_up,) = in_order([whole_call((units, units), s.gate_up_own, s.gate_up_other)])
    s.tokens_second = tokens_sent[1]
    del s.gate_up_own, s.gate_up_other, s.grad_tokens
    s.end()

    s.chunks0 = qkv_chunks(s.near0, s.far0, s.head0, s.tail0)
    s.ring0 = ring_sum_first(s.chunks0)
    s.far1 = send_far(s.near1, (s.tail1[1], s.head1[1]), by_columns)
    s.gain_came = across(s.gain_parts, CORE)
    del s.near0, s.far0, s.head0, s.tail0
    s.end()

    s.last0 = around(rounded_sum(s.chunks0[3], s.ring0[0]), 1)
    s.chunks1 = qkv_chunks(s.near1, s.far1, s.head1, s.tail1)
    s.ring1 = ring_sum_first(s.chunks1)
    s.gain_parts = s.gain_parts + s.gain_came
    s.gain_came = across(s.gain_parts, ACROSS_X)
    del s.near1, s.far1, s.head1, s.tail1
    s.end()

    query_total = rounded_sum(s.chunks0[0], s.ring0[1], s.last0)
    s.total0 = jnp.concatenate([query_total, s.out_total], 1)
    s.spread0 = near(s.total0)
    s.last1 = around(rounded_sum(s.chunks1[3], s.ring1[0]), 1)
    s.gain_parts = s.gain_parts + s.gain_came
    s.gain_came = across(s.gain_parts, ACROSS_Y)
    del s.chunks0, s.ring0, s.last0, s.out_total
    s.end()

    s.spread_far0 = far(*s.spread0)
    s.total1 = rounded_sum(s.chunks1[0], s.ring1[1], s.last1)
    s.spread1 = near(s.total1)
    s.gain_parts = s.gain_parts + s.gain_came
    s.gain_came = lax.ppermute(s.gain_parts, "shard", [(i, i ^ 1) for i in range(shards)])
    del s.chunks1, s.ring1, s.last1
    s.end()

    s.own0 = jnp.concatenate([s.total0, *s.spread0, *s.spread_far0], 0)
    s.other0 = across(s.own0, CORE)
    s.spread_far1 = far(*s.spread1)
    s.gain_parts = s.gain_parts + s.gain_came
    s.gain_came = lax.ppermute(s.gain_parts, "shard", [(i, i ^ 2) for i in range(shards)])
    del s.total0, s.spread0, s.spread_far0
    s.end()

    s.own1 = jnp.concatenate([s.total1, *s.spread1, *s.spread_far1], 0)
    s.other1 = across(s.own1, CORE)
    (s.whole0,) = in_order([whole_call((head_columns, head_columns), s.own0, s.other0)])
    gain_sums = s.gain_parts + s.gain_came
    s.wide = lax.dynamic_slice_in_dim(
        gain_sums[: 2 * width].reshape(2, width), shard_at * piece, piece, 1
    )
    s.narrow = gain_sums[2 * width :]
    del s.own0, s.other0, s.total1, s.spread1, s.spread_far1
    s.end()

    ((whole_key, whole_value),) = in_order(
        [whole_call((head_dim, head_dim), s.own1, s.other1)]
    )
    return (
        jnp.stack(in_turn([s.output_first, s.output_second])),
        jnp.stack(in_turn([s.tokens_first, s.tokens_second])),
        s.wide[0],
        s.whole0[0],
        whole_key,
        whole_value,
        s.narrow[:head_dim],
        s.narrow[head_dim:],
        s.whole0[1],
        s.wide[1],
        *s.whole_gate_up,
        *s.whole_down,
    )


def solution(mesh):
    sizes = (mesh.shape["rep"], mesh.shape["shard"])
    return jax.shard_map(
        on_device_block if sizes == (8, 4) else on_device,
        mesh=mesh,
        in_specs=(
            P("rep", "shard", None),
            P("rep"),
            P("shard"),
            P("shard", None),
            P("shard", None),
            P("shard", None),
            P(),
            P(),
            P("shard", None),
            P("shard"),
            P("shard", None),
            P("shard", None),
            P("shard", None),
            P("rep", "shard", None),
        ),
        out_specs=(
            P("rep", "shard", None),
            P("rep", "shard", None),
            P("shard"),
            P("shard", None),
            P("shard", None),
            P("shard", None),
            P(),
            P(),
            P("shard", None),
            P("shard"),
            P("shard", None),
            P("shard", None),
            P("shard", None),
        ),
        check_vma=False,
    )
```

```python
import jax
import jax.numpy as jnp
from jax import lax
from jax.experimental import pallas as pl
from jax.experimental.pallas import tpu as pltpu
from jax.sharding import PartitionSpec as P

WINDOW = 512


EPS = 1e-06
ROPE_BASE = 1000000.0
NEG = -1e30


def passed_along(x, axis, by):
    devices = lax.axis_size(axis)
    pairs = [(i, i + by) for i in range(devices) if 0 <= i + by < devices]
    return lax.ppermute(x, axis, pairs)


def tables(positions, head_dim):
    half = head_dim // 2
    freq = ROPE_BASE ** (-jnp.arange(half, dtype=jnp.float32) * 2.0 / head_dim)
    angle = positions.astype(jnp.float32)[:, None] * freq[None, :]
    angle = jnp.concatenate([angle, angle], -1)
    return (jnp.cos(angle)[None, :, None, :], jnp.sin(angle)[None, :, None, :])


def rotated_rows(value_rows):
    half = value_rows.shape[-1] // 2
    return jnp.concatenate([-value_rows[..., half:], value_rows[..., :half]], -1)


def head_norm(raw, gain):
    inverse = lax.rsqrt(jnp.mean(raw * raw, -1, keepdims=True) + EPS)
    unit = raw * inverse
    return (unit, inverse, unit * gain)


def norm_back(unit, inverse, grad_unit):
    return inverse * (grad_unit - unit * jnp.mean(grad_unit * unit, -1, keepdims=True))


def head_norm_back(unit, inverse, grad_normed, gain):
    grad_raw = norm_back(unit, inverse, grad_normed * gain)
    return (grad_raw, jnp.sum(unit * grad_normed, axis=(0, 1, 2)))


def scores(query_rows, keys, allowed, scale):
    raw = (
        jnp.einsum("sqhgd,skhd->shgqk", query_rows, keys, preferred_element_type=jnp.float32)
        * scale
    )
    return jnp.where(allowed[:, None, None], raw, NEG)


def outer(left, right):
    return jnp.einsum("rc,rf->cf", left, right, preferred_element_type=jnp.float32)


def on_device(
    tokens,
    lengths,
    attn_gain,
    w_query,
    key_matrix,
    value_matrix,
    query_gain,
    key_gain,
    w_out,
    mlp_gain,
    w_gate,
    w_up,
    w_down,
    cotangent,
):
    seq_count, piece, width = tokens.shape
    head_dim = query_gain.shape[0]
    heads_q = w_query.shape[1] // head_dim
    heads_kv = key_matrix.shape[1] // head_dim
    groups = heads_q // heads_kv
    rows = seq_count * piece
    scale = head_dim ** (-0.5)
    reach = (WINDOW + piece - 2) // piece
    owned = width // lax.axis_size("shard")
    shard_at = lax.axis_index("shard")
    query_pos = shard_at * piece + jnp.arange(piece, dtype=jnp.int32)
    key_pos = (shard_at - reach) * piece + jnp.arange((reach + 1) * piece, dtype=jnp.int32)
    near = (
        (key_pos[None, :] <= query_pos[:, None])
        & (query_pos[:, None] - key_pos[None, :] < WINDOW)
        & (key_pos[None, :] >= 0)
    )
    live = (key_pos[None, None, :] < lengths[:, None, None]) | (
        key_pos[None, :] == query_pos[:, None]
    )[None]
    allowed = near[None] & live
    valid = (query_pos[None, :] < lengths[:, None]).astype(jnp.float32).reshape(rows, 1)
    cosine_table, sine_table = tables(query_pos, head_dim)
    x_rows = tokens.astype(jnp.float32).reshape(rows, width)
    inverse_in = lax.rsqrt(jnp.mean(x_rows * x_rows, -1, keepdims=True) + EPS)
    x_unit = x_rows * inverse_in
    gain_piece = lax.all_gather(attn_gain, "shard", axis=0, tiled=True)
    query_piece = lax.all_gather(w_query, "shard", axis=0, tiled=True)
    key_piece = lax.all_gather(key_matrix, "shard", axis=0, tiled=True)
    value_piece = lax.all_gather(value_matrix, "shard", axis=0, tiled=True)
    normed_piece = (x_unit * gain_piece.astype(jnp.float32)).astype(jnp.bfloat16)
    acc_q = jnp.dot(normed_piece, query_piece, preferred_element_type=jnp.float32)
    acc_k = jnp.dot(normed_piece, key_piece, preferred_element_type=jnp.float32)
    acc_v = jnp.dot(normed_piece, value_piece, preferred_element_type=jnp.float32)
    normalized_rows = normed_piece
    gains = gain_piece.astype(jnp.float32)
    attn_in = normalized_rows
    attn_gains = gains
    query_unit, query_inverse, query_rows_normalized = head_norm(
        acc_q.reshape(seq_count, piece, heads_q, head_dim), query_gain.astype(jnp.float32)
    )
    key_unit, key_inverse, key_normed = head_norm(
        acc_k.reshape(seq_count, piece, heads_kv, head_dim), key_gain.astype(jnp.float32)
    )
    query_rows = (
        (query_rows_normalized * cosine_table + rotated_rows(query_rows_normalized) * sine_table)
        .astype(jnp.bfloat16)
        .reshape(seq_count, piece, heads_kv, groups, head_dim)
    )
    keys_own = (key_normed * cosine_table + rotated_rows(key_normed) * sine_table).astype(
        jnp.bfloat16
    )
    values_own = acc_v.reshape(seq_count, piece, heads_kv, head_dim).astype(jnp.bfloat16)
    own_pair = jnp.stack([keys_own, values_own])
    parts = []
    for fetch_back in range(reach, 0, -1):
        parts.append(passed_along(own_pair, "shard", fetch_back))
    parts.append(own_pair)
    near_pair = jnp.concatenate(parts, 2)
    score = scores(query_rows, near_pair[0], allowed, scale)
    top = jnp.max(score, -1, keepdims=True)
    expo = jnp.exp(score - top)
    total = jnp.sum(expo, -1, keepdims=True)
    prob = expo / total
    log_total = top + jnp.log(total)
    mixed = jnp.einsum(
        "shgqk,skhd->sqhgd",
        prob.astype(jnp.bfloat16),
        near_pair[1],
        preferred_element_type=jnp.float32,
    )
    mixed_rows = mixed.reshape(rows, heads_q * head_dim).astype(jnp.bfloat16)
    resid = x_rows + jnp.einsum(
        "rf,nf->rn",
        mixed_rows,
        lax.all_gather(w_out, "shard", axis=0, tiled=True),
        preferred_element_type=jnp.float32,
    )
    inverse_mid = lax.rsqrt(jnp.mean(resid * resid, -1, keepdims=True) + EPS)
    mid_unit = resid * inverse_mid
    gain_piece = lax.all_gather(mlp_gain, "shard", axis=0, tiled=True)
    gate_piece = lax.all_gather(w_gate, "shard", axis=0, tiled=True)
    up_piece = lax.all_gather(w_up, "shard", axis=0, tiled=True)
    normed_piece = (mid_unit * gain_piece.astype(jnp.float32)).astype(jnp.bfloat16)
    acc_gate = jnp.dot(normed_piece, gate_piece, preferred_element_type=jnp.float32)
    acc_up = jnp.dot(normed_piece, up_piece, preferred_element_type=jnp.float32)
    normalized_rows = normed_piece
    gains = gain_piece.astype(jnp.float32)
    mlp_in = normalized_rows
    sigma = jax.nn.sigmoid(acc_gate)
    swish = acc_gate * sigma
    act = (swish * acc_up).astype(jnp.bfloat16)
    mlp_out = jnp.einsum(
        "rf,nf->rn",
        act,
        lax.all_gather(w_down, "shard", axis=0, tiled=True),
        preferred_element_type=jnp.float32,
    )
    output = (valid * (resid + mlp_out)).astype(jnp.bfloat16).reshape(seq_count, piece, width)
    grad_y = cotangent.astype(jnp.float32).reshape(rows, width) * valid
    grad_y_low = grad_y.astype(jnp.bfloat16)
    grad_act = jnp.dot(
        grad_y_low,
        lax.all_gather(w_down, "shard", axis=0, tiled=True),
        preferred_element_type=jnp.float32,
    )
    grad_gate = (grad_act * acc_up * sigma * (1.0 + acc_gate * (1.0 - sigma))).astype(jnp.bfloat16)
    grad_up = (grad_act * swish).astype(jnp.bfloat16)
    gate_piece, up_piece = lax.all_gather((w_gate, w_up), "shard", axis=0, tiled=True)
    grad_mid = jnp.einsum(
        "rf,nf->rn", grad_gate, gate_piece, preferred_element_type=jnp.float32
    ) + jnp.einsum("rf,nf->rn", grad_up, up_piece, preferred_element_type=jnp.float32)
    grad_resid = grad_y + norm_back(mid_unit, inverse_mid, grad_mid * gains)
    mlp_gain_part = jnp.sum(mid_unit * grad_mid, 0)
    normalized_rows = mlp_in
    mlp_grads = jax.tree.map(
        lambda part: lax.psum_scatter(
            part.astype(jnp.bfloat16), "shard", scatter_dimension=0, tiled=True
        ).astype(jnp.float32),
        (
            outer(normalized_rows, grad_gate),
            outer(normalized_rows, grad_up),
            outer(grad_y_low, act),
        ),
    )
    resid_low = grad_resid.astype(jnp.bfloat16)
    grad_mixed = jnp.dot(
        resid_low,
        lax.all_gather(w_out, "shard", axis=0, tiled=True),
        preferred_element_type=jnp.float32,
    )
    grad_mixed = grad_mixed.astype(jnp.bfloat16).reshape(
        seq_count, piece, heads_kv, groups, head_dim
    )
    prob_again = jnp.exp(scores(query_rows, near_pair[0], allowed, scale) - log_total)
    grad_prob = jnp.einsum(
        "sqhgd,skhd->shgqk", grad_mixed, near_pair[1], preferred_element_type=jnp.float32
    )
    grad_values = jnp.einsum(
        "shgqk,sqhgd->skhd",
        prob_again.astype(jnp.bfloat16),
        grad_mixed,
        preferred_element_type=jnp.float32,
    )
    grad_score = (
        prob_again * (grad_prob - jnp.sum(prob_again * grad_prob, -1, keepdims=True))
    ).astype(jnp.bfloat16)
    grad_queries = (
        jnp.einsum(
            "shgqk,skhd->sqhgd", grad_score, near_pair[0], preferred_element_type=jnp.float32
        )
        * scale
    )
    grad_keys = (
        jnp.einsum("shgqk,sqhgd->skhd", grad_score, query_rows, preferred_element_type=jnp.float32)
        * scale
    )
    grad_pair = jnp.stack([grad_keys, grad_values])
    own_grad = grad_pair[:, :, reach * piece :]
    for back in range(1, reach + 1):
        lower = (reach - back) * piece
        own_grad = own_grad + passed_along(grad_pair[:, :, lower : lower + piece], "shard", -back)
    grad_query_post = grad_queries.reshape(seq_count, piece, heads_q, head_dim)
    grad_query_normed = grad_query_post * cosine_table - rotated_rows(grad_query_post * sine_table)
    grad_key_normed = own_grad[0] * cosine_table - rotated_rows(own_grad[0] * sine_table)
    grad_query_raw, query_gain_grad = head_norm_back(
        query_unit, query_inverse, grad_query_normed, query_gain.astype(jnp.float32)
    )
    grad_key_raw, key_gain_grad = head_norm_back(
        key_unit, key_inverse, grad_key_normed, key_gain.astype(jnp.float32)
    )
    grad_query_low = grad_query_raw.reshape(rows, heads_q * head_dim).astype(jnp.bfloat16)
    grad_key_low = grad_key_raw.reshape(rows, heads_kv * head_dim).astype(jnp.bfloat16)
    grad_value_low = own_grad[1].reshape(rows, heads_kv * head_dim).astype(jnp.bfloat16)
    query_piece, key_piece, value_piece = lax.all_gather(
        (w_query, key_matrix, value_matrix), "shard", axis=0, tiled=True
    )
    grad_in = (
        jnp.einsum("rf,nf->rn", grad_query_low, query_piece, preferred_element_type=jnp.float32)
        + jnp.einsum("rf,nf->rn", grad_key_low, key_piece, preferred_element_type=jnp.float32)
        + jnp.einsum("rf,nf->rn", grad_value_low, value_piece, preferred_element_type=jnp.float32)
    )
    grad_tokens = (
        (grad_resid + norm_back(x_unit, inverse_in, grad_in * attn_gains))
        .astype(jnp.bfloat16)
        .reshape(seq_count, piece, width)
    )
    attn_gain_part = jnp.sum(x_unit * grad_in, 0)
    normalized_rows = attn_in
    attn_grads = jax.tree.map(
        lambda part: lax.psum_scatter(
            part.astype(jnp.bfloat16), "shard", scatter_dimension=0, tiled=True
        ).astype(jnp.float32),
        (
            outer(normalized_rows, grad_query_low),
            outer(normalized_rows, grad_key_low),
            outer(normalized_rows, grad_value_low),
            outer(resid_low, mixed_rows),
        ),
    )
    head_grads = lax.psum(
        (query_gain_grad, key_gain_grad, attn_gain_part, mlp_gain_part), ("rep", "shard")
    )
    attn_gain_total = lax.dynamic_slice_in_dim(head_grads[2], shard_at * owned, owned, 0)
    mlp_gain_total = lax.dynamic_slice_in_dim(head_grads[3], shard_at * owned, owned, 0)
    summed = (
        lax.psum(attn_grads[0].astype(jnp.bfloat16), "rep").astype(jnp.float32),
        lax.psum(attn_grads[1].astype(jnp.bfloat16), "rep").astype(jnp.float32),
        lax.psum(attn_grads[2].astype(jnp.bfloat16), "rep").astype(jnp.float32),
        lax.psum(attn_grads[3].astype(jnp.bfloat16), "rep").astype(jnp.float32),
        lax.psum(mlp_grads[0].astype(jnp.bfloat16), "rep").astype(jnp.float32),
        lax.psum(mlp_grads[1].astype(jnp.bfloat16), "rep").astype(jnp.float32),
        lax.psum(mlp_grads[2].astype(jnp.bfloat16), "rep").astype(jnp.float32),
    )
    attn_grads = summed[:4]
    mlp_grads = summed[4:]
    return (
        output,
        grad_tokens,
        attn_gain_total,
        attn_grads[0],
        attn_grads[1],
        attn_grads[2],
        head_grads[0],
        head_grads[1],
        attn_grads[3],
        mlp_gain_total,
        mlp_grads[0],
        mlp_grads[1],
        mlp_grads[2],
    )


CORE, ACROSS_X, ACROSS_Y = 1, 2, 4
VMEM_BYTES = 56 * 2**20
FREE = pl.CostEstimate(flops=1, bytes_accessed=1, transcendentals=0)


def across(x, mask):
    count = lax.axis_size("rep")
    return lax.ppermute(x, "rep", [(i, i ^ mask) for i in range(count)])


def around(x, by):
    count = lax.axis_size("shard")
    return lax.ppermute(x, "shard", [(i, (i + by) % count) for i in range(count)])


class Stage(dict):
    __getattr__ = dict.__getitem__
    __setattr__ = dict.__setitem__
    __delattr__ = dict.__delitem__

    def end(self):
        self.update(lax.optimization_barrier(dict(self)))


def in_order(calls):
    outs = []
    for call, first, *rest in calls:
        if outs:
            last = outs[-1][0] if isinstance(outs[-1], (list, tuple)) else outs[-1]
            first = lax.optimization_barrier((first, last))[0]
        outs.append(call(first, *rest))
    return outs


def ring_sum_first(chunks):
    return around(chunks[2], 1), around(chunks[1], -1)


def near(piece):
    return across(piece, ACROSS_X), across(piece, ACROSS_Y)


def far(from_x, from_y):
    half = from_x.shape[0] // 2
    return across(from_x[:half], ACROSS_Y), across(from_y[half:], ACROSS_X)


def rounded_sum(*parts):
    return sum(part.astype(jnp.float32) for part in parts).astype(jnp.bfloat16)


def sequence_pairs(turn):
    groups, shards = lax.axis_size("rep"), lax.axis_size("shard")
    pairs = []
    for group in range(groups):
        chip, core = divmod(group, 2)
        for at in range(shards):
            to_group, to_shard = 2 * chip + at // 2, 2 * core + (turn ^ (at & 1))
            pairs.append((group * shards + at, to_group * shards + to_shard))
    return pairs


def rolled(x):
    count, at = lax.axis_size("shard"), lax.axis_index("shard")
    width = x.shape[1] // count
    return jnp.concatenate(
        [lax.dynamic_slice_in_dim(x, ((at - i) % count) * width, width, 1) for i in range(count)],
        1,
    )


def sequence_cuts(x):
    odd = lax.axis_index("shard") & 1
    return [lax.dynamic_index_in_dim(x, turn ^ odd, 0, keepdims=False) for turn in range(2)]


def to_sequence(cut, turn):
    return lax.ppermute(cut, ("rep", "shard"), sequence_pairs(turn))


def from_sequences_send(x):
    odd = lax.axis_index("shard") & 1
    x = x.reshape(2, x.shape[0] // 2, x.shape[1])
    return [
        lax.ppermute(
            lax.dynamic_index_in_dim(x, turn ^ odd, 0, keepdims=False),
            ("rep", "shard"),
            [(to, at) for at, to in sequence_pairs(turn)],
        )
        for turn in range(2)
    ]


def in_turn(came):
    even = lax.axis_index("shard") & 1 == 0
    return [jnp.where(even, came[0], came[1]), jnp.where(even, came[1], came[0])]


def column_block(weights, at):
    cuts = [w.shape[1] // 8 for w in weights]
    return jnp.concatenate(
        [lax.dynamic_slice_in_dim(w, at * cut, cut, 1) for w, cut in zip(weights, cuts)], 1
    )


def whole_columns(me, own, other, widths, part=0):
    rows, columns = own.shape[0] // 4, sum(widths)

    def body(me_ref, own_ref, other_ref, *outs):
        def put(block):
            start = 0
            for out, width in zip(outs, widths):
                out[...] = block[:, start : start + width].astype(jnp.float32)
                start += width

        mine = (me_ref[0] ^ pl.program_id(0)) & 1 == 0
        pl.when(mine)(lambda: put(own_ref))
        pl.when(jnp.logical_not(mine))(lambda: put(other_ref))

    spec = pl.BlockSpec((rows, columns), lambda i, at: ((at[0] ^ i) >> 1, part))
    return pl.pallas_call(
        body,
        grid_spec=pltpu.PrefetchScalarGridSpec(
            num_scalar_prefetch=1,
            grid=(8,),
            in_specs=[spec, spec],
            out_specs=[pl.BlockSpec((rows, w), lambda i, at: (0, i)) for w in widths],
        ),
        out_shape=[jax.ShapeDtypeStruct((rows, 8 * w), jnp.float32) for w in widths],
        compiler_params=pltpu.CompilerParams(vmem_limit_bytes=VMEM_BYTES),
        cost_estimate=FREE,
        name="whole_columns",
    )(me, own, other)


def turned(x):
    return pltpu.roll(x, x.shape[-1] // 2, x.ndim - 1)


def nt(left, right):
    return lax.dot_general(
        left, right, (((1,), (1,)), ((), ())), preferred_element_type=jnp.float32
    )


def tn(left, right):
    return lax.dot_general(
        left, right, (((0,), (0,)), ((), ())), preferred_element_type=jnp.float32
    )


def unit_of(raw):
    inverse = lax.rsqrt(jnp.mean(raw * raw, -1, keepdims=True) + EPS)
    return raw * inverse, inverse


def project_body(
    normed, own0, came0, own1, came1, cosine, sine, gains, raw, query, key_value
):
    step = own0.shape[0]
    dim = cosine.shape[1]
    for block, (own, came) in enumerate(((own0, came0), (own1, came1))):
        at = block * 4 * dim
        raw[:, at : at + 4 * dim] = jnp.dot(
            normed[:, :step], own[...], preferred_element_type=jnp.float32
        ) + jnp.dot(normed[:, step:], came[...], preferred_element_type=jnp.float32)
        for i in range(3):
            unit, _ = unit_of(raw[:, at + i * dim : at + (i + 1) * dim])
            head = unit * gains[i // 2 : i // 2 + 1, :]
            head = (head * cosine[...] + turned(head) * sine[...]).astype(jnp.bfloat16)
            if i < 2:
                query[:, (2 * block + i) * dim : (2 * block + i + 1) * dim] = head
            else:
                key_value[:, 2 * block * dim : (2 * block + 1) * dim] = head
        key_value[:, (2 * block + 1) * dim : (2 * block + 2) * dim] = raw[
            :, at + 3 * dim : at + 4 * dim
        ].astype(jnp.bfloat16)


def window_mask(info, part, rows, columns):
    half = columns - rows
    row = lax.broadcasted_iota(jnp.int32, (rows, columns), 0)
    column = lax.broadcasted_iota(jnp.int32, (rows, columns), 1)
    gap = column - row - half
    slot = column + ((info[0] - 1) * half + part * rows)
    allowed = (gap <= 0) & (gap > -half) & (slot >= 0) & ((slot < info[1]) | (gap == 0))
    mask = jnp.where(allowed, 0.0, NEG)
    return jnp.concatenate([mask, mask], 0)


def two_heads(ref, at, block, dim):
    return jnp.concatenate(
        [ref[at, h * dim : (h + 1) * dim] for h in (2 * block, 2 * block + 1)], 0
    )


def key_columns(block, dim):
    key = slice(2 * block * dim, (2 * block + 1) * dim)
    value = slice((2 * block + 1) * dim, (2 * block + 2) * dim)
    return key, value


def seen_pair(before, own, part, block, dim):
    here, there = key_columns(block, dim), key_columns(1 - block, dim)
    rows = own.shape[0] // 2
    if part == 0:
        return [
            jnp.concatenate([before[:, t], own[:rows, h]], 0) for h, t in zip(here, there)
        ]
    return [jnp.concatenate([before[rows:, t], own[:, h]], 0) for h, t in zip(here, there)]


def attend_body(info, query, before, own, mixed, log_total):
    dim = own.shape[1] // 4
    rows = query.shape[0] // 2
    for part in range(2):
        at = slice(part * rows, (part + 1) * rows)
        mask = window_mask(info, part, rows, 3 * rows)
        for block in range(2):
            keys, values = seen_pair(before, own, part, block, dim)
            score = nt(two_heads(query, at, block, dim), keys) * dim**-0.5 + mask
            top = jnp.max(score, -1, keepdims=True)
            expo = jnp.exp(score - top)
            total = jnp.sum(expo, -1, keepdims=True)
            prob = (expo * (1.0 / total)).astype(jnp.bfloat16)
            out = jnp.dot(prob, values, preferred_element_type=jnp.float32).astype(jnp.bfloat16)
            log = jnp.broadcast_to(top + jnp.log(total), (2 * rows, dim))
            for i in range(2):
                on = slice((2 * block + i) * dim, (2 * block + i + 1) * dim)
                mixed[at, on] = out[i * rows : (i + 1) * rows]
                log_total[at, on] = log[i * rows : (i + 1) * rows]


def attend_back_body(
    info, query, before, own, log_total, grad_resid, weight0, weight1, raw, cosine, sine, gain,
    grad_query, grad_own, grad_before, gain_part, grad_keys, grad_values, grad_mixed,
):
    dim = own.shape[1] // 4
    rows = query.shape[0] // 2
    scale = dim**-0.5
    gain_total = jnp.zeros((1, dim), jnp.float32)
    masks = [window_mask(info, part, rows, 3 * rows) for part in range(2)]
    for block, weight in enumerate((weight0, weight1)):
        on = slice(2 * block * dim, 2 * (block + 1) * dim)
        grad_mixed[:, on] = jnp.dot(
            grad_resid[...], weight[...], preferred_element_type=jnp.float32
        ).astype(jnp.bfloat16)
        grad_keys[...] = jnp.zeros_like(grad_keys)
        grad_values[...] = jnp.zeros_like(grad_values)
        for part in range(2):
            keys, values = seen_pair(before, own, part, block, dim)
            at = slice(part * rows, (part + 1) * rows)
            seen = slice(part * rows, part * rows + 3 * rows)
            queries = two_heads(query, at, block, dim)
            grads = two_heads(grad_mixed, at, block, dim)
            log = two_heads(log_total, at, block, dim)[:, :1]
            prob = jnp.exp(nt(queries, keys) * scale + masks[part] - log)
            grad_prob = nt(grads, values)
            inner = jnp.sum(prob * grad_prob, -1, keepdims=True)
            grad_score = (prob * (grad_prob - inner)).astype(jnp.bfloat16)
            grad_values[seen, :] += tn(prob.astype(jnp.bfloat16), grads)
            grad_keys[seen, :] += tn(grad_score, queries) * scale
            both = jnp.dot(grad_score, keys, preferred_element_type=jnp.float32) * scale
            for i in range(2):
                head = 2 * block + i
                back = both[i * rows : (i + 1) * rows]
                back = back * cosine[at, :] - turned(back) * sine[at, :]
                there = (2 * head - head % 2) * dim
                unit, inverse = unit_of(raw[at, there : there + dim])
                gain_total += jnp.sum(unit * back, 0, keepdims=True)
                back = back * gain[...]
                back = inverse * (back - unit * jnp.mean(back * unit, -1, keepdims=True))
                grad_query[at, head * dim : (head + 1) * dim] = back.astype(jnp.bfloat16)
        for grad, here, there in zip(
            (grad_keys, grad_values), key_columns(block, dim), key_columns(1 - block, dim)
        ):
            grad_before[:, there] = grad[: 2 * rows, :].astype(jnp.bfloat16)
            grad_own[:, here] = grad[2 * rows :, :]
    gain_part[...] = gain_total


def finish_body(grad_query, grad_own, came, raw, cosine, sine, gain, even, odd, gain_part):
    dim = cosine.shape[1]
    total = jnp.zeros((1, dim), jnp.float32)
    for block, out in enumerate((even, odd)):
        key, value = key_columns(block, dim)
        back = grad_own[:, key] + came[:, key].astype(jnp.float32)
        back = back * cosine[...] - turned(back) * sine[...]
        unit, inverse = unit_of(raw[:, (4 * block + 2) * dim : (4 * block + 3) * dim])
        total += jnp.sum(unit * back, 0, keepdims=True)
        back = back * gain[...]
        back = inverse * (back - unit * jnp.mean(back * unit, -1, keepdims=True))
        out[:, : 2 * dim] = grad_query[:, 2 * block * dim : (2 * block + 2) * dim]
        out[:, 2 * dim : 3 * dim] = back.astype(jnp.bfloat16)
        grad_value = grad_own[:, value] + came[:, value].astype(jnp.float32)
        out[:, 3 * dim :] = grad_value.astype(jnp.bfloat16)
    gain_part[...] = total


def vmem_call(body, outs, scratch=(), scalars=0, name=None):
    def call(*args):
        in_specs = [
            pl.BlockSpec(memory_space=pltpu.SMEM if i < scalars else pltpu.VMEM)
            for i in range(len(args))
        ]
        return pl.pallas_call(
            body,
            grid=(1,),
            out_shape=outs,
            in_specs=in_specs,
            out_specs=jax.tree.map(lambda _: pl.BlockSpec(memory_space=pltpu.VMEM), outs),
            scratch_shapes=scratch,
            compiler_params=pltpu.CompilerParams(vmem_limit_bytes=VMEM_BYTES),
        cost_estimate=FREE,
            name=name,
        )(*args)

    return call


def hidden_units(mids, grads_y, weights):
    width, units = weights.shape[0], weights.shape[1] // 3
    count = len(mids)
    heights = [m.shape[0] for m in mids]
    rows, cut = sum(heights), units // 3

    def body(*refs):
        gate_w, up_w, w_down, act, grad_gate, grad_up = refs[2 * count :]
        start = 0
        for mid, grad_y in zip(refs[:count], refs[count : 2 * count]):
            at = slice(start, start + mid.shape[0])
            start += mid.shape[0]
            gate = jnp.dot(mid[...], gate_w[...], preferred_element_type=jnp.float32)
            up = jnp.dot(mid[...], up_w[...], preferred_element_type=jnp.float32)
            grad_act = jnp.dot(grad_y[...], w_down[...], preferred_element_type=jnp.float32)
            sigma = jax.nn.sigmoid(gate)
            swish = gate * sigma
            act[at, :] = (swish * up).astype(jnp.bfloat16)
            slope = grad_act * up * sigma * (1.0 + gate * (1.0 - sigma))
            grad_gate[at, :] = slope.astype(jnp.bfloat16)
            grad_up[at, :] = (grad_act * swish).astype(jnp.bfloat16)

    row_specs = [
        pl.BlockSpec((h, width), lambda j: (0, 0), pipeline_mode=pl.Buffered(1)) for h in heights
    ]
    return pl.pallas_call(
        body,
        grid=(3,),
        out_shape=[jax.ShapeDtypeStruct((rows, units), jnp.bfloat16)] * 3,
        in_specs=[
            *row_specs,
            *row_specs,
            pl.BlockSpec((width, cut), lambda j: (0, j)),
            pl.BlockSpec((width, cut), lambda j: (0, j + 3)),
            pl.BlockSpec((width, cut), lambda j: (0, j + 6)),
        ],
        out_specs=[pl.BlockSpec((rows, cut), lambda j: (0, j))] * 3,
        compiler_params=pltpu.CompilerParams(vmem_limit_bytes=VMEM_BYTES),
        cost_estimate=FREE,
        name="hidden_units",
    )(*mids, *grads_y, weights, weights, weights)


def from_hidden(pairs, eighths):
    count, parts = len(pairs), len(eighths)
    rows, units = pairs[0][0].shape[0] // 8, pairs[0][0].shape[1]
    width = pairs[0][1].shape[0]
    cut = width // 4

    def body(*refs):
        ins, outs = refs[: -(parts // 2)], refs[-(parts // 2) :]
        total = 0.0
        for i in range(count):
            part = ins[i * (parts + 1) : (i + 1) * (parts + 1)]
            left = jnp.concatenate([p[...] for p in part[:-1]], 0)
            total = total + nt(left, part[-1][...])
        for i, out in enumerate(outs):
            out[...] = total[2 * i * rows : 2 * (i + 1) * rows].astype(jnp.bfloat16)

    specs, args = [], []
    for left, right, at in pairs:
        specs += [pl.BlockSpec((rows, units), lambda j, e=e: (e, 0)) for e in eighths]
        specs.append(pl.BlockSpec((cut, units), lambda j, at=at: (j, at)))
        args += [left] * parts + [right]
    return pl.pallas_call(
        body,
        grid=(4,),
        out_shape=[jax.ShapeDtypeStruct((2 * rows, width), jnp.bfloat16)] * (parts // 2),
        in_specs=specs,
        out_specs=[pl.BlockSpec((2 * rows, cut), lambda j: (0, j))] * (parts // 2),
        compiler_params=pltpu.CompilerParams(vmem_limit_bytes=VMEM_BYTES),
        cost_estimate=FREE,
        name="from_hidden",
    )(*args)


def row_outer(lefts, groups, first, tiles, added=None, places=None, part=None):
    rights = [right for group in groups for right in group]
    places = range(len(rights)) if places is None else places
    added = [] if added is None else [added] * len(rights)
    width = lefts[0].shape[1]
    tile = width // 8
    count = len(lefts)
    rows = sum(left.shape[0] for left in lefts)
    wide = rights[0].shape[1] // (1 if part is None else 2)
    columns = [wide * len(group) for group in groups]

    def body(*refs):
        left_refs = refs[:count]
        right_refs = refs[count : count + len(rights)]
        add_refs = refs[count + len(rights) : count + len(rights) + len(added)]
        outs = refs[count + len(rights) + len(added) :]
        place = 0
        for i, group in enumerate(groups):
            column = 0
            for _ in group:
                on = slice(column, column + wide)
                total, start = 0.0, 0
                for left in left_refs:
                    stop = start + left.shape[0]
                    total = total + tn(left[...], right_refs[place][start:stop, :])
                    start = stop
                if added:
                    total = total + add_refs[place][...].astype(jnp.float32)
                outs[i][:, on] = total.astype(jnp.bfloat16)
                place += 1
                column += wide

    return pl.pallas_call(
        body,
        grid=(tiles,),
        out_shape=[jax.ShapeDtypeStruct((tiles * tile, c), jnp.bfloat16) for c in columns],
        in_specs=[
            *(pl.BlockSpec((left.shape[0], tile), lambda j: (0, j + first)) for left in lefts),
            *(
                pl.BlockSpec(
                    (right.shape[0], wide), lambda j: (0, part or 0), pipeline_mode=pl.Buffered(1)
                )
                for right in rights
            ),
            *(
                pl.BlockSpec((tile, wide), lambda j, at=at: (j + first, at))
                for at in places[: len(added)]
            ),
        ],
        out_specs=[pl.BlockSpec((tile, c), lambda j: (j, 0)) for c in columns],
        compiler_params=pltpu.CompilerParams(vmem_limit_bytes=VMEM_BYTES),
        cost_estimate=pl.CostEstimate(
            flops=2 * rows * tiles * tile * sum(columns),
            bytes_accessed=2 * rows * (width + sum(columns)),
            transcendentals=0,
        ),
        name="row_outer",
    )(*lefts, *rights, *added)


def close_body(x, *refs):
    mixed, weights = refs[:4], refs[4:12]
    gains, resid, mid = refs[12:]
    at = pl.program_id(0)
    step = x.shape[1]
    columns = weights[0].shape[1]
    total = x[...].astype(jnp.float32)
    for i in range(8):
        part = mixed[i // 2][:, (i % 2) * columns : (i % 2 + 1) * columns]
        total = total + nt(part, weights[i][...])
    resid[:, pl.ds(pl.multiple_of(at * step, step), step)] = total

    @pl.when(at == 3)
    def _():
        unit, _ = unit_of(resid[...])
        mid[...] = (unit * gains[...]).astype(jnp.bfloat16)


def close_attention(x, mixed, weights, gains):
    rows, width = x.shape
    step = width // 4
    whole = lambda a: pl.BlockSpec(a.shape, lambda j: (0, 0))
    return pl.pallas_call(
        close_body,
        grid=(4,),
        out_shape=[
            jax.ShapeDtypeStruct((rows, width), jnp.float32),
            jax.ShapeDtypeStruct((rows, width), jnp.bfloat16),
        ],
        in_specs=[
            pl.BlockSpec((rows, step), lambda j: (0, j)),
            *(whole(m) for m in mixed),
            *(pl.BlockSpec((step, w.shape[1]), lambda j: (j, 0)) for w in weights),
            whole(gains),
        ],
        out_specs=[pl.BlockSpec((rows, width), lambda j: (0, 0))] * 2,
        compiler_params=pltpu.CompilerParams(vmem_limit_bytes=VMEM_BYTES),
        cost_estimate=FREE,
        name="close_attention",
    )(x, *mixed, *weights, gains)


def back_to_rows(blocks, weights):
    rows = blocks[0].shape[0]
    step, columns = weights[0][0].shape
    count = len(blocks)

    def body(*refs):
        lefts = refs[:count]
        hbm = refs[count : 3 * count]
        out = refs[3 * count]
        held, sems = refs[3 * count + 1 :]
        copies = []
        for i in range(count):
            own, came = hbm[2 * i : 2 * i + 2]
            copies.append(
                [
                    pltpu.make_async_copy(own, held.at[i, :step], sems.at[i, 0]),
                    pltpu.make_async_copy(came, held.at[i, step:], sems.at[i, 1]),
                ]
            )
        for some in copies:
            for copy in some:
                copy.start()
        for i in range(count):
            for copy in copies[i]:
                copy.wait()
            for k in range(4):
                on = slice(k * step, (k + 1) * step)
                part = nt(lefts[i][...], held[i, on])
                if i == 0:
                    out[:, on] = part
                else:
                    out[:, on] += part

    return pl.pallas_call(
        body,
        grid=(1,),
        out_shape=jax.ShapeDtypeStruct((rows, 4 * step), jnp.float32),
        in_specs=[pl.BlockSpec(memory_space=pltpu.VMEM)] * count
        + [pl.BlockSpec(memory_space=pl.ANY)] * (2 * count),
        out_specs=pl.BlockSpec(memory_space=pltpu.VMEM),
        scratch_shapes=[
            pltpu.VMEM((count, 4 * step, columns), jnp.bfloat16),
            pltpu.SemaphoreType.DMA((count, 2)),
        ],
        compiler_params=pltpu.CompilerParams(vmem_limit_bytes=VMEM_BYTES),
        cost_estimate=FREE,
        name="back_to_rows",
    )(*blocks, *(part for w in weights for part in w))


def on_device_block(
    tokens,
    lengths,
    attn_gain,
    w_query,
    key_matrix,
    value_matrix,
    query_gain,
    key_gain,
    w_out,
    mlp_gain,
    w_gate,
    w_up,
    w_down,
    cotangent,
):
    low, full = jnp.bfloat16, jnp.float32
    width = tokens.shape[2]
    head_dim = query_gain.shape[0]
    shards = lax.axis_size("shard")
    shard_at = lax.axis_index("shard")
    me = lax.axis_index("rep")
    core = me & 1
    count = lax.axis_size("rep")

    s = Stage()
    piece = width // shards

    s.own_blocks = [
        column_block((w_query, key_matrix, value_matrix), me ^ i) for i in range(8)
    ]
    gain_rows = jnp.concatenate(
        [jnp.stack([attn_gain, mlp_gain]), jnp.zeros((14, piece), low)], 0
    )
    travelling = jnp.concatenate([s.own_blocks[0], gain_rows], 0)
    s.tokens_cuts, s.cotangent_cuts = sequence_cuts(tokens), sequence_cuts(cotangent)
    s.out_block = column_block((w_out,), me)
    s.ffn_block = column_block((w_gate, w_up, w_down), me)
    s.before, s.behind = around(travelling, 1), around(travelling, -1)
    s.other_lengths = across(lengths, CORE)
    s.end()

    s.ahead = around(s.before, 1)
    tokens_sent = [to_sequence(cut, turn) for turn, cut in enumerate(s.tokens_cuts)]
    out_own = lax.all_gather(s.out_block, "shard", axis=0, tiled=True)
    del s.out_block, s.tokens_cuts
    s.end()

    parts = (s.before, s.ahead, s.behind)
    s.came = jnp.concatenate([part[:piece] for part in parts], 0)
    s.gains = jnp.concatenate([gain_rows[:2], *(part[piece : piece + 2] for part in parts)], 1)
    s.came_near = near(s.came)
    s.came_own = across(s.came, CORE)
    s.x_came = tokens_sent
    del s.before, s.behind, s.ahead
    s.end()

    grad_y_sent = [to_sequence(cut, turn) for turn, cut in enumerate(s.cotangent_cuts)]
    s.came_far = far(*s.came_near)
    s.came_other = [s.came_own, *(across(block, CORE) for block in s.came_near)]
    gains = rolled(s.gains.astype(full))
    s.mlp_gains = gains[1:]
    s.attn_gains = gains[:1]
    s.x_low = jnp.concatenate(in_turn(s.x_came), 0)
    rows = s.x_low.shape[0]
    x_rows = s.x_low.astype(full)
    s.inverse_in = lax.rsqrt(jnp.mean(x_rows * x_rows, -1, keepdims=True) + EPS)
    s.normed = rolled((x_rows * s.inverse_in * s.attn_gains).astype(low))
    query_gains = query_gain.astype(full)[None]
    key_gains = key_gain.astype(full)[None]
    s.head_gains = jnp.concatenate([query_gains, key_gains], 0)
    both = jnp.where(
        core == 0,
        jnp.concatenate([lengths, s.other_lengths]),
        jnp.concatenate([s.other_lengths, lengths]),
    )
    length = lax.dynamic_index_in_dim(both, shard_at, 0, keepdims=False)
    s.info = jnp.stack([core, length]).astype(jnp.int32)
    query_pos = core * rows + jnp.arange(rows, dtype=jnp.int32)
    s.valid = (query_pos < length)[:, None].astype(full)
    cosine, sine = tables(query_pos, head_dim)
    s.cosine, sine = cosine[0, :, 0], sine[0, :, 0]
    s.sine = jnp.concatenate([-sine[:, : head_dim // 2], sine[:, head_dim // 2 :]], 1)
    s.out_own = out_own
    del s.gains, s.x_came, s.other_lengths, s.cotangent_cuts, s.came_own
    s.end()

    head_columns = 2 * head_dim
    block_columns = 4 * head_dim
    quad_rows = jax.ShapeDtypeStruct((rows, block_columns), low)
    quad_sums = jax.ShapeDtypeStruct((rows, block_columns), full)
    gain_sum = jax.ShapeDtypeStruct((1, head_dim), full)
    project = vmem_call(
        project_body,
        [jax.ShapeDtypeStruct((rows, 2 * block_columns), full), quad_rows, quad_rows],
        name="project",
    )
    attend = vmem_call(attend_body, [quad_rows, quad_sums], scalars=1, name="attend")
    attend_back = vmem_call(
        attend_back_body,
        [quad_rows, quad_sums, quad_rows, gain_sum],
        scratch=[pltpu.VMEM((2 * rows, head_dim), full)] * 2
        + [pltpu.VMEM((rows, block_columns), low)],
        scalars=1,
        name="attend_back",
    )
    finish = vmem_call(finish_body, [quad_rows, quad_rows, gain_sum], name="finish")
    upward = [(i, i + 1) for i in range(0, count, 2)]
    downward = [(i + 1, i) for i in range(0, count, 2)]

    def project_call(i, came, other):
        return (
            project, s.normed, s.own_blocks[2 * i], came, s.own_blocks[2 * i + 1], other,
            s.cosine, s.sine, s.head_gains,
        )

    def attend_call(projected, earlier):
        return (
            lambda query, own, before: attend(s.info, query, before, own),
            *projected[1:], earlier,
        )

    came_last = jnp.concatenate(s.came_far, 0)
    s.came_last = (came_last, across(came_last, CORE))
    s.out_near = near(s.out_own)
    s.out_own_other = across(s.out_own, CORE)
    s.projected = in_order(
        [
            project_call(i, block, other)
            for i, (block, other) in enumerate(zip((s.came, *s.came_near), s.came_other))
        ]
    )
    s.grad_y_came = grad_y_sent
    del s.came_far
    s.end()

    ffn_own = lax.all_gather(s.ffn_block, "shard", axis=0, tiled=True)
    grad_y = jnp.concatenate(in_turn(s.grad_y_came), 0)
    s.grad_y = jnp.where(s.valid > 0, grad_y, jnp.zeros_like(grad_y))
    grad_y_near = near(s.grad_y)
    s.out_far = far(*s.out_near)
    s.out_near_other = [across(block, CORE) for block in s.out_near]
    s.earlier = [lax.ppermute(p[2], "rep", upward) for p in s.projected]
    (s.projected_last,) = in_order([project_call(3, *s.came_last)])
    del s.ffn_block, s.grad_y_came
    s.end()

    out_last = jnp.concatenate(s.out_far, 0)
    s.out_last = (out_last, across(out_last, CORE))
    s.earlier_last = lax.ppermute(s.projected_last[2], "rep", upward)
    s.attended = in_order([attend_call(*pair) for pair in zip(s.projected, s.earlier)])
    s.grad_y_near = grad_y_near
    del s.out_far
    s.end()

    s.projected = [*s.projected, s.projected_last]
    s.earlier = [*s.earlier, s.earlier_last]
    s.out_blocks = [
        s.out_own, s.out_own_other, s.out_near[0], s.out_near_other[0], s.out_near[1],
        s.out_near_other[1], *s.out_last,
    ]
    (last,) = in_order([attend_call(s.projected_last, s.earlier_last)])
    s.attended = [*s.attended, last]
    s.mixed = [a[0] for a in s.attended]
    s.resid, s.mid = close_attention(s.x_low, s.mixed, s.out_blocks, s.mlp_gains)
    s.grad_y_far = far(*s.grad_y_near)
    s.came = [s.came, *s.came_near, s.came_last[0]]
    s.came_other = [*s.came_other, s.came_last[1]]
    del s.came_near, s.came_last
    del s.out_own, s.out_own_other, s.out_near, s.out_near_other, s.out_last
    del s.projected_last, s.earlier_last
    s.end()

    s.mid_near = near(s.mid)
    s.end()

    s.mid_far = far(*s.mid_near)
    s.ffn_own = ffn_own
    s.end()

    s.mids = [s.mid, *s.mid_near, *s.mid_far]
    s.grads_y = [s.grad_y, *s.grad_y_near, *s.grad_y_far]
    s.ffn_other = across(s.ffn_own, CORE)
    units = s.ffn_own.shape[1] // 3
    s.hidden_own = hidden_units(s.mids, s.grads_y, s.ffn_own)
    del s.mid, s.mid_near, s.mid_far, s.grad_y_near, s.grad_y_far
    s.end()

    def gate_up_pairs():
        return [
            (hidden[i], weights, i - 1)
            for hidden, weights in ((s.hidden_own, s.ffn_own), (s.hidden_other, s.ffn_other))
            for i in (1, 2)
        ]

    def down_pairs():
        return [(s.hidden_own[0], s.ffn_own, 2), (s.hidden_other[0], s.ffn_other, 2)]

    def from_hidden_call(pairs, eighths):
        return (
            lambda first: from_hidden([(first, *pairs[0][1:]), *pairs[1:]], eighths),
            pairs[0][0],
        )

    def outer_call(lefts, rights, *added):
        return lambda first: row_outer(lefts, [[first, *rights[1:]]], 0, 8, *added)[0], rights[0]

    def send_near(sent):
        return across(sent[0], ACROSS_X), across(sent[1], ACROSS_Y)

    def send_far(came, rest, split):
        one_tail, two_head = rest
        return (
            across(rounded_sum(one_tail, split(came[1])[1]), ACROSS_X),
            across(rounded_sum(two_head, split(came[0])[1]), ACROSS_Y),
        )

    def total(came, came_far, own, split):
        head, tail = own
        full_sum = lambda *parts: sum(part.astype(full) for part in parts)
        return jnp.concatenate(
            [
                full_sum(head, split(came[0])[0], came_far[1]),
                full_sum(tail, split(came[1])[0], came_far[0]),
            ],
            0,
        )

    by_rows = lambda a: jnp.split(a, 2, 0)
    by_columns = lambda a: jnp.split(a, 2, 1)
    to_plane, rest_of_plane = (2, 6, 5, 7), (3, 4, 0, 1)

    s.hidden_other = hidden_units(s.mids, s.grads_y, s.ffn_other)
    (s.down_outer,) = in_order([outer_call(s.grads_y, s.hidden_other[:1])])
    s.end()

    s.down_came = across(s.down_outer, CORE)
    s.mid_sent = from_hidden(gate_up_pairs(), to_plane)
    del s.down_outer
    s.end()

    s.mid_came = send_near(s.mid_sent)
    s.down_mine, s.mid_rest, s.gate_up_outer = in_order(
        [
            outer_call(s.grads_y, s.hidden_own[:1], s.down_came),
            from_hidden_call(gate_up_pairs(), rest_of_plane),
            outer_call(s.mids, s.hidden_other[1:]),
        ]
    )
    del s.mid_sent, s.down_came
    s.end()

    down_total = lax.psum_scatter(s.down_mine, "shard", scatter_dimension=0, tiled=True)
    s.mid_came_far = send_far(s.mid_came, by_rows(s.mid_rest[0]), by_rows)
    s.gate_up_came = across(s.gate_up_outer, CORE)
    s.mlp_sent, s.mlp_rest = in_order(
        [
            from_hidden_call(down_pairs(), to_plane),
            from_hidden_call(down_pairs(), rest_of_plane),
        ]
    )
    del s.gate_up_outer, s.down_mine
    s.end()

    def back_call(i):
        raw, query, own_pair = s.projected[i]
        return (
            lambda query, *rest: attend_back(s.info, query, *rest),
            query, s.earlier[i], own_pair, s.attended[i][1], s.resid_low,
            *s.out_blocks[2 * i : 2 * i + 2], raw, s.cosine, s.sine, s.head_gains[:1],
        )

    def finish_call(i):
        return (
            finish, s.backs[i][0], s.backs[i][1], s.returned[i], s.projected[i][0],
            s.cosine, s.sine, s.head_gains[1:],
        )

    def give_back(*chips):
        s.returned = s.returned | {
            i: lax.ppermute(s.backs[i][2], "rep", downward) for i in chips
        }

    def odd_call(left, blocks, part=None):
        return lambda first: row_outer([first], [blocks], 0, 8, part=part)[0], left

    def head_call(left, blocks, came, part=None, places=(0, 1, 2, 3)):
        groups = [[blocks[1], blocks[3]], [blocks[2]], [blocks[0]]]
        at = [places[i] for i in (1, 3, 2, 0)]
        return lambda first: row_outer([first], groups, 0, 4, came, at, part), left

    def tail_call(left, blocks, came, part=None, places=(0, 1, 2, 3)):
        groups = [[blocks[2], blocks[3]], [blocks[1]], [blocks[0]]]
        at = [places[i] for i in (2, 3, 1, 0)]
        return lambda first: row_outer([first], groups, 4, 4, came, at, part), left

    s.mlp_came = send_near(s.mlp_sent)
    grad_mid = total(s.mid_came, s.mid_came_far, by_rows(s.mid_rest[1]), by_rows)
    inverse_mid = lax.rsqrt(jnp.mean(s.resid * s.resid, -1, keepdims=True) + EPS)
    mid_unit = s.resid * inverse_mid
    s.mlp_gain_part = jnp.sum(mid_unit * grad_mid, 0)
    s.grad_resid = s.grad_y.astype(full) + norm_back(
        mid_unit, inverse_mid, grad_mid * s.mlp_gains
    )
    s.resid_low = s.grad_resid.astype(low)
    s.resid_rolled = rolled(s.resid_low)
    s.returned = {}
    back, s.out_odd, s.gate_up_mine = in_order(
        [
            back_call(3),
            odd_call(s.resid_rolled, s.mixed, 1),
            outer_call(s.mids, s.hidden_own[1:], s.gate_up_came),
        ]
    )
    s.backs = {3: back}
    s.down_total = down_total
    del s.mid_came, s.mid_came_far, s.mid_rest, s.gate_up_came, s.hidden_own, s.hidden_other
    del s.mids, s.grads_y, s.ffn_own, s.ffn_other, s.mlp_sent
    s.end()

    gate_up_total = lax.psum_scatter(s.gate_up_mine, "shard", scatter_dimension=0, tiled=True)
    s.mlp_came_far = send_far(s.mlp_came, by_rows(s.mlp_rest[0]), by_rows)
    s.out_came = across(s.out_odd, CORE)
    give_back(3)
    back1, back2 = in_order([back_call(1), back_call(2)])
    s.backs = s.backs | {1: back1, 2: back2}
    del s.out_odd, s.gate_up_mine
    s.end()

    s.down_near = near(s.down_total)
    give_back(1, 2)
    s.out_head, s.out_tail = in_order(
        [
            head_call(s.resid_rolled, s.mixed, s.out_came, 0),
            tail_call(s.resid_rolled, s.mixed, s.out_came, 0),
        ]
    )
    del s.out_came
    s.end()

    s.out_near = send_near((s.out_head[0], s.out_tail[0]))
    back, finished = in_order([back_call(0), finish_call(3)])
    s.backs = s.backs | {0: back}
    s.finished = {3: finished}
    s.end()

    s.out_far = send_far(s.out_near, (s.out_tail[1], s.out_head[1]), by_columns)
    s.down_far = far(*s.down_near)
    mlp_out = total(s.mlp_came, s.mlp_came_far, by_rows(s.mlp_rest[1]), by_rows)
    s.output = (s.valid * (s.resid + mlp_out)).astype(low)
    give_back(0)
    finished1, finished2 = in_order([finish_call(1), finish_call(2)])
    s.finished = s.finished | {1: finished1, 2: finished2}
    s.gate_up_total = gate_up_total
    del s.mlp_came, s.mlp_came_far, s.mlp_rest, s.resid
    s.end()

    output_sent = from_sequences_send(s.output)
    gate_up_near = near(s.gate_up_total)
    (finished,) = in_order([finish_call(0)])
    s.finished = s.finished | {0: finished}
    (s.odd,) = in_order([odd_call(s.normed, [s.finished[i][1] for i in range(4)])])
    s.end()

    my_group = me.astype(jnp.int32)[None]

    def whole_call(widths, own, other, part=0):
        return lambda first: whole_columns(my_group, first, other, widths, part), own

    s.qkv_came = across(s.odd, CORE)
    out_sum = total(s.out_near, s.out_far, (s.out_head[2], s.out_tail[2]), by_columns)
    s.out_chunks = jnp.split(out_sum.astype(low), shards, 0)
    weights = [
        pair
        for i in range(4)
        for pair in (
            (s.own_blocks[2 * i], s.came[i]), (s.own_blocks[2 * i + 1], s.came_other[i])
        )
    ]
    blocks = [part for i in range(4) for part in s.finished[i][:2]]
    grad_in = rolled(back_to_rows(blocks, weights))
    x_unit = s.x_low.astype(full) * s.inverse_in
    s.gain_parts = jnp.concatenate(
        [
            jnp.sum(x_unit * grad_in, 0),
            s.mlp_gain_part,
            sum(s.backs[i][3] for i in range(4))[0],
            sum(s.finished[i][2] for i in range(4))[0],
        ]
    )
    s.grad_tokens = (
        s.grad_resid + norm_back(x_unit, s.inverse_in, grad_in * s.attn_gains)
    ).astype(low)
    s.down_spread = jnp.concatenate([s.down_total, *s.down_near, *s.down_far], 0)
    s.down_spread_other = across(s.down_spread, CORE)
    s.gate_up_near = gate_up_near
    s.output_first = output_sent[0]
    del s.odd, s.out_near, s.out_far, s.out_head, s.out_tail, s.backs, s.output
    del s.own_blocks, s.came, s.came_other, s.grad_resid, s.x_low
    del s.down_total, s.down_near, s.down_far
    s.end()

    even = [s.finished[i][0] for i in range(4)]
    s.head0, s.tail0, s.head1, s.tail1 = in_order(
        [
            call(s.normed, even, s.qkv_came, half, range(half, 8, 2))
            for half in range(2)
            for call in (head_call, tail_call)
        ]
    )
    tokens_sent = from_sequences_send(s.grad_tokens)
    s.output_second = output_sent[1]
    s.out_ring = ring_sum_first(s.out_chunks)
    s.gate_up_far = far(*s.gate_up_near)
    del s.qkv_came, s.finished
    s.end()

    def qkv_chunks(came, came_far, head, tail):
        own = total(came, came_far, (head[2], tail[2]), by_columns)
        return jnp.split(own.astype(low), shards, 0)

    s.near0 = send_near((s.head0[0], s.tail0[0]))
    s.gate_up_own = jnp.concatenate([s.gate_up_total, *s.gate_up_near, *s.gate_up_far], 0)
    s.gate_up_other = across(s.gate_up_own, CORE)
    (s.whole_down,) = in_order([whole_call((units,), s.down_spread, s.down_spread_other)])
    s.out_ring_last = around(rounded_sum(s.out_chunks[3], s.out_ring[0]), 1)
    s.tokens_first = tokens_sent[0]
    del s.down_spread, s.down_spread_other
    del s.gate_up_near, s.gate_up_far, s.gate_up_total
    s.end()

    s.far0 = send_far(s.near0, (s.tail0[1], s.head0[1]), by_columns)
    s.near1 = send_near((s.head1[0], s.tail1[0]))
    s.out_total = rounded_sum(s.out_chunks[0], s.out_ring[1], s.out_ring_last)
    (s.whole_gate_up,) = in_order([whole_call((units, units), s.gate_up_own, s.gate_up_other)])
    s.tokens_second = tokens_sent[1]
    del s.gate_up_own, s.gate_up_other, s.grad_tokens
    del s.out_chunks, s.out_ring, s.out_ring_last
    s.end()

    s.chunks0 = qkv_chunks(s.near0, s.far0, s.head0, s.tail0)
    s.ring0 = ring_sum_first(s.chunks0)
    s.far1 = send_far(s.near1, (s.tail1[1], s.head1[1]), by_columns)
    s.gain_came = across(s.gain_parts, CORE)
    del s.near0, s.far0, s.head0, s.tail0
    s.end()

    s.last0 = around(rounded_sum(s.chunks0[3], s.ring0[0]), 1)
    s.chunks1 = qkv_chunks(s.near1, s.far1, s.head1, s.tail1)
    s.ring1 = ring_sum_first(s.chunks1)
    s.gain_parts = s.gain_parts + s.gain_came
    s.gain_came = across(s.gain_parts, ACROSS_X)
    del s.near1, s.far1, s.head1, s.tail1
    s.end()

    query_total = rounded_sum(s.chunks0[0], s.ring0[1], s.last0)
    s.total0 = jnp.concatenate([query_total, s.out_total], 1)
    s.spread0 = near(s.total0)
    s.last1 = around(rounded_sum(s.chunks1[3], s.ring1[0]), 1)
    s.gain_parts = s.gain_parts + s.gain_came
    s.gain_came = across(s.gain_parts, ACROSS_Y)
    del s.chunks0, s.ring0, s.last0, s.out_total
    s.end()

    s.spread_far0 = far(*s.spread0)
    s.total1 = rounded_sum(s.chunks1[0], s.ring1[1], s.last1)
    s.spread1 = near(s.total1)
    s.gain_parts = s.gain_parts + s.gain_came
    s.gain_came = lax.ppermute(s.gain_parts, "shard", [(i, i ^ 1) for i in range(shards)])
    del s.chunks1, s.ring1, s.last1
    s.end()

    s.own0 = jnp.concatenate([s.total0, *s.spread0, *s.spread_far0], 0)
    s.other0 = across(s.own0, CORE)
    s.spread_far1 = far(*s.spread1)
    s.gain_parts = s.gain_parts + s.gain_came
    s.gain_came = lax.ppermute(s.gain_parts, "shard", [(i, i ^ 2) for i in range(shards)])
    del s.total0, s.spread0, s.spread_far0
    s.end()

    s.own1 = jnp.concatenate([s.total1, *s.spread1, *s.spread_far1], 0)
    s.other1 = across(s.own1, CORE)
    (s.whole0,) = in_order([whole_call((head_columns, head_columns), s.own0, s.other0)])
    gain_sums = s.gain_parts + s.gain_came
    s.wide = lax.dynamic_slice_in_dim(
        gain_sums[: 2 * width].reshape(2, width), shard_at * piece, piece, 1
    )
    s.narrow = gain_sums[2 * width :]
    del s.own0, s.other0, s.total1, s.spread1, s.spread_far1
    s.end()

    ((whole_key, whole_value),) = in_order(
        [whole_call((head_dim, head_dim), s.own1, s.other1)]
    )
    return (
        jnp.stack(in_turn([s.output_first, s.output_second])),
        jnp.stack(in_turn([s.tokens_first, s.tokens_second])),
        s.wide[0],
        s.whole0[0],
        whole_key,
        whole_value,
        s.narrow[:head_dim],
        s.narrow[head_dim:],
        s.whole0[1],
        s.wide[1],
        *s.whole_gate_up,
        *s.whole_down,
    )


def solution(mesh):
    sizes = (mesh.shape["rep"], mesh.shape["shard"])
    return jax.shard_map(
        on_device_block if sizes == (8, 4) else on_device,
        mesh=mesh,
        in_specs=(
            P("rep", "shard", None),
            P("rep"),
            P("shard"),
            P("shard", None),
            P("shard", None),
            P("shard", None),
            P(),
            P(),
            P("shard", None),
            P("shard"),
            P("shard", None),
            P("shard", None),
            P("shard", None),
            P("rep", "shard", None),
        ),
        out_specs=(
            P("rep", "shard", None),
            P("rep", "shard", None),
            P("shard"),
            P("shard", None),
            P("shard", None),
            P("shard", None),
            P(),
            P(),
            P("shard", None),
            P("shard"),
            P("shard", None),
            P("shard", None),
            P("shard", None),
        ),
        check_vma=False,
    )
```

```python
import jax
import jax.numpy as jnp
from jax import lax
from jax.experimental import pallas as pl
from jax.experimental.pallas import tpu as pltpu
from jax.sharding import PartitionSpec as P

WINDOW = 512


EPS = 1e-06
ROPE_BASE = 1000000.0
NEG = -1e30


def passed_along(x, axis, by):
    devices = lax.axis_size(axis)
    pairs = [(i, i + by) for i in range(devices) if 0 <= i + by < devices]
    return lax.ppermute(x, axis, pairs)


def tables(positions, head_dim):
    half = head_dim // 2
    freq = ROPE_BASE ** (-jnp.arange(half, dtype=jnp.float32) * 2.0 / head_dim)
    angle = positions.astype(jnp.float32)[:, None] * freq[None, :]
    angle = jnp.concatenate([angle, angle], -1)
    return (jnp.cos(angle)[None, :, None, :], jnp.sin(angle)[None, :, None, :])


def rotated_rows(value_rows):
    half = value_rows.shape[-1] // 2
    return jnp.concatenate([-value_rows[..., half:], value_rows[..., :half]], -1)


def head_norm(raw, gain):
    inverse = lax.rsqrt(jnp.mean(raw * raw, -1, keepdims=True) + EPS)
    unit = raw * inverse
    return (unit, inverse, unit * gain)


def norm_back(unit, inverse, grad_unit):
    return inverse * (grad_unit - unit * jnp.mean(grad_unit * unit, -1, keepdims=True))


def head_norm_back(unit, inverse, grad_normed, gain):
    grad_raw = norm_back(unit, inverse, grad_normed * gain)
    return (grad_raw, jnp.sum(unit * grad_normed, axis=(0, 1, 2)))


def scores(query_rows, keys, allowed, scale):
    raw = (
        jnp.einsum("sqhgd,skhd->shgqk", query_rows, keys, preferred_element_type=jnp.float32)
        * scale
    )
    return jnp.where(allowed[:, None, None], raw, NEG)


def outer(left, right):
    return jnp.einsum("rc,rf->cf", left, right, preferred_element_type=jnp.float32)


def on_device(
    tokens,
    lengths,
    attn_gain,
    w_query,
    key_matrix,
    value_matrix,
    query_gain,
    key_gain,
    w_out,
    mlp_gain,
    w_gate,
    w_up,
    w_down,
    cotangent,
):
    seq_count, piece, width = tokens.shape
    head_dim = query_gain.shape[0]
    heads_q = w_query.shape[1] // head_dim
    heads_kv = key_matrix.shape[1] // head_dim
    groups = heads_q // heads_kv
    rows = seq_count * piece
    scale = head_dim ** (-0.5)
    reach = (WINDOW + piece - 2) // piece
    owned = width // lax.axis_size("shard")
    shard_at = lax.axis_index("shard")
    query_pos = shard_at * piece + jnp.arange(piece, dtype=jnp.int32)
    key_pos = (shard_at - reach) * piece + jnp.arange((reach + 1) * piece, dtype=jnp.int32)
    near = (
        (key_pos[None, :] <= query_pos[:, None])
        & (query_pos[:, None] - key_pos[None, :] < WINDOW)
        & (key_pos[None, :] >= 0)
    )
    live = (key_pos[None, None, :] < lengths[:, None, None]) | (
        key_pos[None, :] == query_pos[:, None]
    )[None]
    allowed = near[None] & live
    valid = (query_pos[None, :] < lengths[:, None]).astype(jnp.float32).reshape(rows, 1)
    cosine_table, sine_table = tables(query_pos, head_dim)
    x_rows = tokens.astype(jnp.float32).reshape(rows, width)
    inverse_in = lax.rsqrt(jnp.mean(x_rows * x_rows, -1, keepdims=True) + EPS)
    x_unit = x_rows * inverse_in
    gain_piece = lax.all_gather(attn_gain, "shard", axis=0, tiled=True)
    query_piece = lax.all_gather(w_query, "shard", axis=0, tiled=True)
    key_piece = lax.all_gather(key_matrix, "shard", axis=0, tiled=True)
    value_piece = lax.all_gather(value_matrix, "shard", axis=0, tiled=True)
    normed_piece = (x_unit * gain_piece.astype(jnp.float32)).astype(jnp.bfloat16)
    acc_q = jnp.dot(normed_piece, query_piece, preferred_element_type=jnp.float32)
    acc_k = jnp.dot(normed_piece, key_piece, preferred_element_type=jnp.float32)
    acc_v = jnp.dot(normed_piece, value_piece, preferred_element_type=jnp.float32)
    normalized_rows = normed_piece
    gains = gain_piece.astype(jnp.float32)
    attn_in = normalized_rows
    attn_gains = gains
    query_unit, query_inverse, query_rows_normalized = head_norm(
        acc_q.reshape(seq_count, piece, heads_q, head_dim), query_gain.astype(jnp.float32)
    )
    key_unit, key_inverse, key_normed = head_norm(
        acc_k.reshape(seq_count, piece, heads_kv, head_dim), key_gain.astype(jnp.float32)
    )
    query_rows = (
        (query_rows_normalized * cosine_table + rotated_rows(query_rows_normalized) * sine_table)
        .astype(jnp.bfloat16)
        .reshape(seq_count, piece, heads_kv, groups, head_dim)
    )
    keys_own = (key_normed * cosine_table + rotated_rows(key_normed) * sine_table).astype(
        jnp.bfloat16
    )
    values_own = acc_v.reshape(seq_count, piece, heads_kv, head_dim).astype(jnp.bfloat16)
    own_pair = jnp.stack([keys_own, values_own])
    parts = []
    for fetch_back in range(reach, 0, -1):
        parts.append(passed_along(own_pair, "shard", fetch_back))
    parts.append(own_pair)
    near_pair = jnp.concatenate(parts, 2)
    score = scores(query_rows, near_pair[0], allowed, scale)
    top = jnp.max(score, -1, keepdims=True)
    expo = jnp.exp(score - top)
    total = jnp.sum(expo, -1, keepdims=True)
    prob = expo / total
    log_total = top + jnp.log(total)
    mixed = jnp.einsum(
        "shgqk,skhd->sqhgd",
        prob.astype(jnp.bfloat16),
        near_pair[1],
        preferred_element_type=jnp.float32,
    )
    mixed_rows = mixed.reshape(rows, heads_q * head_dim).astype(jnp.bfloat16)
    resid = x_rows + jnp.einsum(
        "rf,nf->rn",
        mixed_rows,
        lax.all_gather(w_out, "shard", axis=0, tiled=True),
        preferred_element_type=jnp.float32,
    )
    inverse_mid = lax.rsqrt(jnp.mean(resid * resid, -1, keepdims=True) + EPS)
    mid_unit = resid * inverse_mid
    gain_piece = lax.all_gather(mlp_gain, "shard", axis=0, tiled=True)
    gate_piece = lax.all_gather(w_gate, "shard", axis=0, tiled=True)
    up_piece = lax.all_gather(w_up, "shard", axis=0, tiled=True)
    normed_piece = (mid_unit * gain_piece.astype(jnp.float32)).astype(jnp.bfloat16)
    acc_gate = jnp.dot(normed_piece, gate_piece, preferred_element_type=jnp.float32)
    acc_up = jnp.dot(normed_piece, up_piece, preferred_element_type=jnp.float32)
    normalized_rows = normed_piece
    gains = gain_piece.astype(jnp.float32)
    mlp_in = normalized_rows
    sigma = jax.nn.sigmoid(acc_gate)
    swish = acc_gate * sigma
    act = (swish * acc_up).astype(jnp.bfloat16)
    mlp_out = jnp.einsum(
        "rf,nf->rn",
        act,
        lax.all_gather(w_down, "shard", axis=0, tiled=True),
        preferred_element_type=jnp.float32,
    )
    output = (valid * (resid + mlp_out)).astype(jnp.bfloat16).reshape(seq_count, piece, width)
    grad_y = cotangent.astype(jnp.float32).reshape(rows, width) * valid
    grad_y_low = grad_y.astype(jnp.bfloat16)
    grad_act = jnp.dot(
        grad_y_low,
        lax.all_gather(w_down, "shard", axis=0, tiled=True),
        preferred_element_type=jnp.float32,
    )
    grad_gate = (grad_act * acc_up * sigma * (1.0 + acc_gate * (1.0 - sigma))).astype(jnp.bfloat16)
    grad_up = (grad_act * swish).astype(jnp.bfloat16)
    gate_piece, up_piece = lax.all_gather((w_gate, w_up), "shard", axis=0, tiled=True)
    grad_mid = jnp.einsum(
        "rf,nf->rn", grad_gate, gate_piece, preferred_element_type=jnp.float32
    ) + jnp.einsum("rf,nf->rn", grad_up, up_piece, preferred_element_type=jnp.float32)
    grad_resid = grad_y + norm_back(mid_unit, inverse_mid, grad_mid * gains)
    mlp_gain_part = jnp.sum(mid_unit * grad_mid, 0)
    normalized_rows = mlp_in
    mlp_grads = jax.tree.map(
        lambda part: lax.psum_scatter(
            part.astype(jnp.bfloat16), "shard", scatter_dimension=0, tiled=True
        ).astype(jnp.float32),
        (
            outer(normalized_rows, grad_gate),
            outer(normalized_rows, grad_up),
            outer(grad_y_low, act),
        ),
    )
    resid_low = grad_resid.astype(jnp.bfloat16)
    grad_mixed = jnp.dot(
        resid_low,
        lax.all_gather(w_out, "shard", axis=0, tiled=True),
        preferred_element_type=jnp.float32,
    )
    grad_mixed = grad_mixed.astype(jnp.bfloat16).reshape(
        seq_count, piece, heads_kv, groups, head_dim
    )
    prob_again = jnp.exp(scores(query_rows, near_pair[0], allowed, scale) - log_total)
    grad_prob = jnp.einsum(
        "sqhgd,skhd->shgqk", grad_mixed, near_pair[1], preferred_element_type=jnp.float32
    )
    grad_values = jnp.einsum(
        "shgqk,sqhgd->skhd",
        prob_again.astype(jnp.bfloat16),
        grad_mixed,
        preferred_element_type=jnp.float32,
    )
    grad_score = (
        prob_again * (grad_prob - jnp.sum(prob_again * grad_prob, -1, keepdims=True))
    ).astype(jnp.bfloat16)
    grad_queries = (
        jnp.einsum(
            "shgqk,skhd->sqhgd", grad_score, near_pair[0], preferred_element_type=jnp.float32
        )
        * scale
    )
    grad_keys = (
        jnp.einsum("shgqk,sqhgd->skhd", grad_score, query_rows, preferred_element_type=jnp.float32)
        * scale
    )
    grad_pair = jnp.stack([grad_keys, grad_values])
    own_grad = grad_pair[:, :, reach * piece :]
    for back in range(1, reach + 1):
        lower = (reach - back) * piece
        own_grad = own_grad + passed_along(grad_pair[:, :, lower : lower + piece], "shard", -back)
    grad_query_post = grad_queries.reshape(seq_count, piece, heads_q, head_dim)
    grad_query_normed = grad_query_post * cosine_table - rotated_rows(grad_query_post * sine_table)
    grad_key_normed = own_grad[0] * cosine_table - rotated_rows(own_grad[0] * sine_table)
    grad_query_raw, query_gain_grad = head_norm_back(
        query_unit, query_inverse, grad_query_normed, query_gain.astype(jnp.float32)
    )
    grad_key_raw, key_gain_grad = head_norm_back(
        key_unit, key_inverse, grad_key_normed, key_gain.astype(jnp.float32)
    )
    grad_query_low = grad_query_raw.reshape(rows, heads_q * head_dim).astype(jnp.bfloat16)
    grad_key_low = grad_key_raw.reshape(rows, heads_kv * head_dim).astype(jnp.bfloat16)
    grad_value_low = own_grad[1].reshape(rows, heads_kv * head_dim).astype(jnp.bfloat16)
    query_piece, key_piece, value_piece = lax.all_gather(
        (w_query, key_matrix, value_matrix), "shard", axis=0, tiled=True
    )
    grad_in = (
        jnp.einsum("rf,nf->rn", grad_query_low, query_piece, preferred_element_type=jnp.float32)
        + jnp.einsum("rf,nf->rn", grad_key_low, key_piece, preferred_element_type=jnp.float32)
        + jnp.einsum("rf,nf->rn", grad_value_low, value_piece, preferred_element_type=jnp.float32)
    )
    grad_tokens = (
        (grad_resid + norm_back(x_unit, inverse_in, grad_in * attn_gains))
        .astype(jnp.bfloat16)
        .reshape(seq_count, piece, width)
    )
    attn_gain_part = jnp.sum(x_unit * grad_in, 0)
    normalized_rows = attn_in
    attn_grads = jax.tree.map(
        lambda part: lax.psum_scatter(
            part.astype(jnp.bfloat16), "shard", scatter_dimension=0, tiled=True
        ).astype(jnp.float32),
        (
            outer(normalized_rows, grad_query_low),
            outer(normalized_rows, grad_key_low),
            outer(normalized_rows, grad_value_low),
            outer(resid_low, mixed_rows),
        ),
    )
    head_grads = lax.psum(
        (query_gain_grad, key_gain_grad, attn_gain_part, mlp_gain_part), ("rep", "shard")
    )
    attn_gain_total = lax.dynamic_slice_in_dim(head_grads[2], shard_at * owned, owned, 0)
    mlp_gain_total = lax.dynamic_slice_in_dim(head_grads[3], shard_at * owned, owned, 0)
    summed = (
        lax.psum(attn_grads[0].astype(jnp.bfloat16), "rep").astype(jnp.float32),
        lax.psum(attn_grads[1].astype(jnp.bfloat16), "rep").astype(jnp.float32),
        lax.psum(attn_grads[2].astype(jnp.bfloat16), "rep").astype(jnp.float32),
        lax.psum(attn_grads[3].astype(jnp.bfloat16), "rep").astype(jnp.float32),
        lax.psum(mlp_grads[0].astype(jnp.bfloat16), "rep").astype(jnp.float32),
        lax.psum(mlp_grads[1].astype(jnp.bfloat16), "rep").astype(jnp.float32),
        lax.psum(mlp_grads[2].astype(jnp.bfloat16), "rep").astype(jnp.float32),
    )
    attn_grads = summed[:4]
    mlp_grads = summed[4:]
    return (
        output,
        grad_tokens,
        attn_gain_total,
        attn_grads[0],
        attn_grads[1],
        attn_grads[2],
        head_grads[0],
        head_grads[1],
        attn_grads[3],
        mlp_gain_total,
        mlp_grads[0],
        mlp_grads[1],
        mlp_grads[2],
    )


CORE, ACROSS_X, ACROSS_Y = 1, 2, 4
VMEM_BYTES = 56 * 2**20
FREE = pl.CostEstimate(flops=1, bytes_accessed=1, transcendentals=0)


def across(x, mask):
    count = lax.axis_size("rep")
    return lax.ppermute(x, "rep", [(i, i ^ mask) for i in range(count)])


def around(x, by):
    count = lax.axis_size("shard")
    return lax.ppermute(x, "shard", [(i, (i + by) % count) for i in range(count)])


class Stage(dict):
    __getattr__ = dict.__getitem__
    __setattr__ = dict.__setitem__
    __delattr__ = dict.__delitem__

    def end(self):
        self.update(lax.optimization_barrier(dict(self)))


def in_order(calls):
    outs = []
    for call, first, *rest in calls:
        if outs:
            last = outs[-1][0] if isinstance(outs[-1], (list, tuple)) else outs[-1]
            first = lax.optimization_barrier((first, last))[0]
        outs.append(call(first, *rest))
    return outs


def ring_sum_first(chunks):
    return around(chunks[2], 1), around(chunks[1], -1)


def near(piece):
    return across(piece, ACROSS_X), across(piece, ACROSS_Y)


def far(from_x, from_y):
    half = from_x.shape[0] // 2
    return across(from_x[:half], ACROSS_Y), across(from_y[half:], ACROSS_X)


def rounded_sum(*parts):
    return sum(part.astype(jnp.float32) for part in parts).astype(jnp.bfloat16)


def sequence_pairs(turn):
    groups, shards = lax.axis_size("rep"), lax.axis_size("shard")
    pairs = []
    for group in range(groups):
        chip, core = divmod(group, 2)
        for at in range(shards):
            to_group, to_shard = 2 * chip + at // 2, 2 * core + (turn ^ (at & 1))
            pairs.append((group * shards + at, to_group * shards + to_shard))
    return pairs


def rolled(x):
    count, at = lax.axis_size("shard"), lax.axis_index("shard")
    width = x.shape[1] // count
    return jnp.concatenate(
        [lax.dynamic_slice_in_dim(x, ((at - i) % count) * width, width, 1) for i in range(count)],
        1,
    )


def sequence_cuts(x):
    odd = lax.axis_index("shard") & 1
    return [lax.dynamic_index_in_dim(x, turn ^ odd, 0, keepdims=False) for turn in range(2)]


def to_sequence(cut, turn):
    return lax.ppermute(cut, ("rep", "shard"), sequence_pairs(turn))


def from_sequences_send(x):
    odd = lax.axis_index("shard") & 1
    x = x.reshape(2, x.shape[0] // 2, x.shape[1])
    return [
        lax.ppermute(
            lax.dynamic_index_in_dim(x, turn ^ odd, 0, keepdims=False),
            ("rep", "shard"),
            [(to, at) for at, to in sequence_pairs(turn)],
        )
        for turn in range(2)
    ]


def in_turn(came):
    even = lax.axis_index("shard") & 1 == 0
    return [jnp.where(even, came[0], came[1]), jnp.where(even, came[1], came[0])]


def column_block(weights, at):
    cuts = [w.shape[1] // 8 for w in weights]
    return jnp.concatenate(
        [lax.dynamic_slice_in_dim(w, at * cut, cut, 1) for w, cut in zip(weights, cuts)], 1
    )


def whole_columns(me, own, other, widths, part=0):
    rows, columns = own.shape[0] // 4, sum(widths)

    def body(me_ref, own_ref, other_ref, *outs):
        def put(block):
            start = 0
            for out, width in zip(outs, widths):
                out[...] = block[:, start : start + width].astype(jnp.float32)
                start += width

        mine = (me_ref[0] ^ pl.program_id(0)) & 1 == 0
        pl.when(mine)(lambda: put(own_ref))
        pl.when(jnp.logical_not(mine))(lambda: put(other_ref))

    spec = pl.BlockSpec((rows, columns), lambda i, at: ((at[0] ^ i) >> 1, part))
    return pl.pallas_call(
        body,
        grid_spec=pltpu.PrefetchScalarGridSpec(
            num_scalar_prefetch=1,
            grid=(8,),
            in_specs=[spec, spec],
            out_specs=[pl.BlockSpec((rows, w), lambda i, at: (0, i)) for w in widths],
        ),
        out_shape=[jax.ShapeDtypeStruct((rows, 8 * w), jnp.float32) for w in widths],
        compiler_params=pltpu.CompilerParams(vmem_limit_bytes=VMEM_BYTES),
        cost_estimate=FREE,
        name="whole_columns",
    )(me, own, other)


def turned(x):
    return pltpu.roll(x, x.shape[-1] // 2, x.ndim - 1)


def nt(left, right):
    return lax.dot_general(
        left, right, (((1,), (1,)), ((), ())), preferred_element_type=jnp.float32
    )


def tn(left, right):
    return lax.dot_general(
        left, right, (((0,), (0,)), ((), ())), preferred_element_type=jnp.float32
    )


def unit_of(raw):
    inverse = lax.rsqrt(jnp.mean(raw * raw, -1, keepdims=True) + EPS)
    return raw * inverse, inverse


def project_body(
    normed, own0, came0, own1, came1, cosine, sine, gains, raw, query, key_value
):
    step = own0.shape[0]
    dim = cosine.shape[1]
    for block, (own, came) in enumerate(((own0, came0), (own1, came1))):
        at = block * 4 * dim
        raw[:, at : at + 4 * dim] = jnp.dot(
            normed[:, :step], own[...], preferred_element_type=jnp.float32
        ) + jnp.dot(normed[:, step:], came[...], preferred_element_type=jnp.float32)
        for i in range(3):
            unit, _ = unit_of(raw[:, at + i * dim : at + (i + 1) * dim])
            head = unit * gains[i // 2 : i // 2 + 1, :]
            head = (head * cosine[...] + turned(head) * sine[...]).astype(jnp.bfloat16)
            if i < 2:
                query[:, (2 * block + i) * dim : (2 * block + i + 1) * dim] = head
            else:
                key_value[:, 2 * block * dim : (2 * block + 1) * dim] = head
        key_value[:, (2 * block + 1) * dim : (2 * block + 2) * dim] = raw[
            :, at + 3 * dim : at + 4 * dim
        ].astype(jnp.bfloat16)


def window_mask(info, part, rows, columns):
    half = columns - rows
    row = lax.broadcasted_iota(jnp.int32, (rows, columns), 0)
    column = lax.broadcasted_iota(jnp.int32, (rows, columns), 1)
    gap = column - row - half
    slot = column + ((info[0] - 1) * half + part * rows)
    allowed = (gap <= 0) & (gap > -half) & (slot >= 0) & ((slot < info[1]) | (gap == 0))
    mask = jnp.where(allowed, 0.0, NEG)
    return jnp.concatenate([mask, mask], 0)


def two_heads(ref, at, block, dim):
    return jnp.concatenate(
        [ref[at, h * dim : (h + 1) * dim] for h in (2 * block, 2 * block + 1)], 0
    )


def key_columns(block, dim):
    key = slice(2 * block * dim, (2 * block + 1) * dim)
    value = slice((2 * block + 1) * dim, (2 * block + 2) * dim)
    return key, value


def seen_pair(before, own, part, block, dim):
    here, there = key_columns(block, dim), key_columns(1 - block, dim)
    rows = own.shape[0] // 2
    if part == 0:
        return [
            jnp.concatenate([before[:, t], own[:rows, h]], 0) for h, t in zip(here, there)
        ]
    return [jnp.concatenate([before[rows:, t], own[:, h]], 0) for h, t in zip(here, there)]


def attend_body(info, query, before, own, mixed, log_total):
    dim = own.shape[1] // 4
    rows = query.shape[0] // 2
    for part in range(2):
        at = slice(part * rows, (part + 1) * rows)
        mask = window_mask(info, part, rows, 3 * rows)
        for block in range(2):
            keys, values = seen_pair(before, own, part, block, dim)
            score = nt(two_heads(query, at, block, dim), keys) * dim**-0.5 + mask
            top = jnp.max(score, -1, keepdims=True)
            expo = jnp.exp(score - top)
            total = jnp.sum(expo, -1, keepdims=True)
            prob = (expo * (1.0 / total)).astype(jnp.bfloat16)
            out = jnp.dot(prob, values, preferred_element_type=jnp.float32).astype(jnp.bfloat16)
            log = jnp.broadcast_to(top + jnp.log(total), (2 * rows, dim))
            for i in range(2):
                on = slice((2 * block + i) * dim, (2 * block + i + 1) * dim)
                mixed[at, on] = out[i * rows : (i + 1) * rows]
                log_total[at, on] = log[i * rows : (i + 1) * rows]


def attend_back_body(
    info, query, before, own, log_total, grad_resid, weight0, weight1, raw, cosine, sine, gain,
    grad_query, grad_own, grad_before, gain_part, grad_keys, grad_values, grad_mixed,
):
    dim = own.shape[1] // 4
    rows = query.shape[0] // 2
    scale = dim**-0.5
    gain_total = jnp.zeros((1, dim), jnp.float32)
    masks = [window_mask(info, part, rows, 3 * rows) for part in range(2)]
    for block, weight in enumerate((weight0, weight1)):
        on = slice(2 * block * dim, 2 * (block + 1) * dim)
        grad_mixed[:, on] = jnp.dot(
            grad_resid[...], weight[...], preferred_element_type=jnp.float32
        ).astype(jnp.bfloat16)
        grad_keys[...] = jnp.zeros_like(grad_keys)
        grad_values[...] = jnp.zeros_like(grad_values)
        for part in range(2):
            keys, values = seen_pair(before, own, part, block, dim)
            at = slice(part * rows, (part + 1) * rows)
            seen = slice(part * rows, part * rows + 3 * rows)
            queries = two_heads(query, at, block, dim)
            grads = two_heads(grad_mixed, at, block, dim)
            log = two_heads(log_total, at, block, dim)[:, :1]
            prob = jnp.exp(nt(queries, keys) * scale + masks[part] - log)
            grad_prob = nt(grads, values)
            inner = jnp.sum(prob * grad_prob, -1, keepdims=True)
            grad_score = (prob * (grad_prob - inner)).astype(jnp.bfloat16)
            grad_values[seen, :] += tn(prob.astype(jnp.bfloat16), grads)
            grad_keys[seen, :] += tn(grad_score, queries) * scale
            both = jnp.dot(grad_score, keys, preferred_element_type=jnp.float32) * scale
            for i in range(2):
                head = 2 * block + i
                back = both[i * rows : (i + 1) * rows]
                back = back * cosine[at, :] - turned(back) * sine[at, :]
                there = (2 * head - head % 2) * dim
                unit, inverse = unit_of(raw[at, there : there + dim])
                gain_total += jnp.sum(unit * back, 0, keepdims=True)
                back = back * gain[...]
                back = inverse * (back - unit * jnp.mean(back * unit, -1, keepdims=True))
                grad_query[at, head * dim : (head + 1) * dim] = back.astype(jnp.bfloat16)
        for grad, here, there in zip(
            (grad_keys, grad_values), key_columns(block, dim), key_columns(1 - block, dim)
        ):
            grad_before[:, there] = grad[: 2 * rows, :].astype(jnp.bfloat16)
            grad_own[:, here] = grad[2 * rows :, :]
    gain_part[...] = gain_total


def finish_body(grad_query, grad_own, came, raw, cosine, sine, gain, even, odd, gain_part):
    dim = cosine.shape[1]
    total = jnp.zeros((1, dim), jnp.float32)
    for block, out in enumerate((even, odd)):
        key, value = key_columns(block, dim)
        back = grad_own[:, key] + came[:, key].astype(jnp.float32)
        back = back * cosine[...] - turned(back) * sine[...]
        unit, inverse = unit_of(raw[:, (4 * block + 2) * dim : (4 * block + 3) * dim])
        total += jnp.sum(unit * back, 0, keepdims=True)
        back = back * gain[...]
        back = inverse * (back - unit * jnp.mean(back * unit, -1, keepdims=True))
        out[:, : 2 * dim] = grad_query[:, 2 * block * dim : (2 * block + 2) * dim]
        out[:, 2 * dim : 3 * dim] = back.astype(jnp.bfloat16)
        grad_value = grad_own[:, value] + came[:, value].astype(jnp.float32)
        out[:, 3 * dim :] = grad_value.astype(jnp.bfloat16)
    gain_part[...] = total


class Late:
    def __init__(self, ref, copy):
        self.ref, self.copy, self.shape = ref, copy, ref.shape

    def wait(self):
        if self.copy is not None:
            self.copy.wait()
            self.copy = None

    def __getitem__(self, at):
        self.wait()
        return self.ref[at]


def vmem_call(body, outs, scratch=(), scalars=0, name=None, order=None):
    def call(*args):
        count = len(args) - scalars

        def late_body(*refs):
            held = refs[len(args) + len(outs) : len(args) + len(outs) + count]
            sems = refs[-1]
            late = [
                Late(held[i], pltpu.make_async_copy(refs[scalars + i], held[i], sems.at[i]))
                for i in range(count)
            ]
            for i in order or range(count):
                late[i].copy.start()
            body(
                *refs[:scalars], *late, *refs[len(args) : len(args) + len(outs)],
                *refs[len(args) + len(outs) + count : -1],
            )
            for one in late:
                one.wait()

        return pl.pallas_call(
            late_body,
            grid=(1,),
            out_shape=outs,
            in_specs=[pl.BlockSpec(memory_space=pltpu.SMEM)] * scalars
            + [pl.BlockSpec(memory_space=pl.ANY)] * count,
            out_specs=[pl.BlockSpec(memory_space=pltpu.VMEM)] * len(outs),
            scratch_shapes=[
                *(pltpu.VMEM(a.shape, a.dtype) for a in args[scalars:]),
                *scratch,
                pltpu.SemaphoreType.DMA((count,)),
            ],
            compiler_params=pltpu.CompilerParams(vmem_limit_bytes=VMEM_BYTES),
            cost_estimate=FREE,
            name=name,
        )(*args)

    return call


def hidden_units(mids, grads_y, weights):
    width, units = weights.shape[0], weights.shape[1] // 3
    count = len(mids)
    heights = [m.shape[0] for m in mids]
    rows, cut = sum(heights), units // 3

    def body(*refs):
        gate_w, up_w, w_down, act, grad_gate, grad_up = refs[2 * count : 2 * count + 6]
        held, sems = refs[2 * count + 6 : -1], refs[-1]
        copies = [
            pltpu.make_async_copy(refs[i], held[i], sems.at[i]) for i in range(2 * count)
        ]
        first = pl.program_id(0) == 0

        @pl.when(first)
        def _():
            for i in range(count):
                copies[i].start()
                copies[count + i].start()

        start = 0
        for i, (mid, grad_y) in enumerate(zip(held[:count], held[count:])):

            @pl.when(first)
            def _(i=i):
                copies[i].wait()
                copies[count + i].wait()

            at = slice(start, start + mid.shape[0])
            start += mid.shape[0]
            gate = jnp.dot(mid[...], gate_w[...], preferred_element_type=jnp.float32)
            up = jnp.dot(mid[...], up_w[...], preferred_element_type=jnp.float32)
            grad_act = jnp.dot(grad_y[...], w_down[...], preferred_element_type=jnp.float32)
            sigma = jax.nn.sigmoid(gate)
            swish = gate * sigma
            act[at, :] = (swish * up).astype(jnp.bfloat16)
            slope = grad_act * up * sigma * (1.0 + gate * (1.0 - sigma))
            grad_gate[at, :] = slope.astype(jnp.bfloat16)
            grad_up[at, :] = (grad_act * swish).astype(jnp.bfloat16)

    return pl.pallas_call(
        body,
        grid=(3,),
        out_shape=[jax.ShapeDtypeStruct((rows, units), jnp.bfloat16)] * 3,
        in_specs=[
            *(pl.BlockSpec(memory_space=pl.ANY) for _ in range(2 * count)),
            pl.BlockSpec((width, cut), lambda j: (0, j)),
            pl.BlockSpec((width, cut), lambda j: (0, j + 3)),
            pl.BlockSpec((width, cut), lambda j: (0, j + 6)),
        ],
        out_specs=[pl.BlockSpec((rows, cut), lambda j: (0, j))] * 3,
        scratch_shapes=[
            *(pltpu.VMEM((h, width), jnp.bfloat16) for h in heights + heights),
            pltpu.SemaphoreType.DMA((2 * count,)),
        ],
        compiler_params=pltpu.CompilerParams(vmem_limit_bytes=VMEM_BYTES),
        cost_estimate=FREE,
        name="hidden_units",
    )(*mids, *grads_y, weights, weights, weights)


def from_hidden(pairs, eighths):
    count, parts = len(pairs), len(eighths)
    rows, units = pairs[0][0].shape[0] // 8, pairs[0][0].shape[1]
    width = pairs[0][1].shape[0]
    cut = width // 4

    def body(*refs):
        ins, outs = refs[: -(parts // 2)], refs[-(parts // 2) :]
        total = 0.0
        for i in range(count):
            part = ins[i * (parts + 1) : (i + 1) * (parts + 1)]
            left = jnp.concatenate([p[...] for p in part[:-1]], 0)
            total = total + nt(left, part[-1][...])
        for i, out in enumerate(outs):
            out[...] = total[2 * i * rows : 2 * (i + 1) * rows].astype(jnp.bfloat16)

    specs, args = [], []
    for left, right, at in pairs:
        specs += [pl.BlockSpec((rows, units), lambda j, e=e: (e, 0)) for e in eighths]
        specs.append(pl.BlockSpec((cut, units), lambda j, at=at: (j, at)))
        args += [left] * parts + [right]
    return pl.pallas_call(
        body,
        grid=(4,),
        out_shape=[jax.ShapeDtypeStruct((2 * rows, width), jnp.bfloat16)] * (parts // 2),
        in_specs=specs,
        out_specs=[pl.BlockSpec((2 * rows, cut), lambda j: (0, j))] * (parts // 2),
        compiler_params=pltpu.CompilerParams(vmem_limit_bytes=VMEM_BYTES),
        cost_estimate=FREE,
        name="from_hidden",
    )(*args)


def row_outer(lefts, groups, first, tiles, added=None, places=None, part=None):
    rights = [right for group in groups for right in group]
    places = range(len(rights)) if places is None else places
    added = [] if added is None else [added] * len(rights)
    width = lefts[0].shape[1]
    tile = width // 8
    count = len(lefts)
    rows = sum(left.shape[0] for left in lefts)
    wide = rights[0].shape[1] // (1 if part is None else 2)
    columns = [wide * len(group) for group in groups]

    def body(*refs):
        left_refs = refs[:count]
        right_refs = refs[count : count + len(rights)]
        add_refs = refs[count + len(rights) : count + len(rights) + len(added)]
        outs = refs[count + len(rights) + len(added) :]
        place = 0
        for i, group in enumerate(groups):
            column = 0
            for _ in group:
                on = slice(column, column + wide)
                total, start = 0.0, 0
                for left in left_refs:
                    stop = start + left.shape[0]
                    total = total + tn(left[...], right_refs[place][start:stop, :])
                    start = stop
                if added:
                    total = total + add_refs[place][...].astype(jnp.float32)
                outs[i][:, on] = total.astype(jnp.bfloat16)
                place += 1
                column += wide

    return pl.pallas_call(
        body,
        grid=(tiles,),
        out_shape=[jax.ShapeDtypeStruct((tiles * tile, c), jnp.bfloat16) for c in columns],
        in_specs=[
            *(pl.BlockSpec((left.shape[0], tile), lambda j: (0, j + first)) for left in lefts),
            *(
                pl.BlockSpec(
                    (right.shape[0], wide), lambda j: (0, part or 0), pipeline_mode=pl.Buffered(1)
                )
                for right in rights
            ),
            *(
                pl.BlockSpec((tile, wide), lambda j, at=at: (j + first, at))
                for at in places[: len(added)]
            ),
        ],
        out_specs=[pl.BlockSpec((tile, c), lambda j: (j, 0)) for c in columns],
        compiler_params=pltpu.CompilerParams(vmem_limit_bytes=VMEM_BYTES),
        cost_estimate=pl.CostEstimate(
            flops=2 * rows * tiles * tile * sum(columns),
            bytes_accessed=2 * rows * (width + sum(columns)),
            transcendentals=0,
        ),
        name="row_outer",
    )(*lefts, *rights, *added)


def close_body(x, *refs):
    mixed, weights = refs[:4], refs[4:12]
    gains, resid, mid = refs[12:]
    at = pl.program_id(0)
    step = x.shape[1]
    columns = weights[0].shape[1]
    total = x[...].astype(jnp.float32)
    for i in range(8):
        part = mixed[i // 2][:, (i % 2) * columns : (i % 2 + 1) * columns]
        total = total + nt(part, weights[i][...])
    resid[:, pl.ds(pl.multiple_of(at * step, step), step)] = total

    @pl.when(at == 3)
    def _():
        unit, _ = unit_of(resid[...])
        mid[...] = (unit * gains[...]).astype(jnp.bfloat16)


def close_attention(x, mixed, weights, gains):
    rows, width = x.shape
    step = width // 4
    whole = lambda a: pl.BlockSpec(a.shape, lambda j: (0, 0))
    return pl.pallas_call(
        close_body,
        grid=(4,),
        out_shape=[
            jax.ShapeDtypeStruct((rows, width), jnp.float32),
            jax.ShapeDtypeStruct((rows, width), jnp.bfloat16),
        ],
        in_specs=[
            pl.BlockSpec((rows, step), lambda j: (0, j)),
            *(whole(m) for m in mixed),
            *(pl.BlockSpec((step, w.shape[1]), lambda j: (j, 0)) for w in weights),
            whole(gains),
        ],
        out_specs=[pl.BlockSpec((rows, width), lambda j: (0, 0))] * 2,
        compiler_params=pltpu.CompilerParams(vmem_limit_bytes=VMEM_BYTES),
        cost_estimate=FREE,
        name="close_attention",
    )(x, *mixed, *weights, gains)


def back_to_rows(blocks, weights):
    rows = blocks[0].shape[0]
    step, columns = weights[0][0].shape
    count = len(blocks)

    def body(*refs):
        lefts = refs[:count]
        hbm = refs[count : 3 * count]
        out = refs[3 * count]
        held, sems = refs[3 * count + 1 :]
        copies = []
        for i in range(count):
            own, came = hbm[2 * i : 2 * i + 2]
            copies.append(
                [
                    pltpu.make_async_copy(own, held.at[i, :step], sems.at[i, 0]),
                    pltpu.make_async_copy(came, held.at[i, step:], sems.at[i, 1]),
                ]
            )
        for some in copies:
            for copy in some:
                copy.start()
        for i in range(count):
            for copy in copies[i]:
                copy.wait()
            for k in range(4):
                on = slice(k * step, (k + 1) * step)
                part = nt(lefts[i][...], held[i, on])
                if i == 0:
                    out[:, on] = part
                else:
                    out[:, on] += part

    return pl.pallas_call(
        body,
        grid=(1,),
        out_shape=jax.ShapeDtypeStruct((rows, 4 * step), jnp.float32),
        in_specs=[pl.BlockSpec(memory_space=pltpu.VMEM)] * count
        + [pl.BlockSpec(memory_space=pl.ANY)] * (2 * count),
        out_specs=pl.BlockSpec(memory_space=pltpu.VMEM),
        scratch_shapes=[
            pltpu.VMEM((count, 4 * step, columns), jnp.bfloat16),
            pltpu.SemaphoreType.DMA((count, 2)),
        ],
        compiler_params=pltpu.CompilerParams(vmem_limit_bytes=VMEM_BYTES),
        cost_estimate=FREE,
        name="back_to_rows",
    )(*blocks, *(part for w in weights for part in w))


def on_device_block(
    tokens,
    lengths,
    attn_gain,
    w_query,
    key_matrix,
    value_matrix,
    query_gain,
    key_gain,
    w_out,
    mlp_gain,
    w_gate,
    w_up,
    w_down,
    cotangent,
):
    low, full = jnp.bfloat16, jnp.float32
    width = tokens.shape[2]
    head_dim = query_gain.shape[0]
    shards = lax.axis_size("shard")
    shard_at = lax.axis_index("shard")
    me = lax.axis_index("rep")
    core = me & 1
    count = lax.axis_size("rep")

    s = Stage()
    piece = width // shards

    s.own_blocks = [
        column_block((w_query, key_matrix, value_matrix), me ^ i) for i in range(8)
    ]
    gain_rows = jnp.concatenate(
        [jnp.stack([attn_gain, mlp_gain]), jnp.zeros((14, piece), low)], 0
    )
    travelling = jnp.concatenate([s.own_blocks[0], gain_rows], 0)
    s.tokens_cuts, s.cotangent_cuts = sequence_cuts(tokens), sequence_cuts(cotangent)
    s.out_block = column_block((w_out,), me)
    s.ffn_block = column_block((w_gate, w_up, w_down), me)
    s.before, s.behind = around(travelling, 1), around(travelling, -1)
    s.other_lengths = across(lengths, CORE)
    s.end()

    s.ahead = around(s.before, 1)
    tokens_sent = [to_sequence(cut, turn) for turn, cut in enumerate(s.tokens_cuts)]
    out_own = lax.all_gather(s.out_block, "shard", axis=0, tiled=True)
    del s.out_block, s.tokens_cuts
    s.end()

    parts = (s.before, s.ahead, s.behind)
    s.came = jnp.concatenate([part[:piece] for part in parts], 0)
    s.gains = jnp.concatenate([gain_rows[:2], *(part[piece : piece + 2] for part in parts)], 1)
    s.came_near = near(s.came)
    s.came_own = across(s.came, CORE)
    s.x_came = tokens_sent
    del s.before, s.behind, s.ahead
    s.end()

    grad_y_sent = [to_sequence(cut, turn) for turn, cut in enumerate(s.cotangent_cuts)]
    s.came_far = far(*s.came_near)
    gains = rolled(s.gains.astype(full))
    s.mlp_gains = gains[1:]
    s.attn_gains = gains[:1]
    s.x_low = jnp.concatenate(in_turn(s.x_came), 0)
    rows = s.x_low.shape[0]
    x_rows = s.x_low.astype(full)
    s.inverse_in = lax.rsqrt(jnp.mean(x_rows * x_rows, -1, keepdims=True) + EPS)
    s.normed = rolled((x_rows * s.inverse_in * s.attn_gains).astype(low))
    query_gains = query_gain.astype(full)[None]
    key_gains = key_gain.astype(full)[None]
    s.head_gains = jnp.concatenate([query_gains, key_gains], 0)
    both = jnp.where(
        core == 0,
        jnp.concatenate([lengths, s.other_lengths]),
        jnp.concatenate([s.other_lengths, lengths]),
    )
    length = lax.dynamic_index_in_dim(both, shard_at, 0, keepdims=False)
    s.info = jnp.stack([core, length]).astype(jnp.int32)
    query_pos = core * rows + jnp.arange(rows, dtype=jnp.int32)
    s.valid = (query_pos < length)[:, None].astype(full)
    cosine, sine = tables(query_pos, head_dim)
    s.cosine, sine = cosine[0, :, 0], sine[0, :, 0]
    s.sine = jnp.concatenate([-sine[:, : head_dim // 2], sine[:, head_dim // 2 :]], 1)
    s.out_own = out_own
    del s.gains, s.x_came, s.other_lengths, s.cotangent_cuts
    s.end()

    head_columns = 2 * head_dim
    block_columns = 4 * head_dim
    quad_rows = jax.ShapeDtypeStruct((rows, block_columns), low)
    quad_sums = jax.ShapeDtypeStruct((rows, block_columns), full)
    gain_sum = jax.ShapeDtypeStruct((1, head_dim), full)
    project = vmem_call(
        project_body,
        [jax.ShapeDtypeStruct((rows, 2 * block_columns), full), quad_rows, quad_rows],
        name="project",
    )
    attend = vmem_call(attend_body, [quad_rows, quad_sums], scalars=1, name="attend")
    attend_back = vmem_call(
        attend_back_body,
        [quad_rows, quad_sums, quad_rows, gain_sum],
        scratch=[pltpu.VMEM((2 * rows, head_dim), full)] * 2
        + [pltpu.VMEM((rows, block_columns), low)],
        scalars=1,
        name="attend_back",
        order=(4, 5, 0, 1, 2, 3, 7, 8, 9, 10, 6),
    )
    finish = vmem_call(finish_body, [quad_rows, quad_rows, gain_sum], name="finish")
    upward = [(i, i + 1) for i in range(0, count, 2)]
    downward = [(i + 1, i) for i in range(0, count, 2)]

    def project_call(i, came, other):
        return (
            project, s.normed, s.own_blocks[2 * i], came, s.own_blocks[2 * i + 1], other,
            s.cosine, s.sine, s.head_gains,
        )

    def attend_call(projected, earlier):
        return (
            lambda query, own, before: attend(s.info, query, before, own),
            *projected[1:], earlier,
        )

    came_last = jnp.concatenate(s.came_far, 0)
    s.came_last = (came_last, across(came_last, CORE))
    s.out_near = near(s.out_own)
    s.came_other = [s.came_own, *(across(block, CORE) for block in s.came_near)]
    s.projected = in_order([project_call(0, s.came, s.came_own)])
    s.grad_y_came = grad_y_sent
    del s.came_far, s.came_own
    s.end()

    ffn_own = lax.all_gather(s.ffn_block, "shard", axis=0, tiled=True)
    grad_y = jnp.concatenate(in_turn(s.grad_y_came), 0)
    s.grad_y = jnp.where(s.valid > 0, grad_y, jnp.zeros_like(grad_y))
    grad_y_near = near(s.grad_y)
    s.out_far = far(*s.out_near)
    s.out_own_other = across(s.out_own, CORE)
    s.out_near_other = [across(block, CORE) for block in s.out_near]
    s.earlier = [lax.ppermute(s.projected[0][2], "rep", upward)]
    s.projected = s.projected + in_order(
        [
            project_call(1, s.came_near[0], s.came_other[1]),
            project_call(2, s.came_near[1], s.came_other[2]),
            project_call(3, *s.came_last),
        ]
    )
    del s.ffn_block, s.grad_y_came
    s.end()

    out_last = jnp.concatenate(s.out_far, 0)
    s.out_last = (out_last, across(out_last, CORE))
    s.earlier = s.earlier + [lax.ppermute(p[2], "rep", upward) for p in s.projected[1:]]
    s.attended = in_order([attend_call(s.projected[0], s.earlier[0])])
    del s.out_far
    s.end()

    s.out_blocks = [
        s.out_own, s.out_own_other, s.out_near[0], s.out_near_other[0], s.out_near[1],
        s.out_near_other[1], *s.out_last,
    ]
    s.attended = s.attended + in_order(
        [attend_call(s.projected[i], s.earlier[i]) for i in (1, 2, 3)]
    )
    s.mixed = [a[0] for a in s.attended]
    s.resid, s.mid = close_attention(s.x_low, s.mixed, s.out_blocks, s.mlp_gains)
    s.grad_y_near = grad_y_near
    s.came = [s.came, *s.came_near, s.came_last[0]]
    s.came_other = [*s.came_other, s.came_last[1]]
    del s.came_near, s.came_last
    del s.out_own, s.out_own_other, s.out_near, s.out_near_other, s.out_last
    s.end()

    s.mid_near = near(s.mid)
    s.grad_y_far = far(*s.grad_y_near)
    s.end()

    s.mid_far = far(*s.mid_near)
    s.ffn_own = ffn_own
    s.end()

    s.mids = [s.mid, *s.mid_near, *s.mid_far]
    s.grads_y = [s.grad_y, *s.grad_y_near, *s.grad_y_far]
    s.ffn_other = across(s.ffn_own, CORE)
    units = s.ffn_own.shape[1] // 3
    s.hidden_own = hidden_units(s.mids, s.grads_y, s.ffn_own)
    del s.mid, s.mid_near, s.mid_far, s.grad_y_near, s.grad_y_far
    s.end()

    def gate_up_pairs():
        return [
            (hidden[i], weights, i - 1)
            for hidden, weights in ((s.hidden_own, s.ffn_own), (s.hidden_other, s.ffn_other))
            for i in (1, 2)
        ]

    def down_pairs():
        return [(s.hidden_own[0], s.ffn_own, 2), (s.hidden_other[0], s.ffn_other, 2)]

    def from_hidden_call(pairs, eighths):
        return (
            lambda first: from_hidden([(first, *pairs[0][1:]), *pairs[1:]], eighths),
            pairs[0][0],
        )

    def outer_call(lefts, rights, *added):
        return lambda first: row_outer(lefts, [[first, *rights[1:]]], 0, 8, *added)[0], rights[0]

    def send_near(sent):
        return across(sent[0], ACROSS_X), across(sent[1], ACROSS_Y)

    def send_far(came, rest, split):
        one_tail, two_head = rest
        return (
            across(rounded_sum(one_tail, split(came[1])[1]), ACROSS_X),
            across(rounded_sum(two_head, split(came[0])[1]), ACROSS_Y),
        )

    def total(came, came_far, own, split):
        head, tail = own
        full_sum = lambda *parts: sum(part.astype(full) for part in parts)
        return jnp.concatenate(
            [
                full_sum(head, split(came[0])[0], came_far[1]),
                full_sum(tail, split(came[1])[0], came_far[0]),
            ],
            0,
        )

    by_rows = lambda a: jnp.split(a, 2, 0)
    by_columns = lambda a: jnp.split(a, 2, 1)
    to_plane, rest_of_plane = (2, 6, 5, 7), (3, 4, 0, 1)

    s.hidden_other = hidden_units(s.mids, s.grads_y, s.ffn_other)
    (s.down_outer,) = in_order([outer_call(s.grads_y, s.hidden_other[:1])])
    s.end()

    s.down_came = across(s.down_outer, CORE)
    s.mid_sent = from_hidden(gate_up_pairs(), to_plane)
    del s.down_outer
    s.end()

    s.mid_came = send_near(s.mid_sent)
    s.down_mine, s.mid_rest, s.gate_up_outer = in_order(
        [
            outer_call(s.grads_y, s.hidden_own[:1], s.down_came),
            from_hidden_call(gate_up_pairs(), rest_of_plane),
            outer_call(s.mids, s.hidden_other[1:]),
        ]
    )
    del s.mid_sent, s.down_came
    s.end()

    down_total = lax.psum_scatter(s.down_mine, "shard", scatter_dimension=0, tiled=True)
    s.mid_came_far = send_far(s.mid_came, by_rows(s.mid_rest[0]), by_rows)
    s.gate_up_came = across(s.gate_up_outer, CORE)
    s.mlp_sent, s.mlp_rest = in_order(
        [
            from_hidden_call(down_pairs(), to_plane),
            from_hidden_call(down_pairs(), rest_of_plane),
        ]
    )
    del s.gate_up_outer, s.down_mine
    s.end()

    def back_call(i):
        raw, query, own_pair = s.projected[i]
        return (
            lambda query, *rest: attend_back(s.info, query, *rest),
            query, s.earlier[i], own_pair, s.attended[i][1], s.resid_low,
            *s.out_blocks[2 * i : 2 * i + 2], raw, s.cosine, s.sine, s.head_gains[:1],
        )

    def finish_call(i):
        return (
            finish, s.backs[i][0], s.backs[i][1], s.returned[i], s.projected[i][0],
            s.cosine, s.sine, s.head_gains[1:],
        )

    def give_back(*chips):
        s.returned = s.returned | {
            i: lax.ppermute(s.backs[i][2], "rep", downward) for i in chips
        }

    def odd_call(left, blocks, part=None):
        return lambda first: row_outer([first], [blocks], 0, 8, part=part)[0], left

    def head_call(left, blocks, came, part=None, places=(0, 1, 2, 3)):
        groups = [[blocks[1], blocks[3]], [blocks[2]], [blocks[0]]]
        at = [places[i] for i in (1, 3, 2, 0)]
        return lambda first: row_outer([first], groups, 0, 4, came, at, part), left

    def tail_call(left, blocks, came, part=None, places=(0, 1, 2, 3)):
        groups = [[blocks[2], blocks[3]], [blocks[1]], [blocks[0]]]
        at = [places[i] for i in (2, 3, 1, 0)]
        return lambda first: row_outer([first], groups, 4, 4, came, at, part), left

    s.mlp_came = send_near(s.mlp_sent)
    grad_mid = total(s.mid_came, s.mid_came_far, by_rows(s.mid_rest[1]), by_rows)
    inverse_mid = lax.rsqrt(jnp.mean(s.resid * s.resid, -1, keepdims=True) + EPS)
    mid_unit = s.resid * inverse_mid
    s.mlp_gain_part = jnp.sum(mid_unit * grad_mid, 0)
    s.grad_resid = s.grad_y.astype(full) + norm_back(
        mid_unit, inverse_mid, grad_mid * s.mlp_gains
    )
    s.resid_low = s.grad_resid.astype(low)
    s.resid_rolled = rolled(s.resid_low)
    s.returned = {}
    back, s.out_odd, s.gate_up_mine = in_order(
        [
            back_call(3),
            odd_call(s.resid_rolled, s.mixed, 1),
            outer_call(s.mids, s.hidden_own[1:], s.gate_up_came),
        ]
    )
    s.backs = {3: back}
    s.down_total = down_total
    del s.mid_came, s.mid_came_far, s.mid_rest, s.gate_up_came, s.hidden_own, s.hidden_other
    del s.mids, s.grads_y, s.ffn_own, s.ffn_other, s.mlp_sent
    s.end()

    gate_up_total = lax.psum_scatter(s.gate_up_mine, "shard", scatter_dimension=0, tiled=True)
    s.mlp_came_far = send_far(s.mlp_came, by_rows(s.mlp_rest[0]), by_rows)
    s.out_came = across(s.out_odd, CORE)
    give_back(3)
    back1, back2 = in_order([back_call(1), back_call(2)])
    s.backs = s.backs | {1: back1, 2: back2}
    del s.out_odd, s.gate_up_mine
    s.end()

    s.down_near = near(s.down_total)
    give_back(1, 2)
    s.out_head, s.out_tail, back, finished = in_order(
        [
            head_call(s.resid_rolled, s.mixed, s.out_came, 0),
            tail_call(s.resid_rolled, s.mixed, s.out_came, 0),
            back_call(0),
            finish_call(3),
        ]
    )
    s.backs = s.backs | {0: back}
    s.finished = {3: finished}
    del s.out_came
    s.end()

    s.out_near = send_near((s.out_head[0], s.out_tail[0]))
    mlp_out = total(s.mlp_came, s.mlp_came_far, by_rows(s.mlp_rest[1]), by_rows)
    s.output = (s.valid * (s.resid + mlp_out)).astype(low)
    give_back(0)
    finished1, finished2 = in_order([finish_call(1), finish_call(2)])
    s.finished = s.finished | {1: finished1, 2: finished2}
    del s.mlp_came, s.mlp_came_far, s.mlp_rest, s.resid
    s.end()

    output_sent = from_sequences_send(s.output)
    s.out_far = send_far(s.out_near, (s.out_tail[1], s.out_head[1]), by_columns)
    s.down_far = far(*s.down_near)
    (finished,) = in_order([finish_call(0)])
    s.finished = s.finished | {0: finished}
    (s.odd,) = in_order([odd_call(s.normed, [s.finished[i][1] for i in range(4)])])
    s.gate_up_total = gate_up_total
    s.output_first = output_sent[0]
    del s.output
    s.end()

    my_group = me.astype(jnp.int32)[None]

    def whole_call(widths, own, other, part=0):
        return lambda first: whole_columns(my_group, first, other, widths, part), own

    s.gate_up_near = near(s.gate_up_total)
    s.qkv_came = across(s.odd, CORE)
    out_sum = total(s.out_near, s.out_far, (s.out_head[2], s.out_tail[2]), by_columns)
    s.out_chunks = jnp.split(out_sum.astype(low), shards, 0)
    s.out_ring = ring_sum_first(s.out_chunks)
    weights = [
        pair
        for i in range(4)
        for pair in (
            (s.own_blocks[2 * i], s.came[i]), (s.own_blocks[2 * i + 1], s.came_other[i])
        )
    ]
    blocks = [part for i in range(4) for part in s.finished[i][:2]]
    grad_in = rolled(back_to_rows(blocks, weights))
    x_unit = s.x_low.astype(full) * s.inverse_in
    s.gain_parts = jnp.concatenate(
        [
            jnp.sum(x_unit * grad_in, 0),
            s.mlp_gain_part,
            sum(s.backs[i][3] for i in range(4))[0],
            sum(s.finished[i][2] for i in range(4))[0],
        ]
    )
    s.grad_tokens = (
        s.grad_resid + norm_back(x_unit, s.inverse_in, grad_in * s.attn_gains)
    ).astype(low)
    del s.odd, s.out_near, s.out_far, s.out_head, s.out_tail, s.backs
    del s.own_blocks, s.came, s.came_other, s.grad_resid, s.x_low
    s.end()

    even = [s.finished[i][0] for i in range(4)]
    s.head0, s.tail0, s.head1, s.tail1 = in_order(
        [
            call(s.normed, even, s.qkv_came, half, range(half, 8, 2))
            for half in range(2)
            for call in (head_call, tail_call)
        ]
    )
    tokens_sent = from_sequences_send(s.grad_tokens)
    s.down_spread = jnp.concatenate([s.down_total, *s.down_near, *s.down_far], 0)
    s.down_spread_other = across(s.down_spread, CORE)
    s.output_second = output_sent[1]
    s.out_ring_last = around(rounded_sum(s.out_chunks[3], s.out_ring[0]), 1)
    s.gate_up_far = far(*s.gate_up_near)
    del s.qkv_came, s.finished, s.down_total, s.down_near, s.down_far
    s.end()

    def qkv_chunks(came, came_far, head, tail):
        own = total(came, came_far, (head[2], tail[2]), by_columns)
        return jnp.split(own.astype(low), shards, 0)

    s.near0 = send_near((s.head0[0], s.tail0[0]))
    s.gate_up_own = jnp.concatenate([s.gate_up_total, *s.gate_up_near, *s.gate_up_far], 0)
    s.gate_up_other = across(s.gate_up_own, CORE)
    (s.whole_down,) = in_order([whole_call((units,), s.down_spread, s.down_spread_other)])
    s.out_total = rounded_sum(s.out_chunks[0], s.out_ring[1], s.out_ring_last)
    s.tokens_first = tokens_sent[0]
    del s.down_spread, s.down_spread_other, s.out_chunks, s.out_ring, s.out_ring_last
    del s.gate_up_near, s.gate_up_far, s.gate_up_total
    s.end()

    s.far0 = send_far(s.near0, (s.tail0[1], s.head0[1]), by_columns)
    s.near1 = send_near((s.head1[0], s.tail1[0]))
    (s.whole_gate_up,) = in_order([whole_call((units, units), s.gate_up_own, s.gate_up_other)])
    s.tokens_second = tokens_sent[1]
    del s.gate_up_own, s.gate_up_other, s.grad_tokens
    s.end()

    s.chunks0 = qkv_chunks(s.near0, s.far0, s.head0, s.tail0)
    s.ring0 = ring_sum_first(s.chunks0)
    s.far1 = send_far(s.near1, (s.tail1[1], s.head1[1]), by_columns)
    s.gain_came = across(s.gain_parts, CORE)
    del s.near0, s.far0, s.head0, s.tail0
    s.end()

    s.last0 = around(rounded_sum(s.chunks0[3], s.ring0[0]), 1)
    s.chunks1 = qkv_chunks(s.near1, s.far1, s.head1, s.tail1)
    s.ring1 = ring_sum_first(s.chunks1)
    s.gain_parts = s.gain_parts + s.gain_came
    s.gain_came = across(s.gain_parts, ACROSS_X)
    del s.near1, s.far1, s.head1, s.tail1
    s.end()

    query_total = rounded_sum(s.chunks0[0], s.ring0[1], s.last0)
    s.total0 = jnp.concatenate([query_total, s.out_total], 1)
    s.spread0 = near(s.total0)
    s.last1 = around(rounded_sum(s.chunks1[3], s.ring1[0]), 1)
    s.gain_parts = s.gain_parts + s.gain_came
    s.gain_came = across(s.gain_parts, ACROSS_Y)
    del s.chunks0, s.ring0, s.last0, s.out_total
    s.end()

    s.spread_far0 = far(*s.spread0)
    s.total1 = rounded_sum(s.chunks1[0], s.ring1[1], s.last1)
    s.spread1 = near(s.total1)
    s.gain_parts = s.gain_parts + s.gain_came
    s.gain_came = lax.ppermute(s.gain_parts, "shard", [(i, i ^ 1) for i in range(shards)])
    del s.chunks1, s.ring1, s.last1
    s.end()

    s.own0 = jnp.concatenate([s.total0, *s.spread0, *s.spread_far0], 0)
    s.other0 = across(s.own0, CORE)
    s.spread_far1 = far(*s.spread1)
    s.gain_parts = s.gain_parts + s.gain_came
    s.gain_came = lax.ppermute(s.gain_parts, "shard", [(i, i ^ 2) for i in range(shards)])
    del s.total0, s.spread0, s.spread_far0
    s.end()

    s.own1 = jnp.concatenate([s.total1, *s.spread1, *s.spread_far1], 0)
    s.other1 = across(s.own1, CORE)
    (s.whole0,) = in_order([whole_call((head_columns, head_columns), s.own0, s.other0)])
    gain_sums = s.gain_parts + s.gain_came
    s.wide = lax.dynamic_slice_in_dim(
        gain_sums[: 2 * width].reshape(2, width), shard_at * piece, piece, 1
    )
    s.narrow = gain_sums[2 * width :]
    del s.own0, s.other0, s.total1, s.spread1, s.spread_far1
    s.end()

    ((whole_key, whole_value),) = in_order(
        [whole_call((head_dim, head_dim), s.own1, s.other1)]
    )
    return (
        jnp.stack(in_turn([s.output_first, s.output_second])),
        jnp.stack(in_turn([s.tokens_first, s.tokens_second])),
        s.wide[0],
        s.whole0[0],
        whole_key,
        whole_value,
        s.narrow[:head_dim],
        s.narrow[head_dim:],
        s.whole0[1],
        s.wide[1],
        *s.whole_gate_up,
        *s.whole_down,
    )


def solution(mesh):
    sizes = (mesh.shape["rep"], mesh.shape["shard"])
    return jax.shard_map(
        on_device_block if sizes == (8, 4) else on_device,
        mesh=mesh,
        in_specs=(
            P("rep", "shard", None),
            P("rep"),
            P("shard"),
            P("shard", None),
            P("shard", None),
            P("shard", None),
            P(),
            P(),
            P("shard", None),
            P("shard"),
            P("shard", None),
            P("shard", None),
            P("shard", None),
            P("rep", "shard", None),
        ),
        out_specs=(
            P("rep", "shard", None),
            P("rep", "shard", None),
            P("shard"),
            P("shard", None),
            P("shard", None),
            P("shard", None),
            P(),
            P(),
            P("shard", None),
            P("shard"),
            P("shard", None),
            P("shard", None),
            P("shard", None),
        ),
        check_vma=False,
    )
```

```python
import jax
import jax.numpy as jnp
from jax import lax
from jax.experimental import pallas as pl
from jax.experimental.pallas import tpu as pltpu
from jax.sharding import PartitionSpec as P

WINDOW = 512


EPS = 1e-06
ROPE_BASE = 1000000.0
NEG = -1e30


def passed_along(x, axis, by):
    devices = lax.axis_size(axis)
    pairs = [(i, i + by) for i in range(devices) if 0 <= i + by < devices]
    return lax.ppermute(x, axis, pairs)


def tables(positions, head_dim):
    half = head_dim // 2
    freq = ROPE_BASE ** (-jnp.arange(half, dtype=jnp.float32) * 2.0 / head_dim)
    angle = positions.astype(jnp.float32)[:, None] * freq[None, :]
    angle = jnp.concatenate([angle, angle], -1)
    return (jnp.cos(angle)[None, :, None, :], jnp.sin(angle)[None, :, None, :])


def rotated_rows(value_rows):
    half = value_rows.shape[-1] // 2
    return jnp.concatenate([-value_rows[..., half:], value_rows[..., :half]], -1)


def head_norm(raw, gain):
    inverse = lax.rsqrt(jnp.mean(raw * raw, -1, keepdims=True) + EPS)
    unit = raw * inverse
    return (unit, inverse, unit * gain)


def norm_back(unit, inverse, grad_unit):
    return inverse * (grad_unit - unit * jnp.mean(grad_unit * unit, -1, keepdims=True))


def head_norm_back(unit, inverse, grad_normed, gain):
    grad_raw = norm_back(unit, inverse, grad_normed * gain)
    return (grad_raw, jnp.sum(unit * grad_normed, axis=(0, 1, 2)))


def scores(query_rows, keys, allowed, scale):
    raw = (
        jnp.einsum("sqhgd,skhd->shgqk", query_rows, keys, preferred_element_type=jnp.float32)
        * scale
    )
    return jnp.where(allowed[:, None, None], raw, NEG)


def outer(left, right):
    return jnp.einsum("rc,rf->cf", left, right, preferred_element_type=jnp.float32)


def on_device(
    tokens,
    lengths,
    attn_gain,
    w_query,
    key_matrix,
    value_matrix,
    query_gain,
    key_gain,
    w_out,
    mlp_gain,
    w_gate,
    w_up,
    w_down,
    cotangent,
):
    seq_count, piece, width = tokens.shape
    head_dim = query_gain.shape[0]
    heads_q = w_query.shape[1] // head_dim
    heads_kv = key_matrix.shape[1] // head_dim
    groups = heads_q // heads_kv
    rows = seq_count * piece
    scale = head_dim ** (-0.5)
    reach = (WINDOW + piece - 2) // piece
    owned = width // lax.axis_size("shard")
    shard_at = lax.axis_index("shard")
    query_pos = shard_at * piece + jnp.arange(piece, dtype=jnp.int32)
    key_pos = (shard_at - reach) * piece + jnp.arange((reach + 1) * piece, dtype=jnp.int32)
    near = (
        (key_pos[None, :] <= query_pos[:, None])
        & (query_pos[:, None] - key_pos[None, :] < WINDOW)
        & (key_pos[None, :] >= 0)
    )
    live = (key_pos[None, None, :] < lengths[:, None, None]) | (
        key_pos[None, :] == query_pos[:, None]
    )[None]
    allowed = near[None] & live
    valid = (query_pos[None, :] < lengths[:, None]).astype(jnp.float32).reshape(rows, 1)
    cosine_table, sine_table = tables(query_pos, head_dim)
    x_rows = tokens.astype(jnp.float32).reshape(rows, width)
    inverse_in = lax.rsqrt(jnp.mean(x_rows * x_rows, -1, keepdims=True) + EPS)
    x_unit = x_rows * inverse_in
    gain_piece = lax.all_gather(attn_gain, "shard", axis=0, tiled=True)
    query_piece = lax.all_gather(w_query, "shard", axis=0, tiled=True)
    key_piece = lax.all_gather(key_matrix, "shard", axis=0, tiled=True)
    value_piece = lax.all_gather(value_matrix, "shard", axis=0, tiled=True)
    normed_piece = (x_unit * gain_piece.astype(jnp.float32)).astype(jnp.bfloat16)
    acc_q = jnp.dot(normed_piece, query_piece, preferred_element_type=jnp.float32)
    acc_k = jnp.dot(normed_piece, key_piece, preferred_element_type=jnp.float32)
    acc_v = jnp.dot(normed_piece, value_piece, preferred_element_type=jnp.float32)
    normalized_rows = normed_piece
    gains = gain_piece.astype(jnp.float32)
    attn_in = normalized_rows
    attn_gains = gains
    query_unit, query_inverse, query_rows_normalized = head_norm(
        acc_q.reshape(seq_count, piece, heads_q, head_dim), query_gain.astype(jnp.float32)
    )
    key_unit, key_inverse, key_normed = head_norm(
        acc_k.reshape(seq_count, piece, heads_kv, head_dim), key_gain.astype(jnp.float32)
    )
    query_rows = (
        (query_rows_normalized * cosine_table + rotated_rows(query_rows_normalized) * sine_table)
        .astype(jnp.bfloat16)
        .reshape(seq_count, piece, heads_kv, groups, head_dim)
    )
    keys_own = (key_normed * cosine_table + rotated_rows(key_normed) * sine_table).astype(
        jnp.bfloat16
    )
    values_own = acc_v.reshape(seq_count, piece, heads_kv, head_dim).astype(jnp.bfloat16)
    own_pair = jnp.stack([keys_own, values_own])
    parts = []
    for fetch_back in range(reach, 0, -1):
        parts.append(passed_along(own_pair, "shard", fetch_back))
    parts.append(own_pair)
    near_pair = jnp.concatenate(parts, 2)
    score = scores(query_rows, near_pair[0], allowed, scale)
    top = jnp.max(score, -1, keepdims=True)
    expo = jnp.exp(score - top)
    total = jnp.sum(expo, -1, keepdims=True)
    prob = expo / total
    log_total = top + jnp.log(total)
    mixed = jnp.einsum(
        "shgqk,skhd->sqhgd",
        prob.astype(jnp.bfloat16),
        near_pair[1],
        preferred_element_type=jnp.float32,
    )
    mixed_rows = mixed.reshape(rows, heads_q * head_dim).astype(jnp.bfloat16)
    resid = x_rows + jnp.einsum(
        "rf,nf->rn",
        mixed_rows,
        lax.all_gather(w_out, "shard", axis=0, tiled=True),
        preferred_element_type=jnp.float32,
    )
    inverse_mid = lax.rsqrt(jnp.mean(resid * resid, -1, keepdims=True) + EPS)
    mid_unit = resid * inverse_mid
    gain_piece = lax.all_gather(mlp_gain, "shard", axis=0, tiled=True)
    gate_piece = lax.all_gather(w_gate, "shard", axis=0, tiled=True)
    up_piece = lax.all_gather(w_up, "shard", axis=0, tiled=True)
    normed_piece = (mid_unit * gain_piece.astype(jnp.float32)).astype(jnp.bfloat16)
    acc_gate = jnp.dot(normed_piece, gate_piece, preferred_element_type=jnp.float32)
    acc_up = jnp.dot(normed_piece, up_piece, preferred_element_type=jnp.float32)
    normalized_rows = normed_piece
    gains = gain_piece.astype(jnp.float32)
    mlp_in = normalized_rows
    sigma = jax.nn.sigmoid(acc_gate)
    swish = acc_gate * sigma
    act = (swish * acc_up).astype(jnp.bfloat16)
    mlp_out = jnp.einsum(
        "rf,nf->rn",
        act,
        lax.all_gather(w_down, "shard", axis=0, tiled=True),
        preferred_element_type=jnp.float32,
    )
    output = (valid * (resid + mlp_out)).astype(jnp.bfloat16).reshape(seq_count, piece, width)
    grad_y = cotangent.astype(jnp.float32).reshape(rows, width) * valid
    grad_y_low = grad_y.astype(jnp.bfloat16)
    grad_act = jnp.dot(
        grad_y_low,
        lax.all_gather(w_down, "shard", axis=0, tiled=True),
        preferred_element_type=jnp.float32,
    )
    grad_gate = (grad_act * acc_up * sigma * (1.0 + acc_gate * (1.0 - sigma))).astype(jnp.bfloat16)
    grad_up = (grad_act * swish).astype(jnp.bfloat16)
    gate_piece, up_piece = lax.all_gather((w_gate, w_up), "shard", axis=0, tiled=True)
    grad_mid = jnp.einsum(
        "rf,nf->rn", grad_gate, gate_piece, preferred_element_type=jnp.float32
    ) + jnp.einsum("rf,nf->rn", grad_up, up_piece, preferred_element_type=jnp.float32)
    grad_resid = grad_y + norm_back(mid_unit, inverse_mid, grad_mid * gains)
    mlp_gain_part = jnp.sum(mid_unit * grad_mid, 0)
    normalized_rows = mlp_in
    mlp_grads = jax.tree.map(
        lambda part: lax.psum_scatter(
            part.astype(jnp.bfloat16), "shard", scatter_dimension=0, tiled=True
        ).astype(jnp.float32),
        (
            outer(normalized_rows, grad_gate),
            outer(normalized_rows, grad_up),
            outer(grad_y_low, act),
        ),
    )
    resid_low = grad_resid.astype(jnp.bfloat16)
    grad_mixed = jnp.dot(
        resid_low,
        lax.all_gather(w_out, "shard", axis=0, tiled=True),
        preferred_element_type=jnp.float32,
    )
    grad_mixed = grad_mixed.astype(jnp.bfloat16).reshape(
        seq_count, piece, heads_kv, groups, head_dim
    )
    prob_again = jnp.exp(scores(query_rows, near_pair[0], allowed, scale) - log_total)
    grad_prob = jnp.einsum(
        "sqhgd,skhd->shgqk", grad_mixed, near_pair[1], preferred_element_type=jnp.float32
    )
    grad_values = jnp.einsum(
        "shgqk,sqhgd->skhd",
        prob_again.astype(jnp.bfloat16),
        grad_mixed,
        preferred_element_type=jnp.float32,
    )
    grad_score = (
        prob_again * (grad_prob - jnp.sum(prob_again * grad_prob, -1, keepdims=True))
    ).astype(jnp.bfloat16)
    grad_queries = (
        jnp.einsum(
            "shgqk,skhd->sqhgd", grad_score, near_pair[0], preferred_element_type=jnp.float32
        )
        * scale
    )
    grad_keys = (
        jnp.einsum("shgqk,sqhgd->skhd", grad_score, query_rows, preferred_element_type=jnp.float32)
        * scale
    )
    grad_pair = jnp.stack([grad_keys, grad_values])
    own_grad = grad_pair[:, :, reach * piece :]
    for back in range(1, reach + 1):
        lower = (reach - back) * piece
        own_grad = own_grad + passed_along(grad_pair[:, :, lower : lower + piece], "shard", -back)
    grad_query_post = grad_queries.reshape(seq_count, piece, heads_q, head_dim)
    grad_query_normed = grad_query_post * cosine_table - rotated_rows(grad_query_post * sine_table)
    grad_key_normed = own_grad[0] * cosine_table - rotated_rows(own_grad[0] * sine_table)
    grad_query_raw, query_gain_grad = head_norm_back(
        query_unit, query_inverse, grad_query_normed, query_gain.astype(jnp.float32)
    )
    grad_key_raw, key_gain_grad = head_norm_back(
        key_unit, key_inverse, grad_key_normed, key_gain.astype(jnp.float32)
    )
    grad_query_low = grad_query_raw.reshape(rows, heads_q * head_dim).astype(jnp.bfloat16)
    grad_key_low = grad_key_raw.reshape(rows, heads_kv * head_dim).astype(jnp.bfloat16)
    grad_value_low = own_grad[1].reshape(rows, heads_kv * head_dim).astype(jnp.bfloat16)
    query_piece, key_piece, value_piece = lax.all_gather(
        (w_query, key_matrix, value_matrix), "shard", axis=0, tiled=True
    )
    grad_in = (
        jnp.einsum("rf,nf->rn", grad_query_low, query_piece, preferred_element_type=jnp.float32)
        + jnp.einsum("rf,nf->rn", grad_key_low, key_piece, preferred_element_type=jnp.float32)
        + jnp.einsum("rf,nf->rn", grad_value_low, value_piece, preferred_element_type=jnp.float32)
    )
    grad_tokens = (
        (grad_resid + norm_back(x_unit, inverse_in, grad_in * attn_gains))
        .astype(jnp.bfloat16)
        .reshape(seq_count, piece, width)
    )
    attn_gain_part = jnp.sum(x_unit * grad_in, 0)
    normalized_rows = attn_in
    attn_grads = jax.tree.map(
        lambda part: lax.psum_scatter(
            part.astype(jnp.bfloat16), "shard", scatter_dimension=0, tiled=True
        ).astype(jnp.float32),
        (
            outer(normalized_rows, grad_query_low),
            outer(normalized_rows, grad_key_low),
            outer(normalized_rows, grad_value_low),
            outer(resid_low, mixed_rows),
        ),
    )
    head_grads = lax.psum(
        (query_gain_grad, key_gain_grad, attn_gain_part, mlp_gain_part), ("rep", "shard")
    )
    attn_gain_total = lax.dynamic_slice_in_dim(head_grads[2], shard_at * owned, owned, 0)
    mlp_gain_total = lax.dynamic_slice_in_dim(head_grads[3], shard_at * owned, owned, 0)
    summed = (
        lax.psum(attn_grads[0].astype(jnp.bfloat16), "rep").astype(jnp.float32),
        lax.psum(attn_grads[1].astype(jnp.bfloat16), "rep").astype(jnp.float32),
        lax.psum(attn_grads[2].astype(jnp.bfloat16), "rep").astype(jnp.float32),
        lax.psum(attn_grads[3].astype(jnp.bfloat16), "rep").astype(jnp.float32),
        lax.psum(mlp_grads[0].astype(jnp.bfloat16), "rep").astype(jnp.float32),
        lax.psum(mlp_grads[1].astype(jnp.bfloat16), "rep").astype(jnp.float32),
        lax.psum(mlp_grads[2].astype(jnp.bfloat16), "rep").astype(jnp.float32),
    )
    attn_grads = summed[:4]
    mlp_grads = summed[4:]
    return (
        output,
        grad_tokens,
        attn_gain_total,
        attn_grads[0],
        attn_grads[1],
        attn_grads[2],
        head_grads[0],
        head_grads[1],
        attn_grads[3],
        mlp_gain_total,
        mlp_grads[0],
        mlp_grads[1],
        mlp_grads[2],
    )


CORE, ACROSS_X, ACROSS_Y = 1, 2, 4
VMEM_BYTES = 56 * 2**20
FREE = pl.CostEstimate(flops=1, bytes_accessed=1, transcendentals=0)


def across(x, mask):
    count = lax.axis_size("rep")
    return lax.ppermute(x, "rep", [(i, i ^ mask) for i in range(count)])


def around(x, by):
    count = lax.axis_size("shard")
    return lax.ppermute(x, "shard", [(i, (i + by) % count) for i in range(count)])


class Stage(dict):
    __getattr__ = dict.__getitem__
    __setattr__ = dict.__setitem__
    __delattr__ = dict.__delitem__

    def end(self):
        self.update(lax.optimization_barrier(dict(self)))


def in_order(calls):
    outs = []
    for call, first, *rest in calls:
        if outs:
            last = outs[-1][0] if isinstance(outs[-1], (list, tuple)) else outs[-1]
            first = lax.optimization_barrier((first, last))[0]
        outs.append(call(first, *rest))
    return outs


def ring_sum_first(chunks):
    return around(chunks[2], 1), around(chunks[1], -1)


def near(piece):
    return across(piece, ACROSS_X), across(piece, ACROSS_Y)


def far(from_x, from_y):
    half = from_x.shape[0] // 2
    return across(from_x[:half], ACROSS_Y), across(from_y[half:], ACROSS_X)


def rounded_sum(*parts):
    return sum(part.astype(jnp.float32) for part in parts).astype(jnp.bfloat16)


def sequence_pairs(turn):
    groups, shards = lax.axis_size("rep"), lax.axis_size("shard")
    pairs = []
    for group in range(groups):
        chip, core = divmod(group, 2)
        for at in range(shards):
            to_group, to_shard = 2 * chip + at // 2, 2 * core + (turn ^ (at & 1))
            pairs.append((group * shards + at, to_group * shards + to_shard))
    return pairs


def rolled(x):
    count, at = lax.axis_size("shard"), lax.axis_index("shard")
    width = x.shape[1] // count
    return jnp.concatenate(
        [lax.dynamic_slice_in_dim(x, ((at - i) % count) * width, width, 1) for i in range(count)],
        1,
    )


def sequence_cuts(x):
    odd = lax.axis_index("shard") & 1
    return [lax.dynamic_index_in_dim(x, turn ^ odd, 0, keepdims=False) for turn in range(2)]


def to_sequence(cut, turn):
    return lax.ppermute(cut, ("rep", "shard"), sequence_pairs(turn))


def from_sequences_send(x):
    odd = lax.axis_index("shard") & 1
    x = x.reshape(2, x.shape[0] // 2, x.shape[1])
    return [
        lax.ppermute(
            lax.dynamic_index_in_dim(x, turn ^ odd, 0, keepdims=False),
            ("rep", "shard"),
            [(to, at) for at, to in sequence_pairs(turn)],
        )
        for turn in range(2)
    ]


def in_turn(came):
    even = lax.axis_index("shard") & 1 == 0
    return [jnp.where(even, came[0], came[1]), jnp.where(even, came[1], came[0])]


def column_block(weights, at):
    cuts = [w.shape[1] // 8 for w in weights]
    return jnp.concatenate(
        [lax.dynamic_slice_in_dim(w, at * cut, cut, 1) for w, cut in zip(weights, cuts)], 1
    )


def whole_columns(me, own, other, widths, part=0):
    rows, columns = own.shape[0] // 4, sum(widths)

    def body(me_ref, own_ref, other_ref, *outs):
        def put(block):
            start = 0
            for out, width in zip(outs, widths):
                out[...] = block[:, start : start + width].astype(jnp.float32)
                start += width

        mine = (me_ref[0] ^ pl.program_id(0)) & 1 == 0
        pl.when(mine)(lambda: put(own_ref))
        pl.when(jnp.logical_not(mine))(lambda: put(other_ref))

    spec = pl.BlockSpec((rows, columns), lambda i, at: ((at[0] ^ i) >> 1, part))
    return pl.pallas_call(
        body,
        grid_spec=pltpu.PrefetchScalarGridSpec(
            num_scalar_prefetch=1,
            grid=(8,),
            in_specs=[spec, spec],
            out_specs=[pl.BlockSpec((rows, w), lambda i, at: (0, i)) for w in widths],
        ),
        out_shape=[jax.ShapeDtypeStruct((rows, 8 * w), jnp.float32) for w in widths],
        compiler_params=pltpu.CompilerParams(vmem_limit_bytes=VMEM_BYTES),
        cost_estimate=FREE,
        name="whole_columns",
    )(me, own, other)


def turned(x):
    return pltpu.roll(x, x.shape[-1] // 2, x.ndim - 1)


def nt(left, right):
    return lax.dot_general(
        left, right, (((1,), (1,)), ((), ())), preferred_element_type=jnp.float32
    )


def tn(left, right):
    return lax.dot_general(
        left, right, (((0,), (0,)), ((), ())), preferred_element_type=jnp.float32
    )


def unit_of(raw):
    inverse = lax.rsqrt(jnp.mean(raw * raw, -1, keepdims=True) + EPS)
    return raw * inverse, inverse


def project_body(
    normed, own0, came0, own1, came1, cosine, sine, gains, raw, query, key_value
):
    step = own0.shape[0]
    dim = cosine.shape[1]
    for block, (own, came) in enumerate(((own0, came0), (own1, came1))):
        at = block * 4 * dim
        raw[:, at : at + 4 * dim] = jnp.dot(
            normed[:, :step], own[...], preferred_element_type=jnp.float32
        ) + jnp.dot(normed[:, step:], came[...], preferred_element_type=jnp.float32)
        for i in range(3):
            unit, _ = unit_of(raw[:, at + i * dim : at + (i + 1) * dim])
            head = unit * gains[i // 2 : i // 2 + 1, :]
            head = (head * cosine[...] + turned(head) * sine[...]).astype(jnp.bfloat16)
            if i < 2:
                query[:, (2 * block + i) * dim : (2 * block + i + 1) * dim] = head
            else:
                key_value[:, 2 * block * dim : (2 * block + 1) * dim] = head
        key_value[:, (2 * block + 1) * dim : (2 * block + 2) * dim] = raw[
            :, at + 3 * dim : at + 4 * dim
        ].astype(jnp.bfloat16)


def window_mask(info, part, rows, columns):
    half = columns - rows
    row = lax.broadcasted_iota(jnp.int32, (rows, columns), 0)
    column = lax.broadcasted_iota(jnp.int32, (rows, columns), 1)
    gap = column - row - half
    slot = column + ((info[0] - 1) * half + part * rows)
    allowed = (gap <= 0) & (gap > -half) & (slot >= 0) & ((slot < info[1]) | (gap == 0))
    mask = jnp.where(allowed, 0.0, NEG)
    return jnp.concatenate([mask, mask], 0)


def two_heads(ref, at, block, dim):
    return jnp.concatenate(
        [ref[at, h * dim : (h + 1) * dim] for h in (2 * block, 2 * block + 1)], 0
    )


def key_columns(block, dim):
    key = slice(2 * block * dim, (2 * block + 1) * dim)
    value = slice((2 * block + 1) * dim, (2 * block + 2) * dim)
    return key, value


def seen_pair(before, own, part, block, dim):
    here, there = key_columns(block, dim), key_columns(1 - block, dim)
    rows = own.shape[0] // 2
    if part == 0:
        return [
            jnp.concatenate([before[:, t], own[:rows, h]], 0) for h, t in zip(here, there)
        ]
    return [jnp.concatenate([before[rows:, t], own[:, h]], 0) for h, t in zip(here, there)]


def attend_body(info, query, before, own, mixed, log_total):
    dim = own.shape[1] // 4
    rows = query.shape[0] // 2
    for part in range(2):
        at = slice(part * rows, (part + 1) * rows)
        mask = window_mask(info, part, rows, 3 * rows)
        for block in range(2):
            keys, values = seen_pair(before, own, part, block, dim)
            score = nt(two_heads(query, at, block, dim), keys) * dim**-0.5 + mask
            top = jnp.max(score, -1, keepdims=True)
            expo = jnp.exp(score - top)
            total = jnp.sum(expo, -1, keepdims=True)
            prob = (expo * (1.0 / total)).astype(jnp.bfloat16)
            out = jnp.dot(prob, values, preferred_element_type=jnp.float32).astype(jnp.bfloat16)
            log = jnp.broadcast_to(top + jnp.log(total), (2 * rows, dim))
            for i in range(2):
                on = slice((2 * block + i) * dim, (2 * block + i + 1) * dim)
                mixed[at, on] = out[i * rows : (i + 1) * rows]
                log_total[at, on] = log[i * rows : (i + 1) * rows]


def attend_back_body(
    info, query, before, own, log_total, grad_resid, weight0, weight1, raw, cosine, sine, gain,
    grad_query, grad_own, grad_before, gain_part, grad_keys, grad_values, grad_mixed,
):
    dim = own.shape[1] // 4
    rows = query.shape[0] // 2
    scale = dim**-0.5
    gain_total = jnp.zeros((1, dim), jnp.float32)
    masks = [window_mask(info, part, rows, 3 * rows) for part in range(2)]
    for block, weight in enumerate((weight0, weight1)):
        on = slice(2 * block * dim, 2 * (block + 1) * dim)
        grad_mixed[:, on] = jnp.dot(
            grad_resid[...], weight[...], preferred_element_type=jnp.float32
        ).astype(jnp.bfloat16)
        grad_keys[...] = jnp.zeros_like(grad_keys)
        grad_values[...] = jnp.zeros_like(grad_values)
        for part in range(2):
            keys, values = seen_pair(before, own, part, block, dim)
            at = slice(part * rows, (part + 1) * rows)
            seen = slice(part * rows, part * rows + 3 * rows)
            queries = two_heads(query, at, block, dim)
            grads = two_heads(grad_mixed, at, block, dim)
            log = two_heads(log_total, at, block, dim)[:, :1]
            prob = jnp.exp(nt(queries, keys) * scale + masks[part] - log)
            grad_prob = nt(grads, values)
            inner = jnp.sum(prob * grad_prob, -1, keepdims=True)
            grad_score = (prob * (grad_prob - inner)).astype(jnp.bfloat16)
            grad_values[seen, :] += tn(prob.astype(jnp.bfloat16), grads)
            grad_keys[seen, :] += tn(grad_score, queries) * scale
            both = jnp.dot(grad_score, keys, preferred_element_type=jnp.float32) * scale
            for i in range(2):
                head = 2 * block + i
                back = both[i * rows : (i + 1) * rows]
                back = back * cosine[at, :] - turned(back) * sine[at, :]
                there = (2 * head - head % 2) * dim
                unit, inverse = unit_of(raw[at, there : there + dim])
                gain_total += jnp.sum(unit * back, 0, keepdims=True)
                back = back * gain[...]
                back = inverse * (back - unit * jnp.mean(back * unit, -1, keepdims=True))
                grad_query[at, head * dim : (head + 1) * dim] = back.astype(jnp.bfloat16)
        for grad, here, there in zip(
            (grad_keys, grad_values), key_columns(block, dim), key_columns(1 - block, dim)
        ):
            grad_before[:, there] = grad[: 2 * rows, :].astype(jnp.bfloat16)
            grad_own[:, here] = grad[2 * rows :, :]
    gain_part[...] = gain_total


def finish_body(grad_query, grad_own, came, raw, cosine, sine, gain, even, odd, gain_part):
    dim = cosine.shape[1]
    total = jnp.zeros((1, dim), jnp.float32)
    for block, out in enumerate((even, odd)):
        key, value = key_columns(block, dim)
        back = grad_own[:, key] + came[:, key].astype(jnp.float32)
        back = back * cosine[...] - turned(back) * sine[...]
        unit, inverse = unit_of(raw[:, (4 * block + 2) * dim : (4 * block + 3) * dim])
        total += jnp.sum(unit * back, 0, keepdims=True)
        back = back * gain[...]
        back = inverse * (back - unit * jnp.mean(back * unit, -1, keepdims=True))
        out[:, : 2 * dim] = grad_query[:, 2 * block * dim : (2 * block + 2) * dim]
        out[:, 2 * dim : 3 * dim] = back.astype(jnp.bfloat16)
        grad_value = grad_own[:, value] + came[:, value].astype(jnp.float32)
        out[:, 3 * dim :] = grad_value.astype(jnp.bfloat16)
    gain_part[...] = total


def vmem_call(body, outs, scratch=(), scalars=0, name=None):
    def call(*args):
        in_specs = [
            pl.BlockSpec(memory_space=pltpu.SMEM if i < scalars else pltpu.VMEM)
            for i in range(len(args))
        ]
        return pl.pallas_call(
            body,
            grid=(1,),
            out_shape=outs,
            in_specs=in_specs,
            out_specs=jax.tree.map(lambda _: pl.BlockSpec(memory_space=pltpu.VMEM), outs),
            scratch_shapes=scratch,
            compiler_params=pltpu.CompilerParams(vmem_limit_bytes=VMEM_BYTES),
        cost_estimate=FREE,
            name=name,
        )(*args)

    return call


def hidden_units(mids, grads_y, weights):
    width, units = weights.shape[0], weights.shape[1] // 3
    count = len(mids)
    heights = [m.shape[0] for m in mids]
    rows, cut = sum(heights), units // 3

    def body(*refs):
        gate_w, up_w, w_down, act, grad_gate, grad_up = refs[2 * count :]
        start = 0
        for mid, grad_y in zip(refs[:count], refs[count : 2 * count]):
            at = slice(start, start + mid.shape[0])
            start += mid.shape[0]
            gate = jnp.dot(mid[...], gate_w[...], preferred_element_type=jnp.float32)
            up = jnp.dot(mid[...], up_w[...], preferred_element_type=jnp.float32)
            grad_act = jnp.dot(grad_y[...], w_down[...], preferred_element_type=jnp.float32)
            sigma = jax.nn.sigmoid(gate)
            swish = gate * sigma
            act[at, :] = (swish * up).astype(jnp.bfloat16)
            slope = grad_act * up * sigma * (1.0 + gate * (1.0 - sigma))
            grad_gate[at, :] = slope.astype(jnp.bfloat16)
            grad_up[at, :] = (grad_act * swish).astype(jnp.bfloat16)

    row_specs = [
        pl.BlockSpec((h, width), lambda j: (0, 0), pipeline_mode=pl.Buffered(1)) for h in heights
    ]
    return pl.pallas_call(
        body,
        grid=(3,),
        out_shape=[jax.ShapeDtypeStruct((rows, units), jnp.bfloat16)] * 3,
        in_specs=[
            *row_specs,
            *row_specs,
            pl.BlockSpec((width, cut), lambda j: (0, j)),
            pl.BlockSpec((width, cut), lambda j: (0, j + 3)),
            pl.BlockSpec((width, cut), lambda j: (0, j + 6)),
        ],
        out_specs=[pl.BlockSpec((rows, cut), lambda j: (0, j))] * 3,
        compiler_params=pltpu.CompilerParams(vmem_limit_bytes=VMEM_BYTES),
        cost_estimate=FREE,
        name="hidden_units",
    )(*mids, *grads_y, weights, weights, weights)


def from_hidden(pairs, eighths):
    count, parts = len(pairs), len(eighths)
    rows, units = pairs[0][0].shape[0] // 8, pairs[0][0].shape[1]
    width = pairs[0][1].shape[0]
    cut = width // 4

    def body(*refs):
        ins, outs = refs[: -(parts // 2)], refs[-(parts // 2) :]
        total = 0.0
        for i in range(count):
            part = ins[i * (parts + 1) : (i + 1) * (parts + 1)]
            left = jnp.concatenate([p[...] for p in part[:-1]], 0)
            total = total + nt(left, part[-1][...])
        for i, out in enumerate(outs):
            out[...] = total[2 * i * rows : 2 * (i + 1) * rows].astype(jnp.bfloat16)

    specs, args = [], []
    for left, right, at in pairs:
        specs += [pl.BlockSpec((rows, units), lambda j, e=e: (e, 0)) for e in eighths]
        specs.append(pl.BlockSpec((cut, units), lambda j, at=at: (j, at)))
        args += [left] * parts + [right]
    return pl.pallas_call(
        body,
        grid=(4,),
        out_shape=[jax.ShapeDtypeStruct((2 * rows, width), jnp.bfloat16)] * (parts // 2),
        in_specs=specs,
        out_specs=[pl.BlockSpec((2 * rows, cut), lambda j: (0, j))] * (parts // 2),
        compiler_params=pltpu.CompilerParams(vmem_limit_bytes=VMEM_BYTES),
        cost_estimate=FREE,
        name="from_hidden",
    )(*args)


def row_outer(lefts, groups, first, tiles, added=None, places=None, part=None):
    rights = [right for group in groups for right in group]
    places = range(len(rights)) if places is None else places
    added = [] if added is None else [added] * len(rights)
    width = lefts[0].shape[1]
    tile = width // 8
    count = len(lefts)
    rows = sum(left.shape[0] for left in lefts)
    wide = rights[0].shape[1] // (1 if part is None else 2)
    columns = [wide * len(group) for group in groups]

    def body(*refs):
        left_refs = refs[:count]
        right_refs = refs[count : count + len(rights)]
        add_refs = refs[count + len(rights) : count + len(rights) + len(added)]
        outs = refs[count + len(rights) + len(added) :]
        place = 0
        for i, group in enumerate(groups):
            column = 0
            for _ in group:
                on = slice(column, column + wide)
                total, start = 0.0, 0
                for left in left_refs:
                    stop = start + left.shape[0]
                    total = total + tn(left[...], right_refs[place][start:stop, :])
                    start = stop
                if added:
                    total = total + add_refs[place][...].astype(jnp.float32)
                outs[i][:, on] = total.astype(jnp.bfloat16)
                place += 1
                column += wide

    return pl.pallas_call(
        body,
        grid=(tiles,),
        out_shape=[jax.ShapeDtypeStruct((tiles * tile, c), jnp.bfloat16) for c in columns],
        in_specs=[
            *(pl.BlockSpec((left.shape[0], tile), lambda j: (0, j + first)) for left in lefts),
            *(
                pl.BlockSpec(
                    (right.shape[0], wide), lambda j: (0, part or 0), pipeline_mode=pl.Buffered(1)
                )
                for right in rights
            ),
            *(
                pl.BlockSpec((tile, wide), lambda j, at=at: (j + first, at))
                for at in places[: len(added)]
            ),
        ],
        out_specs=[pl.BlockSpec((tile, c), lambda j: (j, 0)) for c in columns],
        compiler_params=pltpu.CompilerParams(vmem_limit_bytes=VMEM_BYTES),
        cost_estimate=pl.CostEstimate(
            flops=2 * rows * tiles * tile * sum(columns),
            bytes_accessed=2 * rows * (width + sum(columns)),
            transcendentals=0,
        ),
        name="row_outer",
    )(*lefts, *rights, *added)


def close_body(x, *refs):
    mixed, weights = refs[:4], refs[4:12]
    gains, resid, mid = refs[12:]
    at = pl.program_id(0)
    step = x.shape[1]
    columns = weights[0].shape[1]
    total = x[...].astype(jnp.float32)
    for i in range(8):
        part = mixed[i // 2][:, (i % 2) * columns : (i % 2 + 1) * columns]
        total = total + nt(part, weights[i][...])
    resid[:, pl.ds(pl.multiple_of(at * step, step), step)] = total

    @pl.when(at == 3)
    def _():
        unit, _ = unit_of(resid[...])
        mid[...] = (unit * gains[...]).astype(jnp.bfloat16)


def close_attention(x, mixed, weights, gains):
    rows, width = x.shape
    step = width // 4
    whole = lambda a: pl.BlockSpec(a.shape, lambda j: (0, 0))
    return pl.pallas_call(
        close_body,
        grid=(4,),
        out_shape=[
            jax.ShapeDtypeStruct((rows, width), jnp.float32),
            jax.ShapeDtypeStruct((rows, width), jnp.bfloat16),
        ],
        in_specs=[
            pl.BlockSpec((rows, step), lambda j: (0, j)),
            *(whole(m) for m in mixed),
            *(pl.BlockSpec((step, w.shape[1]), lambda j: (j, 0)) for w in weights),
            whole(gains),
        ],
        out_specs=[pl.BlockSpec((rows, width), lambda j: (0, 0))] * 2,
        compiler_params=pltpu.CompilerParams(vmem_limit_bytes=VMEM_BYTES),
        cost_estimate=FREE,
        name="close_attention",
    )(x, *mixed, *weights, gains)


def back_to_rows(blocks, weights):
    rows = blocks[0].shape[0]
    step, columns = weights[0][0].shape
    count = len(blocks)

    def body(*refs):
        lefts = refs[:count]
        hbm = refs[count : 3 * count]
        out = refs[3 * count]
        held, sems = refs[3 * count + 1 :]
        copies = []
        for i in range(count):
            own, came = hbm[2 * i : 2 * i + 2]
            copies.append(
                [
                    pltpu.make_async_copy(own, held.at[i, :step], sems.at[i, 0]),
                    pltpu.make_async_copy(came, held.at[i, step:], sems.at[i, 1]),
                ]
            )
        for some in copies:
            for copy in some:
                copy.start()
        for i in range(count):
            for copy in copies[i]:
                copy.wait()
            for k in range(4):
                on = slice(k * step, (k + 1) * step)
                part = nt(lefts[i][...], held[i, on])
                if i == 0:
                    out[:, on] = part
                else:
                    out[:, on] += part

    return pl.pallas_call(
        body,
        grid=(1,),
        out_shape=jax.ShapeDtypeStruct((rows, 4 * step), jnp.float32),
        in_specs=[pl.BlockSpec(memory_space=pltpu.VMEM)] * count
        + [pl.BlockSpec(memory_space=pl.ANY)] * (2 * count),
        out_specs=pl.BlockSpec(memory_space=pltpu.VMEM),
        scratch_shapes=[
            pltpu.VMEM((count, 4 * step, columns), jnp.bfloat16),
            pltpu.SemaphoreType.DMA((count, 2)),
        ],
        compiler_params=pltpu.CompilerParams(vmem_limit_bytes=VMEM_BYTES),
        cost_estimate=FREE,
        name="back_to_rows",
    )(*blocks, *(part for w in weights for part in w))


def on_device_block(
    tokens,
    lengths,
    attn_gain,
    w_query,
    key_matrix,
    value_matrix,
    query_gain,
    key_gain,
    w_out,
    mlp_gain,
    w_gate,
    w_up,
    w_down,
    cotangent,
):
    low, full = jnp.bfloat16, jnp.float32
    width = tokens.shape[2]
    head_dim = query_gain.shape[0]
    shards = lax.axis_size("shard")
    shard_at = lax.axis_index("shard")
    me = lax.axis_index("rep")
    core = me & 1
    count = lax.axis_size("rep")

    s = Stage()
    piece = width // shards

    s.own_blocks = [
        column_block((w_query, key_matrix, value_matrix), me ^ i) for i in range(8)
    ]
    gain_rows = jnp.concatenate(
        [jnp.stack([attn_gain, mlp_gain]), jnp.zeros((14, piece), low)], 0
    )
    travelling = jnp.concatenate([s.own_blocks[0], gain_rows], 0)
    s.tokens_cuts, s.cotangent_cuts = sequence_cuts(tokens), sequence_cuts(cotangent)
    s.out_block = column_block((w_out,), me)
    s.ffn_block = column_block((w_gate, w_up, w_down), me)
    s.before, s.behind = around(travelling, 1), around(travelling, -1)
    s.other_lengths = across(lengths, CORE)
    s.end()

    s.ahead = around(s.before, 1)
    tokens_sent = [to_sequence(cut, turn) for turn, cut in enumerate(s.tokens_cuts)]
    out_own = lax.all_gather(s.out_block, "shard", axis=0, tiled=True)
    del s.out_block, s.tokens_cuts
    s.end()

    parts = (s.before, s.ahead, s.behind)
    s.came = jnp.concatenate([part[:piece] for part in parts], 0)
    s.gains = jnp.concatenate([gain_rows[:2], *(part[piece : piece + 2] for part in parts)], 1)
    s.came_near = near(s.came)
    s.came_own = across(s.came, CORE)
    s.x_came = tokens_sent
    del s.before, s.behind, s.ahead
    s.end()

    grad_y_sent = [to_sequence(cut, turn) for turn, cut in enumerate(s.cotangent_cuts)]
    s.came_far = far(*s.came_near)
    s.came_other = [s.came_own, *(across(block, CORE) for block in s.came_near)]
    gains = rolled(s.gains.astype(full))
    s.mlp_gains = gains[1:]
    s.attn_gains = gains[:1]
    s.x_low = jnp.concatenate(in_turn(s.x_came), 0)
    rows = s.x_low.shape[0]
    x_rows = s.x_low.astype(full)
    s.inverse_in = lax.rsqrt(jnp.mean(x_rows * x_rows, -1, keepdims=True) + EPS)
    s.normed = rolled((x_rows * s.inverse_in * s.attn_gains).astype(low))
    query_gains = query_gain.astype(full)[None]
    key_gains = key_gain.astype(full)[None]
    s.head_gains = jnp.concatenate([query_gains, key_gains], 0)
    both = jnp.where(
        core == 0,
        jnp.concatenate([lengths, s.other_lengths]),
        jnp.concatenate([s.other_lengths, lengths]),
    )
    length = lax.dynamic_index_in_dim(both, shard_at, 0, keepdims=False)
    s.info = jnp.stack([core, length]).astype(jnp.int32)
    query_pos = core * rows + jnp.arange(rows, dtype=jnp.int32)
    s.valid = (query_pos < length)[:, None].astype(full)
    cosine, sine = tables(query_pos, head_dim)
    s.cosine, sine = cosine[0, :, 0], sine[0, :, 0]
    s.sine = jnp.concatenate([-sine[:, : head_dim // 2], sine[:, head_dim // 2 :]], 1)
    s.out_own = out_own
    del s.gains, s.x_came, s.other_lengths, s.cotangent_cuts, s.came_own
    s.end()

    head_columns = 2 * head_dim
    block_columns = 4 * head_dim
    quad_rows = jax.ShapeDtypeStruct((rows, block_columns), low)
    quad_sums = jax.ShapeDtypeStruct((rows, block_columns), full)
    gain_sum = jax.ShapeDtypeStruct((1, head_dim), full)
    project = vmem_call(
        project_body,
        [jax.ShapeDtypeStruct((rows, 2 * block_columns), full), quad_rows, quad_rows],
        name="project",
    )
    attend = vmem_call(attend_body, [quad_rows, quad_sums], scalars=1, name="attend")
    attend_back = vmem_call(
        attend_back_body,
        [quad_rows, quad_sums, quad_rows, gain_sum],
        scratch=[pltpu.VMEM((2 * rows, head_dim), full)] * 2
        + [pltpu.VMEM((rows, block_columns), low)],
        scalars=1,
        name="attend_back",
    )
    finish = vmem_call(finish_body, [quad_rows, quad_rows, gain_sum], name="finish")
    upward = [(i, i + 1) for i in range(0, count, 2)]
    downward = [(i + 1, i) for i in range(0, count, 2)]

    def project_call(i, came, other):
        return (
            project, s.normed, s.own_blocks[2 * i], came, s.own_blocks[2 * i + 1], other,
            s.cosine, s.sine, s.head_gains,
        )

    def attend_call(projected, earlier):
        return (
            lambda query, own, before: attend(s.info, query, before, own),
            *projected[1:], earlier,
        )

    came_last = jnp.concatenate(s.came_far, 0)
    s.came_last = (came_last, across(came_last, CORE))
    s.out_near = near(s.out_own)
    s.out_own_other = across(s.out_own, CORE)
    s.projected = in_order(
        [
            project_call(i, block, other)
            for i, (block, other) in enumerate(zip((s.came, *s.came_near), s.came_other))
        ]
    )
    s.grad_y_came = grad_y_sent
    del s.came_far
    s.end()

    ffn_own = lax.all_gather(s.ffn_block, "shard", axis=0, tiled=True)
    grad_y = jnp.concatenate(in_turn(s.grad_y_came), 0)
    s.grad_y = jnp.where(s.valid > 0, grad_y, jnp.zeros_like(grad_y))
    grad_y_near = near(s.grad_y)
    s.out_far = far(*s.out_near)
    s.out_near_other = [across(block, CORE) for block in s.out_near]
    s.earlier = [lax.ppermute(p[2], "rep", upward) for p in s.projected]
    (s.projected_last,) = in_order([project_call(3, *s.came_last)])
    del s.ffn_block, s.grad_y_came
    s.end()

    out_last = jnp.concatenate(s.out_far, 0)
    s.out_last = (out_last, across(out_last, CORE))
    s.earlier_last = lax.ppermute(s.projected_last[2], "rep", upward)
    s.attended = in_order([attend_call(*pair) for pair in zip(s.projected, s.earlier)])
    s.grad_y_near = grad_y_near
    del s.out_far
    s.end()

    s.projected = [*s.projected, s.projected_last]
    s.earlier = [*s.earlier, s.earlier_last]
    s.out_blocks = [
        s.out_own, s.out_own_other, s.out_near[0], s.out_near_other[0], s.out_near[1],
        s.out_near_other[1], *s.out_last,
    ]
    (last,) = in_order([attend_call(s.projected_last, s.earlier_last)])
    s.attended = [*s.attended, last]
    s.mixed = [a[0] for a in s.attended]
    s.resid, s.mid = close_attention(s.x_low, s.mixed, s.out_blocks, s.mlp_gains)
    s.grad_y_far = far(*s.grad_y_near)
    s.came = [s.came, *s.came_near, s.came_last[0]]
    s.came_other = [*s.came_other, s.came_last[1]]
    del s.came_near, s.came_last
    del s.out_own, s.out_own_other, s.out_near, s.out_near_other, s.out_last
    del s.projected_last, s.earlier_last
    s.end()

    s.mid_near = near(s.mid)
    s.end()

    s.mid_far = far(*s.mid_near)
    s.ffn_own = ffn_own
    s.end()

    s.mids = [s.mid, *s.mid_near, *s.mid_far]
    s.grads_y = [s.grad_y, *s.grad_y_near, *s.grad_y_far]
    s.ffn_other = across(s.ffn_own, CORE)
    units = s.ffn_own.shape[1] // 3
    s.hidden_own = hidden_units(s.mids, s.grads_y, s.ffn_own)
    del s.mid, s.mid_near, s.mid_far, s.grad_y_near, s.grad_y_far
    s.end()

    def gate_up_pairs():
        return [
            (hidden[i], weights, i - 1)
            for hidden, weights in ((s.hidden_own, s.ffn_own), (s.hidden_other, s.ffn_other))
            for i in (1, 2)
        ]

    def down_pairs():
        return [(s.hidden_own[0], s.ffn_own, 2), (s.hidden_other[0], s.ffn_other, 2)]

    def from_hidden_call(pairs, eighths):
        return (
            lambda first: from_hidden([(first, *pairs[0][1:]), *pairs[1:]], eighths),
            pairs[0][0],
        )

    def outer_call(lefts, rights, *added):
        return lambda first: row_outer(lefts, [[first, *rights[1:]]], 0, 8, *added)[0], rights[0]

    def send_near(sent):
        return across(sent[0], ACROSS_X), across(sent[1], ACROSS_Y)

    def send_far(came, rest, split):
        one_tail, two_head = rest
        return (
            across(rounded_sum(one_tail, split(came[1])[1]), ACROSS_X),
            across(rounded_sum(two_head, split(came[0])[1]), ACROSS_Y),
        )

    def total(came, came_far, own, split):
        head, tail = own
        full_sum = lambda *parts: sum(part.astype(full) for part in parts)
        return jnp.concatenate(
            [
                full_sum(head, split(came[0])[0], came_far[1]),
                full_sum(tail, split(came[1])[0], came_far[0]),
            ],
            0,
        )

    by_rows = lambda a: jnp.split(a, 2, 0)
    by_columns = lambda a: jnp.split(a, 2, 1)
    to_plane, rest_of_plane = (2, 6, 5, 7), (3, 4, 0, 1)

    s.hidden_other = hidden_units(s.mids, s.grads_y, s.ffn_other)
    (s.down_outer,) = in_order([outer_call(s.grads_y, s.hidden_other[:1])])
    s.end()

    s.down_came = across(s.down_outer, CORE)
    s.mid_sent = from_hidden(gate_up_pairs(), to_plane)
    del s.down_outer
    s.end()

    s.mid_came = send_near(s.mid_sent)
    s.down_mine, s.mid_rest, s.gate_up_outer = in_order(
        [
            outer_call(s.grads_y, s.hidden_own[:1], s.down_came),
            from_hidden_call(gate_up_pairs(), rest_of_plane),
            outer_call(s.mids, s.hidden_other[1:]),
        ]
    )
    del s.mid_sent, s.down_came
    s.end()

    down_total = lax.psum_scatter(s.down_mine, "shard", scatter_dimension=0, tiled=True)
    s.mid_came_far = send_far(s.mid_came, by_rows(s.mid_rest[0]), by_rows)
    s.gate_up_came = across(s.gate_up_outer, CORE)
    s.mlp_sent, s.mlp_rest = in_order(
        [
            from_hidden_call(down_pairs(), to_plane),
            from_hidden_call(down_pairs(), rest_of_plane),
        ]
    )
    del s.gate_up_outer, s.down_mine
    s.end()

    def back_call(i):
        raw, query, own_pair = s.projected[i]
        return (
            lambda query, *rest: attend_back(s.info, query, *rest),
            query, s.earlier[i], own_pair, s.attended[i][1], s.resid_low,
            *s.out_blocks[2 * i : 2 * i + 2], raw, s.cosine, s.sine, s.head_gains[:1],
        )

    def finish_call(i):
        return (
            finish, s.backs[i][0], s.backs[i][1], s.returned[i], s.projected[i][0],
            s.cosine, s.sine, s.head_gains[1:],
        )

    def give_back(*chips):
        s.returned = s.returned | {
            i: lax.ppermute(s.backs[i][2], "rep", downward) for i in chips
        }

    def odd_call(left, blocks, part=None):
        return lambda first: row_outer([first], [blocks], 0, 8, part=part)[0], left

    def head_call(left, blocks, came, part=None, places=(0, 1, 2, 3)):
        groups = [[blocks[1], blocks[3]], [blocks[2]], [blocks[0]]]
        at = [places[i] for i in (1, 3, 2, 0)]
        return lambda first: row_outer([first], groups, 0, 4, came, at, part), left

    def tail_call(left, blocks, came, part=None, places=(0, 1, 2, 3)):
        groups = [[blocks[2], blocks[3]], [blocks[1]], [blocks[0]]]
        at = [places[i] for i in (2, 3, 1, 0)]
        return lambda first: row_outer([first], groups, 4, 4, came, at, part), left

    s.mlp_came = send_near(s.mlp_sent)
    grad_mid = total(s.mid_came, s.mid_came_far, by_rows(s.mid_rest[1]), by_rows)
    inverse_mid = lax.rsqrt(jnp.mean(s.resid * s.resid, -1, keepdims=True) + EPS)
    mid_unit = s.resid * inverse_mid
    s.mlp_gain_part = jnp.sum(mid_unit * grad_mid, 0)
    s.grad_resid = s.grad_y.astype(full) + norm_back(
        mid_unit, inverse_mid, grad_mid * s.mlp_gains
    )
    s.resid_low = s.grad_resid.astype(low)
    s.resid_rolled = rolled(s.resid_low)
    s.returned = {}
    back, s.out_odd, s.gate_up_mine = in_order(
        [
            back_call(3),
            odd_call(s.resid_rolled, s.mixed, 1),
            outer_call(s.mids, s.hidden_own[1:], s.gate_up_came),
        ]
    )
    s.backs = {3: back}
    s.down_total = down_total
    del s.mid_came, s.mid_came_far, s.mid_rest, s.gate_up_came, s.hidden_own, s.hidden_other
    del s.mids, s.grads_y, s.ffn_own, s.ffn_other, s.mlp_sent
    s.end()

    gate_up_total = lax.psum_scatter(s.gate_up_mine, "shard", scatter_dimension=0, tiled=True)
    s.mlp_came_far = send_far(s.mlp_came, by_rows(s.mlp_rest[0]), by_rows)
    s.out_came = across(s.out_odd, CORE)
    give_back(3)
    back1, back2 = in_order([back_call(1), back_call(2)])
    s.backs = s.backs | {1: back1, 2: back2}
    del s.out_odd, s.gate_up_mine
    s.end()

    s.down_near = near(s.down_total)
    give_back(1, 2)
    s.out_head, s.out_tail, back, finished = in_order(
        [
            head_call(s.resid_rolled, s.mixed, s.out_came, 0),
            tail_call(s.resid_rolled, s.mixed, s.out_came, 0),
            back_call(0),
            finish_call(3),
        ]
    )
    s.backs = s.backs | {0: back}
    s.finished = {3: finished}
    del s.out_came
    s.end()

    s.out_near = send_near((s.out_head[0], s.out_tail[0]))
    mlp_out = total(s.mlp_came, s.mlp_came_far, by_rows(s.mlp_rest[1]), by_rows)
    s.output = (s.valid * (s.resid + mlp_out)).astype(low)
    give_back(0)
    finished1, finished2 = in_order([finish_call(1), finish_call(2)])
    s.finished = s.finished | {1: finished1, 2: finished2}
    del s.mlp_came, s.mlp_came_far, s.mlp_rest, s.resid
    s.end()

    output_sent = from_sequences_send(s.output)
    s.out_far = send_far(s.out_near, (s.out_tail[1], s.out_head[1]), by_columns)
    s.down_far = far(*s.down_near)
    (finished,) = in_order([finish_call(0)])
    s.finished = s.finished | {0: finished}
    (s.odd,) = in_order([odd_call(s.normed, [s.finished[i][1] for i in range(4)])])
    s.gate_up_total = gate_up_total
    s.output_first = output_sent[0]
    del s.output
    s.end()

    my_group = me.astype(jnp.int32)[None]

    def whole_call(widths, own, other, part=0):
        return lambda first: whole_columns(my_group, first, other, widths, part), own

    s.gate_up_near = near(s.gate_up_total)
    s.qkv_came = across(s.odd, CORE)
    out_sum = total(s.out_near, s.out_far, (s.out_head[2], s.out_tail[2]), by_columns)
    s.out_chunks = jnp.split(out_sum.astype(low), shards, 0)
    s.out_ring = ring_sum_first(s.out_chunks)
    weights = [
        pair
        for i in range(4)
        for pair in (
            (s.own_blocks[2 * i], s.came[i]), (s.own_blocks[2 * i + 1], s.came_other[i])
        )
    ]
    blocks = [part for i in range(4) for part in s.finished[i][:2]]
    grad_in = rolled(back_to_rows(blocks, weights))
    x_unit = s.x_low.astype(full) * s.inverse_in
    s.gain_parts = jnp.concatenate(
        [
            jnp.sum(x_unit * grad_in, 0),
            s.mlp_gain_part,
            sum(s.backs[i][3] for i in range(4))[0],
            sum(s.finished[i][2] for i in range(4))[0],
        ]
    )
    s.grad_tokens = (
        s.grad_resid + norm_back(x_unit, s.inverse_in, grad_in * s.attn_gains)
    ).astype(low)
    del s.odd, s.out_near, s.out_far, s.out_head, s.out_tail, s.backs
    del s.own_blocks, s.came, s.came_other, s.grad_resid, s.x_low
    s.end()

    even = [s.finished[i][0] for i in range(4)]
    s.head0, s.tail0, s.head1, s.tail1 = in_order(
        [
            call(s.normed, even, s.qkv_came, half, range(half, 8, 2))
            for half in range(2)
            for call in (head_call, tail_call)
        ]
    )
    tokens_sent = from_sequences_send(s.grad_tokens)
    s.down_spread = jnp.concatenate([s.down_total, *s.down_near, *s.down_far], 0)
    s.down_spread_other = across(s.down_spread, CORE)
    s.output_second = output_sent[1]
    s.gate_up_far = far(*s.gate_up_near)
    del s.qkv_came, s.finished, s.down_total, s.down_near, s.down_far
    s.end()

    def qkv_chunks(came, came_far, head, tail):
        own = total(came, came_far, (head[2], tail[2]), by_columns)
        return jnp.split(own.astype(low), shards, 0)

    s.near0 = send_near((s.head0[0], s.tail0[0]))
    s.out_ring_last = around(rounded_sum(s.out_chunks[3], s.out_ring[0]), 1)
    s.tokens_first = tokens_sent[0]
    s.gain_came = across(s.gain_parts, CORE)
    s.end()

    s.far0 = send_far(s.near0, (s.tail0[1], s.head0[1]), by_columns)
    s.near1 = send_near((s.head1[0], s.tail1[0]))
    (s.whole_down,) = in_order([whole_call((units,), s.down_spread, s.down_spread_other)])
    first = lax.optimization_barrier((s.gate_up_total, s.whole_down[0]))[0]
    s.gate_up_own = jnp.concatenate([first, *s.gate_up_near, *s.gate_up_far], 0)
    s.out_total = rounded_sum(s.out_chunks[0], s.out_ring[1], s.out_ring_last)
    s.gain_parts = s.gain_parts + s.gain_came
    s.tokens_second = tokens_sent[1]
    del s.down_spread, s.down_spread_other, s.out_chunks, s.out_ring, s.out_ring_last
    del s.gate_up_near, s.gate_up_far, s.gate_up_total, s.grad_tokens
    s.end()

    s.chunks0 = qkv_chunks(s.near0, s.far0, s.head0, s.tail0)
    s.ring0 = ring_sum_first(s.chunks0)
    s.far1 = send_far(s.near1, (s.tail1[1], s.head1[1]), by_columns)
    s.gate_up_other = across(s.gate_up_own, CORE)
    del s.near0, s.far0, s.head0, s.tail0
    s.end()

    s.last0 = around(rounded_sum(s.chunks0[3], s.ring0[0]), 1)
    s.chunks1 = qkv_chunks(s.near1, s.far1, s.head1, s.tail1)
    s.ring1 = ring_sum_first(s.chunks1)
    s.gain_came = across(s.gain_parts, ACROSS_X)
    (s.whole_gate_up,) = in_order([whole_call((units, units), s.gate_up_own, s.gate_up_other)])
    del s.gate_up_own, s.gate_up_other
    del s.near1, s.far1, s.head1, s.tail1
    s.end()

    query_total = rounded_sum(s.chunks0[0], s.ring0[1], s.last0)
    s.total0 = jnp.concatenate([query_total, s.out_total], 1)
    s.spread0 = near(s.total0)
    s.last1 = around(rounded_sum(s.chunks1[3], s.ring1[0]), 1)
    s.gain_parts = s.gain_parts + s.gain_came
    s.gain_came = across(s.gain_parts, ACROSS_Y)
    del s.chunks0, s.ring0, s.last0, s.out_total
    s.end()

    s.spread_far0 = far(*s.spread0)
    s.total1 = rounded_sum(s.chunks1[0], s.ring1[1], s.last1)
    s.spread1 = near(s.total1)
    s.gain_parts = s.gain_parts + s.gain_came
    s.gain_came = lax.ppermute(s.gain_parts, "shard", [(i, i ^ 1) for i in range(shards)])
    del s.chunks1, s.ring1, s.last1
    s.end()

    s.own0 = jnp.concatenate([s.total0, *s.spread0, *s.spread_far0], 0)
    s.other0 = across(s.own0, CORE)
    s.spread_far1 = far(*s.spread1)
    s.gain_parts = s.gain_parts + s.gain_came
    s.gain_came = lax.ppermute(s.gain_parts, "shard", [(i, i ^ 2) for i in range(shards)])
    del s.total0, s.spread0, s.spread_far0
    s.end()

    s.own1 = jnp.concatenate([s.total1, *s.spread1, *s.spread_far1], 0)
    s.other1 = across(s.own1, CORE)
    (s.whole0,) = in_order([whole_call((head_columns, head_columns), s.own0, s.other0)])
    gain_sums = s.gain_parts + s.gain_came
    s.wide = lax.dynamic_slice_in_dim(
        gain_sums[: 2 * width].reshape(2, width), shard_at * piece, piece, 1
    )
    s.narrow = gain_sums[2 * width :]
    del s.own0, s.other0, s.total1, s.spread1, s.spread_far1
    s.end()

    ((whole_key, whole_value),) = in_order(
        [whole_call((head_dim, head_dim), s.own1, s.other1)]
    )
    return (
        jnp.stack(in_turn([s.output_first, s.output_second])),
        jnp.stack(in_turn([s.tokens_first, s.tokens_second])),
        s.wide[0],
        s.whole0[0],
        whole_key,
        whole_value,
        s.narrow[:head_dim],
        s.narrow[head_dim:],
        s.whole0[1],
        s.wide[1],
        *s.whole_gate_up,
        *s.whole_down,
    )


def solution(mesh):
    sizes = (mesh.shape["rep"], mesh.shape["shard"])
    return jax.shard_map(
        on_device_block if sizes == (8, 4) else on_device,
        mesh=mesh,
        in_specs=(
            P("rep", "shard", None),
            P("rep"),
            P("shard"),
            P("shard", None),
            P("shard", None),
            P("shard", None),
            P(),
            P(),
            P("shard", None),
            P("shard"),
            P("shard", None),
            P("shard", None),
            P("shard", None),
            P("rep", "shard", None),
        ),
        out_specs=(
            P("rep", "shard", None),
            P("rep", "shard", None),
            P("shard"),
            P("shard", None),
            P("shard", None),
            P("shard", None),
            P(),
            P(),
            P("shard", None),
            P("shard"),
            P("shard", None),
            P("shard", None),
            P("shard", None),
        ),
        check_vma=False,
    )
```

```python
import jax
import jax.numpy as jnp
from jax import lax
from jax.experimental import pallas as pl
from jax.experimental.pallas import tpu as pltpu
from jax.sharding import PartitionSpec as P

WINDOW = 512


EPS = 1e-06
ROPE_BASE = 1000000.0
NEG = -1e30


def passed_along(x, axis, by):
    devices = lax.axis_size(axis)
    pairs = [(i, i + by) for i in range(devices) if 0 <= i + by < devices]
    return lax.ppermute(x, axis, pairs)


def tables(positions, head_dim):
    half = head_dim // 2
    freq = ROPE_BASE ** (-jnp.arange(half, dtype=jnp.float32) * 2.0 / head_dim)
    angle = positions.astype(jnp.float32)[:, None] * freq[None, :]
    angle = jnp.concatenate([angle, angle], -1)
    return (jnp.cos(angle)[None, :, None, :], jnp.sin(angle)[None, :, None, :])


def rotated_rows(value_rows):
    half = value_rows.shape[-1] // 2
    return jnp.concatenate([-value_rows[..., half:], value_rows[..., :half]], -1)


def head_norm(raw, gain):
    inverse = lax.rsqrt(jnp.mean(raw * raw, -1, keepdims=True) + EPS)
    unit = raw * inverse
    return (unit, inverse, unit * gain)


def norm_back(unit, inverse, grad_unit):
    return inverse * (grad_unit - unit * jnp.mean(grad_unit * unit, -1, keepdims=True))


def head_norm_back(unit, inverse, grad_normed, gain):
    grad_raw = norm_back(unit, inverse, grad_normed * gain)
    return (grad_raw, jnp.sum(unit * grad_normed, axis=(0, 1, 2)))


def scores(query_rows, keys, allowed, scale):
    raw = (
        jnp.einsum("sqhgd,skhd->shgqk", query_rows, keys, preferred_element_type=jnp.float32)
        * scale
    )
    return jnp.where(allowed[:, None, None], raw, NEG)


def outer(left, right):
    return jnp.einsum("rc,rf->cf", left, right, preferred_element_type=jnp.float32)


def on_device(
    tokens,
    lengths,
    attn_gain,
    w_query,
    key_matrix,
    value_matrix,
    query_gain,
    key_gain,
    w_out,
    mlp_gain,
    w_gate,
    w_up,
    w_down,
    cotangent,
):
    seq_count, piece, width = tokens.shape
    head_dim = query_gain.shape[0]
    heads_q = w_query.shape[1] // head_dim
    heads_kv = key_matrix.shape[1] // head_dim
    groups = heads_q // heads_kv
    rows = seq_count * piece
    scale = head_dim ** (-0.5)
    reach = (WINDOW + piece - 2) // piece
    owned = width // lax.axis_size("shard")
    shard_at = lax.axis_index("shard")
    query_pos = shard_at * piece + jnp.arange(piece, dtype=jnp.int32)
    key_pos = (shard_at - reach) * piece + jnp.arange((reach + 1) * piece, dtype=jnp.int32)
    near = (
        (key_pos[None, :] <= query_pos[:, None])
        & (query_pos[:, None] - key_pos[None, :] < WINDOW)
        & (key_pos[None, :] >= 0)
    )
    live = (key_pos[None, None, :] < lengths[:, None, None]) | (
        key_pos[None, :] == query_pos[:, None]
    )[None]
    allowed = near[None] & live
    valid = (query_pos[None, :] < lengths[:, None]).astype(jnp.float32).reshape(rows, 1)
    cosine_table, sine_table = tables(query_pos, head_dim)
    x_rows = tokens.astype(jnp.float32).reshape(rows, width)
    inverse_in = lax.rsqrt(jnp.mean(x_rows * x_rows, -1, keepdims=True) + EPS)
    x_unit = x_rows * inverse_in
    gain_piece = lax.all_gather(attn_gain, "shard", axis=0, tiled=True)
    query_piece = lax.all_gather(w_query, "shard", axis=0, tiled=True)
    key_piece = lax.all_gather(key_matrix, "shard", axis=0, tiled=True)
    value_piece = lax.all_gather(value_matrix, "shard", axis=0, tiled=True)
    normed_piece = (x_unit * gain_piece.astype(jnp.float32)).astype(jnp.bfloat16)
    acc_q = jnp.dot(normed_piece, query_piece, preferred_element_type=jnp.float32)
    acc_k = jnp.dot(normed_piece, key_piece, preferred_element_type=jnp.float32)
    acc_v = jnp.dot(normed_piece, value_piece, preferred_element_type=jnp.float32)
    normalized_rows = normed_piece
    gains = gain_piece.astype(jnp.float32)
    attn_in = normalized_rows
    attn_gains = gains
    query_unit, query_inverse, query_rows_normalized = head_norm(
        acc_q.reshape(seq_count, piece, heads_q, head_dim), query_gain.astype(jnp.float32)
    )
    key_unit, key_inverse, key_normed = head_norm(
        acc_k.reshape(seq_count, piece, heads_kv, head_dim), key_gain.astype(jnp.float32)
    )
    query_rows = (
        (query_rows_normalized * cosine_table + rotated_rows(query_rows_normalized) * sine_table)
        .astype(jnp.bfloat16)
        .reshape(seq_count, piece, heads_kv, groups, head_dim)
    )
    keys_own = (key_normed * cosine_table + rotated_rows(key_normed) * sine_table).astype(
        jnp.bfloat16
    )
    values_own = acc_v.reshape(seq_count, piece, heads_kv, head_dim).astype(jnp.bfloat16)
    own_pair = jnp.stack([keys_own, values_own])
    parts = []
    for fetch_back in range(reach, 0, -1):
        parts.append(passed_along(own_pair, "shard", fetch_back))
    parts.append(own_pair)
    near_pair = jnp.concatenate(parts, 2)
    score = scores(query_rows, near_pair[0], allowed, scale)
    top = jnp.max(score, -1, keepdims=True)
    expo = jnp.exp(score - top)
    total = jnp.sum(expo, -1, keepdims=True)
    prob = expo / total
    log_total = top + jnp.log(total)
    mixed = jnp.einsum(
        "shgqk,skhd->sqhgd",
        prob.astype(jnp.bfloat16),
        near_pair[1],
        preferred_element_type=jnp.float32,
    )
    mixed_rows = mixed.reshape(rows, heads_q * head_dim).astype(jnp.bfloat16)
    resid = x_rows + jnp.einsum(
        "rf,nf->rn",
        mixed_rows,
        lax.all_gather(w_out, "shard", axis=0, tiled=True),
        preferred_element_type=jnp.float32,
    )
    inverse_mid = lax.rsqrt(jnp.mean(resid * resid, -1, keepdims=True) + EPS)
    mid_unit = resid * inverse_mid
    gain_piece = lax.all_gather(mlp_gain, "shard", axis=0, tiled=True)
    gate_piece = lax.all_gather(w_gate, "shard", axis=0, tiled=True)
    up_piece = lax.all_gather(w_up, "shard", axis=0, tiled=True)
    normed_piece = (mid_unit * gain_piece.astype(jnp.float32)).astype(jnp.bfloat16)
    acc_gate = jnp.dot(normed_piece, gate_piece, preferred_element_type=jnp.float32)
    acc_up = jnp.dot(normed_piece, up_piece, preferred_element_type=jnp.float32)
    normalized_rows = normed_piece
    gains = gain_piece.astype(jnp.float32)
    mlp_in = normalized_rows
    sigma = jax.nn.sigmoid(acc_gate)
    swish = acc_gate * sigma
    act = (swish * acc_up).astype(jnp.bfloat16)
    mlp_out = jnp.einsum(
        "rf,nf->rn",
        act,
        lax.all_gather(w_down, "shard", axis=0, tiled=True),
        preferred_element_type=jnp.float32,
    )
    output = (valid * (resid + mlp_out)).astype(jnp.bfloat16).reshape(seq_count, piece, width)
    grad_y = cotangent.astype(jnp.float32).reshape(rows, width) * valid
    grad_y_low = grad_y.astype(jnp.bfloat16)
    grad_act = jnp.dot(
        grad_y_low,
        lax.all_gather(w_down, "shard", axis=0, tiled=True),
        preferred_element_type=jnp.float32,
    )
    grad_gate = (grad_act * acc_up * sigma * (1.0 + acc_gate * (1.0 - sigma))).astype(jnp.bfloat16)
    grad_up = (grad_act * swish).astype(jnp.bfloat16)
    gate_piece, up_piece = lax.all_gather((w_gate, w_up), "shard", axis=0, tiled=True)
    grad_mid = jnp.einsum(
        "rf,nf->rn", grad_gate, gate_piece, preferred_element_type=jnp.float32
    ) + jnp.einsum("rf,nf->rn", grad_up, up_piece, preferred_element_type=jnp.float32)
    grad_resid = grad_y + norm_back(mid_unit, inverse_mid, grad_mid * gains)
    mlp_gain_part = jnp.sum(mid_unit * grad_mid, 0)
    normalized_rows = mlp_in
    mlp_grads = jax.tree.map(
        lambda part: lax.psum_scatter(
            part.astype(jnp.bfloat16), "shard", scatter_dimension=0, tiled=True
        ).astype(jnp.float32),
        (
            outer(normalized_rows, grad_gate),
            outer(normalized_rows, grad_up),
            outer(grad_y_low, act),
        ),
    )
    resid_low = grad_resid.astype(jnp.bfloat16)
    grad_mixed = jnp.dot(
        resid_low,
        lax.all_gather(w_out, "shard", axis=0, tiled=True),
        preferred_element_type=jnp.float32,
    )
    grad_mixed = grad_mixed.astype(jnp.bfloat16).reshape(
        seq_count, piece, heads_kv, groups, head_dim
    )
    prob_again = jnp.exp(scores(query_rows, near_pair[0], allowed, scale) - log_total)
    grad_prob = jnp.einsum(
        "sqhgd,skhd->shgqk", grad_mixed, near_pair[1], preferred_element_type=jnp.float32
    )
    grad_values = jnp.einsum(
        "shgqk,sqhgd->skhd",
        prob_again.astype(jnp.bfloat16),
        grad_mixed,
        preferred_element_type=jnp.float32,
    )
    grad_score = (
        prob_again * (grad_prob - jnp.sum(prob_again * grad_prob, -1, keepdims=True))
    ).astype(jnp.bfloat16)
    grad_queries = (
        jnp.einsum(
            "shgqk,skhd->sqhgd", grad_score, near_pair[0], preferred_element_type=jnp.float32
        )
        * scale
    )
    grad_keys = (
        jnp.einsum("shgqk,sqhgd->skhd", grad_score, query_rows, preferred_element_type=jnp.float32)
        * scale
    )
    grad_pair = jnp.stack([grad_keys, grad_values])
    own_grad = grad_pair[:, :, reach * piece :]
    for back in range(1, reach + 1):
        lower = (reach - back) * piece
        own_grad = own_grad + passed_along(grad_pair[:, :, lower : lower + piece], "shard", -back)
    grad_query_post = grad_queries.reshape(seq_count, piece, heads_q, head_dim)
    grad_query_normed = grad_query_post * cosine_table - rotated_rows(grad_query_post * sine_table)
    grad_key_normed = own_grad[0] * cosine_table - rotated_rows(own_grad[0] * sine_table)
    grad_query_raw, query_gain_grad = head_norm_back(
        query_unit, query_inverse, grad_query_normed, query_gain.astype(jnp.float32)
    )
    grad_key_raw, key_gain_grad = head_norm_back(
        key_unit, key_inverse, grad_key_normed, key_gain.astype(jnp.float32)
    )
    grad_query_low = grad_query_raw.reshape(rows, heads_q * head_dim).astype(jnp.bfloat16)
    grad_key_low = grad_key_raw.reshape(rows, heads_kv * head_dim).astype(jnp.bfloat16)
    grad_value_low = own_grad[1].reshape(rows, heads_kv * head_dim).astype(jnp.bfloat16)
    query_piece, key_piece, value_piece = lax.all_gather(
        (w_query, key_matrix, value_matrix), "shard", axis=0, tiled=True
    )
    grad_in = (
        jnp.einsum("rf,nf->rn", grad_query_low, query_piece, preferred_element_type=jnp.float32)
        + jnp.einsum("rf,nf->rn", grad_key_low, key_piece, preferred_element_type=jnp.float32)
        + jnp.einsum("rf,nf->rn", grad_value_low, value_piece, preferred_element_type=jnp.float32)
    )
    grad_tokens = (
        (grad_resid + norm_back(x_unit, inverse_in, grad_in * attn_gains))
        .astype(jnp.bfloat16)
        .reshape(seq_count, piece, width)
    )
    attn_gain_part = jnp.sum(x_unit * grad_in, 0)
    normalized_rows = attn_in
    attn_grads = jax.tree.map(
        lambda part: lax.psum_scatter(
            part.astype(jnp.bfloat16), "shard", scatter_dimension=0, tiled=True
        ).astype(jnp.float32),
        (
            outer(normalized_rows, grad_query_low),
            outer(normalized_rows, grad_key_low),
            outer(normalized_rows, grad_value_low),
            outer(resid_low, mixed_rows),
        ),
    )
    head_grads = lax.psum(
        (query_gain_grad, key_gain_grad, attn_gain_part, mlp_gain_part), ("rep", "shard")
    )
    attn_gain_total = lax.dynamic_slice_in_dim(head_grads[2], shard_at * owned, owned, 0)
    mlp_gain_total = lax.dynamic_slice_in_dim(head_grads[3], shard_at * owned, owned, 0)
    summed = (
        lax.psum(attn_grads[0].astype(jnp.bfloat16), "rep").astype(jnp.float32),
        lax.psum(attn_grads[1].astype(jnp.bfloat16), "rep").astype(jnp.float32),
        lax.psum(attn_grads[2].astype(jnp.bfloat16), "rep").astype(jnp.float32),
        lax.psum(attn_grads[3].astype(jnp.bfloat16), "rep").astype(jnp.float32),
        lax.psum(mlp_grads[0].astype(jnp.bfloat16), "rep").astype(jnp.float32),
        lax.psum(mlp_grads[1].astype(jnp.bfloat16), "rep").astype(jnp.float32),
        lax.psum(mlp_grads[2].astype(jnp.bfloat16), "rep").astype(jnp.float32),
    )
    attn_grads = summed[:4]
    mlp_grads = summed[4:]
    return (
        output,
        grad_tokens,
        attn_gain_total,
        attn_grads[0],
        attn_grads[1],
        attn_grads[2],
        head_grads[0],
        head_grads[1],
        attn_grads[3],
        mlp_gain_total,
        mlp_grads[0],
        mlp_grads[1],
        mlp_grads[2],
    )


CORE, ACROSS_X, ACROSS_Y = 1, 2, 4
VMEM_BYTES = 56 * 2**20
FREE = pl.CostEstimate(flops=1, bytes_accessed=1, transcendentals=0)


def across(x, mask):
    count = lax.axis_size("rep")
    return lax.ppermute(x, "rep", [(i, i ^ mask) for i in range(count)])


def around(x, by):
    count = lax.axis_size("shard")
    return lax.ppermute(x, "shard", [(i, (i + by) % count) for i in range(count)])


class Stage(dict):
    __getattr__ = dict.__getitem__
    __setattr__ = dict.__setitem__
    __delattr__ = dict.__delitem__

    def end(self):
        self.update(lax.optimization_barrier(dict(self)))


def in_order(calls):
    outs = []
    for call, first, *rest in calls:
        if outs:
            last = outs[-1][0] if isinstance(outs[-1], (list, tuple)) else outs[-1]
            first = lax.optimization_barrier((first, last))[0]
        outs.append(call(first, *rest))
    return outs


def ring_sum_first(chunks):
    return around(chunks[2], 1), around(chunks[1], -1)


def near(piece):
    return across(piece, ACROSS_X), across(piece, ACROSS_Y)


def far(from_x, from_y):
    half = from_x.shape[0] // 2
    return across(from_x[:half], ACROSS_Y), across(from_y[half:], ACROSS_X)


def rounded_sum(*parts):
    return sum(part.astype(jnp.float32) for part in parts).astype(jnp.bfloat16)


def sequence_pairs(turn):
    groups, shards = lax.axis_size("rep"), lax.axis_size("shard")
    pairs = []
    for group in range(groups):
        chip, core = divmod(group, 2)
        for at in range(shards):
            to_group, to_shard = 2 * chip + at // 2, 2 * core + (turn ^ (at & 1))
            pairs.append((group * shards + at, to_group * shards + to_shard))
    return pairs


def rolled(x):
    count, at = lax.axis_size("shard"), lax.axis_index("shard")
    width = x.shape[1] // count
    return jnp.concatenate(
        [lax.dynamic_slice_in_dim(x, ((at - i) % count) * width, width, 1) for i in range(count)],
        1,
    )


def sequence_cuts(x):
    odd = lax.axis_index("shard") & 1
    return [lax.dynamic_index_in_dim(x, turn ^ odd, 0, keepdims=False) for turn in range(2)]


def to_sequence(cut, turn):
    return lax.ppermute(cut, ("rep", "shard"), sequence_pairs(turn))


def from_sequences_send(x):
    odd = lax.axis_index("shard") & 1
    x = x.reshape(2, x.shape[0] // 2, x.shape[1])
    return [
        lax.ppermute(
            lax.dynamic_index_in_dim(x, turn ^ odd, 0, keepdims=False),
            ("rep", "shard"),
            [(to, at) for at, to in sequence_pairs(turn)],
        )
        for turn in range(2)
    ]


def in_turn(came):
    even = lax.axis_index("shard") & 1 == 0
    return [jnp.where(even, came[0], came[1]), jnp.where(even, came[1], came[0])]


def column_block(weights, at):
    cuts = [w.shape[1] // 8 for w in weights]
    return jnp.concatenate(
        [lax.dynamic_slice_in_dim(w, at * cut, cut, 1) for w, cut in zip(weights, cuts)], 1
    )


def whole_columns(me, own, other, widths, part=0):
    rows, columns = own.shape[0] // 4, sum(widths)

    def body(me_ref, own_ref, other_ref, *outs):
        def put(block):
            start = 0
            for out, width in zip(outs, widths):
                out[...] = block[:, start : start + width].astype(jnp.float32)
                start += width

        mine = (me_ref[0] ^ pl.program_id(0)) & 1 == 0
        pl.when(mine)(lambda: put(own_ref))
        pl.when(jnp.logical_not(mine))(lambda: put(other_ref))

    spec = pl.BlockSpec((rows, columns), lambda i, at: ((at[0] ^ i) >> 1, part))
    return pl.pallas_call(
        body,
        grid_spec=pltpu.PrefetchScalarGridSpec(
            num_scalar_prefetch=1,
            grid=(8,),
            in_specs=[spec, spec],
            out_specs=[pl.BlockSpec((rows, w), lambda i, at: (0, i)) for w in widths],
        ),
        out_shape=[jax.ShapeDtypeStruct((rows, 8 * w), jnp.float32) for w in widths],
        compiler_params=pltpu.CompilerParams(vmem_limit_bytes=VMEM_BYTES),
        cost_estimate=FREE,
        name="whole_columns",
    )(me, own, other)


def turned(x):
    return pltpu.roll(x, x.shape[-1] // 2, x.ndim - 1)


def nt(left, right):
    return lax.dot_general(
        left, right, (((1,), (1,)), ((), ())), preferred_element_type=jnp.float32
    )


def tn(left, right):
    return lax.dot_general(
        left, right, (((0,), (0,)), ((), ())), preferred_element_type=jnp.float32
    )


def unit_of(raw):
    inverse = lax.rsqrt(jnp.mean(raw * raw, -1, keepdims=True) + EPS)
    return raw * inverse, inverse


def project_body(
    normed, own0, came0, own1, came1, cosine, sine, gains, raw, query, key_value
):
    step = own0.shape[0]
    dim = cosine.shape[1]
    for block, (own, came) in enumerate(((own0, came0), (own1, came1))):
        at = block * 4 * dim
        raw[:, at : at + 4 * dim] = jnp.dot(
            normed[:, :step], own[...], preferred_element_type=jnp.float32
        ) + jnp.dot(normed[:, step:], came[...], preferred_element_type=jnp.float32)
        for i in range(3):
            unit, _ = unit_of(raw[:, at + i * dim : at + (i + 1) * dim])
            head = unit * gains[i // 2 : i // 2 + 1, :]
            head = (head * cosine[...] + turned(head) * sine[...]).astype(jnp.bfloat16)
            if i < 2:
                query[:, (2 * block + i) * dim : (2 * block + i + 1) * dim] = head
            else:
                key_value[:, 2 * block * dim : (2 * block + 1) * dim] = head
        key_value[:, (2 * block + 1) * dim : (2 * block + 2) * dim] = raw[
            :, at + 3 * dim : at + 4 * dim
        ].astype(jnp.bfloat16)


def window_mask(info, part, rows, columns):
    half = columns - rows
    row = lax.broadcasted_iota(jnp.int32, (rows, columns), 0)
    column = lax.broadcasted_iota(jnp.int32, (rows, columns), 1)
    gap = column - row - half
    slot = column + ((info[0] - 1) * half + part * rows)
    allowed = (gap <= 0) & (gap > -half) & (slot >= 0) & ((slot < info[1]) | (gap == 0))
    mask = jnp.where(allowed, 0.0, NEG)
    return jnp.concatenate([mask, mask], 0)


def two_heads(ref, at, block, dim):
    return jnp.concatenate(
        [ref[at, h * dim : (h + 1) * dim] for h in (2 * block, 2 * block + 1)], 0
    )


def key_columns(block, dim):
    key = slice(2 * block * dim, (2 * block + 1) * dim)
    value = slice((2 * block + 1) * dim, (2 * block + 2) * dim)
    return key, value


def seen_pair(before, own, part, block, dim):
    here, there = key_columns(block, dim), key_columns(1 - block, dim)
    rows = own.shape[0] // 2
    if part == 0:
        return [
            jnp.concatenate([before[:, t], own[:rows, h]], 0) for h, t in zip(here, there)
        ]
    return [jnp.concatenate([before[rows:, t], own[:, h]], 0) for h, t in zip(here, there)]


def attend_body(info, query, before, own, mixed, log_total):
    dim = own.shape[1] // 4
    rows = query.shape[0] // 2
    for part in range(2):
        at = slice(part * rows, (part + 1) * rows)
        mask = window_mask(info, part, rows, 3 * rows)
        for block in range(2):
            keys, values = seen_pair(before, own, part, block, dim)
            score = nt(two_heads(query, at, block, dim), keys) * dim**-0.5 + mask
            top = jnp.max(score, -1, keepdims=True)
            expo = jnp.exp(score - top)
            total = jnp.sum(expo, -1, keepdims=True)
            prob = (expo * (1.0 / total)).astype(jnp.bfloat16)
            out = jnp.dot(prob, values, preferred_element_type=jnp.float32).astype(jnp.bfloat16)
            log = jnp.broadcast_to(top + jnp.log(total), (2 * rows, dim))
            for i in range(2):
                on = slice((2 * block + i) * dim, (2 * block + i + 1) * dim)
                mixed[at, on] = out[i * rows : (i + 1) * rows]
                log_total[at, on] = log[i * rows : (i + 1) * rows]


def attend_back_body(
    info, query, before, own, log_total, grad_resid, weight0, weight1, raw, cosine, sine, gain,
    grad_query, grad_own, grad_before, gain_part, grad_keys, grad_values, grad_mixed,
):
    dim = own.shape[1] // 4
    rows = query.shape[0] // 2
    scale = dim**-0.5
    gain_total = jnp.zeros((1, dim), jnp.float32)
    masks = [window_mask(info, part, rows, 3 * rows) for part in range(2)]
    for block, weight in enumerate((weight0, weight1)):
        on = slice(2 * block * dim, 2 * (block + 1) * dim)
        grad_mixed[:, on] = jnp.dot(
            grad_resid[...], weight[...], preferred_element_type=jnp.float32
        ).astype(jnp.bfloat16)
        grad_keys[...] = jnp.zeros_like(grad_keys)
        grad_values[...] = jnp.zeros_like(grad_values)
        for part in range(2):
            keys, values = seen_pair(before, own, part, block, dim)
            at = slice(part * rows, (part + 1) * rows)
            seen = slice(part * rows, part * rows + 3 * rows)
            queries = two_heads(query, at, block, dim)
            grads = two_heads(grad_mixed, at, block, dim)
            log = two_heads(log_total, at, block, dim)[:, :1]
            prob = jnp.exp(nt(queries, keys) * scale + masks[part] - log)
            grad_prob = nt(grads, values)
            inner = jnp.sum(prob * grad_prob, -1, keepdims=True)
            grad_score = (prob * (grad_prob - inner)).astype(jnp.bfloat16)
            grad_values[seen, :] += tn(prob.astype(jnp.bfloat16), grads)
            grad_keys[seen, :] += tn(grad_score, queries) * scale
            both = jnp.dot(grad_score, keys, preferred_element_type=jnp.float32) * scale
            for i in range(2):
                head = 2 * block + i
                back = both[i * rows : (i + 1) * rows]
                back = back * cosine[at, :] - turned(back) * sine[at, :]
                there = (2 * head - head % 2) * dim
                unit, inverse = unit_of(raw[at, there : there + dim])
                gain_total += jnp.sum(unit * back, 0, keepdims=True)
                back = back * gain[...]
                back = inverse * (back - unit * jnp.mean(back * unit, -1, keepdims=True))
                grad_query[at, head * dim : (head + 1) * dim] = back.astype(jnp.bfloat16)
        for grad, here, there in zip(
            (grad_keys, grad_values), key_columns(block, dim), key_columns(1 - block, dim)
        ):
            grad_before[:, there] = grad[: 2 * rows, :].astype(jnp.bfloat16)
            grad_own[:, here] = grad[2 * rows :, :]
    gain_part[...] = gain_total


def finish_body(grad_query, grad_own, came, raw, cosine, sine, gain, even, odd, gain_part):
    dim = cosine.shape[1]
    total = jnp.zeros((1, dim), jnp.float32)
    for block, out in enumerate((even, odd)):
        key, value = key_columns(block, dim)
        back = grad_own[:, key] + came[:, key].astype(jnp.float32)
        back = back * cosine[...] - turned(back) * sine[...]
        unit, inverse = unit_of(raw[:, (4 * block + 2) * dim : (4 * block + 3) * dim])
        total += jnp.sum(unit * back, 0, keepdims=True)
        back = back * gain[...]
        back = inverse * (back - unit * jnp.mean(back * unit, -1, keepdims=True))
        out[:, : 2 * dim] = grad_query[:, 2 * block * dim : (2 * block + 2) * dim]
        out[:, 2 * dim : 3 * dim] = back.astype(jnp.bfloat16)
        grad_value = grad_own[:, value] + came[:, value].astype(jnp.float32)
        out[:, 3 * dim :] = grad_value.astype(jnp.bfloat16)
    gain_part[...] = total


def vmem_call(body, outs, scratch=(), scalars=0, name=None):
    def call(*args):
        in_specs = [
            pl.BlockSpec(memory_space=pltpu.SMEM if i < scalars else pltpu.VMEM)
            for i in range(len(args))
        ]
        return pl.pallas_call(
            body,
            grid=(1,),
            out_shape=outs,
            in_specs=in_specs,
            out_specs=jax.tree.map(lambda _: pl.BlockSpec(memory_space=pltpu.VMEM), outs),
            scratch_shapes=scratch,
            compiler_params=pltpu.CompilerParams(vmem_limit_bytes=VMEM_BYTES),
        cost_estimate=FREE,
            name=name,
        )(*args)

    return call


def hidden_units(mids, grads_y, weights):
    width, units = weights.shape[0], weights.shape[1] // 3
    count = len(mids)
    heights = [m.shape[0] for m in mids]
    rows, cut = sum(heights), units // 3

    def body(*refs):
        gate_w, up_w, w_down, act, grad_gate, grad_up = refs[2 * count :]
        start = 0
        for mid, grad_y in zip(refs[:count], refs[count : 2 * count]):
            at = slice(start, start + mid.shape[0])
            start += mid.shape[0]
            gate = jnp.dot(mid[...], gate_w[...], preferred_element_type=jnp.float32)
            up = jnp.dot(mid[...], up_w[...], preferred_element_type=jnp.float32)
            grad_act = jnp.dot(grad_y[...], w_down[...], preferred_element_type=jnp.float32)
            sigma = jax.nn.sigmoid(gate)
            swish = gate * sigma
            act[at, :] = (swish * up).astype(jnp.bfloat16)
            slope = grad_act * up * sigma * (1.0 + gate * (1.0 - sigma))
            grad_gate[at, :] = slope.astype(jnp.bfloat16)
            grad_up[at, :] = (grad_act * swish).astype(jnp.bfloat16)

    row_specs = [
        pl.BlockSpec((h, width), lambda j: (0, 0), pipeline_mode=pl.Buffered(1)) for h in heights
    ]
    return pl.pallas_call(
        body,
        grid=(3,),
        out_shape=[jax.ShapeDtypeStruct((rows, units), jnp.bfloat16)] * 3,
        in_specs=[
            *row_specs,
            *row_specs,
            pl.BlockSpec((width, cut), lambda j: (0, j)),
            pl.BlockSpec((width, cut), lambda j: (0, j + 3)),
            pl.BlockSpec((width, cut), lambda j: (0, j + 6)),
        ],
        out_specs=[pl.BlockSpec((rows, cut), lambda j: (0, j))] * 3,
        compiler_params=pltpu.CompilerParams(vmem_limit_bytes=VMEM_BYTES),
        cost_estimate=FREE,
        name="hidden_units",
    )(*mids, *grads_y, weights, weights, weights)


def from_hidden(pairs, eighths):
    count, parts = len(pairs), len(eighths)
    rows, units = pairs[0][0].shape[0] // 8, pairs[0][0].shape[1]
    width = pairs[0][1].shape[0]
    cut = width // 4

    def body(*refs):
        ins, outs = refs[: -(parts // 2)], refs[-(parts // 2) :]
        total = 0.0
        for i in range(count):
            part = ins[i * (parts + 1) : (i + 1) * (parts + 1)]
            left = jnp.concatenate([p[...] for p in part[:-1]], 0)
            total = total + nt(left, part[-1][...])
        for i, out in enumerate(outs):
            out[...] = total[2 * i * rows : 2 * (i + 1) * rows].astype(jnp.bfloat16)

    specs, args = [], []
    for left, right, at in pairs:
        specs += [pl.BlockSpec((rows, units), lambda j, e=e: (e, 0)) for e in eighths]
        specs.append(pl.BlockSpec((cut, units), lambda j, at=at: (j, at)))
        args += [left] * parts + [right]
    return pl.pallas_call(
        body,
        grid=(4,),
        out_shape=[jax.ShapeDtypeStruct((2 * rows, width), jnp.bfloat16)] * (parts // 2),
        in_specs=specs,
        out_specs=[pl.BlockSpec((2 * rows, cut), lambda j: (0, j))] * (parts // 2),
        compiler_params=pltpu.CompilerParams(vmem_limit_bytes=VMEM_BYTES),
        cost_estimate=FREE,
        name="from_hidden",
    )(*args)


def row_outer(lefts, groups, first, tiles, added=None, places=None, part=None):
    rights = [right for group in groups for right in group]
    places = range(len(rights)) if places is None else places
    added = [] if added is None else [added] * len(rights)
    width = lefts[0].shape[1]
    tile = width // 8
    count = len(lefts)
    rows = sum(left.shape[0] for left in lefts)
    wide = rights[0].shape[1] // (1 if part is None else 2)
    columns = [wide * len(group) for group in groups]

    def body(*refs):
        left_refs = refs[:count]
        right_refs = refs[count : count + len(rights)]
        add_refs = refs[count + len(rights) : count + len(rights) + len(added)]
        outs = refs[count + len(rights) + len(added) :]
        place = 0
        for i, group in enumerate(groups):
            column = 0
            for _ in group:
                on = slice(column, column + wide)
                total, start = 0.0, 0
                for left in left_refs:
                    stop = start + left.shape[0]
                    total = total + tn(left[...], right_refs[place][start:stop, :])
                    start = stop
                if added:
                    total = total + add_refs[place][...].astype(jnp.float32)
                outs[i][:, on] = total.astype(jnp.bfloat16)
                place += 1
                column += wide

    return pl.pallas_call(
        body,
        grid=(tiles,),
        out_shape=[jax.ShapeDtypeStruct((tiles * tile, c), jnp.bfloat16) for c in columns],
        in_specs=[
            *(pl.BlockSpec((left.shape[0], tile), lambda j: (0, j + first)) for left in lefts),
            *(
                pl.BlockSpec(
                    (right.shape[0], wide), lambda j: (0, part or 0), pipeline_mode=pl.Buffered(1)
                )
                for right in rights
            ),
            *(
                pl.BlockSpec((tile, wide), lambda j, at=at: (j + first, at))
                for at in places[: len(added)]
            ),
        ],
        out_specs=[pl.BlockSpec((tile, c), lambda j: (j, 0)) for c in columns],
        compiler_params=pltpu.CompilerParams(vmem_limit_bytes=VMEM_BYTES),
        cost_estimate=pl.CostEstimate(
            flops=2 * rows * tiles * tile * sum(columns),
            bytes_accessed=2 * rows * (width + sum(columns)),
            transcendentals=0,
        ),
        name="row_outer",
    )(*lefts, *rights, *added)


def close_body(x, *refs):
    mixed, weights = refs[:4], refs[4:12]
    gains, resid, mid = refs[12:]
    at = pl.program_id(0)
    step = x.shape[1]
    columns = weights[0].shape[1]
    total = x[...].astype(jnp.float32)
    for i in range(8):
        part = mixed[i // 2][:, (i % 2) * columns : (i % 2 + 1) * columns]
        total = total + nt(part, weights[i][...])
    resid[:, pl.ds(pl.multiple_of(at * step, step), step)] = total

    @pl.when(at == 3)
    def _():
        unit, _ = unit_of(resid[...])
        mid[...] = (unit * gains[...]).astype(jnp.bfloat16)


def close_attention(x, mixed, weights, gains):
    rows, width = x.shape
    step = width // 4
    whole = lambda a: pl.BlockSpec(a.shape, lambda j: (0, 0))
    return pl.pallas_call(
        close_body,
        grid=(4,),
        out_shape=[
            jax.ShapeDtypeStruct((rows, width), jnp.float32),
            jax.ShapeDtypeStruct((rows, width), jnp.bfloat16),
        ],
        in_specs=[
            pl.BlockSpec((rows, step), lambda j: (0, j)),
            *(whole(m) for m in mixed),
            *(pl.BlockSpec((step, w.shape[1]), lambda j: (j, 0)) for w in weights),
            whole(gains),
        ],
        out_specs=[pl.BlockSpec((rows, width), lambda j: (0, 0))] * 2,
        compiler_params=pltpu.CompilerParams(vmem_limit_bytes=VMEM_BYTES),
        cost_estimate=FREE,
        name="close_attention",
    )(x, *mixed, *weights, gains)


def back_to_rows(blocks, weights):
    rows = blocks[0].shape[0]
    step, columns = weights[0][0].shape
    count = len(blocks)

    def body(*refs):
        lefts = refs[:count]
        hbm = refs[count : 3 * count]
        out = refs[3 * count]
        held, sems = refs[3 * count + 1 :]
        copies = []
        for i in range(count):
            own, came = hbm[2 * i : 2 * i + 2]
            copies.append(
                [
                    pltpu.make_async_copy(own, held.at[i, :step], sems.at[i, 0]),
                    pltpu.make_async_copy(came, held.at[i, step:], sems.at[i, 1]),
                ]
            )
        for some in copies:
            for copy in some:
                copy.start()
        for i in range(count):
            for copy in copies[i]:
                copy.wait()
            for k in range(4):
                on = slice(k * step, (k + 1) * step)
                part = nt(lefts[i][...], held[i, on])
                if i == 0:
                    out[:, on] = part
                else:
                    out[:, on] += part

    return pl.pallas_call(
        body,
        grid=(1,),
        out_shape=jax.ShapeDtypeStruct((rows, 4 * step), jnp.float32),
        in_specs=[pl.BlockSpec(memory_space=pltpu.VMEM)] * count
        + [pl.BlockSpec(memory_space=pl.ANY)] * (2 * count),
        out_specs=pl.BlockSpec(memory_space=pltpu.VMEM),
        scratch_shapes=[
            pltpu.VMEM((count, 4 * step, columns), jnp.bfloat16),
            pltpu.SemaphoreType.DMA((count, 2)),
        ],
        compiler_params=pltpu.CompilerParams(vmem_limit_bytes=VMEM_BYTES),
        cost_estimate=FREE,
        name="back_to_rows",
    )(*blocks, *(part for w in weights for part in w))


def on_device_block(
    tokens,
    lengths,
    attn_gain,
    w_query,
    key_matrix,
    value_matrix,
    query_gain,
    key_gain,
    w_out,
    mlp_gain,
    w_gate,
    w_up,
    w_down,
    cotangent,
):
    low, full = jnp.bfloat16, jnp.float32
    width = tokens.shape[2]
    head_dim = query_gain.shape[0]
    shards = lax.axis_size("shard")
    shard_at = lax.axis_index("shard")
    me = lax.axis_index("rep")
    core = me & 1
    count = lax.axis_size("rep")

    s = Stage()
    piece = width // shards

    s.own_blocks = [
        column_block((w_query, key_matrix, value_matrix), me ^ i) for i in range(8)
    ]
    gain_rows = jnp.concatenate(
        [jnp.stack([attn_gain, mlp_gain]), jnp.zeros((14, piece), low)], 0
    )
    travelling = jnp.concatenate([s.own_blocks[0], gain_rows], 0)
    s.tokens_cuts, s.cotangent_cuts = sequence_cuts(tokens), sequence_cuts(cotangent)
    s.out_block = column_block((w_out,), me)
    s.ffn_block = column_block((w_gate, w_up, w_down), me)
    s.before, s.behind = around(travelling, 1), around(travelling, -1)
    s.other_lengths = across(lengths, CORE)
    s.end()

    s.ahead = around(s.before, 1)
    tokens_sent = [to_sequence(cut, turn) for turn, cut in enumerate(s.tokens_cuts)]
    out_own = lax.all_gather(s.out_block, "shard", axis=0, tiled=True)
    del s.out_block, s.tokens_cuts
    s.end()

    parts = (s.before, s.ahead, s.behind)
    s.came = jnp.concatenate([part[:piece] for part in parts], 0)
    s.gains = jnp.concatenate([gain_rows[:2], *(part[piece : piece + 2] for part in parts)], 1)
    s.came_near = near(s.came)
    s.came_own = across(s.came, CORE)
    s.x_came = tokens_sent
    del s.before, s.behind, s.ahead
    s.end()

    grad_y_sent = [to_sequence(cut, turn) for turn, cut in enumerate(s.cotangent_cuts)]
    s.came_far = far(*s.came_near)
    s.came_other = [s.came_own, *(across(block, CORE) for block in s.came_near)]
    gains = rolled(s.gains.astype(full))
    s.mlp_gains = gains[1:]
    s.attn_gains = gains[:1]
    s.x_low = jnp.concatenate(in_turn(s.x_came), 0)
    rows = s.x_low.shape[0]
    x_rows = s.x_low.astype(full)
    s.inverse_in = lax.rsqrt(jnp.mean(x_rows * x_rows, -1, keepdims=True) + EPS)
    s.normed = rolled((x_rows * s.inverse_in * s.attn_gains).astype(low))
    query_gains = query_gain.astype(full)[None]
    key_gains = key_gain.astype(full)[None]
    s.head_gains = jnp.concatenate([query_gains, key_gains], 0)
    both = jnp.where(
        core == 0,
        jnp.concatenate([lengths, s.other_lengths]),
        jnp.concatenate([s.other_lengths, lengths]),
    )
    length = lax.dynamic_index_in_dim(both, shard_at, 0, keepdims=False)
    s.info = jnp.stack([core, length]).astype(jnp.int32)
    query_pos = core * rows + jnp.arange(rows, dtype=jnp.int32)
    s.valid = (query_pos < length)[:, None].astype(full)
    cosine, sine = tables(query_pos, head_dim)
    s.cosine, sine = cosine[0, :, 0], sine[0, :, 0]
    s.sine = jnp.concatenate([-sine[:, : head_dim // 2], sine[:, head_dim // 2 :]], 1)
    s.out_own = out_own
    del s.gains, s.x_came, s.other_lengths, s.cotangent_cuts, s.came_own
    s.end()

    head_columns = 2 * head_dim
    block_columns = 4 * head_dim
    quad_rows = jax.ShapeDtypeStruct((rows, block_columns), low)
    quad_sums = jax.ShapeDtypeStruct((rows, block_columns), full)
    gain_sum = jax.ShapeDtypeStruct((1, head_dim), full)
    project = vmem_call(
        project_body,
        [jax.ShapeDtypeStruct((rows, 2 * block_columns), full), quad_rows, quad_rows],
        name="project",
    )
    attend = vmem_call(attend_body, [quad_rows, quad_sums], scalars=1, name="attend")
    attend_back = vmem_call(
        attend_back_body,
        [quad_rows, quad_sums, quad_rows, gain_sum],
        scratch=[pltpu.VMEM((2 * rows, head_dim), full)] * 2
        + [pltpu.VMEM((rows, block_columns), low)],
        scalars=1,
        name="attend_back",
    )
    finish = vmem_call(finish_body, [quad_rows, quad_rows, gain_sum], name="finish")
    upward = [(i, i + 1) for i in range(0, count, 2)]
    downward = [(i + 1, i) for i in range(0, count, 2)]

    def project_call(i, came, other):
        return (
            project, s.normed, s.own_blocks[2 * i], came, s.own_blocks[2 * i + 1], other,
            s.cosine, s.sine, s.head_gains,
        )

    def attend_call(projected, earlier):
        return (
            lambda query, own, before: attend(s.info, query, before, own),
            *projected[1:], earlier,
        )

    came_last = jnp.concatenate(s.came_far, 0)
    s.came_last = (came_last, across(came_last, CORE))
    s.out_near = near(s.out_own)
    s.out_own_other = across(s.out_own, CORE)
    s.projected = in_order(
        [
            project_call(i, block, other)
            for i, (block, other) in enumerate(zip((s.came, *s.came_near), s.came_other))
        ]
    )
    s.grad_y_came = grad_y_sent
    del s.came_far
    s.end()

    ffn_own = lax.all_gather(s.ffn_block, "shard", axis=0, tiled=True)
    grad_y = jnp.concatenate(in_turn(s.grad_y_came), 0)
    s.grad_y = jnp.where(s.valid > 0, grad_y, jnp.zeros_like(grad_y))
    grad_y_near = near(s.grad_y)
    s.out_far = far(*s.out_near)
    s.out_near_other = [across(block, CORE) for block in s.out_near]
    s.earlier = [lax.ppermute(p[2], "rep", upward) for p in s.projected]
    (s.projected_last,) = in_order([project_call(3, *s.came_last)])
    del s.ffn_block, s.grad_y_came
    s.end()

    out_last = jnp.concatenate(s.out_far, 0)
    s.out_last = (out_last, across(out_last, CORE))
    s.earlier_last = lax.ppermute(s.projected_last[2], "rep", upward)
    s.attended = in_order([attend_call(*pair) for pair in zip(s.projected, s.earlier)])
    s.grad_y_near = grad_y_near
    del s.out_far
    s.end()

    s.projected = [*s.projected, s.projected_last]
    s.earlier = [*s.earlier, s.earlier_last]
    s.out_blocks = [
        s.out_own, s.out_own_other, s.out_near[0], s.out_near_other[0], s.out_near[1],
        s.out_near_other[1], *s.out_last,
    ]
    (last,) = in_order([attend_call(s.projected_last, s.earlier_last)])
    s.attended = [*s.attended, last]
    s.mixed = [a[0] for a in s.attended]
    s.resid, s.mid = close_attention(s.x_low, s.mixed, s.out_blocks, s.mlp_gains)
    s.grad_y_far = far(*s.grad_y_near)
    s.came = [s.came, *s.came_near, s.came_last[0]]
    s.came_other = [*s.came_other, s.came_last[1]]
    del s.came_near, s.came_last
    del s.out_own, s.out_own_other, s.out_near, s.out_near_other, s.out_last
    del s.projected_last, s.earlier_last
    s.end()

    s.mid_near = near(s.mid)
    s.end()

    s.mid_far = far(*s.mid_near)
    s.ffn_own = ffn_own
    s.end()

    s.mids = [s.mid, *s.mid_near, *s.mid_far]
    s.grads_y = [s.grad_y, *s.grad_y_near, *s.grad_y_far]
    s.ffn_other = across(s.ffn_own, CORE)
    units = s.ffn_own.shape[1] // 3
    s.hidden_own = hidden_units(s.mids, s.grads_y, s.ffn_own)
    del s.mid, s.mid_near, s.mid_far, s.grad_y_near, s.grad_y_far
    s.end()

    def gate_up_pairs():
        return [
            (hidden[i], weights, i - 1)
            for hidden, weights in ((s.hidden_own, s.ffn_own), (s.hidden_other, s.ffn_other))
            for i in (1, 2)
        ]

    def down_pairs():
        return [(s.hidden_own[0], s.ffn_own, 2), (s.hidden_other[0], s.ffn_other, 2)]

    def from_hidden_call(pairs, eighths):
        return (
            lambda first: from_hidden([(first, *pairs[0][1:]), *pairs[1:]], eighths),
            pairs[0][0],
        )

    def outer_call(lefts, rights, *added):
        return lambda first: row_outer(lefts, [[first, *rights[1:]]], 0, 8, *added)[0], rights[0]

    def send_near(sent):
        return across(sent[0], ACROSS_X), across(sent[1], ACROSS_Y)

    def send_far(came, rest, split):
        one_tail, two_head = rest
        return (
            across(rounded_sum(one_tail, split(came[1])[1]), ACROSS_X),
            across(rounded_sum(two_head, split(came[0])[1]), ACROSS_Y),
        )

    def total(came, came_far, own, split):
        head, tail = own
        full_sum = lambda *parts: sum(part.astype(full) for part in parts)
        return jnp.concatenate(
            [
                full_sum(head, split(came[0])[0], came_far[1]),
                full_sum(tail, split(came[1])[0], came_far[0]),
            ],
            0,
        )

    by_rows = lambda a: jnp.split(a, 2, 0)
    by_columns = lambda a: jnp.split(a, 2, 1)
    to_plane, rest_of_plane = (2, 6, 5, 7), (3, 4, 0, 1)

    s.hidden_other = hidden_units(s.mids, s.grads_y, s.ffn_other)
    (s.down_outer,) = in_order([outer_call(s.grads_y, s.hidden_other[:1])])
    s.end()

    s.down_came = across(s.down_outer, CORE)
    s.mid_sent = from_hidden(gate_up_pairs(), to_plane)
    del s.down_outer
    s.end()

    s.mid_came = send_near(s.mid_sent)
    s.down_mine, s.mid_rest, s.gate_up_outer = in_order(
        [
            outer_call(s.grads_y, s.hidden_own[:1], s.down_came),
            from_hidden_call(gate_up_pairs(), rest_of_plane),
            outer_call(s.mids, s.hidden_other[1:]),
        ]
    )
    del s.mid_sent, s.down_came
    s.end()

    down_total = lax.psum_scatter(s.down_mine, "shard", scatter_dimension=0, tiled=True)
    s.mid_came_far = send_far(s.mid_came, by_rows(s.mid_rest[0]), by_rows)
    s.gate_up_came = across(s.gate_up_outer, CORE)
    s.mlp_sent, s.mlp_rest = in_order(
        [
            from_hidden_call(down_pairs(), to_plane),
            from_hidden_call(down_pairs(), rest_of_plane),
        ]
    )
    del s.gate_up_outer, s.down_mine
    s.end()

    def back_call(i):
        raw, query, own_pair = s.projected[i]
        return (
            lambda query, *rest: attend_back(s.info, query, *rest),
            query, s.earlier[i], own_pair, s.attended[i][1], s.resid_low,
            *s.out_blocks[2 * i : 2 * i + 2], raw, s.cosine, s.sine, s.head_gains[:1],
        )

    def finish_call(i):
        return (
            finish, s.backs[i][0], s.backs[i][1], s.returned[i], s.projected[i][0],
            s.cosine, s.sine, s.head_gains[1:],
        )

    def give_back(*chips):
        s.returned = s.returned | {
            i: lax.ppermute(s.backs[i][2], "rep", downward) for i in chips
        }

    def odd_call(left, blocks, part=None):
        return lambda first: row_outer([first], [blocks], 0, 8, part=part)[0], left

    def head_call(left, blocks, came, part=None, places=(0, 1, 2, 3)):
        groups = [[blocks[1], blocks[3]], [blocks[2]], [blocks[0]]]
        at = [places[i] for i in (1, 3, 2, 0)]
        return lambda first: row_outer([first], groups, 0, 4, came, at, part), left

    def tail_call(left, blocks, came, part=None, places=(0, 1, 2, 3)):
        groups = [[blocks[2], blocks[3]], [blocks[1]], [blocks[0]]]
        at = [places[i] for i in (2, 3, 1, 0)]
        return lambda first: row_outer([first], groups, 4, 4, came, at, part), left

    s.mlp_came = send_near(s.mlp_sent)
    grad_mid = total(s.mid_came, s.mid_came_far, by_rows(s.mid_rest[1]), by_rows)
    inverse_mid = lax.rsqrt(jnp.mean(s.resid * s.resid, -1, keepdims=True) + EPS)
    mid_unit = s.resid * inverse_mid
    s.mlp_gain_part = jnp.sum(mid_unit * grad_mid, 0)
    s.grad_resid = s.grad_y.astype(full) + norm_back(
        mid_unit, inverse_mid, grad_mid * s.mlp_gains
    )
    s.resid_low = s.grad_resid.astype(low)
    s.resid_rolled = rolled(s.resid_low)
    s.returned = {}
    back, s.out_odd, s.gate_up_mine = in_order(
        [
            back_call(3),
            odd_call(s.resid_rolled, s.mixed, 1),
            outer_call(s.mids, s.hidden_own[1:], s.gate_up_came),
        ]
    )
    s.backs = {3: back}
    s.down_total = down_total
    del s.mid_came, s.mid_came_far, s.mid_rest, s.gate_up_came, s.hidden_own, s.hidden_other
    del s.mids, s.grads_y, s.ffn_own, s.ffn_other, s.mlp_sent
    s.end()

    gate_up_total = lax.psum_scatter(s.gate_up_mine, "shard", scatter_dimension=0, tiled=True)
    s.mlp_came_far = send_far(s.mlp_came, by_rows(s.mlp_rest[0]), by_rows)
    s.out_came = across(s.out_odd, CORE)
    give_back(3)
    back1, back2 = in_order([back_call(1), back_call(2)])
    s.backs = s.backs | {1: back1, 2: back2}
    del s.out_odd, s.gate_up_mine
    s.end()

    s.down_near = near(s.down_total)
    give_back(1, 2)
    s.out_head, s.out_tail, back, finished = in_order(
        [
            head_call(s.resid_rolled, s.mixed, s.out_came, 0),
            tail_call(s.resid_rolled, s.mixed, s.out_came, 0),
            back_call(0),
            finish_call(3),
        ]
    )
    s.backs = s.backs | {0: back}
    s.finished = {3: finished}
    del s.out_came
    s.end()

    s.out_near = send_near((s.out_head[0], s.out_tail[0]))
    mlp_out = total(s.mlp_came, s.mlp_came_far, by_rows(s.mlp_rest[1]), by_rows)
    s.output = (s.valid * (s.resid + mlp_out)).astype(low)
    give_back(0)
    finished1, finished2 = in_order([finish_call(1), finish_call(2)])
    s.finished = s.finished | {1: finished1, 2: finished2}
    del s.mlp_came, s.mlp_came_far, s.mlp_rest, s.resid
    s.end()

    output_sent = from_sequences_send(s.output)
    s.out_far = send_far(s.out_near, (s.out_tail[1], s.out_head[1]), by_columns)
    s.down_far = far(*s.down_near)
    (finished,) = in_order([finish_call(0)])
    s.finished = s.finished | {0: finished}
    (s.odd,) = in_order([odd_call(s.normed, [s.finished[i][1] for i in range(4)])])
    s.gate_up_total = gate_up_total
    s.output_first = output_sent[0]
    del s.output
    s.end()

    my_group = me.astype(jnp.int32)[None]

    def whole_call(widths, own, other, part=0):
        return lambda first: whole_columns(my_group, first, other, widths, part), own

    s.gate_up_near = near(s.gate_up_total)
    s.qkv_came = across(s.odd, CORE)
    out_sum = total(s.out_near, s.out_far, (s.out_head[2], s.out_tail[2]), by_columns)
    s.out_chunks = jnp.split(out_sum.astype(low), shards, 0)
    s.out_ring = ring_sum_first(s.out_chunks)
    weights = [
        pair
        for i in range(4)
        for pair in (
            (s.own_blocks[2 * i], s.came[i]), (s.own_blocks[2 * i + 1], s.came_other[i])
        )
    ]
    blocks = [part for i in range(4) for part in s.finished[i][:2]]
    grad_in = rolled(back_to_rows(blocks, weights))
    x_unit = s.x_low.astype(full) * s.inverse_in
    s.gain_parts = jnp.concatenate(
        [
            jnp.sum(x_unit * grad_in, 0),
            s.mlp_gain_part,
            sum(s.backs[i][3] for i in range(4))[0],
            sum(s.finished[i][2] for i in range(4))[0],
        ]
    )
    s.grad_tokens = (
        s.grad_resid + norm_back(x_unit, s.inverse_in, grad_in * s.attn_gains)
    ).astype(low)
    del s.odd, s.out_near, s.out_far, s.out_head, s.out_tail, s.backs
    del s.own_blocks, s.came, s.came_other, s.grad_resid, s.x_low
    s.end()

    even = [s.finished[i][0] for i in range(4)]
    s.head0, s.tail0, s.head1, s.tail1 = in_order(
        [
            call(s.normed, even, s.qkv_came, half, range(half, 8, 2))
            for half in range(2)
            for call in (head_call, tail_call)
        ]
    )
    tokens_sent = from_sequences_send(
        lax.optimization_barrier((s.grad_tokens, s.tail1[0]))[0]
    )
    s.down_spread = jnp.concatenate([s.down_total, *s.down_near, *s.down_far], 0)
    s.down_spread_other = across(s.down_spread, CORE)
    s.output_second = output_sent[1]
    s.gate_up_far = far(*s.gate_up_near)
    del s.qkv_came, s.finished, s.down_total, s.down_near, s.down_far
    s.end()

    def qkv_chunks(came, came_far, head, tail):
        own = total(came, came_far, (head[2], tail[2]), by_columns)
        return jnp.split(own.astype(low), shards, 0)

    s.near0 = send_near((s.head0[0], s.tail0[0]))
    s.out_ring_last = around(rounded_sum(s.out_chunks[3], s.out_ring[0]), 1)
    s.tokens_first = tokens_sent[0]
    s.gain_came = across(s.gain_parts, CORE)
    s.end()

    s.far0 = send_far(s.near0, (s.tail0[1], s.head0[1]), by_columns)
    s.near1 = send_near((s.head1[0], s.tail1[0]))
    (s.whole_down,) = in_order([whole_call((units,), s.down_spread, s.down_spread_other)])
    first = lax.optimization_barrier((s.gate_up_total, s.whole_down[0]))[0]
    s.gate_up_own = jnp.concatenate([first, *s.gate_up_near, *s.gate_up_far], 0)
    s.out_total = rounded_sum(s.out_chunks[0], s.out_ring[1], s.out_ring_last)
    s.gain_parts = s.gain_parts + s.gain_came
    s.tokens_second = tokens_sent[1]
    del s.down_spread, s.down_spread_other, s.out_chunks, s.out_ring, s.out_ring_last
    del s.gate_up_near, s.gate_up_far, s.gate_up_total, s.grad_tokens
    s.end()

    s.chunks0 = qkv_chunks(s.near0, s.far0, s.head0, s.tail0)
    s.ring0 = ring_sum_first(s.chunks0)
    s.far1 = send_far(s.near1, (s.tail1[1], s.head1[1]), by_columns)
    s.gate_up_other = across(s.gate_up_own, CORE)
    del s.near0, s.far0, s.head0, s.tail0
    s.end()

    s.last0 = around(rounded_sum(s.chunks0[3], s.ring0[0]), 1)
    s.chunks1 = qkv_chunks(s.near1, s.far1, s.head1, s.tail1)
    s.ring1 = ring_sum_first(s.chunks1)
    s.gain_came = across(s.gain_parts, ACROSS_X)
    ((s.whole_gate,),) = in_order([whole_call((units,), s.gate_up_own, s.gate_up_other)])
    del s.near1, s.far1, s.head1, s.tail1
    s.end()

    query_total = rounded_sum(s.chunks0[0], s.ring0[1], s.last0)
    s.total0 = jnp.concatenate([query_total, s.out_total], 1)
    s.spread0 = near(s.total0)
    s.last1 = around(rounded_sum(s.chunks1[3], s.ring1[0]), 1)
    s.gain_parts = s.gain_parts + s.gain_came
    s.gain_came = across(s.gain_parts, ACROSS_Y)
    ((s.whole_up,),) = in_order([whole_call((units,), s.gate_up_own, s.gate_up_other, 1)])
    del s.gate_up_own, s.gate_up_other
    del s.chunks0, s.ring0, s.last0, s.out_total
    s.end()

    s.spread_far0 = far(*s.spread0)
    s.total1 = rounded_sum(s.chunks1[0], s.ring1[1], s.last1)
    s.spread1 = near(s.total1)
    s.gain_parts = s.gain_parts + s.gain_came
    s.gain_came = lax.ppermute(s.gain_parts, "shard", [(i, i ^ 1) for i in range(shards)])
    del s.chunks1, s.ring1, s.last1
    s.end()

    s.own0 = jnp.concatenate([s.total0, *s.spread0, *s.spread_far0], 0)
    s.other0 = across(s.own0, CORE)
    s.spread_far1 = far(*s.spread1)
    s.gain_parts = s.gain_parts + s.gain_came
    s.gain_came = lax.ppermute(s.gain_parts, "shard", [(i, i ^ 2) for i in range(shards)])
    del s.total0, s.spread0, s.spread_far0
    s.end()

    s.own1 = jnp.concatenate([s.total1, *s.spread1, *s.spread_far1], 0)
    s.other1 = across(s.own1, CORE)
    (s.whole0,) = in_order([whole_call((head_columns, head_columns), s.own0, s.other0)])
    gain_sums = s.gain_parts + s.gain_came
    s.wide = lax.dynamic_slice_in_dim(
        gain_sums[: 2 * width].reshape(2, width), shard_at * piece, piece, 1
    )
    s.narrow = gain_sums[2 * width :]
    del s.own0, s.other0, s.total1, s.spread1, s.spread_far1
    s.end()

    ((whole_key, whole_value),) = in_order(
        [whole_call((head_dim, head_dim), s.own1, s.other1)]
    )
    return (
        jnp.stack(in_turn([s.output_first, s.output_second])),
        jnp.stack(in_turn([s.tokens_first, s.tokens_second])),
        s.wide[0],
        s.whole0[0],
        whole_key,
        whole_value,
        s.narrow[:head_dim],
        s.narrow[head_dim:],
        s.whole0[1],
        s.wide[1],
        s.whole_gate,
        s.whole_up,
        *s.whole_down,
    )


def solution(mesh):
    sizes = (mesh.shape["rep"], mesh.shape["shard"])
    return jax.shard_map(
        on_device_block if sizes == (8, 4) else on_device,
        mesh=mesh,
        in_specs=(
            P("rep", "shard", None),
            P("rep"),
            P("shard"),
            P("shard", None),
            P("shard", None),
            P("shard", None),
            P(),
            P(),
            P("shard", None),
            P("shard"),
            P("shard", None),
            P("shard", None),
            P("shard", None),
            P("rep", "shard", None),
        ),
        out_specs=(
            P("rep", "shard", None),
            P("rep", "shard", None),
            P("shard"),
            P("shard", None),
            P("shard", None),
            P("shard", None),
            P(),
            P(),
            P("shard", None),
            P("shard"),
            P("shard", None),
            P("shard", None),
            P("shard", None),
        ),
        check_vma=False,
    )
```

```python
import jax
import jax.numpy as jnp
from jax import lax
from jax.experimental import pallas as pl
from jax.experimental.pallas import tpu as pltpu
from jax.sharding import PartitionSpec as P

WINDOW = 512


EPS = 1e-06
ROPE_BASE = 1000000.0
NEG = -1e30


def passed_along(x, axis, by):
    devices = lax.axis_size(axis)
    pairs = [(i, i + by) for i in range(devices) if 0 <= i + by < devices]
    return lax.ppermute(x, axis, pairs)


def tables(positions, head_dim):
    half = head_dim // 2
    freq = ROPE_BASE ** (-jnp.arange(half, dtype=jnp.float32) * 2.0 / head_dim)
    angle = positions.astype(jnp.float32)[:, None] * freq[None, :]
    angle = jnp.concatenate([angle, angle], -1)
    return (jnp.cos(angle)[None, :, None, :], jnp.sin(angle)[None, :, None, :])


def rotated_rows(value_rows):
    half = value_rows.shape[-1] // 2
    return jnp.concatenate([-value_rows[..., half:], value_rows[..., :half]], -1)


def head_norm(raw, gain):
    inverse = lax.rsqrt(jnp.mean(raw * raw, -1, keepdims=True) + EPS)
    unit = raw * inverse
    return (unit, inverse, unit * gain)


def norm_back(unit, inverse, grad_unit):
    return inverse * (grad_unit - unit * jnp.mean(grad_unit * unit, -1, keepdims=True))


def head_norm_back(unit, inverse, grad_normed, gain):
    grad_raw = norm_back(unit, inverse, grad_normed * gain)
    return (grad_raw, jnp.sum(unit * grad_normed, axis=(0, 1, 2)))


def scores(query_rows, keys, allowed, scale):
    raw = (
        jnp.einsum("sqhgd,skhd->shgqk", query_rows, keys, preferred_element_type=jnp.float32)
        * scale
    )
    return jnp.where(allowed[:, None, None], raw, NEG)


def outer(left, right):
    return jnp.einsum("rc,rf->cf", left, right, preferred_element_type=jnp.float32)


def on_device(
    tokens,
    lengths,
    attn_gain,
    w_query,
    key_matrix,
    value_matrix,
    query_gain,
    key_gain,
    w_out,
    mlp_gain,
    w_gate,
    w_up,
    w_down,
    cotangent,
):
    seq_count, piece, width = tokens.shape
    head_dim = query_gain.shape[0]
    heads_q = w_query.shape[1] // head_dim
    heads_kv = key_matrix.shape[1] // head_dim
    groups = heads_q // heads_kv
    rows = seq_count * piece
    scale = head_dim ** (-0.5)
    reach = (WINDOW + piece - 2) // piece
    owned = width // lax.axis_size("shard")
    shard_at = lax.axis_index("shard")
    query_pos = shard_at * piece + jnp.arange(piece, dtype=jnp.int32)
    key_pos = (shard_at - reach) * piece + jnp.arange((reach + 1) * piece, dtype=jnp.int32)
    near = (
        (key_pos[None, :] <= query_pos[:, None])
        & (query_pos[:, None] - key_pos[None, :] < WINDOW)
        & (key_pos[None, :] >= 0)
    )
    live = (key_pos[None, None, :] < lengths[:, None, None]) | (
        key_pos[None, :] == query_pos[:, None]
    )[None]
    allowed = near[None] & live
    valid = (query_pos[None, :] < lengths[:, None]).astype(jnp.float32).reshape(rows, 1)
    cosine_table, sine_table = tables(query_pos, head_dim)
    x_rows = tokens.astype(jnp.float32).reshape(rows, width)
    inverse_in = lax.rsqrt(jnp.mean(x_rows * x_rows, -1, keepdims=True) + EPS)
    x_unit = x_rows * inverse_in
    gain_piece = lax.all_gather(attn_gain, "shard", axis=0, tiled=True)
    query_piece = lax.all_gather(w_query, "shard", axis=0, tiled=True)
    key_piece = lax.all_gather(key_matrix, "shard", axis=0, tiled=True)
    value_piece = lax.all_gather(value_matrix, "shard", axis=0, tiled=True)
    normed_piece = (x_unit * gain_piece.astype(jnp.float32)).astype(jnp.bfloat16)
    acc_q = jnp.dot(normed_piece, query_piece, preferred_element_type=jnp.float32)
    acc_k = jnp.dot(normed_piece, key_piece, preferred_element_type=jnp.float32)
    acc_v = jnp.dot(normed_piece, value_piece, preferred_element_type=jnp.float32)
    normalized_rows = normed_piece
    gains = gain_piece.astype(jnp.float32)
    attn_in = normalized_rows
    attn_gains = gains
    query_unit, query_inverse, query_rows_normalized = head_norm(
        acc_q.reshape(seq_count, piece, heads_q, head_dim), query_gain.astype(jnp.float32)
    )
    key_unit, key_inverse, key_normed = head_norm(
        acc_k.reshape(seq_count, piece, heads_kv, head_dim), key_gain.astype(jnp.float32)
    )
    query_rows = (
        (query_rows_normalized * cosine_table + rotated_rows(query_rows_normalized) * sine_table)
        .astype(jnp.bfloat16)
        .reshape(seq_count, piece, heads_kv, groups, head_dim)
    )
    keys_own = (key_normed * cosine_table + rotated_rows(key_normed) * sine_table).astype(
        jnp.bfloat16
    )
    values_own = acc_v.reshape(seq_count, piece, heads_kv, head_dim).astype(jnp.bfloat16)
    own_pair = jnp.stack([keys_own, values_own])
    parts = []
    for fetch_back in range(reach, 0, -1):
        parts.append(passed_along(own_pair, "shard", fetch_back))
    parts.append(own_pair)
    near_pair = jnp.concatenate(parts, 2)
    score = scores(query_rows, near_pair[0], allowed, scale)
    top = jnp.max(score, -1, keepdims=True)
    expo = jnp.exp(score - top)
    total = jnp.sum(expo, -1, keepdims=True)
    prob = expo / total
    log_total = top + jnp.log(total)
    mixed = jnp.einsum(
        "shgqk,skhd->sqhgd",
        prob.astype(jnp.bfloat16),
        near_pair[1],
        preferred_element_type=jnp.float32,
    )
    mixed_rows = mixed.reshape(rows, heads_q * head_dim).astype(jnp.bfloat16)
    resid = x_rows + jnp.einsum(
        "rf,nf->rn",
        mixed_rows,
        lax.all_gather(w_out, "shard", axis=0, tiled=True),
        preferred_element_type=jnp.float32,
    )
    inverse_mid = lax.rsqrt(jnp.mean(resid * resid, -1, keepdims=True) + EPS)
    mid_unit = resid * inverse_mid
    gain_piece = lax.all_gather(mlp_gain, "shard", axis=0, tiled=True)
    gate_piece = lax.all_gather(w_gate, "shard", axis=0, tiled=True)
    up_piece = lax.all_gather(w_up, "shard", axis=0, tiled=True)
    normed_piece = (mid_unit * gain_piece.astype(jnp.float32)).astype(jnp.bfloat16)
    acc_gate = jnp.dot(normed_piece, gate_piece, preferred_element_type=jnp.float32)
    acc_up = jnp.dot(normed_piece, up_piece, preferred_element_type=jnp.float32)
    normalized_rows = normed_piece
    gains = gain_piece.astype(jnp.float32)
    mlp_in = normalized_rows
    sigma = jax.nn.sigmoid(acc_gate)
    swish = acc_gate * sigma
    act = (swish * acc_up).astype(jnp.bfloat16)
    mlp_out = jnp.einsum(
        "rf,nf->rn",
        act,
        lax.all_gather(w_down, "shard", axis=0, tiled=True),
        preferred_element_type=jnp.float32,
    )
    output = (valid * (resid + mlp_out)).astype(jnp.bfloat16).reshape(seq_count, piece, width)
    grad_y = cotangent.astype(jnp.float32).reshape(rows, width) * valid
    grad_y_low = grad_y.astype(jnp.bfloat16)
    grad_act = jnp.dot(
        grad_y_low,
        lax.all_gather(w_down, "shard", axis=0, tiled=True),
        preferred_element_type=jnp.float32,
    )
    grad_gate = (grad_act * acc_up * sigma * (1.0 + acc_gate * (1.0 - sigma))).astype(jnp.bfloat16)
    grad_up = (grad_act * swish).astype(jnp.bfloat16)
    gate_piece, up_piece = lax.all_gather((w_gate, w_up), "shard", axis=0, tiled=True)
    grad_mid = jnp.einsum(
        "rf,nf->rn", grad_gate, gate_piece, preferred_element_type=jnp.float32
    ) + jnp.einsum("rf,nf->rn", grad_up, up_piece, preferred_element_type=jnp.float32)
    grad_resid = grad_y + norm_back(mid_unit, inverse_mid, grad_mid * gains)
    mlp_gain_part = jnp.sum(mid_unit * grad_mid, 0)
    normalized_rows = mlp_in
    mlp_grads = jax.tree.map(
        lambda part: lax.psum_scatter(
            part.astype(jnp.bfloat16), "shard", scatter_dimension=0, tiled=True
        ).astype(jnp.float32),
        (
            outer(normalized_rows, grad_gate),
            outer(normalized_rows, grad_up),
            outer(grad_y_low, act),
        ),
    )
    resid_low = grad_resid.astype(jnp.bfloat16)
    grad_mixed = jnp.dot(
        resid_low,
        lax.all_gather(w_out, "shard", axis=0, tiled=True),
        preferred_element_type=jnp.float32,
    )
    grad_mixed = grad_mixed.astype(jnp.bfloat16).reshape(
        seq_count, piece, heads_kv, groups, head_dim
    )
    prob_again = jnp.exp(scores(query_rows, near_pair[0], allowed, scale) - log_total)
    grad_prob = jnp.einsum(
        "sqhgd,skhd->shgqk", grad_mixed, near_pair[1], preferred_element_type=jnp.float32
    )
    grad_values = jnp.einsum(
        "shgqk,sqhgd->skhd",
        prob_again.astype(jnp.bfloat16),
        grad_mixed,
        preferred_element_type=jnp.float32,
    )
    grad_score = (
        prob_again * (grad_prob - jnp.sum(prob_again * grad_prob, -1, keepdims=True))
    ).astype(jnp.bfloat16)
    grad_queries = (
        jnp.einsum(
            "shgqk,skhd->sqhgd", grad_score, near_pair[0], preferred_element_type=jnp.float32
        )
        * scale
    )
    grad_keys = (
        jnp.einsum("shgqk,sqhgd->skhd", grad_score, query_rows, preferred_element_type=jnp.float32)
        * scale
    )
    grad_pair = jnp.stack([grad_keys, grad_values])
    own_grad = grad_pair[:, :, reach * piece :]
    for back in range(1, reach + 1):
        lower = (reach - back) * piece
        own_grad = own_grad + passed_along(grad_pair[:, :, lower : lower + piece], "shard", -back)
    grad_query_post = grad_queries.reshape(seq_count, piece, heads_q, head_dim)
    grad_query_normed = grad_query_post * cosine_table - rotated_rows(grad_query_post * sine_table)
    grad_key_normed = own_grad[0] * cosine_table - rotated_rows(own_grad[0] * sine_table)
    grad_query_raw, query_gain_grad = head_norm_back(
        query_unit, query_inverse, grad_query_normed, query_gain.astype(jnp.float32)
    )
    grad_key_raw, key_gain_grad = head_norm_back(
        key_unit, key_inverse, grad_key_normed, key_gain.astype(jnp.float32)
    )
    grad_query_low = grad_query_raw.reshape(rows, heads_q * head_dim).astype(jnp.bfloat16)
    grad_key_low = grad_key_raw.reshape(rows, heads_kv * head_dim).astype(jnp.bfloat16)
    grad_value_low = own_grad[1].reshape(rows, heads_kv * head_dim).astype(jnp.bfloat16)
    query_piece, key_piece, value_piece = lax.all_gather(
        (w_query, key_matrix, value_matrix), "shard", axis=0, tiled=True
    )
    grad_in = (
        jnp.einsum("rf,nf->rn", grad_query_low, query_piece, preferred_element_type=jnp.float32)
        + jnp.einsum("rf,nf->rn", grad_key_low, key_piece, preferred_element_type=jnp.float32)
        + jnp.einsum("rf,nf->rn", grad_value_low, value_piece, preferred_element_type=jnp.float32)
    )
    grad_tokens = (
        (grad_resid + norm_back(x_unit, inverse_in, grad_in * attn_gains))
        .astype(jnp.bfloat16)
        .reshape(seq_count, piece, width)
    )
    attn_gain_part = jnp.sum(x_unit * grad_in, 0)
    normalized_rows = attn_in
    attn_grads = jax.tree.map(
        lambda part: lax.psum_scatter(
            part.astype(jnp.bfloat16), "shard", scatter_dimension=0, tiled=True
        ).astype(jnp.float32),
        (
            outer(normalized_rows, grad_query_low),
            outer(normalized_rows, grad_key_low),
            outer(normalized_rows, grad_value_low),
            outer(resid_low, mixed_rows),
        ),
    )
    head_grads = lax.psum(
        (query_gain_grad, key_gain_grad, attn_gain_part, mlp_gain_part), ("rep", "shard")
    )
    attn_gain_total = lax.dynamic_slice_in_dim(head_grads[2], shard_at * owned, owned, 0)
    mlp_gain_total = lax.dynamic_slice_in_dim(head_grads[3], shard_at * owned, owned, 0)
    summed = (
        lax.psum(attn_grads[0].astype(jnp.bfloat16), "rep").astype(jnp.float32),
        lax.psum(attn_grads[1].astype(jnp.bfloat16), "rep").astype(jnp.float32),
        lax.psum(attn_grads[2].astype(jnp.bfloat16), "rep").astype(jnp.float32),
        lax.psum(attn_grads[3].astype(jnp.bfloat16), "rep").astype(jnp.float32),
        lax.psum(mlp_grads[0].astype(jnp.bfloat16), "rep").astype(jnp.float32),
        lax.psum(mlp_grads[1].astype(jnp.bfloat16), "rep").astype(jnp.float32),
        lax.psum(mlp_grads[2].astype(jnp.bfloat16), "rep").astype(jnp.float32),
    )
    attn_grads = summed[:4]
    mlp_grads = summed[4:]
    return (
        output,
        grad_tokens,
        attn_gain_total,
        attn_grads[0],
        attn_grads[1],
        attn_grads[2],
        head_grads[0],
        head_grads[1],
        attn_grads[3],
        mlp_gain_total,
        mlp_grads[0],
        mlp_grads[1],
        mlp_grads[2],
    )


CORE, ACROSS_X, ACROSS_Y = 1, 2, 4
VMEM_BYTES = 56 * 2**20
FREE = pl.CostEstimate(flops=1, bytes_accessed=1, transcendentals=0)


def across(x, mask):
    count = lax.axis_size("rep")
    return lax.ppermute(x, "rep", [(i, i ^ mask) for i in range(count)])


def around(x, by):
    count = lax.axis_size("shard")
    return lax.ppermute(x, "shard", [(i, (i + by) % count) for i in range(count)])


class Stage(dict):
    __getattr__ = dict.__getitem__
    __setattr__ = dict.__setitem__
    __delattr__ = dict.__delitem__

    def end(self):
        self.update(lax.optimization_barrier(dict(self)))


def in_order(calls):
    outs = []
    for call, first, *rest in calls:
        if outs:
            last = outs[-1][0] if isinstance(outs[-1], (list, tuple)) else outs[-1]
            first = lax.optimization_barrier((first, last))[0]
        outs.append(call(first, *rest))
    return outs


def ring_sum_first(chunks):
    return around(chunks[2], 1), around(chunks[1], -1)


def near(piece):
    return across(piece, ACROSS_X), across(piece, ACROSS_Y)


def far(from_x, from_y):
    half = from_x.shape[0] // 2
    return across(from_x[:half], ACROSS_Y), across(from_y[half:], ACROSS_X)


def rounded_sum(*parts):
    return sum(part.astype(jnp.float32) for part in parts).astype(jnp.bfloat16)


def sequence_pairs(turn):
    groups, shards = lax.axis_size("rep"), lax.axis_size("shard")
    pairs = []
    for group in range(groups):
        chip, core = divmod(group, 2)
        for at in range(shards):
            to_group, to_shard = 2 * chip + at // 2, 2 * core + (turn ^ (at & 1))
            pairs.append((group * shards + at, to_group * shards + to_shard))
    return pairs


def rolled(x):
    count, at = lax.axis_size("shard"), lax.axis_index("shard")
    width = x.shape[1] // count
    return jnp.concatenate(
        [lax.dynamic_slice_in_dim(x, ((at - i) % count) * width, width, 1) for i in range(count)],
        1,
    )


def sequence_cuts(x):
    odd = lax.axis_index("shard") & 1
    return [lax.dynamic_index_in_dim(x, turn ^ odd, 0, keepdims=False) for turn in range(2)]


def to_sequence(cut, turn):
    return lax.ppermute(cut, ("rep", "shard"), sequence_pairs(turn))


def from_sequences_send(x):
    odd = lax.axis_index("shard") & 1
    x = x.reshape(2, x.shape[0] // 2, x.shape[1])
    return [
        lax.ppermute(
            lax.dynamic_index_in_dim(x, turn ^ odd, 0, keepdims=False),
            ("rep", "shard"),
            [(to, at) for at, to in sequence_pairs(turn)],
        )
        for turn in range(2)
    ]


def in_turn(came):
    even = lax.axis_index("shard") & 1 == 0
    return [jnp.where(even, came[0], came[1]), jnp.where(even, came[1], came[0])]


def column_block(weights, at):
    cuts = [w.shape[1] // 8 for w in weights]
    return jnp.concatenate(
        [lax.dynamic_slice_in_dim(w, at * cut, cut, 1) for w, cut in zip(weights, cuts)], 1
    )


def whole_columns(me, own, other, widths, part=0):
    rows, columns = own.shape[0] // 4, sum(widths)

    def body(me_ref, own_ref, other_ref, *outs):
        def put(block):
            start = 0
            for out, width in zip(outs, widths):
                out[...] = block[:, start : start + width].astype(jnp.float32)
                start += width

        mine = (me_ref[0] ^ pl.program_id(0)) & 1 == 0
        pl.when(mine)(lambda: put(own_ref))
        pl.when(jnp.logical_not(mine))(lambda: put(other_ref))

    spec = pl.BlockSpec((rows, columns), lambda i, at: ((at[0] ^ i) >> 1, part))
    return pl.pallas_call(
        body,
        grid_spec=pltpu.PrefetchScalarGridSpec(
            num_scalar_prefetch=1,
            grid=(8,),
            in_specs=[spec, spec],
            out_specs=[pl.BlockSpec((rows, w), lambda i, at: (0, i)) for w in widths],
        ),
        out_shape=[jax.ShapeDtypeStruct((rows, 8 * w), jnp.float32) for w in widths],
        compiler_params=pltpu.CompilerParams(vmem_limit_bytes=VMEM_BYTES),
        cost_estimate=FREE,
        name="whole_columns",
    )(me, own, other)


def turned(x):
    return pltpu.roll(x, x.shape[-1] // 2, x.ndim - 1)


def nt(left, right):
    return lax.dot_general(
        left, right, (((1,), (1,)), ((), ())), preferred_element_type=jnp.float32
    )


def tn(left, right):
    return lax.dot_general(
        left, right, (((0,), (0,)), ((), ())), preferred_element_type=jnp.float32
    )


def unit_of(raw):
    inverse = lax.rsqrt(jnp.mean(raw * raw, -1, keepdims=True) + EPS)
    return raw * inverse, inverse


def project_body(
    normed, own0, came0, own1, came1, cosine, sine, gains, raw, query, key_value
):
    step = own0.shape[0]
    dim = cosine.shape[1]
    for block, (own, came) in enumerate(((own0, came0), (own1, came1))):
        at = block * 4 * dim
        raw[:, at : at + 4 * dim] = jnp.dot(
            normed[:, :step], own[...], preferred_element_type=jnp.float32
        ) + jnp.dot(normed[:, step:], came[...], preferred_element_type=jnp.float32)
        for i in range(3):
            unit, _ = unit_of(raw[:, at + i * dim : at + (i + 1) * dim])
            head = unit * gains[i // 2 : i // 2 + 1, :]
            head = (head * cosine[...] + turned(head) * sine[...]).astype(jnp.bfloat16)
            if i < 2:
                query[:, (2 * block + i) * dim : (2 * block + i + 1) * dim] = head
            else:
                key_value[:, 2 * block * dim : (2 * block + 1) * dim] = head
        key_value[:, (2 * block + 1) * dim : (2 * block + 2) * dim] = raw[
            :, at + 3 * dim : at + 4 * dim
        ].astype(jnp.bfloat16)


def window_mask(info, part, rows, columns):
    half = columns - rows
    row = lax.broadcasted_iota(jnp.int32, (rows, columns), 0)
    column = lax.broadcasted_iota(jnp.int32, (rows, columns), 1)
    gap = column - row - half
    slot = column + ((info[0] - 1) * half + part * rows)
    allowed = (gap <= 0) & (gap > -half) & (slot >= 0) & ((slot < info[1]) | (gap == 0))
    mask = jnp.where(allowed, 0.0, NEG)
    return jnp.concatenate([mask, mask], 0)


def two_heads(ref, at, block, dim):
    return jnp.concatenate(
        [ref[at, h * dim : (h + 1) * dim] for h in (2 * block, 2 * block + 1)], 0
    )


def key_columns(block, dim):
    key = slice(2 * block * dim, (2 * block + 1) * dim)
    value = slice((2 * block + 1) * dim, (2 * block + 2) * dim)
    return key, value


def seen_pair(before, own, part, block, dim):
    here, there = key_columns(block, dim), key_columns(1 - block, dim)
    rows = own.shape[0] // 2
    if part == 0:
        return [
            jnp.concatenate([before[:, t], own[:rows, h]], 0) for h, t in zip(here, there)
        ]
    return [jnp.concatenate([before[rows:, t], own[:, h]], 0) for h, t in zip(here, there)]


def attend_body(info, query, before, own, mixed, log_total):
    dim = own.shape[1] // 4
    rows = query.shape[0] // 2
    for part in range(2):
        at = slice(part * rows, (part + 1) * rows)
        mask = window_mask(info, part, rows, 3 * rows)
        for block in range(2):
            keys, values = seen_pair(before, own, part, block, dim)
            score = nt(two_heads(query, at, block, dim), keys) * dim**-0.5 + mask
            top = jnp.max(score, -1, keepdims=True)
            expo = jnp.exp(score - top)
            total = jnp.sum(expo, -1, keepdims=True)
            prob = (expo * (1.0 / total)).astype(jnp.bfloat16)
            out = jnp.dot(prob, values, preferred_element_type=jnp.float32).astype(jnp.bfloat16)
            log = jnp.broadcast_to(top + jnp.log(total), (2 * rows, dim))
            for i in range(2):
                on = slice((2 * block + i) * dim, (2 * block + i + 1) * dim)
                mixed[at, on] = out[i * rows : (i + 1) * rows]
                log_total[at, on] = log[i * rows : (i + 1) * rows]


def attend_back_body(
    info, query, before, own, log_total, grad_resid, weight0, weight1, raw, cosine, sine, gain,
    grad_query, grad_own, grad_before, gain_part, grad_keys, grad_values, grad_mixed,
):
    dim = own.shape[1] // 4
    rows = query.shape[0] // 2
    scale = dim**-0.5
    gain_total = jnp.zeros((1, dim), jnp.float32)
    masks = [window_mask(info, part, rows, 3 * rows) for part in range(2)]
    for block, weight in enumerate((weight0, weight1)):
        on = slice(2 * block * dim, 2 * (block + 1) * dim)
        grad_mixed[:, on] = jnp.dot(
            grad_resid[...], weight[...], preferred_element_type=jnp.float32
        ).astype(jnp.bfloat16)
        grad_keys[...] = jnp.zeros_like(grad_keys)
        grad_values[...] = jnp.zeros_like(grad_values)
        for part in range(2):
            keys, values = seen_pair(before, own, part, block, dim)
            at = slice(part * rows, (part + 1) * rows)
            seen = slice(part * rows, part * rows + 3 * rows)
            queries = two_heads(query, at, block, dim)
            grads = two_heads(grad_mixed, at, block, dim)
            log = two_heads(log_total, at, block, dim)[:, :1]
            prob = jnp.exp(nt(queries, keys) * scale + masks[part] - log)
            grad_prob = nt(grads, values)
            inner = jnp.sum(prob * grad_prob, -1, keepdims=True)
            grad_score = (prob * (grad_prob - inner)).astype(jnp.bfloat16)
            grad_values[seen, :] += tn(prob.astype(jnp.bfloat16), grads)
            grad_keys[seen, :] += tn(grad_score, queries) * scale
            both = jnp.dot(grad_score, keys, preferred_element_type=jnp.float32) * scale
            for i in range(2):
                head = 2 * block + i
                back = both[i * rows : (i + 1) * rows]
                back = back * cosine[at, :] - turned(back) * sine[at, :]
                there = (2 * head - head % 2) * dim
                unit, inverse = unit_of(raw[at, there : there + dim])
                gain_total += jnp.sum(unit * back, 0, keepdims=True)
                back = back * gain[...]
                back = inverse * (back - unit * jnp.mean(back * unit, -1, keepdims=True))
                grad_query[at, head * dim : (head + 1) * dim] = back.astype(jnp.bfloat16)
        for grad, here, there in zip(
            (grad_keys, grad_values), key_columns(block, dim), key_columns(1 - block, dim)
        ):
            grad_before[:, there] = grad[: 2 * rows, :].astype(jnp.bfloat16)
            grad_own[:, here] = grad[2 * rows :, :]
    gain_part[...] = gain_total


def finish_body(grad_query, grad_own, came, raw, cosine, sine, gain, even, odd, gain_part):
    dim = cosine.shape[1]
    total = jnp.zeros((1, dim), jnp.float32)
    for block, out in enumerate((even, odd)):
        key, value = key_columns(block, dim)
        back = grad_own[:, key] + came[:, key].astype(jnp.float32)
        back = back * cosine[...] - turned(back) * sine[...]
        unit, inverse = unit_of(raw[:, (4 * block + 2) * dim : (4 * block + 3) * dim])
        total += jnp.sum(unit * back, 0, keepdims=True)
        back = back * gain[...]
        back = inverse * (back - unit * jnp.mean(back * unit, -1, keepdims=True))
        out[:, : 2 * dim] = grad_query[:, 2 * block * dim : (2 * block + 2) * dim]
        out[:, 2 * dim : 3 * dim] = back.astype(jnp.bfloat16)
        grad_value = grad_own[:, value] + came[:, value].astype(jnp.float32)
        out[:, 3 * dim :] = grad_value.astype(jnp.bfloat16)
    gain_part[...] = total


def vmem_call(body, outs, scratch=(), scalars=0, name=None):
    def call(*args):
        in_specs = [
            pl.BlockSpec(memory_space=pltpu.SMEM if i < scalars else pltpu.VMEM)
            for i in range(len(args))
        ]
        return pl.pallas_call(
            body,
            grid=(1,),
            out_shape=outs,
            in_specs=in_specs,
            out_specs=jax.tree.map(lambda _: pl.BlockSpec(memory_space=pltpu.VMEM), outs),
            scratch_shapes=scratch,
            compiler_params=pltpu.CompilerParams(vmem_limit_bytes=VMEM_BYTES),
        cost_estimate=FREE,
            name=name,
        )(*args)

    return call


def hidden_units(mids, grads_y, weights):
    width, units = weights.shape[0], weights.shape[1] // 3
    count = len(mids)
    heights = [m.shape[0] for m in mids]
    rows, cut = sum(heights), units // 3

    def body(*refs):
        gate_w, up_w, w_down, act, grad_gate, grad_up = refs[2 * count :]
        start = 0
        for mid, grad_y in zip(refs[:count], refs[count : 2 * count]):
            at = slice(start, start + mid.shape[0])
            start += mid.shape[0]
            gate = jnp.dot(mid[...], gate_w[...], preferred_element_type=jnp.float32)
            up = jnp.dot(mid[...], up_w[...], preferred_element_type=jnp.float32)
            grad_act = jnp.dot(grad_y[...], w_down[...], preferred_element_type=jnp.float32)
            sigma = jax.nn.sigmoid(gate)
            swish = gate * sigma
            act[at, :] = (swish * up).astype(jnp.bfloat16)
            slope = grad_act * up * sigma * (1.0 + gate * (1.0 - sigma))
            grad_gate[at, :] = slope.astype(jnp.bfloat16)
            grad_up[at, :] = (grad_act * swish).astype(jnp.bfloat16)

    row_specs = [
        pl.BlockSpec((h, width), lambda j: (0, 0), pipeline_mode=pl.Buffered(1)) for h in heights
    ]
    return pl.pallas_call(
        body,
        grid=(3,),
        out_shape=[jax.ShapeDtypeStruct((rows, units), jnp.bfloat16)] * 3,
        in_specs=[
            *row_specs,
            *row_specs,
            pl.BlockSpec((width, cut), lambda j: (0, j)),
            pl.BlockSpec((width, cut), lambda j: (0, j + 3)),
            pl.BlockSpec((width, cut), lambda j: (0, j + 6)),
        ],
        out_specs=[pl.BlockSpec((rows, cut), lambda j: (0, j))] * 3,
        compiler_params=pltpu.CompilerParams(vmem_limit_bytes=VMEM_BYTES),
        cost_estimate=FREE,
        name="hidden_units",
    )(*mids, *grads_y, weights, weights, weights)


def from_hidden(pairs, eighths):
    count, parts = len(pairs), len(eighths)
    rows, units = pairs[0][0].shape[0] // 8, pairs[0][0].shape[1]
    width = pairs[0][1].shape[0]
    cut = width // 4

    def body(*refs):
        ins, outs = refs[: -(parts // 2)], refs[-(parts // 2) :]
        total = 0.0
        for i in range(count):
            part = ins[i * (parts + 1) : (i + 1) * (parts + 1)]
            left = jnp.concatenate([p[...] for p in part[:-1]], 0)
            total = total + nt(left, part[-1][...])
        for i, out in enumerate(outs):
            out[...] = total[2 * i * rows : 2 * (i + 1) * rows].astype(jnp.bfloat16)

    specs, args = [], []
    for left, right, at in pairs:
        specs += [pl.BlockSpec((rows, units), lambda j, e=e: (e, 0)) for e in eighths]
        specs.append(pl.BlockSpec((cut, units), lambda j, at=at: (j, at)))
        args += [left] * parts + [right]
    return pl.pallas_call(
        body,
        grid=(4,),
        out_shape=[jax.ShapeDtypeStruct((2 * rows, width), jnp.bfloat16)] * (parts // 2),
        in_specs=specs,
        out_specs=[pl.BlockSpec((2 * rows, cut), lambda j: (0, j))] * (parts // 2),
        compiler_params=pltpu.CompilerParams(vmem_limit_bytes=VMEM_BYTES),
        cost_estimate=FREE,
        name="from_hidden",
    )(*args)


def row_outer(lefts, groups, first, tiles, added=None, places=None, part=None):
    rights = [right for group in groups for right in group]
    places = range(len(rights)) if places is None else places
    added = [] if added is None else [added] * len(rights)
    width = lefts[0].shape[1]
    tile = width // 8
    count = len(lefts)
    rows = sum(left.shape[0] for left in lefts)
    wide = rights[0].shape[1] // (1 if part is None else 2)
    columns = [wide * len(group) for group in groups]

    def body(*refs):
        left_refs = refs[:count]
        right_refs = refs[count : count + len(rights)]
        add_refs = refs[count + len(rights) : count + len(rights) + len(added)]
        outs = refs[count + len(rights) + len(added) :]
        place = 0
        for i, group in enumerate(groups):
            column = 0
            for _ in group:
                on = slice(column, column + wide)
                total, start = 0.0, 0
                for left in left_refs:
                    stop = start + left.shape[0]
                    total = total + tn(left[...], right_refs[place][start:stop, :])
                    start = stop
                if added:
                    total = total + add_refs[place][...].astype(jnp.float32)
                outs[i][:, on] = total.astype(jnp.bfloat16)
                place += 1
                column += wide

    return pl.pallas_call(
        body,
        grid=(tiles,),
        out_shape=[jax.ShapeDtypeStruct((tiles * tile, c), jnp.bfloat16) for c in columns],
        in_specs=[
            *(pl.BlockSpec((left.shape[0], tile), lambda j: (0, j + first)) for left in lefts),
            *(
                pl.BlockSpec(
                    (right.shape[0], wide), lambda j: (0, part or 0), pipeline_mode=pl.Buffered(1)
                )
                for right in rights
            ),
            *(
                pl.BlockSpec((tile, wide), lambda j, at=at: (j + first, at))
                for at in places[: len(added)]
            ),
        ],
        out_specs=[pl.BlockSpec((tile, c), lambda j: (j, 0)) for c in columns],
        compiler_params=pltpu.CompilerParams(vmem_limit_bytes=VMEM_BYTES),
        cost_estimate=pl.CostEstimate(
            flops=2 * rows * tiles * tile * sum(columns),
            bytes_accessed=2 * rows * (width + sum(columns)),
            transcendentals=0,
        ),
        name="row_outer",
    )(*lefts, *rights, *added)


def close_body(x, *refs):
    mixed, weights = refs[:4], refs[4:12]
    gains, resid, mid = refs[12:]
    at = pl.program_id(0)
    step = x.shape[1]
    columns = weights[0].shape[1]
    total = x[...].astype(jnp.float32)
    for i in range(8):
        part = mixed[i // 2][:, (i % 2) * columns : (i % 2 + 1) * columns]
        total = total + nt(part, weights[i][...])
    resid[:, pl.ds(pl.multiple_of(at * step, step), step)] = total

    @pl.when(at == 3)
    def _():
        unit, _ = unit_of(resid[...])
        mid[...] = (unit * gains[...]).astype(jnp.bfloat16)


def close_attention(x, mixed, weights, gains):
    rows, width = x.shape
    step = width // 4
    whole = lambda a: pl.BlockSpec(a.shape, lambda j: (0, 0))
    return pl.pallas_call(
        close_body,
        grid=(4,),
        out_shape=[
            jax.ShapeDtypeStruct((rows, width), jnp.float32),
            jax.ShapeDtypeStruct((rows, width), jnp.bfloat16),
        ],
        in_specs=[
            pl.BlockSpec((rows, step), lambda j: (0, j)),
            *(whole(m) for m in mixed),
            *(pl.BlockSpec((step, w.shape[1]), lambda j: (j, 0)) for w in weights),
            whole(gains),
        ],
        out_specs=[pl.BlockSpec((rows, width), lambda j: (0, 0))] * 2,
        compiler_params=pltpu.CompilerParams(vmem_limit_bytes=VMEM_BYTES),
        cost_estimate=FREE,
        name="close_attention",
    )(x, *mixed, *weights, gains)


def back_to_rows(blocks, weights):
    rows = blocks[0].shape[0]
    step, columns = weights[0][0].shape
    count = len(blocks)

    def body(*refs):
        lefts = refs[:count]
        hbm = refs[count : 3 * count]
        out = refs[3 * count]
        held, sems = refs[3 * count + 1 :]
        copies = []
        for i in range(count):
            own, came = hbm[2 * i : 2 * i + 2]
            copies.append(
                [
                    pltpu.make_async_copy(own, held.at[i, :step], sems.at[i, 0]),
                    pltpu.make_async_copy(came, held.at[i, step:], sems.at[i, 1]),
                ]
            )
        for some in copies:
            for copy in some:
                copy.start()
        for i in range(count):
            for copy in copies[i]:
                copy.wait()
            for k in range(4):
                on = slice(k * step, (k + 1) * step)
                part = nt(lefts[i][...], held[i, on])
                if i == 0:
                    out[:, on] = part
                else:
                    out[:, on] += part

    return pl.pallas_call(
        body,
        grid=(1,),
        out_shape=jax.ShapeDtypeStruct((rows, 4 * step), jnp.float32),
        in_specs=[pl.BlockSpec(memory_space=pltpu.VMEM)] * count
        + [pl.BlockSpec(memory_space=pl.ANY)] * (2 * count),
        out_specs=pl.BlockSpec(memory_space=pltpu.VMEM),
        scratch_shapes=[
            pltpu.VMEM((count, 4 * step, columns), jnp.bfloat16),
            pltpu.SemaphoreType.DMA((count, 2)),
        ],
        compiler_params=pltpu.CompilerParams(vmem_limit_bytes=VMEM_BYTES),
        cost_estimate=FREE,
        name="back_to_rows",
    )(*blocks, *(part for w in weights for part in w))


def on_device_block(
    tokens,
    lengths,
    attn_gain,
    w_query,
    key_matrix,
    value_matrix,
    query_gain,
    key_gain,
    w_out,
    mlp_gain,
    w_gate,
    w_up,
    w_down,
    cotangent,
):
    low, full = jnp.bfloat16, jnp.float32
    width = tokens.shape[2]
    head_dim = query_gain.shape[0]
    shards = lax.axis_size("shard")
    shard_at = lax.axis_index("shard")
    me = lax.axis_index("rep")
    core = me & 1
    count = lax.axis_size("rep")

    s = Stage()
    s.cotangent = cotangent
    piece = width // shards

    s.own_blocks = [
        column_block((w_query, key_matrix, value_matrix), me ^ i) for i in range(8)
    ]
    gain_rows = jnp.concatenate(
        [jnp.stack([attn_gain, mlp_gain]), jnp.zeros((14, piece), low)], 0
    )
    travelling = jnp.concatenate([s.own_blocks[0], gain_rows], 0)
    s.tokens = tokens
    s.out_block = column_block((w_out,), me)
    s.ffn_block = column_block((w_gate, w_up, w_down), me)
    s.before, s.behind = around(travelling, 1), around(travelling, -1)
    s.other_lengths = across(lengths, CORE)
    s.end()

    s.ahead = around(s.before, 1)
    tokens_sent = [to_sequence(cut, turn) for turn, cut in enumerate(sequence_cuts(s.tokens))]
    out_own = lax.all_gather(s.out_block, "shard", axis=0, tiled=True)
    del s.out_block, s.tokens
    s.end()

    parts = (s.before, s.ahead, s.behind)
    s.came = jnp.concatenate([part[:piece] for part in parts], 0)
    s.gains = jnp.concatenate([gain_rows[:2], *(part[piece : piece + 2] for part in parts)], 1)
    s.came_near = near(s.came)
    s.came_own = across(s.came, CORE)
    s.x_came = tokens_sent
    del s.before, s.behind, s.ahead
    s.end()

    grad_y_sent = [
        to_sequence(cut, turn) for turn, cut in enumerate(sequence_cuts(s.cotangent))
    ]
    s.came_far = far(*s.came_near)
    s.came_other = [s.came_own, *(across(block, CORE) for block in s.came_near)]
    gains = rolled(s.gains.astype(full))
    s.mlp_gains = gains[1:]
    s.attn_gains = gains[:1]
    s.x_low = jnp.concatenate(in_turn(s.x_came), 0)
    rows = s.x_low.shape[0]
    x_rows = s.x_low.astype(full)
    s.inverse_in = lax.rsqrt(jnp.mean(x_rows * x_rows, -1, keepdims=True) + EPS)
    s.normed = rolled((x_rows * s.inverse_in * s.attn_gains).astype(low))
    query_gains = query_gain.astype(full)[None]
    key_gains = key_gain.astype(full)[None]
    s.head_gains = jnp.concatenate([query_gains, key_gains], 0)
    both = jnp.where(
        core == 0,
        jnp.concatenate([lengths, s.other_lengths]),
        jnp.concatenate([s.other_lengths, lengths]),
    )
    length = lax.dynamic_index_in_dim(both, shard_at, 0, keepdims=False)
    s.info = jnp.stack([core, length]).astype(jnp.int32)
    query_pos = core * rows + jnp.arange(rows, dtype=jnp.int32)
    s.valid = (query_pos < length)[:, None].astype(full)
    cosine, sine = tables(query_pos, head_dim)
    s.cosine, sine = cosine[0, :, 0], sine[0, :, 0]
    s.sine = jnp.concatenate([-sine[:, : head_dim // 2], sine[:, head_dim // 2 :]], 1)
    s.out_own = out_own
    del s.gains, s.x_came, s.other_lengths, s.cotangent, s.came_own
    s.end()

    head_columns = 2 * head_dim
    block_columns = 4 * head_dim
    quad_rows = jax.ShapeDtypeStruct((rows, block_columns), low)
    quad_sums = jax.ShapeDtypeStruct((rows, block_columns), full)
    gain_sum = jax.ShapeDtypeStruct((1, head_dim), full)
    project = vmem_call(
        project_body,
        [jax.ShapeDtypeStruct((rows, 2 * block_columns), full), quad_rows, quad_rows],
        name="project",
    )
    attend = vmem_call(attend_body, [quad_rows, quad_sums], scalars=1, name="attend")
    attend_back = vmem_call(
        attend_back_body,
        [quad_rows, quad_sums, quad_rows, gain_sum],
        scratch=[pltpu.VMEM((2 * rows, head_dim), full)] * 2
        + [pltpu.VMEM((rows, block_columns), low)],
        scalars=1,
        name="attend_back",
    )
    finish = vmem_call(finish_body, [quad_rows, quad_rows, gain_sum], name="finish")
    upward = [(i, i + 1) for i in range(0, count, 2)]
    downward = [(i + 1, i) for i in range(0, count, 2)]

    def project_call(i, came, other):
        return (
            project, s.normed, s.own_blocks[2 * i], came, s.own_blocks[2 * i + 1], other,
            s.cosine, s.sine, s.head_gains,
        )

    def attend_call(projected, earlier):
        return (
            lambda query, own, before: attend(s.info, query, before, own),
            *projected[1:], earlier,
        )

    came_last = jnp.concatenate(s.came_far, 0)
    s.came_last = (came_last, across(came_last, CORE))
    s.out_near = near(s.out_own)
    s.out_own_other = across(s.out_own, CORE)
    s.projected = in_order(
        [
            project_call(i, block, other)
            for i, (block, other) in enumerate(zip((s.came, *s.came_near), s.came_other))
        ]
    )
    s.grad_y_came = grad_y_sent
    del s.came_far
    s.end()

    ffn_own = lax.all_gather(s.ffn_block, "shard", axis=0, tiled=True)
    grad_y = jnp.concatenate(in_turn(s.grad_y_came), 0)
    s.grad_y = jnp.where(s.valid > 0, grad_y, jnp.zeros_like(grad_y))
    grad_y_near = near(s.grad_y)
    s.out_far = far(*s.out_near)
    s.out_near_other = [across(block, CORE) for block in s.out_near]
    s.earlier = [lax.ppermute(p[2], "rep", upward) for p in s.projected]
    (s.projected_last,) = in_order([project_call(3, *s.came_last)])
    del s.ffn_block, s.grad_y_came
    s.end()

    out_last = jnp.concatenate(s.out_far, 0)
    s.out_last = (out_last, across(out_last, CORE))
    s.earlier_last = lax.ppermute(s.projected_last[2], "rep", upward)
    s.attended = in_order([attend_call(*pair) for pair in zip(s.projected, s.earlier)])
    s.grad_y_near = grad_y_near
    del s.out_far
    s.end()

    s.projected = [*s.projected, s.projected_last]
    s.earlier = [*s.earlier, s.earlier_last]
    s.out_blocks = [
        s.out_own, s.out_own_other, s.out_near[0], s.out_near_other[0], s.out_near[1],
        s.out_near_other[1], *s.out_last,
    ]
    (last,) = in_order([attend_call(s.projected_last, s.earlier_last)])
    s.attended = [*s.attended, last]
    s.mixed = [a[0] for a in s.attended]
    s.resid, s.mid = close_attention(s.x_low, s.mixed, s.out_blocks, s.mlp_gains)
    s.grad_y_far = far(*s.grad_y_near)
    s.came = [s.came, *s.came_near, s.came_last[0]]
    s.came_other = [*s.came_other, s.came_last[1]]
    del s.came_near, s.came_last
    del s.out_own, s.out_own_other, s.out_near, s.out_near_other, s.out_last
    del s.projected_last, s.earlier_last
    s.end()

    s.mid_near = near(s.mid)
    s.end()

    s.mid_far = far(*s.mid_near)
    s.ffn_own = ffn_own
    s.end()

    s.mids = [s.mid, *s.mid_near, *s.mid_far]
    s.grads_y = [s.grad_y, *s.grad_y_near, *s.grad_y_far]
    s.ffn_other = across(s.ffn_own, CORE)
    units = s.ffn_own.shape[1] // 3
    s.hidden_own = hidden_units(s.mids, s.grads_y, s.ffn_own)
    del s.mid, s.mid_near, s.mid_far, s.grad_y_near, s.grad_y_far
    s.end()

    def gate_up_pairs():
        return [
            (hidden[i], weights, i - 1)
            for hidden, weights in ((s.hidden_own, s.ffn_own), (s.hidden_other, s.ffn_other))
            for i in (1, 2)
        ]

    def down_pairs():
        return [(s.hidden_own[0], s.ffn_own, 2), (s.hidden_other[0], s.ffn_other, 2)]

    def from_hidden_call(pairs, eighths):
        return (
            lambda first: from_hidden([(first, *pairs[0][1:]), *pairs[1:]], eighths),
            pairs[0][0],
        )

    def outer_call(lefts, rights, *added):
        return lambda first: row_outer(lefts, [[first, *rights[1:]]], 0, 8, *added)[0], rights[0]

    def send_near(sent):
        return across(sent[0], ACROSS_X), across(sent[1], ACROSS_Y)

    def send_far(came, rest, split):
        one_tail, two_head = rest
        return (
            across(rounded_sum(one_tail, split(came[1])[1]), ACROSS_X),
            across(rounded_sum(two_head, split(came[0])[1]), ACROSS_Y),
        )

    def total(came, came_far, own, split):
        head, tail = own
        full_sum = lambda *parts: sum(part.astype(full) for part in parts)
        return jnp.concatenate(
            [
                full_sum(head, split(came[0])[0], came_far[1]),
                full_sum(tail, split(came[1])[0], came_far[0]),
            ],
            0,
        )

    by_rows = lambda a: jnp.split(a, 2, 0)
    by_columns = lambda a: jnp.split(a, 2, 1)
    to_plane, rest_of_plane = (2, 6, 5, 7), (3, 4, 0, 1)

    s.hidden_other = hidden_units(s.mids, s.grads_y, s.ffn_other)
    (s.down_outer,) = in_order([outer_call(s.grads_y, s.hidden_other[:1])])
    s.end()

    s.down_came = across(s.down_outer, CORE)
    s.mid_sent = from_hidden(gate_up_pairs(), to_plane)
    del s.down_outer
    s.end()

    s.mid_came = send_near(s.mid_sent)
    s.down_mine, s.mid_rest, s.gate_up_outer = in_order(
        [
            outer_call(s.grads_y, s.hidden_own[:1], s.down_came),
            from_hidden_call(gate_up_pairs(), rest_of_plane),
            outer_call(s.mids, s.hidden_other[1:]),
        ]
    )
    del s.mid_sent, s.down_came
    s.end()

    down_total = lax.psum_scatter(s.down_mine, "shard", scatter_dimension=0, tiled=True)
    s.mid_came_far = send_far(s.mid_came, by_rows(s.mid_rest[0]), by_rows)
    s.gate_up_came = across(s.gate_up_outer, CORE)
    s.mlp_sent, s.mlp_rest = in_order(
        [
            from_hidden_call(down_pairs(), to_plane),
            from_hidden_call(down_pairs(), rest_of_plane),
        ]
    )
    del s.gate_up_outer, s.down_mine
    s.end()

    def back_call(i):
        raw, query, own_pair = s.projected[i]
        return (
            lambda query, *rest: attend_back(s.info, query, *rest),
            query, s.earlier[i], own_pair, s.attended[i][1], s.resid_low,
            *s.out_blocks[2 * i : 2 * i + 2], raw, s.cosine, s.sine, s.head_gains[:1],
        )

    def finish_call(i):
        return (
            finish, s.backs[i][0], s.backs[i][1], s.returned[i], s.projected[i][0],
            s.cosine, s.sine, s.head_gains[1:],
        )

    def give_back(*chips):
        s.returned = s.returned | {
            i: lax.ppermute(s.backs[i][2], "rep", downward) for i in chips
        }

    def odd_call(left, blocks, part=None):
        return lambda first: row_outer([first], [blocks], 0, 8, part=part)[0], left

    def head_call(left, blocks, came, part=None, places=(0, 1, 2, 3)):
        groups = [[blocks[1], blocks[3]], [blocks[2]], [blocks[0]]]
        at = [places[i] for i in (1, 3, 2, 0)]
        return lambda first: row_outer([first], groups, 0, 4, came, at, part), left

    def tail_call(left, blocks, came, part=None, places=(0, 1, 2, 3)):
        groups = [[blocks[2], blocks[3]], [blocks[1]], [blocks[0]]]
        at = [places[i] for i in (2, 3, 1, 0)]
        return lambda first: row_outer([first], groups, 4, 4, came, at, part), left

    s.mlp_came = send_near(s.mlp_sent)
    grad_mid = total(s.mid_came, s.mid_came_far, by_rows(s.mid_rest[1]), by_rows)
    inverse_mid = lax.rsqrt(jnp.mean(s.resid * s.resid, -1, keepdims=True) + EPS)
    mid_unit = s.resid * inverse_mid
    s.mlp_gain_part = jnp.sum(mid_unit * grad_mid, 0)
    s.grad_resid = s.grad_y.astype(full) + norm_back(
        mid_unit, inverse_mid, grad_mid * s.mlp_gains
    )
    s.resid_low = s.grad_resid.astype(low)
    s.resid_rolled = rolled(s.resid_low)
    s.returned = {}
    back, s.out_odd, s.gate_up_mine = in_order(
        [
            back_call(3),
            odd_call(s.resid_rolled, s.mixed, 1),
            outer_call(s.mids, s.hidden_own[1:], s.gate_up_came),
        ]
    )
    s.backs = {3: back}
    s.down_total = down_total
    del s.mid_came, s.mid_came_far, s.mid_rest, s.gate_up_came, s.hidden_own, s.hidden_other
    del s.mids, s.grads_y, s.ffn_own, s.ffn_other, s.mlp_sent
    s.end()

    gate_up_total = lax.psum_scatter(s.gate_up_mine, "shard", scatter_dimension=0, tiled=True)
    s.mlp_came_far = send_far(s.mlp_came, by_rows(s.mlp_rest[0]), by_rows)
    s.out_came = across(s.out_odd, CORE)
    give_back(3)
    back1, back2 = in_order([back_call(1), back_call(2)])
    s.backs = s.backs | {1: back1, 2: back2}
    del s.out_odd, s.gate_up_mine
    s.end()

    s.down_near = near(s.down_total)
    give_back(1, 2)
    s.out_head, s.out_tail, back, finished = in_order(
        [
            head_call(s.resid_rolled, s.mixed, s.out_came, 0),
            tail_call(s.resid_rolled, s.mixed, s.out_came, 0),
            back_call(0),
            finish_call(3),
        ]
    )
    s.backs = s.backs | {0: back}
    s.finished = {3: finished}
    del s.out_came
    s.end()

    s.out_near = send_near((s.out_head[0], s.out_tail[0]))
    mlp_out = total(s.mlp_came, s.mlp_came_far, by_rows(s.mlp_rest[1]), by_rows)
    s.output = (s.valid * (s.resid + mlp_out)).astype(low)
    give_back(0)
    finished1, finished2 = in_order([finish_call(1), finish_call(2)])
    s.finished = s.finished | {1: finished1, 2: finished2}
    del s.mlp_came, s.mlp_came_far, s.mlp_rest, s.resid
    s.end()

    output_sent = from_sequences_send(s.output)
    s.out_far = send_far(s.out_near, (s.out_tail[1], s.out_head[1]), by_columns)
    s.down_far = far(*s.down_near)
    (finished,) = in_order([finish_call(0)])
    s.finished = s.finished | {0: finished}
    (s.odd,) = in_order([odd_call(s.normed, [s.finished[i][1] for i in range(4)])])
    s.gate_up_total = gate_up_total
    s.output_first = output_sent[0]
    del s.output
    s.end()

    my_group = me.astype(jnp.int32)[None]

    def whole_call(widths, own, other, part=0):
        return lambda first: whole_columns(my_group, first, other, widths, part), own

    s.gate_up_near = near(s.gate_up_total)
    s.qkv_came = across(s.odd, CORE)
    out_sum = total(s.out_near, s.out_far, (s.out_head[2], s.out_tail[2]), by_columns)
    s.out_chunks = jnp.split(out_sum.astype(low), shards, 0)
    s.out_ring = ring_sum_first(s.out_chunks)
    weights = [
        pair
        for i in range(4)
        for pair in (
            (s.own_blocks[2 * i], s.came[i]), (s.own_blocks[2 * i + 1], s.came_other[i])
        )
    ]
    blocks = [part for i in range(4) for part in s.finished[i][:2]]
    grad_in = rolled(back_to_rows(blocks, weights))
    x_unit = s.x_low.astype(full) * s.inverse_in
    s.gain_parts = jnp.concatenate(
        [
            jnp.sum(x_unit * grad_in, 0),
            s.mlp_gain_part,
            sum(s.backs[i][3] for i in range(4))[0],
            sum(s.finished[i][2] for i in range(4))[0],
        ]
    )
    s.grad_tokens = (
        s.grad_resid + norm_back(x_unit, s.inverse_in, grad_in * s.attn_gains)
    ).astype(low)
    del s.odd, s.out_near, s.out_far, s.out_head, s.out_tail, s.backs
    del s.own_blocks, s.came, s.came_other, s.grad_resid, s.x_low
    s.end()

    even = [s.finished[i][0] for i in range(4)]
    s.head0, s.tail0, s.head1, s.tail1 = in_order(
        [
            call(s.normed, even, s.qkv_came, half, range(half, 8, 2))
            for half in range(2)
            for call in (head_call, tail_call)
        ]
    )
    tokens_sent = from_sequences_send(
        lax.optimization_barrier((s.grad_tokens, s.tail1[0]))[0]
    )
    s.down_spread = jnp.concatenate([s.down_total, *s.down_near, *s.down_far], 0)
    s.down_spread_other = across(s.down_spread, CORE)
    s.output_second = output_sent[1]
    s.gate_up_far = far(*s.gate_up_near)
    del s.qkv_came, s.finished, s.down_total, s.down_near, s.down_far
    s.end()

    def qkv_chunks(came, came_far, head, tail):
        own = total(came, came_far, (head[2], tail[2]), by_columns)
        return jnp.split(own.astype(low), shards, 0)

    s.near0 = send_near((s.head0[0], s.tail0[0]))
    s.out_ring_last = around(rounded_sum(s.out_chunks[3], s.out_ring[0]), 1)
    s.tokens_first = tokens_sent[0]
    s.gain_came = across(s.gain_parts, CORE)
    s.end()

    s.far0 = send_far(s.near0, (s.tail0[1], s.head0[1]), by_columns)
    s.near1 = send_near((s.head1[0], s.tail1[0]))
    (s.whole_down,) = in_order([whole_call((units,), s.down_spread, s.down_spread_other)])
    first = lax.optimization_barrier((s.gate_up_total, s.whole_down[0]))[0]
    s.gate_up_own = jnp.concatenate([first, *s.gate_up_near, *s.gate_up_far], 0)
    s.out_total = rounded_sum(s.out_chunks[0], s.out_ring[1], s.out_ring_last)
    s.gain_parts = s.gain_parts + s.gain_came
    s.tokens_second = tokens_sent[1]
    del s.down_spread, s.down_spread_other, s.out_chunks, s.out_ring, s.out_ring_last
    del s.gate_up_near, s.gate_up_far, s.gate_up_total, s.grad_tokens
    s.end()

    s.chunks0 = qkv_chunks(s.near0, s.far0, s.head0, s.tail0)
    s.ring0 = ring_sum_first(s.chunks0)
    s.far1 = send_far(s.near1, (s.tail1[1], s.head1[1]), by_columns)
    s.gate_up_other = across(s.gate_up_own, CORE)
    del s.near0, s.far0, s.head0, s.tail0
    s.end()

    s.last0 = around(rounded_sum(s.chunks0[3], s.ring0[0]), 1)
    s.chunks1 = qkv_chunks(s.near1, s.far1, s.head1, s.tail1)
    s.ring1 = ring_sum_first(s.chunks1)
    s.gain_came = across(s.gain_parts, ACROSS_X)
    ((s.whole_gate,),) = in_order([whole_call((units,), s.gate_up_own, s.gate_up_other)])
    del s.near1, s.far1, s.head1, s.tail1
    s.end()

    query_total = rounded_sum(s.chunks0[0], s.ring0[1], s.last0)
    s.total0 = jnp.concatenate([query_total, s.out_total], 1)
    s.spread0 = near(s.total0)
    s.last1 = around(rounded_sum(s.chunks1[3], s.ring1[0]), 1)
    s.gain_parts = s.gain_parts + s.gain_came
    s.gain_came = across(s.gain_parts, ACROSS_Y)
    ((s.whole_up,),) = in_order([whole_call((units,), s.gate_up_own, s.gate_up_other, 1)])
    del s.gate_up_own, s.gate_up_other
    del s.chunks0, s.ring0, s.last0, s.out_total
    s.end()

    s.spread_far0 = far(*s.spread0)
    s.total1 = rounded_sum(s.chunks1[0], s.ring1[1], s.last1)
    s.spread1 = near(s.total1)
    s.gain_parts = s.gain_parts + s.gain_came
    s.gain_came = lax.ppermute(s.gain_parts, "shard", [(i, i ^ 1) for i in range(shards)])
    del s.chunks1, s.ring1, s.last1
    s.end()

    s.own0 = jnp.concatenate([s.total0, *s.spread0, *s.spread_far0], 0)
    s.other0 = across(s.own0, CORE)
    s.spread_far1 = far(*s.spread1)
    s.gain_parts = s.gain_parts + s.gain_came
    s.gain_came = lax.ppermute(s.gain_parts, "shard", [(i, i ^ 2) for i in range(shards)])
    del s.total0, s.spread0, s.spread_far0
    s.end()

    s.own1 = jnp.concatenate([s.total1, *s.spread1, *s.spread_far1], 0)
    s.other1 = across(s.own1, CORE)
    (s.whole0,) = in_order([whole_call((head_columns, head_columns), s.own0, s.other0)])
    gain_sums = s.gain_parts + s.gain_came
    s.wide = lax.dynamic_slice_in_dim(
        gain_sums[: 2 * width].reshape(2, width), shard_at * piece, piece, 1
    )
    s.narrow = gain_sums[2 * width :]
    del s.own0, s.other0, s.total1, s.spread1, s.spread_far1
    s.end()

    ((whole_key, whole_value),) = in_order(
        [whole_call((head_dim, head_dim), s.own1, s.other1)]
    )
    return (
        jnp.stack(in_turn([s.output_first, s.output_second])),
        jnp.stack(in_turn([s.tokens_first, s.tokens_second])),
        s.wide[0],
        s.whole0[0],
        whole_key,
        whole_value,
        s.narrow[:head_dim],
        s.narrow[head_dim:],
        s.whole0[1],
        s.wide[1],
        s.whole_gate,
        s.whole_up,
        *s.whole_down,
    )


def solution(mesh):
    sizes = (mesh.shape["rep"], mesh.shape["shard"])
    return jax.shard_map(
        on_device_block if sizes == (8, 4) else on_device,
        mesh=mesh,
        in_specs=(
            P("rep", "shard", None),
            P("rep"),
            P("shard"),
            P("shard", None),
            P("shard", None),
            P("shard", None),
            P(),
            P(),
            P("shard", None),
            P("shard"),
            P("shard", None),
            P("shard", None),
            P("shard", None),
            P("rep", "shard", None),
        ),
        out_specs=(
            P("rep", "shard", None),
            P("rep", "shard", None),
            P("shard"),
            P("shard", None),
            P("shard", None),
            P("shard", None),
            P(),
            P(),
            P("shard", None),
            P("shard"),
            P("shard", None),
            P("shard", None),
            P("shard", None),
        ),
        check_vma=False,
    )
```

```python
import jax
import jax.numpy as jnp
from jax import lax
from jax.experimental import pallas as pl
from jax.experimental.pallas import tpu as pltpu
from jax.sharding import PartitionSpec as P

WINDOW = 512


EPS = 1e-06
ROPE_BASE = 1000000.0
NEG = -1e30


def passed_along(x, axis, by):
    devices = lax.axis_size(axis)
    pairs = [(i, i + by) for i in range(devices) if 0 <= i + by < devices]
    return lax.ppermute(x, axis, pairs)


def tables(positions, head_dim):
    half = head_dim // 2
    freq = ROPE_BASE ** (-jnp.arange(half, dtype=jnp.float32) * 2.0 / head_dim)
    angle = positions.astype(jnp.float32)[:, None] * freq[None, :]
    angle = jnp.concatenate([angle, angle], -1)
    return (jnp.cos(angle)[None, :, None, :], jnp.sin(angle)[None, :, None, :])


def rotated_rows(value_rows):
    half = value_rows.shape[-1] // 2
    return jnp.concatenate([-value_rows[..., half:], value_rows[..., :half]], -1)


def head_norm(raw, gain):
    inverse = lax.rsqrt(jnp.mean(raw * raw, -1, keepdims=True) + EPS)
    unit = raw * inverse
    return (unit, inverse, unit * gain)


def norm_back(unit, inverse, grad_unit):
    return inverse * (grad_unit - unit * jnp.mean(grad_unit * unit, -1, keepdims=True))


def head_norm_back(unit, inverse, grad_normed, gain):
    grad_raw = norm_back(unit, inverse, grad_normed * gain)
    return (grad_raw, jnp.sum(unit * grad_normed, axis=(0, 1, 2)))


def scores(query_rows, keys, allowed, scale):
    raw = (
        jnp.einsum("sqhgd,skhd->shgqk", query_rows, keys, preferred_element_type=jnp.float32)
        * scale
    )
    return jnp.where(allowed[:, None, None], raw, NEG)


def outer(left, right):
    return jnp.einsum("rc,rf->cf", left, right, preferred_element_type=jnp.float32)


def on_device(
    tokens,
    lengths,
    attn_gain,
    w_query,
    key_matrix,
    value_matrix,
    query_gain,
    key_gain,
    w_out,
    mlp_gain,
    w_gate,
    w_up,
    w_down,
    cotangent,
):
    seq_count, piece, width = tokens.shape
    head_dim = query_gain.shape[0]
    heads_q = w_query.shape[1] // head_dim
    heads_kv = key_matrix.shape[1] // head_dim
    groups = heads_q // heads_kv
    rows = seq_count * piece
    scale = head_dim ** (-0.5)
    reach = (WINDOW + piece - 2) // piece
    owned = width // lax.axis_size("shard")
    shard_at = lax.axis_index("shard")
    query_pos = shard_at * piece + jnp.arange(piece, dtype=jnp.int32)
    key_pos = (shard_at - reach) * piece + jnp.arange((reach + 1) * piece, dtype=jnp.int32)
    near = (
        (key_pos[None, :] <= query_pos[:, None])
        & (query_pos[:, None] - key_pos[None, :] < WINDOW)
        & (key_pos[None, :] >= 0)
    )
    live = (key_pos[None, None, :] < lengths[:, None, None]) | (
        key_pos[None, :] == query_pos[:, None]
    )[None]
    allowed = near[None] & live
    valid = (query_pos[None, :] < lengths[:, None]).astype(jnp.float32).reshape(rows, 1)
    cosine_table, sine_table = tables(query_pos, head_dim)
    x_rows = tokens.astype(jnp.float32).reshape(rows, width)
    inverse_in = lax.rsqrt(jnp.mean(x_rows * x_rows, -1, keepdims=True) + EPS)
    x_unit = x_rows * inverse_in
    gain_piece = lax.all_gather(attn_gain, "shard", axis=0, tiled=True)
    query_piece = lax.all_gather(w_query, "shard", axis=0, tiled=True)
    key_piece = lax.all_gather(key_matrix, "shard", axis=0, tiled=True)
    value_piece = lax.all_gather(value_matrix, "shard", axis=0, tiled=True)
    normed_piece = (x_unit * gain_piece.astype(jnp.float32)).astype(jnp.bfloat16)
    acc_q = jnp.dot(normed_piece, query_piece, preferred_element_type=jnp.float32)
    acc_k = jnp.dot(normed_piece, key_piece, preferred_element_type=jnp.float32)
    acc_v = jnp.dot(normed_piece, value_piece, preferred_element_type=jnp.float32)
    normalized_rows = normed_piece
    gains = gain_piece.astype(jnp.float32)
    attn_in = normalized_rows
    attn_gains = gains
    query_unit, query_inverse, query_rows_normalized = head_norm(
        acc_q.reshape(seq_count, piece, heads_q, head_dim), query_gain.astype(jnp.float32)
    )
    key_unit, key_inverse, key_normed = head_norm(
        acc_k.reshape(seq_count, piece, heads_kv, head_dim), key_gain.astype(jnp.float32)
    )
    query_rows = (
        (query_rows_normalized * cosine_table + rotated_rows(query_rows_normalized) * sine_table)
        .astype(jnp.bfloat16)
        .reshape(seq_count, piece, heads_kv, groups, head_dim)
    )
    keys_own = (key_normed * cosine_table + rotated_rows(key_normed) * sine_table).astype(
        jnp.bfloat16
    )
    values_own = acc_v.reshape(seq_count, piece, heads_kv, head_dim).astype(jnp.bfloat16)
    own_pair = jnp.stack([keys_own, values_own])
    parts = []
    for fetch_back in range(reach, 0, -1):
        parts.append(passed_along(own_pair, "shard", fetch_back))
    parts.append(own_pair)
    near_pair = jnp.concatenate(parts, 2)
    score = scores(query_rows, near_pair[0], allowed, scale)
    top = jnp.max(score, -1, keepdims=True)
    expo = jnp.exp(score - top)
    total = jnp.sum(expo, -1, keepdims=True)
    prob = expo / total
    log_total = top + jnp.log(total)
    mixed = jnp.einsum(
        "shgqk,skhd->sqhgd",
        prob.astype(jnp.bfloat16),
        near_pair[1],
        preferred_element_type=jnp.float32,
    )
    mixed_rows = mixed.reshape(rows, heads_q * head_dim).astype(jnp.bfloat16)
    resid = x_rows + jnp.einsum(
        "rf,nf->rn",
        mixed_rows,
        lax.all_gather(w_out, "shard", axis=0, tiled=True),
        preferred_element_type=jnp.float32,
    )
    inverse_mid = lax.rsqrt(jnp.mean(resid * resid, -1, keepdims=True) + EPS)
    mid_unit = resid * inverse_mid
    gain_piece = lax.all_gather(mlp_gain, "shard", axis=0, tiled=True)
    gate_piece = lax.all_gather(w_gate, "shard", axis=0, tiled=True)
    up_piece = lax.all_gather(w_up, "shard", axis=0, tiled=True)
    normed_piece = (mid_unit * gain_piece.astype(jnp.float32)).astype(jnp.bfloat16)
    acc_gate = jnp.dot(normed_piece, gate_piece, preferred_element_type=jnp.float32)
    acc_up = jnp.dot(normed_piece, up_piece, preferred_element_type=jnp.float32)
    normalized_rows = normed_piece
    gains = gain_piece.astype(jnp.float32)
    mlp_in = normalized_rows
    sigma = jax.nn.sigmoid(acc_gate)
    swish = acc_gate * sigma
    act = (swish * acc_up).astype(jnp.bfloat16)
    mlp_out = jnp.einsum(
        "rf,nf->rn",
        act,
        lax.all_gather(w_down, "shard", axis=0, tiled=True),
        preferred_element_type=jnp.float32,
    )
    output = (valid * (resid + mlp_out)).astype(jnp.bfloat16).reshape(seq_count, piece, width)
    grad_y = cotangent.astype(jnp.float32).reshape(rows, width) * valid
    grad_y_low = grad_y.astype(jnp.bfloat16)
    grad_act = jnp.dot(
        grad_y_low,
        lax.all_gather(w_down, "shard", axis=0, tiled=True),
        preferred_element_type=jnp.float32,
    )
    grad_gate = (grad_act * acc_up * sigma * (1.0 + acc_gate * (1.0 - sigma))).astype(jnp.bfloat16)
    grad_up = (grad_act * swish).astype(jnp.bfloat16)
    gate_piece, up_piece = lax.all_gather((w_gate, w_up), "shard", axis=0, tiled=True)
    grad_mid = jnp.einsum(
        "rf,nf->rn", grad_gate, gate_piece, preferred_element_type=jnp.float32
    ) + jnp.einsum("rf,nf->rn", grad_up, up_piece, preferred_element_type=jnp.float32)
    grad_resid = grad_y + norm_back(mid_unit, inverse_mid, grad_mid * gains)
    mlp_gain_part = jnp.sum(mid_unit * grad_mid, 0)
    normalized_rows = mlp_in
    mlp_grads = jax.tree.map(
        lambda part: lax.psum_scatter(
            part.astype(jnp.bfloat16), "shard", scatter_dimension=0, tiled=True
        ).astype(jnp.float32),
        (
            outer(normalized_rows, grad_gate),
            outer(normalized_rows, grad_up),
            outer(grad_y_low, act),
        ),
    )
    resid_low = grad_resid.astype(jnp.bfloat16)
    grad_mixed = jnp.dot(
        resid_low,
        lax.all_gather(w_out, "shard", axis=0, tiled=True),
        preferred_element_type=jnp.float32,
    )
    grad_mixed = grad_mixed.astype(jnp.bfloat16).reshape(
        seq_count, piece, heads_kv, groups, head_dim
    )
    prob_again = jnp.exp(scores(query_rows, near_pair[0], allowed, scale) - log_total)
    grad_prob = jnp.einsum(
        "sqhgd,skhd->shgqk", grad_mixed, near_pair[1], preferred_element_type=jnp.float32
    )
    grad_values = jnp.einsum(
        "shgqk,sqhgd->skhd",
        prob_again.astype(jnp.bfloat16),
        grad_mixed,
        preferred_element_type=jnp.float32,
    )
    grad_score = (
        prob_again * (grad_prob - jnp.sum(prob_again * grad_prob, -1, keepdims=True))
    ).astype(jnp.bfloat16)
    grad_queries = (
        jnp.einsum(
            "shgqk,skhd->sqhgd", grad_score, near_pair[0], preferred_element_type=jnp.float32
        )
        * scale
    )
    grad_keys = (
        jnp.einsum("shgqk,sqhgd->skhd", grad_score, query_rows, preferred_element_type=jnp.float32)
        * scale
    )
    grad_pair = jnp.stack([grad_keys, grad_values])
    own_grad = grad_pair[:, :, reach * piece :]
    for back in range(1, reach + 1):
        lower = (reach - back) * piece
        own_grad = own_grad + passed_along(grad_pair[:, :, lower : lower + piece], "shard", -back)
    grad_query_post = grad_queries.reshape(seq_count, piece, heads_q, head_dim)
    grad_query_normed = grad_query_post * cosine_table - rotated_rows(grad_query_post * sine_table)
    grad_key_normed = own_grad[0] * cosine_table - rotated_rows(own_grad[0] * sine_table)
    grad_query_raw, query_gain_grad = head_norm_back(
        query_unit, query_inverse, grad_query_normed, query_gain.astype(jnp.float32)
    )
    grad_key_raw, key_gain_grad = head_norm_back(
        key_unit, key_inverse, grad_key_normed, key_gain.astype(jnp.float32)
    )
    grad_query_low = grad_query_raw.reshape(rows, heads_q * head_dim).astype(jnp.bfloat16)
    grad_key_low = grad_key_raw.reshape(rows, heads_kv * head_dim).astype(jnp.bfloat16)
    grad_value_low = own_grad[1].reshape(rows, heads_kv * head_dim).astype(jnp.bfloat16)
    query_piece, key_piece, value_piece = lax.all_gather(
        (w_query, key_matrix, value_matrix), "shard", axis=0, tiled=True
    )
    grad_in = (
        jnp.einsum("rf,nf->rn", grad_query_low, query_piece, preferred_element_type=jnp.float32)
        + jnp.einsum("rf,nf->rn", grad_key_low, key_piece, preferred_element_type=jnp.float32)
        + jnp.einsum("rf,nf->rn", grad_value_low, value_piece, preferred_element_type=jnp.float32)
    )
    grad_tokens = (
        (grad_resid + norm_back(x_unit, inverse_in, grad_in * attn_gains))
        .astype(jnp.bfloat16)
        .reshape(seq_count, piece, width)
    )
    attn_gain_part = jnp.sum(x_unit * grad_in, 0)
    normalized_rows = attn_in
    attn_grads = jax.tree.map(
        lambda part: lax.psum_scatter(
            part.astype(jnp.bfloat16), "shard", scatter_dimension=0, tiled=True
        ).astype(jnp.float32),
        (
            outer(normalized_rows, grad_query_low),
            outer(normalized_rows, grad_key_low),
            outer(normalized_rows, grad_value_low),
            outer(resid_low, mixed_rows),
        ),
    )
    head_grads = lax.psum(
        (query_gain_grad, key_gain_grad, attn_gain_part, mlp_gain_part), ("rep", "shard")
    )
    attn_gain_total = lax.dynamic_slice_in_dim(head_grads[2], shard_at * owned, owned, 0)
    mlp_gain_total = lax.dynamic_slice_in_dim(head_grads[3], shard_at * owned, owned, 0)
    summed = (
        lax.psum(attn_grads[0].astype(jnp.bfloat16), "rep").astype(jnp.float32),
        lax.psum(attn_grads[1].astype(jnp.bfloat16), "rep").astype(jnp.float32),
        lax.psum(attn_grads[2].astype(jnp.bfloat16), "rep").astype(jnp.float32),
        lax.psum(attn_grads[3].astype(jnp.bfloat16), "rep").astype(jnp.float32),
        lax.psum(mlp_grads[0].astype(jnp.bfloat16), "rep").astype(jnp.float32),
        lax.psum(mlp_grads[1].astype(jnp.bfloat16), "rep").astype(jnp.float32),
        lax.psum(mlp_grads[2].astype(jnp.bfloat16), "rep").astype(jnp.float32),
    )
    attn_grads = summed[:4]
    mlp_grads = summed[4:]
    return (
        output,
        grad_tokens,
        attn_gain_total,
        attn_grads[0],
        attn_grads[1],
        attn_grads[2],
        head_grads[0],
        head_grads[1],
        attn_grads[3],
        mlp_gain_total,
        mlp_grads[0],
        mlp_grads[1],
        mlp_grads[2],
    )


CORE, ACROSS_X, ACROSS_Y = 1, 2, 4
VMEM_BYTES = 56 * 2**20
FREE = pl.CostEstimate(flops=1, bytes_accessed=1, transcendentals=0)


def across(x, mask):
    count = lax.axis_size("rep")
    return lax.ppermute(x, "rep", [(i, i ^ mask) for i in range(count)])


def around(x, by):
    count = lax.axis_size("shard")
    return lax.ppermute(x, "shard", [(i, (i + by) % count) for i in range(count)])


class Stage(dict):
    __getattr__ = dict.__getitem__
    __setattr__ = dict.__setitem__
    __delattr__ = dict.__delitem__

    def end(self):
        self.update(lax.optimization_barrier(dict(self)))


def in_order(calls):
    outs = []
    for call, first, *rest in calls:
        if outs:
            last = outs[-1][0] if isinstance(outs[-1], (list, tuple)) else outs[-1]
            first = lax.optimization_barrier((first, last))[0]
        outs.append(call(first, *rest))
    return outs


def ring_sum_first(chunks):
    return around(chunks[2], 1), around(chunks[1], -1)


def near(piece):
    return across(piece, ACROSS_X), across(piece, ACROSS_Y)


def far(from_x, from_y):
    half = from_x.shape[0] // 2
    return across(from_x[:half], ACROSS_Y), across(from_y[half:], ACROSS_X)


def rounded_sum(*parts):
    return sum(part.astype(jnp.float32) for part in parts).astype(jnp.bfloat16)


def sequence_pairs(turn):
    groups, shards = lax.axis_size("rep"), lax.axis_size("shard")
    pairs = []
    for group in range(groups):
        chip, core = divmod(group, 2)
        for at in range(shards):
            to_group, to_shard = 2 * chip + at // 2, 2 * core + (turn ^ (at & 1))
            pairs.append((group * shards + at, to_group * shards + to_shard))
    return pairs


def rolled(x):
    count, at = lax.axis_size("shard"), lax.axis_index("shard")
    width = x.shape[1] // count
    return jnp.concatenate(
        [lax.dynamic_slice_in_dim(x, ((at - i) % count) * width, width, 1) for i in range(count)],
        1,
    )


def sequence_cuts(x):
    odd = lax.axis_index("shard") & 1
    return [lax.dynamic_index_in_dim(x, turn ^ odd, 0, keepdims=False) for turn in range(2)]


def to_sequence(cut, turn):
    return lax.ppermute(cut, ("rep", "shard"), sequence_pairs(turn))


def from_sequences_send(x):
    odd = lax.axis_index("shard") & 1
    x = x.reshape(2, x.shape[0] // 2, x.shape[1])
    return [
        lax.ppermute(
            lax.dynamic_index_in_dim(x, turn ^ odd, 0, keepdims=False),
            ("rep", "shard"),
            [(to, at) for at, to in sequence_pairs(turn)],
        )
        for turn in range(2)
    ]


def in_turn(came):
    even = lax.axis_index("shard") & 1 == 0
    return [jnp.where(even, came[0], came[1]), jnp.where(even, came[1], came[0])]


def column_block(weights, at):
    cuts = [w.shape[1] // 8 for w in weights]
    return jnp.concatenate(
        [lax.dynamic_slice_in_dim(w, at * cut, cut, 1) for w, cut in zip(weights, cuts)], 1
    )


def whole_columns(me, own, other, widths, part=0):
    rows, columns = own.shape[0] // 4, sum(widths)

    def body(me_ref, own_ref, other_ref, *outs):
        def put(blocks):
            start = 0
            for out, width in zip(outs, widths):
                for at, block in enumerate(blocks):
                    out[:, at * width : (at + 1) * width] = block[
                        :, start : start + width
                    ].astype(jnp.float32)
                start += width

        even = me_ref[0] & 1 == 0
        pl.when(even)(lambda: put((own_ref, other_ref)))
        pl.when(jnp.logical_not(even))(lambda: put((other_ref, own_ref)))

    spec = pl.BlockSpec((rows, columns), lambda i, at: ((at[0] >> 1) ^ i, part))
    return pl.pallas_call(
        body,
        grid_spec=pltpu.PrefetchScalarGridSpec(
            num_scalar_prefetch=1,
            grid=(4,),
            in_specs=[spec, spec],
            out_specs=[pl.BlockSpec((rows, 2 * w), lambda i, at: (0, i)) for w in widths],
        ),
        out_shape=[jax.ShapeDtypeStruct((rows, 8 * w), jnp.float32) for w in widths],
        compiler_params=pltpu.CompilerParams(vmem_limit_bytes=VMEM_BYTES),
        cost_estimate=FREE,
        name="whole_columns",
    )(me, own, other)


def turned(x):
    return pltpu.roll(x, x.shape[-1] // 2, x.ndim - 1)


def nt(left, right):
    return lax.dot_general(
        left, right, (((1,), (1,)), ((), ())), preferred_element_type=jnp.float32
    )


def tn(left, right):
    return lax.dot_general(
        left, right, (((0,), (0,)), ((), ())), preferred_element_type=jnp.float32
    )


def unit_of(raw):
    inverse = lax.rsqrt(jnp.mean(raw * raw, -1, keepdims=True) + EPS)
    return raw * inverse, inverse


def project_body(
    normed, own0, came0, own1, came1, cosine, sine, gains, raw, query, key_value
):
    step = own0.shape[0]
    dim = cosine.shape[1]
    for block, (own, came) in enumerate(((own0, came0), (own1, came1))):
        at = block * 4 * dim
        raw[:, at : at + 4 * dim] = jnp.dot(
            normed[:, :step], own[...], preferred_element_type=jnp.float32
        ) + jnp.dot(normed[:, step:], came[...], preferred_element_type=jnp.float32)
        for i in range(3):
            unit, _ = unit_of(raw[:, at + i * dim : at + (i + 1) * dim])
            head = unit * gains[i // 2 : i // 2 + 1, :]
            head = (head * cosine[...] + turned(head) * sine[...]).astype(jnp.bfloat16)
            if i < 2:
                query[:, (2 * block + i) * dim : (2 * block + i + 1) * dim] = head
            else:
                key_value[:, 2 * block * dim : (2 * block + 1) * dim] = head
        key_value[:, (2 * block + 1) * dim : (2 * block + 2) * dim] = raw[
            :, at + 3 * dim : at + 4 * dim
        ].astype(jnp.bfloat16)


def window_mask(info, part, rows, columns):
    half = columns - rows
    row = lax.broadcasted_iota(jnp.int32, (rows, columns), 0)
    column = lax.broadcasted_iota(jnp.int32, (rows, columns), 1)
    gap = column - row - half
    slot = column + ((info[0] - 1) * half + part * rows)
    allowed = (gap <= 0) & (gap > -half) & (slot >= 0) & ((slot < info[1]) | (gap == 0))
    mask = jnp.where(allowed, 0.0, NEG)
    return jnp.concatenate([mask, mask], 0)


def two_heads(ref, at, block, dim):
    return jnp.concatenate(
        [ref[at, h * dim : (h + 1) * dim] for h in (2 * block, 2 * block + 1)], 0
    )


def key_columns(block, dim):
    key = slice(2 * block * dim, (2 * block + 1) * dim)
    value = slice((2 * block + 1) * dim, (2 * block + 2) * dim)
    return key, value


def seen_pair(before, own, part, block, dim):
    here, there = key_columns(block, dim), key_columns(1 - block, dim)
    rows = own.shape[0] // 2
    if part == 0:
        return [
            jnp.concatenate([before[:, t], own[:rows, h]], 0) for h, t in zip(here, there)
        ]
    return [jnp.concatenate([before[rows:, t], own[:, h]], 0) for h, t in zip(here, there)]


def attend_body(info, query, before, own, mixed, log_total):
    dim = own.shape[1] // 4
    rows = query.shape[0] // 2
    for part in range(2):
        at = slice(part * rows, (part + 1) * rows)
        mask = window_mask(info, part, rows, 3 * rows)
        for block in range(2):
            keys, values = seen_pair(before, own, part, block, dim)
            score = nt(two_heads(query, at, block, dim), keys) * dim**-0.5 + mask
            top = jnp.max(score, -1, keepdims=True)
            expo = jnp.exp(score - top)
            total = jnp.sum(expo, -1, keepdims=True)
            prob = (expo * (1.0 / total)).astype(jnp.bfloat16)
            out = jnp.dot(prob, values, preferred_element_type=jnp.float32).astype(jnp.bfloat16)
            log = jnp.broadcast_to(top + jnp.log(total), (2 * rows, dim))
            for i in range(2):
                on = slice((2 * block + i) * dim, (2 * block + i + 1) * dim)
                mixed[at, on] = out[i * rows : (i + 1) * rows]
                log_total[at, on] = log[i * rows : (i + 1) * rows]


def attend_back_body(
    info, query, before, own, log_total, grad_resid, weight0, weight1, raw, cosine, sine, gain,
    grad_query, grad_own, grad_before, gain_part, grad_keys, grad_values, grad_mixed,
):
    dim = own.shape[1] // 4
    rows = query.shape[0] // 2
    scale = dim**-0.5
    gain_total = jnp.zeros((1, dim), jnp.float32)
    masks = [window_mask(info, part, rows, 3 * rows) for part in range(2)]
    for block, weight in enumerate((weight0, weight1)):
        on = slice(2 * block * dim, 2 * (block + 1) * dim)
        grad_mixed[:, on] = jnp.dot(
            grad_resid[...], weight[...], preferred_element_type=jnp.float32
        ).astype(jnp.bfloat16)
        grad_keys[...] = jnp.zeros_like(grad_keys)
        grad_values[...] = jnp.zeros_like(grad_values)
        for part in range(2):
            keys, values = seen_pair(before, own, part, block, dim)
            at = slice(part * rows, (part + 1) * rows)
            seen = slice(part * rows, part * rows + 3 * rows)
            queries = two_heads(query, at, block, dim)
            grads = two_heads(grad_mixed, at, block, dim)
            log = two_heads(log_total, at, block, dim)[:, :1]
            prob = jnp.exp(nt(queries, keys) * scale + masks[part] - log)
            grad_prob = nt(grads, values)
            inner = jnp.sum(prob * grad_prob, -1, keepdims=True)
            grad_score = (prob * (grad_prob - inner)).astype(jnp.bfloat16)
            grad_values[seen, :] += tn(prob.astype(jnp.bfloat16), grads)
            grad_keys[seen, :] += tn(grad_score, queries) * scale
            both = jnp.dot(grad_score, keys, preferred_element_type=jnp.float32) * scale
            for i in range(2):
                head = 2 * block + i
                back = both[i * rows : (i + 1) * rows]
                back = back * cosine[at, :] - turned(back) * sine[at, :]
                there = (2 * head - head % 2) * dim
                unit, inverse = unit_of(raw[at, there : there + dim])
                gain_total += jnp.sum(unit * back, 0, keepdims=True)
                back = back * gain[...]
                back = inverse * (back - unit * jnp.mean(back * unit, -1, keepdims=True))
                grad_query[at, head * dim : (head + 1) * dim] = back.astype(jnp.bfloat16)
        for grad, here, there in zip(
            (grad_keys, grad_values), key_columns(block, dim), key_columns(1 - block, dim)
        ):
            grad_before[:, there] = grad[: 2 * rows, :].astype(jnp.bfloat16)
            grad_own[:, here] = grad[2 * rows :, :]
    gain_part[...] = gain_total


def finish_body(grad_query, grad_own, came, raw, cosine, sine, gain, even, odd, gain_part):
    dim = cosine.shape[1]
    total = jnp.zeros((1, dim), jnp.float32)
    for block, out in enumerate((even, odd)):
        key, value = key_columns(block, dim)
        back = grad_own[:, key] + came[:, key].astype(jnp.float32)
        back = back * cosine[...] - turned(back) * sine[...]
        unit, inverse = unit_of(raw[:, (4 * block + 2) * dim : (4 * block + 3) * dim])
        total += jnp.sum(unit * back, 0, keepdims=True)
        back = back * gain[...]
        back = inverse * (back - unit * jnp.mean(back * unit, -1, keepdims=True))
        out[:, : 2 * dim] = grad_query[:, 2 * block * dim : (2 * block + 2) * dim]
        out[:, 2 * dim : 3 * dim] = back.astype(jnp.bfloat16)
        grad_value = grad_own[:, value] + came[:, value].astype(jnp.float32)
        out[:, 3 * dim :] = grad_value.astype(jnp.bfloat16)
    gain_part[...] = total


def vmem_call(body, outs, scratch=(), scalars=0, name=None):
    def call(*args):
        in_specs = [
            pl.BlockSpec(memory_space=pltpu.SMEM if i < scalars else pltpu.VMEM)
            for i in range(len(args))
        ]
        return pl.pallas_call(
            body,
            grid=(1,),
            out_shape=outs,
            in_specs=in_specs,
            out_specs=jax.tree.map(lambda _: pl.BlockSpec(memory_space=pltpu.VMEM), outs),
            scratch_shapes=scratch,
            compiler_params=pltpu.CompilerParams(vmem_limit_bytes=VMEM_BYTES),
        cost_estimate=FREE,
            name=name,
        )(*args)

    return call


def hidden_units(mids, grads_y, weights):
    width, units = weights.shape[0], weights.shape[1] // 3
    count = len(mids)
    heights = [m.shape[0] for m in mids]
    rows, cut = sum(heights), units // 3

    def body(*refs):
        gate_w, up_w, w_down, act, grad_gate, grad_up = refs[2 * count :]
        start = 0
        for mid, grad_y in zip(refs[:count], refs[count : 2 * count]):
            at = slice(start, start + mid.shape[0])
            start += mid.shape[0]
            gate = jnp.dot(mid[...], gate_w[...], preferred_element_type=jnp.float32)
            up = jnp.dot(mid[...], up_w[...], preferred_element_type=jnp.float32)
            grad_act = jnp.dot(grad_y[...], w_down[...], preferred_element_type=jnp.float32)
            sigma = jax.nn.sigmoid(gate)
            swish = gate * sigma
            act[at, :] = (swish * up).astype(jnp.bfloat16)
            slope = grad_act * up * sigma * (1.0 + gate * (1.0 - sigma))
            grad_gate[at, :] = slope.astype(jnp.bfloat16)
            grad_up[at, :] = (grad_act * swish).astype(jnp.bfloat16)

    row_specs = [
        pl.BlockSpec((h, width), lambda j: (0, 0), pipeline_mode=pl.Buffered(1)) for h in heights
    ]
    return pl.pallas_call(
        body,
        grid=(3,),
        out_shape=[jax.ShapeDtypeStruct((rows, units), jnp.bfloat16)] * 3,
        in_specs=[
            *row_specs,
            *row_specs,
            pl.BlockSpec((width, cut), lambda j: (0, j)),
            pl.BlockSpec((width, cut), lambda j: (0, j + 3)),
            pl.BlockSpec((width, cut), lambda j: (0, j + 6)),
        ],
        out_specs=[pl.BlockSpec((rows, cut), lambda j: (0, j))] * 3,
        compiler_params=pltpu.CompilerParams(vmem_limit_bytes=VMEM_BYTES),
        cost_estimate=FREE,
        name="hidden_units",
    )(*mids, *grads_y, weights, weights, weights)


def from_hidden(pairs, eighths):
    count, parts = len(pairs), len(eighths)
    rows, units = pairs[0][0].shape[0] // 8, pairs[0][0].shape[1]
    width = pairs[0][1].shape[0]
    cut = width // 4

    def body(*refs):
        ins, outs = refs[: -(parts // 2)], refs[-(parts // 2) :]
        total = 0.0
        for i in range(count):
            part = ins[i * (parts + 1) : (i + 1) * (parts + 1)]
            left = jnp.concatenate([p[...] for p in part[:-1]], 0)
            total = total + nt(left, part[-1][...])
        for i, out in enumerate(outs):
            out[...] = total[2 * i * rows : 2 * (i + 1) * rows].astype(jnp.bfloat16)

    specs, args = [], []
    for left, right, at in pairs:
        specs += [pl.BlockSpec((rows, units), lambda j, e=e: (e, 0)) for e in eighths]
        specs.append(pl.BlockSpec((cut, units), lambda j, at=at: (j, at)))
        args += [left] * parts + [right]
    return pl.pallas_call(
        body,
        grid=(4,),
        out_shape=[jax.ShapeDtypeStruct((2 * rows, width), jnp.bfloat16)] * (parts // 2),
        in_specs=specs,
        out_specs=[pl.BlockSpec((2 * rows, cut), lambda j: (0, j))] * (parts // 2),
        compiler_params=pltpu.CompilerParams(vmem_limit_bytes=VMEM_BYTES),
        cost_estimate=FREE,
        name="from_hidden",
    )(*args)


def row_outer(lefts, groups, first, tiles, added=None, places=None, part=None):
    rights = [right for group in groups for right in group]
    places = range(len(rights)) if places is None else places
    added = [] if added is None else [added] * len(rights)
    width = lefts[0].shape[1]
    tile = width // 8
    count = len(lefts)
    rows = sum(left.shape[0] for left in lefts)
    wide = rights[0].shape[1] // (1 if part is None else 2)
    columns = [wide * len(group) for group in groups]

    def body(*refs):
        left_refs = refs[:count]
        right_refs = refs[count : count + len(rights)]
        add_refs = refs[count + len(rights) : count + len(rights) + len(added)]
        outs = refs[count + len(rights) + len(added) :]
        place = 0
        for i, group in enumerate(groups):
            column = 0
            for _ in group:
                on = slice(column, column + wide)
                total, start = 0.0, 0
                for left in left_refs:
                    stop = start + left.shape[0]
                    total = total + tn(left[...], right_refs[place][start:stop, :])
                    start = stop
                if added:
                    total = total + add_refs[place][...].astype(jnp.float32)
                outs[i][:, on] = total.astype(jnp.bfloat16)
                place += 1
                column += wide

    return pl.pallas_call(
        body,
        grid=(tiles,),
        out_shape=[jax.ShapeDtypeStruct((tiles * tile, c), jnp.bfloat16) for c in columns],
        in_specs=[
            *(pl.BlockSpec((left.shape[0], tile), lambda j: (0, j + first)) for left in lefts),
            *(
                pl.BlockSpec(
                    (right.shape[0], wide), lambda j: (0, part or 0), pipeline_mode=pl.Buffered(1)
                )
                for right in rights
            ),
            *(
                pl.BlockSpec((tile, wide), lambda j, at=at: (j + first, at))
                for at in places[: len(added)]
            ),
        ],
        out_specs=[pl.BlockSpec((tile, c), lambda j: (j, 0)) for c in columns],
        compiler_params=pltpu.CompilerParams(vmem_limit_bytes=VMEM_BYTES),
        cost_estimate=pl.CostEstimate(
            flops=2 * rows * tiles * tile * sum(columns),
            bytes_accessed=2 * rows * (width + sum(columns)),
            transcendentals=0,
        ),
        name="row_outer",
    )(*lefts, *rights, *added)


def close_body(x, *refs):
    mixed, weights = refs[:4], refs[4:12]
    gains, resid, mid = refs[12:]
    at = pl.program_id(0)
    step = x.shape[1]
    columns = weights[0].shape[1]
    total = x[...].astype(jnp.float32)
    for i in range(8):
        part = mixed[i // 2][:, (i % 2) * columns : (i % 2 + 1) * columns]
        total = total + nt(part, weights[i][...])
    resid[:, pl.ds(pl.multiple_of(at * step, step), step)] = total

    @pl.when(at == 3)
    def _():
        unit, _ = unit_of(resid[...])
        mid[...] = (unit * gains[...]).astype(jnp.bfloat16)


def close_attention(x, mixed, weights, gains):
    rows, width = x.shape
    step = width // 4
    whole = lambda a: pl.BlockSpec(a.shape, lambda j: (0, 0))
    return pl.pallas_call(
        close_body,
        grid=(4,),
        out_shape=[
            jax.ShapeDtypeStruct((rows, width), jnp.float32),
            jax.ShapeDtypeStruct((rows, width), jnp.bfloat16),
        ],
        in_specs=[
            pl.BlockSpec((rows, step), lambda j: (0, j)),
            *(whole(m) for m in mixed),
            *(pl.BlockSpec((step, w.shape[1]), lambda j: (j, 0)) for w in weights),
            whole(gains),
        ],
        out_specs=[pl.BlockSpec((rows, width), lambda j: (0, 0))] * 2,
        compiler_params=pltpu.CompilerParams(vmem_limit_bytes=VMEM_BYTES),
        cost_estimate=FREE,
        name="close_attention",
    )(x, *mixed, *weights, gains)


def back_to_rows(blocks, weights):
    rows = blocks[0].shape[0]
    step, columns = weights[0][0].shape
    count = len(blocks)

    def body(*refs):
        lefts = refs[:count]
        hbm = refs[count : 3 * count]
        out = refs[3 * count]
        held, sems = refs[3 * count + 1 :]
        copies = []
        for i in range(count):
            own, came = hbm[2 * i : 2 * i + 2]
            copies.append(
                [
                    pltpu.make_async_copy(own, held.at[i, :step], sems.at[i, 0]),
                    pltpu.make_async_copy(came, held.at[i, step:], sems.at[i, 1]),
                ]
            )
        for some in copies:
            for copy in some:
                copy.start()
        for i in range(count):
            for copy in copies[i]:
                copy.wait()
            for k in range(4):
                on = slice(k * step, (k + 1) * step)
                part = nt(lefts[i][...], held[i, on])
                if i == 0:
                    out[:, on] = part
                else:
                    out[:, on] += part

    return pl.pallas_call(
        body,
        grid=(1,),
        out_shape=jax.ShapeDtypeStruct((rows, 4 * step), jnp.float32),
        in_specs=[pl.BlockSpec(memory_space=pltpu.VMEM)] * count
        + [pl.BlockSpec(memory_space=pl.ANY)] * (2 * count),
        out_specs=pl.BlockSpec(memory_space=pltpu.VMEM),
        scratch_shapes=[
            pltpu.VMEM((count, 4 * step, columns), jnp.bfloat16),
            pltpu.SemaphoreType.DMA((count, 2)),
        ],
        compiler_params=pltpu.CompilerParams(vmem_limit_bytes=VMEM_BYTES),
        cost_estimate=FREE,
        name="back_to_rows",
    )(*blocks, *(part for w in weights for part in w))


def on_device_block(
    tokens,
    lengths,
    attn_gain,
    w_query,
    key_matrix,
    value_matrix,
    query_gain,
    key_gain,
    w_out,
    mlp_gain,
    w_gate,
    w_up,
    w_down,
    cotangent,
):
    low, full = jnp.bfloat16, jnp.float32
    width = tokens.shape[2]
    head_dim = query_gain.shape[0]
    shards = lax.axis_size("shard")
    shard_at = lax.axis_index("shard")
    me = lax.axis_index("rep")
    core = me & 1
    count = lax.axis_size("rep")

    s = Stage()
    s.cotangent = cotangent
    piece = width // shards

    s.own_blocks = [
        column_block((w_query, key_matrix, value_matrix), me ^ i) for i in range(8)
    ]
    gain_rows = jnp.concatenate(
        [jnp.stack([attn_gain, mlp_gain]), jnp.zeros((14, piece), low)], 0
    )
    travelling = jnp.concatenate([s.own_blocks[0], gain_rows], 0)
    s.tokens = tokens
    s.out_block = column_block((w_out,), me)
    s.ffn_block = column_block((w_gate, w_up, w_down), me)
    s.before, s.behind = around(travelling, 1), around(travelling, -1)
    s.other_lengths = across(lengths, CORE)
    s.end()

    s.ahead = around(s.before, 1)
    tokens_sent = [to_sequence(cut, turn) for turn, cut in enumerate(sequence_cuts(s.tokens))]
    out_own = lax.all_gather(s.out_block, "shard", axis=0, tiled=True)
    del s.out_block, s.tokens
    s.end()

    parts = (s.before, s.ahead, s.behind)
    s.came = jnp.concatenate([part[:piece] for part in parts], 0)
    s.gains = jnp.concatenate([gain_rows[:2], *(part[piece : piece + 2] for part in parts)], 1)
    s.came_near = near(s.came)
    s.came_own = across(s.came, CORE)
    s.x_came = tokens_sent
    del s.before, s.behind, s.ahead
    s.end()

    grad_y_sent = [
        to_sequence(cut, turn) for turn, cut in enumerate(sequence_cuts(s.cotangent))
    ]
    s.came_far = far(*s.came_near)
    s.came_other = [s.came_own, *(across(block, CORE) for block in s.came_near)]
    gains = rolled(s.gains.astype(full))
    s.mlp_gains = gains[1:]
    s.attn_gains = gains[:1]
    s.x_low = jnp.concatenate(in_turn(s.x_came), 0)
    rows = s.x_low.shape[0]
    x_rows = s.x_low.astype(full)
    s.inverse_in = lax.rsqrt(jnp.mean(x_rows * x_rows, -1, keepdims=True) + EPS)
    s.normed = rolled((x_rows * s.inverse_in * s.attn_gains).astype(low))
    query_gains = query_gain.astype(full)[None]
    key_gains = key_gain.astype(full)[None]
    s.head_gains = jnp.concatenate([query_gains, key_gains], 0)
    both = jnp.where(
        core == 0,
        jnp.concatenate([lengths, s.other_lengths]),
        jnp.concatenate([s.other_lengths, lengths]),
    )
    length = lax.dynamic_index_in_dim(both, shard_at, 0, keepdims=False)
    s.info = jnp.stack([core, length]).astype(jnp.int32)
    query_pos = core * rows + jnp.arange(rows, dtype=jnp.int32)
    s.valid = (query_pos < length)[:, None].astype(full)
    cosine, sine = tables(query_pos, head_dim)
    s.cosine, sine = cosine[0, :, 0], sine[0, :, 0]
    s.sine = jnp.concatenate([-sine[:, : head_dim // 2], sine[:, head_dim // 2 :]], 1)
    s.out_own = out_own
    del s.gains, s.x_came, s.other_lengths, s.cotangent, s.came_own
    s.end()

    head_columns = 2 * head_dim
    block_columns = 4 * head_dim
    quad_rows = jax.ShapeDtypeStruct((rows, block_columns), low)
    quad_sums = jax.ShapeDtypeStruct((rows, block_columns), full)
    gain_sum = jax.ShapeDtypeStruct((1, head_dim), full)
    project = vmem_call(
        project_body,
        [jax.ShapeDtypeStruct((rows, 2 * block_columns), full), quad_rows, quad_rows],
        name="project",
    )
    attend = vmem_call(attend_body, [quad_rows, quad_sums], scalars=1, name="attend")
    attend_back = vmem_call(
        attend_back_body,
        [quad_rows, quad_sums, quad_rows, gain_sum],
        scratch=[pltpu.VMEM((2 * rows, head_dim), full)] * 2
        + [pltpu.VMEM((rows, block_columns), low)],
        scalars=1,
        name="attend_back",
    )
    finish = vmem_call(finish_body, [quad_rows, quad_rows, gain_sum], name="finish")
    upward = [(i, i + 1) for i in range(0, count, 2)]
    downward = [(i + 1, i) for i in range(0, count, 2)]

    def project_call(i, came, other):
        return (
            project, s.normed, s.own_blocks[2 * i], came, s.own_blocks[2 * i + 1], other,
            s.cosine, s.sine, s.head_gains,
        )

    def attend_call(projected, earlier):
        return (
            lambda query, own, before: attend(s.info, query, before, own),
            *projected[1:], earlier,
        )

    came_last = jnp.concatenate(s.came_far, 0)
    s.came_last = (came_last, across(came_last, CORE))
    s.out_near = near(s.out_own)
    s.out_own_other = across(s.out_own, CORE)
    s.projected = in_order(
        [
            project_call(i, block, other)
            for i, (block, other) in enumerate(zip((s.came, *s.came_near), s.came_other))
        ]
    )
    s.grad_y_came = grad_y_sent
    del s.came_far
    s.end()

    ffn_own = lax.all_gather(s.ffn_block, "shard", axis=0, tiled=True)
    grad_y = jnp.concatenate(in_turn(s.grad_y_came), 0)
    s.grad_y = jnp.where(s.valid > 0, grad_y, jnp.zeros_like(grad_y))
    grad_y_near = near(s.grad_y)
    s.out_far = far(*s.out_near)
    s.out_near_other = [across(block, CORE) for block in s.out_near]
    s.earlier = [lax.ppermute(p[2], "rep", upward) for p in s.projected]
    (s.projected_last,) = in_order([project_call(3, *s.came_last)])
    del s.ffn_block, s.grad_y_came
    s.end()

    out_last = jnp.concatenate(s.out_far, 0)
    s.out_last = (out_last, across(out_last, CORE))
    s.earlier_last = lax.ppermute(s.projected_last[2], "rep", upward)
    s.attended = in_order([attend_call(*pair) for pair in zip(s.projected, s.earlier)])
    s.grad_y_near = grad_y_near
    del s.out_far
    s.end()

    s.projected = [*s.projected, s.projected_last]
    s.earlier = [*s.earlier, s.earlier_last]
    s.out_blocks = [
        s.out_own, s.out_own_other, s.out_near[0], s.out_near_other[0], s.out_near[1],
        s.out_near_other[1], *s.out_last,
    ]
    (last,) = in_order([attend_call(s.projected_last, s.earlier_last)])
    s.attended = [*s.attended, last]
    s.mixed = [a[0] for a in s.attended]
    s.resid, s.mid = close_attention(s.x_low, s.mixed, s.out_blocks, s.mlp_gains)
    s.grad_y_far = far(*s.grad_y_near)
    s.came = [s.came, *s.came_near, s.came_last[0]]
    s.came_other = [*s.came_other, s.came_last[1]]
    del s.came_near, s.came_last
    del s.out_own, s.out_own_other, s.out_near, s.out_near_other, s.out_last
    del s.projected_last, s.earlier_last
    s.end()

    s.mid_near = near(s.mid)
    s.end()

    s.mid_far = far(*s.mid_near)
    s.ffn_own = ffn_own
    s.end()

    s.mids = [s.mid, *s.mid_near, *s.mid_far]
    s.grads_y = [s.grad_y, *s.grad_y_near, *s.grad_y_far]
    s.ffn_other = across(s.ffn_own, CORE)
    units = s.ffn_own.shape[1] // 3
    s.hidden_own = hidden_units(s.mids, s.grads_y, s.ffn_own)
    del s.mid, s.mid_near, s.mid_far, s.grad_y_near, s.grad_y_far
    s.end()

    def gate_up_pairs():
        return [
            (hidden[i], weights, i - 1)
            for hidden, weights in ((s.hidden_own, s.ffn_own), (s.hidden_other, s.ffn_other))
            for i in (1, 2)
        ]

    def down_pairs():
        return [(s.hidden_own[0], s.ffn_own, 2), (s.hidden_other[0], s.ffn_other, 2)]

    def from_hidden_call(pairs, eighths):
        return (
            lambda first: from_hidden([(first, *pairs[0][1:]), *pairs[1:]], eighths),
            pairs[0][0],
        )

    def outer_call(lefts, rights, *added):
        return lambda first: row_outer(lefts, [[first, *rights[1:]]], 0, 8, *added)[0], rights[0]

    def send_near(sent):
        return across(sent[0], ACROSS_X), across(sent[1], ACROSS_Y)

    def send_far(came, rest, split):
        one_tail, two_head = rest
        return (
            across(rounded_sum(one_tail, split(came[1])[1]), ACROSS_X),
            across(rounded_sum(two_head, split(came[0])[1]), ACROSS_Y),
        )

    def total(came, came_far, own, split):
        head, tail = own
        full_sum = lambda *parts: sum(part.astype(full) for part in parts)
        return jnp.concatenate(
            [
                full_sum(head, split(came[0])[0], came_far[1]),
                full_sum(tail, split(came[1])[0], came_far[0]),
            ],
            0,
        )

    by_rows = lambda a: jnp.split(a, 2, 0)
    by_columns = lambda a: jnp.split(a, 2, 1)
    to_plane, rest_of_plane = (2, 6, 5, 7), (3, 4, 0, 1)

    s.hidden_other = hidden_units(s.mids, s.grads_y, s.ffn_other)
    (s.down_outer,) = in_order([outer_call(s.grads_y, s.hidden_other[:1])])
    s.end()

    s.down_came = across(s.down_outer, CORE)
    s.mid_sent = from_hidden(gate_up_pairs(), to_plane)
    del s.down_outer
    s.end()

    s.mid_came = send_near(s.mid_sent)
    s.down_mine, s.mid_rest, s.gate_up_outer = in_order(
        [
            outer_call(s.grads_y, s.hidden_own[:1], s.down_came),
            from_hidden_call(gate_up_pairs(), rest_of_plane),
            outer_call(s.mids, s.hidden_other[1:]),
        ]
    )
    del s.mid_sent, s.down_came
    s.end()

    down_total = lax.psum_scatter(s.down_mine, "shard", scatter_dimension=0, tiled=True)
    s.mid_came_far = send_far(s.mid_came, by_rows(s.mid_rest[0]), by_rows)
    s.gate_up_came = across(s.gate_up_outer, CORE)
    s.mlp_sent, s.mlp_rest = in_order(
        [
            from_hidden_call(down_pairs(), to_plane),
            from_hidden_call(down_pairs(), rest_of_plane),
        ]
    )
    del s.gate_up_outer, s.down_mine
    s.end()

    def back_call(i):
        raw, query, own_pair = s.projected[i]
        return (
            lambda query, *rest: attend_back(s.info, query, *rest),
            query, s.earlier[i], own_pair, s.attended[i][1], s.resid_low,
            *s.out_blocks[2 * i : 2 * i + 2], raw, s.cosine, s.sine, s.head_gains[:1],
        )

    def finish_call(i):
        return (
            finish, s.backs[i][0], s.backs[i][1], s.returned[i], s.projected[i][0],
            s.cosine, s.sine, s.head_gains[1:],
        )

    def give_back(*chips):
        s.returned = s.returned | {
            i: lax.ppermute(s.backs[i][2], "rep", downward) for i in chips
        }

    def odd_call(left, blocks, part=None):
        return lambda first: row_outer([first], [blocks], 0, 8, part=part)[0], left

    def head_call(left, blocks, came, part=None, places=(0, 1, 2, 3)):
        groups = [[blocks[1], blocks[3]], [blocks[2]], [blocks[0]]]
        at = [places[i] for i in (1, 3, 2, 0)]
        return lambda first: row_outer([first], groups, 0, 4, came, at, part), left

    def tail_call(left, blocks, came, part=None, places=(0, 1, 2, 3)):
        groups = [[blocks[2], blocks[3]], [blocks[1]], [blocks[0]]]
        at = [places[i] for i in (2, 3, 1, 0)]
        return lambda first: row_outer([first], groups, 4, 4, came, at, part), left

    s.mlp_came = send_near(s.mlp_sent)
    grad_mid = total(s.mid_came, s.mid_came_far, by_rows(s.mid_rest[1]), by_rows)
    inverse_mid = lax.rsqrt(jnp.mean(s.resid * s.resid, -1, keepdims=True) + EPS)
    mid_unit = s.resid * inverse_mid
    s.mlp_gain_part = jnp.sum(mid_unit * grad_mid, 0)
    s.grad_resid = s.grad_y.astype(full) + norm_back(
        mid_unit, inverse_mid, grad_mid * s.mlp_gains
    )
    s.resid_low = s.grad_resid.astype(low)
    s.resid_rolled = rolled(s.resid_low)
    s.returned = {}
    back, s.out_odd, s.gate_up_mine = in_order(
        [
            back_call(3),
            odd_call(s.resid_rolled, s.mixed, 1),
            outer_call(s.mids, s.hidden_own[1:], s.gate_up_came),
        ]
    )
    s.backs = {3: back}
    s.down_total = down_total
    del s.mid_came, s.mid_came_far, s.mid_rest, s.gate_up_came, s.hidden_own, s.hidden_other
    del s.mids, s.grads_y, s.ffn_own, s.ffn_other, s.mlp_sent
    s.end()

    gate_up_total = lax.psum_scatter(s.gate_up_mine, "shard", scatter_dimension=0, tiled=True)
    s.mlp_came_far = send_far(s.mlp_came, by_rows(s.mlp_rest[0]), by_rows)
    s.out_came = across(s.out_odd, CORE)
    give_back(3)
    back1, back2 = in_order([back_call(1), back_call(2)])
    s.backs = s.backs | {1: back1, 2: back2}
    del s.out_odd, s.gate_up_mine
    s.end()

    s.down_near = near(s.down_total)
    give_back(1, 2)
    s.out_head, s.out_tail, back, finished = in_order(
        [
            head_call(s.resid_rolled, s.mixed, s.out_came, 0),
            tail_call(s.resid_rolled, s.mixed, s.out_came, 0),
            back_call(0),
            finish_call(3),
        ]
    )
    s.backs = s.backs | {0: back}
    s.finished = {3: finished}
    del s.out_came
    s.end()

    s.out_near = send_near((s.out_head[0], s.out_tail[0]))
    mlp_out = total(s.mlp_came, s.mlp_came_far, by_rows(s.mlp_rest[1]), by_rows)
    s.output = (s.valid * (s.resid + mlp_out)).astype(low)
    give_back(0)
    finished1, finished2 = in_order([finish_call(1), finish_call(2)])
    s.finished = s.finished | {1: finished1, 2: finished2}
    del s.mlp_came, s.mlp_came_far, s.mlp_rest, s.resid
    s.end()

    output_sent = from_sequences_send(s.output)
    s.out_far = send_far(s.out_near, (s.out_tail[1], s.out_head[1]), by_columns)
    s.down_far = far(*s.down_near)
    (finished,) = in_order([finish_call(0)])
    s.finished = s.finished | {0: finished}
    (s.odd,) = in_order([odd_call(s.normed, [s.finished[i][1] for i in range(4)])])
    s.gate_up_total = gate_up_total
    s.output_first = output_sent[0]
    del s.output
    s.end()

    my_group = me.astype(jnp.int32)[None]

    def whole_call(widths, own, other, part=0):
        return lambda first: whole_columns(my_group, first, other, widths, part), own

    s.gate_up_near = near(s.gate_up_total)
    s.qkv_came = across(s.odd, CORE)
    out_sum = total(s.out_near, s.out_far, (s.out_head[2], s.out_tail[2]), by_columns)
    s.out_chunks = jnp.split(out_sum.astype(low), shards, 0)
    s.out_ring = ring_sum_first(s.out_chunks)
    weights = [
        pair
        for i in range(4)
        for pair in (
            (s.own_blocks[2 * i], s.came[i]), (s.own_blocks[2 * i + 1], s.came_other[i])
        )
    ]
    blocks = [part for i in range(4) for part in s.finished[i][:2]]
    grad_in = rolled(back_to_rows(blocks, weights))
    x_unit = s.x_low.astype(full) * s.inverse_in
    s.gain_parts = jnp.concatenate(
        [
            jnp.sum(x_unit * grad_in, 0),
            s.mlp_gain_part,
            sum(s.backs[i][3] for i in range(4))[0],
            sum(s.finished[i][2] for i in range(4))[0],
        ]
    )
    s.grad_tokens = (
        s.grad_resid + norm_back(x_unit, s.inverse_in, grad_in * s.attn_gains)
    ).astype(low)
    del s.odd, s.out_near, s.out_far, s.out_head, s.out_tail, s.backs
    del s.own_blocks, s.came, s.came_other, s.grad_resid, s.x_low
    s.end()

    even = [s.finished[i][0] for i in range(4)]
    s.head0, s.tail0, s.head1, s.tail1 = in_order(
        [
            call(s.normed, even, s.qkv_came, half, range(half, 8, 2))
            for half in range(2)
            for call in (head_call, tail_call)
        ]
    )
    tokens_sent = from_sequences_send(
        lax.optimization_barrier((s.grad_tokens, s.tail1[0]))[0]
    )
    s.down_spread = jnp.concatenate([s.down_total, *s.down_near, *s.down_far], 0)
    s.down_spread_other = across(s.down_spread, CORE)
    s.output_second = output_sent[1]
    s.gate_up_far = far(*s.gate_up_near)
    del s.qkv_came, s.finished, s.down_total, s.down_near, s.down_far
    s.end()

    def qkv_chunks(came, came_far, head, tail):
        own = total(came, came_far, (head[2], tail[2]), by_columns)
        return jnp.split(own.astype(low), shards, 0)

    s.near0 = send_near((s.head0[0], s.tail0[0]))
    s.out_ring_last = around(rounded_sum(s.out_chunks[3], s.out_ring[0]), 1)
    s.tokens_first = tokens_sent[0]
    s.gain_came = across(s.gain_parts, CORE)
    s.end()

    s.far0 = send_far(s.near0, (s.tail0[1], s.head0[1]), by_columns)
    s.near1 = send_near((s.head1[0], s.tail1[0]))
    (s.whole_down,) = in_order([whole_call((units,), s.down_spread, s.down_spread_other)])
    first = lax.optimization_barrier((s.gate_up_total, s.whole_down[0]))[0]
    s.gate_up_own = jnp.concatenate([first, *s.gate_up_near, *s.gate_up_far], 0)
    s.out_total = rounded_sum(s.out_chunks[0], s.out_ring[1], s.out_ring_last)
    s.gain_parts = s.gain_parts + s.gain_came
    s.tokens_second = tokens_sent[1]
    del s.down_spread, s.down_spread_other, s.out_chunks, s.out_ring, s.out_ring_last
    del s.gate_up_near, s.gate_up_far, s.gate_up_total, s.grad_tokens
    s.end()

    s.chunks0 = qkv_chunks(s.near0, s.far0, s.head0, s.tail0)
    s.ring0 = ring_sum_first(s.chunks0)
    s.far1 = send_far(s.near1, (s.tail1[1], s.head1[1]), by_columns)
    s.gate_up_other = across(s.gate_up_own, CORE)
    del s.near0, s.far0, s.head0, s.tail0
    s.end()

    s.last0 = around(rounded_sum(s.chunks0[3], s.ring0[0]), 1)
    s.chunks1 = qkv_chunks(s.near1, s.far1, s.head1, s.tail1)
    s.ring1 = ring_sum_first(s.chunks1)
    s.gain_came = across(s.gain_parts, ACROSS_X)
    ((s.whole_gate,),) = in_order([whole_call((units,), s.gate_up_own, s.gate_up_other)])
    del s.near1, s.far1, s.head1, s.tail1
    s.end()

    query_total = rounded_sum(s.chunks0[0], s.ring0[1], s.last0)
    s.total0 = jnp.concatenate([query_total, s.out_total], 1)
    s.spread0 = near(s.total0)
    s.last1 = around(rounded_sum(s.chunks1[3], s.ring1[0]), 1)
    s.gain_parts = s.gain_parts + s.gain_came
    s.gain_came = across(s.gain_parts, ACROSS_Y)
    ((s.whole_up,),) = in_order([whole_call((units,), s.gate_up_own, s.gate_up_other, 1)])
    del s.gate_up_own, s.gate_up_other
    del s.chunks0, s.ring0, s.last0, s.out_total
    s.end()

    s.spread_far0 = far(*s.spread0)
    s.total1 = rounded_sum(s.chunks1[0], s.ring1[1], s.last1)
    s.spread1 = near(s.total1)
    s.gain_parts = s.gain_parts + s.gain_came
    s.gain_came = lax.ppermute(s.gain_parts, "shard", [(i, i ^ 1) for i in range(shards)])
    del s.chunks1, s.ring1, s.last1
    s.end()

    s.own0 = jnp.concatenate([s.total0, *s.spread0, *s.spread_far0], 0)
    s.other0 = across(s.own0, CORE)
    s.spread_far1 = far(*s.spread1)
    s.gain_parts = s.gain_parts + s.gain_came
    s.gain_came = lax.ppermute(s.gain_parts, "shard", [(i, i ^ 2) for i in range(shards)])
    del s.total0, s.spread0, s.spread_far0
    s.end()

    s.own1 = jnp.concatenate([s.total1, *s.spread1, *s.spread_far1], 0)
    s.other1 = across(s.own1, CORE)
    (s.whole0,) = in_order([whole_call((head_columns, head_columns), s.own0, s.other0)])
    gain_sums = s.gain_parts + s.gain_came
    s.wide = lax.dynamic_slice_in_dim(
        gain_sums[: 2 * width].reshape(2, width), shard_at * piece, piece, 1
    )
    s.narrow = gain_sums[2 * width :]
    del s.own0, s.other0, s.total1, s.spread1, s.spread_far1
    s.end()

    ((whole_key, whole_value),) = in_order(
        [whole_call((head_dim, head_dim), s.own1, s.other1)]
    )
    return (
        jnp.stack(in_turn([s.output_first, s.output_second])),
        jnp.stack(in_turn([s.tokens_first, s.tokens_second])),
        s.wide[0],
        s.whole0[0],
        whole_key,
        whole_value,
        s.narrow[:head_dim],
        s.narrow[head_dim:],
        s.whole0[1],
        s.wide[1],
        s.whole_gate,
        s.whole_up,
        *s.whole_down,
    )


def solution(mesh):
    sizes = (mesh.shape["rep"], mesh.shape["shard"])
    return jax.shard_map(
        on_device_block if sizes == (8, 4) else on_device,
        mesh=mesh,
        in_specs=(
            P("rep", "shard", None),
            P("rep"),
            P("shard"),
            P("shard", None),
            P("shard", None),
            P("shard", None),
            P(),
            P(),
            P("shard", None),
            P("shard"),
            P("shard", None),
            P("shard", None),
            P("shard", None),
            P("rep", "shard", None),
        ),
        out_specs=(
            P("rep", "shard", None),
            P("rep", "shard", None),
            P("shard"),
            P("shard", None),
            P("shard", None),
            P("shard", None),
            P(),
            P(),
            P("shard", None),
            P("shard"),
            P("shard", None),
            P("shard", None),
            P("shard", None),
        ),
        check_vma=False,
    )
```
